32 devices in a mesh: win: 4 (over x, core), blk: 8 (over z, y).
Axes of the slice: x: 2, y: 2, z: 4, core: 2. Of those that a mesh axis runs over, the one named last changes fastest.
Arguments:
- tokens: bfloat16 [16, 4096, 768], P('win', 'blk'), may hold values from -6 to 6
- cotangent: bfloat16 [16, 4096, 768], P('win', 'blk'), may hold values from -6 to 6
- w_qkv: bfloat16 [768, 2304], replicated, may hold values from -0.21875 to 0.21875
- b_q: float32 [768], replicated, may hold values from -3 to 3
- b_v: float32 [768], replicated, may hold values from -0.6 to 0.6
- w_out: bfloat16 [768, 768], replicated, may hold values from -0.875 to 0.875
- b_out: float32 [768], replicated, may hold values from -2 to 2
- gain_one: float32 [768], replicated, may hold values from 0.5 to 1.5
- shift_one: float32 [768], replicated, may hold values from -2 to 2
- gain_two: float32 [768], replicated, may hold values from 0.5 to 1.5
- shift_two: float32 [768], replicated, may hold values from -2 to 2
- w_up: bfloat16 [768, 3072], replicated, may hold values from -0.21875 to 0.21875
- b_up: float32 [3072], replicated, may hold values from -2 to 2
- w_down: bfloat16 [3072, 768], replicated, may hold values from -0.109375 to 0.109375
- b_down: float32 [768], replicated, may hold values from -2 to 2
- rand_owner: int32 [16, 64, 12, 3], P('win'), may hold values from 0 to 7, all different within a row; in each aligned block of 96 rows (0 to 95, 96 to 191, ..., all dimensions but the last counted through in order) at most 72 rows name the same one
- rand_sub: int32 [16, 64, 12, 3], P('win'), may hold values from 0 to 7
- global_ids: int32 [16, 2], P('win'), may hold values from 0 to 63
- species: int32 [16], replicated, may hold values from 0 to 3
Outputs:
- out_tokens: bfloat16 [16, 4096, 768], P('win', 'blk')
- grad_tokens: bfloat16 [16, 4096, 768], P('win', 'blk')
- grad_w_qkv: float32 [768, 2304], P('blk')
- grad_b_q: float32 [768], P('blk')
- grad_b_v: float32 [768], P('blk')
- grad_w_out: float32 [768, 768], P('blk')
- grad_b_out: float32 [768], P('blk')
- grad_gain_one: float32 [768], P('blk')
- grad_shift_one: float32 [768], P('blk')
- grad_gain_two: float32 [768], P('blk')
- grad_shift_two: float32 [768], P('blk')
- grad_w_up: float32 [768, 3072], P('blk')
- grad_b_up: float32 [3072], P('blk')
- grad_w_down: float32 [3072, 768], P('blk')
- grad_b_down: float32 [768], P('blk')
The draws below stay inside these ranges and needn't reach their ends.
Inputs may be any that keep to these rules, and one draw needn't show every extreme that they name: `rand_owner`: in each window, the rows of the 8 query blocks on one device of blk (all heads and picks) name one value at most 72 times; the 3 values of one query block and head differ.
All inputs are finite; a program needn't handle non-finite values.
Results may differ from the reference program's by a relative error of at most 0.019.
Values may be sent and summed in bfloat16 or wider, within the bound.
A program may use at most 704 MiB of HBM per device.

```python
import math
import jax
import jax.numpy as jnp
import numpy as np
from jax import lax

D = 768
H = 12
HEAD_SIZE = 64
FF = 3072
BS = 64
R = 3
G = 2
NB = 64
SPECIES = 4
WINDOWS = 16
WLEN = 4096
BPD = 8
CAP = 72
N_BLK = 8


def touch_ends(entries, stream_key, least, top_value):
    place = [jax.random.randint(jax.random.fold_in(stream_key, axis), (), 0, length) for axis, length in enumerate(entries.shape)]
    longest = entries.shape.index(max(entries.shape))
    neighbour = place[:longest] + [(place[longest] + 1) % entries.shape[longest]] + place[longest + 1:]
    return entries.at[tuple(place)].set(least).at[tuple(neighbour)].set(top_value)


def block_levels(stream_key, extent, shards, low, largest):
    def one(position, shards_of):
        draws = jax.random.uniform(jax.random.fold_in(jax.random.fold_in(stream_key, 6), position), (shards_of,), jnp.float32, low / len(shards), largest / len(shards))
        return jnp.repeat(jnp.exp(draws), extent[position] // shards_of).reshape((-1,) + (1,) * (len(extent) - position - 1))

    loudness = one(*shards[0])
    for cut in shards[1:]:
        loudness = loudness * one(*cut)
    return loudness


def rank_table(amount, lean):
    weights = [(1 << 20) // math.isqrt(rank ** lean) + 1 for rank in range(1, amount + 1)]
    width = 1 + sum(weights) // (1 << 30)
    return np.cumsum(np.array([max(1, weight // width) for weight in weights]))


def ranked_ids(rng, shape, amount, lean):
    table = rank_table(amount, lean)
    pick = jax.random.randint(jax.random.fold_in(rng, 1), shape, 0, int(table[amount - 1]))
    rank = jnp.searchsorted(jnp.asarray(table, jnp.int32), pick, side="right")
    return jax.random.permutation(jax.random.fold_in(rng, 2), amount)[rank].astype(jnp.int32)


def assign_block(stream_key, own, number, rows, count, top, reach, skew):
    sequence = jax.random.permutation(stream_key, count)
    heavy_load, common = load_shares(count, rows * top, reach, skew, True), load_shares(count, rows * top, reach, skew, False)
    places = jnp.arange(count)

    def named(sizes, offset_by):
        used = int((sizes > 0).sum())
        fixed = max(1, used // 4)
        moved = fixed + (places - fixed + offset_by * (used - fixed)) % max(1, count - fixed)
        return jnp.zeros((count,), jnp.int32).at[sequence[jnp.where(places < fixed, places, moved)]].set(jnp.asarray(sizes, jnp.int32))

    sizes = jnp.where(number % 4 == 0, named(heavy_load, number // 4), named(common, number - number // 4 - 1))
    mixed = jax.random.permutation(jax.random.fold_in(own, 3), count)
    giver, receiver = mixed[0:count // 2 * 2:2], mixed[1:count // 2 * 2:2]
    room = jnp.minimum(sizes[giver] - 1, reach - sizes[receiver]) // 2
    room = jnp.where((giver == sequence[0]) | (receiver == sequence[0]) | (sizes[receiver] == 0), 0, jnp.maximum(room, 0))
    moved = jax.random.randint(jax.random.fold_in(own, 4), (count // 2,), 0, 1 << 20) % (room + 1)
    sizes = sizes.at[giver].add(-moved).at[receiver].add(moved)
    members = jnp.searchsorted(jnp.cumsum(sizes), jnp.arange(rows * top), side="right").astype(jnp.int32)
    listing = members.reshape(top, rows).T
    listing = listing[jax.random.permutation(jax.random.fold_in(own, 1), rows)]
    offset_by = jax.random.randint(jax.random.fold_in(own, 2), (rows, 1), 0, top)
    return jnp.take_along_axis(listing, (jnp.arange(top)[None, :] + offset_by) % top, axis=1)


def load_shares(number_of, total, limit, slope, full):
    loads = [(1 << 20) // math.isqrt(grade ** slope) + 1 for grade in range(1, number_of + 1)]
    largest = limit if full else min(limit, max(-(-total // number_of), total * loads[0] // sum(loads)))
    least = 1 if total - largest >= number_of - 1 else 0
    given, spare = [largest] + [least] * (number_of - 1), total - largest - least * (number_of - 1)
    while spare > 0:
        movable = [i for i in range(1, number_of) if given[i] < largest] or [i for i in range(1, number_of) if given[i] < limit]
        whole, remaining = sum([loads[i] for i in movable]), spare
        for i in movable:
            extra = min(limit - given[i], max(1, remaining * loads[i] // whole), spare)
            given[i] = given[i] + extra
            spare = spare - extra
    return np.array(given)


def bell_draw(key, extent, spread, most, cuts=(), kind=jnp.bfloat16):
    values = jax.random.normal(key, extent, jnp.float32) * spread
    if len(cuts) > 0:
        values = block_levels(key, extent, cuts, -0.22, 0.18) * values
    return jnp.clip(values, min=-most, max=most).astype(kind)


def setup_inputs(seed: int = 0) -> dict:
    key_of = jax.random.split(jax.random.key(seed), 20)
    tokens = bell_draw(key_of[0], (WINDOWS, WLEN, D), 1.0, 6.0, ((0, 4), (1, 8)))
    cotangent = bell_draw(key_of[1], (WINDOWS, WLEN, D), 1.0, 6.0, ((0, 4), (1, 8)))
    w_qkv = bell_draw(key_of[2], (D, 3 * D), D ** -0.5, 0.21875)
    b_q = bell_draw(key_of[3], (D,), 0.5, 3.0, (), jnp.float32)
    b_v = bell_draw(key_of[4], (D,), 0.1, 0.6, (), jnp.float32)
    w_out = bell_draw(key_of[5], (D, D), (D // 16) ** -0.5, 0.875)
    b_out = bell_draw(key_of[6], (D,), 0.3, 2.0, (), jnp.float32)
    gain_one = jnp.clip(1.0 + 0.1 * jax.random.normal(key_of[7], (D,), jnp.float32), 0.5, 1.5)
    shift_one = bell_draw(key_of[8], (D,), 0.3, 2.0, (), jnp.float32)
    gain_two = jnp.clip(1.0 + 0.1 * jax.random.normal(key_of[9], (D,), jnp.float32), 0.5, 1.5)
    shift_two = bell_draw(key_of[10], (D,), 0.3, 2.0, (), jnp.float32)
    w_up = bell_draw(key_of[11], (D, FF), D ** -0.5, 0.21875)
    b_up = bell_draw(key_of[12], (FF,), 0.3, 2.0, (), jnp.float32)
    w_down = bell_draw(key_of[13], (FF, D), FF ** -0.5, 0.109375)
    b_down = bell_draw(key_of[14], (D,), 0.3, 2.0, (), jnp.float32)
    rand_owner_keys = jax.random.split(jax.random.fold_in(key_of[15], 1), WINDOWS * NB * H // (BPD * H))
    rand_owner_turns = jax.random.permutation(jax.random.fold_in(key_of[15], 3), WINDOWS * NB * H // (BPD * H))
    rand_owner = jax.vmap(lambda own, number: assign_block(jax.random.fold_in(key_of[15], 2), own, number, BPD * H, N_BLK, R, CAP, 2))(rand_owner_keys, rand_owner_turns).reshape((WINDOWS, NB, H, R))
    rand_sub = touch_ends(jax.random.randint(key_of[16], (WINDOWS, NB, H, R), 0, BPD), jax.random.fold_in(key_of[16], 1), 0, BPD - 1).astype(jnp.int32)
    global_ids = touch_ends(jax.random.randint(key_of[17], (WINDOWS, G), 0, NB), jax.random.fold_in(key_of[17], 1), 0, NB - 1).astype(jnp.int32)
    species = touch_ends(ranked_ids(key_of[18], (WINDOWS,), SPECIES, 2), jax.random.fold_in(key_of[18], 3), 0, SPECIES - 1).astype(jnp.int32)
    return dict(tokens=tokens, cotangent=cotangent, w_qkv=w_qkv, b_q=b_q, b_v=b_v, w_out=w_out, b_out=b_out, gain_one=gain_one, shift_one=shift_one, gain_two=gain_two, shift_two=shift_two, w_up=w_up, b_up=b_up, w_down=w_down, b_down=b_down, rand_owner=rand_owner, rand_sub=rand_sub, global_ids=global_ids, species=species)


@jax.custom_vjp
def lower_precision(v):
    return lax.optimization_barrier(v.astype(jnp.bfloat16)).astype(jnp.float32)

@jax.custom_vjp
def lower_precision_back(v):
    return v

def low_keep(v):
    return (lower_precision(v), None)

def low_pass(kept, grad):
    return (grad,)

def back_keep(v):
    return (v, None)

def back_low(kept, grad):
    return (lower_precision(grad),)
lower_precision.defvjp(low_keep, low_pass)
lower_precision_back.defvjp(back_keep, back_low)
epsilon = 1e-05
masked_score = -1000000000.0

def matmul(left, right):
    return jnp.dot(left, right, precision=lax.Precision.HIGHEST, preferred_element_type=jnp.float32)

def layer_norm(values, norm_gain, norm_shift):
    average = lax.optimization_barrier(jnp.mean(values, axis=-1, keepdims=True))
    centred = values - average
    variance = lax.optimization_barrier(jnp.mean(centred * centred, axis=-1, keepdims=True))
    return centred * lax.rsqrt(variance + epsilon) * norm_gain + norm_shift

def assemble(blocks_in, chosen, global_row):
    padded = jnp.pad(blocks_in, ((1, 1), (0, 0), (0, 0)))
    global_part = jnp.broadcast_to(blocks_in[global_row][None], (NB, G, BS, blocks_in.shape[2]))
    stacked = jnp.concatenate([padded[:-2][:, None], blocks_in[:, None], padded[2:][:, None], global_part, blocks_in[chosen]], axis=1)
    return stacked.reshape(NB, (3 + G + R) * BS, blocks_in.shape[2])

def head_attend(query_block, gathered_keys, gathered_values, key_valid):
    score_matrix = lower_precision_back(jnp.einsum('odp,ovp->odv', query_block, gathered_keys, precision=lax.Precision.HIGHEST) * HEAD_SIZE ** (-0.5))
    score_matrix = jnp.where(key_valid[:, None, :], score_matrix, masked_score)
    weight_tree = jax.nn.softmax(score_matrix, axis=-1)
    return jnp.einsum('irw,iwn->irn', lower_precision(weight_tree), gathered_values, precision=lax.Precision.HIGHEST)

def window_forward(tokens_f, params, chosen, global_row):
    w_qkv, b_q, b_v, w_out, b_out, gain_one, shift_one, gain_two, shift_two, w_up, b_up, w_down, b_down = params
    normed = lower_precision(layer_norm(tokens_f, gain_one, shift_one))
    joined = matmul(normed, w_qkv)
    query_block = lower_precision(lower_precision_back(joined[:, :D] + b_q))
    key_all = lower_precision(lower_precision_back(joined[:, D:2 * D]))
    value_all = lower_precision(lower_precision_back(joined[:, 2 * D:] + b_v))

    def to_heads(tensor):
        return tensor.reshape(NB, BS, H, HEAD_SIZE).transpose(2, 0, 1, 3)
    block_pos = jnp.arange(NB)
    block_flags = jnp.concatenate([(block_pos > 0)[:, None], jnp.ones((NB, 1), jnp.bool_), (block_pos < NB - 1)[:, None], jnp.ones((NB, G + R), jnp.bool_)], axis=1)
    key_valid = jnp.repeat(block_flags, BS, axis=1)

    def one_head(operands):
        head_query, head_key, head_value, head_chosen = operands
        return head_attend(head_query, assemble(head_key, head_chosen, global_row), assemble(head_value, head_chosen, global_row), key_valid)
    attended = lax.map(jax.checkpoint(one_head), (to_heads(query_block), to_heads(key_all), to_heads(value_all), chosen.transpose(1, 0, 2)))
    merged = lower_precision(lower_precision_back(attended.transpose(1, 2, 0, 3).reshape(NB * BS, D)))
    residual = tokens_f + lower_precision_back(matmul(merged, w_out) + b_out)
    second = lower_precision(layer_norm(residual, gain_two, shift_two))
    inner_f = lower_precision_back(matmul(second, w_up) + b_up)
    active = lower_precision(jax.nn.gelu(inner_f, approximate=False))
    return residual + lower_precision_back(matmul(active, w_down) + b_down)

def reference(tokens, cotangent, w_qkv, b_q, b_v, w_out, b_out, gain_one, shift_one, gain_two, shift_two, w_up, b_up, w_down, b_down, rand_owner, rand_sub, global_ids, species):
    params = tuple((grad_item.astype(jnp.float32) for grad_item in (w_qkv, b_q, b_v, w_out, b_out, gain_one, shift_one, gain_two, shift_two, w_up, b_up, w_down, b_down)))
    chosen_all = (rand_owner * BPD + rand_sub).astype(jnp.int32)
    counts = lax.optimization_barrier(jnp.sum((species[:, None] == jnp.arange(SPECIES, dtype=jnp.int32)[None, :]).astype(jnp.float32), axis=0))
    window_scale = jnp.sqrt(WINDOWS / (SPECIES * counts[species]))

    def scan_step(totals, inputs):
        window_tokens, window_cot, window_chosen, window_global, scale_one = inputs

        def forward(values, weight_tree):
            return window_forward(values, weight_tree, window_chosen, window_global)
        result, pull_back = jax.vjp(forward, window_tokens.astype(jnp.float32), params)
        grad_inputs, grad_params = pull_back(window_cot.astype(jnp.float32) * scale_one)
        totals = jax.tree.map(lambda left, right: left + right, totals, grad_params)
        return (totals, (result.astype(jnp.bfloat16), grad_inputs.astype(jnp.bfloat16)))
    zero_grads = jax.tree.map(jnp.zeros_like, params)
    totals, (outputs, grad_tokens) = lax.scan(scan_step, zero_grads, (tokens, cotangent, chosen_all, global_ids, window_scale))
    return (outputs, grad_tokens, totals[0], totals[1], totals[2], totals[3], totals[4], totals[5], totals[6], totals[7], totals[8], totals[9], totals[10], totals[11], totals[12])
```

```python
from functools import partial

import jax
import jax.numpy as jnp
from jax import lax
from jax.experimental import pallas as pl
from jax.experimental.pallas import tpu as pltpu
from jax.sharding import PartitionSpec as P

SPECIES = 4


epsilon = 1e-05
masked_score = -1000000000.0


def padded(cells, sides, width):
    for axis, dim in sides:
        count = lax.axis_size(axis)
        ends = count - 1
        head = lax.slice_in_dim(cells, 0, width, axis=dim)
        tail = lax.slice_in_dim(cells, cells.shape[dim] - width, cells.shape[dim], axis=dim)
        cells = jnp.concatenate(
            [
                lax.ppermute(tail, axis, [(i, (i + 1) % count) for i in range(ends)]),
                cells,
                lax.ppermute(head, axis, [((i + 1) % count, i) for i in range(ends)]),
            ],
            axis=dim,
        )
    return cells


def layer_norm(values, norm_gain, norm_shift):
    average = jnp.mean(values, axis=-1, keepdims=True)
    centred = values - average
    variance = jnp.mean(centred * centred, axis=-1, keepdims=True)
    return centred * lax.rsqrt(variance + epsilon) * norm_gain + norm_shift


def take_rows(source, index_rows):
    return jnp.take(source, index_rows, axis=0)


def add_rows(base, index_rows, update):
    return base.at[index_rows].add(update)


def set_rows(base, index_rows, update):
    return base.at[index_rows].set(update)


HEADS_PER_GROUP = 4


def regroup_pairs(win_count, layers, step):
    pairs = []
    for win in range(win_count):
        for blk in range(2 * layers):
            layer, side = blk // 2, blk % 2
            target = ((layer + step) % layers) * 2 + win % 2
            pairs.append((win * 2 * layers + blk, ((win // 2) * 2 + side) * 2 * layers + target))
    return pairs


def flip_pairs(win_count, blk_count, win_bit, blk_bit):
    return [
        (win * blk_count + blk, (win ^ win_bit) * blk_count + (blk ^ blk_bit))
        for win in range(win_count)
        for blk in range(blk_count)
    ]


def swap(value, win_bit, blk_bit):
    pairs = flip_pairs(lax.axis_size("win"), lax.axis_size("blk"), win_bit, blk_bit)
    return lax.ppermute(value, ("win", "blk"), pairs)


def head_masks(lanes, head_dim, dtype):
    lane = lax.broadcasted_iota(jnp.int32, (1, lanes), 1)
    return [(lane // head_dim == h).astype(dtype) for h in range(lanes // head_dim)]


def block_places(table, slot, group, sizes):
    heads, picks, rand_size, half_blocks = sizes
    block = table[rand_size + 2 + slot]
    near = [table[rand_size + 2 + half_blocks + slot], slot, table[rand_size + 2 + 2 * half_blocks + slot]]
    row = (block * heads + group * HEADS_PER_GROUP) * picks
    rand = [[table[row + h * picks + r] for h in range(HEADS_PER_GROUP)] for r in range(picks)]
    return block, near, rand


def spread_heads(rows, masks):
    return jnp.concatenate([rows * m for m in masks], axis=0)


def pick_heads(square, masks, height):
    total = square[0:height] * masks[0]
    for h in range(1, len(masks)):
        total = total + square[h * height : (h + 1) * height] * masks[h]
    return total


def key_rows(source, near, glob, rand, low_half):
    parts = [source[p] for p in near] + [source[p] for p in glob]
    for places in rand:
        columns = []
        for c in range(len(places) // 2):
            low = source[places[2 * c], :, c * 128 : (c + 1) * 128]
            high = source[places[2 * c + 1], :, c * 128 : (c + 1) * 128]
            columns.append(jnp.where(low_half, low, high))
        parts.append(jnp.concatenate(columns, axis=1))
    return jnp.concatenate(parts, axis=0)


def mask_scores(scores, block, blocks, block_len):
    first = jnp.where(block > 0, scores[:block_len], masked_score)
    last = jnp.where(block < blocks - 1, scores[2 * block_len : 3 * block_len], masked_score)
    return jnp.concatenate([first, scores[block_len : 2 * block_len], last, scores[3 * block_len :]], axis=0)


def across(left, right):
    return lax.dot_general(left, right, (((1,), (1,)), ((), ())), preferred_element_type=jnp.float32)


def down(left, right):
    return lax.dot_general(left, right, (((0,), (0,)), ((), ())), preferred_element_type=jnp.float32)


def load_halves(target, own, other, half_blocks, block_len):
    lanes = own.shape[-1]
    target[0:half_blocks] = own[...].reshape(half_blocks, block_len, lanes)
    target[half_blocks:] = other[...].reshape(half_blocks, block_len, lanes)


def attend_kernel(sizes, blocks, head_dim, table, q_ref, k_own, k_other, v_own, v_other, o_ref, lse_ref, k_all, v_all):
    heads, picks, rand_size, half_blocks = sizes
    block_len = k_all.shape[1]
    lanes = q_ref.shape[1]
    group = pl.program_id(0)
    load_halves(k_all, k_own, k_other, half_blocks, block_len)
    load_halves(v_all, v_own, v_other, half_blocks, block_len)
    low_half = lax.broadcasted_iota(jnp.int32, (block_len, 128), 1) < head_dim
    masks = head_masks(lanes, head_dim, jnp.bfloat16)
    masks_f = head_masks(lanes, head_dim, jnp.float32)
    glob = [table[rand_size], table[rand_size + 1]]

    def one(slot, carry):
        block, near, rand = block_places(table, slot, group, sizes)
        rows = pl.ds(pl.multiple_of(slot * block_len, block_len), block_len)
        queries = spread_heads(q_ref[rows, :], masks)
        keys = key_rows(k_all, near, glob, rand, low_half)
        scores = mask_scores(across(keys, queries), block, blocks, block_len)
        top = jnp.max(scores, axis=0, keepdims=True)
        weights = jnp.exp(scores - top)
        total = jnp.sum(weights, axis=0, keepdims=True)
        probs = (weights * (1.0 / total)).astype(jnp.bfloat16)
        values = key_rows(v_all, near, glob, rand, low_half)
        o_ref[rows, :] = pick_heads(down(probs, values), masks_f, block_len).astype(jnp.bfloat16)
        lse_ref[0, pl.ds(slot, 1), :] = top + jnp.log(total)
        return carry

    lax.fori_loop(0, half_blocks, one, 0)


def attend_back_kernel(
    sizes, blocks, head_dim, scale, group,
    table, q_ref, k_own, k_other, v_own, v_other, go_ref, lse_ref,
    dq_ref, dk_own, dv_own, dk_other, dv_other,
    k_all, v_all, dk_all, dv_all, dk_glob, dv_glob,
):
    heads, picks, rand_size, half_blocks = sizes
    block_len = k_all.shape[1]
    lanes = q_ref.shape[1]
    f32 = jnp.float32
    load_halves(k_all, k_own, k_other, half_blocks, block_len)
    load_halves(v_all, v_own, v_other, half_blocks, block_len)
    dk_all[...] = jnp.zeros_like(dk_all)
    dv_all[...] = jnp.zeros_like(dv_all)
    dk_glob[...] = jnp.zeros_like(dk_glob)
    dv_glob[...] = jnp.zeros_like(dv_glob)
    low_half = lax.broadcasted_iota(jnp.int32, (block_len, 128), 1) < head_dim
    masks = head_masks(lanes, head_dim, jnp.bfloat16)
    masks_f = head_masks(lanes, head_dim, f32)
    glob = [table[rand_size], table[rand_size + 1]]

    def add_back(grads, near, rand, into, into_glob):
        for n in range(3):
            into[near[n]] += grads[n * block_len : (n + 1) * block_len]
        for n in range(2):
            into_glob[n] += grads[(3 + n) * block_len : (4 + n) * block_len]
        for r in range(picks):
            part = grads[(5 + r) * block_len : (6 + r) * block_len]
            for c in range(lanes // 128):
                cell = part[:, c * 128 : (c + 1) * 128]
                columns = pl.ds(c * 128, 128)
                into[rand[r][2 * c], :, columns] += jnp.where(low_half, cell, 0.0)
                into[rand[r][2 * c + 1], :, columns] += jnp.where(low_half, 0.0, cell)

    def one(slot, carry):
        block, near, rand = block_places(table, slot, group, sizes)
        rows = pl.ds(pl.multiple_of(slot * block_len, block_len), block_len)
        queries = spread_heads(q_ref[rows, :], masks)
        grads_out = spread_heads(go_ref[rows, :], masks)
        keys = key_rows(k_all, near, glob, rand, low_half)
        values = key_rows(v_all, near, glob, rand, low_half)
        scores = mask_scores(across(keys, queries), block, blocks, block_len)
        probs = jnp.exp(scores - lse_ref[0, pl.ds(slot, 1), :])
        grad_probs = across(values, grads_out)
        row_dot = jnp.sum(probs * grad_probs, axis=0, keepdims=True)
        grad_scores = (probs * (grad_probs - row_dot)).astype(jnp.bfloat16)
        add_back(jnp.dot(probs.astype(jnp.bfloat16), grads_out, preferred_element_type=f32), near, rand, dv_all, dv_glob)
        add_back(jnp.dot(grad_scores, queries, preferred_element_type=f32), near, rand, dk_all, dk_glob)
        dq_ref[rows, :] = (pick_heads(down(grad_scores, keys), masks_f, block_len) * scale).astype(jnp.bfloat16)
        return carry

    lax.fori_loop(0, half_blocks, one, 0)
    for n in range(2):
        dk_all[glob[n]] += dk_glob[n]
        dv_all[glob[n]] += dv_glob[n]
    for target, source, start in (
        (dk_own, dk_all, 0), (dv_own, dv_all, 0), (dk_other, dk_all, half_blocks), (dv_other, dv_all, half_blocks),
    ):
        target[...] = source[start : start + half_blocks].astype(jnp.bfloat16).reshape(target.shape)


def general_body(
    tokens,
    cotangent,
    w_qkv,
    b_q,
    b_v,
    w_out,
    b_out,
    gain_one,
    shift_one,
    gain_two,
    shift_two,
    w_up,
    b_up,
    w_down,
    b_down,
    rand_owner,
    rand_sub,
    global_ids,
    species,
):
    blk_count = lax.axis_size("blk")
    blk_pos = lax.axis_index("blk")
    win_pos = lax.axis_index("win")
    windows, length, model_width = tokens.shape
    blocks = rand_owner.shape[1]
    heads = rand_owner.shape[2]
    picks = rand_owner.shape[3]
    glob_count = global_ids.shape[1]
    own_blocks = blocks // blk_count
    block_len = length // own_blocks
    head_dim = model_width // heads
    pair_width = 2 * head_dim
    all_rows = windows * length
    key_count = 3 + glob_count + picks
    per_device = own_blocks * heads * picks
    slot_cap = max(2, 2 * per_device // blk_count)
    score_scale = head_dim ** (-0.5)
    f32 = jnp.float32
    bf16 = jnp.bfloat16
    tokens_f = tokens.reshape(all_rows, model_width).astype(f32)
    normed_f, norm_one_pull = jax.vjp(layer_norm, tokens_f, gain_one, shift_one)
    normed = normed_f.astype(bf16)
    joined = jnp.dot(normed, w_qkv, preferred_element_type=f32)
    query_vals = (joined[:, :model_width] + b_q).astype(bf16)
    key_vals = joined[:, model_width : 2 * model_width].astype(bf16)
    value_vals = (joined[:, 2 * model_width :] + b_v).astype(bf16)

    def to_heads(tensor):
        return tensor.reshape(windows, own_blocks, block_len, heads, head_dim).transpose(
            0, 1, 3, 2, 4
        )

    def from_heads(tensor):
        return tensor.transpose(0, 1, 3, 2, 4).reshape(all_rows, model_width)

    query_heads = to_heads(query_vals)
    local_pairs = jnp.concatenate([to_heads(key_vals), to_heads(value_vals)], axis=-1)
    rimmed = padded(local_pairs, (("blk", 1),), 1)
    block_ids = blk_pos * own_blocks + jnp.arange(own_blocks, dtype=jnp.int32)
    owned_glob = (global_ids[:, :, None] == block_ids[None, None, :]).astype(bf16)
    glob_terms = jnp.einsum("wgb,wbhsc->wghsc", owned_glob, local_pairs, preferred_element_type=f32)
    glob_pairs = lax.psum(glob_terms.astype(jnp.bfloat16), "blk").astype(jnp.float32).astype(bf16)
    owner_rows = rand_owner.reshape(windows, blk_count, per_device)
    sub_rows = rand_sub.reshape(windows, blk_count, per_device)
    owner_hits = (owner_rows[..., None] == jnp.arange(blk_count, dtype=jnp.int32)).astype(jnp.int32)
    slot_rows = jnp.sum(owner_hits * (jnp.cumsum(owner_hits, axis=2) - 1), axis=-1)
    my_owner = lax.dynamic_index_in_dim(owner_rows, blk_pos, 1, keepdims=False)
    my_slot = lax.dynamic_index_in_dim(slot_rows, blk_pos, 1, keepdims=False)
    fetch_index = my_owner * slot_cap + my_slot
    head_of_row = jnp.arange(per_device, dtype=jnp.int32) // picks % heads
    source_rows = sub_rows * heads + head_of_row[None, None, :]
    requester = jnp.arange(blk_count, dtype=jnp.int32)[None, :, None]
    target_rows = jnp.where(
        owner_rows == blk_pos, requester * slot_cap + slot_rows, blk_count * slot_cap
    )
    send_table = jnp.full((windows, blk_count * slot_cap + 1), own_blocks * heads, jnp.int32)
    send_table = jax.vmap(set_rows)(
        send_table, target_rows.reshape(windows, -1), source_rows.reshape(windows, -1)
    )[:, : blk_count * slot_cap]
    flat_pairs = jnp.concatenate(
        [
            local_pairs.reshape(windows, own_blocks * heads, block_len, pair_width),
            jnp.zeros((windows, 1, block_len, pair_width), bf16),
        ],
        axis=1,
    )
    outgoing = jax.vmap(take_rows)(flat_pairs, send_table).reshape(
        windows, blk_count, slot_cap, block_len, pair_width
    )
    incoming = lax.all_to_all(outgoing, "blk", split_axis=1, concat_axis=1, tiled=True).reshape(
        windows, blk_count * slot_cap, block_len, pair_width
    )
    rand_pairs = jax.vmap(take_rows)(incoming, fetch_index).reshape(
        windows, own_blocks, heads, picks, block_len, pair_width
    )
    near_pairs = jnp.stack(
        [rimmed[:, 0:own_blocks], rimmed[:, 1 : own_blocks + 1], rimmed[:, 2 : own_blocks + 2]],
        axis=3,
    )
    far_pairs = jnp.broadcast_to(
        glob_pairs.transpose(0, 2, 1, 3, 4)[:, None],
        (windows, own_blocks, heads, glob_count, block_len, pair_width),
    )
    gathered_keys = jnp.concatenate([near_pairs, far_pairs, rand_pairs], axis=3).reshape(
        windows, own_blocks, heads, key_count * block_len, pair_width
    )
    set_keys = gathered_keys[..., :head_dim]
    set_values = gathered_keys[..., head_dim:]
    block_flags = jnp.concatenate(
        [
            (block_ids > 0)[:, None],
            jnp.ones((own_blocks, 1), jnp.bool_),
            (block_ids < blocks - 1)[:, None],
            jnp.ones((own_blocks, glob_count + picks), jnp.bool_),
        ],
        axis=1,
    )
    key_valid = jnp.repeat(block_flags, block_len, axis=1)[None, :, None, None, :]

    def score_block():
        raw_scores = (
            jnp.einsum("wbhqe,wbhke->wbhqk", query_heads, set_keys, preferred_element_type=f32)
            * score_scale
        )
        return jnp.where(key_valid, raw_scores, masked_score)

    score_matrix = score_block()
    top_score = jnp.max(score_matrix, axis=-1, keepdims=True)
    log_total = top_score + jnp.log(
        jnp.sum(jnp.exp(score_matrix - top_score), axis=-1, keepdims=True)
    )
    probs_low = jnp.exp(score_matrix - log_total).astype(bf16)
    attended = jnp.einsum(
        "wbhqk,wbhke->wbhqe", probs_low, set_values, preferred_element_type=f32
    ).astype(bf16)
    merged = from_heads(attended)
    residual = tokens_f + (jnp.dot(merged, w_out, preferred_element_type=f32) + b_out)
    second_f, norm_two_pull = jax.vjp(layer_norm, residual, gain_two, shift_two)
    second = second_f.astype(bf16)
    inner_f = jnp.dot(second, w_up, preferred_element_type=f32) + b_up
    active_f, gelu_pull = jax.vjp(partial(jax.nn.gelu, approximate=False), inner_f)
    active = active_f.astype(bf16)
    output = residual + (jnp.dot(active, w_down, preferred_element_type=f32) + b_down)
    species_count = jnp.sum(
        (species[:, None] == jnp.arange(SPECIES, dtype=jnp.int32)[None, :]).astype(f32), axis=0
    )
    my_species = lax.dynamic_slice_in_dim(species, win_pos * windows, windows)
    own_count = jnp.sum(
        (my_species[:, None] == jnp.arange(SPECIES, dtype=jnp.int32)[None, :]).astype(f32)
        * species_count[None, :],
        axis=1,
    )
    window_scale = jnp.sqrt(species.shape[0] / (SPECIES * own_count))
    upstream = (cotangent.astype(f32) * window_scale[:, None, None]).reshape(all_rows, model_width)
    grad_branch = upstream.astype(bf16)
    grad_w_down = jnp.einsum("tf,td->fd", active, grad_branch, preferred_element_type=f32)
    grad_b_down = jnp.sum(grad_branch, axis=0, dtype=f32)
    grad_active = jnp.einsum("td,fd->tf", grad_branch, w_down, preferred_element_type=f32)
    grad_inner = gelu_pull(grad_active)[0].astype(bf16)
    grad_w_up = jnp.einsum("td,tf->df", second, grad_inner, preferred_element_type=f32)
    grad_b_up = jnp.sum(grad_inner, axis=0, dtype=f32)
    grad_second = jnp.einsum("tf,df->td", grad_inner, w_up, preferred_element_type=f32)
    grad_resid_norm, grad_gain_two, grad_shift_two = norm_two_pull(grad_second)
    grad_resid = upstream + grad_resid_norm
    grad_proj = grad_resid.astype(bf16)
    grad_w_out = jnp.einsum("ti,to->io", merged, grad_proj, preferred_element_type=f32)
    grad_b_out = jnp.sum(grad_proj, axis=0, dtype=f32)
    grad_attended = to_heads(
        jnp.einsum("to,io->ti", grad_proj, w_out, preferred_element_type=f32).astype(bf16)
    )
    probs_full = jnp.exp(score_block() - log_total)
    grad_probs = jnp.einsum(
        "wbhqe,wbhke->wbhqk", grad_attended, set_values, preferred_element_type=f32
    )
    grad_set_values = jnp.einsum(
        "wbhqk,wbhqe->wbhke", probs_full.astype(bf16), grad_attended, preferred_element_type=f32
    )
    row_dot = jnp.sum(probs_full * grad_probs, axis=-1, keepdims=True)
    grad_scores = (probs_full * (grad_probs - row_dot)).astype(bf16)
    grad_query = (
        jnp.einsum("wbhqk,wbhke->wbhqe", grad_scores, set_keys, preferred_element_type=f32)
        * score_scale
    )
    grad_set_keys = (
        jnp.einsum("wbhqk,wbhqe->wbhke", grad_scores, query_heads, preferred_element_type=f32)
        * score_scale
    )
    grad_set = jnp.concatenate([grad_set_keys, grad_set_values], axis=-1).reshape(
        windows, own_blocks, heads, key_count, block_len, pair_width
    )
    extended = (
        jnp.pad(grad_set[:, :, :, 1], ((0, 0), (1, 1), (0, 0), (0, 0), (0, 0)))
        + jnp.pad(grad_set[:, :, :, 0], ((0, 0), (0, 2), (0, 0), (0, 0), (0, 0)))
        + jnp.pad(grad_set[:, :, :, 2], ((0, 0), (2, 0), (0, 0), (0, 0), (0, 0)))
    )
    edge_grads = jnp.concatenate([extended[:, :1], extended[:, own_blocks + 1 :]], axis=1)
    edge_back = padded(edge_grads.astype(jnp.bfloat16), (("blk", 1),), 1).astype(edge_grads.dtype)
    pair_grad = extended[:, 1 : own_blocks + 1]
    pair_grad = pair_grad.at[:, 0].add(edge_back[:, 0]).at[:, own_blocks - 1].add(edge_back[:, 3])
    glob_grad = jnp.sum(grad_set[:, :, :, 3 : 3 + glob_count], axis=1).transpose(0, 2, 1, 3, 4)
    glob_total = lax.psum(glob_grad.astype(jnp.bfloat16), "blk").astype(jnp.float32)
    pair_grad = pair_grad + jnp.einsum(
        "wgb,wghsc->wbhsc", owned_glob.astype(f32), glob_total, precision=lax.Precision.HIGHEST
    )
    rand_grad = grad_set[:, :, :, 3 + glob_count :].reshape(
        windows, per_device, block_len, pair_width
    )
    back_out = jax.vmap(add_rows)(
        jnp.zeros((windows, blk_count * slot_cap, block_len, pair_width), f32),
        fetch_index,
        rand_grad,
    )
    back_in = lax.all_to_all(
        back_out.reshape(windows, blk_count, slot_cap, block_len, pair_width).astype(jnp.bfloat16),
        "blk",
        split_axis=1,
        concat_axis=1,
        tiled=True,
    ).astype(jnp.float32)
    owner_sum = jax.vmap(add_rows)(
        jnp.zeros((windows, own_blocks * heads + 1, block_len, pair_width), f32),
        send_table,
        back_in.reshape(windows, blk_count * slot_cap, block_len, pair_width),
    )
    pair_grad = pair_grad + owner_sum[:, : own_blocks * heads].reshape(
        windows, own_blocks, heads, block_len, pair_width
    )
    grad_keys = from_heads(pair_grad[..., :head_dim].astype(bf16))
    grad_values = from_heads(pair_grad[..., head_dim:].astype(bf16))
    grad_joined = jnp.concatenate(
        [from_heads(grad_query.astype(bf16)), grad_keys, grad_values], axis=1
    )
    grad_w_qkv = jnp.einsum("td,tc->dc", normed, grad_joined, preferred_element_type=f32)
    grad_b_q = jnp.sum(grad_joined[:, :model_width], axis=0, dtype=f32)
    grad_b_v = jnp.sum(grad_joined[:, 2 * model_width :], axis=0, dtype=f32)
    grad_normed = jnp.einsum("tc,dc->td", grad_joined, w_qkv, preferred_element_type=f32)
    grad_tok_norm, grad_gain_one, grad_shift_one = norm_one_pull(grad_normed)
    grad_tokens = (grad_resid + grad_tok_norm).astype(bf16).reshape(windows, length, model_width)
    local_grads = (
        grad_w_qkv,
        grad_b_q,
        grad_b_v,
        grad_w_out,
        grad_b_out,
        grad_gain_one,
        grad_shift_one,
        grad_gain_two,
        grad_shift_two,
        grad_w_up,
        grad_b_up,
        grad_w_down,
        grad_b_down,
    )
    packed_grads = jnp.concatenate(
        [grad_item.reshape(blk_count, -1) for grad_item in local_grads], axis=1
    )
    total_cols = packed_grads.shape[1]
    win_count = lax.axis_size("win")
    pad_cols = -total_cols % win_count
    shard_sum = lax.psum_scatter(
        packed_grads.astype(jnp.bfloat16), "blk", scatter_dimension=0, tiled=True
    ).astype(jnp.float32)
    split_shard = jnp.pad(shard_sum, ((0, 0), (0, pad_cols))).reshape(win_count, -1)
    group_piece = lax.psum_scatter(
        split_shard.astype(jnp.bfloat16), "win", scatter_dimension=0, tiled=True
    ).astype(jnp.float32)
    summed = (
        lax.all_gather(group_piece.astype(jnp.bfloat16), "win", axis=0, tiled=True)
        .astype(group_piece.dtype)
        .reshape(1, -1)[:, :total_cols]
    )
    shards = []
    offset = 0
    for grad_item in local_grads:
        entry_count = grad_item.size // blk_count
        shards.append(
            summed[0, offset : offset + entry_count].reshape(
                (grad_item.shape[0] // blk_count,) + grad_item.shape[1:]
            )
        )
        offset = offset + entry_count
    out_tokens = output.astype(bf16).reshape(windows, length, model_width)
    return (
        out_tokens,
        grad_tokens,
        shards[0],
        shards[1],
        shards[2],
        shards[3],
        shards[4],
        shards[5],
        shards[6],
        shards[7],
        shards[8],
        shards[9],
        shards[10],
        shards[11],
        shards[12],
    )


def layer_step(*arguments):
    windows = arguments[0].shape[0]
    paired = lax.axis_size("blk") == 2 * windows and lax.axis_size("win") % 2 == 0
    return (paired_body if paired else general_body)(*arguments)


def paired_body(
    tokens,
    cotangent,
    w_qkv,
    b_q,
    b_v,
    w_out,
    b_out,
    gain_one,
    shift_one,
    gain_two,
    shift_two,
    w_up,
    b_up,
    w_down,
    b_down,
    rand_owner,
    rand_sub,
    global_ids,
    species,
):
    f32 = jnp.float32
    bf16 = jnp.bfloat16
    win_count = lax.axis_size("win")
    blk_count = lax.axis_size("blk")
    win_pos = lax.axis_index("win")
    blk_pos = lax.axis_index("blk")
    layers, length, width = tokens.shape
    core, layer, side = win_pos % 2, blk_pos // 2, blk_pos % 2
    blocks, heads, picks = rand_owner.shape[1:]
    own_blocks = blocks // blk_count
    half_blocks = blocks // 2
    block_len = length // own_blocks
    head_dim = width // heads
    all_rows = layers * length
    lanes = HEADS_PER_GROUP * head_dim
    groups = heads // HEADS_PER_GROUP
    score_scale = head_dim ** (-0.5)

    def regroup(value):
        parts = []
        for step in range(layers):
            part = lax.dynamic_index_in_dim(value, (layer + step) % layers, 0, keepdims=False)
            parts.append(lax.ppermute(part, ("win", "blk"), regroup_pairs(win_count, layers, step)))
        return jnp.concatenate(parts, axis=0)

    def regroup_back(value):
        result = jnp.zeros((layers, length, width), value.dtype)
        for step in range(layers):
            pairs = [(b, a) for a, b in regroup_pairs(win_count, layers, step)]
            part = lax.ppermute(value[step * length : (step + 1) * length], ("win", "blk"), pairs)
            result = lax.dynamic_update_index_in_dim(result, part, (layer + step) % layers, 0)
        return result

    rows_in = regroup(tokens)
    cot_in = regroup(cotangent)

    rand_size = blocks * heads * picks
    named = jnp.concatenate(
        [
            lax.dynamic_index_in_dim((rand_owner * own_blocks + rand_sub).reshape(layers, rand_size), layer, 0, keepdims=False),
            lax.dynamic_index_in_dim(global_ids, layer, 0, keepdims=False),
        ]
    )
    named = jnp.where(side == core, named, swap(named, 1, 0))

    def place_of(block):
        owner = block // own_blocks
        half = jnp.where(owner % 2 == core, 0, half_blocks)
        return half + ((layer - owner // 2) % layers) * own_blocks + block % own_blocks

    slot = jnp.arange(half_blocks, dtype=jnp.int32)
    slot_block = (((layer - slot // own_blocks) % layers) * 2 + core) * own_blocks + slot % own_blocks
    table = jnp.concatenate(
        [
            place_of(named),
            slot_block,
            place_of(jnp.maximum(slot_block - 1, 0)),
            place_of(jnp.minimum(slot_block + 1, blocks - 1)),
        ]
    )
    sizes = (heads, picks, rand_size, half_blocks)

    tokens_f = rows_in.astype(f32)
    normed_f, norm_one_pull = jax.vjp(layer_norm, tokens_f, gain_one, shift_one)
    normed = normed_f.astype(bf16)
    joined = jnp.dot(normed, w_qkv, preferred_element_type=f32)
    query = (joined[:, :width] + b_q).astype(bf16) * jnp.asarray(score_scale, bf16)
    key_value = jnp.concatenate([joined[:, width : 2 * width], joined[:, 2 * width :] + b_v], axis=1).astype(bf16)
    key_value_other = swap(key_value, 1, 0)

    def lane_block(first):
        return pl.BlockSpec((all_rows, lanes), lambda g, t: (0, first + g))

    store = pltpu.VMEM((blocks, block_len, lanes), bf16)
    attended, log_total = pl.pallas_call(
        partial(attend_kernel, sizes, blocks, head_dim),
        grid_spec=pltpu.PrefetchScalarGridSpec(
            num_scalar_prefetch=1,
            grid=(groups,),
            in_specs=[lane_block(0), lane_block(0), lane_block(0), lane_block(groups), lane_block(groups)],
            out_specs=[lane_block(0), pl.BlockSpec((1, half_blocks, lanes), lambda g, t: (g, 0, 0))],
            scratch_shapes=[store, store],
        ),
        out_shape=[
            jax.ShapeDtypeStruct((all_rows, width), bf16),
            jax.ShapeDtypeStruct((groups, half_blocks, lanes), f32),
        ],
        compiler_params=pltpu.CompilerParams(vmem_limit_bytes=56 << 20),
        cost_estimate=pl.CostEstimate(flops=4 * all_rows * 512 * width, bytes_accessed=25 << 20, transcendentals=all_rows * 512 * heads),
        name="attend",
    )(table, query, key_value, key_value_other, key_value, key_value_other)

    merged = attended
    residual = tokens_f + (jnp.dot(merged, w_out, preferred_element_type=f32) + b_out)
    second_f, norm_two_pull = jax.vjp(layer_norm, residual, gain_two, shift_two)
    second = second_f.astype(bf16)
    inner_f = jnp.dot(second, w_up, preferred_element_type=f32) + b_up
    active_f, gelu_pull = jax.vjp(partial(jax.nn.gelu, approximate=False), inner_f)
    active = active_f.astype(bf16)
    output = residual + (jnp.dot(active, w_down, preferred_element_type=f32) + b_down)
    out_tokens = regroup_back(output.astype(bf16))

    species_count = jnp.sum(
        (species[:, None] == jnp.arange(SPECIES, dtype=jnp.int32)[None, :]).astype(f32), axis=0
    )
    my_window = ((win_pos // 2) * 2 + side) * layers + layer
    my_species = lax.dynamic_index_in_dim(species, my_window, 0, keepdims=False)
    own_count = jnp.sum(
        (my_species == jnp.arange(SPECIES, dtype=jnp.int32)).astype(f32) * species_count
    )
    window_scale = jnp.sqrt(species.shape[0] / (SPECIES * own_count))
    upstream = cot_in.astype(f32) * window_scale
    grad_branch = upstream.astype(bf16)
    grad_w_down = jnp.einsum("tf,td->fd", active, grad_branch, preferred_element_type=f32)
    grad_b_down = jnp.sum(grad_branch, axis=0, dtype=f32)
    grad_active = jnp.einsum("td,fd->tf", grad_branch, w_down, preferred_element_type=f32)
    grad_inner = gelu_pull(grad_active)[0].astype(bf16)
    grad_w_up = jnp.einsum("td,tf->df", second, grad_inner, preferred_element_type=f32)
    grad_b_up = jnp.sum(grad_inner, axis=0, dtype=f32)
    grad_second = jnp.einsum("tf,df->td", grad_inner, w_up, preferred_element_type=f32)
    grad_resid_norm, grad_gain_two, grad_shift_two = norm_two_pull(grad_second)
    grad_resid = upstream + grad_resid_norm
    grad_proj = grad_resid.astype(bf16)
    grad_w_out = jnp.einsum("ti,to->io", merged, grad_proj, preferred_element_type=f32)
    grad_b_out = jnp.sum(grad_proj, axis=0, dtype=f32)
    grad_attended = jnp.einsum("to,io->ti", grad_proj, w_out, preferred_element_type=f32).astype(bf16)

    half_shape = jax.ShapeDtypeStruct((all_rows, lanes), bf16)
    grad_rows = []
    for group in range(groups):
        def column(first):
            return pl.BlockSpec((all_rows, lanes), lambda g, t: (0, first))
        whole = pl.BlockSpec((all_rows, lanes), lambda g, t: (0, 0))
        grad_store = pltpu.VMEM((blocks, block_len, lanes), f32)
        glob_store = pltpu.VMEM((2, block_len, lanes), f32)
        grad_rows.append(
            pl.pallas_call(
                partial(attend_back_kernel, sizes, blocks, head_dim, score_scale, group),
                grid_spec=pltpu.PrefetchScalarGridSpec(
                    num_scalar_prefetch=1,
                    grid=(1,),
                    in_specs=[
                        column(group), column(group), column(group), column(groups + group), column(groups + group), column(group),
                        pl.BlockSpec((1, half_blocks, lanes), lambda g, t: (group, 0, 0)),
                    ],
                    out_specs=[whole] * 5,
                    scratch_shapes=[store, store, grad_store, grad_store, glob_store, glob_store],
                ),
                out_shape=[half_shape] * 5,
                compiler_params=pltpu.CompilerParams(vmem_limit_bytes=56 << 20),
                cost_estimate=pl.CostEstimate(flops=10 * all_rows * 512 * lanes, bytes_accessed=12 << 20, transcendentals=all_rows * 512 * HEADS_PER_GROUP),
                name="attend_back",
            )(table, query, key_value, key_value_other, key_value, key_value_other, grad_attended, log_total)
        )
    grad_parts = [[], [], []]
    for dq, dk_own, dv_own, dk_other, dv_other in grad_rows:
        grad_parts[0].append(dq)
        for kind, own, other in ((1, dk_own, dk_other), (2, dv_own, dv_other)):
            grad_parts[kind].append((own.astype(f32) + swap(other, 1, 0).astype(f32)).astype(bf16))
    grad_joined = jnp.concatenate(grad_parts[0] + grad_parts[1] + grad_parts[2], axis=1)

    grad_w_qkv = jnp.einsum("td,tc->dc", normed, grad_joined, preferred_element_type=f32)
    grad_b_q = jnp.sum(grad_joined[:, :width], axis=0, dtype=f32)
    grad_b_v = jnp.sum(grad_joined[:, 2 * width :], axis=0, dtype=f32)
    grad_normed = jnp.einsum("tc,dc->td", grad_joined, w_qkv, preferred_element_type=f32)
    grad_tok_norm, grad_gain_one, grad_shift_one = norm_one_pull(grad_normed)
    grad_tokens = regroup_back((grad_resid + grad_tok_norm).astype(bf16))

    def shard_rows(grads):
        rows = jnp.concatenate([g.reshape(blk_count, -1, width) for g in grads], axis=1)
        return jnp.pad(rows.astype(bf16), ((0, 0), (0, -rows.shape[1] % (16 * win_count)), (0, 0)))

    def reduce_shards(rows):
        pieces = win_count
        size = rows.shape[1] // pieces
        cells = rows.reshape(layers, 2, win_count // 2, 2, size, width)

        def halve(cells, axis, bit, win_bit, blk_bit):
            keep = lax.dynamic_index_in_dim(cells, bit, axis, keepdims=False)
            send = lax.dynamic_index_in_dim(cells, 1 - bit, axis, keepdims=False)
            return (keep.astype(f32) + swap(send, win_bit, blk_bit).astype(f32)).astype(bf16)

        cells = halve(cells, 3, core, 1, 0)
        cells = halve(cells, 1, side, 0, 1)
        hop = 2
        while cells.shape[1] > 1:
            count = cells.shape[1]
            cells = cells.reshape((layers, count // 2, 2) + cells.shape[2:])
            cells = halve(cells, 2, (win_pos // hop) % 2, hop, 0)
            hop *= 2
        cells = cells[:, 0]
        hop = 1
        while cells.shape[0] > 1:
            cells = cells.reshape((cells.shape[0] // 2, 2) + cells.shape[1:])
            cells = halve(cells, 1, (layer // hop) % 2, 0, 2 * hop)
            hop *= 2
        return lax.all_gather(cells[0], "win", axis=0, tiled=True)

    def columns_first(grad):
        count = grad.shape[1] // width
        return grad.reshape(blk_count, -1, count, width).transpose(0, 2, 1, 3)

    def rows_again(rows, count):
        return rows.reshape(count, -1, width).transpose(1, 0, 2).reshape(-1, count * width)

    def vectors(parts):
        flat = jnp.concatenate([p.reshape(blk_count, -1) for p in parts], axis=1)
        return jnp.pad(flat, ((0, 0), (0, -flat.shape[1] % width)))

    early = reduce_shards(
        shard_rows([columns_first(grad_w_up), grad_w_down, grad_w_out, vectors([grad_b_out, grad_gain_two, grad_shift_two, grad_b_up, grad_b_down])])
    ).astype(f32)
    late = reduce_shards(
        shard_rows([columns_first(grad_w_qkv), vectors([grad_b_q, grad_b_v, grad_gain_one, grad_shift_one])])
    ).astype(f32)
    part = width // blk_count
    wide = w_up.shape[1] // width
    done_up = rows_again(early[: wide * part], wide)
    done_down = early[wide * part : 2 * wide * part]
    done_out = early[2 * wide * part : (2 * wide + 1) * part]
    early_vec = early[(2 * wide + 1) * part :].reshape(-1)
    done_qkv = rows_again(late[: 3 * part], 3)
    late_vec = late[3 * part :].reshape(-1)
    return (
        out_tokens,
        grad_tokens,
        done_qkv,
        late_vec[:part],
        late_vec[part : 2 * part],
        done_out,
        early_vec[:part],
        late_vec[2 * part : 3 * part],
        late_vec[3 * part : 4 * part],
        early_vec[part : 2 * part],
        early_vec[2 * part : 3 * part],
        done_up,
        early_vec[3 * part : (3 + wide) * part],
        done_down,
        early_vec[(3 + wide) * part : (4 + wide) * part],
    )


def solution(mesh):
    placed = (
        P("win", "blk", None),
        P("win", "blk", None),
        P(),
        P(),
        P(),
        P(),
        P(),
        P(),
        P(),
        P(),
        P(),
        P(),
        P(),
        P(),
        P(),
        P("win", None, None, None),
        P("win", None, None, None),
        P("win", None),
        P(),
    )
    return jax.shard_map(
        layer_step,
        mesh=mesh,
        in_specs=placed,
        out_specs=(
            P("win", "blk", None),
            P("win", "blk", None),
            P("blk", None),
            P("blk"),
            P("blk"),
            P("blk", None),
            P("blk"),
            P("blk"),
            P("blk"),
            P("blk"),
            P("blk"),
            P("blk", None),
            P("blk"),
            P("blk", None),
            P("blk"),
        ),
        check_vma=False,
    )
```

```python
from functools import partial

import jax
import jax.numpy as jnp
from jax import lax
from jax.experimental import pallas as pl
from jax.experimental.pallas import tpu as pltpu
from jax.sharding import PartitionSpec as P

SPECIES = 4


epsilon = 1e-05
masked_score = -1000000000.0


def padded(cells, sides, width):
    for axis, dim in sides:
        count = lax.axis_size(axis)
        ends = count - 1
        head = lax.slice_in_dim(cells, 0, width, axis=dim)
        tail = lax.slice_in_dim(cells, cells.shape[dim] - width, cells.shape[dim], axis=dim)
        cells = jnp.concatenate(
            [
                lax.ppermute(tail, axis, [(i, (i + 1) % count) for i in range(ends)]),
                cells,
                lax.ppermute(head, axis, [((i + 1) % count, i) for i in range(ends)]),
            ],
            axis=dim,
        )
    return cells


def layer_norm(values, norm_gain, norm_shift):
    average = jnp.mean(values, axis=-1, keepdims=True)
    centred = values - average
    variance = jnp.mean(centred * centred, axis=-1, keepdims=True)
    return centred * lax.rsqrt(variance + epsilon) * norm_gain + norm_shift


def take_rows(source, index_rows):
    return jnp.take(source, index_rows, axis=0)


def add_rows(base, index_rows, update):
    return base.at[index_rows].add(update)


def set_rows(base, index_rows, update):
    return base.at[index_rows].set(update)


HEADS_PER_GROUP = 4


def regroup_pairs(win_count, layers, step):
    pairs = []
    for win in range(win_count):
        for blk in range(2 * layers):
            layer, side = blk // 2, blk % 2
            target = ((layer + step) % layers) * 2 + win % 2
            pairs.append((win * 2 * layers + blk, ((win // 2) * 2 + side) * 2 * layers + target))
    return pairs


def flip_pairs(win_count, blk_count, win_bit, blk_bit):
    return [
        (win * blk_count + blk, (win ^ win_bit) * blk_count + (blk ^ blk_bit))
        for win in range(win_count)
        for blk in range(blk_count)
    ]


def swap(value, win_bit, blk_bit):
    pairs = flip_pairs(lax.axis_size("win"), lax.axis_size("blk"), win_bit, blk_bit)
    return lax.ppermute(value, ("win", "blk"), pairs)


def head_masks(lanes, head_dim, dtype):
    lane = lax.broadcasted_iota(jnp.int32, (1, lanes), 1)
    return [(lane // head_dim == h).astype(dtype) for h in range(lanes // head_dim)]


def block_places(table, slot, group, sizes):
    heads, picks, rand_size, half_blocks = sizes
    block = table[rand_size + 2 + slot]
    near = [table[rand_size + 2 + half_blocks + slot], slot, table[rand_size + 2 + 2 * half_blocks + slot]]
    row = (block * heads + group * HEADS_PER_GROUP) * picks
    rand = [[table[row + h * picks + r] for h in range(HEADS_PER_GROUP)] for r in range(picks)]
    return block, near, rand


def spread_heads(rows, masks):
    return jnp.concatenate([rows * m for m in masks], axis=0)


def pick_heads(square, masks, height):
    total = square[0:height] * masks[0]
    for h in range(1, len(masks)):
        total = total + square[h * height : (h + 1) * height] * masks[h]
    return total


def key_rows(source, near, glob, rand, low_half):
    parts = [source[p] for p in near] + [source[p] for p in glob]
    for places in rand:
        columns = []
        for c in range(len(places) // 2):
            low = source[places[2 * c], :, c * 128 : (c + 1) * 128]
            high = source[places[2 * c + 1], :, c * 128 : (c + 1) * 128]
            columns.append(jnp.where(low_half, low, high))
        parts.append(jnp.concatenate(columns, axis=1))
    return jnp.concatenate(parts, axis=0)


def mask_scores(scores, block, blocks, block_len):
    first = jnp.where(block > 0, scores[:block_len], masked_score)
    last = jnp.where(block < blocks - 1, scores[2 * block_len : 3 * block_len], masked_score)
    return jnp.concatenate([first, scores[block_len : 2 * block_len], last, scores[3 * block_len :]], axis=0)


def across(left, right):
    return lax.dot_general(left, right, (((1,), (1,)), ((), ())), preferred_element_type=jnp.float32)


def down(left, right):
    return lax.dot_general(left, right, (((0,), (0,)), ((), ())), preferred_element_type=jnp.float32)


def load_halves(target, own, other, half_blocks, block_len):
    lanes = own.shape[-1]
    target[0:half_blocks] = own[...].reshape(half_blocks, block_len, lanes)
    target[half_blocks:] = other[...].reshape(half_blocks, block_len, lanes)


def attend_kernel(sizes, blocks, head_dim, table, q_ref, k_own, k_other, v_own, v_other, o_ref, lse_ref, k_all, v_all):
    heads, picks, rand_size, half_blocks = sizes
    block_len = k_all.shape[1]
    lanes = q_ref.shape[1]
    group = pl.program_id(0)
    load_halves(k_all, k_own, k_other, half_blocks, block_len)
    load_halves(v_all, v_own, v_other, half_blocks, block_len)
    low_half = lax.broadcasted_iota(jnp.int32, (block_len, 128), 1) < head_dim
    masks = head_masks(lanes, head_dim, jnp.bfloat16)
    masks_f = head_masks(lanes, head_dim, jnp.float32)
    glob = [table[rand_size], table[rand_size + 1]]

    def one(slot, carry):
        block, near, rand = block_places(table, slot, group, sizes)
        rows = pl.ds(pl.multiple_of(slot * block_len, block_len), block_len)
        queries = spread_heads(q_ref[rows, :], masks)
        keys = key_rows(k_all, near, glob, rand, low_half)
        scores = mask_scores(across(keys, queries), block, blocks, block_len)
        top = jnp.max(scores, axis=0, keepdims=True)
        weights = jnp.exp(scores - top)
        total = jnp.sum(weights, axis=0, keepdims=True)
        probs = (weights * (1.0 / total)).astype(jnp.bfloat16)
        values = key_rows(v_all, near, glob, rand, low_half)
        o_ref[rows, :] = pick_heads(down(probs, values), masks_f, block_len).astype(jnp.bfloat16)
        lse_ref[0, pl.ds(slot, 1), :] = top + jnp.log(total)
        return carry

    lax.fori_loop(0, half_blocks, one, 0)


def attend_back_kernel(
    sizes, blocks, head_dim, scale, group,
    table, q_ref, k_own, k_other, v_own, v_other, go_ref, lse_ref, after,
    dq_ref, own_ref, other_ref,
    k_all, v_all, dk_all, dv_all, dk_glob, dv_glob,
):
    heads, picks, rand_size, half_blocks = sizes
    block_len = k_all.shape[1]
    lanes = q_ref.shape[1]
    f32 = jnp.float32
    load_halves(k_all, k_own, k_other, half_blocks, block_len)
    load_halves(v_all, v_own, v_other, half_blocks, block_len)
    dk_all[...] = jnp.zeros_like(dk_all)
    dv_all[...] = jnp.zeros_like(dv_all)
    dk_glob[...] = jnp.zeros_like(dk_glob)
    dv_glob[...] = jnp.zeros_like(dv_glob)
    low_half = lax.broadcasted_iota(jnp.int32, (block_len, 128), 1) < head_dim
    masks = head_masks(lanes, head_dim, jnp.bfloat16)
    masks_f = head_masks(lanes, head_dim, f32)
    glob = [table[rand_size], table[rand_size + 1]]

    def add_back(grads, near, rand, into, into_glob):
        for n in range(3):
            into[near[n]] += grads[n * block_len : (n + 1) * block_len]
        for n in range(2):
            into_glob[n] += grads[(3 + n) * block_len : (4 + n) * block_len]
        for r in range(picks):
            part = grads[(5 + r) * block_len : (6 + r) * block_len]
            for c in range(lanes // 128):
                cell = part[:, c * 128 : (c + 1) * 128]
                columns = pl.ds(c * 128, 128)
                into[rand[r][2 * c], :, columns] += jnp.where(low_half, cell, 0.0)
                into[rand[r][2 * c + 1], :, columns] += jnp.where(low_half, 0.0, cell)

    def one(slot, carry):
        block, near, rand = block_places(table, slot, group, sizes)
        rows = pl.ds(pl.multiple_of(slot * block_len, block_len), block_len)
        queries = spread_heads(q_ref[rows, :], masks)
        grads_out = spread_heads(go_ref[rows, :], masks)
        keys = key_rows(k_all, near, glob, rand, low_half)
        values = key_rows(v_all, near, glob, rand, low_half)
        scores = mask_scores(across(keys, queries), block, blocks, block_len)
        probs = jnp.exp(scores - lse_ref[0, pl.ds(slot, 1), :])
        grad_probs = across(values, grads_out)
        row_dot = jnp.sum(probs * grad_probs, axis=0, keepdims=True)
        grad_scores = (probs * (grad_probs - row_dot)).astype(jnp.bfloat16)
        add_back(jnp.dot(probs.astype(jnp.bfloat16), grads_out, preferred_element_type=f32), near, rand, dv_all, dv_glob)
        add_back(jnp.dot(grad_scores, queries, preferred_element_type=f32), near, rand, dk_all, dk_glob)
        dq_ref[rows, :] = (pick_heads(down(grad_scores, keys), masks_f, block_len) * scale).astype(jnp.bfloat16)
        return carry

    lax.fori_loop(0, half_blocks, one, 0)
    for n in range(2):
        dk_all[glob[n]] += dk_glob[n]
        dv_all[glob[n]] += dv_glob[n]
    for target, start in ((own_ref, 0), (other_ref, half_blocks)):
        for n, source in enumerate((dk_all, dv_all)):
            cells = source[start : start + half_blocks].astype(jnp.bfloat16)
            target[:, n * lanes : (n + 1) * lanes] = cells.reshape(half_blocks * block_len, lanes)


def norm_parts(values):
    average = jnp.mean(values, axis=-1, keepdims=True)
    centred = values - average
    rstd = lax.rsqrt(jnp.mean(centred * centred, axis=-1, keepdims=True) + epsilon)
    return centred * rstd, rstd


def norm_back(grad, normal, rstd, gain):
    scaled = grad * gain
    first = jnp.mean(scaled, axis=-1, keepdims=True)
    second = jnp.mean(scaled * normal, axis=-1, keepdims=True)
    return rstd * (scaled - first - normal * second)


def normal_parts(values):
    size = jnp.abs(values)
    bottom = 1.0 + (0.3275911 * 0.5**0.5) * size
    t = pl.reciprocal(bottom, approx=True)
    t = t * (2.0 - bottom * t)
    bell = jnp.exp(-0.5 * values * values)
    poly = t * (0.127414796 + t * (-0.142248368 + t * (0.7107068705 + t * (-0.7265760135 + t * 0.5307027145))))
    tail = poly * bell
    cdf = jnp.where(values < 0, tail, 1.0 - tail)
    return cdf, values * bell * 0.3989422804014327


def column_sum(values):
    return jnp.sum(values, axis=0, keepdims=True)


def qkv_kernel(scale, rows_ref, gain, shift, weight, bias, q_ref, kv_ref):
    width = rows_ref.shape[1]
    normal, _ = norm_parts(rows_ref[...].astype(jnp.float32))
    normed = (normal * gain[...] + shift[...]).astype(jnp.bfloat16)

    def part(n):
        columns = slice(n * width, (n + 1) * width)
        return jnp.dot(normed, weight[:, columns], preferred_element_type=jnp.float32)

    q_ref[...] = (part(0) + bias[0:1]).astype(jnp.bfloat16) * jnp.asarray(scale, jnp.bfloat16)
    kv_ref[:, :width] = part(1).astype(jnp.bfloat16)
    kv_ref[:, width:] = (part(2) + bias[1:2]).astype(jnp.bfloat16)


def ffn_kernel(
    chunk, shards,
    place, scale, rows_ref, att_ref, cot_ref, w_out, b_out, gain, shift, w_up, b_up, w_down, b_down,
    out_ref, resid_ref, go_ref, vec_ref, vec_up_ref, keep_ref, send_ref,
    acc_up, acc_down, acc_out, stage, sems,
):
    f32, bf16 = jnp.float32, jnp.bfloat16
    step, steps = pl.program_id(0), pl.num_programs(0)
    width, wide = w_up.shape

    @pl.when(step == 0)
    def _():
        for ref in (acc_up, acc_down, acc_out, vec_ref, vec_up_ref):
            ref[...] = jnp.zeros_like(ref)

    att = att_ref[...]
    residual = rows_ref[...].astype(f32) + (jnp.dot(att, w_out[...], preferred_element_type=f32) + b_out[...])
    normal, rstd = norm_parts(residual)
    second = (normal * gain[...] + shift[...]).astype(bf16)
    upstream = cot_ref[...].astype(f32) * scale[0]
    branch = upstream.astype(bf16)
    second_t = second.T
    branch_t = branch.T
    total = residual + b_down[...]
    grad_second = jnp.zeros_like(residual)
    for first in range(0, wide, chunk):
        part = slice(first, first + chunk)
        inner = jnp.dot(second, w_up[:, part], preferred_element_type=f32) + b_up[:, part]
        grad_active = across(branch, w_down[part, :])
        cdf, slope = normal_parts(inner)
        active = (inner * cdf).astype(bf16)
        grad_inner_f = grad_active * (cdf + slope)
        grad_inner = grad_inner_f.astype(bf16)
        total = total + jnp.dot(active, w_down[part, :], preferred_element_type=f32)
        grad_second = grad_second + across(grad_inner, w_up[:, part])
        acc_down[:, part] += jnp.dot(branch_t, active, preferred_element_type=f32)
        acc_up[:, part] += jnp.dot(second_t, grad_inner, preferred_element_type=f32)
        vec_up_ref[:, part] += column_sum(grad_inner_f)
    out_ref[...] = total.astype(bf16)
    grad_resid = upstream + norm_back(grad_second, normal, rstd, gain[...])
    resid_ref[...] = grad_resid
    grad_proj = grad_resid.astype(bf16)
    go_ref[...] = across(grad_proj, w_out[...]).astype(bf16)
    acc_out[...] += jnp.dot(att.T, grad_proj, preferred_element_type=f32)
    vec_ref[0:1] += column_sum(grad_resid)
    vec_ref[1:2] += column_sum(grad_second * normal)
    vec_ref[2:3] += column_sum(grad_second)
    vec_ref[3:4] += column_sum(upstream)

    @pl.when(step == steps - 1)
    def _():
        core = place[0]
        part = width // shards
        down_part = wide // shards
        count = wide // width
        rows = stage.shape[1]
        size = rows // 4

        def copies(b, slot):
            moves = []
            for piece in range(4):
                source = stage.at[slot, pl.ds(piece * size, size)]
                for bit, target in ((0, keep_ref), (1, send_ref)):
                    moves.append((piece % 2, bit, pltpu.make_async_copy(source, target.at[b, piece // 2], sems.at[slot, piece])))
            return moves

        def act(b, slot, what):
            for parity, bit, move in copies(b, slot):
                @pl.when((parity != core) == (bit == 1))
                def _():
                    getattr(move, what)()

        for b in range(shards):
            slot = b % 2
            if b >= 2:
                act(b - 2, slot, "wait")
            for k in range(count):
                stage[slot, k * part : (k + 1) * part] = acc_up[b * part : (b + 1) * part, k * width : (k + 1) * width].astype(bf16)
            base = count * part
            half = width // 2
            for k in range(2):
                stage[slot, base : base + half, k * half : (k + 1) * half] = acc_down[
                    k * half : (k + 1) * half, b * down_part : (b + 1) * down_part
                ].astype(bf16)
            base += half
            stage[slot, base : base + part] = acc_out[b * part : (b + 1) * part, :].astype(bf16)
            stage[slot, base + part :] = jnp.zeros((rows - base - part, width), bf16)
            act(b, slot, "start")
        for b in range(shards - 2, shards):
            act(b, b % 2, "wait")


def input_grad_kernel(groups, *refs):
    f32, bf16 = jnp.float32, jnp.bfloat16
    parts = refs[: 3 * groups]
    rows_ref, resid_ref, gain, shift, weight, tok_ref, joined_ref, normed_ref, vec_ref = refs[3 * groups :]
    width = rows_ref.shape[1]
    lanes = width // groups

    @pl.when(pl.program_id(0) == 0)
    def _():
        vec_ref[...] = jnp.zeros_like(vec_ref)

    for g in range(groups):
        dq, own, other = parts[3 * g : 3 * g + 3]
        columns = slice(g * lanes, (g + 1) * lanes)
        joined_ref[:, columns] = dq[...]
        both = (own[...].astype(f32) + other[...].astype(f32)).astype(bf16)
        joined_ref[:, width + g * lanes : width + (g + 1) * lanes] = both[:, :lanes]
        joined_ref[:, 2 * width + g * lanes : 2 * width + (g + 1) * lanes] = both[:, lanes:]
        vec_ref[0:1, columns] += column_sum(dq[...].astype(f32))
        vec_ref[1:2, columns] += column_sum(both[:, lanes:].astype(f32))
    grad = across(joined_ref[...], weight[...])
    normal, rstd = norm_parts(rows_ref[...].astype(f32))
    normed_ref[...] = (normal * gain[...] + shift[...]).astype(bf16)
    vec_ref[2:3] += column_sum(grad * normal)
    vec_ref[3:4] += column_sum(grad)
    tok_ref[...] = (resid_ref[...] + norm_back(grad, normal, rstd, gain[...])).astype(bf16)


def weight_grad_kernel(normed_ref, joined_ref, out_ref, turned):
    @pl.when(pl.program_id(0) == 0)
    def _():
        turned[...] = normed_ref[...].T

    width = normed_ref.shape[1]
    shards = out_ref.shape[0]
    full = jnp.dot(turned[...], joined_ref[...], preferred_element_type=jnp.float32).astype(jnp.bfloat16)
    out_ref[...] = full.reshape(shards, width // shards, width)


def general_body(
    tokens,
    cotangent,
    w_qkv,
    b_q,
    b_v,
    w_out,
    b_out,
    gain_one,
    shift_one,
    gain_two,
    shift_two,
    w_up,
    b_up,
    w_down,
    b_down,
    rand_owner,
    rand_sub,
    global_ids,
    species,
):
    blk_count = lax.axis_size("blk")
    blk_pos = lax.axis_index("blk")
    win_pos = lax.axis_index("win")
    windows, length, model_width = tokens.shape
    blocks = rand_owner.shape[1]
    heads = rand_owner.shape[2]
    picks = rand_owner.shape[3]
    glob_count = global_ids.shape[1]
    own_blocks = blocks // blk_count
    block_len = length // own_blocks
    head_dim = model_width // heads
    pair_width = 2 * head_dim
    all_rows = windows * length
    key_count = 3 + glob_count + picks
    per_device = own_blocks * heads * picks
    slot_cap = max(2, 2 * per_device // blk_count)
    score_scale = head_dim ** (-0.5)
    f32 = jnp.float32
    bf16 = jnp.bfloat16
    tokens_f = tokens.reshape(all_rows, model_width).astype(f32)
    normed_f, norm_one_pull = jax.vjp(layer_norm, tokens_f, gain_one, shift_one)
    normed = normed_f.astype(bf16)
    joined = jnp.dot(normed, w_qkv, preferred_element_type=f32)
    query_vals = (joined[:, :model_width] + b_q).astype(bf16)
    key_vals = joined[:, model_width : 2 * model_width].astype(bf16)
    value_vals = (joined[:, 2 * model_width :] + b_v).astype(bf16)

    def to_heads(tensor):
        return tensor.reshape(windows, own_blocks, block_len, heads, head_dim).transpose(
            0, 1, 3, 2, 4
        )

    def from_heads(tensor):
        return tensor.transpose(0, 1, 3, 2, 4).reshape(all_rows, model_width)

    query_heads = to_heads(query_vals)
    local_pairs = jnp.concatenate([to_heads(key_vals), to_heads(value_vals)], axis=-1)
    rimmed = padded(local_pairs, (("blk", 1),), 1)
    block_ids = blk_pos * own_blocks + jnp.arange(own_blocks, dtype=jnp.int32)
    owned_glob = (global_ids[:, :, None] == block_ids[None, None, :]).astype(bf16)
    glob_terms = jnp.einsum("wgb,wbhsc->wghsc", owned_glob, local_pairs, preferred_element_type=f32)
    glob_pairs = lax.psum(glob_terms.astype(jnp.bfloat16), "blk").astype(jnp.float32).astype(bf16)
    owner_rows = rand_owner.reshape(windows, blk_count, per_device)
    sub_rows = rand_sub.reshape(windows, blk_count, per_device)
    owner_hits = (owner_rows[..., None] == jnp.arange(blk_count, dtype=jnp.int32)).astype(jnp.int32)
    slot_rows = jnp.sum(owner_hits * (jnp.cumsum(owner_hits, axis=2) - 1), axis=-1)
    my_owner = lax.dynamic_index_in_dim(owner_rows, blk_pos, 1, keepdims=False)
    my_slot = lax.dynamic_index_in_dim(slot_rows, blk_pos, 1, keepdims=False)
    fetch_index = my_owner * slot_cap + my_slot
    head_of_row = jnp.arange(per_device, dtype=jnp.int32) // picks % heads
    source_rows = sub_rows * heads + head_of_row[None, None, :]
    requester = jnp.arange(blk_count, dtype=jnp.int32)[None, :, None]
    target_rows = jnp.where(
        owner_rows == blk_pos, requester * slot_cap + slot_rows, blk_count * slot_cap
    )
    send_table = jnp.full((windows, blk_count * slot_cap + 1), own_blocks * heads, jnp.int32)
    send_table = jax.vmap(set_rows)(
        send_table, target_rows.reshape(windows, -1), source_rows.reshape(windows, -1)
    )[:, : blk_count * slot_cap]
    flat_pairs = jnp.concatenate(
        [
            local_pairs.reshape(windows, own_blocks * heads, block_len, pair_width),
            jnp.zeros((windows, 1, block_len, pair_width), bf16),
        ],
        axis=1,
    )
    outgoing = jax.vmap(take_rows)(flat_pairs, send_table).reshape(
        windows, blk_count, slot_cap, block_len, pair_width
    )
    incoming = lax.all_to_all(outgoing, "blk", split_axis=1, concat_axis=1, tiled=True).reshape(
        windows, blk_count * slot_cap, block_len, pair_width
    )
    rand_pairs = jax.vmap(take_rows)(incoming, fetch_index).reshape(
        windows, own_blocks, heads, picks, block_len, pair_width
    )
    near_pairs = jnp.stack(
        [rimmed[:, 0:own_blocks], rimmed[:, 1 : own_blocks + 1], rimmed[:, 2 : own_blocks + 2]],
        axis=3,
    )
    far_pairs = jnp.broadcast_to(
        glob_pairs.transpose(0, 2, 1, 3, 4)[:, None],
        (windows, own_blocks, heads, glob_count, block_len, pair_width),
    )
    gathered_keys = jnp.concatenate([near_pairs, far_pairs, rand_pairs], axis=3).reshape(
        windows, own_blocks, heads, key_count * block_len, pair_width
    )
    set_keys = gathered_keys[..., :head_dim]
    set_values = gathered_keys[..., head_dim:]
    block_flags = jnp.concatenate(
        [
            (block_ids > 0)[:, None],
            jnp.ones((own_blocks, 1), jnp.bool_),
            (block_ids < blocks - 1)[:, None],
            jnp.ones((own_blocks, glob_count + picks), jnp.bool_),
        ],
        axis=1,
    )
    key_valid = jnp.repeat(block_flags, block_len, axis=1)[None, :, None, None, :]

    def score_block():
        raw_scores = (
            jnp.einsum("wbhqe,wbhke->wbhqk", query_heads, set_keys, preferred_element_type=f32)
            * score_scale
        )
        return jnp.where(key_valid, raw_scores, masked_score)

    score_matrix = score_block()
    top_score = jnp.max(score_matrix, axis=-1, keepdims=True)
    log_total = top_score + jnp.log(
        jnp.sum(jnp.exp(score_matrix - top_score), axis=-1, keepdims=True)
    )
    probs_low = jnp.exp(score_matrix - log_total).astype(bf16)
    attended = jnp.einsum(
        "wbhqk,wbhke->wbhqe", probs_low, set_values, preferred_element_type=f32
    ).astype(bf16)
    merged = from_heads(attended)
    residual = tokens_f + (jnp.dot(merged, w_out, preferred_element_type=f32) + b_out)
    second_f, norm_two_pull = jax.vjp(layer_norm, residual, gain_two, shift_two)
    second = second_f.astype(bf16)
    inner_f = jnp.dot(second, w_up, preferred_element_type=f32) + b_up
    active_f, gelu_pull = jax.vjp(partial(jax.nn.gelu, approximate=False), inner_f)
    active = active_f.astype(bf16)
    output = residual + (jnp.dot(active, w_down, preferred_element_type=f32) + b_down)
    species_count = jnp.sum(
        (species[:, None] == jnp.arange(SPECIES, dtype=jnp.int32)[None, :]).astype(f32), axis=0
    )
    my_species = lax.dynamic_slice_in_dim(species, win_pos * windows, windows)
    own_count = jnp.sum(
        (my_species[:, None] == jnp.arange(SPECIES, dtype=jnp.int32)[None, :]).astype(f32)
        * species_count[None, :],
        axis=1,
    )
    window_scale = jnp.sqrt(species.shape[0] / (SPECIES * own_count))
    upstream = (cotangent.astype(f32) * window_scale[:, None, None]).reshape(all_rows, model_width)
    grad_branch = upstream.astype(bf16)
    grad_w_down = jnp.einsum("tf,td->fd", active, grad_branch, preferred_element_type=f32)
    grad_b_down = jnp.sum(grad_branch, axis=0, dtype=f32)
    grad_active = jnp.einsum("td,fd->tf", grad_branch, w_down, preferred_element_type=f32)
    grad_inner = gelu_pull(grad_active)[0].astype(bf16)
    grad_w_up = jnp.einsum("td,tf->df", second, grad_inner, preferred_element_type=f32)
    grad_b_up = jnp.sum(grad_inner, axis=0, dtype=f32)
    grad_second = jnp.einsum("tf,df->td", grad_inner, w_up, preferred_element_type=f32)
    grad_resid_norm, grad_gain_two, grad_shift_two = norm_two_pull(grad_second)
    grad_resid = upstream + grad_resid_norm
    grad_proj = grad_resid.astype(bf16)
    grad_w_out = jnp.einsum("ti,to->io", merged, grad_proj, preferred_element_type=f32)
    grad_b_out = jnp.sum(grad_proj, axis=0, dtype=f32)
    grad_attended = to_heads(
        jnp.einsum("to,io->ti", grad_proj, w_out, preferred_element_type=f32).astype(bf16)
    )
    probs_full = jnp.exp(score_block() - log_total)
    grad_probs = jnp.einsum(
        "wbhqe,wbhke->wbhqk", grad_attended, set_values, preferred_element_type=f32
    )
    grad_set_values = jnp.einsum(
        "wbhqk,wbhqe->wbhke", probs_full.astype(bf16), grad_attended, preferred_element_type=f32
    )
    row_dot = jnp.sum(probs_full * grad_probs, axis=-1, keepdims=True)
    grad_scores = (probs_full * (grad_probs - row_dot)).astype(bf16)
    grad_query = (
        jnp.einsum("wbhqk,wbhke->wbhqe", grad_scores, set_keys, preferred_element_type=f32)
        * score_scale
    )
    grad_set_keys = (
        jnp.einsum("wbhqk,wbhqe->wbhke", grad_scores, query_heads, preferred_element_type=f32)
        * score_scale
    )
    grad_set = jnp.concatenate([grad_set_keys, grad_set_values], axis=-1).reshape(
        windows, own_blocks, heads, key_count, block_len, pair_width
    )
    extended = (
        jnp.pad(grad_set[:, :, :, 1], ((0, 0), (1, 1), (0, 0), (0, 0), (0, 0)))
        + jnp.pad(grad_set[:, :, :, 0], ((0, 0), (0, 2), (0, 0), (0, 0), (0, 0)))
        + jnp.pad(grad_set[:, :, :, 2], ((0, 0), (2, 0), (0, 0), (0, 0), (0, 0)))
    )
    edge_grads = jnp.concatenate([extended[:, :1], extended[:, own_blocks + 1 :]], axis=1)
    edge_back = padded(edge_grads.astype(jnp.bfloat16), (("blk", 1),), 1).astype(edge_grads.dtype)
    pair_grad = extended[:, 1 : own_blocks + 1]
    pair_grad = pair_grad.at[:, 0].add(edge_back[:, 0]).at[:, own_blocks - 1].add(edge_back[:, 3])
    glob_grad = jnp.sum(grad_set[:, :, :, 3 : 3 + glob_count], axis=1).transpose(0, 2, 1, 3, 4)
    glob_total = lax.psum(glob_grad.astype(jnp.bfloat16), "blk").astype(jnp.float32)
    pair_grad = pair_grad + jnp.einsum(
        "wgb,wghsc->wbhsc", owned_glob.astype(f32), glob_total, precision=lax.Precision.HIGHEST
    )
    rand_grad = grad_set[:, :, :, 3 + glob_count :].reshape(
        windows, per_device, block_len, pair_width
    )
    back_out = jax.vmap(add_rows)(
        jnp.zeros((windows, blk_count * slot_cap, block_len, pair_width), f32),
        fetch_index,
        rand_grad,
    )
    back_in = lax.all_to_all(
        back_out.reshape(windows, blk_count, slot_cap, block_len, pair_width).astype(jnp.bfloat16),
        "blk",
        split_axis=1,
        concat_axis=1,
        tiled=True,
    ).astype(jnp.float32)
    owner_sum = jax.vmap(add_rows)(
        jnp.zeros((windows, own_blocks * heads + 1, block_len, pair_width), f32),
        send_table,
        back_in.reshape(windows, blk_count * slot_cap, block_len, pair_width),
    )
    pair_grad = pair_grad + owner_sum[:, : own_blocks * heads].reshape(
        windows, own_blocks, heads, block_len, pair_width
    )
    grad_keys = from_heads(pair_grad[..., :head_dim].astype(bf16))
    grad_values = from_heads(pair_grad[..., head_dim:].astype(bf16))
    grad_joined = jnp.concatenate(
        [from_heads(grad_query.astype(bf16)), grad_keys, grad_values], axis=1
    )
    grad_w_qkv = jnp.einsum("td,tc->dc", normed, grad_joined, preferred_element_type=f32)
    grad_b_q = jnp.sum(grad_joined[:, :model_width], axis=0, dtype=f32)
    grad_b_v = jnp.sum(grad_joined[:, 2 * model_width :], axis=0, dtype=f32)
    grad_normed = jnp.einsum("tc,dc->td", grad_joined, w_qkv, preferred_element_type=f32)
    grad_tok_norm, grad_gain_one, grad_shift_one = norm_one_pull(grad_normed)
    grad_tokens = (grad_resid + grad_tok_norm).astype(bf16).reshape(windows, length, model_width)
    local_grads = (
        grad_w_qkv,
        grad_b_q,
        grad_b_v,
        grad_w_out,
        grad_b_out,
        grad_gain_one,
        grad_shift_one,
        grad_gain_two,
        grad_shift_two,
        grad_w_up,
        grad_b_up,
        grad_w_down,
        grad_b_down,
    )
    packed_grads = jnp.concatenate(
        [grad_item.reshape(blk_count, -1) for grad_item in local_grads], axis=1
    )
    total_cols = packed_grads.shape[1]
    win_count = lax.axis_size("win")
    pad_cols = -total_cols % win_count
    shard_sum = lax.psum_scatter(
        packed_grads.astype(jnp.bfloat16), "blk", scatter_dimension=0, tiled=True
    ).astype(jnp.float32)
    split_shard = jnp.pad(shard_sum, ((0, 0), (0, pad_cols))).reshape(win_count, -1)
    group_piece = lax.psum_scatter(
        split_shard.astype(jnp.bfloat16), "win", scatter_dimension=0, tiled=True
    ).astype(jnp.float32)
    summed = (
        lax.all_gather(group_piece.astype(jnp.bfloat16), "win", axis=0, tiled=True)
        .astype(group_piece.dtype)
        .reshape(1, -1)[:, :total_cols]
    )
    shards = []
    offset = 0
    for grad_item in local_grads:
        entry_count = grad_item.size // blk_count
        shards.append(
            summed[0, offset : offset + entry_count].reshape(
                (grad_item.shape[0] // blk_count,) + grad_item.shape[1:]
            )
        )
        offset = offset + entry_count
    out_tokens = output.astype(bf16).reshape(windows, length, model_width)
    return (
        out_tokens,
        grad_tokens,
        shards[0],
        shards[1],
        shards[2],
        shards[3],
        shards[4],
        shards[5],
        shards[6],
        shards[7],
        shards[8],
        shards[9],
        shards[10],
        shards[11],
        shards[12],
    )


def layer_step(*arguments):
    windows = arguments[0].shape[0]
    paired = lax.axis_size("blk") == 2 * windows and lax.axis_size("win") % 2 == 0
    return (paired_body if paired else general_body)(*arguments)


def paired_body(
    tokens,
    cotangent,
    w_qkv,
    b_q,
    b_v,
    w_out,
    b_out,
    gain_one,
    shift_one,
    gain_two,
    shift_two,
    w_up,
    b_up,
    w_down,
    b_down,
    rand_owner,
    rand_sub,
    global_ids,
    species,
):
    f32 = jnp.float32
    bf16 = jnp.bfloat16
    win_count = lax.axis_size("win")
    blk_count = lax.axis_size("blk")
    win_pos = lax.axis_index("win")
    blk_pos = lax.axis_index("blk")
    layers, length, width = tokens.shape
    core, layer, side = win_pos % 2, blk_pos // 2, blk_pos % 2
    blocks, heads, picks = rand_owner.shape[1:]
    own_blocks = blocks // blk_count
    half_blocks = blocks // 2
    block_len = length // own_blocks
    head_dim = width // heads
    all_rows = layers * length
    lanes = HEADS_PER_GROUP * head_dim
    groups = heads // HEADS_PER_GROUP
    score_scale = head_dim ** (-0.5)

    def regroup(value):
        parts = []
        for step in range(layers):
            part = lax.dynamic_index_in_dim(value, (layer + step) % layers, 0, keepdims=False)
            parts.append(lax.ppermute(part, ("win", "blk"), regroup_pairs(win_count, layers, step)))
        return jnp.concatenate(parts, axis=0)

    def regroup_back(value):
        result = jnp.zeros((layers, length, width), value.dtype)
        for step in range(layers):
            pairs = [(b, a) for a, b in regroup_pairs(win_count, layers, step)]
            part = lax.ppermute(value[step * length : (step + 1) * length], ("win", "blk"), pairs)
            result = lax.dynamic_update_index_in_dim(result, part, (layer + step) % layers, 0)
        return result

    rows_in = regroup(tokens)
    cot_in = regroup(cotangent)

    rand_size = blocks * heads * picks
    named = jnp.concatenate(
        [
            lax.dynamic_index_in_dim((rand_owner * own_blocks + rand_sub).reshape(layers, rand_size), layer, 0, keepdims=False),
            lax.dynamic_index_in_dim(global_ids, layer, 0, keepdims=False),
        ]
    )
    named = jnp.where(side == core, named, swap(named, 1, 0))

    def place_of(block):
        owner = block // own_blocks
        half = jnp.where(owner % 2 == core, 0, half_blocks)
        return half + ((layer - owner // 2) % layers) * own_blocks + block % own_blocks

    slot = jnp.arange(half_blocks, dtype=jnp.int32)
    slot_block = (((layer - slot // own_blocks) % layers) * 2 + core) * own_blocks + slot % own_blocks
    table = jnp.concatenate(
        [
            place_of(named),
            slot_block,
            place_of(jnp.maximum(slot_block - 1, 0)),
            place_of(jnp.minimum(slot_block + 1, blocks - 1)),
        ]
    )
    sizes = (heads, picks, rand_size, half_blocks)

    tile = min(512, all_rows)

    def by_rows(columns):
        return pl.BlockSpec((tile, columns), lambda i: (i, 0))

    def whole(*shape, once=True):
        mode = pl.Buffered(1) if once else None
        return pl.BlockSpec(shape, lambda i: (0,) * len(shape), pipeline_mode=mode)

    scalars = pl.BlockSpec(memory_space=pltpu.SMEM)
    wide = w_up.shape[1]
    params = pltpu.CompilerParams(vmem_limit_bytes=60 << 20)
    row = lambda vector: vector.reshape(1, -1)
    query, key_value = pl.pallas_call(
        partial(qkv_kernel, score_scale),
        grid=(all_rows // tile,),
        in_specs=[by_rows(width), whole(1, width), whole(1, width), whole(width, 3 * width), whole(2, width)],
        out_specs=[by_rows(width), by_rows(2 * width)],
        out_shape=[jax.ShapeDtypeStruct((all_rows, width), bf16), jax.ShapeDtypeStruct((all_rows, 2 * width), bf16)],
        compiler_params=params,
        cost_estimate=pl.CostEstimate(flops=6 * all_rows * width * width, bytes_accessed=16 << 20, transcendentals=0),
        name="qkv",
    )(rows_in, row(gain_one), row(shift_one), w_qkv, jnp.stack([b_q, b_v]))
    key_value_other = swap(key_value, 1, 0)

    def lane_block(first):
        return pl.BlockSpec((all_rows, lanes), lambda g, t: (0, first + g))

    store = pltpu.VMEM((blocks, block_len, lanes), bf16)
    attended, log_total = pl.pallas_call(
        partial(attend_kernel, sizes, blocks, head_dim),
        grid_spec=pltpu.PrefetchScalarGridSpec(
            num_scalar_prefetch=1,
            grid=(groups,),
            in_specs=[lane_block(0), lane_block(0), lane_block(0), lane_block(groups), lane_block(groups)],
            out_specs=[lane_block(0), pl.BlockSpec((1, half_blocks, lanes), lambda g, t: (g, 0, 0))],
            scratch_shapes=[store, store],
        ),
        out_shape=[
            jax.ShapeDtypeStruct((all_rows, width), bf16),
            jax.ShapeDtypeStruct((groups, half_blocks, lanes), f32),
        ],
        compiler_params=pltpu.CompilerParams(vmem_limit_bytes=56 << 20),
        cost_estimate=pl.CostEstimate(flops=4 * all_rows * 512 * width, bytes_accessed=25 << 20, transcendentals=all_rows * 512 * heads),
        name="attend",
    )(table, query, key_value, key_value_other, key_value, key_value_other)

    species_count = jnp.sum(
        (species[:, None] == jnp.arange(SPECIES, dtype=jnp.int32)[None, :]).astype(f32), axis=0
    )
    my_window = ((win_pos // 2) * 2 + side) * layers + layer
    my_species = lax.dynamic_index_in_dim(species, my_window, 0, keepdims=False)
    own_count = jnp.sum(
        (my_species == jnp.arange(SPECIES, dtype=jnp.int32)).astype(f32) * species_count
    )
    window_scale = jnp.sqrt(species.shape[0] / (SPECIES * own_count))
    payload = 2 * wide // blk_count + width // blk_count
    payload += -payload % (16 * win_count)
    stays = jax.ShapeDtypeStruct((blk_count, win_count // 2, payload // win_count, width), bf16)
    any_place = pl.BlockSpec(memory_space=pl.ANY)
    output, grad_resid, grad_attended, vec_two, vec_up, early_keep, early_send = pl.pallas_call(
        partial(ffn_kernel, 512, blk_count),
        grid=(all_rows // tile,),
        in_specs=[
            scalars, scalars, by_rows(width), by_rows(width), by_rows(width), whole(width, width), whole(1, width), whole(1, width),
            whole(1, width), whole(width, wide), whole(1, wide), whole(wide, width), whole(1, width),
        ],
        out_specs=[by_rows(width), by_rows(width), by_rows(width), whole(4, width), whole(1, wide), any_place, any_place],
        out_shape=[
            jax.ShapeDtypeStruct((all_rows, width), bf16),
            jax.ShapeDtypeStruct((all_rows, width), f32),
            jax.ShapeDtypeStruct((all_rows, width), bf16),
            jax.ShapeDtypeStruct((4, width), f32),
            jax.ShapeDtypeStruct((1, wide), f32),
            stays,
            stays,
        ],
        scratch_shapes=[
            pltpu.VMEM((width, wide), f32),
            pltpu.VMEM((width, wide), f32),
            pltpu.VMEM((width, width), f32),
            pltpu.VMEM((2, payload, width), bf16),
            pltpu.SemaphoreType.DMA((2, 4)),
        ],
        compiler_params=params,
        cost_estimate=pl.CostEstimate(flops=6 * all_rows * width * (2 * wide + width), bytes_accessed=60 << 20, transcendentals=all_rows * wide),
        name="ffn",
    )(
        core.reshape(1), window_scale.reshape(1), rows_in, attended, cot_in, w_out, row(b_out), row(gain_two), row(shift_two),
        w_up, row(b_up), w_down, row(b_down),
    )
    out_tokens = regroup_back(output)

    grad_parts = []
    early_other = swap(early_send, 1, 0)
    for group in range(groups):
        after = early_other if group == 1 else table
        def column(first):
            return pl.BlockSpec((all_rows, lanes), lambda g, t: (0, first))

        def full(columns):
            return pl.BlockSpec((all_rows, columns), lambda g, t: (0, 0))

        grad_store = pltpu.VMEM((blocks, block_len, lanes), f32)
        glob_store = pltpu.VMEM((2, block_len, lanes), f32)
        dq, own, other = pl.pallas_call(
            partial(attend_back_kernel, sizes, blocks, head_dim, score_scale, group),
            grid_spec=pltpu.PrefetchScalarGridSpec(
                num_scalar_prefetch=1,
                grid=(1,),
                in_specs=[
                    column(group), column(group), column(group), column(groups + group), column(groups + group), column(group),
                    pl.BlockSpec((1, half_blocks, lanes), lambda g, t: (group, 0, 0)), any_place,
                ],
                out_specs=[full(lanes), full(2 * lanes), full(2 * lanes)],
                scratch_shapes=[store, store, grad_store, grad_store, glob_store, glob_store],
            ),
            out_shape=[jax.ShapeDtypeStruct((all_rows, n * lanes), bf16) for n in (1, 2, 2)],
            compiler_params=params,
            cost_estimate=pl.CostEstimate(flops=10 * all_rows * 512 * lanes, bytes_accessed=12 << 20, transcendentals=all_rows * 512 * HEADS_PER_GROUP),
            name="attend_back",
        )(table, query, key_value, key_value_other, key_value, key_value_other, grad_attended, log_total, after)
        grad_parts += [dq, own, swap(other, 1, 0)]

    grad_tokens, grad_joined, normed, vec_one = pl.pallas_call(
        partial(input_grad_kernel, groups),
        grid=(all_rows // tile,),
        in_specs=[by_rows(p.shape[1]) for p in grad_parts]
        + [by_rows(width), by_rows(width), whole(1, width), whole(1, width), whole(width, 3 * width)],
        out_specs=[by_rows(width), by_rows(3 * width), by_rows(width), whole(4, width)],
        out_shape=[
            jax.ShapeDtypeStruct((all_rows, width), bf16),
            jax.ShapeDtypeStruct((all_rows, 3 * width), bf16),
            jax.ShapeDtypeStruct((all_rows, width), bf16),
            jax.ShapeDtypeStruct((4, width), f32),
        ],
        compiler_params=params,
        cost_estimate=pl.CostEstimate(flops=6 * all_rows * width * width, bytes_accessed=50 << 20, transcendentals=0),
        name="input_grad",
    )(*grad_parts, rows_in, grad_resid, row(gain_one), row(shift_one), w_qkv)
    grad_tokens = regroup_back(grad_tokens)
    part = width // blk_count
    late_rows = 3 * part + 32
    late_rows += -late_rows % (16 * win_count)
    late_cells = pl.pallas_call(
        weight_grad_kernel,
        grid=(3,),
        in_specs=[whole(all_rows, width), pl.BlockSpec((all_rows, width), lambda i: (0, i))],
        out_specs=pl.BlockSpec((blk_count, part, width), lambda i: (0, i, 0)),
        out_shape=jax.ShapeDtypeStruct((blk_count, late_rows, width), bf16),
        scratch_shapes=[pltpu.VMEM((width, all_rows), bf16)],
        compiler_params=params,
        cost_estimate=pl.CostEstimate(flops=6 * all_rows * width * width, bytes_accessed=20 << 20, transcendentals=0),
        name="weight_grad",
    )(normed, grad_joined)
    vec_rows = jnp.concatenate(
        [vec_two.reshape(4, blk_count, part), vec_one.reshape(4, blk_count, part)], axis=0
    ).transpose(1, 0, 2).reshape(blk_count, 8 * part)
    vec_rows = jnp.concatenate([vec_rows, vec_up.reshape(blk_count, wide // blk_count)], axis=1)
    vec_rows = jnp.pad(vec_rows, ((0, 0), (0, -vec_rows.shape[1] % width))).reshape(blk_count, -1, width)
    vec_rows = jnp.pad(vec_rows, ((0, 0), (0, late_rows - 3 * part - vec_rows.shape[1]), (0, 0))).astype(bf16)
    late_cells = lax.dynamic_update_slice(late_cells, vec_rows, (0, 3 * part, 0))

    def add_low(keep, other):
        return (keep.astype(f32) + other.astype(f32)).astype(bf16)

    def reduce_shards(cells):
        def halve(cells, axis, bit, win_bit, blk_bit):
            keep = lax.dynamic_index_in_dim(cells, bit, axis, keepdims=False)
            send = lax.dynamic_index_in_dim(cells, 1 - bit, axis, keepdims=False)
            return add_low(keep, swap(send, win_bit, blk_bit))

        cells = cells.reshape((layers, 2) + cells.shape[1:])
        cells = halve(cells, 1, side, 0, 1)
        hop = 2
        while cells.shape[1] > 1:
            count = cells.shape[1]
            cells = cells.reshape((layers, count // 2, 2) + cells.shape[2:])
            cells = halve(cells, 2, (win_pos // hop) % 2, hop, 0)
            hop *= 2
        cells = cells[:, 0]
        hop = 1
        while cells.shape[0] > 1:
            cells = cells.reshape((cells.shape[0] // 2, 2) + cells.shape[1:])
            cells = halve(cells, 1, (layer // hop) % 2, 0, 2 * hop)
            hop *= 2
        return lax.all_gather(cells[0], "win", axis=0, tiled=True)

    late_cells = late_cells.reshape(blk_count, win_count // 2, 2, late_rows // win_count, width)
    late_keep = lax.dynamic_index_in_dim(late_cells, core, 2, keepdims=False)
    late_send = lax.dynamic_index_in_dim(late_cells, 1 - core, 2, keepdims=False)
    early = reduce_shards(add_low(early_keep, early_other)).astype(f32)
    late = reduce_shards(add_low(late_keep, swap(late_send, 1, 0))).astype(f32)

    def rows_again(rows, count):
        return rows.reshape(count, -1, width).transpose(1, 0, 2).reshape(-1, count * width)

    count = wide // width
    half = width // 2
    done_up = rows_again(early[: count * part], count)
    done_down = early[count * part : count * part + half].reshape(half, 2, wide // blk_count).transpose(2, 1, 0).reshape(-1, width)
    done_out = early[count * part + half : (count + 1) * part + half]
    done_qkv = rows_again(late[: 3 * part], 3)
    vec = late[3 * part :].reshape(-1)
    piece = lambda n: vec[n * part : (n + 1) * part]
    return (
        out_tokens,
        grad_tokens,
        done_qkv,
        piece(4),
        piece(5),
        done_out,
        piece(0),
        piece(6),
        piece(7),
        piece(1),
        piece(2),
        done_up,
        vec[8 * part : 8 * part + wide // blk_count],
        done_down,
        piece(3),
    )


def solution(mesh):
    placed = (
        P("win", "blk", None),
        P("win", "blk", None),
        P(),
        P(),
        P(),
        P(),
        P(),
        P(),
        P(),
        P(),
        P(),
        P(),
        P(),
        P(),
        P(),
        P("win", None, None, None),
        P("win", None, None, None),
        P("win", None),
        P(),
    )
    return jax.shard_map(
        layer_step,
        mesh=mesh,
        in_specs=placed,
        out_specs=(
            P("win", "blk", None),
            P("win", "blk", None),
            P("blk", None),
            P("blk"),
            P("blk"),
            P("blk", None),
            P("blk"),
            P("blk"),
            P("blk"),
            P("blk"),
            P("blk"),
            P("blk", None),
            P("blk"),
            P("blk", None),
            P("blk"),
        ),
        check_vma=False,
    )
```

```python
from functools import partial

import jax
import jax.numpy as jnp
from jax import lax
from jax.experimental import pallas as pl
from jax.experimental.pallas import tpu as pltpu
from jax.sharding import PartitionSpec as P

SPECIES = 4


epsilon = 1e-05
masked_score = -1000000000.0


def padded(cells, sides, width):
    for axis, dim in sides:
        count = lax.axis_size(axis)
        ends = count - 1
        head = lax.slice_in_dim(cells, 0, width, axis=dim)
        tail = lax.slice_in_dim(cells, cells.shape[dim] - width, cells.shape[dim], axis=dim)
        cells = jnp.concatenate(
            [
                lax.ppermute(tail, axis, [(i, (i + 1) % count) for i in range(ends)]),
                cells,
                lax.ppermute(head, axis, [((i + 1) % count, i) for i in range(ends)]),
            ],
            axis=dim,
        )
    return cells


def layer_norm(values, norm_gain, norm_shift):
    average = jnp.mean(values, axis=-1, keepdims=True)
    centred = values - average
    variance = jnp.mean(centred * centred, axis=-1, keepdims=True)
    return centred * lax.rsqrt(variance + epsilon) * norm_gain + norm_shift


def take_rows(source, index_rows):
    return jnp.take(source, index_rows, axis=0)


def add_rows(base, index_rows, update):
    return base.at[index_rows].add(update)


def set_rows(base, index_rows, update):
    return base.at[index_rows].set(update)


HEADS_PER_GROUP = 4


def regroup_pairs(win_count, layers, step):
    pairs = []
    for win in range(win_count):
        for blk in range(2 * layers):
            layer, side = blk // 2, blk % 2
            target = ((layer + step) % layers) * 2 + win % 2
            pairs.append((win * 2 * layers + blk, ((win // 2) * 2 + side) * 2 * layers + target))
    return pairs


def flip_pairs(win_count, blk_count, win_bit, blk_bit):
    return [
        (win * blk_count + blk, (win ^ win_bit) * blk_count + (blk ^ blk_bit))
        for win in range(win_count)
        for blk in range(blk_count)
    ]


def swap(value, win_bit, blk_bit):
    pairs = flip_pairs(lax.axis_size("win"), lax.axis_size("blk"), win_bit, blk_bit)
    return lax.ppermute(value, ("win", "blk"), pairs)


def head_masks(lanes, head_dim, dtype):
    lane = lax.broadcasted_iota(jnp.int32, (1, lanes), 1)
    return [(lane // head_dim == h).astype(dtype) for h in range(lanes // head_dim)]


def block_places(table, slot, group, sizes):
    heads, picks, rand_size, half_blocks = sizes
    block = table[rand_size + 2 + slot]
    near = [table[rand_size + 2 + half_blocks + slot], slot, table[rand_size + 2 + 2 * half_blocks + slot]]
    row = (block * heads + group * HEADS_PER_GROUP) * picks
    rand = [[table[row + h * picks + r] for h in range(HEADS_PER_GROUP)] for r in range(picks)]
    return block, near, rand


def spread_heads(rows, masks):
    return jnp.concatenate([rows * m for m in masks], axis=0)


def pick_heads(square, masks, height):
    total = square[0:height] * masks[0]
    for h in range(1, len(masks)):
        total = total + square[h * height : (h + 1) * height] * masks[h]
    return total


def key_rows(source, near, glob, rand, low_half):
    parts = [source[p] for p in near] + [source[p] for p in glob]
    for places in rand:
        columns = []
        for c in range(len(places) // 2):
            low = source[places[2 * c], :, c * 128 : (c + 1) * 128]
            high = source[places[2 * c + 1], :, c * 128 : (c + 1) * 128]
            columns.append(jnp.where(low_half, low, high))
        parts.append(jnp.concatenate(columns, axis=1))
    return jnp.concatenate(parts, axis=0)


def mask_scores(scores, block, blocks, block_len):
    first = jnp.where(block > 0, scores[:block_len], masked_score)
    last = jnp.where(block < blocks - 1, scores[2 * block_len : 3 * block_len], masked_score)
    return jnp.concatenate([first, scores[block_len : 2 * block_len], last, scores[3 * block_len :]], axis=0)


def across(left, right):
    return lax.dot_general(left, right, (((1,), (1,)), ((), ())), preferred_element_type=jnp.float32)


def down(left, right):
    return lax.dot_general(left, right, (((0,), (0,)), ((), ())), preferred_element_type=jnp.float32)


def load_halves(target, own, other, half_blocks, block_len):
    lanes = own.shape[-1]
    target[0:half_blocks] = own[...].reshape(half_blocks, block_len, lanes)
    target[half_blocks:] = other[...].reshape(half_blocks, block_len, lanes)


def attend_kernel(sizes, blocks, head_dim, table, q_ref, k_own, k_other, v_own, v_other, o_ref, lse_ref, k_all, v_all):
    heads, picks, rand_size, half_blocks = sizes
    block_len = k_all.shape[1]
    lanes = q_ref.shape[1]
    group = pl.program_id(0)
    load_halves(k_all, k_own, k_other, half_blocks, block_len)
    load_halves(v_all, v_own, v_other, half_blocks, block_len)
    low_half = lax.broadcasted_iota(jnp.int32, (block_len, 128), 1) < head_dim
    masks = head_masks(lanes, head_dim, jnp.bfloat16)
    masks_f = head_masks(lanes, head_dim, jnp.float32)
    glob = [table[rand_size], table[rand_size + 1]]

    def one(slot, carry):
        block, near, rand = block_places(table, slot, group, sizes)
        rows = pl.ds(pl.multiple_of(slot * block_len, block_len), block_len)
        queries = spread_heads(q_ref[rows, :], masks)
        keys = key_rows(k_all, near, glob, rand, low_half)
        scores = mask_scores(across(keys, queries), block, blocks, block_len)
        top = jnp.max(scores, axis=0, keepdims=True)
        weights = jnp.exp(scores - top)
        total = jnp.sum(weights, axis=0, keepdims=True)
        probs = (weights * (1.0 / total)).astype(jnp.bfloat16)
        values = key_rows(v_all, near, glob, rand, low_half)
        o_ref[rows, :] = pick_heads(down(probs, values), masks_f, block_len).astype(jnp.bfloat16)
        lse_ref[0, pl.ds(slot, 1), :] = top + jnp.log(total)
        return carry

    lax.fori_loop(0, half_blocks, one, 0, unroll=min(8, half_blocks))


def attend_back_kernel(
    sizes, blocks, head_dim, scale, group,
    table, q_ref, k_own, k_other, v_own, v_other, go_ref, lse_ref, *refs,
):
    dq_ref, own_ref, other_ref, k_all, v_all, dk_all, dv_all, dk_glob, dv_glob = refs[-9:]
    heads, picks, rand_size, half_blocks = sizes
    block_len = k_all.shape[1]
    lanes = q_ref.shape[1]
    f32 = jnp.float32
    load_halves(k_all, k_own, k_other, half_blocks, block_len)
    load_halves(v_all, v_own, v_other, half_blocks, block_len)
    dk_all[...] = jnp.zeros_like(dk_all)
    dv_all[...] = jnp.zeros_like(dv_all)
    dk_glob[...] = jnp.zeros_like(dk_glob)
    dv_glob[...] = jnp.zeros_like(dv_glob)
    low_half = lax.broadcasted_iota(jnp.int32, (block_len, 128), 1) < head_dim
    masks = head_masks(lanes, head_dim, jnp.bfloat16)
    masks_f = head_masks(lanes, head_dim, f32)
    glob = [table[rand_size], table[rand_size + 1]]

    def add_back(grads, near, rand, into, into_glob):
        for n in range(3):
            into[near[n]] += grads[n * block_len : (n + 1) * block_len]
        for n in range(2):
            into_glob[n] += grads[(3 + n) * block_len : (4 + n) * block_len]
        for r in range(picks):
            part = grads[(5 + r) * block_len : (6 + r) * block_len]
            for c in range(lanes // 128):
                cell = part[:, c * 128 : (c + 1) * 128]
                columns = pl.ds(c * 128, 128)
                into[rand[r][2 * c], :, columns] += jnp.where(low_half, cell, 0.0)
                into[rand[r][2 * c + 1], :, columns] += jnp.where(low_half, 0.0, cell)

    def one(slot, carry):
        block, near, rand = block_places(table, slot, group, sizes)
        rows = pl.ds(pl.multiple_of(slot * block_len, block_len), block_len)
        queries = spread_heads(q_ref[rows, :], masks)
        grads_out = spread_heads(go_ref[rows, :], masks)
        keys = key_rows(k_all, near, glob, rand, low_half)
        values = key_rows(v_all, near, glob, rand, low_half)
        scores = mask_scores(across(keys, queries), block, blocks, block_len)
        probs = jnp.exp(scores - lse_ref[0, pl.ds(slot, 1), :])
        grad_probs = across(values, grads_out)
        row_dot = jnp.sum(probs * grad_probs, axis=0, keepdims=True)
        grad_scores = (probs * (grad_probs - row_dot)).astype(jnp.bfloat16)
        add_back(jnp.dot(probs.astype(jnp.bfloat16), grads_out, preferred_element_type=f32), near, rand, dv_all, dv_glob)
        add_back(jnp.dot(grad_scores, queries, preferred_element_type=f32), near, rand, dk_all, dk_glob)
        dq_ref[rows, :] = (pick_heads(down(grad_scores, keys), masks_f, block_len) * scale).astype(jnp.bfloat16)
        return carry

    lax.fori_loop(0, half_blocks, one, 0, unroll=min(8, half_blocks))
    for n in range(2):
        dk_all[glob[n]] += dk_glob[n]
        dv_all[glob[n]] += dv_glob[n]
    for target, start in ((own_ref, 0), (other_ref, half_blocks)):
        for n, source in enumerate((dk_all, dv_all)):
            cells = source[start : start + half_blocks].astype(jnp.bfloat16)
            target[:, n * lanes : (n + 1) * lanes] = cells.reshape(half_blocks * block_len, lanes)


def norm_parts(values):
    average = jnp.mean(values, axis=-1, keepdims=True)
    centred = values - average
    rstd = lax.rsqrt(jnp.mean(centred * centred, axis=-1, keepdims=True) + epsilon)
    return centred * rstd, rstd


def norm_back(grad, normal, rstd, gain):
    scaled = grad * gain
    first = jnp.mean(scaled, axis=-1, keepdims=True)
    second = jnp.mean(scaled * normal, axis=-1, keepdims=True)
    return rstd * (scaled - first - normal * second)


def normal_parts(values):
    cdf = 0.5 + 0.5 * lax.erf(values * 0.5**0.5)
    return cdf, values * jnp.exp(-0.5 * values * values) * 0.3989422804014327


def column_sum(values):
    return jnp.sum(values, axis=0, keepdims=True)


def qkv_kernel(scale, rows_ref, gain, shift, weight, bias, q_ref, kv_ref):
    width = rows_ref.shape[1]
    normal, _ = norm_parts(rows_ref[...].astype(jnp.float32))
    normed = (normal * gain[...] + shift[...]).astype(jnp.bfloat16)

    def part(n):
        columns = slice(n * width, (n + 1) * width)
        return jnp.dot(normed, weight[:, columns], preferred_element_type=jnp.float32)

    q_ref[...] = (part(0) + bias[0:1]).astype(jnp.bfloat16) * jnp.asarray(scale, jnp.bfloat16)
    kv_ref[:, :width] = part(1).astype(jnp.bfloat16)
    kv_ref[:, width:] = (part(2) + bias[1:2]).astype(jnp.bfloat16)


def ffn_kernel(
    chunk, shards, cot_count,
    place, scale, rows_ref, att_ref, *refs,
):
    cot_parts = refs[:cot_count]
    (
        w_out, b_out, gain, shift, w_up, b_up, w_down, b_down,
        out_ref, resid_ref, go_ref, vec_ref, vec_up_ref, keep_ref, send_ref,
        acc_up, acc_down, acc_out, stage, sems, active_all, inner_all, cot_rows, cot_sems,
    ) = refs[cot_count:]
    f32, bf16 = jnp.float32, jnp.bfloat16
    step, steps = pl.program_id(0), pl.num_programs(0)
    width, wide = w_up.shape

    slot = step % 2

    def fetch(number):
        for n, part in enumerate(cot_parts):
            @pl.when(number == n)
            def _():
                pltpu.make_async_copy(part, cot_rows.at[n % 2], cot_sems.at[n % 2]).start()

    @pl.when(step == 0)
    def _():
        fetch(step)

    fetch(step + 1)

    @pl.when(step == 0)
    def _():
        for ref in (acc_up, acc_down, acc_out, vec_ref, vec_up_ref):
            ref[...] = jnp.zeros_like(ref)

    att = att_ref[...]
    residual = rows_ref[...].astype(f32) + (jnp.dot(att, w_out[...], preferred_element_type=f32) + b_out[...])
    normal, rstd = norm_parts(residual)
    second = (normal * gain[...] + shift[...]).astype(bf16)
    pltpu.make_async_copy(cot_parts[0], cot_rows.at[slot], cot_sems.at[slot]).wait()
    upstream = cot_rows[slot].astype(f32) * scale[0]
    branch = upstream.astype(bf16)
    second_t = second.T
    branch_t = branch.T
    total = residual + b_down[...]
    grad_second = jnp.zeros_like(residual)
    def raise_part(first):
        part = slice(first, first + chunk)
        inner = jnp.dot(second, w_up[:, part], preferred_element_type=f32) + b_up[:, part]
        return inner, across(branch, w_down[part, :])

    ahead = raise_part(0)
    for first in range(0, wide, chunk):
        part = slice(first, first + chunk)
        inner, grad_active = ahead
        if first + chunk < wide:
            ahead = raise_part(first + chunk)
        cdf, slope = normal_parts(inner)
        active = (inner * cdf).astype(bf16)
        grad_inner_f = grad_active * (cdf + slope)
        grad_inner = grad_inner_f.astype(bf16)
        active_all[:, part] = active
        inner_all[:, part] = grad_inner
        acc_down[:, part] += jnp.dot(branch_t, active, preferred_element_type=f32)
        acc_up[:, part] += jnp.dot(second_t, grad_inner, preferred_element_type=f32)
        vec_up_ref[:, part] += column_sum(grad_inner_f)
    total = total + jnp.dot(active_all[...], w_down[...], preferred_element_type=f32)
    grad_second = across(inner_all[...], w_up[...])
    out_ref[...] = total.astype(bf16)
    grad_resid = upstream + norm_back(grad_second, normal, rstd, gain[...])
    grad_proj = grad_resid.astype(bf16)
    resid_ref[...] = grad_proj
    go_ref[...] = across(grad_proj, w_out[...]).astype(bf16)
    acc_out[...] += jnp.dot(att.T, grad_proj, preferred_element_type=f32)
    vec_ref[0:1] += column_sum(grad_resid)
    vec_ref[1:2] += column_sum(grad_second * normal)
    vec_ref[2:3] += column_sum(grad_second)
    vec_ref[3:4] += column_sum(upstream)

    @pl.when(step == steps - 1)
    def _():
        core = place[0]
        part = width // shards
        down_part = wide // shards
        count = wide // width
        rows = stage.shape[1]
        size = rows // 4

        def copies(b, slot):
            moves = []
            for piece in range(4):
                source = stage.at[slot, pl.ds(piece * size, size)]
                for bit, target in ((0, keep_ref), (1, send_ref)):
                    moves.append((piece % 2, bit, pltpu.make_async_copy(source, target.at[b, piece // 2], sems.at[slot, piece])))
            return moves

        def act(b, slot, what):
            for parity, bit, move in copies(b, slot):
                @pl.when((parity != core) == (bit == 1))
                def _():
                    getattr(move, what)()

        for b in range(shards):
            slot = b % 2
            if b >= 2:
                act(b - 2, slot, "wait")
            for k in range(count):
                stage[slot, k * part : (k + 1) * part] = acc_up[b * part : (b + 1) * part, k * width : (k + 1) * width].astype(bf16)
            base = count * part
            half = width // 2
            for k in range(2):
                stage[slot, base : base + half, k * half : (k + 1) * half] = acc_down[
                    k * half : (k + 1) * half, b * down_part : (b + 1) * down_part
                ].astype(bf16)
            base += half
            stage[slot, base : base + part] = acc_out[b * part : (b + 1) * part, :].astype(bf16)
            stage[slot, base + part :] = jnp.zeros((rows - base - part, width), bf16)
            act(b, slot, "start")
        for b in range(shards - 2, shards):
            act(b, b % 2, "wait")


def input_grad_kernel(groups, *refs):
    f32, bf16 = jnp.float32, jnp.bfloat16
    parts = refs[: 3 * groups]
    rows_ref, resid_ref, gain, shift, weight = refs[3 * groups : 3 * groups + 5]
    tok_ref, joined_ref, normed_ref, vec_ref = refs[-4:]
    width = rows_ref.shape[1]
    lanes = width // groups

    @pl.when(pl.program_id(0) == 0)
    def _():
        vec_ref[...] = jnp.zeros_like(vec_ref)

    for g in range(groups):
        dq, own, other = parts[3 * g : 3 * g + 3]
        columns = slice(g * lanes, (g + 1) * lanes)
        joined_ref[:, columns] = dq[...]
        both = (own[...].astype(f32) + other[...].astype(f32)).astype(bf16)
        joined_ref[:, width + g * lanes : width + (g + 1) * lanes] = both[:, :lanes]
        joined_ref[:, 2 * width + g * lanes : 2 * width + (g + 1) * lanes] = both[:, lanes:]
        vec_ref[0:1, columns] += column_sum(dq[...].astype(f32))
        vec_ref[1:2, columns] += column_sum(both[:, lanes:].astype(f32))
    grad = across(joined_ref[...], weight[...])
    normal, rstd = norm_parts(rows_ref[...].astype(f32))
    normed_ref[...] = (normal * gain[...] + shift[...]).astype(bf16)
    vec_ref[2:3] += column_sum(grad * normal)
    vec_ref[3:4] += column_sum(grad)
    tok_ref[...] = (resid_ref[...].astype(f32) + norm_back(grad, normal, rstd, gain[...])).astype(bf16)


def weight_grad_kernel(normed_ref, joined_ref, *refs):
    out_ref, turned = refs[-2:]

    @pl.when(pl.program_id(0) == 0)
    def _():
        turned[...] = normed_ref[...].T

    width = normed_ref.shape[1]
    shards = out_ref.shape[0]
    full = jnp.dot(turned[...], joined_ref[...], preferred_element_type=jnp.float32).astype(jnp.bfloat16)
    out_ref[...] = full.reshape(shards, width // shards, width)


def general_body(
    tokens,
    cotangent,
    w_qkv,
    b_q,
    b_v,
    w_out,
    b_out,
    gain_one,
    shift_one,
    gain_two,
    shift_two,
    w_up,
    b_up,
    w_down,
    b_down,
    rand_owner,
    rand_sub,
    global_ids,
    species,
):
    blk_count = lax.axis_size("blk")
    blk_pos = lax.axis_index("blk")
    win_pos = lax.axis_index("win")
    windows, length, model_width = tokens.shape
    blocks = rand_owner.shape[1]
    heads = rand_owner.shape[2]
    picks = rand_owner.shape[3]
    glob_count = global_ids.shape[1]
    own_blocks = blocks // blk_count
    block_len = length // own_blocks
    head_dim = model_width // heads
    pair_width = 2 * head_dim
    all_rows = windows * length
    key_count = 3 + glob_count + picks
    per_device = own_blocks * heads * picks
    slot_cap = max(2, 2 * per_device // blk_count)
    score_scale = head_dim ** (-0.5)
    f32 = jnp.float32
    bf16 = jnp.bfloat16
    tokens_f = tokens.reshape(all_rows, model_width).astype(f32)
    normed_f, norm_one_pull = jax.vjp(layer_norm, tokens_f, gain_one, shift_one)
    normed = normed_f.astype(bf16)
    joined = jnp.dot(normed, w_qkv, preferred_element_type=f32)
    query_vals = (joined[:, :model_width] + b_q).astype(bf16)
    key_vals = joined[:, model_width : 2 * model_width].astype(bf16)
    value_vals = (joined[:, 2 * model_width :] + b_v).astype(bf16)

    def to_heads(tensor):
        return tensor.reshape(windows, own_blocks, block_len, heads, head_dim).transpose(
            0, 1, 3, 2, 4
        )

    def from_heads(tensor):
        return tensor.transpose(0, 1, 3, 2, 4).reshape(all_rows, model_width)

    query_heads = to_heads(query_vals)
    local_pairs = jnp.concatenate([to_heads(key_vals), to_heads(value_vals)], axis=-1)
    rimmed = padded(local_pairs, (("blk", 1),), 1)
    block_ids = blk_pos * own_blocks + jnp.arange(own_blocks, dtype=jnp.int32)
    owned_glob = (global_ids[:, :, None] == block_ids[None, None, :]).astype(bf16)
    glob_terms = jnp.einsum("wgb,wbhsc->wghsc", owned_glob, local_pairs, preferred_element_type=f32)
    glob_pairs = lax.psum(glob_terms.astype(jnp.bfloat16), "blk").astype(jnp.float32).astype(bf16)
    owner_rows = rand_owner.reshape(windows, blk_count, per_device)
    sub_rows = rand_sub.reshape(windows, blk_count, per_device)
    owner_hits = (owner_rows[..., None] == jnp.arange(blk_count, dtype=jnp.int32)).astype(jnp.int32)
    slot_rows = jnp.sum(owner_hits * (jnp.cumsum(owner_hits, axis=2) - 1), axis=-1)
    my_owner = lax.dynamic_index_in_dim(owner_rows, blk_pos, 1, keepdims=False)
    my_slot = lax.dynamic_index_in_dim(slot_rows, blk_pos, 1, keepdims=False)
    fetch_index = my_owner * slot_cap + my_slot
    head_of_row = jnp.arange(per_device, dtype=jnp.int32) // picks % heads
    source_rows = sub_rows * heads + head_of_row[None, None, :]
    requester = jnp.arange(blk_count, dtype=jnp.int32)[None, :, None]
    target_rows = jnp.where(
        owner_rows == blk_pos, requester * slot_cap + slot_rows, blk_count * slot_cap
    )
    send_table = jnp.full((windows, blk_count * slot_cap + 1), own_blocks * heads, jnp.int32)
    send_table = jax.vmap(set_rows)(
        send_table, target_rows.reshape(windows, -1), source_rows.reshape(windows, -1)
    )[:, : blk_count * slot_cap]
    flat_pairs = jnp.concatenate(
        [
            local_pairs.reshape(windows, own_blocks * heads, block_len, pair_width),
            jnp.zeros((windows, 1, block_len, pair_width), bf16),
        ],
        axis=1,
    )
    outgoing = jax.vmap(take_rows)(flat_pairs, send_table).reshape(
        windows, blk_count, slot_cap, block_len, pair_width
    )
    incoming = lax.all_to_all(outgoing, "blk", split_axis=1, concat_axis=1, tiled=True).reshape(
        windows, blk_count * slot_cap, block_len, pair_width
    )
    rand_pairs = jax.vmap(take_rows)(incoming, fetch_index).reshape(
        windows, own_blocks, heads, picks, block_len, pair_width
    )
    near_pairs = jnp.stack(
        [rimmed[:, 0:own_blocks], rimmed[:, 1 : own_blocks + 1], rimmed[:, 2 : own_blocks + 2]],
        axis=3,
    )
    far_pairs = jnp.broadcast_to(
        glob_pairs.transpose(0, 2, 1, 3, 4)[:, None],
        (windows, own_blocks, heads, glob_count, block_len, pair_width),
    )
    gathered_keys = jnp.concatenate([near_pairs, far_pairs, rand_pairs], axis=3).reshape(
        windows, own_blocks, heads, key_count * block_len, pair_width
    )
    set_keys = gathered_keys[..., :head_dim]
    set_values = gathered_keys[..., head_dim:]
    block_flags = jnp.concatenate(
        [
            (block_ids > 0)[:, None],
            jnp.ones((own_blocks, 1), jnp.bool_),
            (block_ids < blocks - 1)[:, None],
            jnp.ones((own_blocks, glob_count + picks), jnp.bool_),
        ],
        axis=1,
    )
    key_valid = jnp.repeat(block_flags, block_len, axis=1)[None, :, None, None, :]

    def score_block():
        raw_scores = (
            jnp.einsum("wbhqe,wbhke->wbhqk", query_heads, set_keys, preferred_element_type=f32)
            * score_scale
        )
        return jnp.where(key_valid, raw_scores, masked_score)

    score_matrix = score_block()
    top_score = jnp.max(score_matrix, axis=-1, keepdims=True)
    log_total = top_score + jnp.log(
        jnp.sum(jnp.exp(score_matrix - top_score), axis=-1, keepdims=True)
    )
    probs_low = jnp.exp(score_matrix - log_total).astype(bf16)
    attended = jnp.einsum(
        "wbhqk,wbhke->wbhqe", probs_low, set_values, preferred_element_type=f32
    ).astype(bf16)
    merged = from_heads(attended)
    residual = tokens_f + (jnp.dot(merged, w_out, preferred_element_type=f32) + b_out)
    second_f, norm_two_pull = jax.vjp(layer_norm, residual, gain_two, shift_two)
    second = second_f.astype(bf16)
    inner_f = jnp.dot(second, w_up, preferred_element_type=f32) + b_up
    active_f, gelu_pull = jax.vjp(partial(jax.nn.gelu, approximate=False), inner_f)
    active = active_f.astype(bf16)
    output = residual + (jnp.dot(active, w_down, preferred_element_type=f32) + b_down)
    species_count = jnp.sum(
        (species[:, None] == jnp.arange(SPECIES, dtype=jnp.int32)[None, :]).astype(f32), axis=0
    )
    my_species = lax.dynamic_slice_in_dim(species, win_pos * windows, windows)
    own_count = jnp.sum(
        (my_species[:, None] == jnp.arange(SPECIES, dtype=jnp.int32)[None, :]).astype(f32)
        * species_count[None, :],
        axis=1,
    )
    window_scale = jnp.sqrt(species.shape[0] / (SPECIES * own_count))
    upstream = (cotangent.astype(f32) * window_scale[:, None, None]).reshape(all_rows, model_width)
    grad_branch = upstream.astype(bf16)
    grad_w_down = jnp.einsum("tf,td->fd", active, grad_branch, preferred_element_type=f32)
    grad_b_down = jnp.sum(grad_branch, axis=0, dtype=f32)
    grad_active = jnp.einsum("td,fd->tf", grad_branch, w_down, preferred_element_type=f32)
    grad_inner = gelu_pull(grad_active)[0].astype(bf16)
    grad_w_up = jnp.einsum("td,tf->df", second, grad_inner, preferred_element_type=f32)
    grad_b_up = jnp.sum(grad_inner, axis=0, dtype=f32)
    grad_second = jnp.einsum("tf,df->td", grad_inner, w_up, preferred_element_type=f32)
    grad_resid_norm, grad_gain_two, grad_shift_two = norm_two_pull(grad_second)
    grad_resid = upstream + grad_resid_norm
    grad_proj = grad_resid.astype(bf16)
    grad_w_out = jnp.einsum("ti,to->io", merged, grad_proj, preferred_element_type=f32)
    grad_b_out = jnp.sum(grad_proj, axis=0, dtype=f32)
    grad_attended = to_heads(
        jnp.einsum("to,io->ti", grad_proj, w_out, preferred_element_type=f32).astype(bf16)
    )
    probs_full = jnp.exp(score_block() - log_total)
    grad_probs = jnp.einsum(
        "wbhqe,wbhke->wbhqk", grad_attended, set_values, preferred_element_type=f32
    )
    grad_set_values = jnp.einsum(
        "wbhqk,wbhqe->wbhke", probs_full.astype(bf16), grad_attended, preferred_element_type=f32
    )
    row_dot = jnp.sum(probs_full * grad_probs, axis=-1, keepdims=True)
    grad_scores = (probs_full * (grad_probs - row_dot)).astype(bf16)
    grad_query = (
        jnp.einsum("wbhqk,wbhke->wbhqe", grad_scores, set_keys, preferred_element_type=f32)
        * score_scale
    )
    grad_set_keys = (
        jnp.einsum("wbhqk,wbhqe->wbhke", grad_scores, query_heads, preferred_element_type=f32)
        * score_scale
    )
    grad_set = jnp.concatenate([grad_set_keys, grad_set_values], axis=-1).reshape(
        windows, own_blocks, heads, key_count, block_len, pair_width
    )
    extended = (
        jnp.pad(grad_set[:, :, :, 1], ((0, 0), (1, 1), (0, 0), (0, 0), (0, 0)))
        + jnp.pad(grad_set[:, :, :, 0], ((0, 0), (0, 2), (0, 0), (0, 0), (0, 0)))
        + jnp.pad(grad_set[:, :, :, 2], ((0, 0), (2, 0), (0, 0), (0, 0), (0, 0)))
    )
    edge_grads = jnp.concatenate([extended[:, :1], extended[:, own_blocks + 1 :]], axis=1)
    edge_back = padded(edge_grads.astype(jnp.bfloat16), (("blk", 1),), 1).astype(edge_grads.dtype)
    pair_grad = extended[:, 1 : own_blocks + 1]
    pair_grad = pair_grad.at[:, 0].add(edge_back[:, 0]).at[:, own_blocks - 1].add(edge_back[:, 3])
    glob_grad = jnp.sum(grad_set[:, :, :, 3 : 3 + glob_count], axis=1).transpose(0, 2, 1, 3, 4)
    glob_total = lax.psum(glob_grad.astype(jnp.bfloat16), "blk").astype(jnp.float32)
    pair_grad = pair_grad + jnp.einsum(
        "wgb,wghsc->wbhsc", owned_glob.astype(f32), glob_total, precision=lax.Precision.HIGHEST
    )
    rand_grad = grad_set[:, :, :, 3 + glob_count :].reshape(
        windows, per_device, block_len, pair_width
    )
    back_out = jax.vmap(add_rows)(
        jnp.zeros((windows, blk_count * slot_cap, block_len, pair_width), f32),
        fetch_index,
        rand_grad,
    )
    back_in = lax.all_to_all(
        back_out.reshape(windows, blk_count, slot_cap, block_len, pair_width).astype(jnp.bfloat16),
        "blk",
        split_axis=1,
        concat_axis=1,
        tiled=True,
    ).astype(jnp.float32)
    owner_sum = jax.vmap(add_rows)(
        jnp.zeros((windows, own_blocks * heads + 1, block_len, pair_width), f32),
        send_table,
        back_in.reshape(windows, blk_count * slot_cap, block_len, pair_width),
    )
    pair_grad = pair_grad + owner_sum[:, : own_blocks * heads].reshape(
        windows, own_blocks, heads, block_len, pair_width
    )
    grad_keys = from_heads(pair_grad[..., :head_dim].astype(bf16))
    grad_values = from_heads(pair_grad[..., head_dim:].astype(bf16))
    grad_joined = jnp.concatenate(
        [from_heads(grad_query.astype(bf16)), grad_keys, grad_values], axis=1
    )
    grad_w_qkv = jnp.einsum("td,tc->dc", normed, grad_joined, preferred_element_type=f32)
    grad_b_q = jnp.sum(grad_joined[:, :model_width], axis=0, dtype=f32)
    grad_b_v = jnp.sum(grad_joined[:, 2 * model_width :], axis=0, dtype=f32)
    grad_normed = jnp.einsum("tc,dc->td", grad_joined, w_qkv, preferred_element_type=f32)
    grad_tok_norm, grad_gain_one, grad_shift_one = norm_one_pull(grad_normed)
    grad_tokens = (grad_resid + grad_tok_norm).astype(bf16).reshape(windows, length, model_width)
    local_grads = (
        grad_w_qkv,
        grad_b_q,
        grad_b_v,
        grad_w_out,
        grad_b_out,
        grad_gain_one,
        grad_shift_one,
        grad_gain_two,
        grad_shift_two,
        grad_w_up,
        grad_b_up,
        grad_w_down,
        grad_b_down,
    )
    packed_grads = jnp.concatenate(
        [grad_item.reshape(blk_count, -1) for grad_item in local_grads], axis=1
    )
    total_cols = packed_grads.shape[1]
    win_count = lax.axis_size("win")
    pad_cols = -total_cols % win_count
    shard_sum = lax.psum_scatter(
        packed_grads.astype(jnp.bfloat16), "blk", scatter_dimension=0, tiled=True
    ).astype(jnp.float32)
    split_shard = jnp.pad(shard_sum, ((0, 0), (0, pad_cols))).reshape(win_count, -1)
    group_piece = lax.psum_scatter(
        split_shard.astype(jnp.bfloat16), "win", scatter_dimension=0, tiled=True
    ).astype(jnp.float32)
    summed = (
        lax.all_gather(group_piece.astype(jnp.bfloat16), "win", axis=0, tiled=True)
        .astype(group_piece.dtype)
        .reshape(1, -1)[:, :total_cols]
    )
    shards = []
    offset = 0
    for grad_item in local_grads:
        entry_count = grad_item.size // blk_count
        shards.append(
            summed[0, offset : offset + entry_count].reshape(
                (grad_item.shape[0] // blk_count,) + grad_item.shape[1:]
            )
        )
        offset = offset + entry_count
    out_tokens = output.astype(bf16).reshape(windows, length, model_width)
    return (
        out_tokens,
        grad_tokens,
        shards[0],
        shards[1],
        shards[2],
        shards[3],
        shards[4],
        shards[5],
        shards[6],
        shards[7],
        shards[8],
        shards[9],
        shards[10],
        shards[11],
        shards[12],
    )


def layer_step(*arguments):
    windows = arguments[0].shape[0]
    paired = lax.axis_size("blk") == 2 * windows and lax.axis_size("win") == 4 and windows & (windows - 1) == 0
    return (paired_body if paired else general_body)(*arguments)


def paired_body(
    tokens,
    cotangent,
    w_qkv,
    b_q,
    b_v,
    w_out,
    b_out,
    gain_one,
    shift_one,
    gain_two,
    shift_two,
    w_up,
    b_up,
    w_down,
    b_down,
    rand_owner,
    rand_sub,
    global_ids,
    species,
):
    f32 = jnp.float32
    bf16 = jnp.bfloat16
    win_count = lax.axis_size("win")
    blk_count = lax.axis_size("blk")
    win_pos = lax.axis_index("win")
    blk_pos = lax.axis_index("blk")
    layers, length, width = tokens.shape
    core, layer, side = win_pos % 2, blk_pos // 2, blk_pos % 2
    blocks, heads, picks = rand_owner.shape[1:]
    own_blocks = blocks // blk_count
    half_blocks = blocks // 2
    block_len = length // own_blocks
    head_dim = width // heads
    all_rows = layers * length
    lanes = HEADS_PER_GROUP * head_dim
    groups = heads // HEADS_PER_GROUP
    score_scale = head_dim ** (-0.5)

    def regroup(value):
        parts = []
        for step in range(layers):
            part = lax.dynamic_index_in_dim(value, (layer + step) % layers, 0, keepdims=False)
            parts.append(lax.ppermute(part, ("win", "blk"), regroup_pairs(win_count, layers, step)))
        return parts

    def send_back(value):
        parts = []
        for step in range(layers):
            pairs = [(b, a) for a, b in regroup_pairs(win_count, layers, step)]
            parts.append(lax.ppermute(value[step * length : (step + 1) * length], ("win", "blk"), pairs))
        return parts

    def in_order(parts):
        result = jnp.zeros((layers, length, width), parts[0].dtype)
        for step, part in enumerate(parts):
            result = lax.dynamic_update_index_in_dim(result, part, (layer + step) % layers, 0)
        return result

    def takes(micros):
        return pl.CostEstimate(flops=micros * 1_000_000_000, bytes_accessed=micros * 1_000_000, transcendentals=0)

    rows_in = jnp.concatenate(regroup(tokens), axis=0)
    cot_in = regroup(cotangent)

    rand_size = blocks * heads * picks
    named = jnp.concatenate(
        [
            lax.dynamic_index_in_dim((rand_owner * own_blocks + rand_sub).reshape(layers, rand_size), layer, 0, keepdims=False),
            lax.dynamic_index_in_dim(global_ids, layer, 0, keepdims=False),
        ]
    )
    named = jnp.where(side == core, named, swap(named, 1, 0))

    def place_of(block):
        owner = block // own_blocks
        half = jnp.where(owner % 2 == core, 0, half_blocks)
        return half + ((layer - owner // 2) % layers) * own_blocks + block % own_blocks

    slot = jnp.arange(half_blocks, dtype=jnp.int32)
    slot_block = (((layer - slot // own_blocks) % layers) * 2 + core) * own_blocks + slot % own_blocks
    table = jnp.concatenate(
        [
            place_of(named),
            slot_block,
            place_of(jnp.maximum(slot_block - 1, 0)),
            place_of(jnp.minimum(slot_block + 1, blocks - 1)),
        ]
    )
    sizes = (heads, picks, rand_size, half_blocks)

    tile = length

    def by_rows(columns):
        return pl.BlockSpec((tile, columns), lambda i: (i, 0))

    def whole(*shape, once=True):
        mode = pl.Buffered(1) if once else None
        return pl.BlockSpec(shape, lambda i: (0,) * len(shape), pipeline_mode=mode)

    scalars = pl.BlockSpec(memory_space=pltpu.SMEM)
    wide = w_up.shape[1]
    params = pltpu.CompilerParams(vmem_limit_bytes=60 << 20)
    row = lambda vector: vector.reshape(1, -1)
    query, key_value = pl.pallas_call(
        partial(qkv_kernel, score_scale),
        grid=(all_rows // tile,),
        in_specs=[by_rows(width), whole(1, width), whole(1, width), whole(width, 3 * width), whole(2, width)],
        out_specs=[by_rows(width), by_rows(2 * width)],
        out_shape=[jax.ShapeDtypeStruct((all_rows, width), bf16), jax.ShapeDtypeStruct((all_rows, 2 * width), bf16)],
        compiler_params=params,
        cost_estimate=takes(12),
        name="qkv",
    )(rows_in, row(gain_one), row(shift_one), w_qkv, jnp.stack([b_q, b_v]))
    key_value_other = swap(key_value, 1, 0)

    def lane_block(first):
        return pl.BlockSpec((all_rows, lanes), lambda g, t: (0, first + g))

    store = pltpu.VMEM((blocks, block_len, lanes), bf16)
    attended, log_total = pl.pallas_call(
        partial(attend_kernel, sizes, blocks, head_dim),
        grid_spec=pltpu.PrefetchScalarGridSpec(
            num_scalar_prefetch=1,
            grid=(groups,),
            in_specs=[lane_block(0), lane_block(0), lane_block(0), lane_block(groups), lane_block(groups)],
            out_specs=[lane_block(0), pl.BlockSpec((1, half_blocks, lanes), lambda g, t: (g, 0, 0))],
            scratch_shapes=[store, store],
        ),
        out_shape=[
            jax.ShapeDtypeStruct((all_rows, width), bf16),
            jax.ShapeDtypeStruct((groups, half_blocks, lanes), f32),
        ],
        compiler_params=pltpu.CompilerParams(vmem_limit_bytes=56 << 20),
        cost_estimate=takes(37),
        name="attend",
    )(table, query, key_value, key_value_other, key_value, key_value_other)

    species_count = jnp.sum(
        (species[:, None] == jnp.arange(SPECIES, dtype=jnp.int32)[None, :]).astype(f32), axis=0
    )
    my_window = ((win_pos // 2) * 2 + side) * layers + layer
    my_species = lax.dynamic_index_in_dim(species, my_window, 0, keepdims=False)
    own_count = jnp.sum(
        (my_species == jnp.arange(SPECIES, dtype=jnp.int32)).astype(f32) * species_count
    )
    window_scale = jnp.sqrt(species.shape[0] / (SPECIES * own_count))
    payload = 2 * wide // blk_count + width // blk_count
    payload += -payload % (16 * win_count)
    stays = jax.ShapeDtypeStruct((blk_count, win_count // 2, payload // win_count, width), bf16)
    any_place = pl.BlockSpec(memory_space=pl.ANY)
    output, grad_resid, grad_attended, vec_two, vec_up, early_keep, early_send = pl.pallas_call(
        partial(ffn_kernel, 256, blk_count, layers),
        grid=(layers,),
        in_specs=[
            scalars, scalars, by_rows(width), by_rows(width), *[any_place] * layers, whole(width, width), whole(1, width), whole(1, width),
            whole(1, width), whole(width, wide), whole(1, wide), whole(wide, width), whole(1, width),
        ],
        out_specs=[by_rows(width), by_rows(width), by_rows(width), whole(4, width), whole(1, wide), any_place, any_place],
        out_shape=[
            jax.ShapeDtypeStruct((all_rows, width), bf16),
            jax.ShapeDtypeStruct((all_rows, width), bf16),
            jax.ShapeDtypeStruct((all_rows, width), bf16),
            jax.ShapeDtypeStruct((4, width), f32),
            jax.ShapeDtypeStruct((1, wide), f32),
            stays,
            stays,
        ],
        scratch_shapes=[
            pltpu.VMEM((width, wide), f32),
            pltpu.VMEM((width, wide), f32),
            pltpu.VMEM((width, width), f32),
            pltpu.VMEM((2, payload, width), bf16),
            pltpu.SemaphoreType.DMA((2, 4)),
            pltpu.VMEM((length, wide), bf16),
            pltpu.VMEM((length, wide), bf16),
            pltpu.VMEM((2, length, width), bf16),
            pltpu.SemaphoreType.DMA((2,)),
        ],
        compiler_params=params,
        cost_estimate=takes(90),
        name="ffn",
    )(
        core.reshape(1), window_scale.reshape(1), rows_in, attended, *cot_in, w_out, row(b_out), row(gain_two), row(shift_two),
        w_up, row(b_up), w_down, row(b_down),
    )
    out_parts = send_back(output)

    pair = win_pos // 2

    def add_low(keep, other):
        return (keep.astype(f32) + other.astype(f32)).astype(bf16)

    def halve(cells, axis, bit, win_bit, blk_bit):
        keep = lax.dynamic_index_in_dim(cells, bit, axis, keepdims=False)
        send = lax.dynamic_index_in_dim(cells, 1 - bit, axis, keepdims=False)
        return keep, swap(send, win_bit, blk_bit)

    def first_halves(cells):
        cells = cells.reshape((layers, 2) + cells.shape[1:])
        middle = cells.shape[3] // 2
        return halve(cells[:, :, :, :middle], 1, side, 0, 1), halve(cells[:, :, :, middle:], 2, pair, 2, 0)

    def second_halves(left, right):
        return halve(add_low(*left), 1, pair, 2, 0), halve(add_low(*right), 1, side, 0, 1)

    def last_halves(left, right):
        cells = jnp.concatenate([add_low(*left), add_low(*right)], axis=1)
        hop = 1
        while cells.shape[0] > 1:
            cells = cells.reshape((cells.shape[0] // 2, 2) + cells.shape[1:])
            cells = add_low(*halve(cells, 1, (layer // hop) % 2, 0, 2 * hop))
            hop *= 2
        return lax.all_gather(cells[0], "win", axis=0, tiled=True).astype(f32)

    grad_parts = []
    early_other = swap(early_send, 1, 0)
    for group in range(groups):
        after = []
        if group == 1:
            after = [early_other]
        if group == 2:
            early_first = first_halves(add_low(early_keep, early_other))
            after = [received for _, received in early_first]
        def column(first):
            return pl.BlockSpec((all_rows, lanes), lambda g, t: (0, first))

        def full(columns):
            return pl.BlockSpec((all_rows, columns), lambda g, t: (0, 0))

        grad_store = pltpu.VMEM((blocks, block_len, lanes), f32)
        glob_store = pltpu.VMEM((2, block_len, lanes), f32)
        dq, own, other = pl.pallas_call(
            partial(attend_back_kernel, sizes, blocks, head_dim, score_scale, group),
            grid_spec=pltpu.PrefetchScalarGridSpec(
                num_scalar_prefetch=1,
                grid=(1,),
                in_specs=[
                    column(group), column(group), column(group), column(groups + group), column(groups + group), column(group),
                    pl.BlockSpec((1, half_blocks, lanes), lambda g, t: (group, 0, 0)),
                    *[any_place] * len(after),
                ],
                out_specs=[full(lanes), full(2 * lanes), full(2 * lanes)],
                scratch_shapes=[store, store, grad_store, grad_store, glob_store, glob_store],
            ),
            out_shape=[jax.ShapeDtypeStruct((all_rows, n * lanes), bf16) for n in (1, 2, 2)],
            compiler_params=params,
            cost_estimate=takes(25),
            name="attend_back",
        )(table, query, key_value, key_value_other, key_value, key_value_other, grad_attended, log_total, *after)
        grad_parts += [dq, own, swap(other, 1, 0)]

    early_second = second_halves(*early_first)
    grad_tokens, grad_joined, normed, vec_one = pl.pallas_call(
        partial(input_grad_kernel, groups),
        grid=(all_rows // tile,),
        in_specs=[by_rows(p.shape[1]) for p in grad_parts]
        + [by_rows(width), by_rows(width), whole(1, width), whole(1, width), whole(width, 3 * width)]
        + [any_place] * layers,
        out_specs=[by_rows(width), by_rows(3 * width), by_rows(width), whole(4, width)],
        out_shape=[
            jax.ShapeDtypeStruct((all_rows, width), bf16),
            jax.ShapeDtypeStruct((all_rows, 3 * width), bf16),
            jax.ShapeDtypeStruct((all_rows, width), bf16),
            jax.ShapeDtypeStruct((4, width), f32),
        ],
        compiler_params=params,
        cost_estimate=takes(16),
        name="input_grad",
    )(*grad_parts, rows_in, grad_resid, row(gain_one), row(shift_one), w_qkv, *out_parts)
    grad_tokens_parts = send_back(grad_tokens)
    part = width // blk_count
    late_rows = 3 * part + 32
    late_rows += -late_rows % (16 * win_count)
    late_cells = pl.pallas_call(
        weight_grad_kernel,
        grid=(3,),
        in_specs=[whole(all_rows, width), pl.BlockSpec((all_rows, width), lambda i: (0, i)), any_place, any_place],
        out_specs=pl.BlockSpec((blk_count, part, width), lambda i: (0, i, 0)),
        out_shape=jax.ShapeDtypeStruct((blk_count, late_rows, width), bf16),
        scratch_shapes=[pltpu.VMEM((width, all_rows), bf16)],
        compiler_params=params,
        cost_estimate=takes(12),
        name="weight_grad",
    )(normed, grad_joined, early_second[0][1], early_second[1][1])
    vec_rows = jnp.concatenate(
        [vec_two.reshape(4, blk_count, part), vec_one.reshape(4, blk_count, part)], axis=0
    ).transpose(1, 0, 2).reshape(blk_count, 8 * part)
    vec_rows = jnp.concatenate([vec_rows, vec_up.reshape(blk_count, wide // blk_count)], axis=1)
    vec_rows = jnp.pad(vec_rows, ((0, 0), (0, -vec_rows.shape[1] % width))).reshape(blk_count, -1, width)
    vec_rows = jnp.pad(vec_rows, ((0, 0), (0, late_rows - 3 * part - vec_rows.shape[1]), (0, 0))).astype(bf16)
    late_cells = lax.dynamic_update_slice(late_cells, vec_rows, (0, 3 * part, 0))

    late_cells = late_cells.reshape(blk_count, win_count // 2, 2, late_rows // win_count, width)
    late_keep = lax.dynamic_index_in_dim(late_cells, core, 2, keepdims=False)
    late_send = lax.dynamic_index_in_dim(late_cells, 1 - core, 2, keepdims=False)
    early = last_halves(*early_second)
    late = last_halves(*second_halves(*first_halves(add_low(late_keep, swap(late_send, 1, 0)))))

    def rows_again(rows, count):
        return rows.reshape(count, -1, width).transpose(1, 0, 2).reshape(-1, count * width)

    count = wide // width
    half = width // 2
    done_up = rows_again(early[: count * part], count)
    done_down = early[count * part : count * part + half].reshape(half, 2, wide // blk_count).transpose(2, 1, 0).reshape(-1, width)
    done_out = early[count * part + half : (count + 1) * part + half]
    done_qkv = rows_again(late[: 3 * part], 3)
    vec = late[3 * part :].reshape(-1)
    piece = lambda n: vec[n * part : (n + 1) * part]
    return (
        in_order(out_parts),
        in_order(grad_tokens_parts),
        done_qkv,
        piece(4),
        piece(5),
        done_out,
        piece(0),
        piece(6),
        piece(7),
        piece(1),
        piece(2),
        done_up,
        vec[8 * part : 8 * part + wide // blk_count],
        done_down,
        piece(3),
    )


def solution(mesh):
    placed = (
        P("win", "blk", None),
        P("win", "blk", None),
        P(),
        P(),
        P(),
        P(),
        P(),
        P(),
        P(),
        P(),
        P(),
        P(),
        P(),
        P(),
        P(),
        P("win", None, None, None),
        P("win", None, None, None),
        P("win", None),
        P(),
    )
    return jax.shard_map(
        layer_step,
        mesh=mesh,
        in_specs=placed,
        out_specs=(
            P("win", "blk", None),
            P("win", "blk", None),
            P("blk", None),
            P("blk"),
            P("blk"),
            P("blk", None),
            P("blk"),
            P("blk"),
            P("blk"),
            P("blk"),
            P("blk"),
            P("blk", None),
            P("blk"),
            P("blk", None),
            P("blk"),
        ),
        check_vma=False,
    )
```

```python
from functools import partial

import jax
import jax.numpy as jnp
from jax import lax
from jax.experimental import pallas as pl
from jax.experimental.pallas import tpu as pltpu
from jax.sharding import PartitionSpec as P

SPECIES = 4


epsilon = 1e-05
masked_score = -1000000000.0


def padded(cells, sides, width):
    for axis, dim in sides:
        count = lax.axis_size(axis)
        ends = count - 1
        head = lax.slice_in_dim(cells, 0, width, axis=dim)
        tail = lax.slice_in_dim(cells, cells.shape[dim] - width, cells.shape[dim], axis=dim)
        cells = jnp.concatenate(
            [
                lax.ppermute(tail, axis, [(i, (i + 1) % count) for i in range(ends)]),
                cells,
                lax.ppermute(head, axis, [((i + 1) % count, i) for i in range(ends)]),
            ],
            axis=dim,
        )
    return cells


def layer_norm(values, norm_gain, norm_shift):
    average = jnp.mean(values, axis=-1, keepdims=True)
    centred = values - average
    variance = jnp.mean(centred * centred, axis=-1, keepdims=True)
    return centred * lax.rsqrt(variance + epsilon) * norm_gain + norm_shift


def take_rows(source, index_rows):
    return jnp.take(source, index_rows, axis=0)


def add_rows(base, index_rows, update):
    return base.at[index_rows].add(update)


def set_rows(base, index_rows, update):
    return base.at[index_rows].set(update)


HEADS_PER_GROUP = 4


def regroup_pairs(win_count, layers, step):
    pairs = []
    for win in range(win_count):
        for blk in range(2 * layers):
            layer, side = blk // 2, blk % 2
            target = ((layer + step) % layers) * 2 + win % 2
            pairs.append((win * 2 * layers + blk, ((win // 2) * 2 + side) * 2 * layers + target))
    return pairs


def flip_pairs(win_count, blk_count, win_bit, blk_bit):
    return [
        (win * blk_count + blk, (win ^ win_bit) * blk_count + (blk ^ blk_bit))
        for win in range(win_count)
        for blk in range(blk_count)
    ]


def swap(value, win_bit, blk_bit):
    pairs = flip_pairs(lax.axis_size("win"), lax.axis_size("blk"), win_bit, blk_bit)
    return lax.ppermute(value, ("win", "blk"), pairs)


def head_masks(lanes, head_dim, dtype):
    lane = lax.broadcasted_iota(jnp.int32, (1, lanes), 1)
    return [(lane // head_dim == h).astype(dtype) for h in range(lanes // head_dim)]


def block_places(table, slot, group, sizes):
    heads, picks, rand_size, half_blocks = sizes
    block = table[rand_size + 2 + slot]
    near = [table[rand_size + 2 + half_blocks + slot], slot, table[rand_size + 2 + 2 * half_blocks + slot]]
    row = (block * heads + group * HEADS_PER_GROUP) * picks
    rand = [[table[row + h * picks + r] for h in range(HEADS_PER_GROUP)] for r in range(picks)]
    return block, near, rand


def spread_heads(rows, masks):
    return jnp.concatenate([rows * m for m in masks], axis=0)


def pick_heads(square, masks, height):
    total = square[0:height] * masks[0]
    for h in range(1, len(masks)):
        total = total + square[h * height : (h + 1) * height] * masks[h]
    return total


def key_rows(source, near, glob, rand, low_half):
    parts = [source[p] for p in near] + [source[p] for p in glob]
    for places in rand:
        columns = []
        for c in range(len(places) // 2):
            low = source[places[2 * c], :, c * 128 : (c + 1) * 128]
            high = source[places[2 * c + 1], :, c * 128 : (c + 1) * 128]
            columns.append(jnp.where(low_half, low, high))
        parts.append(jnp.concatenate(columns, axis=1))
    return jnp.concatenate(parts, axis=0)


def mask_scores(scores, block, blocks, block_len):
    first = jnp.where(block > 0, scores[:block_len], masked_score)
    last = jnp.where(block < blocks - 1, scores[2 * block_len : 3 * block_len], masked_score)
    return jnp.concatenate([first, scores[block_len : 2 * block_len], last, scores[3 * block_len :]], axis=0)


def across(left, right):
    return lax.dot_general(left, right, (((1,), (1,)), ((), ())), preferred_element_type=jnp.float32)


def down(left, right):
    return lax.dot_general(left, right, (((0,), (0,)), ((), ())), preferred_element_type=jnp.float32)


def load_halves(target, own, other, half_blocks, block_len):
    lanes = own.shape[-1]
    target[0:half_blocks] = own[...].reshape(half_blocks, block_len, lanes)
    target[half_blocks:] = other[...].reshape(half_blocks, block_len, lanes)


def attend_kernel(sizes, blocks, head_dim, table, q_ref, k_own, k_other, v_own, v_other, o_ref, lse_ref, k_all, v_all):
    heads, picks, rand_size, half_blocks = sizes
    block_len = k_all.shape[1]
    lanes = q_ref.shape[1]
    group = pl.program_id(0)
    load_halves(k_all, k_own, k_other, half_blocks, block_len)
    load_halves(v_all, v_own, v_other, half_blocks, block_len)
    low_half = lax.broadcasted_iota(jnp.int32, (block_len, 128), 1) < head_dim
    masks = head_masks(lanes, head_dim, jnp.bfloat16)
    masks_f = head_masks(lanes, head_dim, jnp.float32)
    glob = [table[rand_size], table[rand_size + 1]]

    def one(slot, carry):
        block, near, rand = block_places(table, slot, group, sizes)
        rows = pl.ds(pl.multiple_of(slot * block_len, block_len), block_len)
        queries = spread_heads(q_ref[rows, :], masks)
        keys = key_rows(k_all, near, glob, rand, low_half)
        scores = mask_scores(across(keys, queries), block, blocks, block_len)
        top = jnp.max(scores, axis=0, keepdims=True)
        weights = jnp.exp(scores - top)
        total = jnp.sum(weights, axis=0, keepdims=True)
        probs = (weights * (1.0 / total)).astype(jnp.bfloat16)
        values = key_rows(v_all, near, glob, rand, low_half)
        o_ref[rows, :] = pick_heads(down(probs, values), masks_f, block_len).astype(jnp.bfloat16)
        lse_ref[0, pl.ds(slot, 1), :] = top + jnp.log(total)
        return carry

    lax.fori_loop(0, half_blocks, one, 0, unroll=min(8, half_blocks))


def attend_back_kernel(
    sizes, blocks, head_dim, scale, group,
    table, q_ref, k_own, k_other, v_own, v_other, go_ref, lse_ref, *refs,
):
    dq_ref, own_ref, other_ref, k_all, v_all, dk_all, dv_all, dk_glob, dv_glob = refs[-9:]
    heads, picks, rand_size, half_blocks = sizes
    block_len = k_all.shape[1]
    lanes = q_ref.shape[1]
    f32 = jnp.float32
    load_halves(k_all, k_own, k_other, half_blocks, block_len)
    load_halves(v_all, v_own, v_other, half_blocks, block_len)
    dk_all[...] = jnp.zeros_like(dk_all)
    dv_all[...] = jnp.zeros_like(dv_all)
    dk_glob[...] = jnp.zeros_like(dk_glob)
    dv_glob[...] = jnp.zeros_like(dv_glob)
    low_half = lax.broadcasted_iota(jnp.int32, (block_len, 128), 1) < head_dim
    masks = head_masks(lanes, head_dim, jnp.bfloat16)
    masks_f = head_masks(lanes, head_dim, f32)
    glob = [table[rand_size], table[rand_size + 1]]

    def add_back(grads, near, rand, into, into_glob):
        for n in range(3):
            into[near[n]] += grads[n * block_len : (n + 1) * block_len]
        for n in range(2):
            into_glob[n] += grads[(3 + n) * block_len : (4 + n) * block_len]
        for r in range(picks):
            part = grads[(5 + r) * block_len : (6 + r) * block_len]
            for c in range(lanes // 128):
                cell = part[:, c * 128 : (c + 1) * 128]
                columns = pl.ds(c * 128, 128)
                into[rand[r][2 * c], :, columns] += jnp.where(low_half, cell, 0.0)
                into[rand[r][2 * c + 1], :, columns] += jnp.where(low_half, 0.0, cell)

    def one(slot, carry):
        block, near, rand = block_places(table, slot, group, sizes)
        rows = pl.ds(pl.multiple_of(slot * block_len, block_len), block_len)
        queries = spread_heads(q_ref[rows, :], masks)
        grads_out = spread_heads(go_ref[rows, :], masks)
        keys = key_rows(k_all, near, glob, rand, low_half)
        values = key_rows(v_all, near, glob, rand, low_half)
        scores = mask_scores(across(keys, queries), block, blocks, block_len)
        probs = jnp.exp(scores - lse_ref[0, pl.ds(slot, 1), :])
        grad_probs = across(values, grads_out)
        row_dot = jnp.sum(probs * grad_probs, axis=0, keepdims=True)
        grad_scores = (probs * (grad_probs - row_dot)).astype(jnp.bfloat16)
        add_back(jnp.dot(probs.astype(jnp.bfloat16), grads_out, preferred_element_type=f32), near, rand, dv_all, dv_glob)
        add_back(jnp.dot(grad_scores, queries, preferred_element_type=f32), near, rand, dk_all, dk_glob)
        dq_ref[rows, :] = (pick_heads(down(grad_scores, keys), masks_f, block_len) * scale).astype(jnp.bfloat16)
        return carry

    lax.fori_loop(0, half_blocks, one, 0, unroll=min(8, half_blocks))
    for n in range(2):
        dk_all[glob[n]] += dk_glob[n]
        dv_all[glob[n]] += dv_glob[n]
    for target, start in ((own_ref, 0), (other_ref, half_blocks)):
        for n, source in enumerate((dk_all, dv_all)):
            cells = source[start : start + half_blocks].astype(jnp.bfloat16)
            target[:, n * lanes : (n + 1) * lanes] = cells.reshape(half_blocks * block_len, lanes)


def norm_parts(values):
    average = jnp.mean(values, axis=-1, keepdims=True)
    centred = values - average
    rstd = lax.rsqrt(jnp.mean(centred * centred, axis=-1, keepdims=True) + epsilon)
    return centred * rstd, rstd


def norm_back(grad, normal, rstd, gain):
    scaled = grad * gain
    first = jnp.mean(scaled, axis=-1, keepdims=True)
    second = jnp.mean(scaled * normal, axis=-1, keepdims=True)
    return rstd * (scaled - first - normal * second)


def normal_parts(values):
    cdf = 0.5 + 0.5 * lax.erf(values * 0.5**0.5)
    return cdf, values * jnp.exp(-0.5 * values * values) * 0.3989422804014327


def column_sum(values):
    return jnp.sum(values, axis=0, keepdims=True)


def qkv_kernel(scale, rows_ref, gain, shift, weight, bias, q_ref, kv_ref):
    width = rows_ref.shape[1]
    normal, _ = norm_parts(rows_ref[...].astype(jnp.float32))
    normed = (normal * gain[...] + shift[...]).astype(jnp.bfloat16)

    def part(n):
        columns = slice(n * width, (n + 1) * width)
        return jnp.dot(normed, weight[:, columns], preferred_element_type=jnp.float32)

    q_ref[...] = (part(0) + bias[0:1]).astype(jnp.bfloat16) * jnp.asarray(scale, jnp.bfloat16)
    kv_ref[:, :width] = part(1).astype(jnp.bfloat16)
    kv_ref[:, width:] = (part(2) + bias[1:2]).astype(jnp.bfloat16)


MESH = pl.DeviceIdType.MESH


def tile_order(number):
    return jnp.where(number == 0, 2, jnp.where(number == 2, 3, jnp.where(number == 3, 0, number)))


def position():
    win, blk = lax.axis_index("win"), lax.axis_index("blk")
    return win, blk, win % 2, blk // 2, blk % 2


def owner_of(tile, layers):
    win, blk, core, layer, side = position()
    return (win // 2) * 2 + side, ((layer + layers - tile) % layers) * 2 + core


def greet_owners(layers):
    barrier = pltpu.get_barrier_semaphore()
    _, _, core, _, side = position()
    for tile in range(1, layers):
        pl.semaphore_signal(barrier, inc=1, device_id=owner_of(tile, layers), device_id_type=MESH)

    @pl.when(side != core)
    def _():
        pl.semaphore_signal(barrier, inc=1, device_id=owner_of(0, layers), device_id_type=MESH)
        pl.semaphore_wait(barrier, layers)

    @pl.when(side == core)
    def _():
        pl.semaphore_wait(barrier, layers - 1)


def return_tile(tile, source, target, send_sem, recv_sems, start):
    _, _, core, layer, side = position()
    layers = target.shape[0]
    stays = (tile == 0) & (side == core)

    @pl.when(stays)
    def _():
        move = pltpu.make_async_copy(source, target.at[layer], recv_sems.at[tile])
        move.start() if start else move.wait()

    @pl.when(jnp.logical_not(stays))
    def _():
        move = pltpu.make_async_remote_copy(
            src_ref=source, dst_ref=target.at[layer], send_sem=send_sem, recv_sem=recv_sems.at[tile],
            device_id=owner_of(tile, layers), device_id_type=MESH,
        )
        move.start() if start else move.wait()


def ffn_kernel(
    chunk, shards, cot_count,
    scale, rows_ref, att_ref, *refs,
):
    cot_parts = refs[:cot_count]
    (
        w_out, b_out, gain, shift, w_up, b_up, w_down, b_down,
        out_ref, resid_ref, go_ref, vec_ref, vec_up_ref, keep_ref, send_ref,
        acc_up, acc_down, acc_out, stage, sems, active_all, inner_all, cot_rows, cot_sems, out_rows, send_sems, recv_sems,
    ) = refs[cot_count:]
    f32, bf16 = jnp.float32, jnp.bfloat16
    step, steps = pl.program_id(0), pl.num_programs(0)
    width, wide = w_up.shape

    slot = step % 2

    def fetch(number):
        for n, part in enumerate(cot_parts):
            @pl.when((number < steps) & (tile_order(number) == n))
            def _():
                pltpu.make_async_copy(part, cot_rows.at[number % 2], cot_sems.at[number % 2]).start()

    @pl.when(step == 0)
    def _():
        greet_owners(steps)

    @pl.when(step == 0)
    def _():
        fetch(step)

    fetch(step + 1)

    @pl.when(step == 0)
    def _():
        for ref in (acc_up, acc_down, acc_out, vec_ref, vec_up_ref):
            ref[...] = jnp.zeros_like(ref)

    att = att_ref[...]
    residual = rows_ref[...].astype(f32) + (jnp.dot(att, w_out[...], preferred_element_type=f32) + b_out[...])
    normal, rstd = norm_parts(residual)
    second = (normal * gain[...] + shift[...]).astype(bf16)
    pltpu.make_async_copy(cot_parts[0], cot_rows.at[slot], cot_sems.at[slot]).wait()
    upstream = cot_rows[slot].astype(f32) * scale[0]
    branch = upstream.astype(bf16)
    second_t = second.T
    branch_t = branch.T
    total = residual + b_down[...]
    grad_second = jnp.zeros_like(residual)
    def raise_part(first):
        part = slice(first, first + chunk)
        inner = jnp.dot(second, w_up[:, part], preferred_element_type=f32) + b_up[:, part]
        return inner, across(branch, w_down[part, :])

    ahead = raise_part(0)
    for first in range(0, wide, chunk):
        part = slice(first, first + chunk)
        inner, grad_active = ahead
        if first + chunk < wide:
            ahead = raise_part(first + chunk)
        cdf, slope = normal_parts(inner)
        active = (inner * cdf).astype(bf16)
        grad_inner_f = grad_active * (cdf + slope)
        grad_inner = grad_inner_f.astype(bf16)
        active_all[:, part] = active
        inner_all[:, part] = grad_inner
        acc_down[:, part] += jnp.dot(branch_t, active, preferred_element_type=f32)
        acc_up[:, part] += jnp.dot(second_t, grad_inner, preferred_element_type=f32)
        vec_up_ref[:, part] += column_sum(grad_inner_f)
    total = total + jnp.dot(active_all[...], w_down[...], preferred_element_type=f32)
    grad_second = across(inner_all[...], w_up[...])
    out_rows[step] = total.astype(bf16)
    return_tile(tile_order(step), out_rows.at[step], out_ref, send_sems.at[step], recv_sems, True)
    grad_resid = upstream + norm_back(grad_second, normal, rstd, gain[...])
    grad_proj = grad_resid.astype(bf16)
    resid_ref[...] = grad_proj
    go_ref[...] = across(grad_proj, w_out[...]).astype(bf16)
    acc_out[...] += jnp.dot(att.T, grad_proj, preferred_element_type=f32)
    vec_ref[0:1] += column_sum(grad_resid)
    vec_ref[1:2] += column_sum(grad_second * normal)
    vec_ref[2:3] += column_sum(grad_second)
    vec_ref[3:4] += column_sum(upstream)

    @pl.when(step == steps - 1)
    def _():
        core = lax.axis_index("win") % 2
        part = width // shards
        down_part = wide // shards
        count = wide // width
        rows = stage.shape[1]
        size = rows // 4

        def copies(b, slot):
            moves = []
            for piece in range(4):
                source = stage.at[slot, pl.ds(piece * size, size)]
                for bit, target in ((0, keep_ref), (1, send_ref)):
                    moves.append((piece % 2, bit, pltpu.make_async_copy(source, target.at[b, piece // 2], sems.at[slot, piece])))
            return moves

        def act(b, slot, what):
            for parity, bit, move in copies(b, slot):
                @pl.when((parity != core) == (bit == 1))
                def _():
                    getattr(move, what)()

        for b in range(shards):
            slot = b % 2
            if b >= 2:
                act(b - 2, slot, "wait")
            for k in range(count):
                stage[slot, k * part : (k + 1) * part] = acc_up[b * part : (b + 1) * part, k * width : (k + 1) * width].astype(bf16)
            base = count * part
            half = width // 2
            for k in range(2):
                stage[slot, base : base + half, k * half : (k + 1) * half] = acc_down[
                    k * half : (k + 1) * half, b * down_part : (b + 1) * down_part
                ].astype(bf16)
            base += half
            stage[slot, base : base + part] = acc_out[b * part : (b + 1) * part, :].astype(bf16)
            stage[slot, base + part :] = jnp.zeros((rows - base - part, width), bf16)
            act(b, slot, "start")
        for b in range(shards - 2, shards):
            act(b, b % 2, "wait")
        for n in range(cot_count):
            return_tile(tile_order(n), out_rows.at[n], out_ref, send_sems.at[n], recv_sems, False)


def input_grad_kernel(groups, *refs):
    f32, bf16 = jnp.float32, jnp.bfloat16
    parts = refs[: 3 * groups]
    rows_ref, resid_ref, gain, shift, weight = refs[3 * groups : 3 * groups + 5]
    tok_ref, joined_ref, normed_ref, vec_ref = refs[-4:]
    width = rows_ref.shape[1]
    lanes = width // groups

    @pl.when(pl.program_id(0) == 0)
    def _():
        vec_ref[...] = jnp.zeros_like(vec_ref)

    for g in range(groups):
        dq, own, other = parts[3 * g : 3 * g + 3]
        columns = slice(g * lanes, (g + 1) * lanes)
        joined_ref[:, columns] = dq[...]
        both = (own[...].astype(f32) + other[...].astype(f32)).astype(bf16)
        joined_ref[:, width + g * lanes : width + (g + 1) * lanes] = both[:, :lanes]
        joined_ref[:, 2 * width + g * lanes : 2 * width + (g + 1) * lanes] = both[:, lanes:]
        vec_ref[0:1, columns] += column_sum(dq[...].astype(f32))
        vec_ref[1:2, columns] += column_sum(both[:, lanes:].astype(f32))
    grad = across(joined_ref[...], weight[...])
    normal, rstd = norm_parts(rows_ref[...].astype(f32))
    normed_ref[...] = (normal * gain[...] + shift[...]).astype(bf16)
    vec_ref[2:3] += column_sum(grad * normal)
    vec_ref[3:4] += column_sum(grad)
    tok_ref[...] = (resid_ref[...].astype(f32) + norm_back(grad, normal, rstd, gain[...])).astype(bf16)


def weight_grad_kernel(normed_ref, joined_ref, *refs):
    out_ref, turned = refs[-2:]

    @pl.when(pl.program_id(0) == 0)
    def _():
        turned[...] = normed_ref[...].T

    width = normed_ref.shape[1]
    shards = out_ref.shape[0]
    full = jnp.dot(turned[...], joined_ref[...], preferred_element_type=jnp.float32).astype(jnp.bfloat16)
    out_ref[...] = full.reshape(shards, width // shards, width)


def general_body(
    tokens,
    cotangent,
    w_qkv,
    b_q,
    b_v,
    w_out,
    b_out,
    gain_one,
    shift_one,
    gain_two,
    shift_two,
    w_up,
    b_up,
    w_down,
    b_down,
    rand_owner,
    rand_sub,
    global_ids,
    species,
):
    blk_count = lax.axis_size("blk")
    blk_pos = lax.axis_index("blk")
    win_pos = lax.axis_index("win")
    windows, length, model_width = tokens.shape
    blocks = rand_owner.shape[1]
    heads = rand_owner.shape[2]
    picks = rand_owner.shape[3]
    glob_count = global_ids.shape[1]
    own_blocks = blocks // blk_count
    block_len = length // own_blocks
    head_dim = model_width // heads
    pair_width = 2 * head_dim
    all_rows = windows * length
    key_count = 3 + glob_count + picks
    per_device = own_blocks * heads * picks
    slot_cap = max(2, 2 * per_device // blk_count)
    score_scale = head_dim ** (-0.5)
    f32 = jnp.float32
    bf16 = jnp.bfloat16
    tokens_f = tokens.reshape(all_rows, model_width).astype(f32)
    normed_f, norm_one_pull = jax.vjp(layer_norm, tokens_f, gain_one, shift_one)
    normed = normed_f.astype(bf16)
    joined = jnp.dot(normed, w_qkv, preferred_element_type=f32)
    query_vals = (joined[:, :model_width] + b_q).astype(bf16)
    key_vals = joined[:, model_width : 2 * model_width].astype(bf16)
    value_vals = (joined[:, 2 * model_width :] + b_v).astype(bf16)

    def to_heads(tensor):
        return tensor.reshape(windows, own_blocks, block_len, heads, head_dim).transpose(
            0, 1, 3, 2, 4
        )

    def from_heads(tensor):
        return tensor.transpose(0, 1, 3, 2, 4).reshape(all_rows, model_width)

    query_heads = to_heads(query_vals)
    local_pairs = jnp.concatenate([to_heads(key_vals), to_heads(value_vals)], axis=-1)
    rimmed = padded(local_pairs, (("blk", 1),), 1)
    block_ids = blk_pos * own_blocks + jnp.arange(own_blocks, dtype=jnp.int32)
    owned_glob = (global_ids[:, :, None] == block_ids[None, None, :]).astype(bf16)
    glob_terms = jnp.einsum("wgb,wbhsc->wghsc", owned_glob, local_pairs, preferred_element_type=f32)
    glob_pairs = lax.psum(glob_terms.astype(jnp.bfloat16), "blk").astype(jnp.float32).astype(bf16)
    owner_rows = rand_owner.reshape(windows, blk_count, per_device)
    sub_rows = rand_sub.reshape(windows, blk_count, per_device)
    owner_hits = (owner_rows[..., None] == jnp.arange(blk_count, dtype=jnp.int32)).astype(jnp.int32)
    slot_rows = jnp.sum(owner_hits * (jnp.cumsum(owner_hits, axis=2) - 1), axis=-1)
    my_owner = lax.dynamic_index_in_dim(owner_rows, blk_pos, 1, keepdims=False)
    my_slot = lax.dynamic_index_in_dim(slot_rows, blk_pos, 1, keepdims=False)
    fetch_index = my_owner * slot_cap + my_slot
    head_of_row = jnp.arange(per_device, dtype=jnp.int32) // picks % heads
    source_rows = sub_rows * heads + head_of_row[None, None, :]
    requester = jnp.arange(blk_count, dtype=jnp.int32)[None, :, None]
    target_rows = jnp.where(
        owner_rows == blk_pos, requester * slot_cap + slot_rows, blk_count * slot_cap
    )
    send_table = jnp.full((windows, blk_count * slot_cap + 1), own_blocks * heads, jnp.int32)
    send_table = jax.vmap(set_rows)(
        send_table, target_rows.reshape(windows, -1), source_rows.reshape(windows, -1)
    )[:, : blk_count * slot_cap]
    flat_pairs = jnp.concatenate(
        [
            local_pairs.reshape(windows, own_blocks * heads, block_len, pair_width),
            jnp.zeros((windows, 1, block_len, pair_width), bf16),
        ],
        axis=1,
    )
    outgoing = jax.vmap(take_rows)(flat_pairs, send_table).reshape(
        windows, blk_count, slot_cap, block_len, pair_width
    )
    incoming = lax.all_to_all(outgoing, "blk", split_axis=1, concat_axis=1, tiled=True).reshape(
        windows, blk_count * slot_cap, block_len, pair_width
    )
    rand_pairs = jax.vmap(take_rows)(incoming, fetch_index).reshape(
        windows, own_blocks, heads, picks, block_len, pair_width
    )
    near_pairs = jnp.stack(
        [rimmed[:, 0:own_blocks], rimmed[:, 1 : own_blocks + 1], rimmed[:, 2 : own_blocks + 2]],
        axis=3,
    )
    far_pairs = jnp.broadcast_to(
        glob_pairs.transpose(0, 2, 1, 3, 4)[:, None],
        (windows, own_blocks, heads, glob_count, block_len, pair_width),
    )
    gathered_keys = jnp.concatenate([near_pairs, far_pairs, rand_pairs], axis=3).reshape(
        windows, own_blocks, heads, key_count * block_len, pair_width
    )
    set_keys = gathered_keys[..., :head_dim]
    set_values = gathered_keys[..., head_dim:]
    block_flags = jnp.concatenate(
        [
            (block_ids > 0)[:, None],
            jnp.ones((own_blocks, 1), jnp.bool_),
            (block_ids < blocks - 1)[:, None],
            jnp.ones((own_blocks, glob_count + picks), jnp.bool_),
        ],
        axis=1,
    )
    key_valid = jnp.repeat(block_flags, block_len, axis=1)[None, :, None, None, :]

    def score_block():
        raw_scores = (
            jnp.einsum("wbhqe,wbhke->wbhqk", query_heads, set_keys, preferred_element_type=f32)
            * score_scale
        )
        return jnp.where(key_valid, raw_scores, masked_score)

    score_matrix = score_block()
    top_score = jnp.max(score_matrix, axis=-1, keepdims=True)
    log_total = top_score + jnp.log(
        jnp.sum(jnp.exp(score_matrix - top_score), axis=-1, keepdims=True)
    )
    probs_low = jnp.exp(score_matrix - log_total).astype(bf16)
    attended = jnp.einsum(
        "wbhqk,wbhke->wbhqe", probs_low, set_values, preferred_element_type=f32
    ).astype(bf16)
    merged = from_heads(attended)
    residual = tokens_f + (jnp.dot(merged, w_out, preferred_element_type=f32) + b_out)
    second_f, norm_two_pull = jax.vjp(layer_norm, residual, gain_two, shift_two)
    second = second_f.astype(bf16)
    inner_f = jnp.dot(second, w_up, preferred_element_type=f32) + b_up
    active_f, gelu_pull = jax.vjp(partial(jax.nn.gelu, approximate=False), inner_f)
    active = active_f.astype(bf16)
    output = residual + (jnp.dot(active, w_down, preferred_element_type=f32) + b_down)
    species_count = jnp.sum(
        (species[:, None] == jnp.arange(SPECIES, dtype=jnp.int32)[None, :]).astype(f32), axis=0
    )
    my_species = lax.dynamic_slice_in_dim(species, win_pos * windows, windows)
    own_count = jnp.sum(
        (my_species[:, None] == jnp.arange(SPECIES, dtype=jnp.int32)[None, :]).astype(f32)
        * species_count[None, :],
        axis=1,
    )
    window_scale = jnp.sqrt(species.shape[0] / (SPECIES * own_count))
    upstream = (cotangent.astype(f32) * window_scale[:, None, None]).reshape(all_rows, model_width)
    grad_branch = upstream.astype(bf16)
    grad_w_down = jnp.einsum("tf,td->fd", active, grad_branch, preferred_element_type=f32)
    grad_b_down = jnp.sum(grad_branch, axis=0, dtype=f32)
    grad_active = jnp.einsum("td,fd->tf", grad_branch, w_down, preferred_element_type=f32)
    grad_inner = gelu_pull(grad_active)[0].astype(bf16)
    grad_w_up = jnp.einsum("td,tf->df", second, grad_inner, preferred_element_type=f32)
    grad_b_up = jnp.sum(grad_inner, axis=0, dtype=f32)
    grad_second = jnp.einsum("tf,df->td", grad_inner, w_up, preferred_element_type=f32)
    grad_resid_norm, grad_gain_two, grad_shift_two = norm_two_pull(grad_second)
    grad_resid = upstream + grad_resid_norm
    grad_proj = grad_resid.astype(bf16)
    grad_w_out = jnp.einsum("ti,to->io", merged, grad_proj, preferred_element_type=f32)
    grad_b_out = jnp.sum(grad_proj, axis=0, dtype=f32)
    grad_attended = to_heads(
        jnp.einsum("to,io->ti", grad_proj, w_out, preferred_element_type=f32).astype(bf16)
    )
    probs_full = jnp.exp(score_block() - log_total)
    grad_probs = jnp.einsum(
        "wbhqe,wbhke->wbhqk", grad_attended, set_values, preferred_element_type=f32
    )
    grad_set_values = jnp.einsum(
        "wbhqk,wbhqe->wbhke", probs_full.astype(bf16), grad_attended, preferred_element_type=f32
    )
    row_dot = jnp.sum(probs_full * grad_probs, axis=-1, keepdims=True)
    grad_scores = (probs_full * (grad_probs - row_dot)).astype(bf16)
    grad_query = (
        jnp.einsum("wbhqk,wbhke->wbhqe", grad_scores, set_keys, preferred_element_type=f32)
        * score_scale
    )
    grad_set_keys = (
        jnp.einsum("wbhqk,wbhqe->wbhke", grad_scores, query_heads, preferred_element_type=f32)
        * score_scale
    )
    grad_set = jnp.concatenate([grad_set_keys, grad_set_values], axis=-1).reshape(
        windows, own_blocks, heads, key_count, block_len, pair_width
    )
    extended = (
        jnp.pad(grad_set[:, :, :, 1], ((0, 0), (1, 1), (0, 0), (0, 0), (0, 0)))
        + jnp.pad(grad_set[:, :, :, 0], ((0, 0), (0, 2), (0, 0), (0, 0), (0, 0)))
        + jnp.pad(grad_set[:, :, :, 2], ((0, 0), (2, 0), (0, 0), (0, 0), (0, 0)))
    )
    edge_grads = jnp.concatenate([extended[:, :1], extended[:, own_blocks + 1 :]], axis=1)
    edge_back = padded(edge_grads.astype(jnp.bfloat16), (("blk", 1),), 1).astype(edge_grads.dtype)
    pair_grad = extended[:, 1 : own_blocks + 1]
    pair_grad = pair_grad.at[:, 0].add(edge_back[:, 0]).at[:, own_blocks - 1].add(edge_back[:, 3])
    glob_grad = jnp.sum(grad_set[:, :, :, 3 : 3 + glob_count], axis=1).transpose(0, 2, 1, 3, 4)
    glob_total = lax.psum(glob_grad.astype(jnp.bfloat16), "blk").astype(jnp.float32)
    pair_grad = pair_grad + jnp.einsum(
        "wgb,wghsc->wbhsc", owned_glob.astype(f32), glob_total, precision=lax.Precision.HIGHEST
    )
    rand_grad = grad_set[:, :, :, 3 + glob_count :].reshape(
        windows, per_device, block_len, pair_width
    )
    back_out = jax.vmap(add_rows)(
        jnp.zeros((windows, blk_count * slot_cap, block_len, pair_width), f32),
        fetch_index,
        rand_grad,
    )
    back_in = lax.all_to_all(
        back_out.reshape(windows, blk_count, slot_cap, block_len, pair_width).astype(jnp.bfloat16),
        "blk",
        split_axis=1,
        concat_axis=1,
        tiled=True,
    ).astype(jnp.float32)
    owner_sum = jax.vmap(add_rows)(
        jnp.zeros((windows, own_blocks * heads + 1, block_len, pair_width), f32),
        send_table,
        back_in.reshape(windows, blk_count * slot_cap, block_len, pair_width),
    )
    pair_grad = pair_grad + owner_sum[:, : own_blocks * heads].reshape(
        windows, own_blocks, heads, block_len, pair_width
    )
    grad_keys = from_heads(pair_grad[..., :head_dim].astype(bf16))
    grad_values = from_heads(pair_grad[..., head_dim:].astype(bf16))
    grad_joined = jnp.concatenate(
        [from_heads(grad_query.astype(bf16)), grad_keys, grad_values], axis=1
    )
    grad_w_qkv = jnp.einsum("td,tc->dc", normed, grad_joined, preferred_element_type=f32)
    grad_b_q = jnp.sum(grad_joined[:, :model_width], axis=0, dtype=f32)
    grad_b_v = jnp.sum(grad_joined[:, 2 * model_width :], axis=0, dtype=f32)
    grad_normed = jnp.einsum("tc,dc->td", grad_joined, w_qkv, preferred_element_type=f32)
    grad_tok_norm, grad_gain_one, grad_shift_one = norm_one_pull(grad_normed)
    grad_tokens = (grad_resid + grad_tok_norm).astype(bf16).reshape(windows, length, model_width)
    local_grads = (
        grad_w_qkv,
        grad_b_q,
        grad_b_v,
        grad_w_out,
        grad_b_out,
        grad_gain_one,
        grad_shift_one,
        grad_gain_two,
        grad_shift_two,
        grad_w_up,
        grad_b_up,
        grad_w_down,
        grad_b_down,
    )
    packed_grads = jnp.concatenate(
        [grad_item.reshape(blk_count, -1) for grad_item in local_grads], axis=1
    )
    total_cols = packed_grads.shape[1]
    win_count = lax.axis_size("win")
    pad_cols = -total_cols % win_count
    shard_sum = lax.psum_scatter(
        packed_grads.astype(jnp.bfloat16), "blk", scatter_dimension=0, tiled=True
    ).astype(jnp.float32)
    split_shard = jnp.pad(shard_sum, ((0, 0), (0, pad_cols))).reshape(win_count, -1)
    group_piece = lax.psum_scatter(
        split_shard.astype(jnp.bfloat16), "win", scatter_dimension=0, tiled=True
    ).astype(jnp.float32)
    summed = (
        lax.all_gather(group_piece.astype(jnp.bfloat16), "win", axis=0, tiled=True)
        .astype(group_piece.dtype)
        .reshape(1, -1)[:, :total_cols]
    )
    shards = []
    offset = 0
    for grad_item in local_grads:
        entry_count = grad_item.size // blk_count
        shards.append(
            summed[0, offset : offset + entry_count].reshape(
                (grad_item.shape[0] // blk_count,) + grad_item.shape[1:]
            )
        )
        offset = offset + entry_count
    out_tokens = output.astype(bf16).reshape(windows, length, model_width)
    return (
        out_tokens,
        grad_tokens,
        shards[0],
        shards[1],
        shards[2],
        shards[3],
        shards[4],
        shards[5],
        shards[6],
        shards[7],
        shards[8],
        shards[9],
        shards[10],
        shards[11],
        shards[12],
    )


def layer_step(*arguments):
    windows = arguments[0].shape[0]
    paired = lax.axis_size("blk") == 2 * windows and lax.axis_size("win") == 4 and windows == 4
    return (paired_body if paired else general_body)(*arguments)


def paired_body(
    tokens,
    cotangent,
    w_qkv,
    b_q,
    b_v,
    w_out,
    b_out,
    gain_one,
    shift_one,
    gain_two,
    shift_two,
    w_up,
    b_up,
    w_down,
    b_down,
    rand_owner,
    rand_sub,
    global_ids,
    species,
):
    f32 = jnp.float32
    bf16 = jnp.bfloat16
    win_count = lax.axis_size("win")
    blk_count = lax.axis_size("blk")
    win_pos = lax.axis_index("win")
    blk_pos = lax.axis_index("blk")
    layers, length, width = tokens.shape
    core, layer, side = win_pos % 2, blk_pos // 2, blk_pos % 2
    blocks, heads, picks = rand_owner.shape[1:]
    own_blocks = blocks // blk_count
    half_blocks = blocks // 2
    block_len = length // own_blocks
    head_dim = width // heads
    all_rows = layers * length
    lanes = HEADS_PER_GROUP * head_dim
    groups = heads // HEADS_PER_GROUP
    score_scale = head_dim ** (-0.5)

    def regroup(value):
        parts = []
        for step in range(layers):
            part = lax.dynamic_index_in_dim(value, (layer + step) % layers, 0, keepdims=False)
            parts.append(lax.ppermute(part, ("win", "blk"), regroup_pairs(win_count, layers, step)))
        return parts

    def send_back(value):
        parts = []
        for step in range(layers):
            pairs = [(b, a) for a, b in regroup_pairs(win_count, layers, step)]
            parts.append(lax.ppermute(value[step * length : (step + 1) * length], ("win", "blk"), pairs))
        return parts

    def in_order(parts):
        result = jnp.zeros((layers, length, width), parts[0].dtype)
        for step, part in enumerate(parts):
            result = lax.dynamic_update_index_in_dim(result, part, (layer + step) % layers, 0)
        return result

    def takes(micros):
        return pl.CostEstimate(flops=micros * 1_000_000_000, bytes_accessed=micros * 1_000_000, transcendentals=0)

    rows_in = jnp.concatenate(regroup(tokens), axis=0)
    cot_in = regroup(cotangent)

    rand_size = blocks * heads * picks
    named = jnp.concatenate(
        [
            lax.dynamic_index_in_dim((rand_owner * own_blocks + rand_sub).reshape(layers, rand_size), layer, 0, keepdims=False),
            lax.dynamic_index_in_dim(global_ids, layer, 0, keepdims=False),
        ]
    )
    named = jnp.where(side == core, named, swap(named, 1, 0))

    def place_of(block):
        owner = block // own_blocks
        half = jnp.where(owner % 2 == core, 0, half_blocks)
        return half + ((layer - owner // 2) % layers) * own_blocks + block % own_blocks

    slot = jnp.arange(half_blocks, dtype=jnp.int32)
    slot_block = (((layer - slot // own_blocks) % layers) * 2 + core) * own_blocks + slot % own_blocks
    table = jnp.concatenate(
        [
            place_of(named),
            slot_block,
            place_of(jnp.maximum(slot_block - 1, 0)),
            place_of(jnp.minimum(slot_block + 1, blocks - 1)),
        ]
    )
    sizes = (heads, picks, rand_size, half_blocks)

    tile = length

    def by_rows(columns):
        return pl.BlockSpec((tile, columns), lambda i: (i, 0))

    def by_tile(columns):
        return pl.BlockSpec((tile, columns), lambda i: (tile_order(i), 0))

    def whole(*shape, once=True):
        mode = pl.Buffered(1) if once else None
        return pl.BlockSpec(shape, lambda i: (0,) * len(shape), pipeline_mode=mode)

    scalars = pl.BlockSpec(memory_space=pltpu.SMEM)
    wide = w_up.shape[1]
    params = pltpu.CompilerParams(vmem_limit_bytes=60 << 20)
    row = lambda vector: vector.reshape(1, -1)
    query, key_value = pl.pallas_call(
        partial(qkv_kernel, score_scale),
        grid=(all_rows // tile,),
        in_specs=[by_rows(width), whole(1, width), whole(1, width), whole(width, 3 * width), whole(2, width)],
        out_specs=[by_rows(width), by_rows(2 * width)],
        out_shape=[jax.ShapeDtypeStruct((all_rows, width), bf16), jax.ShapeDtypeStruct((all_rows, 2 * width), bf16)],
        compiler_params=params,
        cost_estimate=takes(12),
        name="qkv",
    )(rows_in, row(gain_one), row(shift_one), w_qkv, jnp.stack([b_q, b_v]))
    key_value_other = swap(key_value, 1, 0)

    def lane_block(first):
        return pl.BlockSpec((all_rows, lanes), lambda g, t: (0, first + g))

    store = pltpu.VMEM((blocks, block_len, lanes), bf16)
    attended, log_total = pl.pallas_call(
        partial(attend_kernel, sizes, blocks, head_dim),
        grid_spec=pltpu.PrefetchScalarGridSpec(
            num_scalar_prefetch=1,
            grid=(groups,),
            in_specs=[lane_block(0), lane_block(0), lane_block(0), lane_block(groups), lane_block(groups)],
            out_specs=[lane_block(0), pl.BlockSpec((1, half_blocks, lanes), lambda g, t: (g, 0, 0))],
            scratch_shapes=[store, store],
        ),
        out_shape=[
            jax.ShapeDtypeStruct((all_rows, width), bf16),
            jax.ShapeDtypeStruct((groups, half_blocks, lanes), f32),
        ],
        compiler_params=pltpu.CompilerParams(vmem_limit_bytes=56 << 20),
        cost_estimate=takes(37),
        name="attend",
    )(table, query, key_value, key_value_other, key_value, key_value_other)

    species_count = jnp.sum(
        (species[:, None] == jnp.arange(SPECIES, dtype=jnp.int32)[None, :]).astype(f32), axis=0
    )
    my_window = ((win_pos // 2) * 2 + side) * layers + layer
    my_species = lax.dynamic_index_in_dim(species, my_window, 0, keepdims=False)
    own_count = jnp.sum(
        (my_species == jnp.arange(SPECIES, dtype=jnp.int32)).astype(f32) * species_count
    )
    window_scale = jnp.sqrt(species.shape[0] / (SPECIES * own_count))
    payload = 2 * wide // blk_count + width // blk_count
    payload += -payload % (16 * win_count)
    stays = jax.ShapeDtypeStruct((blk_count, win_count // 2, payload // win_count, width), bf16)
    any_place = pl.BlockSpec(memory_space=pl.ANY)
    out_tokens, grad_resid, grad_attended, vec_two, vec_up, early_keep, early_send = pl.pallas_call(
        partial(ffn_kernel, 256, blk_count, layers),
        grid=(layers,),
        in_specs=[
            scalars, by_tile(width), by_tile(width), *[any_place] * layers, whole(width, width), whole(1, width), whole(1, width),
            whole(1, width), whole(width, wide), whole(1, wide), whole(wide, width), whole(1, width),
        ],
        out_specs=[any_place, by_tile(width), by_tile(width), whole(4, width), whole(1, wide), any_place, any_place],
        out_shape=[
            jax.ShapeDtypeStruct((layers, length, width), bf16),
            jax.ShapeDtypeStruct((all_rows, width), bf16),
            jax.ShapeDtypeStruct((all_rows, width), bf16),
            jax.ShapeDtypeStruct((4, width), f32),
            jax.ShapeDtypeStruct((1, wide), f32),
            stays,
            stays,
        ],
        scratch_shapes=[
            pltpu.VMEM((width, wide), f32),
            pltpu.VMEM((width, wide), f32),
            pltpu.VMEM((width, width), f32),
            pltpu.VMEM((2, payload, width), bf16),
            pltpu.SemaphoreType.DMA((2, 4)),
            pltpu.VMEM((length, wide), bf16),
            pltpu.VMEM((length, wide), bf16),
            pltpu.VMEM((2, length, width), bf16),
            pltpu.SemaphoreType.DMA((2,)),
            pltpu.VMEM((layers, length, width), bf16),
            pltpu.SemaphoreType.DMA((layers,)),
            pltpu.SemaphoreType.DMA((layers,)),
        ],
        compiler_params=pltpu.CompilerParams(vmem_limit_bytes=60 << 20, collective_id=1, has_side_effects=True),
        cost_estimate=takes(90),
        name="ffn",
    )(
        window_scale.reshape(1), rows_in, attended, *cot_in, w_out, row(b_out), row(gain_two), row(shift_two),
        w_up, row(b_up), w_down, row(b_down),
    )

    pair = win_pos // 2

    def add_low(keep, other):
        return (keep.astype(f32) + other.astype(f32)).astype(bf16)

    def halve(cells, axis, bit, win_bit, blk_bit):
        keep = lax.dynamic_index_in_dim(cells, bit, axis, keepdims=False)
        send = lax.dynamic_index_in_dim(cells, 1 - bit, axis, keepdims=False)
        return keep, swap(send, win_bit, blk_bit)

    def first_halves(cells):
        cells = cells.reshape((layers, 2) + cells.shape[1:])
        middle = cells.shape[3] // 2
        return halve(cells[:, :, :, :middle], 1, side, 0, 1), halve(cells[:, :, :, middle:], 2, pair, 2, 0)

    def second_halves(left, right):
        return halve(add_low(*left), 1, pair, 2, 0), halve(add_low(*right), 1, side, 0, 1)

    def last_halves(left, right):
        cells = jnp.concatenate([add_low(*left), add_low(*right)], axis=1)
        hop = 1
        while cells.shape[0] > 1:
            cells = cells.reshape((cells.shape[0] // 2, 2) + cells.shape[1:])
            cells = add_low(*halve(cells, 1, (layer // hop) % 2, 0, 2 * hop))
            hop *= 2
        return lax.all_gather(cells[0], "win", axis=0, tiled=True).astype(f32)

    grad_parts = []
    early_other = swap(early_send, 1, 0)
    for group in range(groups):
        after = []
        if group == 1:
            after = [early_other]
        if group == 2:
            early_first = first_halves(add_low(early_keep, early_other))
            after = [received for _, received in early_first]
        def column(first):
            return pl.BlockSpec((all_rows, lanes), lambda g, t: (0, first))

        def full(columns):
            return pl.BlockSpec((all_rows, columns), lambda g, t: (0, 0))

        grad_store = pltpu.VMEM((blocks, block_len, lanes), f32)
        glob_store = pltpu.VMEM((2, block_len, lanes), f32)
        dq, own, other = pl.pallas_call(
            partial(attend_back_kernel, sizes, blocks, head_dim, score_scale, group),
            grid_spec=pltpu.PrefetchScalarGridSpec(
                num_scalar_prefetch=1,
                grid=(1,),
                in_specs=[
                    column(group), column(group), column(group), column(groups + group), column(groups + group), column(group),
                    pl.BlockSpec((1, half_blocks, lanes), lambda g, t: (group, 0, 0)),
                    *[any_place] * len(after),
                ],
                out_specs=[full(lanes), full(2 * lanes), full(2 * lanes)],
                scratch_shapes=[store, store, grad_store, grad_store, glob_store, glob_store],
            ),
            out_shape=[jax.ShapeDtypeStruct((all_rows, n * lanes), bf16) for n in (1, 2, 2)],
            compiler_params=params,
            cost_estimate=takes(25),
            name="attend_back",
        )(table, query, key_value, key_value_other, key_value, key_value_other, grad_attended, log_total, *after)
        grad_parts += [dq, own, swap(other, 1, 0)]

    early_second = second_halves(*early_first)
    grad_tokens, grad_joined, normed, vec_one = pl.pallas_call(
        partial(input_grad_kernel, groups),
        grid=(all_rows // tile,),
        in_specs=[by_rows(p.shape[1]) for p in grad_parts]
        + [by_rows(width), by_rows(width), whole(1, width), whole(1, width), whole(width, 3 * width)]
        + [any_place] * 2,
        out_specs=[by_rows(width), by_rows(3 * width), by_rows(width), whole(4, width)],
        out_shape=[
            jax.ShapeDtypeStruct((all_rows, width), bf16),
            jax.ShapeDtypeStruct((all_rows, 3 * width), bf16),
            jax.ShapeDtypeStruct((all_rows, width), bf16),
            jax.ShapeDtypeStruct((4, width), f32),
        ],
        compiler_params=params,
        cost_estimate=takes(16),
        name="input_grad",
    )(*grad_parts, rows_in, grad_resid, row(gain_one), row(shift_one), w_qkv, early_second[0][1], early_second[1][1])
    grad_tokens_parts = send_back(grad_tokens)
    part = width // blk_count
    late_rows = 3 * part + 32
    late_rows += -late_rows % (16 * win_count)
    late_cells = pl.pallas_call(
        weight_grad_kernel,
        grid=(3,),
        in_specs=[whole(all_rows, width), pl.BlockSpec((all_rows, width), lambda i: (0, i)), ],
        out_specs=pl.BlockSpec((blk_count, part, width), lambda i: (0, i, 0)),
        out_shape=jax.ShapeDtypeStruct((blk_count, late_rows, width), bf16),
        scratch_shapes=[pltpu.VMEM((width, all_rows), bf16)],
        compiler_params=params,
        cost_estimate=takes(12),
        name="weight_grad",
    )(normed, grad_joined)
    vec_rows = jnp.concatenate(
        [vec_two.reshape(4, blk_count, part), vec_one.reshape(4, blk_count, part)], axis=0
    ).transpose(1, 0, 2).reshape(blk_count, 8 * part)
    vec_rows = jnp.concatenate([vec_rows, vec_up.reshape(blk_count, wide // blk_count)], axis=1)
    vec_rows = jnp.pad(vec_rows, ((0, 0), (0, -vec_rows.shape[1] % width))).reshape(blk_count, -1, width)
    vec_rows = jnp.pad(vec_rows, ((0, 0), (0, late_rows - 3 * part - vec_rows.shape[1]), (0, 0))).astype(bf16)
    late_cells = lax.dynamic_update_slice(late_cells, vec_rows, (0, 3 * part, 0))

    late_cells = late_cells.reshape(blk_count, win_count // 2, 2, late_rows // win_count, width)
    late_keep = lax.dynamic_index_in_dim(late_cells, core, 2, keepdims=False)
    late_send = lax.dynamic_index_in_dim(late_cells, 1 - core, 2, keepdims=False)
    early = last_halves(*early_second)
    late = last_halves(*second_halves(*first_halves(add_low(late_keep, swap(late_send, 1, 0)))))

    def rows_again(rows, count):
        return rows.reshape(count, -1, width).transpose(1, 0, 2).reshape(-1, count * width)

    count = wide // width
    half = width // 2
    done_up = rows_again(early[: count * part], count)
    done_down = early[count * part : count * part + half].reshape(half, 2, wide // blk_count).transpose(2, 1, 0).reshape(-1, width)
    done_out = early[count * part + half : (count + 1) * part + half]
    done_qkv = rows_again(late[: 3 * part], 3)
    vec = late[3 * part :].reshape(-1)
    piece = lambda n: vec[n * part : (n + 1) * part]
    return (
        out_tokens,
        in_order(grad_tokens_parts),
        done_qkv,
        piece(4),
        piece(5),
        done_out,
        piece(0),
        piece(6),
        piece(7),
        piece(1),
        piece(2),
        done_up,
        vec[8 * part : 8 * part + wide // blk_count],
        done_down,
        piece(3),
    )


def solution(mesh):
    placed = (
        P("win", "blk", None),
        P("win", "blk", None),
        P(),
        P(),
        P(),
        P(),
        P(),
        P(),
        P(),
        P(),
        P(),
        P(),
        P(),
        P(),
        P(),
        P("win", None, None, None),
        P("win", None, None, None),
        P("win", None),
        P(),
    )
    return jax.shard_map(
        layer_step,
        mesh=mesh,
        in_specs=placed,
        out_specs=(
            P("win", "blk", None),
            P("win", "blk", None),
            P("blk", None),
            P("blk"),
            P("blk"),
            P("blk", None),
            P("blk"),
            P("blk"),
            P("blk"),
            P("blk"),
            P("blk"),
            P("blk", None),
            P("blk"),
            P("blk", None),
            P("blk"),
        ),
        check_vma=False,
    )
```

```python
from functools import partial

import jax
import jax.numpy as jnp
from jax import lax
from jax.experimental import pallas as pl
from jax.experimental.pallas import tpu as pltpu
from jax.sharding import PartitionSpec as P

SPECIES = 4


epsilon = 1e-05
masked_score = -1000000000.0


def padded(cells, sides, width):
    for axis, dim in sides:
        count = lax.axis_size(axis)
        ends = count - 1
        head = lax.slice_in_dim(cells, 0, width, axis=dim)
        tail = lax.slice_in_dim(cells, cells.shape[dim] - width, cells.shape[dim], axis=dim)
        cells = jnp.concatenate(
            [
                lax.ppermute(tail, axis, [(i, (i + 1) % count) for i in range(ends)]),
                cells,
                lax.ppermute(head, axis, [((i + 1) % count, i) for i in range(ends)]),
            ],
            axis=dim,
        )
    return cells


def layer_norm(values, norm_gain, norm_shift):
    average = jnp.mean(values, axis=-1, keepdims=True)
    centred = values - average
    variance = jnp.mean(centred * centred, axis=-1, keepdims=True)
    return centred * lax.rsqrt(variance + epsilon) * norm_gain + norm_shift


def take_rows(source, index_rows):
    return jnp.take(source, index_rows, axis=0)


def add_rows(base, index_rows, update):
    return base.at[index_rows].add(update)


def set_rows(base, index_rows, update):
    return base.at[index_rows].set(update)


HEADS_PER_GROUP = 4


def regroup_pairs(win_count, layers, step):
    pairs = []
    for win in range(win_count):
        for blk in range(2 * layers):
            layer, side = blk // 2, blk % 2
            target = ((layer + step) % layers) * 2 + win % 2
            pairs.append((win * 2 * layers + blk, ((win // 2) * 2 + side) * 2 * layers + target))
    return pairs


def flip_pairs(win_count, blk_count, win_bit, blk_bit):
    return [
        (win * blk_count + blk, (win ^ win_bit) * blk_count + (blk ^ blk_bit))
        for win in range(win_count)
        for blk in range(blk_count)
    ]


def swap(value, win_bit, blk_bit):
    pairs = flip_pairs(lax.axis_size("win"), lax.axis_size("blk"), win_bit, blk_bit)
    return lax.ppermute(value, ("win", "blk"), pairs)


def head_masks(lanes, head_dim, dtype):
    lane = lax.broadcasted_iota(jnp.int32, (1, lanes), 1)
    return [(lane // head_dim == h).astype(dtype) for h in range(lanes // head_dim)]


def block_places(table, slot, group, sizes):
    heads, picks, rand_size, half_blocks = sizes
    block = table[rand_size + 2 + slot]
    near = [table[rand_size + 2 + half_blocks + slot], slot, table[rand_size + 2 + 2 * half_blocks + slot]]
    row = (block * heads + group * HEADS_PER_GROUP) * picks
    rand = [[table[row + h * picks + r] for h in range(HEADS_PER_GROUP)] for r in range(picks)]
    return block, near, rand


def spread_heads(rows, masks):
    return jnp.concatenate([rows * m for m in masks], axis=0)


def pick_heads(square, masks, height):
    total = square[0:height] * masks[0]
    for h in range(1, len(masks)):
        total = total + square[h * height : (h + 1) * height] * masks[h]
    return total


def key_rows(source, near, glob, rand, low_half):
    parts = [source[p] for p in near] + [source[p] for p in glob]
    for places in rand:
        columns = []
        for c in range(len(places) // 2):
            low = source[places[2 * c], :, c * 128 : (c + 1) * 128]
            high = source[places[2 * c + 1], :, c * 128 : (c + 1) * 128]
            columns.append(jnp.where(low_half, low, high))
        parts.append(jnp.concatenate(columns, axis=1))
    return jnp.concatenate(parts, axis=0)


def mask_scores(scores, block, blocks, block_len):
    first = jnp.where(block > 0, scores[:block_len], masked_score)
    last = jnp.where(block < blocks - 1, scores[2 * block_len : 3 * block_len], masked_score)
    return jnp.concatenate([first, scores[block_len : 2 * block_len], last, scores[3 * block_len :]], axis=0)


def across(left, right):
    return lax.dot_general(left, right, (((1,), (1,)), ((), ())), preferred_element_type=jnp.float32)


def down(left, right):
    return lax.dot_general(left, right, (((0,), (0,)), ((), ())), preferred_element_type=jnp.float32)


def load_halves(target, own, other, half_blocks, block_len):
    lanes = own.shape[-1]
    target[0:half_blocks] = own[...].reshape(half_blocks, block_len, lanes)
    target[half_blocks:] = other[...].reshape(half_blocks, block_len, lanes)


def attend_kernel(sizes, blocks, head_dim, table, q_ref, k_own, k_other, v_own, v_other, o_ref, lse_ref, k_all, v_all):
    heads, picks, rand_size, half_blocks = sizes
    block_len = k_all.shape[1]
    lanes = q_ref.shape[1]
    group = pl.program_id(0)
    load_halves(k_all, k_own, k_other, half_blocks, block_len)
    load_halves(v_all, v_own, v_other, half_blocks, block_len)
    low_half = lax.broadcasted_iota(jnp.int32, (block_len, 128), 1) < head_dim
    masks = head_masks(lanes, head_dim, jnp.bfloat16)
    masks_f = head_masks(lanes, head_dim, jnp.float32)
    glob = [table[rand_size], table[rand_size + 1]]

    def one(slot, carry):
        block, near, rand = block_places(table, slot, group, sizes)
        rows = pl.ds(pl.multiple_of(slot * block_len, block_len), block_len)
        queries = spread_heads(q_ref[rows, :], masks)
        keys = key_rows(k_all, near, glob, rand, low_half)
        scores = mask_scores(across(keys, queries), block, blocks, block_len)
        top = jnp.max(scores, axis=0, keepdims=True)
        weights = jnp.exp(scores - top)
        total = jnp.sum(weights, axis=0, keepdims=True)
        probs = (weights * (1.0 / total)).astype(jnp.bfloat16)
        values = key_rows(v_all, near, glob, rand, low_half)
        o_ref[rows, :] = pick_heads(down(probs, values), masks_f, block_len).astype(jnp.bfloat16)
        lse_ref[0, pl.ds(slot, 1), :] = top + jnp.log(total)
        return carry

    lax.fori_loop(0, half_blocks, one, 0, unroll=min(8, half_blocks))


def attend_back_kernel(
    sizes, blocks, head_dim, scale, group,
    table, q_ref, k_own, k_other, v_own, v_other, go_ref, lse_ref, *refs,
):
    dq_ref, own_ref, other_ref, k_all, v_all, dk_all, dv_all, dk_glob, dv_glob = refs[-9:]
    heads, picks, rand_size, half_blocks = sizes
    block_len = k_all.shape[1]
    lanes = q_ref.shape[1]
    f32 = jnp.float32
    load_halves(k_all, k_own, k_other, half_blocks, block_len)
    load_halves(v_all, v_own, v_other, half_blocks, block_len)
    dk_all[...] = jnp.zeros_like(dk_all)
    dv_all[...] = jnp.zeros_like(dv_all)
    dk_glob[...] = jnp.zeros_like(dk_glob)
    dv_glob[...] = jnp.zeros_like(dv_glob)
    low_half = lax.broadcasted_iota(jnp.int32, (block_len, 128), 1) < head_dim
    masks = head_masks(lanes, head_dim, jnp.bfloat16)
    masks_f = head_masks(lanes, head_dim, f32)
    glob = [table[rand_size], table[rand_size + 1]]

    def add_back(grads, near, rand, into, into_glob):
        for n in range(3):
            into[near[n]] += grads[n * block_len : (n + 1) * block_len]
        for n in range(2):
            into_glob[n] += grads[(3 + n) * block_len : (4 + n) * block_len]
        for r in range(picks):
            part = grads[(5 + r) * block_len : (6 + r) * block_len]
            for c in range(lanes // 128):
                cell = part[:, c * 128 : (c + 1) * 128]
                columns = pl.ds(c * 128, 128)
                into[rand[r][2 * c], :, columns] += jnp.where(low_half, cell, 0.0)
                into[rand[r][2 * c + 1], :, columns] += jnp.where(low_half, 0.0, cell)

    def one(slot, carry):
        block, near, rand = block_places(table, slot, group, sizes)
        rows = pl.ds(pl.multiple_of(slot * block_len, block_len), block_len)
        queries = spread_heads(q_ref[rows, :], masks)
        grads_out = spread_heads(go_ref[rows, :], masks)
        keys = key_rows(k_all, near, glob, rand, low_half)
        values = key_rows(v_all, near, glob, rand, low_half)
        scores = mask_scores(across(keys, queries), block, blocks, block_len)
        probs = jnp.exp(scores - lse_ref[0, pl.ds(slot, 1), :])
        grad_probs = across(values, grads_out)
        row_dot = jnp.sum(probs * grad_probs, axis=0, keepdims=True)
        grad_scores = (probs * (grad_probs - row_dot)).astype(jnp.bfloat16)
        add_back(jnp.dot(probs.astype(jnp.bfloat16), grads_out, preferred_element_type=f32), near, rand, dv_all, dv_glob)
        add_back(jnp.dot(grad_scores, queries, preferred_element_type=f32), near, rand, dk_all, dk_glob)
        dq_ref[rows, :] = (pick_heads(down(grad_scores, keys), masks_f, block_len) * scale).astype(jnp.bfloat16)
        return carry

    lax.fori_loop(0, half_blocks, one, 0, unroll=min(8, half_blocks))
    for n in range(2):
        dk_all[glob[n]] += dk_glob[n]
        dv_all[glob[n]] += dv_glob[n]
    for target, start in ((own_ref, 0), (other_ref, half_blocks)):
        for n, source in enumerate((dk_all, dv_all)):
            cells = source[start : start + half_blocks].astype(jnp.bfloat16)
            target[:, n * lanes : (n + 1) * lanes] = cells.reshape(half_blocks * block_len, lanes)


def norm_parts(values):
    average = jnp.mean(values, axis=-1, keepdims=True)
    centred = values - average
    rstd = lax.rsqrt(jnp.mean(centred * centred, axis=-1, keepdims=True) + epsilon)
    return centred * rstd, rstd


def norm_back(grad, normal, rstd, gain):
    scaled = grad * gain
    first = jnp.mean(scaled, axis=-1, keepdims=True)
    second = jnp.mean(scaled * normal, axis=-1, keepdims=True)
    return rstd * (scaled - first - normal * second)


def normal_parts(values):
    cdf = 0.5 + 0.5 * lax.erf(values * 0.5**0.5)
    return cdf, values * jnp.exp(-0.5 * values * values) * 0.3989422804014327


def column_sum(values):
    return jnp.sum(values, axis=0, keepdims=True)


def qkv_kernel(scale, rows_ref, gain, shift, weight, bias, q_ref, kv_ref):
    width = rows_ref.shape[1]
    normal, _ = norm_parts(rows_ref[...].astype(jnp.float32))
    normed = (normal * gain[...] + shift[...]).astype(jnp.bfloat16)

    def part(n):
        columns = slice(n * width, (n + 1) * width)
        return jnp.dot(normed, weight[:, columns], preferred_element_type=jnp.float32)

    q_ref[...] = (part(0) + bias[0:1]).astype(jnp.bfloat16) * jnp.asarray(scale, jnp.bfloat16)
    kv_ref[:, :width] = part(1).astype(jnp.bfloat16)
    kv_ref[:, width:] = (part(2) + bias[1:2]).astype(jnp.bfloat16)


MESH = pl.DeviceIdType.MESH


def tile_order(number):
    return jnp.where(number == 0, 2, jnp.where(number == 2, 3, jnp.where(number == 3, 0, number)))


def position():
    win, blk = lax.axis_index("win"), lax.axis_index("blk")
    return win, blk, win % 2, blk // 2, blk % 2


def owner_of(tile, layers):
    win, blk, core, layer, side = position()
    return (win // 2) * 2 + side, ((layer + layers - tile) % layers) * 2 + core


def greet_owners(layers, others=0):
    barrier = pltpu.get_barrier_semaphore()
    _, _, core, _, side = position()
    for tile in range(1, layers):
        pl.semaphore_signal(barrier, inc=1, device_id=owner_of(tile, layers), device_id_type=MESH)

    @pl.when(side != core)
    def _():
        pl.semaphore_signal(barrier, inc=1, device_id=owner_of(0, layers), device_id_type=MESH)
        pl.semaphore_wait(barrier, layers + others)

    @pl.when(side == core)
    def _():
        pl.semaphore_wait(barrier, layers - 1 + others)


def return_tile(tile, source, target, send_sem, recv_sems, start):
    _, _, core, layer, side = position()
    layers = target.shape[0]
    stays = (tile == 0) & (side == core)

    @pl.when(stays)
    def _():
        move = pltpu.make_async_copy(source, target.at[layer], recv_sems.at[tile])
        move.start() if start else move.wait()

    @pl.when(jnp.logical_not(stays))
    def _():
        move = pltpu.make_async_remote_copy(
            src_ref=source, dst_ref=target.at[layer], send_sem=send_sem, recv_sem=recv_sems.at[tile],
            device_id=owner_of(tile, layers), device_id_type=MESH,
        )
        move.start() if start else move.wait()


def ffn_kernel(
    chunk, shards, cot_count,
    scale, rows_ref, att_ref, *refs,
):
    cot_parts = refs[:cot_count]
    (
        w_out, b_out, gain, shift, w_up, b_up, w_down, b_down,
        out_ref, resid_ref, go_ref, vec_ref, vec_up_ref, keep_ref, send_ref,
        acc_up, acc_down, acc_out, stage, sems, active_all, inner_all, cot_rows, cot_sems, out_rows, send_sems, recv_sems,
    ) = refs[cot_count:]
    f32, bf16 = jnp.float32, jnp.bfloat16
    step, steps = pl.program_id(0), pl.num_programs(0)
    width, wide = w_up.shape

    slot = step % 2

    def fetch(number):
        for n, part in enumerate(cot_parts):
            @pl.when((number < steps) & (tile_order(number) == n))
            def _():
                pltpu.make_async_copy(part, cot_rows.at[number % 2], cot_sems.at[number % 2]).start()

    @pl.when(step == 0)
    def _():
        greet_owners(steps)

    @pl.when(step == 0)
    def _():
        fetch(step)

    fetch(step + 1)

    @pl.when(step == 0)
    def _():
        for ref in (acc_up, acc_down, acc_out, vec_ref, vec_up_ref):
            ref[...] = jnp.zeros_like(ref)

    att = att_ref[...]
    residual = rows_ref[...].astype(f32) + (jnp.dot(att, w_out[...], preferred_element_type=f32) + b_out[...])
    normal, rstd = norm_parts(residual)
    second = (normal * gain[...] + shift[...]).astype(bf16)
    pltpu.make_async_copy(cot_parts[0], cot_rows.at[slot], cot_sems.at[slot]).wait()
    upstream = cot_rows[slot].astype(f32) * scale[0]
    branch = upstream.astype(bf16)
    second_t = second.T
    branch_t = branch.T
    total = residual + b_down[...]
    grad_second = jnp.zeros_like(residual)
    def raise_part(first):
        part = slice(first, first + chunk)
        inner = jnp.dot(second, w_up[:, part], preferred_element_type=f32) + b_up[:, part]
        return inner, across(branch, w_down[part, :])

    ahead = raise_part(0)
    for first in range(0, wide, chunk):
        part = slice(first, first + chunk)
        inner, grad_active = ahead
        if first + chunk < wide:
            ahead = raise_part(first + chunk)
        cdf, slope = normal_parts(inner)
        active = (inner * cdf).astype(bf16)
        grad_inner_f = grad_active * (cdf + slope)
        grad_inner = grad_inner_f.astype(bf16)
        active_all[:, part] = active
        inner_all[:, part] = grad_inner
        acc_down[:, part] += jnp.dot(branch_t, active, preferred_element_type=f32)
        acc_up[:, part] += jnp.dot(second_t, grad_inner, preferred_element_type=f32)
        vec_up_ref[:, part] += column_sum(grad_inner_f)
    total = total + jnp.dot(active_all[...], w_down[...], preferred_element_type=f32)
    grad_second = across(inner_all[...], w_up[...])
    out_rows[step] = total.astype(bf16)
    return_tile(tile_order(step), out_rows.at[step], out_ref, send_sems.at[step], recv_sems, True)
    grad_resid = upstream + norm_back(grad_second, normal, rstd, gain[...])
    grad_proj = grad_resid.astype(bf16)
    resid_ref[...] = grad_proj
    go_ref[...] = across(grad_proj, w_out[...]).astype(bf16)
    acc_out[...] += jnp.dot(att.T, grad_proj, preferred_element_type=f32)
    vec_ref[0:1] += column_sum(grad_resid)
    vec_ref[1:2] += column_sum(grad_second * normal)
    vec_ref[2:3] += column_sum(grad_second)
    vec_ref[3:4] += column_sum(upstream)

    @pl.when(step == steps - 1)
    def _():
        core = lax.axis_index("win") % 2
        part = width // shards
        down_part = wide // shards
        count = wide // width
        rows = stage.shape[1]
        size = rows // 4

        def copies(b, slot):
            moves = []
            for piece in range(4):
                source = stage.at[slot, pl.ds(piece * size, size)]
                for bit, target in ((0, keep_ref), (1, send_ref)):
                    moves.append((piece % 2, bit, pltpu.make_async_copy(source, target.at[b, piece // 2], sems.at[slot, piece])))
            return moves

        def act(b, slot, what):
            for parity, bit, move in copies(b, slot):
                @pl.when((parity != core) == (bit == 1))
                def _():
                    getattr(move, what)()

        for b in range(shards):
            slot = b % 2
            if b >= 2:
                act(b - 2, slot, "wait")
            for k in range(count):
                stage[slot, k * part : (k + 1) * part] = acc_up[b * part : (b + 1) * part, k * width : (k + 1) * width].astype(bf16)
            base = count * part
            half = width // 2
            for k in range(2):
                stage[slot, base : base + half, k * half : (k + 1) * half] = acc_down[
                    k * half : (k + 1) * half, b * down_part : (b + 1) * down_part
                ].astype(bf16)
            base += half
            stage[slot, base : base + part] = acc_out[b * part : (b + 1) * part, :].astype(bf16)
            stage[slot, base + part :] = jnp.zeros((rows - base - part, width), bf16)
            act(b, slot, "start")
        for b in range(shards - 2, shards):
            act(b, b % 2, "wait")
        for n in range(cot_count):
            return_tile(tile_order(n), out_rows.at[n], out_ref, send_sems.at[n], recv_sems, False)


def row_cuts(count, part, size):
    cuts = []
    for k in range(count):
        start = k * part
        while start < (k + 1) * part:
            end = min((k + 1) * part, (start // size + 1) * size)
            cuts.append((k, start - k * part, end - start, start // size, start % size))
            start = end
    return cuts


def add_into(target, got):
    target[...] = (target[...].astype(jnp.float32) + got[...].astype(jnp.float32)).astype(jnp.bfloat16)


def finish_kernel(groups, *refs):
    f32, bf16 = jnp.float32, jnp.bfloat16
    parts = refs[: 3 * groups]
    (
        rows_ref, resid_ref, gain, shift, weight, vec_two, vec_up, early_keep, early_other, early_left, early_right,
        tok_ref, late_ref, early_ref,
        joined, turned, vec, out_rows, cells, core_got, early_cells, early_more,
        late_bufs, early_bufs, send_sems, recv_sems, load_sems, chain_send, chain_recv, keep_sems,
    ) = refs[3 * groups :]
    step, steps = pl.program_id(0), pl.num_programs(0)
    length, width = rows_ref.shape
    lanes = width // groups
    part = width // 8
    win, blk, core, layer, side = position()
    pair, low, high = win // 2, layer % 2, layer // 2
    core_peer = (win + 1 - 2 * core, blk)
    pair_peer = (win + 2 - 4 * pair, blk)
    side_peer = (win, blk + 1 - 2 * side)
    low_peer = (win, blk + 2 - 4 * low)
    high_peer = (win, blk + 4 - 8 * high)

    def remote(source, target, number, peer):
        return pltpu.make_async_remote_copy(
            src_ref=source, dst_ref=target, send_sem=chain_send.at[number], recv_sem=chain_recv.at[number],
            device_id=peer, device_id_type=MESH,
        )

    def loads():
        moves = []
        for n, (source, left_more, right_more) in enumerate(((early_keep, None, None), (early_other, None, None))):
            moves.append((source.at[0, :, side], (early_cells, early_more)[n].at[0]))
            moves.append((source.at[1, :, :, pair], (early_cells, early_more)[n].at[1]))
        moves.append((early_left, early_bufs[0].at[0]))
        moves.append((early_right, early_bufs[0].at[1]))
        return [pltpu.make_async_copy(a, b, load_sems.at[n]) for n, (a, b) in enumerate(moves)]

    def second_step(state, got, base):
        return [
            remote(state.at[0, :, 1 - pair], got.at[0], base, pair_peer),
            remote(state.at[1, :, 1 - side], got.at[1], base + 1, side_peer),
        ]

    def add_second(state, got, mid):
        for z in range(2):
            mid[0, z] = (state[0, z, pair].astype(f32) + got[0, z].astype(f32)).astype(bf16)
            mid[1, z] = (state[1, z, side].astype(f32) + got[1, z].astype(f32)).astype(bf16)

    def low_step(mid, got, base):
        return [remote(mid.at[:, 1 - low], got, base, low_peer)]

    def add_low_step(mid, got):
        for z in range(2):
            add_into(mid.at[z, low], got.at[z])

    def high_step(mid, got, base):
        return [remote(mid.at[1 - high, low], got, base, high_peer)]

    def add_high_step(mid, got, final):
        final[...] = (mid[high, low].astype(f32) + got[...].astype(f32)).astype(bf16)

    def share(final, target, base):
        return [
            remote(final, target.at[win], base, core_peer),
            remote(final, target.at[win], base + 1, pair_peer),
        ]

    def pass_on(target, base):
        return [remote(target.at[win + 2 - 4 * pair], target.at[win + 2 - 4 * pair], base, core_peer)]

    def start(moves):
        for move in moves:
            move.start()

    def wait(moves):
        for move in moves:
            move.wait()

    _, early_second, early_mid, early_low, early_high, early_final = early_bufs
    late_first, late_second, late_mid, late_low, late_high, late_final = late_bufs
    early_state = early_cells
    first_left, first_right = 0, 1
    early_base, late_base = 8, 0

    @pl.when(step == 0)
    def _():
        barrier = pltpu.get_barrier_semaphore()
        for peer in (core_peer, pair_peer, side_peer, low_peer, high_peer):
            pl.semaphore_signal(barrier, inc=1, device_id=peer, device_id_type=MESH)
        start(loads())
        greet_owners(steps, 5)
        vec[...] = jnp.zeros_like(vec)

    tile = tile_order(step)
    rows = pl.ds(pl.multiple_of(tile * length, length), length)
    for g in range(groups):
        dq, own, other = parts[3 * g : 3 * g + 3]
        columns = slice(g * lanes, (g + 1) * lanes)
        joined[rows, columns] = dq[...]
        both = (own[...].astype(f32) + other[...].astype(f32)).astype(bf16)
        joined[rows, width + g * lanes : width + (g + 1) * lanes] = both[:, :lanes]
        joined[rows, 2 * width + g * lanes : 2 * width + (g + 1) * lanes] = both[:, lanes:]
        vec[0:1, columns] += column_sum(dq[...].astype(f32))
        vec[1:2, columns] += column_sum(both[:, lanes:].astype(f32))
    grad = across(joined[rows, :], weight[...])
    normal, rstd = norm_parts(rows_ref[...].astype(f32))
    turned[tile] = (normal * gain[...] + shift[...]).astype(bf16).T
    vec[2:3] += column_sum(grad * normal)
    vec[3:4] += column_sum(grad)
    out_rows[step] = (resid_ref[...].astype(f32) + norm_back(grad, normal, rstd, gain[...])).astype(bf16)
    return_tile(tile, out_rows.at[step], tok_ref, send_sems.at[step], recv_sems, True)

    @pl.when(step == 0)
    def _():
        wait(loads())
        for half in range(2):
            for z in range(2):
                for n in range(2):
                    early_state[half, z, n] = (
                        early_state[half, z, n].astype(f32) + early_more[half, z, n].astype(f32) + early_bufs[0][half, z, n].astype(f32)
                    ).astype(bf16)
        start(second_step(early_state, early_second, early_base))

    @pl.when(step == steps - 1)
    def _():
        wait(second_step(early_state, early_second, early_base))
        add_second(early_state, early_second, early_mid)
        start(low_step(early_mid, early_low, early_base + 2))
        size = cells.shape[5]
        cuts = row_cuts(3, part, size)
        for k in range(3):
            full = jnp.dot(turned[0], joined[0:length, k * width : (k + 1) * width], preferred_element_type=f32)
            for n in range(1, 4):
                full = full + jnp.dot(
                    turned[n], joined[n * length : (n + 1) * length, k * width : (k + 1) * width], preferred_element_type=f32
                )
            for b in range(8):
                for which, first, count, piece, row in cuts:
                    if which == k:
                        cells[piece % 2, b // 4, b // 2 % 2, b % 2, piece // 2, row : row + count] = full[
                            b * part + first : b * part + first + count
                        ].astype(bf16)
        tail = jnp.concatenate(
            [vec[...], vec_two[...]] + [vec_up[:, n * width : (n + 1) * width] for n in range(4)]
            + [jnp.zeros((4 * size - 3 * part - 12, width), f32)],
            axis=0,
        ).astype(bf16)
        for b in range(8):
            cells[1, b // 4, b // 2 % 2, b % 2, 1, 3 * part - 3 * size :] = tail
        exchange = [remote(cells.at[1 - core], core_got, late_base, core_peer)]
        start(exchange)
        wait(low_step(early_mid, early_low, early_base + 2))
        add_low_step(early_mid, early_low)
        start(high_step(early_mid, early_high, early_base + 3))
        wait(exchange)
        mine = cells.at[core]
        for b in range(8):
            for x in range(2):
                add_into(mine.at[b // 4, b // 2 % 2, b % 2, x], core_got.at[b // 4, b // 2 % 2, b % 2, x])
        first = [
            remote(mine.at[0, :, 1 - side], late_first.at[0], late_base + 1, side_peer),
            remote(mine.at[1, :, :, 1 - pair], late_first.at[1], late_base + 2, pair_peer),
        ]
        start(first)
        wait(high_step(early_mid, early_high, early_base + 3))
        add_high_step(early_mid, early_high, early_final)
        start(share(early_final, early_ref, early_base + 4))
        keep_early = pltpu.make_async_copy(early_final, early_ref.at[win], keep_sems.at[0])
        keep_early.start()
        wait(first)
        state = core_got.at[0]
        for z in range(2):
            for n in range(2):
                state[0, z, n] = (mine[0, z, side, n].astype(f32) + late_first[0, z, n].astype(f32)).astype(bf16)
                state[1, z, n] = (mine[1, z, n, pair].astype(f32) + late_first[1, z, n].astype(f32)).astype(bf16)
        start(second_step(state, late_second, late_base + 3))
        wait(share(early_final, early_ref, early_base + 4))
        start(pass_on(early_ref, early_base + 6))
        wait(second_step(state, late_second, late_base + 3))
        add_second(state, late_second, late_mid)
        start(low_step(late_mid, late_low, late_base + 5))
        wait(low_step(late_mid, late_low, late_base + 5))
        add_low_step(late_mid, late_low)
        start(high_step(late_mid, late_high, late_base + 6))
        wait(high_step(late_mid, late_high, late_base + 6))
        add_high_step(late_mid, late_high, late_final)
        start(share(late_final, late_ref, early_base + 7))
        keep_late = pltpu.make_async_copy(late_final, late_ref.at[win], keep_sems.at[1])
        keep_late.start()
        wait(share(late_final, late_ref, early_base + 7))
        start(pass_on(late_ref, early_base + 9))
        wait(pass_on(early_ref, early_base + 6))
        wait(pass_on(late_ref, early_base + 9))
        keep_early.wait()
        keep_late.wait()
        for n in range(4):
            return_tile(tile_order(n), out_rows.at[n], tok_ref, send_sems.at[n], recv_sems, False)


def general_body(
    tokens,
    cotangent,
    w_qkv,
    b_q,
    b_v,
    w_out,
    b_out,
    gain_one,
    shift_one,
    gain_two,
    shift_two,
    w_up,
    b_up,
    w_down,
    b_down,
    rand_owner,
    rand_sub,
    global_ids,
    species,
):
    blk_count = lax.axis_size("blk")
    blk_pos = lax.axis_index("blk")
    win_pos = lax.axis_index("win")
    windows, length, model_width = tokens.shape
    blocks = rand_owner.shape[1]
    heads = rand_owner.shape[2]
    picks = rand_owner.shape[3]
    glob_count = global_ids.shape[1]
    own_blocks = blocks // blk_count
    block_len = length // own_blocks
    head_dim = model_width // heads
    pair_width = 2 * head_dim
    all_rows = windows * length
    key_count = 3 + glob_count + picks
    per_device = own_blocks * heads * picks
    slot_cap = max(2, 2 * per_device // blk_count)
    score_scale = head_dim ** (-0.5)
    f32 = jnp.float32
    bf16 = jnp.bfloat16
    tokens_f = tokens.reshape(all_rows, model_width).astype(f32)
    normed_f, norm_one_pull = jax.vjp(layer_norm, tokens_f, gain_one, shift_one)
    normed = normed_f.astype(bf16)
    joined = jnp.dot(normed, w_qkv, preferred_element_type=f32)
    query_vals = (joined[:, :model_width] + b_q).astype(bf16)
    key_vals = joined[:, model_width : 2 * model_width].astype(bf16)
    value_vals = (joined[:, 2 * model_width :] + b_v).astype(bf16)

    def to_heads(tensor):
        return tensor.reshape(windows, own_blocks, block_len, heads, head_dim).transpose(
            0, 1, 3, 2, 4
        )

    def from_heads(tensor):
        return tensor.transpose(0, 1, 3, 2, 4).reshape(all_rows, model_width)

    query_heads = to_heads(query_vals)
    local_pairs = jnp.concatenate([to_heads(key_vals), to_heads(value_vals)], axis=-1)
    rimmed = padded(local_pairs, (("blk", 1),), 1)
    block_ids = blk_pos * own_blocks + jnp.arange(own_blocks, dtype=jnp.int32)
    owned_glob = (global_ids[:, :, None] == block_ids[None, None, :]).astype(bf16)
    glob_terms = jnp.einsum("wgb,wbhsc->wghsc", owned_glob, local_pairs, preferred_element_type=f32)
    glob_pairs = lax.psum(glob_terms.astype(jnp.bfloat16), "blk").astype(jnp.float32).astype(bf16)
    owner_rows = rand_owner.reshape(windows, blk_count, per_device)
    sub_rows = rand_sub.reshape(windows, blk_count, per_device)
    owner_hits = (owner_rows[..., None] == jnp.arange(blk_count, dtype=jnp.int32)).astype(jnp.int32)
    slot_rows = jnp.sum(owner_hits * (jnp.cumsum(owner_hits, axis=2) - 1), axis=-1)
    my_owner = lax.dynamic_index_in_dim(owner_rows, blk_pos, 1, keepdims=False)
    my_slot = lax.dynamic_index_in_dim(slot_rows, blk_pos, 1, keepdims=False)
    fetch_index = my_owner * slot_cap + my_slot
    head_of_row = jnp.arange(per_device, dtype=jnp.int32) // picks % heads
    source_rows = sub_rows * heads + head_of_row[None, None, :]
    requester = jnp.arange(blk_count, dtype=jnp.int32)[None, :, None]
    target_rows = jnp.where(
        owner_rows == blk_pos, requester * slot_cap + slot_rows, blk_count * slot_cap
    )
    send_table = jnp.full((windows, blk_count * slot_cap + 1), own_blocks * heads, jnp.int32)
    send_table = jax.vmap(set_rows)(
        send_table, target_rows.reshape(windows, -1), source_rows.reshape(windows, -1)
    )[:, : blk_count * slot_cap]
    flat_pairs = jnp.concatenate(
        [
            local_pairs.reshape(windows, own_blocks * heads, block_len, pair_width),
            jnp.zeros((windows, 1, block_len, pair_width), bf16),
        ],
        axis=1,
    )
    outgoing = jax.vmap(take_rows)(flat_pairs, send_table).reshape(
        windows, blk_count, slot_cap, block_len, pair_width
    )
    incoming = lax.all_to_all(outgoing, "blk", split_axis=1, concat_axis=1, tiled=True).reshape(
        windows, blk_count * slot_cap, block_len, pair_width
    )
    rand_pairs = jax.vmap(take_rows)(incoming, fetch_index).reshape(
        windows, own_blocks, heads, picks, block_len, pair_width
    )
    near_pairs = jnp.stack(
        [rimmed[:, 0:own_blocks], rimmed[:, 1 : own_blocks + 1], rimmed[:, 2 : own_blocks + 2]],
        axis=3,
    )
    far_pairs = jnp.broadcast_to(
        glob_pairs.transpose(0, 2, 1, 3, 4)[:, None],
        (windows, own_blocks, heads, glob_count, block_len, pair_width),
    )
    gathered_keys = jnp.concatenate([near_pairs, far_pairs, rand_pairs], axis=3).reshape(
        windows, own_blocks, heads, key_count * block_len, pair_width
    )
    set_keys = gathered_keys[..., :head_dim]
    set_values = gathered_keys[..., head_dim:]
    block_flags = jnp.concatenate(
        [
            (block_ids > 0)[:, None],
            jnp.ones((own_blocks, 1), jnp.bool_),
            (block_ids < blocks - 1)[:, None],
            jnp.ones((own_blocks, glob_count + picks), jnp.bool_),
        ],
        axis=1,
    )
    key_valid = jnp.repeat(block_flags, block_len, axis=1)[None, :, None, None, :]

    def score_block():
        raw_scores = (
            jnp.einsum("wbhqe,wbhke->wbhqk", query_heads, set_keys, preferred_element_type=f32)
            * score_scale
        )
        return jnp.where(key_valid, raw_scores, masked_score)

    score_matrix = score_block()
    top_score = jnp.max(score_matrix, axis=-1, keepdims=True)
    log_total = top_score + jnp.log(
        jnp.sum(jnp.exp(score_matrix - top_score), axis=-1, keepdims=True)
    )
    probs_low = jnp.exp(score_matrix - log_total).astype(bf16)
    attended = jnp.einsum(
        "wbhqk,wbhke->wbhqe", probs_low, set_values, preferred_element_type=f32
    ).astype(bf16)
    merged = from_heads(attended)
    residual = tokens_f + (jnp.dot(merged, w_out, preferred_element_type=f32) + b_out)
    second_f, norm_two_pull = jax.vjp(layer_norm, residual, gain_two, shift_two)
    second = second_f.astype(bf16)
    inner_f = jnp.dot(second, w_up, preferred_element_type=f32) + b_up
    active_f, gelu_pull = jax.vjp(partial(jax.nn.gelu, approximate=False), inner_f)
    active = active_f.astype(bf16)
    output = residual + (jnp.dot(active, w_down, preferred_element_type=f32) + b_down)
    species_count = jnp.sum(
        (species[:, None] == jnp.arange(SPECIES, dtype=jnp.int32)[None, :]).astype(f32), axis=0
    )
    my_species = lax.dynamic_slice_in_dim(species, win_pos * windows, windows)
    own_count = jnp.sum(
        (my_species[:, None] == jnp.arange(SPECIES, dtype=jnp.int32)[None, :]).astype(f32)
        * species_count[None, :],
        axis=1,
    )
    window_scale = jnp.sqrt(species.shape[0] / (SPECIES * own_count))
    upstream = (cotangent.astype(f32) * window_scale[:, None, None]).reshape(all_rows, model_width)
    grad_branch = upstream.astype(bf16)
    grad_w_down = jnp.einsum("tf,td->fd", active, grad_branch, preferred_element_type=f32)
    grad_b_down = jnp.sum(grad_branch, axis=0, dtype=f32)
    grad_active = jnp.einsum("td,fd->tf", grad_branch, w_down, preferred_element_type=f32)
    grad_inner = gelu_pull(grad_active)[0].astype(bf16)
    grad_w_up = jnp.einsum("td,tf->df", second, grad_inner, preferred_element_type=f32)
    grad_b_up = jnp.sum(grad_inner, axis=0, dtype=f32)
    grad_second = jnp.einsum("tf,df->td", grad_inner, w_up, preferred_element_type=f32)
    grad_resid_norm, grad_gain_two, grad_shift_two = norm_two_pull(grad_second)
    grad_resid = upstream + grad_resid_norm
    grad_proj = grad_resid.astype(bf16)
    grad_w_out = jnp.einsum("ti,to->io", merged, grad_proj, preferred_element_type=f32)
    grad_b_out = jnp.sum(grad_proj, axis=0, dtype=f32)
    grad_attended = to_heads(
        jnp.einsum("to,io->ti", grad_proj, w_out, preferred_element_type=f32).astype(bf16)
    )
    probs_full = jnp.exp(score_block() - log_total)
    grad_probs = jnp.einsum(
        "wbhqe,wbhke->wbhqk", grad_attended, set_values, preferred_element_type=f32
    )
    grad_set_values = jnp.einsum(
        "wbhqk,wbhqe->wbhke", probs_full.astype(bf16), grad_attended, preferred_element_type=f32
    )
    row_dot = jnp.sum(probs_full * grad_probs, axis=-1, keepdims=True)
    grad_scores = (probs_full * (grad_probs - row_dot)).astype(bf16)
    grad_query = (
        jnp.einsum("wbhqk,wbhke->wbhqe", grad_scores, set_keys, preferred_element_type=f32)
        * score_scale
    )
    grad_set_keys = (
        jnp.einsum("wbhqk,wbhqe->wbhke", grad_scores, query_heads, preferred_element_type=f32)
        * score_scale
    )
    grad_set = jnp.concatenate([grad_set_keys, grad_set_values], axis=-1).reshape(
        windows, own_blocks, heads, key_count, block_len, pair_width
    )
    extended = (
        jnp.pad(grad_set[:, :, :, 1], ((0, 0), (1, 1), (0, 0), (0, 0), (0, 0)))
        + jnp.pad(grad_set[:, :, :, 0], ((0, 0), (0, 2), (0, 0), (0, 0), (0, 0)))
        + jnp.pad(grad_set[:, :, :, 2], ((0, 0), (2, 0), (0, 0), (0, 0), (0, 0)))
    )
    edge_grads = jnp.concatenate([extended[:, :1], extended[:, own_blocks + 1 :]], axis=1)
    edge_back = padded(edge_grads.astype(jnp.bfloat16), (("blk", 1),), 1).astype(edge_grads.dtype)
    pair_grad = extended[:, 1 : own_blocks + 1]
    pair_grad = pair_grad.at[:, 0].add(edge_back[:, 0]).at[:, own_blocks - 1].add(edge_back[:, 3])
    glob_grad = jnp.sum(grad_set[:, :, :, 3 : 3 + glob_count], axis=1).transpose(0, 2, 1, 3, 4)
    glob_total = lax.psum(glob_grad.astype(jnp.bfloat16), "blk").astype(jnp.float32)
    pair_grad = pair_grad + jnp.einsum(
        "wgb,wghsc->wbhsc", owned_glob.astype(f32), glob_total, precision=lax.Precision.HIGHEST
    )
    rand_grad = grad_set[:, :, :, 3 + glob_count :].reshape(
        windows, per_device, block_len, pair_width
    )
    back_out = jax.vmap(add_rows)(
        jnp.zeros((windows, blk_count * slot_cap, block_len, pair_width), f32),
        fetch_index,
        rand_grad,
    )
    back_in = lax.all_to_all(
        back_out.reshape(windows, blk_count, slot_cap, block_len, pair_width).astype(jnp.bfloat16),
        "blk",
        split_axis=1,
        concat_axis=1,
        tiled=True,
    ).astype(jnp.float32)
    owner_sum = jax.vmap(add_rows)(
        jnp.zeros((windows, own_blocks * heads + 1, block_len, pair_width), f32),
        send_table,
        back_in.reshape(windows, blk_count * slot_cap, block_len, pair_width),
    )
    pair_grad = pair_grad + owner_sum[:, : own_blocks * heads].reshape(
        windows, own_blocks, heads, block_len, pair_width
    )
    grad_keys = from_heads(pair_grad[..., :head_dim].astype(bf16))
    grad_values = from_heads(pair_grad[..., head_dim:].astype(bf16))
    grad_joined = jnp.concatenate(
        [from_heads(grad_query.astype(bf16)), grad_keys, grad_values], axis=1
    )
    grad_w_qkv = jnp.einsum("td,tc->dc", normed, grad_joined, preferred_element_type=f32)
    grad_b_q = jnp.sum(grad_joined[:, :model_width], axis=0, dtype=f32)
    grad_b_v = jnp.sum(grad_joined[:, 2 * model_width :], axis=0, dtype=f32)
    grad_normed = jnp.einsum("tc,dc->td", grad_joined, w_qkv, preferred_element_type=f32)
    grad_tok_norm, grad_gain_one, grad_shift_one = norm_one_pull(grad_normed)
    grad_tokens = (grad_resid + grad_tok_norm).astype(bf16).reshape(windows, length, model_width)
    local_grads = (
        grad_w_qkv,
        grad_b_q,
        grad_b_v,
        grad_w_out,
        grad_b_out,
        grad_gain_one,
        grad_shift_one,
        grad_gain_two,
        grad_shift_two,
        grad_w_up,
        grad_b_up,
        grad_w_down,
        grad_b_down,
    )
    packed_grads = jnp.concatenate(
        [grad_item.reshape(blk_count, -1) for grad_item in local_grads], axis=1
    )
    total_cols = packed_grads.shape[1]
    win_count = lax.axis_size("win")
    pad_cols = -total_cols % win_count
    shard_sum = lax.psum_scatter(
        packed_grads.astype(jnp.bfloat16), "blk", scatter_dimension=0, tiled=True
    ).astype(jnp.float32)
    split_shard = jnp.pad(shard_sum, ((0, 0), (0, pad_cols))).reshape(win_count, -1)
    group_piece = lax.psum_scatter(
        split_shard.astype(jnp.bfloat16), "win", scatter_dimension=0, tiled=True
    ).astype(jnp.float32)
    summed = (
        lax.all_gather(group_piece.astype(jnp.bfloat16), "win", axis=0, tiled=True)
        .astype(group_piece.dtype)
        .reshape(1, -1)[:, :total_cols]
    )
    shards = []
    offset = 0
    for grad_item in local_grads:
        entry_count = grad_item.size // blk_count
        shards.append(
            summed[0, offset : offset + entry_count].reshape(
                (grad_item.shape[0] // blk_count,) + grad_item.shape[1:]
            )
        )
        offset = offset + entry_count
    out_tokens = output.astype(bf16).reshape(windows, length, model_width)
    return (
        out_tokens,
        grad_tokens,
        shards[0],
        shards[1],
        shards[2],
        shards[3],
        shards[4],
        shards[5],
        shards[6],
        shards[7],
        shards[8],
        shards[9],
        shards[10],
        shards[11],
        shards[12],
    )


def layer_step(*arguments):
    windows = arguments[0].shape[0]
    paired = lax.axis_size("blk") == 2 * windows and lax.axis_size("win") == 4 and windows == 4
    return (paired_body if paired else general_body)(*arguments)


def paired_body(
    tokens,
    cotangent,
    w_qkv,
    b_q,
    b_v,
    w_out,
    b_out,
    gain_one,
    shift_one,
    gain_two,
    shift_two,
    w_up,
    b_up,
    w_down,
    b_down,
    rand_owner,
    rand_sub,
    global_ids,
    species,
):
    f32 = jnp.float32
    bf16 = jnp.bfloat16
    win_count = lax.axis_size("win")
    blk_count = lax.axis_size("blk")
    win_pos = lax.axis_index("win")
    blk_pos = lax.axis_index("blk")
    layers, length, width = tokens.shape
    core, layer, side = win_pos % 2, blk_pos // 2, blk_pos % 2
    blocks, heads, picks = rand_owner.shape[1:]
    own_blocks = blocks // blk_count
    half_blocks = blocks // 2
    block_len = length // own_blocks
    head_dim = width // heads
    all_rows = layers * length
    lanes = HEADS_PER_GROUP * head_dim
    groups = heads // HEADS_PER_GROUP
    score_scale = head_dim ** (-0.5)

    def regroup(value):
        parts = []
        for step in range(layers):
            part = lax.dynamic_index_in_dim(value, (layer + step) % layers, 0, keepdims=False)
            parts.append(lax.ppermute(part, ("win", "blk"), regroup_pairs(win_count, layers, step)))
        return parts

    def send_back(value):
        parts = []
        for step in range(layers):
            pairs = [(b, a) for a, b in regroup_pairs(win_count, layers, step)]
            parts.append(lax.ppermute(value[step * length : (step + 1) * length], ("win", "blk"), pairs))
        return parts

    def in_order(parts):
        result = jnp.zeros((layers, length, width), parts[0].dtype)
        for step, part in enumerate(parts):
            result = lax.dynamic_update_index_in_dim(result, part, (layer + step) % layers, 0)
        return result

    def takes(micros):
        return pl.CostEstimate(flops=micros * 1_000_000_000, bytes_accessed=micros * 1_000_000, transcendentals=0)

    rows_in = jnp.concatenate(regroup(tokens), axis=0)
    cot_in = regroup(cotangent)

    rand_size = blocks * heads * picks
    named = jnp.concatenate(
        [
            lax.dynamic_index_in_dim((rand_owner * own_blocks + rand_sub).reshape(layers, rand_size), layer, 0, keepdims=False),
            lax.dynamic_index_in_dim(global_ids, layer, 0, keepdims=False),
        ]
    )
    named = jnp.where(side == core, named, swap(named, 1, 0))

    def place_of(block):
        owner = block // own_blocks
        half = jnp.where(owner % 2 == core, 0, half_blocks)
        return half + ((layer - owner // 2) % layers) * own_blocks + block % own_blocks

    slot = jnp.arange(half_blocks, dtype=jnp.int32)
    slot_block = (((layer - slot // own_blocks) % layers) * 2 + core) * own_blocks + slot % own_blocks
    table = jnp.concatenate(
        [
            place_of(named),
            slot_block,
            place_of(jnp.maximum(slot_block - 1, 0)),
            place_of(jnp.minimum(slot_block + 1, blocks - 1)),
        ]
    )
    sizes = (heads, picks, rand_size, half_blocks)

    tile = length

    def by_rows(columns):
        return pl.BlockSpec((tile, columns), lambda i: (i, 0))

    def by_tile(columns):
        return pl.BlockSpec((tile, columns), lambda i: (tile_order(i), 0))

    def whole(*shape, once=True):
        mode = pl.Buffered(1) if once else None
        return pl.BlockSpec(shape, lambda i: (0,) * len(shape), pipeline_mode=mode)

    scalars = pl.BlockSpec(memory_space=pltpu.SMEM)
    wide = w_up.shape[1]
    params = pltpu.CompilerParams(vmem_limit_bytes=60 << 20)
    row = lambda vector: vector.reshape(1, -1)
    query, key_value = pl.pallas_call(
        partial(qkv_kernel, score_scale),
        grid=(all_rows // tile,),
        in_specs=[by_rows(width), whole(1, width), whole(1, width), whole(width, 3 * width), whole(2, width)],
        out_specs=[by_rows(width), by_rows(2 * width)],
        out_shape=[jax.ShapeDtypeStruct((all_rows, width), bf16), jax.ShapeDtypeStruct((all_rows, 2 * width), bf16)],
        compiler_params=params,
        cost_estimate=takes(12),
        name="qkv",
    )(rows_in, row(gain_one), row(shift_one), w_qkv, jnp.stack([b_q, b_v]))
    key_value_other = swap(key_value, 1, 0)

    def lane_block(first):
        return pl.BlockSpec((all_rows, lanes), lambda g, t: (0, first + g))

    store = pltpu.VMEM((blocks, block_len, lanes), bf16)
    attended, log_total = pl.pallas_call(
        partial(attend_kernel, sizes, blocks, head_dim),
        grid_spec=pltpu.PrefetchScalarGridSpec(
            num_scalar_prefetch=1,
            grid=(groups,),
            in_specs=[lane_block(0), lane_block(0), lane_block(0), lane_block(groups), lane_block(groups)],
            out_specs=[lane_block(0), pl.BlockSpec((1, half_blocks, lanes), lambda g, t: (g, 0, 0))],
            scratch_shapes=[store, store],
        ),
        out_shape=[
            jax.ShapeDtypeStruct((all_rows, width), bf16),
            jax.ShapeDtypeStruct((groups, half_blocks, lanes), f32),
        ],
        compiler_params=pltpu.CompilerParams(vmem_limit_bytes=56 << 20),
        cost_estimate=takes(37),
        name="attend",
    )(table, query, key_value, key_value_other, key_value, key_value_other)

    species_count = jnp.sum(
        (species[:, None] == jnp.arange(SPECIES, dtype=jnp.int32)[None, :]).astype(f32), axis=0
    )
    my_window = ((win_pos // 2) * 2 + side) * layers + layer
    my_species = lax.dynamic_index_in_dim(species, my_window, 0, keepdims=False)
    own_count = jnp.sum(
        (my_species == jnp.arange(SPECIES, dtype=jnp.int32)).astype(f32) * species_count
    )
    window_scale = jnp.sqrt(species.shape[0] / (SPECIES * own_count))
    payload = 2 * wide // blk_count + width // blk_count
    payload += -payload % (16 * win_count)
    stays = jax.ShapeDtypeStruct((blk_count, win_count // 2, payload // win_count, width), bf16)
    any_place = pl.BlockSpec(memory_space=pl.ANY)
    out_tokens, grad_resid, grad_attended, vec_two, vec_up, early_keep, early_send = pl.pallas_call(
        partial(ffn_kernel, 256, blk_count, layers),
        grid=(layers,),
        in_specs=[
            scalars, by_tile(width), by_tile(width), *[any_place] * layers, whole(width, width), whole(1, width), whole(1, width),
            whole(1, width), whole(width, wide), whole(1, wide), whole(wide, width), whole(1, width),
        ],
        out_specs=[any_place, by_tile(width), by_tile(width), whole(4, width), whole(1, wide), any_place, any_place],
        out_shape=[
            jax.ShapeDtypeStruct((layers, length, width), bf16),
            jax.ShapeDtypeStruct((all_rows, width), bf16),
            jax.ShapeDtypeStruct((all_rows, width), bf16),
            jax.ShapeDtypeStruct((4, width), f32),
            jax.ShapeDtypeStruct((1, wide), f32),
            stays,
            stays,
        ],
        scratch_shapes=[
            pltpu.VMEM((width, wide), f32),
            pltpu.VMEM((width, wide), f32),
            pltpu.VMEM((width, width), f32),
            pltpu.VMEM((2, payload, width), bf16),
            pltpu.SemaphoreType.DMA((2, 4)),
            pltpu.VMEM((length, wide), bf16),
            pltpu.VMEM((length, wide), bf16),
            pltpu.VMEM((2, length, width), bf16),
            pltpu.SemaphoreType.DMA((2,)),
            pltpu.VMEM((layers, length, width), bf16),
            pltpu.SemaphoreType.DMA((layers,)),
            pltpu.SemaphoreType.DMA((layers,)),
        ],
        compiler_params=pltpu.CompilerParams(vmem_limit_bytes=60 << 20, collective_id=1, has_side_effects=True),
        cost_estimate=takes(90),
        name="ffn",
    )(
        window_scale.reshape(1), rows_in, attended, *cot_in, w_out, row(b_out), row(gain_two), row(shift_two),
        w_up, row(b_up), w_down, row(b_down),
    )

    pair = win_pos // 2

    def add_low(keep, other):
        return (keep.astype(f32) + other.astype(f32)).astype(bf16)

    early_rows = payload // win_count
    late_rows = 3 * width // blk_count + 32
    late_size = late_rows // win_count

    def early_send_part(half, axis, bit, win_bit, blk_bit):
        parts = [
            lax.dynamic_index_in_dim(cells.reshape(2, 2, 2, 2, early_rows, width)[half], 1 - bit, axis, keepdims=False)
            for cells in (early_keep, early_other)
        ]
        return swap(add_low(*parts), win_bit, blk_bit)

    grad_parts = []
    early_other = swap(early_send, 1, 0)
    for group in range(groups):
        after = [early_other] if group == 1 else []
        if group == 1:
            early_left = early_send_part(0, 1, side, 0, 1)
            early_right = early_send_part(1, 2, pair, 2, 0)

        def column(first):
            return pl.BlockSpec((all_rows, lanes), lambda g, t: (0, first))

        def full(columns):
            return pl.BlockSpec((all_rows, columns), lambda g, t: (0, 0))

        grad_store = pltpu.VMEM((blocks, block_len, lanes), f32)
        glob_store = pltpu.VMEM((2, block_len, lanes), f32)
        dq, own, other = pl.pallas_call(
            partial(attend_back_kernel, sizes, blocks, head_dim, score_scale, group),
            grid_spec=pltpu.PrefetchScalarGridSpec(
                num_scalar_prefetch=1,
                grid=(1,),
                in_specs=[
                    column(group), column(group), column(group), column(groups + group), column(groups + group), column(group),
                    pl.BlockSpec((1, half_blocks, lanes), lambda g, t: (group, 0, 0)),
                    *[any_place] * len(after),
                ],
                out_specs=[full(lanes), full(2 * lanes), full(2 * lanes)],
                scratch_shapes=[store, store, grad_store, grad_store, glob_store, glob_store],
            ),
            out_shape=[jax.ShapeDtypeStruct((all_rows, n * lanes), bf16) for n in (1, 2, 2)],
            compiler_params=params,
            cost_estimate=takes(25),
            name="attend_back",
        )(table, query, key_value, key_value_other, key_value, key_value_other, grad_attended, log_total, *after)
        grad_parts += [dq, own, swap(other, 1, 0)]

    def vmem(*shape):
        return pltpu.VMEM(shape, bf16)

    first_shape, mid_shape, low_shape = (2, 2, 2), (2, 2), (2,)
    chain = lambda size: [vmem(*lead, size, width) for lead in (first_shape, mid_shape, mid_shape, low_shape, (), ())]
    grad_tokens, late, early = pl.pallas_call(
        partial(finish_kernel, groups),
        grid=(layers,),
        in_specs=[by_tile(p.shape[1]) for p in grad_parts]
        + [by_tile(width), by_tile(width), whole(1, width), whole(1, width), whole(width, 3 * width), whole(4, width), whole(1, wide)]
        + [any_place] * 4,
        out_specs=[any_place] * 3,
        out_shape=[
            jax.ShapeDtypeStruct((layers, length, width), bf16),
            jax.ShapeDtypeStruct((win_count, late_size, width), bf16),
            jax.ShapeDtypeStruct((win_count, early_rows, width), bf16),
        ],
        scratch_shapes=[
            vmem(all_rows, 3 * width),
            vmem(layers, width, length),
            pltpu.VMEM((4, width), f32),
            vmem(layers, length, width),
            vmem(2, 2, 2, 2, 2, late_size, width),
            vmem(2, 2, 2, 2, late_size, width),
            vmem(2, 2, 2, early_rows, width),
            vmem(2, 2, 2, early_rows, width),
            chain(late_size),
            chain(early_rows),
            pltpu.SemaphoreType.DMA((layers,)),
            pltpu.SemaphoreType.DMA((layers,)),
            pltpu.SemaphoreType.DMA((6,)),
            pltpu.SemaphoreType.DMA((18,)),
            pltpu.SemaphoreType.DMA((18,)),
            pltpu.SemaphoreType.DMA((2,)),
        ],
        compiler_params=pltpu.CompilerParams(vmem_limit_bytes=62 << 20, collective_id=2, has_side_effects=True),
        cost_estimate=takes(90),
        name="finish",
    )(
        *grad_parts, rows_in, grad_resid, row(gain_one), row(shift_one), w_qkv, vec_two, vec_up,
        early_keep.reshape(2, 2, 2, 2, early_rows, width), early_other.reshape(2, 2, 2, 2, early_rows, width), early_left, early_right,
    )
    early = early.reshape(-1, width).astype(f32)
    late = late.reshape(-1, width).astype(f32)
    part = width // blk_count

    def rows_again(rows, count):
        return rows.reshape(count, -1, width).transpose(1, 0, 2).reshape(-1, count * width)

    count = wide // width
    half = width // 2
    done_up = rows_again(early[: count * part], count)
    done_down = early[count * part : count * part + half].reshape(half, 2, wide // blk_count).transpose(2, 1, 0).reshape(-1, width)
    done_out = early[count * part + half : (count + 1) * part + half]
    done_qkv = rows_again(late[: 3 * part], 3)
    vec = lax.dynamic_slice_in_dim(late[3 * part : 3 * part + 8], blk_pos * part, part, axis=1)
    vec_wide = lax.dynamic_slice_in_dim(late[3 * part + 8 : 3 * part + 8 + count].reshape(-1), blk_pos * (wide // blk_count), wide // blk_count)
    return (
        out_tokens,
        grad_tokens,
        done_qkv,
        vec[0],
        vec[1],
        done_out,
        vec[4],
        vec[2],
        vec[3],
        vec[5],
        vec[6],
        done_up,
        vec_wide,
        done_down,
        vec[7],
    )


def solution(mesh):
    placed = (
        P("win", "blk", None),
        P("win", "blk", None),
        P(),
        P(),
        P(),
        P(),
        P(),
        P(),
        P(),
        P(),
        P(),
        P(),
        P(),
        P(),
        P(),
        P("win", None, None, None),
        P("win", None, None, None),
        P("win", None),
        P(),
    )
    return jax.shard_map(
        layer_step,
        mesh=mesh,
        in_specs=placed,
        out_specs=(
            P("win", "blk", None),
            P("win", "blk", None),
            P("blk", None),
            P("blk"),
            P("blk"),
            P("blk", None),
            P("blk"),
            P("blk"),
            P("blk"),
            P("blk"),
            P("blk"),
            P("blk", None),
            P("blk"),
            P("blk", None),
            P("blk"),
        ),
        check_vma=False,
    )
```

```python
from functools import partial

import jax
import jax.numpy as jnp
from jax import lax
from jax.experimental import pallas as pl
from jax.experimental.pallas import tpu as pltpu
from jax.sharding import PartitionSpec as P

SPECIES = 4


epsilon = 1e-05
masked_score = -1000000000.0


def padded(cells, sides, width):
    for axis, dim in sides:
        count = lax.axis_size(axis)
        ends = count - 1
        head = lax.slice_in_dim(cells, 0, width, axis=dim)
        tail = lax.slice_in_dim(cells, cells.shape[dim] - width, cells.shape[dim], axis=dim)
        cells = jnp.concatenate(
            [
                lax.ppermute(tail, axis, [(i, (i + 1) % count) for i in range(ends)]),
                cells,
                lax.ppermute(head, axis, [((i + 1) % count, i) for i in range(ends)]),
            ],
            axis=dim,
        )
    return cells


def layer_norm(values, norm_gain, norm_shift):
    average = jnp.mean(values, axis=-1, keepdims=True)
    centred = values - average
    variance = jnp.mean(centred * centred, axis=-1, keepdims=True)
    return centred * lax.rsqrt(variance + epsilon) * norm_gain + norm_shift


def take_rows(source, index_rows):
    return jnp.take(source, index_rows, axis=0)


def add_rows(base, index_rows, update):
    return base.at[index_rows].add(update)


def set_rows(base, index_rows, update):
    return base.at[index_rows].set(update)


HEADS_PER_GROUP = 4


def regroup_pairs(win_count, layers, step):
    pairs = []
    for win in range(win_count):
        for blk in range(2 * layers):
            layer, side = blk // 2, blk % 2
            target = ((layer + step) % layers) * 2 + win % 2
            pairs.append((win * 2 * layers + blk, ((win // 2) * 2 + side) * 2 * layers + target))
    return pairs


def flip_pairs(win_count, blk_count, win_bit, blk_bit):
    return [
        (win * blk_count + blk, (win ^ win_bit) * blk_count + (blk ^ blk_bit))
        for win in range(win_count)
        for blk in range(blk_count)
    ]


def swap(value, win_bit, blk_bit):
    pairs = flip_pairs(lax.axis_size("win"), lax.axis_size("blk"), win_bit, blk_bit)
    return lax.ppermute(value, ("win", "blk"), pairs)


def head_masks(lanes, head_dim, dtype):
    lane = lax.broadcasted_iota(jnp.int32, (1, lanes), 1)
    return [(lane // head_dim == h).astype(dtype) for h in range(lanes // head_dim)]


def block_places(table, slot, group, sizes):
    heads, picks, rand_size, half_blocks = sizes
    block = table[rand_size + 2 + slot]
    near = [table[rand_size + 2 + half_blocks + slot], slot, table[rand_size + 2 + 2 * half_blocks + slot]]
    row = (block * heads + group * HEADS_PER_GROUP) * picks
    rand = [[table[row + h * picks + r] for h in range(HEADS_PER_GROUP)] for r in range(picks)]
    return block, near, rand


def spread_heads(rows, masks):
    return jnp.concatenate([rows * m for m in masks], axis=0)


def pick_heads(square, masks, height):
    total = square[0:height] * masks[0]
    for h in range(1, len(masks)):
        total = total + square[h * height : (h + 1) * height] * masks[h]
    return total


def key_rows(source, near, glob, rand, low_half):
    parts = [source[p] for p in near] + [source[p] for p in glob]
    for places in rand:
        columns = []
        for c in range(len(places) // 2):
            low = source[places[2 * c], :, c * 128 : (c + 1) * 128]
            high = source[places[2 * c + 1], :, c * 128 : (c + 1) * 128]
            columns.append(jnp.where(low_half, low, high))
        parts.append(jnp.concatenate(columns, axis=1))
    return jnp.concatenate(parts, axis=0)


def mask_scores(scores, block, blocks, block_len):
    first = jnp.where(block > 0, scores[:block_len], masked_score)
    last = jnp.where(block < blocks - 1, scores[2 * block_len : 3 * block_len], masked_score)
    return jnp.concatenate([first, scores[block_len : 2 * block_len], last, scores[3 * block_len :]], axis=0)


def across(left, right):
    return lax.dot_general(left, right, (((1,), (1,)), ((), ())), preferred_element_type=jnp.float32)


def down(left, right):
    return lax.dot_general(left, right, (((0,), (0,)), ((), ())), preferred_element_type=jnp.float32)


def load_halves(target, own, other, half_blocks, block_len):
    lanes = own.shape[-1]
    target[0:half_blocks] = own[...].reshape(half_blocks, block_len, lanes)
    target[half_blocks:] = other[...].reshape(half_blocks, block_len, lanes)


def attend_kernel(sizes, blocks, head_dim, table, q_ref, k_own, k_other, v_own, v_other, o_ref, lse_ref, k_all, v_all):
    heads, picks, rand_size, half_blocks = sizes
    block_len = k_all.shape[1]
    lanes = q_ref.shape[1]
    group = pl.program_id(0)
    load_halves(k_all, k_own, k_other, half_blocks, block_len)
    load_halves(v_all, v_own, v_other, half_blocks, block_len)
    low_half = lax.broadcasted_iota(jnp.int32, (block_len, 128), 1) < head_dim
    masks = head_masks(lanes, head_dim, jnp.bfloat16)
    masks_f = head_masks(lanes, head_dim, jnp.float32)
    glob = [table[rand_size], table[rand_size + 1]]

    def one(slot, carry):
        block, near, rand = block_places(table, slot, group, sizes)
        rows = pl.ds(pl.multiple_of(slot * block_len, block_len), block_len)
        queries = spread_heads(q_ref[rows, :], masks)
        keys = key_rows(k_all, near, glob, rand, low_half)
        scores = mask_scores(across(keys, queries), block, blocks, block_len)
        top = jnp.max(scores, axis=0, keepdims=True)
        weights = jnp.exp(scores - top)
        total = jnp.sum(weights, axis=0, keepdims=True)
        probs = (weights * (1.0 / total)).astype(jnp.bfloat16)
        values = key_rows(v_all, near, glob, rand, low_half)
        o_ref[rows, :] = pick_heads(down(probs, values), masks_f, block_len).astype(jnp.bfloat16)
        lse_ref[0, pl.ds(slot, 1), :] = top + jnp.log(total)
        return carry

    lax.fori_loop(0, half_blocks, one, 0, unroll=min(8, half_blocks))


def attend_back_kernel(
    sizes, blocks, head_dim, scale, group,
    table, q_ref, k_own, k_other, v_own, v_other, go_ref, lse_ref, *refs,
):
    dq_ref, own_ref, other_ref, k_all, v_all, dk_all, dv_all, dk_glob, dv_glob = refs[-9:]
    heads, picks, rand_size, half_blocks = sizes
    block_len = k_all.shape[1]
    lanes = q_ref.shape[1]
    f32 = jnp.float32
    load_halves(k_all, k_own, k_other, half_blocks, block_len)
    load_halves(v_all, v_own, v_other, half_blocks, block_len)
    dk_all[...] = jnp.zeros_like(dk_all)
    dv_all[...] = jnp.zeros_like(dv_all)
    dk_glob[...] = jnp.zeros_like(dk_glob)
    dv_glob[...] = jnp.zeros_like(dv_glob)
    low_half = lax.broadcasted_iota(jnp.int32, (block_len, 128), 1) < head_dim
    masks = head_masks(lanes, head_dim, jnp.bfloat16)
    masks_f = head_masks(lanes, head_dim, f32)
    glob = [table[rand_size], table[rand_size + 1]]

    def add_back(grads, near, rand, into, into_glob):
        for n in range(3):
            into[near[n]] += grads[n * block_len : (n + 1) * block_len]
        for n in range(2):
            into_glob[n] += grads[(3 + n) * block_len : (4 + n) * block_len]
        for r in range(picks):
            part = grads[(5 + r) * block_len : (6 + r) * block_len]
            for c in range(lanes // 128):
                cell = part[:, c * 128 : (c + 1) * 128]
                columns = pl.ds(c * 128, 128)
                into[rand[r][2 * c], :, columns] += jnp.where(low_half, cell, 0.0)
                into[rand[r][2 * c + 1], :, columns] += jnp.where(low_half, 0.0, cell)

    def one(slot, carry):
        block, near, rand = block_places(table, slot, group, sizes)
        rows = pl.ds(pl.multiple_of(slot * block_len, block_len), block_len)
        queries = spread_heads(q_ref[rows, :], masks)
        grads_out = spread_heads(go_ref[rows, :], masks)
        keys = key_rows(k_all, near, glob, rand, low_half)
        values = key_rows(v_all, near, glob, rand, low_half)
        scores = mask_scores(across(keys, queries), block, blocks, block_len)
        probs = jnp.exp(scores - lse_ref[0, pl.ds(slot, 1), :])
        grad_probs = across(values, grads_out)
        row_dot = jnp.sum(probs * grad_probs, axis=0, keepdims=True)
        grad_scores = (probs * (grad_probs - row_dot)).astype(jnp.bfloat16)
        add_back(jnp.dot(probs.astype(jnp.bfloat16), grads_out, preferred_element_type=f32), near, rand, dv_all, dv_glob)
        add_back(jnp.dot(grad_scores, queries, preferred_element_type=f32), near, rand, dk_all, dk_glob)
        dq_ref[rows, :] = (pick_heads(down(grad_scores, keys), masks_f, block_len) * scale).astype(jnp.bfloat16)
        return carry

    lax.fori_loop(0, half_blocks, one, 0, unroll=min(8, half_blocks))
    for n in range(2):
        dk_all[glob[n]] += dk_glob[n]
        dv_all[glob[n]] += dv_glob[n]
    for target, start in ((own_ref, 0), (other_ref, half_blocks)):
        for n, source in enumerate((dk_all, dv_all)):
            cells = source[start : start + half_blocks].astype(jnp.bfloat16)
            target[:, n * lanes : (n + 1) * lanes] = cells.reshape(half_blocks * block_len, lanes)


def norm_parts(values):
    average = jnp.mean(values, axis=-1, keepdims=True)
    centred = values - average
    rstd = lax.rsqrt(jnp.mean(centred * centred, axis=-1, keepdims=True) + epsilon)
    return centred * rstd, rstd


def norm_back(grad, normal, rstd, gain):
    scaled = grad * gain
    first = jnp.mean(scaled, axis=-1, keepdims=True)
    second = jnp.mean(scaled * normal, axis=-1, keepdims=True)
    return rstd * (scaled - first - normal * second)


def normal_parts(values):
    cdf = 0.5 + 0.5 * lax.erf(values * 0.5**0.5)
    return cdf, values * jnp.exp(-0.5 * values * values) * 0.3989422804014327


def column_sum(values):
    return jnp.sum(values, axis=0, keepdims=True)


def qkv_kernel(scale, rows_ref, gain, shift, weight, bias, q_ref, kv_ref):
    width = rows_ref.shape[1]
    normal, _ = norm_parts(rows_ref[...].astype(jnp.float32))
    normed = (normal * gain[...] + shift[...]).astype(jnp.bfloat16)

    def part(n):
        columns = slice(n * width, (n + 1) * width)
        return jnp.dot(normed, weight[:, columns], preferred_element_type=jnp.float32)

    q_ref[...] = (part(0) + bias[0:1]).astype(jnp.bfloat16) * jnp.asarray(scale, jnp.bfloat16)
    kv_ref[:, :width] = part(1).astype(jnp.bfloat16)
    kv_ref[:, width:] = (part(2) + bias[1:2]).astype(jnp.bfloat16)


MESH = pl.DeviceIdType.MESH


def tile_order(number):
    return jnp.where(number == 0, 2, jnp.where(number == 2, 3, jnp.where(number == 3, 0, number)))


def position():
    win, blk = lax.axis_index("win"), lax.axis_index("blk")
    return win, blk, win % 2, blk // 2, blk % 2


def owner_of(tile, layers):
    win, blk, core, layer, side = position()
    return (win // 2) * 2 + side, ((layer + layers - tile) % layers) * 2 + core


def greet_owners(layers, peers):
    barrier = pltpu.get_barrier_semaphore()
    others = len(peers)
    for peer in peers:
        pl.semaphore_signal(barrier, inc=1, device_id=peer, device_id_type=MESH)
    _, _, core, _, side = position()
    for tile in range(1, layers):
        pl.semaphore_signal(barrier, inc=1, device_id=owner_of(tile, layers), device_id_type=MESH)

    @pl.when(side != core)
    def _():
        pl.semaphore_signal(barrier, inc=1, device_id=owner_of(0, layers), device_id_type=MESH)
        pl.semaphore_wait(barrier, layers + others)

    @pl.when(side == core)
    def _():
        pl.semaphore_wait(barrier, layers - 1 + others)


def return_tile(tile, source, target, send_sem, recv_sems, start):
    _, _, core, layer, side = position()
    layers = target.shape[0]
    stays = (tile == 0) & (side == core)

    @pl.when(stays)
    def _():
        move = pltpu.make_async_copy(source, target.at[layer], recv_sems.at[tile])
        move.start() if start else move.wait()

    @pl.when(jnp.logical_not(stays))
    def _():
        move = pltpu.make_async_remote_copy(
            src_ref=source, dst_ref=target.at[layer], send_sem=send_sem, recv_sem=recv_sems.at[tile],
            device_id=owner_of(tile, layers), device_id_type=MESH,
        )
        move.start() if start else move.wait()


def ffn_kernel(
    chunk, shards, cot_count,
    scale, rows_ref, att_ref, *refs,
):
    cot_parts = refs[:cot_count]
    (
        w_out, b_out, gain, shift, w_up, b_up, w_down, b_down,
        out_ref, resid_ref, go_ref, vec_ref, vec_up_ref, keep_ref, send_ref,
        acc_up, acc_down, acc_out, stage, sems, active_all, inner_all, cot_rows, cot_sems, out_rows, send_sems, recv_sems, cell_sems,
    ) = refs[cot_count:]
    f32, bf16 = jnp.float32, jnp.bfloat16
    step, steps = pl.program_id(0), pl.num_programs(0)
    width, wide = w_up.shape

    slot = step % 2

    def fetch(number):
        for n, part in enumerate(cot_parts):
            @pl.when((number < steps) & (tile_order(number) == n))
            def _():
                pltpu.make_async_copy(part, cot_rows.at[number % 2], cot_sems.at[number % 2]).start()

    win, blk, core, _, _ = position()

    @pl.when(step == 0)
    def _():
        greet_owners(steps, [(win + 1 - 2 * core, blk)])

    @pl.when(step == 0)
    def _():
        fetch(step)

    fetch(step + 1)

    @pl.when(step == 0)
    def _():
        for ref in (acc_up, acc_down, acc_out, vec_ref, vec_up_ref):
            ref[...] = jnp.zeros_like(ref)

    att = att_ref[...]
    residual = rows_ref[...].astype(f32) + (jnp.dot(att, w_out[...], preferred_element_type=f32) + b_out[...])
    normal, rstd = norm_parts(residual)
    second = (normal * gain[...] + shift[...]).astype(bf16)
    pltpu.make_async_copy(cot_parts[0], cot_rows.at[slot], cot_sems.at[slot]).wait()
    upstream = cot_rows[slot].astype(f32) * scale[0]
    branch = upstream.astype(bf16)
    second_t = second.T
    branch_t = branch.T
    total = residual + b_down[...]
    grad_second = jnp.zeros_like(residual)
    def raise_part(first):
        part = slice(first, first + chunk)
        inner = jnp.dot(second, w_up[:, part], preferred_element_type=f32) + b_up[:, part]
        return inner, across(branch, w_down[part, :])

    ahead = raise_part(0)
    for first in range(0, wide, chunk):
        part = slice(first, first + chunk)
        inner, grad_active = ahead
        if first + chunk < wide:
            ahead = raise_part(first + chunk)
        cdf, slope = normal_parts(inner)
        active = (inner * cdf).astype(bf16)
        grad_inner_f = grad_active * (cdf + slope)
        grad_inner = grad_inner_f.astype(bf16)
        active_all[:, part] = active
        inner_all[:, part] = grad_inner
        acc_down[:, part] += jnp.dot(branch_t, active, preferred_element_type=f32)
        acc_up[:, part] += jnp.dot(second_t, grad_inner, preferred_element_type=f32)
        vec_up_ref[:, part] += column_sum(grad_inner_f)
    total = total + jnp.dot(active_all[...], w_down[...], preferred_element_type=f32)
    grad_second = across(inner_all[...], w_up[...])
    out_rows[step] = total.astype(bf16)
    return_tile(tile_order(step), out_rows.at[step], out_ref, send_sems.at[step], recv_sems, True)
    grad_resid = upstream + norm_back(grad_second, normal, rstd, gain[...])
    grad_proj = grad_resid.astype(bf16)
    resid_ref[...] = grad_proj
    go_ref[...] = across(grad_proj, w_out[...]).astype(bf16)
    acc_out[...] += jnp.dot(att.T, grad_proj, preferred_element_type=f32)
    vec_ref[0:1] += column_sum(grad_resid)
    vec_ref[1:2] += column_sum(grad_second * normal)
    vec_ref[2:3] += column_sum(grad_second)
    vec_ref[3:4] += column_sum(upstream)

    @pl.when(step == steps - 1)
    def _():
        part = width // shards
        down_part = wide // shards
        count = wide // width
        rows = stage.shape[1]
        size = rows // 4

        def act(b, slot, what):
            for piece in range(4):
                source = stage.at[slot, pl.ds(piece * size, size)]
                cell = (b, piece // 2)

                @pl.when(piece % 2 == core)
                def _():
                    move = pltpu.make_async_copy(source, keep_ref.at[cell], sems.at[slot, piece])
                    move.start() if what == "start" else move.wait()

                @pl.when(piece % 2 != core)
                def _():
                    move = pltpu.make_async_remote_copy(
                        src_ref=source, dst_ref=send_ref.at[cell], send_sem=sems.at[slot, piece], recv_sem=cell_sems.at[b, piece // 2],
                        device_id=(win + 1 - 2 * core, blk), device_id_type=MESH,
                    )
                    if what == "start":
                        move.start()
                    else:
                        move.wait_send()

        for b in range(shards):
            slot = b % 2
            if b >= 2:
                act(b - 2, slot, "wait")
            for k in range(count):
                stage[slot, k * part : (k + 1) * part] = acc_up[b * part : (b + 1) * part, k * width : (k + 1) * width].astype(bf16)
            base = count * part
            half = width // 2
            for k in range(2):
                stage[slot, base : base + half, k * half : (k + 1) * half] = acc_down[
                    k * half : (k + 1) * half, b * down_part : (b + 1) * down_part
                ].astype(bf16)
            base += half
            stage[slot, base : base + part] = acc_out[b * part : (b + 1) * part, :].astype(bf16)
            stage[slot, base + part :] = jnp.zeros((rows - base - part, width), bf16)
            act(b, slot, "start")
        for b in range(shards - 2, shards):
            act(b, b % 2, "wait")
        for b in range(shards):
            for x in range(2):
                pltpu.make_async_remote_copy(
                    src_ref=keep_ref.at[b, x], dst_ref=send_ref.at[b, x], send_sem=sems.at[0, 0], recv_sem=cell_sems.at[b, x],
                    device_id=(win + 1 - 2 * core, blk), device_id_type=MESH,
                ).wait_recv()
        for n in range(cot_count):
            return_tile(tile_order(n), out_rows.at[n], out_ref, send_sems.at[n], recv_sems, False)


def row_cuts(count, part, size):
    cuts = []
    for k in range(count):
        start = k * part
        while start < (k + 1) * part:
            end = min((k + 1) * part, (start // size + 1) * size)
            cuts.append((k, start - k * part, end - start, start // size, start % size))
            start = end
    return cuts


def add_into(target, got):
    target[...] = (target[...].astype(jnp.float32) + got[...].astype(jnp.float32)).astype(jnp.bfloat16)


def finish_kernel(groups, *refs):
    f32, bf16 = jnp.float32, jnp.bfloat16
    parts = refs[: 3 * groups]
    (
        rows_ref, resid_ref, gain, shift, weight, vec_two, vec_up, early_keep, early_other,
        tok_ref, late_ref, early_ref,
        joined, turned, vec, out_rows, cells, core_got, late_bufs, early_bufs, send_sems, recv_sems, load_sems, chain_send, chain_recv, keep_sems,
    ) = refs[3 * groups :]
    step, steps = pl.program_id(0), pl.num_programs(0)
    length, width = rows_ref.shape
    lanes = width // groups
    part = width // 8
    win, blk, core, layer, side = position()
    pair, low, high = win // 2, layer % 2, layer // 2
    core_peer = (win + 1 - 2 * core, blk)
    pair_peer = (win + 2 - 4 * pair, blk)
    side_peer = (win, blk + 1 - 2 * side)
    low_peer = (win, blk + 2 - 4 * low)
    high_peer = (win, blk + 4 - 8 * high)

    def remote(source, target, number, peer):
        return pltpu.make_async_remote_copy(
            src_ref=source, dst_ref=target, send_sem=chain_send.at[number], recv_sem=chain_recv.at[number],
            device_id=peer, device_id_type=MESH,
        )

    early_mid, early_more, early_high, early_final = early_bufs

    def loads():
        moves = ((early_keep, early_mid), (early_other, early_more))
        return [pltpu.make_async_copy(a, b, load_sems.at[n]) for n, (a, b) in enumerate(moves)]

    def second_step(state, got, base):
        return [
            remote(state.at[0, :, 1 - pair], got.at[0], base, pair_peer),
            remote(state.at[1, :, 1 - side], got.at[1], base + 1, side_peer),
        ]

    def add_second(state, got, mid):
        for z in range(2):
            mid[0, z] = (state[0, z, pair].astype(f32) + got[0, z].astype(f32)).astype(bf16)
            mid[1, z] = (state[1, z, side].astype(f32) + got[1, z].astype(f32)).astype(bf16)

    def low_step(mid, got, base):
        return [remote(mid.at[:, 1 - low], got, base, low_peer)]

    def add_low_step(mid, got):
        for z in range(2):
            got[z] = (mid[z, low].astype(f32) + got[z].astype(f32)).astype(bf16)

    def high_step(mid, got, base):
        return [remote(mid.at[1 - high], got, base, high_peer)]

    def add_high_step(mid, got, final):
        final[...] = (mid[high].astype(f32) + got[...].astype(f32)).astype(bf16)

    def share(final, target, base):
        return [
            remote(final, target.at[win], base, core_peer),
            remote(final, target.at[win], base + 1, pair_peer),
        ]

    def pass_on(target, base):
        return [remote(target.at[win + 2 - 4 * pair], target.at[win + 2 - 4 * pair], base, core_peer)]

    def start(moves):
        for move in moves:
            move.start()

    def wait(moves):
        for move in moves:
            move.wait()

    late_first, late_second, late_mid, late_low, late_high, late_final = late_bufs
    early_base, late_base = 8, 0

    @pl.when(step == 0)
    def _():
        start(loads())
        greet_owners(steps, [core_peer, pair_peer, side_peer, low_peer, high_peer])
        wait(loads())
        for z in range(2):
            add_into(early_mid.at[z], early_more.at[z])
        start(high_step(early_mid, early_high, early_base))
        vec[...] = jnp.zeros_like(vec)

    tile = tile_order(step)
    rows = pl.ds(pl.multiple_of(tile * length, length), length)
    for g in range(groups):
        dq, own, other = parts[3 * g : 3 * g + 3]
        columns = slice(g * lanes, (g + 1) * lanes)
        joined[rows, columns] = dq[...]
        both = (own[...].astype(f32) + other[...].astype(f32)).astype(bf16)
        joined[rows, width + g * lanes : width + (g + 1) * lanes] = both[:, :lanes]
        joined[rows, 2 * width + g * lanes : 2 * width + (g + 1) * lanes] = both[:, lanes:]
        vec[0:1, columns] += column_sum(dq[...].astype(f32))
        vec[1:2, columns] += column_sum(both[:, lanes:].astype(f32))
    grad = across(joined[rows, :], weight[...])
    normal, rstd = norm_parts(rows_ref[...].astype(f32))
    turned[tile] = (normal * gain[...] + shift[...]).astype(bf16).T
    vec[2:3] += column_sum(grad * normal)
    vec[3:4] += column_sum(grad)
    out_rows[step] = (resid_ref[...].astype(f32) + norm_back(grad, normal, rstd, gain[...])).astype(bf16)
    return_tile(tile, out_rows.at[step], tok_ref, send_sems.at[step], recv_sems, True)

    @pl.when(step == 1)
    def _():
        wait(high_step(early_mid, early_high, early_base))
        add_high_step(early_mid, early_high, early_final)
        start(share(early_final, early_ref, early_base + 1))
        pltpu.make_async_copy(early_final, early_ref.at[win], keep_sems.at[0]).start()

    @pl.when(step == steps - 1)
    def _():
        size = cells.shape[5]
        cuts = row_cuts(3, part, size)
        for k in range(3):
            full = jnp.dot(turned[0], joined[0:length, k * width : (k + 1) * width], preferred_element_type=f32)
            for n in range(1, 4):
                full = full + jnp.dot(
                    turned[n], joined[n * length : (n + 1) * length, k * width : (k + 1) * width], preferred_element_type=f32
                )
            for b in range(8):
                for which, first, count, piece, row in cuts:
                    if which == k:
                        cells[piece % 2, b // 4, b // 2 % 2, b % 2, piece // 2, row : row + count] = full[
                            b * part + first : b * part + first + count
                        ].astype(bf16)
        tail = jnp.concatenate(
            [vec[...], vec_two[...]] + [vec_up[:, n * width : (n + 1) * width] for n in range(4)]
            + [jnp.zeros((4 * size - 3 * part - 12, width), f32)],
            axis=0,
        ).astype(bf16)
        for b in range(8):
            cells[1, b // 4, b // 2 % 2, b % 2, 1, 3 * part - 3 * size :] = tail
        exchange = [remote(cells.at[1 - core], core_got, late_base, core_peer)]
        start(exchange)
        wait(share(early_final, early_ref, early_base + 1))
        start(pass_on(early_ref, early_base + 3))
        wait(exchange)
        mine = cells.at[core]
        for b in range(8):
            for x in range(2):
                add_into(mine.at[b // 4, b // 2 % 2, b % 2, x], core_got.at[b // 4, b // 2 % 2, b % 2, x])
        first = [
            remote(mine.at[0, :, 1 - side], late_first.at[0], late_base + 1, side_peer),
            remote(mine.at[1, :, :, 1 - pair], late_first.at[1], late_base + 2, pair_peer),
        ]
        start(first)
        wait(first)
        state = core_got.at[0]
        for z in range(2):
            for n in range(2):
                state[0, z, n] = (mine[0, z, side, n].astype(f32) + late_first[0, z, n].astype(f32)).astype(bf16)
                state[1, z, n] = (mine[1, z, n, pair].astype(f32) + late_first[1, z, n].astype(f32)).astype(bf16)
        start(second_step(state, late_second, late_base + 3))
        wait(second_step(state, late_second, late_base + 3))
        add_second(state, late_second, late_mid)
        start(low_step(late_mid, late_low, late_base + 5))
        wait(low_step(late_mid, late_low, late_base + 5))
        add_low_step(late_mid, late_low)
        start(high_step(late_low, late_high, late_base + 6))
        wait(high_step(late_low, late_high, late_base + 6))
        add_high_step(late_low, late_high, late_final)
        start(share(late_final, late_ref, early_base + 4))
        keep_late = pltpu.make_async_copy(late_final, late_ref.at[win], keep_sems.at[1])
        keep_late.start()
        wait(share(late_final, late_ref, early_base + 4))
        start(pass_on(late_ref, early_base + 6))
        wait(pass_on(early_ref, early_base + 3))
        wait(pass_on(late_ref, early_base + 6))
        pltpu.make_async_copy(early_final, early_ref.at[win], keep_sems.at[0]).wait()
        keep_late.wait()
        for n in range(4):
            return_tile(tile_order(n), out_rows.at[n], tok_ref, send_sems.at[n], recv_sems, False)


def first_send_kernel(place, keep_left, other_left, keep_right, other_right, left_ref, right_ref):
    for keep, other, target in ((keep_left, other_left, left_ref), (keep_right, other_right, right_ref)):
        target[...] = (keep[...].astype(jnp.float32) + other[...].astype(jnp.float32)).astype(jnp.bfloat16).reshape(target.shape)


def sum_low(target, refs):
    total = refs[0][...].astype(jnp.float32)
    for ref in refs[1:]:
        total = total + ref[...].astype(jnp.float32)
    target[...] = total.astype(jnp.bfloat16).reshape(target.shape)


def second_send_kernel(place, *refs):
    for n in range(4):
        sum_low(refs[12 + n], refs[3 * n : 3 * n + 3])


def third_send_kernel(place, *refs):
    for n in range(4):
        sum_low(refs[8 + n], refs[2 * n : 2 * n + 2])


def unpack_kernel(early, late, qkv_ref, out_ref, up_ref, down_ref):
    f32 = jnp.float32
    part, width = out_ref.shape
    count = up_ref.shape[1] // width
    half = width // 2

    def cells(source, first, rows):
        size = source.shape[1]
        parts = []
        while rows > 0:
            take = min(rows, size - first % size)
            parts.append(source[first // size, first % size : first % size + take])
            first, rows = first + take, rows - take
        return (parts[0] if len(parts) == 1 else jnp.concatenate(parts, axis=0)).astype(f32)

    for k in range(3):
        qkv_ref[:, k * width : (k + 1) * width] = cells(late, k * part, part)
    for k in range(count):
        up_ref[:, k * width : (k + 1) * width] = cells(early, k * part, part)
    turned = cells(early, count * part, half)
    down_ref[:, :half] = turned[:, :half].T
    down_ref[:, half:] = turned[:, half:].T
    out_ref[...] = cells(early, count * part + half, part)


def general_body(
    tokens,
    cotangent,
    w_qkv,
    b_q,
    b_v,
    w_out,
    b_out,
    gain_one,
    shift_one,
    gain_two,
    shift_two,
    w_up,
    b_up,
    w_down,
    b_down,
    rand_owner,
    rand_sub,
    global_ids,
    species,
):
    blk_count = lax.axis_size("blk")
    blk_pos = lax.axis_index("blk")
    win_pos = lax.axis_index("win")
    windows, length, model_width = tokens.shape
    blocks = rand_owner.shape[1]
    heads = rand_owner.shape[2]
    picks = rand_owner.shape[3]
    glob_count = global_ids.shape[1]
    own_blocks = blocks // blk_count
    block_len = length // own_blocks
    head_dim = model_width // heads
    pair_width = 2 * head_dim
    all_rows = windows * length
    key_count = 3 + glob_count + picks
    per_device = own_blocks * heads * picks
    slot_cap = max(2, 2 * per_device // blk_count)
    score_scale = head_dim ** (-0.5)
    f32 = jnp.float32
    bf16 = jnp.bfloat16
    tokens_f = tokens.reshape(all_rows, model_width).astype(f32)
    normed_f, norm_one_pull = jax.vjp(layer_norm, tokens_f, gain_one, shift_one)
    normed = normed_f.astype(bf16)
    joined = jnp.dot(normed, w_qkv, preferred_element_type=f32)
    query_vals = (joined[:, :model_width] + b_q).astype(bf16)
    key_vals = joined[:, model_width : 2 * model_width].astype(bf16)
    value_vals = (joined[:, 2 * model_width :] + b_v).astype(bf16)

    def to_heads(tensor):
        return tensor.reshape(windows, own_blocks, block_len, heads, head_dim).transpose(
            0, 1, 3, 2, 4
        )

    def from_heads(tensor):
        return tensor.transpose(0, 1, 3, 2, 4).reshape(all_rows, model_width)

    query_heads = to_heads(query_vals)
    local_pairs = jnp.concatenate([to_heads(key_vals), to_heads(value_vals)], axis=-1)
    rimmed = padded(local_pairs, (("blk", 1),), 1)
    block_ids = blk_pos * own_blocks + jnp.arange(own_blocks, dtype=jnp.int32)
    owned_glob = (global_ids[:, :, None] == block_ids[None, None, :]).astype(bf16)
    glob_terms = jnp.einsum("wgb,wbhsc->wghsc", owned_glob, local_pairs, preferred_element_type=f32)
    glob_pairs = lax.psum(glob_terms.astype(jnp.bfloat16), "blk").astype(jnp.float32).astype(bf16)
    owner_rows = rand_owner.reshape(windows, blk_count, per_device)
    sub_rows = rand_sub.reshape(windows, blk_count, per_device)
    owner_hits = (owner_rows[..., None] == jnp.arange(blk_count, dtype=jnp.int32)).astype(jnp.int32)
    slot_rows = jnp.sum(owner_hits * (jnp.cumsum(owner_hits, axis=2) - 1), axis=-1)
    my_owner = lax.dynamic_index_in_dim(owner_rows, blk_pos, 1, keepdims=False)
    my_slot = lax.dynamic_index_in_dim(slot_rows, blk_pos, 1, keepdims=False)
    fetch_index = my_owner * slot_cap + my_slot
    head_of_row = jnp.arange(per_device, dtype=jnp.int32) // picks % heads
    source_rows = sub_rows * heads + head_of_row[None, None, :]
    requester = jnp.arange(blk_count, dtype=jnp.int32)[None, :, None]
    target_rows = jnp.where(
        owner_rows == blk_pos, requester * slot_cap + slot_rows, blk_count * slot_cap
    )
    send_table = jnp.full((windows, blk_count * slot_cap + 1), own_blocks * heads, jnp.int32)
    send_table = jax.vmap(set_rows)(
        send_table, target_rows.reshape(windows, -1), source_rows.reshape(windows, -1)
    )[:, : blk_count * slot_cap]
    flat_pairs = jnp.concatenate(
        [
            local_pairs.reshape(windows, own_blocks * heads, block_len, pair_width),
            jnp.zeros((windows, 1, block_len, pair_width), bf16),
        ],
        axis=1,
    )
    outgoing = jax.vmap(take_rows)(flat_pairs, send_table).reshape(
        windows, blk_count, slot_cap, block_len, pair_width
    )
    incoming = lax.all_to_all(outgoing, "blk", split_axis=1, concat_axis=1, tiled=True).reshape(
        windows, blk_count * slot_cap, block_len, pair_width
    )
    rand_pairs = jax.vmap(take_rows)(incoming, fetch_index).reshape(
        windows, own_blocks, heads, picks, block_len, pair_width
    )
    near_pairs = jnp.stack(
        [rimmed[:, 0:own_blocks], rimmed[:, 1 : own_blocks + 1], rimmed[:, 2 : own_blocks + 2]],
        axis=3,
    )
    far_pairs = jnp.broadcast_to(
        glob_pairs.transpose(0, 2, 1, 3, 4)[:, None],
        (windows, own_blocks, heads, glob_count, block_len, pair_width),
    )
    gathered_keys = jnp.concatenate([near_pairs, far_pairs, rand_pairs], axis=3).reshape(
        windows, own_blocks, heads, key_count * block_len, pair_width
    )
    set_keys = gathered_keys[..., :head_dim]
    set_values = gathered_keys[..., head_dim:]
    block_flags = jnp.concatenate(
        [
            (block_ids > 0)[:, None],
            jnp.ones((own_blocks, 1), jnp.bool_),
            (block_ids < blocks - 1)[:, None],
            jnp.ones((own_blocks, glob_count + picks), jnp.bool_),
        ],
        axis=1,
    )
    key_valid = jnp.repeat(block_flags, block_len, axis=1)[None, :, None, None, :]

    def score_block():
        raw_scores = (
            jnp.einsum("wbhqe,wbhke->wbhqk", query_heads, set_keys, preferred_element_type=f32)
            * score_scale
        )
        return jnp.where(key_valid, raw_scores, masked_score)

    score_matrix = score_block()
    top_score = jnp.max(score_matrix, axis=-1, keepdims=True)
    log_total = top_score + jnp.log(
        jnp.sum(jnp.exp(score_matrix - top_score), axis=-1, keepdims=True)
    )
    probs_low = jnp.exp(score_matrix - log_total).astype(bf16)
    attended = jnp.einsum(
        "wbhqk,wbhke->wbhqe", probs_low, set_values, preferred_element_type=f32
    ).astype(bf16)
    merged = from_heads(attended)
    residual = tokens_f + (jnp.dot(merged, w_out, preferred_element_type=f32) + b_out)
    second_f, norm_two_pull = jax.vjp(layer_norm, residual, gain_two, shift_two)
    second = second_f.astype(bf16)
    inner_f = jnp.dot(second, w_up, preferred_element_type=f32) + b_up
    active_f, gelu_pull = jax.vjp(partial(jax.nn.gelu, approximate=False), inner_f)
    active = active_f.astype(bf16)
    output = residual + (jnp.dot(active, w_down, preferred_element_type=f32) + b_down)
    species_count = jnp.sum(
        (species[:, None] == jnp.arange(SPECIES, dtype=jnp.int32)[None, :]).astype(f32), axis=0
    )
    my_species = lax.dynamic_slice_in_dim(species, win_pos * windows, windows)
    own_count = jnp.sum(
        (my_species[:, None] == jnp.arange(SPECIES, dtype=jnp.int32)[None, :]).astype(f32)
        * species_count[None, :],
        axis=1,
    )
    window_scale = jnp.sqrt(species.shape[0] / (SPECIES * own_count))
    upstream = (cotangent.astype(f32) * window_scale[:, None, None]).reshape(all_rows, model_width)
    grad_branch = upstream.astype(bf16)
    grad_w_down = jnp.einsum("tf,td->fd", active, grad_branch, preferred_element_type=f32)
    grad_b_down = jnp.sum(grad_branch, axis=0, dtype=f32)
    grad_active = jnp.einsum("td,fd->tf", grad_branch, w_down, preferred_element_type=f32)
    grad_inner = gelu_pull(grad_active)[0].astype(bf16)
    grad_w_up = jnp.einsum("td,tf->df", second, grad_inner, preferred_element_type=f32)
    grad_b_up = jnp.sum(grad_inner, axis=0, dtype=f32)
    grad_second = jnp.einsum("tf,df->td", grad_inner, w_up, preferred_element_type=f32)
    grad_resid_norm, grad_gain_two, grad_shift_two = norm_two_pull(grad_second)
    grad_resid = upstream + grad_resid_norm
    grad_proj = grad_resid.astype(bf16)
    grad_w_out = jnp.einsum("ti,to->io", merged, grad_proj, preferred_element_type=f32)
    grad_b_out = jnp.sum(grad_proj, axis=0, dtype=f32)
    grad_attended = to_heads(
        jnp.einsum("to,io->ti", grad_proj, w_out, preferred_element_type=f32).astype(bf16)
    )
    probs_full = jnp.exp(score_block() - log_total)
    grad_probs = jnp.einsum(
        "wbhqe,wbhke->wbhqk", grad_attended, set_values, preferred_element_type=f32
    )
    grad_set_values = jnp.einsum(
        "wbhqk,wbhqe->wbhke", probs_full.astype(bf16), grad_attended, preferred_element_type=f32
    )
    row_dot = jnp.sum(probs_full * grad_probs, axis=-1, keepdims=True)
    grad_scores = (probs_full * (grad_probs - row_dot)).astype(bf16)
    grad_query = (
        jnp.einsum("wbhqk,wbhke->wbhqe", grad_scores, set_keys, preferred_element_type=f32)
        * score_scale
    )
    grad_set_keys = (
        jnp.einsum("wbhqk,wbhqe->wbhke", grad_scores, query_heads, preferred_element_type=f32)
        * score_scale
    )
    grad_set = jnp.concatenate([grad_set_keys, grad_set_values], axis=-1).reshape(
        windows, own_blocks, heads, key_count, block_len, pair_width
    )
    extended = (
        jnp.pad(grad_set[:, :, :, 1], ((0, 0), (1, 1), (0, 0), (0, 0), (0, 0)))
        + jnp.pad(grad_set[:, :, :, 0], ((0, 0), (0, 2), (0, 0), (0, 0), (0, 0)))
        + jnp.pad(grad_set[:, :, :, 2], ((0, 0), (2, 0), (0, 0), (0, 0), (0, 0)))
    )
    edge_grads = jnp.concatenate([extended[:, :1], extended[:, own_blocks + 1 :]], axis=1)
    edge_back = padded(edge_grads.astype(jnp.bfloat16), (("blk", 1),), 1).astype(edge_grads.dtype)
    pair_grad = extended[:, 1 : own_blocks + 1]
    pair_grad = pair_grad.at[:, 0].add(edge_back[:, 0]).at[:, own_blocks - 1].add(edge_back[:, 3])
    glob_grad = jnp.sum(grad_set[:, :, :, 3 : 3 + glob_count], axis=1).transpose(0, 2, 1, 3, 4)
    glob_total = lax.psum(glob_grad.astype(jnp.bfloat16), "blk").astype(jnp.float32)
    pair_grad = pair_grad + jnp.einsum(
        "wgb,wghsc->wbhsc", owned_glob.astype(f32), glob_total, precision=lax.Precision.HIGHEST
    )
    rand_grad = grad_set[:, :, :, 3 + glob_count :].reshape(
        windows, per_device, block_len, pair_width
    )
    back_out = jax.vmap(add_rows)(
        jnp.zeros((windows, blk_count * slot_cap, block_len, pair_width), f32),
        fetch_index,
        rand_grad,
    )
    back_in = lax.all_to_all(
        back_out.reshape(windows, blk_count, slot_cap, block_len, pair_width).astype(jnp.bfloat16),
        "blk",
        split_axis=1,
        concat_axis=1,
        tiled=True,
    ).astype(jnp.float32)
    owner_sum = jax.vmap(add_rows)(
        jnp.zeros((windows, own_blocks * heads + 1, block_len, pair_width), f32),
        send_table,
        back_in.reshape(windows, blk_count * slot_cap, block_len, pair_width),
    )
    pair_grad = pair_grad + owner_sum[:, : own_blocks * heads].reshape(
        windows, own_blocks, heads, block_len, pair_width
    )
    grad_keys = from_heads(pair_grad[..., :head_dim].astype(bf16))
    grad_values = from_heads(pair_grad[..., head_dim:].astype(bf16))
    grad_joined = jnp.concatenate(
        [from_heads(grad_query.astype(bf16)), grad_keys, grad_values], axis=1
    )
    grad_w_qkv = jnp.einsum("td,tc->dc", normed, grad_joined, preferred_element_type=f32)
    grad_b_q = jnp.sum(grad_joined[:, :model_width], axis=0, dtype=f32)
    grad_b_v = jnp.sum(grad_joined[:, 2 * model_width :], axis=0, dtype=f32)
    grad_normed = jnp.einsum("tc,dc->td", grad_joined, w_qkv, preferred_element_type=f32)
    grad_tok_norm, grad_gain_one, grad_shift_one = norm_one_pull(grad_normed)
    grad_tokens = (grad_resid + grad_tok_norm).astype(bf16).reshape(windows, length, model_width)
    local_grads = (
        grad_w_qkv,
        grad_b_q,
        grad_b_v,
        grad_w_out,
        grad_b_out,
        grad_gain_one,
        grad_shift_one,
        grad_gain_two,
        grad_shift_two,
        grad_w_up,
        grad_b_up,
        grad_w_down,
        grad_b_down,
    )
    packed_grads = jnp.concatenate(
        [grad_item.reshape(blk_count, -1) for grad_item in local_grads], axis=1
    )
    total_cols = packed_grads.shape[1]
    win_count = lax.axis_size("win")
    pad_cols = -total_cols % win_count
    shard_sum = lax.psum_scatter(
        packed_grads.astype(jnp.bfloat16), "blk", scatter_dimension=0, tiled=True
    ).astype(jnp.float32)
    split_shard = jnp.pad(shard_sum, ((0, 0), (0, pad_cols))).reshape(win_count, -1)
    group_piece = lax.psum_scatter(
        split_shard.astype(jnp.bfloat16), "win", scatter_dimension=0, tiled=True
    ).astype(jnp.float32)
    summed = (
        lax.all_gather(group_piece.astype(jnp.bfloat16), "win", axis=0, tiled=True)
        .astype(group_piece.dtype)
        .reshape(1, -1)[:, :total_cols]
    )
    shards = []
    offset = 0
    for grad_item in local_grads:
        entry_count = grad_item.size // blk_count
        shards.append(
            summed[0, offset : offset + entry_count].reshape(
                (grad_item.shape[0] // blk_count,) + grad_item.shape[1:]
            )
        )
        offset = offset + entry_count
    out_tokens = output.astype(bf16).reshape(windows, length, model_width)
    return (
        out_tokens,
        grad_tokens,
        shards[0],
        shards[1],
        shards[2],
        shards[3],
        shards[4],
        shards[5],
        shards[6],
        shards[7],
        shards[8],
        shards[9],
        shards[10],
        shards[11],
        shards[12],
    )


def layer_step(*arguments):
    windows = arguments[0].shape[0]
    paired = lax.axis_size("blk") == 2 * windows and lax.axis_size("win") == 4 and windows == 4
    return (paired_body if paired else general_body)(*arguments)


def paired_body(
    tokens,
    cotangent,
    w_qkv,
    b_q,
    b_v,
    w_out,
    b_out,
    gain_one,
    shift_one,
    gain_two,
    shift_two,
    w_up,
    b_up,
    w_down,
    b_down,
    rand_owner,
    rand_sub,
    global_ids,
    species,
):
    f32 = jnp.float32
    bf16 = jnp.bfloat16
    win_count = lax.axis_size("win")
    blk_count = lax.axis_size("blk")
    win_pos = lax.axis_index("win")
    blk_pos = lax.axis_index("blk")
    layers, length, width = tokens.shape
    core, layer, side = win_pos % 2, blk_pos // 2, blk_pos % 2
    blocks, heads, picks = rand_owner.shape[1:]
    own_blocks = blocks // blk_count
    half_blocks = blocks // 2
    block_len = length // own_blocks
    head_dim = width // heads
    all_rows = layers * length
    lanes = HEADS_PER_GROUP * head_dim
    groups = heads // HEADS_PER_GROUP
    score_scale = head_dim ** (-0.5)

    def regroup(value):
        parts = []
        for step in range(layers):
            part = lax.dynamic_index_in_dim(value, (layer + step) % layers, 0, keepdims=False)
            parts.append(lax.ppermute(part, ("win", "blk"), regroup_pairs(win_count, layers, step)))
        return parts

    def send_back(value):
        parts = []
        for step in range(layers):
            pairs = [(b, a) for a, b in regroup_pairs(win_count, layers, step)]
            parts.append(lax.ppermute(value[step * length : (step + 1) * length], ("win", "blk"), pairs))
        return parts

    def in_order(parts):
        result = jnp.zeros((layers, length, width), parts[0].dtype)
        for step, part in enumerate(parts):
            result = lax.dynamic_update_index_in_dim(result, part, (layer + step) % layers, 0)
        return result

    def takes(micros):
        return pl.CostEstimate(flops=micros * 1_000_000_000, bytes_accessed=micros * 1_000_000, transcendentals=0)

    rows_in = jnp.concatenate(regroup(tokens), axis=0)
    cot_in = regroup(cotangent)

    rand_size = blocks * heads * picks
    named = jnp.concatenate(
        [
            lax.dynamic_index_in_dim((rand_owner * own_blocks + rand_sub).reshape(layers, rand_size), layer, 0, keepdims=False),
            lax.dynamic_index_in_dim(global_ids, layer, 0, keepdims=False),
        ]
    )
    named = jnp.where(side == core, named, swap(named, 1, 0))

    def place_of(block):
        owner = block // own_blocks
        half = jnp.where(owner % 2 == core, 0, half_blocks)
        return half + ((layer - owner // 2) % layers) * own_blocks + block % own_blocks

    slot = jnp.arange(half_blocks, dtype=jnp.int32)
    slot_block = (((layer - slot // own_blocks) % layers) * 2 + core) * own_blocks + slot % own_blocks
    table = jnp.concatenate(
        [
            place_of(named),
            slot_block,
            place_of(jnp.maximum(slot_block - 1, 0)),
            place_of(jnp.minimum(slot_block + 1, blocks - 1)),
        ]
    )
    sizes = (heads, picks, rand_size, half_blocks)

    tile = length

    def by_rows(columns):
        return pl.BlockSpec((tile, columns), lambda i: (i, 0))

    def by_tile(columns):
        return pl.BlockSpec((tile, columns), lambda i: (tile_order(i), 0))

    def whole(*shape, once=True):
        mode = pl.Buffered(1) if once else None
        return pl.BlockSpec(shape, lambda i: (0,) * len(shape), pipeline_mode=mode)

    scalars = pl.BlockSpec(memory_space=pltpu.SMEM)
    wide = w_up.shape[1]
    params = pltpu.CompilerParams(vmem_limit_bytes=60 << 20)
    row = lambda vector: vector.reshape(1, -1)
    query, key_value = pl.pallas_call(
        partial(qkv_kernel, score_scale),
        grid=(all_rows // tile,),
        in_specs=[by_rows(width), whole(1, width), whole(1, width), whole(width, 3 * width), whole(2, width)],
        out_specs=[by_rows(width), by_rows(2 * width)],
        out_shape=[jax.ShapeDtypeStruct((all_rows, width), bf16), jax.ShapeDtypeStruct((all_rows, 2 * width), bf16)],
        compiler_params=params,
        cost_estimate=takes(12),
        name="qkv",
    )(rows_in, row(gain_one), row(shift_one), w_qkv, jnp.stack([b_q, b_v]))
    key_value_other = swap(key_value, 1, 0)

    def lane_block(first):
        return pl.BlockSpec((all_rows, lanes), lambda g, t: (0, first + g))

    store = pltpu.VMEM((blocks, block_len, lanes), bf16)
    attended, log_total = pl.pallas_call(
        partial(attend_kernel, sizes, blocks, head_dim),
        grid_spec=pltpu.PrefetchScalarGridSpec(
            num_scalar_prefetch=1,
            grid=(groups,),
            in_specs=[lane_block(0), lane_block(0), lane_block(0), lane_block(groups), lane_block(groups)],
            out_specs=[lane_block(0), pl.BlockSpec((1, half_blocks, lanes), lambda g, t: (g, 0, 0))],
            scratch_shapes=[store, store],
        ),
        out_shape=[
            jax.ShapeDtypeStruct((all_rows, width), bf16),
            jax.ShapeDtypeStruct((groups, half_blocks, lanes), f32),
        ],
        compiler_params=pltpu.CompilerParams(vmem_limit_bytes=56 << 20),
        cost_estimate=takes(37),
        name="attend",
    )(table, query, key_value, key_value_other, key_value, key_value_other)

    species_count = jnp.sum(
        (species[:, None] == jnp.arange(SPECIES, dtype=jnp.int32)[None, :]).astype(f32), axis=0
    )
    my_window = ((win_pos // 2) * 2 + side) * layers + layer
    my_species = lax.dynamic_index_in_dim(species, my_window, 0, keepdims=False)
    own_count = jnp.sum(
        (my_species == jnp.arange(SPECIES, dtype=jnp.int32)).astype(f32) * species_count
    )
    window_scale = jnp.sqrt(species.shape[0] / (SPECIES * own_count))
    payload = 2 * wide // blk_count + width // blk_count
    payload += -payload % (16 * win_count)
    stays = jax.ShapeDtypeStruct((blk_count, win_count // 2, payload // win_count, width), bf16)
    any_place = pl.BlockSpec(memory_space=pl.ANY)
    out_tokens, grad_resid, grad_attended, vec_two, vec_up, early_keep, early_other = pl.pallas_call(
        partial(ffn_kernel, 256, blk_count, layers),
        grid=(layers,),
        in_specs=[
            scalars, by_tile(width), by_tile(width), *[any_place] * layers, whole(width, width), whole(1, width), whole(1, width),
            whole(1, width), whole(width, wide), whole(1, wide), whole(wide, width), whole(1, width),
        ],
        out_specs=[any_place, by_tile(width), by_tile(width), whole(4, width), whole(1, wide), any_place, any_place],
        out_shape=[
            jax.ShapeDtypeStruct((layers, length, width), bf16),
            jax.ShapeDtypeStruct((all_rows, width), bf16),
            jax.ShapeDtypeStruct((all_rows, width), bf16),
            jax.ShapeDtypeStruct((4, width), f32),
            jax.ShapeDtypeStruct((1, wide), f32),
            stays,
            stays,
        ],
        scratch_shapes=[
            pltpu.VMEM((width, wide), f32),
            pltpu.VMEM((width, wide), f32),
            pltpu.VMEM((width, width), f32),
            pltpu.VMEM((2, payload, width), bf16),
            pltpu.SemaphoreType.DMA((2, 4)),
            pltpu.VMEM((length, wide), bf16),
            pltpu.VMEM((length, wide), bf16),
            pltpu.VMEM((2, length, width), bf16),
            pltpu.SemaphoreType.DMA((2,)),
            pltpu.VMEM((layers, length, width), bf16),
            pltpu.SemaphoreType.DMA((layers,)),
            pltpu.SemaphoreType.DMA((layers,)),
            pltpu.SemaphoreType.DMA((blk_count, 2)),
        ],
        compiler_params=pltpu.CompilerParams(vmem_limit_bytes=60 << 20, collective_id=1, has_side_effects=True),
        cost_estimate=takes(90),
        name="ffn",
    )(
        window_scale.reshape(1), rows_in, attended, *cot_in, w_out, row(b_out), row(gain_two), row(shift_two),
        w_up, row(b_up), w_down, row(b_down),
    )

    pair = win_pos // 2
    early_rows = payload // win_count
    late_rows = 3 * width // blk_count + 32
    late_size = late_rows // win_count
    cell = (early_rows, width)
    early_keep = early_keep.reshape((2, 2, 2, 2) + cell)
    early_other = early_other.reshape((2, 2, 2, 2) + cell)
    place = jnp.stack([side, pair, layer % 2])

    def picked(index):
        return pl.BlockSpec((1, 1, 1, 1) + cell, lambda z, n, p: index(z, n, p) + (0, 0))

    def listed(index):
        return pl.BlockSpec((1, 1) + cell, lambda z, n, p: index(z, n, p) + (0, 0))

    def cells_of(count):
        return [jax.ShapeDtypeStruct((2, 2) + cell, bf16)] * count

    def first_send():
        left = picked(lambda z, n, p: (0, z, 1 - p[0], n))
        right = picked(lambda z, n, p: (1, z, n, 1 - p[1]))
        return pl.pallas_call(
            first_send_kernel,
            grid_spec=pltpu.PrefetchScalarGridSpec(
                num_scalar_prefetch=1, grid=(2, 2), in_specs=[left, left, right, right], out_specs=[listed(lambda z, n, p: (z, n))] * 2
            ),
            out_shape=cells_of(2),
            cost_estimate=takes(3),
            name="first_send",
        )(place, early_keep, early_other, early_keep, early_other)

    def second_send(got_left, got_right):
        specs, operands = [], []
        for far in (0, 1):
            bit = lambda n, p, f=far: p[n] if f == 0 else 1 - p[n]
            left = picked(lambda z, n, p, bit=bit: (0, z, p[0], bit(1, p)))
            right = picked(lambda z, n, p, bit=bit: (1, z, bit(0, p), p[1]))
            specs += [left, left, listed(lambda z, n, p, bit=bit: (z, bit(1, p)))]
            operands += [early_keep, early_other, got_left]
            specs += [right, right, listed(lambda z, n, p, bit=bit: (z, bit(0, p)))]
            operands += [early_keep, early_other, got_right]
        rows_spec = pl.BlockSpec((1,) + cell, lambda z, n, p: (z, 0, 0))
        return pl.pallas_call(
            second_send_kernel,
            grid_spec=pltpu.PrefetchScalarGridSpec(num_scalar_prefetch=1, grid=(2, 1), in_specs=specs, out_specs=[rows_spec] * 4),
            out_shape=[jax.ShapeDtypeStruct((2,) + cell, bf16)] * 4,
            cost_estimate=takes(4),
            name="second_send",
        )(place, *operands)

    def third_send(parts, got):
        specs, operands = [], []
        for far in (0, 1):
            spec = pl.BlockSpec((1,) + cell, lambda z, n, p, f=far: (p[2] if f == 0 else 1 - p[2], 0, 0))
            for half in range(2):
                specs += [spec, spec]
                operands += [parts[half], got[half]]
        out = pl.BlockSpec((1,) + cell, lambda z, n, p: (0, 0, 0))
        return pl.pallas_call(
            third_send_kernel,
            grid_spec=pltpu.PrefetchScalarGridSpec(num_scalar_prefetch=1, grid=(1, 1), in_specs=specs, out_specs=[out] * 4),
            out_shape=[jax.ShapeDtypeStruct((1,) + cell, bf16)] * 4,
            cost_estimate=takes(3),
            name="third_send",
        )(place, *operands)

    first_left, first_right = first_send()
    first_left, first_right = swap(first_left, 0, 1), swap(first_right, 2, 0)

    grad_parts = []
    for group in range(groups):
        after = []
        if group == 1:
            keep_left, keep_right, send_left, send_right = second_send(first_left, first_right)
            after = [keep_left]
            second = swap(send_left, 2, 0), swap(send_right, 0, 1)
        if group == 2:
            keep_left, keep_right, send_left, send_right = third_send((keep_left, keep_right), second)
            after = [keep_left]
            third = swap(jnp.concatenate([send_left, send_right], axis=0), 0, 2)

        def column(first):
            return pl.BlockSpec((all_rows, lanes), lambda g, t: (0, first))

        def full(columns):
            return pl.BlockSpec((all_rows, columns), lambda g, t: (0, 0))

        grad_store = pltpu.VMEM((blocks, block_len, lanes), f32)
        glob_store = pltpu.VMEM((2, block_len, lanes), f32)
        dq, own, other = pl.pallas_call(
            partial(attend_back_kernel, sizes, blocks, head_dim, score_scale, group),
            grid_spec=pltpu.PrefetchScalarGridSpec(
                num_scalar_prefetch=1,
                grid=(1,),
                in_specs=[
                    column(group), column(group), column(group), column(groups + group), column(groups + group), column(group),
                    pl.BlockSpec((1, half_blocks, lanes), lambda g, t: (group, 0, 0)),
                    *[any_place] * len(after),
                ],
                out_specs=[full(lanes), full(2 * lanes), full(2 * lanes)],
                scratch_shapes=[store, store, grad_store, grad_store, glob_store, glob_store],
            ),
            out_shape=[jax.ShapeDtypeStruct((all_rows, n * lanes), bf16) for n in (1, 2, 2)],
            compiler_params=params,
            cost_estimate=takes(25),
            name="attend_back",
        )(table, query, key_value, key_value_other, key_value, key_value_other, grad_attended, log_total, *after)
        grad_parts += [dq, own, swap(other, 1, 0)]

    def vmem(*shape):
        return pltpu.VMEM(shape, bf16)

    first_shape, mid_shape, low_shape = (2, 2, 2), (2, 2), (2,)
    chain = lambda size: [vmem(*lead, size, width) for lead in (first_shape, mid_shape, mid_shape, low_shape, (), ())]
    grad_tokens, late, early = pl.pallas_call(
        partial(finish_kernel, groups),
        grid=(layers,),
        in_specs=[by_tile(p.shape[1]) for p in grad_parts]
        + [by_tile(width), by_tile(width), whole(1, width), whole(1, width), whole(width, 3 * width), whole(4, width), whole(1, wide)]
        + [any_place] * 2,
        out_specs=[any_place] * 3,
        out_shape=[
            jax.ShapeDtypeStruct((layers, length, width), bf16),
            jax.ShapeDtypeStruct((win_count, late_size, width), bf16),
            jax.ShapeDtypeStruct((win_count, early_rows, width), bf16),
        ],
        scratch_shapes=[
            vmem(all_rows, 3 * width),
            vmem(layers, width, length),
            pltpu.VMEM((4, width), f32),
            vmem(layers, length, width),
            vmem(2, 2, 2, 2, 2, late_size, width),
            vmem(2, 2, 2, 2, late_size, width),
            chain(late_size),
            [vmem(*lead, early_rows, width) for lead in (low_shape, low_shape, (), ())],
            pltpu.SemaphoreType.DMA((layers,)),
            pltpu.SemaphoreType.DMA((layers,)),
            pltpu.SemaphoreType.DMA((2,)),
            pltpu.SemaphoreType.DMA((15,)),
            pltpu.SemaphoreType.DMA((15,)),
            pltpu.SemaphoreType.DMA((2,)),
        ],
        compiler_params=pltpu.CompilerParams(vmem_limit_bytes=62 << 20, collective_id=2, has_side_effects=True),
        cost_estimate=takes(90),
        name="finish",
    )(
        *grad_parts, rows_in, grad_resid, row(gain_one), row(shift_one), w_qkv, vec_two, vec_up,
        jnp.concatenate([keep_left, keep_right], axis=0), third,
    )
    part = width // blk_count
    count = wide // width
    done_qkv, done_out, done_up, done_down = pl.pallas_call(
        unpack_kernel,
        out_shape=[
            jax.ShapeDtypeStruct(shape, f32)
            for shape in ((part, 3 * width), (part, width), (part, wide), (wide // blk_count, width))
        ],
        compiler_params=params,
        cost_estimate=takes(4),
        name="unpack",
    )(early, late)
    late = late.reshape(-1, width)[3 * part :].astype(f32)
    vec = lax.dynamic_slice_in_dim(late[:8], blk_pos * part, part, axis=1)
    vec_wide = lax.dynamic_slice_in_dim(late[8 : 8 + count].reshape(-1), blk_pos * (wide // blk_count), wide // blk_count)
    return (
        out_tokens,
        grad_tokens,
        done_qkv,
        vec[0],
        vec[1],
        done_out,
        vec[4],
        vec[2],
        vec[3],
        vec[5],
        vec[6],
        done_up,
        vec_wide,
        done_down,
        vec[7],
    )


def solution(mesh):
    placed = (
        P("win", "blk", None),
        P("win", "blk", None),
        P(),
        P(),
        P(),
        P(),
        P(),
        P(),
        P(),
        P(),
        P(),
        P(),
        P(),
        P(),
        P(),
        P("win", None, None, None),
        P("win", None, None, None),
        P("win", None),
        P(),
    )
    return jax.shard_map(
        layer_step,
        mesh=mesh,
        in_specs=placed,
        out_specs=(
            P("win", "blk", None),
            P("win", "blk", None),
            P("blk", None),
            P("blk"),
            P("blk"),
            P("blk", None),
            P("blk"),
            P("blk"),
            P("blk"),
            P("blk"),
            P("blk"),
            P("blk", None),
            P("blk"),
            P("blk", None),
            P("blk"),
        ),
        check_vma=False,
    )
```

```python
from functools import partial

import jax
import jax.numpy as jnp
from jax import lax
from jax.experimental import pallas as pl
from jax.experimental.pallas import tpu as pltpu
from jax.sharding import PartitionSpec as P

SPECIES = 4


epsilon = 1e-05
masked_score = -1000000000.0


def padded(cells, sides, width):
    for axis, dim in sides:
        count = lax.axis_size(axis)
        ends = count - 1
        head = lax.slice_in_dim(cells, 0, width, axis=dim)
        tail = lax.slice_in_dim(cells, cells.shape[dim] - width, cells.shape[dim], axis=dim)
        cells = jnp.concatenate(
            [
                lax.ppermute(tail, axis, [(i, (i + 1) % count) for i in range(ends)]),
                cells,
                lax.ppermute(head, axis, [((i + 1) % count, i) for i in range(ends)]),
            ],
            axis=dim,
        )
    return cells


def layer_norm(values, norm_gain, norm_shift):
    average = jnp.mean(values, axis=-1, keepdims=True)
    centred = values - average
    variance = jnp.mean(centred * centred, axis=-1, keepdims=True)
    return centred * lax.rsqrt(variance + epsilon) * norm_gain + norm_shift


def take_rows(source, index_rows):
    return jnp.take(source, index_rows, axis=0)


def add_rows(base, index_rows, update):
    return base.at[index_rows].add(update)


def set_rows(base, index_rows, update):
    return base.at[index_rows].set(update)


HEADS_PER_GROUP = 4


def regroup_pairs(win_count, layers, step):
    pairs = []
    for win in range(win_count):
        for blk in range(2 * layers):
            layer, side = blk // 2, blk % 2
            target = ((layer + step) % layers) * 2 + win % 2
            pairs.append((win * 2 * layers + blk, ((win // 2) * 2 + side) * 2 * layers + target))
    return pairs


def flip_pairs(win_count, blk_count, win_bit, blk_bit):
    return [
        (win * blk_count + blk, (win ^ win_bit) * blk_count + (blk ^ blk_bit))
        for win in range(win_count)
        for blk in range(blk_count)
    ]


def swap(value, win_bit, blk_bit):
    pairs = flip_pairs(lax.axis_size("win"), lax.axis_size("blk"), win_bit, blk_bit)
    return lax.ppermute(value, ("win", "blk"), pairs)


def head_masks(lanes, head_dim, dtype):
    lane = lax.broadcasted_iota(jnp.int32, (1, lanes), 1)
    return [(lane // head_dim == h).astype(dtype) for h in range(lanes // head_dim)]


def block_places(table, slot, group, sizes):
    heads, picks, rand_size, half_blocks = sizes
    block = table[rand_size + 2 + slot]
    near = [table[rand_size + 2 + half_blocks + slot], slot, table[rand_size + 2 + 2 * half_blocks + slot]]
    row = (block * heads + group * HEADS_PER_GROUP) * picks
    rand = [[table[row + h * picks + r] for h in range(HEADS_PER_GROUP)] for r in range(picks)]
    return block, near, rand


def spread_heads(rows, masks):
    return jnp.concatenate([rows * m for m in masks], axis=0)


def pick_heads(square, masks, height):
    total = square[0:height] * masks[0]
    for h in range(1, len(masks)):
        total = total + square[h * height : (h + 1) * height] * masks[h]
    return total


def key_rows(source, near, glob, rand, low_half):
    parts = [source[p] for p in near] + [source[p] for p in glob]
    for places in rand:
        columns = []
        for c in range(len(places) // 2):
            low = source[places[2 * c], :, c * 128 : (c + 1) * 128]
            high = source[places[2 * c + 1], :, c * 128 : (c + 1) * 128]
            columns.append(jnp.where(low_half, low, high))
        parts.append(jnp.concatenate(columns, axis=1))
    return jnp.concatenate(parts, axis=0)


def mask_scores(scores, block, blocks, block_len):
    first = jnp.where(block > 0, scores[:block_len], masked_score)
    last = jnp.where(block < blocks - 1, scores[2 * block_len : 3 * block_len], masked_score)
    return jnp.concatenate([first, scores[block_len : 2 * block_len], last, scores[3 * block_len :]], axis=0)


def across(left, right):
    return lax.dot_general(left, right, (((1,), (1,)), ((), ())), preferred_element_type=jnp.float32)


def down(left, right):
    return lax.dot_general(left, right, (((0,), (0,)), ((), ())), preferred_element_type=jnp.float32)


def load_halves(target, own, other, half_blocks, block_len):
    lanes = own.shape[-1]
    target[0:half_blocks] = own[...].reshape(half_blocks, block_len, lanes)
    target[half_blocks:] = other[...].reshape(half_blocks, block_len, lanes)


def attend_kernel(sizes, blocks, head_dim, table, q_ref, k_own, k_other, v_own, v_other, o_ref, lse_ref, k_all, v_all):
    heads, picks, rand_size, half_blocks = sizes
    block_len = k_all.shape[1]
    lanes = q_ref.shape[1]
    group = pl.program_id(0)
    load_halves(k_all, k_own, k_other, half_blocks, block_len)
    load_halves(v_all, v_own, v_other, half_blocks, block_len)
    low_half = lax.broadcasted_iota(jnp.int32, (block_len, 128), 1) < head_dim
    masks = head_masks(lanes, head_dim, jnp.bfloat16)
    masks_f = head_masks(lanes, head_dim, jnp.float32)
    glob = [table[rand_size], table[rand_size + 1]]

    def one(slot, carry):
        block, near, rand = block_places(table, slot, group, sizes)
        rows = pl.ds(pl.multiple_of(slot * block_len, block_len), block_len)
        queries = spread_heads(q_ref[rows, :], masks)
        keys = key_rows(k_all, near, glob, rand, low_half)
        scores = mask_scores(across(keys, queries), block, blocks, block_len)
        top = jnp.max(scores, axis=0, keepdims=True)
        weights = jnp.exp(scores - top)
        total = jnp.sum(weights, axis=0, keepdims=True)
        probs = (weights * (1.0 / total)).astype(jnp.bfloat16)
        values = key_rows(v_all, near, glob, rand, low_half)
        o_ref[rows, :] = pick_heads(down(probs, values), masks_f, block_len).astype(jnp.bfloat16)
        lse_ref[0, pl.ds(slot, 1), :] = top + jnp.log(total)
        return carry

    lax.fori_loop(0, half_blocks, one, 0, unroll=min(8, half_blocks))


def attend_back_kernel(
    sizes, blocks, head_dim, scale, group,
    table, q_ref, k_own, k_other, v_own, v_other, go_ref, lse_ref, *refs,
):
    dq_ref, own_ref, other_ref, k_all, v_all, dk_all, dv_all, dk_glob, dv_glob = refs[-9:]
    heads, picks, rand_size, half_blocks = sizes
    block_len = k_all.shape[1]
    lanes = q_ref.shape[1]
    f32 = jnp.float32
    load_halves(k_all, k_own, k_other, half_blocks, block_len)
    load_halves(v_all, v_own, v_other, half_blocks, block_len)
    dk_all[...] = jnp.zeros_like(dk_all)
    dv_all[...] = jnp.zeros_like(dv_all)
    dk_glob[...] = jnp.zeros_like(dk_glob)
    dv_glob[...] = jnp.zeros_like(dv_glob)
    low_half = lax.broadcasted_iota(jnp.int32, (block_len, 128), 1) < head_dim
    masks = head_masks(lanes, head_dim, jnp.bfloat16)
    masks_f = head_masks(lanes, head_dim, f32)
    glob = [table[rand_size], table[rand_size + 1]]

    def add_back(grads, near, rand, into, into_glob):
        for n in range(3):
            into[near[n]] += grads[n * block_len : (n + 1) * block_len]
        for n in range(2):
            into_glob[n] += grads[(3 + n) * block_len : (4 + n) * block_len]
        for r in range(picks):
            part = grads[(5 + r) * block_len : (6 + r) * block_len]
            for c in range(lanes // 128):
                cell = part[:, c * 128 : (c + 1) * 128]
                columns = pl.ds(c * 128, 128)
                into[rand[r][2 * c], :, columns] += jnp.where(low_half, cell, 0.0)
                into[rand[r][2 * c + 1], :, columns] += jnp.where(low_half, 0.0, cell)

    def one(slot, carry):
        block, near, rand = block_places(table, slot, group, sizes)
        rows = pl.ds(pl.multiple_of(slot * block_len, block_len), block_len)
        queries = spread_heads(q_ref[rows, :], masks)
        grads_out = spread_heads(go_ref[rows, :], masks)
        keys = key_rows(k_all, near, glob, rand, low_half)
        values = key_rows(v_all, near, glob, rand, low_half)
        scores = mask_scores(across(keys, queries), block, blocks, block_len)
        probs = jnp.exp(scores - lse_ref[0, pl.ds(slot, 1), :])
        grad_probs = across(values, grads_out)
        row_dot = jnp.sum(probs * grad_probs, axis=0, keepdims=True)
        grad_scores = (probs * (grad_probs - row_dot)).astype(jnp.bfloat16)
        add_back(jnp.dot(probs.astype(jnp.bfloat16), grads_out, preferred_element_type=f32), near, rand, dv_all, dv_glob)
        add_back(jnp.dot(grad_scores, queries, preferred_element_type=f32), near, rand, dk_all, dk_glob)
        dq_ref[rows, :] = (pick_heads(down(grad_scores, keys), masks_f, block_len) * scale).astype(jnp.bfloat16)
        return carry

    lax.fori_loop(0, half_blocks, one, 0, unroll=min(8, half_blocks))
    for n in range(2):
        dk_all[glob[n]] += dk_glob[n]
        dv_all[glob[n]] += dv_glob[n]
    for target, start in ((own_ref, 0), (other_ref, half_blocks)):
        for n, source in enumerate((dk_all, dv_all)):
            cells = source[start : start + half_blocks].astype(jnp.bfloat16)
            target[:, n * lanes : (n + 1) * lanes] = cells.reshape(half_blocks * block_len, lanes)


def norm_parts(values):
    average = jnp.mean(values, axis=-1, keepdims=True)
    centred = values - average
    rstd = lax.rsqrt(jnp.mean(centred * centred, axis=-1, keepdims=True) + epsilon)
    return centred * rstd, rstd


def norm_back(grad, normal, rstd, gain):
    scaled = grad * gain
    first = jnp.mean(scaled, axis=-1, keepdims=True)
    second = jnp.mean(scaled * normal, axis=-1, keepdims=True)
    return rstd * (scaled - first - normal * second)


def normal_parts(values):
    cdf = 0.5 + 0.5 * lax.erf(values * 0.5**0.5)
    return cdf, values * jnp.exp(-0.5 * values * values) * 0.3989422804014327


def column_sum(values):
    return jnp.sum(values, axis=0, keepdims=True)


def qkv_kernel(scale, rows_ref, gain, shift, weight, bias, q_ref, kv_ref):
    width = rows_ref.shape[1]
    normal, _ = norm_parts(rows_ref[...].astype(jnp.float32))
    normed = (normal * gain[...] + shift[...]).astype(jnp.bfloat16)

    def part(n):
        columns = slice(n * width, (n + 1) * width)
        return jnp.dot(normed, weight[:, columns], preferred_element_type=jnp.float32)

    q_ref[...] = (part(0) + bias[0:1]).astype(jnp.bfloat16) * jnp.asarray(scale, jnp.bfloat16)
    kv_ref[:, :width] = part(1).astype(jnp.bfloat16)
    kv_ref[:, width:] = (part(2) + bias[1:2]).astype(jnp.bfloat16)


MESH = pl.DeviceIdType.MESH


def tile_order(number):
    return jnp.where(number == 0, 2, jnp.where(number == 2, 3, jnp.where(number == 3, 0, number)))


def position():
    win, blk = lax.axis_index("win"), lax.axis_index("blk")
    return win, blk, win % 2, blk // 2, blk % 2


def owner_of(tile, layers):
    win, blk, core, layer, side = position()
    return (win // 2) * 2 + side, ((layer + layers - tile) % layers) * 2 + core


def greet_owners(layers, peers):
    barrier = pltpu.get_barrier_semaphore()
    others = len(peers)
    for peer in peers:
        pl.semaphore_signal(barrier, inc=1, device_id=peer, device_id_type=MESH)
    _, _, core, _, side = position()
    for tile in range(1, layers):
        pl.semaphore_signal(barrier, inc=1, device_id=owner_of(tile, layers), device_id_type=MESH)

    @pl.when(side != core)
    def _():
        pl.semaphore_signal(barrier, inc=1, device_id=owner_of(0, layers), device_id_type=MESH)
        pl.semaphore_wait(barrier, layers + others)

    @pl.when(side == core)
    def _():
        pl.semaphore_wait(barrier, layers - 1 + others)


def return_tile(tile, source, target, send_sem, recv_sems, start):
    _, _, core, layer, side = position()
    layers = target.shape[0]
    stays = (tile == 0) & (side == core)

    @pl.when(stays)
    def _():
        move = pltpu.make_async_copy(source, target.at[layer], recv_sems.at[tile])
        move.start() if start else move.wait()

    @pl.when(jnp.logical_not(stays))
    def _():
        move = pltpu.make_async_remote_copy(
            src_ref=source, dst_ref=target.at[layer], send_sem=send_sem, recv_sem=recv_sems.at[tile],
            device_id=owner_of(tile, layers), device_id_type=MESH,
        )
        move.start() if start else move.wait()


def ffn_kernel(
    chunk, shards, cot_count,
    scale, rows_ref, att_ref, *refs,
):
    cot_parts = refs[:cot_count]
    (
        w_out, b_out, gain, shift, w_up, b_up, w_down, b_down,
        out_ref, resid_ref, go_ref, vec_ref, vec_up_ref, keep_ref, send_ref,
        acc_up, acc_down, acc_out, stage, sems, active_all, inner_all, cot_rows, cot_sems, out_rows, send_sems, recv_sems, cell_sems,
    ) = refs[cot_count:]
    f32, bf16 = jnp.float32, jnp.bfloat16
    step, steps = pl.program_id(0), pl.num_programs(0)
    width, wide = w_up.shape

    slot = step % 2

    def fetch(number):
        for n, part in enumerate(cot_parts):
            @pl.when((number < steps) & (tile_order(number) == n))
            def _():
                pltpu.make_async_copy(part, cot_rows.at[number % 2], cot_sems.at[number % 2]).start()

    win, blk, core, _, _ = position()

    @pl.when(step == 0)
    def _():
        greet_owners(steps, [(win + 1 - 2 * core, blk)])

    @pl.when(step == 0)
    def _():
        fetch(step)

    fetch(step + 1)

    @pl.when(step == 0)
    def _():
        for ref in (acc_up, acc_down, acc_out, vec_ref, vec_up_ref):
            ref[...] = jnp.zeros_like(ref)

    att = att_ref[...]
    residual = rows_ref[...].astype(f32) + (jnp.dot(att, w_out[...], preferred_element_type=f32) + b_out[...])
    normal, rstd = norm_parts(residual)
    second = (normal * gain[...] + shift[...]).astype(bf16)
    pltpu.make_async_copy(cot_parts[0], cot_rows.at[slot], cot_sems.at[slot]).wait()
    upstream = cot_rows[slot].astype(f32) * scale[0]
    branch = upstream.astype(bf16)
    second_t = second.T
    branch_t = branch.T
    total = residual + b_down[...]
    grad_second = jnp.zeros_like(residual)
    def raise_part(first):
        part = slice(first, first + chunk)
        inner = jnp.dot(second, w_up[:, part], preferred_element_type=f32) + b_up[:, part]
        return inner, across(branch, w_down[part, :])

    ahead = raise_part(0)
    for first in range(0, wide, chunk):
        part = slice(first, first + chunk)
        inner, grad_active = ahead
        if first + chunk < wide:
            ahead = raise_part(first + chunk)
        cdf, slope = normal_parts(inner)
        active = (inner * cdf).astype(bf16)
        grad_inner_f = grad_active * (cdf + slope)
        grad_inner = grad_inner_f.astype(bf16)
        active_all[:, part] = active
        inner_all[:, part] = grad_inner
        acc_down[:, part] += jnp.dot(branch_t, active, preferred_element_type=f32)
        acc_up[:, part] += jnp.dot(second_t, grad_inner, preferred_element_type=f32)
        vec_up_ref[:, part] += column_sum(grad_inner_f)
    total = total + jnp.dot(active_all[...], w_down[...], preferred_element_type=f32)
    grad_second = across(inner_all[...], w_up[...])
    out_rows[step] = total.astype(bf16)
    return_tile(tile_order(step), out_rows.at[step], out_ref, send_sems.at[step], recv_sems, True)
    grad_resid = upstream + norm_back(grad_second, normal, rstd, gain[...])
    grad_proj = grad_resid.astype(bf16)
    resid_ref[...] = grad_proj
    go_ref[...] = across(grad_proj, w_out[...]).astype(bf16)
    acc_out[...] += jnp.dot(att.T, grad_proj, preferred_element_type=f32)
    vec_ref[0:1] += column_sum(grad_resid)
    vec_ref[1:2] += column_sum(grad_second * normal)
    vec_ref[2:3] += column_sum(grad_second)
    vec_ref[3:4] += column_sum(upstream)

    @pl.when(step == steps - 1)
    def _():
        part = width // shards
        down_part = wide // shards
        count = wide // width
        rows = stage.shape[1]
        size = rows // 4

        def act(b, slot, what):
            for piece in range(4):
                source = stage.at[slot, pl.ds(piece * size, size)]
                cell = (b, piece // 2)

                @pl.when(piece % 2 == core)
                def _():
                    move = pltpu.make_async_copy(source, keep_ref.at[cell], sems.at[slot, piece])
                    move.start() if what == "start" else move.wait()

                @pl.when(piece % 2 != core)
                def _():
                    move = pltpu.make_async_remote_copy(
                        src_ref=source, dst_ref=send_ref.at[cell], send_sem=sems.at[slot, piece], recv_sem=cell_sems.at[b, piece // 2],
                        device_id=(win + 1 - 2 * core, blk), device_id_type=MESH,
                    )
                    if what == "start":
                        move.start()
                    else:
                        move.wait_send()

        for b in range(shards):
            slot = b % 2
            if b >= 2:
                act(b - 2, slot, "wait")
            for k in range(count):
                stage[slot, k * part : (k + 1) * part] = acc_up[b * part : (b + 1) * part, k * width : (k + 1) * width].astype(bf16)
            base = count * part
            half = width // 2
            for k in range(2):
                stage[slot, base : base + half, k * half : (k + 1) * half] = acc_down[
                    k * half : (k + 1) * half, b * down_part : (b + 1) * down_part
                ].astype(bf16)
            base += half
            stage[slot, base : base + part] = acc_out[b * part : (b + 1) * part, :].astype(bf16)
            stage[slot, base + part :] = jnp.zeros((rows - base - part, width), bf16)
            act(b, slot, "start")
        for b in range(shards - 2, shards):
            act(b, b % 2, "wait")
        for b in range(shards):
            for x in range(2):
                pltpu.make_async_remote_copy(
                    src_ref=keep_ref.at[b, x], dst_ref=send_ref.at[b, x], send_sem=sems.at[0, 0], recv_sem=cell_sems.at[b, x],
                    device_id=(win + 1 - 2 * core, blk), device_id_type=MESH,
                ).wait_recv()
        for n in range(cot_count):
            return_tile(tile_order(n), out_rows.at[n], out_ref, send_sems.at[n], recv_sems, False)


def row_cuts(count, part, size):
    cuts = []
    for k in range(count):
        start = k * part
        while start < (k + 1) * part:
            end = min((k + 1) * part, (start // size + 1) * size)
            cuts.append((k, start - k * part, end - start, start // size, start % size))
            start = end
    return cuts


def add_into(target, got):
    target[...] = (target[...].astype(jnp.float32) + got[...].astype(jnp.float32)).astype(jnp.bfloat16)


def finish_kernel(groups, *refs):
    f32, bf16 = jnp.float32, jnp.bfloat16
    parts = refs[: 3 * groups]
    (
        rows_ref, resid_ref, gain, shift, weight, vec_two, vec_up, early_a, early_b, early_c, early_d,
        tok_ref, late_ref, early_ref,
        joined, turned, vec, out_rows, cells, core_got, late_bufs, early_bufs, send_sems, recv_sems, load_sems, chain_send, chain_recv, keep_sems,
    ) = refs[3 * groups :]
    step, steps = pl.program_id(0), pl.num_programs(0)
    length, width = rows_ref.shape
    lanes = width // groups
    part = width // 8
    win, blk, core, layer, side = position()
    pair = win // 2
    core_peer = (win + 1 - 2 * core, blk)
    pair_peer = (win + 2 - 4 * pair, blk)
    side_peer = (win, blk + 1 - 2 * side)
    layer_peers = [(win, ((layer + n) % 4) * 2 + side) for n in (1, 2, 3)]

    def remote(source, target, number, peer):
        return pltpu.make_async_remote_copy(
            src_ref=source, dst_ref=target, send_sem=chain_send.at[number], recv_sem=chain_recv.at[number],
            device_id=peer, device_id_type=MESH,
        )

    early_got, early_final = early_bufs

    def loads():
        return [
            pltpu.make_async_copy(source, early_got.at[n], load_sems.at[n])
            for n, source in enumerate((early_a, early_b, early_c, early_d))
        ]

    def second_step(state, got, base):
        return [
            remote(state.at[0, :, 1 - pair], got.at[0], base, pair_peer),
            remote(state.at[1, :, 1 - side], got.at[1], base + 1, side_peer),
        ]

    def add_second(state, got, mid):
        for z in range(2):
            mid[0, z] = (state[0, z, pair].astype(f32) + got[0, z].astype(f32)).astype(bf16)
            mid[1, z] = (state[1, z, side].astype(f32) + got[1, z].astype(f32)).astype(bf16)

    def layer_step(mid, got, base):
        moves = []
        for n in range(3):
            other = (layer + n + 1) % 4
            moves.append(remote(mid.at[other // 2, other % 2], got.at[n], base + n, layer_peers[n]))
        return moves

    def sum_into(final, parts):
        total = parts[0].astype(f32)
        for one in parts[1:]:
            total = total + one.astype(f32)
        final[...] = total.astype(bf16)

    def share(final, target, base):
        return [
            remote(final, target.at[win], base, core_peer),
            remote(final, target.at[win], base + 1, pair_peer),
        ]

    def pass_on(target, base):
        return [remote(target.at[win + 2 - 4 * pair], target.at[win + 2 - 4 * pair], base, core_peer)]

    def start(moves):
        for move in moves:
            move.start()

    def wait(moves):
        for move in moves:
            move.wait()

    late_first, late_second, late_mid, late_got, late_final = late_bufs
    early_base, late_base = 8, 0

    @pl.when(step == 0)
    def _():
        start(loads())
        greet_owners(steps, [core_peer, pair_peer, side_peer] + layer_peers)
        vec[...] = jnp.zeros_like(vec)

    tile = tile_order(step)
    rows = pl.ds(pl.multiple_of(tile * length, length), length)
    for g in range(groups):
        dq, own, other = parts[3 * g : 3 * g + 3]
        columns = slice(g * lanes, (g + 1) * lanes)
        joined[rows, columns] = dq[...]
        both = (own[...].astype(f32) + other[...].astype(f32)).astype(bf16)
        joined[rows, width + g * lanes : width + (g + 1) * lanes] = both[:, :lanes]
        joined[rows, 2 * width + g * lanes : 2 * width + (g + 1) * lanes] = both[:, lanes:]
        vec[0:1, columns] += column_sum(dq[...].astype(f32))
        vec[1:2, columns] += column_sum(both[:, lanes:].astype(f32))
    grad = across(joined[rows, :], weight[...])
    normal, rstd = norm_parts(rows_ref[...].astype(f32))
    turned[tile] = (normal * gain[...] + shift[...]).astype(bf16).T
    vec[2:3] += column_sum(grad * normal)
    vec[3:4] += column_sum(grad)
    out_rows[step] = (resid_ref[...].astype(f32) + norm_back(grad, normal, rstd, gain[...])).astype(bf16)
    return_tile(tile, out_rows.at[step], tok_ref, send_sems.at[step], recv_sems, True)

    @pl.when(step == 0)
    def _():
        wait(loads())
        sum_into(early_final, [early_got[n] for n in range(4)])
        start(share(early_final, early_ref, early_base))
        pltpu.make_async_copy(early_final, early_ref.at[win], keep_sems.at[0]).start()

    @pl.when(step == steps - 1)
    def _():
        size = cells.shape[5]
        cuts = row_cuts(3, part, size)
        for k in range(3):
            full = jnp.dot(turned[0], joined[0:length, k * width : (k + 1) * width], preferred_element_type=f32)
            for n in range(1, 4):
                full = full + jnp.dot(
                    turned[n], joined[n * length : (n + 1) * length, k * width : (k + 1) * width], preferred_element_type=f32
                )
            for b in range(8):
                for which, first, count, piece, row in cuts:
                    if which == k:
                        cells[piece % 2, b // 4, b // 2 % 2, b % 2, piece // 2, row : row + count] = full[
                            b * part + first : b * part + first + count
                        ].astype(bf16)
        tail = jnp.concatenate(
            [vec[...], vec_two[...]] + [vec_up[:, n * width : (n + 1) * width] for n in range(4)]
            + [jnp.zeros((4 * size - 3 * part - 12, width), f32)],
            axis=0,
        ).astype(bf16)
        for b in range(8):
            cells[1, b // 4, b // 2 % 2, b % 2, 1, 3 * part - 3 * size :] = tail
        exchange = [remote(cells.at[1 - core], core_got, late_base, core_peer)]
        start(exchange)
        wait(share(early_final, early_ref, early_base))
        start(pass_on(early_ref, early_base + 2))
        wait(exchange)
        mine = cells.at[core]
        for b in range(8):
            for x in range(2):
                add_into(mine.at[b // 4, b // 2 % 2, b % 2, x], core_got.at[b // 4, b // 2 % 2, b % 2, x])
        first = [
            remote(mine.at[0, :, 1 - side], late_first.at[0], late_base + 1, side_peer),
            remote(mine.at[1, :, :, 1 - pair], late_first.at[1], late_base + 2, pair_peer),
        ]
        start(first)
        wait(first)
        state = core_got.at[0]
        for z in range(2):
            for n in range(2):
                state[0, z, n] = (mine[0, z, side, n].astype(f32) + late_first[0, z, n].astype(f32)).astype(bf16)
                state[1, z, n] = (mine[1, z, n, pair].astype(f32) + late_first[1, z, n].astype(f32)).astype(bf16)
        start(second_step(state, late_second, late_base + 3))
        wait(second_step(state, late_second, late_base + 3))
        add_second(state, late_second, late_mid)
        across_layers = layer_step(late_mid, late_got, late_base + 5)
        start(across_layers)
        wait(across_layers)
        sum_into(late_final, [late_mid[layer // 2, layer % 2]] + [late_got[n] for n in range(3)])
        start(share(late_final, late_ref, early_base + 3))
        keep_late = pltpu.make_async_copy(late_final, late_ref.at[win], keep_sems.at[1])
        keep_late.start()
        wait(share(late_final, late_ref, early_base + 3))
        start(pass_on(late_ref, early_base + 5))
        wait(pass_on(early_ref, early_base + 2))
        wait(pass_on(late_ref, early_base + 5))
        pltpu.make_async_copy(early_final, early_ref.at[win], keep_sems.at[0]).wait()
        keep_late.wait()
        for n in range(4):
            return_tile(tile_order(n), out_rows.at[n], tok_ref, send_sems.at[n], recv_sems, False)


def first_send_kernel(place, keep_left, other_left, keep_right, other_right, left_ref, right_ref):
    for keep, other, target in ((keep_left, other_left, left_ref), (keep_right, other_right, right_ref)):
        target[...] = (keep[...].astype(jnp.float32) + other[...].astype(jnp.float32)).astype(jnp.bfloat16).reshape(target.shape)


def sum_low(target, refs):
    total = refs[0][...].astype(jnp.float32)
    for ref in refs[1:]:
        total = total + ref[...].astype(jnp.float32)
    target[...] = total.astype(jnp.bfloat16).reshape(target.shape)


def second_send_kernel(place, *refs):
    keep, left, right = refs[12:]
    for n, target in enumerate((keep.at[0], keep.at[1], left, right)):
        sum_low(target, refs[3 * n : 3 * n + 3])


def third_send_kernel(place, *refs):
    for n in range(4):
        keep, left, right = refs[3 * n : 3 * n + 3]
        in_left = (place[3] + n) % 4 < 2
        got = jnp.where(in_left, left[...].astype(jnp.float32), right[...].astype(jnp.float32))
        target = refs[12 + n]
        target[...] = (keep[...].reshape(target.shape).astype(jnp.float32) + got.reshape(target.shape)).astype(jnp.bfloat16)


def unpack_kernel(early, late, qkv_ref, out_ref, up_ref, down_ref):
    f32 = jnp.float32
    part, width = out_ref.shape
    count = up_ref.shape[1] // width
    half = width // 2

    def cells(source, first, rows):
        size = source.shape[1]
        parts = []
        while rows > 0:
            take = min(rows, size - first % size)
            parts.append(source[first // size, first % size : first % size + take])
            first, rows = first + take, rows - take
        return (parts[0] if len(parts) == 1 else jnp.concatenate(parts, axis=0)).astype(f32)

    for k in range(3):
        qkv_ref[:, k * width : (k + 1) * width] = cells(late, k * part, part)
    for k in range(count):
        up_ref[:, k * width : (k + 1) * width] = cells(early, k * part, part)
    turned = cells(early, count * part, half)
    down_ref[:, :half] = turned[:, :half].T
    down_ref[:, half:] = turned[:, half:].T
    out_ref[...] = cells(early, count * part + half, part)


def general_body(
    tokens,
    cotangent,
    w_qkv,
    b_q,
    b_v,
    w_out,
    b_out,
    gain_one,
    shift_one,
    gain_two,
    shift_two,
    w_up,
    b_up,
    w_down,
    b_down,
    rand_owner,
    rand_sub,
    global_ids,
    species,
):
    blk_count = lax.axis_size("blk")
    blk_pos = lax.axis_index("blk")
    win_pos = lax.axis_index("win")
    windows, length, model_width = tokens.shape
    blocks = rand_owner.shape[1]
    heads = rand_owner.shape[2]
    picks = rand_owner.shape[3]
    glob_count = global_ids.shape[1]
    own_blocks = blocks // blk_count
    block_len = length // own_blocks
    head_dim = model_width // heads
    pair_width = 2 * head_dim
    all_rows = windows * length
    key_count = 3 + glob_count + picks
    per_device = own_blocks * heads * picks
    slot_cap = max(2, 2 * per_device // blk_count)
    score_scale = head_dim ** (-0.5)
    f32 = jnp.float32
    bf16 = jnp.bfloat16
    tokens_f = tokens.reshape(all_rows, model_width).astype(f32)
    normed_f, norm_one_pull = jax.vjp(layer_norm, tokens_f, gain_one, shift_one)
    normed = normed_f.astype(bf16)
    joined = jnp.dot(normed, w_qkv, preferred_element_type=f32)
    query_vals = (joined[:, :model_width] + b_q).astype(bf16)
    key_vals = joined[:, model_width : 2 * model_width].astype(bf16)
    value_vals = (joined[:, 2 * model_width :] + b_v).astype(bf16)

    def to_heads(tensor):
        return tensor.reshape(windows, own_blocks, block_len, heads, head_dim).transpose(
            0, 1, 3, 2, 4
        )

    def from_heads(tensor):
        return tensor.transpose(0, 1, 3, 2, 4).reshape(all_rows, model_width)

    query_heads = to_heads(query_vals)
    local_pairs = jnp.concatenate([to_heads(key_vals), to_heads(value_vals)], axis=-1)
    rimmed = padded(local_pairs, (("blk", 1),), 1)
    block_ids = blk_pos * own_blocks + jnp.arange(own_blocks, dtype=jnp.int32)
    owned_glob = (global_ids[:, :, None] == block_ids[None, None, :]).astype(bf16)
    glob_terms = jnp.einsum("wgb,wbhsc->wghsc", owned_glob, local_pairs, preferred_element_type=f32)
    glob_pairs = lax.psum(glob_terms.astype(jnp.bfloat16), "blk").astype(jnp.float32).astype(bf16)
    owner_rows = rand_owner.reshape(windows, blk_count, per_device)
    sub_rows = rand_sub.reshape(windows, blk_count, per_device)
    owner_hits = (owner_rows[..., None] == jnp.arange(blk_count, dtype=jnp.int32)).astype(jnp.int32)
    slot_rows = jnp.sum(owner_hits * (jnp.cumsum(owner_hits, axis=2) - 1), axis=-1)
    my_owner = lax.dynamic_index_in_dim(owner_rows, blk_pos, 1, keepdims=False)
    my_slot = lax.dynamic_index_in_dim(slot_rows, blk_pos, 1, keepdims=False)
    fetch_index = my_owner * slot_cap + my_slot
    head_of_row = jnp.arange(per_device, dtype=jnp.int32) // picks % heads
    source_rows = sub_rows * heads + head_of_row[None, None, :]
    requester = jnp.arange(blk_count, dtype=jnp.int32)[None, :, None]
    target_rows = jnp.where(
        owner_rows == blk_pos, requester * slot_cap + slot_rows, blk_count * slot_cap
    )
    send_table = jnp.full((windows, blk_count * slot_cap + 1), own_blocks * heads, jnp.int32)
    send_table = jax.vmap(set_rows)(
        send_table, target_rows.reshape(windows, -1), source_rows.reshape(windows, -1)
    )[:, : blk_count * slot_cap]
    flat_pairs = jnp.concatenate(
        [
            local_pairs.reshape(windows, own_blocks * heads, block_len, pair_width),
            jnp.zeros((windows, 1, block_len, pair_width), bf16),
        ],
        axis=1,
    )
    outgoing = jax.vmap(take_rows)(flat_pairs, send_table).reshape(
        windows, blk_count, slot_cap, block_len, pair_width
    )
    incoming = lax.all_to_all(outgoing, "blk", split_axis=1, concat_axis=1, tiled=True).reshape(
        windows, blk_count * slot_cap, block_len, pair_width
    )
    rand_pairs = jax.vmap(take_rows)(incoming, fetch_index).reshape(
        windows, own_blocks, heads, picks, block_len, pair_width
    )
    near_pairs = jnp.stack(
        [rimmed[:, 0:own_blocks], rimmed[:, 1 : own_blocks + 1], rimmed[:, 2 : own_blocks + 2]],
        axis=3,
    )
    far_pairs = jnp.broadcast_to(
        glob_pairs.transpose(0, 2, 1, 3, 4)[:, None],
        (windows, own_blocks, heads, glob_count, block_len, pair_width),
    )
    gathered_keys = jnp.concatenate([near_pairs, far_pairs, rand_pairs], axis=3).reshape(
        windows, own_blocks, heads, key_count * block_len, pair_width
    )
    set_keys = gathered_keys[..., :head_dim]
    set_values = gathered_keys[..., head_dim:]
    block_flags = jnp.concatenate(
        [
            (block_ids > 0)[:, None],
            jnp.ones((own_blocks, 1), jnp.bool_),
            (block_ids < blocks - 1)[:, None],
            jnp.ones((own_blocks, glob_count + picks), jnp.bool_),
        ],
        axis=1,
    )
    key_valid = jnp.repeat(block_flags, block_len, axis=1)[None, :, None, None, :]

    def score_block():
        raw_scores = (
            jnp.einsum("wbhqe,wbhke->wbhqk", query_heads, set_keys, preferred_element_type=f32)
            * score_scale
        )
        return jnp.where(key_valid, raw_scores, masked_score)

    score_matrix = score_block()
    top_score = jnp.max(score_matrix, axis=-1, keepdims=True)
    log_total = top_score + jnp.log(
        jnp.sum(jnp.exp(score_matrix - top_score), axis=-1, keepdims=True)
    )
    probs_low = jnp.exp(score_matrix - log_total).astype(bf16)
    attended = jnp.einsum(
        "wbhqk,wbhke->wbhqe", probs_low, set_values, preferred_element_type=f32
    ).astype(bf16)
    merged = from_heads(attended)
    residual = tokens_f + (jnp.dot(merged, w_out, preferred_element_type=f32) + b_out)
    second_f, norm_two_pull = jax.vjp(layer_norm, residual, gain_two, shift_two)
    second = second_f.astype(bf16)
    inner_f = jnp.dot(second, w_up, preferred_element_type=f32) + b_up
    active_f, gelu_pull = jax.vjp(partial(jax.nn.gelu, approximate=False), inner_f)
    active = active_f.astype(bf16)
    output = residual + (jnp.dot(active, w_down, preferred_element_type=f32) + b_down)
    species_count = jnp.sum(
        (species[:, None] == jnp.arange(SPECIES, dtype=jnp.int32)[None, :]).astype(f32), axis=0
    )
    my_species = lax.dynamic_slice_in_dim(species, win_pos * windows, windows)
    own_count = jnp.sum(
        (my_species[:, None] == jnp.arange(SPECIES, dtype=jnp.int32)[None, :]).astype(f32)
        * species_count[None, :],
        axis=1,
    )
    window_scale = jnp.sqrt(species.shape[0] / (SPECIES * own_count))
    upstream = (cotangent.astype(f32) * window_scale[:, None, None]).reshape(all_rows, model_width)
    grad_branch = upstream.astype(bf16)
    grad_w_down = jnp.einsum("tf,td->fd", active, grad_branch, preferred_element_type=f32)
    grad_b_down = jnp.sum(grad_branch, axis=0, dtype=f32)
    grad_active = jnp.einsum("td,fd->tf", grad_branch, w_down, preferred_element_type=f32)
    grad_inner = gelu_pull(grad_active)[0].astype(bf16)
    grad_w_up = jnp.einsum("td,tf->df", second, grad_inner, preferred_element_type=f32)
    grad_b_up = jnp.sum(grad_inner, axis=0, dtype=f32)
    grad_second = jnp.einsum("tf,df->td", grad_inner, w_up, preferred_element_type=f32)
    grad_resid_norm, grad_gain_two, grad_shift_two = norm_two_pull(grad_second)
    grad_resid = upstream + grad_resid_norm
    grad_proj = grad_resid.astype(bf16)
    grad_w_out = jnp.einsum("ti,to->io", merged, grad_proj, preferred_element_type=f32)
    grad_b_out = jnp.sum(grad_proj, axis=0, dtype=f32)
    grad_attended = to_heads(
        jnp.einsum("to,io->ti", grad_proj, w_out, preferred_element_type=f32).astype(bf16)
    )
    probs_full = jnp.exp(score_block() - log_total)
    grad_probs = jnp.einsum(
        "wbhqe,wbhke->wbhqk", grad_attended, set_values, preferred_element_type=f32
    )
    grad_set_values = jnp.einsum(
        "wbhqk,wbhqe->wbhke", probs_full.astype(bf16), grad_attended, preferred_element_type=f32
    )
    row_dot = jnp.sum(probs_full * grad_probs, axis=-1, keepdims=True)
    grad_scores = (probs_full * (grad_probs - row_dot)).astype(bf16)
    grad_query = (
        jnp.einsum("wbhqk,wbhke->wbhqe", grad_scores, set_keys, preferred_element_type=f32)
        * score_scale
    )
    grad_set_keys = (
        jnp.einsum("wbhqk,wbhqe->wbhke", grad_scores, query_heads, preferred_element_type=f32)
        * score_scale
    )
    grad_set = jnp.concatenate([grad_set_keys, grad_set_values], axis=-1).reshape(
        windows, own_blocks, heads, key_count, block_len, pair_width
    )
    extended = (
        jnp.pad(grad_set[:, :, :, 1], ((0, 0), (1, 1), (0, 0), (0, 0), (0, 0)))
        + jnp.pad(grad_set[:, :, :, 0], ((0, 0), (0, 2), (0, 0), (0, 0), (0, 0)))
        + jnp.pad(grad_set[:, :, :, 2], ((0, 0), (2, 0), (0, 0), (0, 0), (0, 0)))
    )
    edge_grads = jnp.concatenate([extended[:, :1], extended[:, own_blocks + 1 :]], axis=1)
    edge_back = padded(edge_grads.astype(jnp.bfloat16), (("blk", 1),), 1).astype(edge_grads.dtype)
    pair_grad = extended[:, 1 : own_blocks + 1]
    pair_grad = pair_grad.at[:, 0].add(edge_back[:, 0]).at[:, own_blocks - 1].add(edge_back[:, 3])
    glob_grad = jnp.sum(grad_set[:, :, :, 3 : 3 + glob_count], axis=1).transpose(0, 2, 1, 3, 4)
    glob_total = lax.psum(glob_grad.astype(jnp.bfloat16), "blk").astype(jnp.float32)
    pair_grad = pair_grad + jnp.einsum(
        "wgb,wghsc->wbhsc", owned_glob.astype(f32), glob_total, precision=lax.Precision.HIGHEST
    )
    rand_grad = grad_set[:, :, :, 3 + glob_count :].reshape(
        windows, per_device, block_len, pair_width
    )
    back_out = jax.vmap(add_rows)(
        jnp.zeros((windows, blk_count * slot_cap, block_len, pair_width), f32),
        fetch_index,
        rand_grad,
    )
    back_in = lax.all_to_all(
        back_out.reshape(windows, blk_count, slot_cap, block_len, pair_width).astype(jnp.bfloat16),
        "blk",
        split_axis=1,
        concat_axis=1,
        tiled=True,
    ).astype(jnp.float32)
    owner_sum = jax.vmap(add_rows)(
        jnp.zeros((windows, own_blocks * heads + 1, block_len, pair_width), f32),
        send_table,
        back_in.reshape(windows, blk_count * slot_cap, block_len, pair_width),
    )
    pair_grad = pair_grad + owner_sum[:, : own_blocks * heads].reshape(
        windows, own_blocks, heads, block_len, pair_width
    )
    grad_keys = from_heads(pair_grad[..., :head_dim].astype(bf16))
    grad_values = from_heads(pair_grad[..., head_dim:].astype(bf16))
    grad_joined = jnp.concatenate(
        [from_heads(grad_query.astype(bf16)), grad_keys, grad_values], axis=1
    )
    grad_w_qkv = jnp.einsum("td,tc->dc", normed, grad_joined, preferred_element_type=f32)
    grad_b_q = jnp.sum(grad_joined[:, :model_width], axis=0, dtype=f32)
    grad_b_v = jnp.sum(grad_joined[:, 2 * model_width :], axis=0, dtype=f32)
    grad_normed = jnp.einsum("tc,dc->td", grad_joined, w_qkv, preferred_element_type=f32)
    grad_tok_norm, grad_gain_one, grad_shift_one = norm_one_pull(grad_normed)
    grad_tokens = (grad_resid + grad_tok_norm).astype(bf16).reshape(windows, length, model_width)
    local_grads = (
        grad_w_qkv,
        grad_b_q,
        grad_b_v,
        grad_w_out,
        grad_b_out,
        grad_gain_one,
        grad_shift_one,
        grad_gain_two,
        grad_shift_two,
        grad_w_up,
        grad_b_up,
        grad_w_down,
        grad_b_down,
    )
    packed_grads = jnp.concatenate(
        [grad_item.reshape(blk_count, -1) for grad_item in local_grads], axis=1
    )
    total_cols = packed_grads.shape[1]
    win_count = lax.axis_size("win")
    pad_cols = -total_cols % win_count
    shard_sum = lax.psum_scatter(
        packed_grads.astype(jnp.bfloat16), "blk", scatter_dimension=0, tiled=True
    ).astype(jnp.float32)
    split_shard = jnp.pad(shard_sum, ((0, 0), (0, pad_cols))).reshape(win_count, -1)
    group_piece = lax.psum_scatter(
        split_shard.astype(jnp.bfloat16), "win", scatter_dimension=0, tiled=True
    ).astype(jnp.float32)
    summed = (
        lax.all_gather(group_piece.astype(jnp.bfloat16), "win", axis=0, tiled=True)
        .astype(group_piece.dtype)
        .reshape(1, -1)[:, :total_cols]
    )
    shards = []
    offset = 0
    for grad_item in local_grads:
        entry_count = grad_item.size // blk_count
        shards.append(
            summed[0, offset : offset + entry_count].reshape(
                (grad_item.shape[0] // blk_count,) + grad_item.shape[1:]
            )
        )
        offset = offset + entry_count
    out_tokens = output.astype(bf16).reshape(windows, length, model_width)
    return (
        out_tokens,
        grad_tokens,
        shards[0],
        shards[1],
        shards[2],
        shards[3],
        shards[4],
        shards[5],
        shards[6],
        shards[7],
        shards[8],
        shards[9],
        shards[10],
        shards[11],
        shards[12],
    )


def layer_step(*arguments):
    windows = arguments[0].shape[0]
    paired = lax.axis_size("blk") == 2 * windows and lax.axis_size("win") == 4 and windows == 4
    return (paired_body if paired else general_body)(*arguments)


def paired_body(
    tokens,
    cotangent,
    w_qkv,
    b_q,
    b_v,
    w_out,
    b_out,
    gain_one,
    shift_one,
    gain_two,
    shift_two,
    w_up,
    b_up,
    w_down,
    b_down,
    rand_owner,
    rand_sub,
    global_ids,
    species,
):
    f32 = jnp.float32
    bf16 = jnp.bfloat16
    win_count = lax.axis_size("win")
    blk_count = lax.axis_size("blk")
    win_pos = lax.axis_index("win")
    blk_pos = lax.axis_index("blk")
    layers, length, width = tokens.shape
    core, layer, side = win_pos % 2, blk_pos // 2, blk_pos % 2
    blocks, heads, picks = rand_owner.shape[1:]
    own_blocks = blocks // blk_count
    half_blocks = blocks // 2
    block_len = length // own_blocks
    head_dim = width // heads
    all_rows = layers * length
    lanes = HEADS_PER_GROUP * head_dim
    groups = heads // HEADS_PER_GROUP
    score_scale = head_dim ** (-0.5)

    def regroup(value):
        parts = []
        for step in range(layers):
            part = lax.dynamic_index_in_dim(value, (layer + step) % layers, 0, keepdims=False)
            parts.append(lax.ppermute(part, ("win", "blk"), regroup_pairs(win_count, layers, step)))
        return parts

    def send_back(value):
        parts = []
        for step in range(layers):
            pairs = [(b, a) for a, b in regroup_pairs(win_count, layers, step)]
            parts.append(lax.ppermute(value[step * length : (step + 1) * length], ("win", "blk"), pairs))
        return parts

    def in_order(parts):
        result = jnp.zeros((layers, length, width), parts[0].dtype)
        for step, part in enumerate(parts):
            result = lax.dynamic_update_index_in_dim(result, part, (layer + step) % layers, 0)
        return result

    def takes(micros):
        return pl.CostEstimate(flops=micros * 1_000_000_000, bytes_accessed=micros * 1_000_000, transcendentals=0)

    rows_in = jnp.concatenate(regroup(tokens), axis=0)
    cot_in = regroup(cotangent)

    rand_size = blocks * heads * picks
    named = jnp.concatenate(
        [
            lax.dynamic_index_in_dim((rand_owner * own_blocks + rand_sub).reshape(layers, rand_size), layer, 0, keepdims=False),
            lax.dynamic_index_in_dim(global_ids, layer, 0, keepdims=False),
        ]
    )
    named = jnp.where(side == core, named, swap(named, 1, 0))

    def place_of(block):
        owner = block // own_blocks
        half = jnp.where(owner % 2 == core, 0, half_blocks)
        return half + ((layer - owner // 2) % layers) * own_blocks + block % own_blocks

    slot = jnp.arange(half_blocks, dtype=jnp.int32)
    slot_block = (((layer - slot // own_blocks) % layers) * 2 + core) * own_blocks + slot % own_blocks
    table = jnp.concatenate(
        [
            place_of(named),
            slot_block,
            place_of(jnp.maximum(slot_block - 1, 0)),
            place_of(jnp.minimum(slot_block + 1, blocks - 1)),
        ]
    )
    sizes = (heads, picks, rand_size, half_blocks)

    tile = length

    def by_rows(columns):
        return pl.BlockSpec((tile, columns), lambda i: (i, 0))

    def by_tile(columns):
        return pl.BlockSpec((tile, columns), lambda i: (tile_order(i), 0))

    def whole(*shape, once=True):
        mode = pl.Buffered(1) if once else None
        return pl.BlockSpec(shape, lambda i: (0,) * len(shape), pipeline_mode=mode)

    scalars = pl.BlockSpec(memory_space=pltpu.SMEM)
    wide = w_up.shape[1]
    params = pltpu.CompilerParams(vmem_limit_bytes=60 << 20)
    row = lambda vector: vector.reshape(1, -1)
    query, key_value = pl.pallas_call(
        partial(qkv_kernel, score_scale),
        grid=(all_rows // tile,),
        in_specs=[by_rows(width), whole(1, width), whole(1, width), whole(width, 3 * width), whole(2, width)],
        out_specs=[by_rows(width), by_rows(2 * width)],
        out_shape=[jax.ShapeDtypeStruct((all_rows, width), bf16), jax.ShapeDtypeStruct((all_rows, 2 * width), bf16)],
        compiler_params=params,
        cost_estimate=takes(12),
        name="qkv",
    )(rows_in, row(gain_one), row(shift_one), w_qkv, jnp.stack([b_q, b_v]))
    key_value_other = swap(key_value, 1, 0)

    def lane_block(first):
        return pl.BlockSpec((all_rows, lanes), lambda g, t: (0, first + g))

    store = pltpu.VMEM((blocks, block_len, lanes), bf16)
    attended, log_total = pl.pallas_call(
        partial(attend_kernel, sizes, blocks, head_dim),
        grid_spec=pltpu.PrefetchScalarGridSpec(
            num_scalar_prefetch=1,
            grid=(groups,),
            in_specs=[lane_block(0), lane_block(0), lane_block(0), lane_block(groups), lane_block(groups)],
            out_specs=[lane_block(0), pl.BlockSpec((1, half_blocks, lanes), lambda g, t: (g, 0, 0))],
            scratch_shapes=[store, store],
        ),
        out_shape=[
            jax.ShapeDtypeStruct((all_rows, width), bf16),
            jax.ShapeDtypeStruct((groups, half_blocks, lanes), f32),
        ],
        compiler_params=pltpu.CompilerParams(vmem_limit_bytes=56 << 20),
        cost_estimate=takes(37),
        name="attend",
    )(table, query, key_value, key_value_other, key_value, key_value_other)

    species_count = jnp.sum(
        (species[:, None] == jnp.arange(SPECIES, dtype=jnp.int32)[None, :]).astype(f32), axis=0
    )
    my_window = ((win_pos // 2) * 2 + side) * layers + layer
    my_species = lax.dynamic_index_in_dim(species, my_window, 0, keepdims=False)
    own_count = jnp.sum(
        (my_species == jnp.arange(SPECIES, dtype=jnp.int32)).astype(f32) * species_count
    )
    window_scale = jnp.sqrt(species.shape[0] / (SPECIES * own_count))
    payload = 2 * wide // blk_count + width // blk_count
    payload += -payload % (16 * win_count)
    stays = jax.ShapeDtypeStruct((blk_count, win_count // 2, payload // win_count, width), bf16)
    any_place = pl.BlockSpec(memory_space=pl.ANY)
    out_tokens, grad_resid, grad_attended, vec_two, vec_up, early_keep, early_other = pl.pallas_call(
        partial(ffn_kernel, 256, blk_count, layers),
        grid=(layers,),
        in_specs=[
            scalars, by_tile(width), by_tile(width), *[any_place] * layers, whole(width, width), whole(1, width), whole(1, width),
            whole(1, width), whole(width, wide), whole(1, wide), whole(wide, width), whole(1, width),
        ],
        out_specs=[any_place, by_tile(width), by_tile(width), whole(4, width), whole(1, wide), any_place, any_place],
        out_shape=[
            jax.ShapeDtypeStruct((layers, length, width), bf16),
            jax.ShapeDtypeStruct((all_rows, width), bf16),
            jax.ShapeDtypeStruct((all_rows, width), bf16),
            jax.ShapeDtypeStruct((4, width), f32),
            jax.ShapeDtypeStruct((1, wide), f32),
            stays,
            stays,
        ],
        scratch_shapes=[
            pltpu.VMEM((width, wide), f32),
            pltpu.VMEM((width, wide), f32),
            pltpu.VMEM((width, width), f32),
            pltpu.VMEM((2, payload, width), bf16),
            pltpu.SemaphoreType.DMA((2, 4)),
            pltpu.VMEM((length, wide), bf16),
            pltpu.VMEM((length, wide), bf16),
            pltpu.VMEM((2, length, width), bf16),
            pltpu.SemaphoreType.DMA((2,)),
            pltpu.VMEM((layers, length, width), bf16),
            pltpu.SemaphoreType.DMA((layers,)),
            pltpu.SemaphoreType.DMA((layers,)),
            pltpu.SemaphoreType.DMA((blk_count, 2)),
        ],
        compiler_params=pltpu.CompilerParams(vmem_limit_bytes=60 << 20, collective_id=1, has_side_effects=True),
        cost_estimate=takes(90),
        name="ffn",
    )(
        window_scale.reshape(1), rows_in, attended, *cot_in, w_out, row(b_out), row(gain_two), row(shift_two),
        w_up, row(b_up), w_down, row(b_down),
    )

    pair = win_pos // 2
    early_rows = payload // win_count
    late_rows = 3 * width // blk_count + 32
    late_size = late_rows // win_count
    cell = (early_rows, width)
    early_keep = early_keep.reshape((2, 2, 2, 2) + cell)
    early_other = early_other.reshape((2, 2, 2, 2) + cell)
    place = jnp.stack([side, pair, side, layer])

    def picked(index):
        return pl.BlockSpec((1, 1, 1, 1) + cell, lambda z, n, p: index(z, n, p) + (0, 0))

    def listed(index):
        return pl.BlockSpec((1, 1) + cell, lambda z, n, p: index(z, n, p) + (0, 0))

    def cells_of(count):
        return [jax.ShapeDtypeStruct((2, 2) + cell, bf16)] * count

    def first_send():
        left = picked(lambda z, n, p: (0, z, 1 - p[0], n))
        right = picked(lambda z, n, p: (1, z, n, 1 - p[1]))
        return pl.pallas_call(
            first_send_kernel,
            grid_spec=pltpu.PrefetchScalarGridSpec(
                num_scalar_prefetch=1, grid=(2, 2), in_specs=[left, left, right, right], out_specs=[listed(lambda z, n, p: (z, n))] * 2
            ),
            out_shape=cells_of(2),
            cost_estimate=takes(3),
            name="first_send",
        )(place, early_keep, early_other, early_keep, early_other)

    def second_send(got_left, got_right):
        specs, operands = [], []
        for far in (0, 1):
            bit = lambda n, p, f=far: p[n] if f == 0 else 1 - p[n]
            left = picked(lambda z, n, p, bit=bit: (0, z, p[0], bit(1, p)))
            right = picked(lambda z, n, p, bit=bit: (1, z, bit(0, p), p[1]))
            specs += [left, left, listed(lambda z, n, p, bit=bit: (z, bit(1, p)))]
            operands += [early_keep, early_other, got_left]
            specs += [right, right, listed(lambda z, n, p, bit=bit: (z, bit(0, p)))]
            operands += [early_keep, early_other, got_right]
        rows_spec = pl.BlockSpec((1,) + cell, lambda z, n, p: (z, 0, 0))
        both_spec = pl.BlockSpec((2, 1) + cell, lambda z, n, p: (0, z, 0, 0))
        return pl.pallas_call(
            second_send_kernel,
            grid_spec=pltpu.PrefetchScalarGridSpec(num_scalar_prefetch=1, grid=(2, 1), in_specs=specs, out_specs=[both_spec, rows_spec, rows_spec]),
            out_shape=cells_of(1) + [jax.ShapeDtypeStruct((2,) + cell, bf16)] * 2,
            cost_estimate=takes(4),
            name="second_send",
        )(place, *operands)

    def third_send(keep, left, right):
        specs = []
        for step in range(layers):
            goal = lambda p, step=step: (p[3] + step) % layers
            specs.append(listed(lambda z, n, p, goal=goal: (goal(p) // 2, goal(p) % 2)))
            specs += [pl.BlockSpec((1,) + cell, lambda z, n, p, goal=goal: (goal(p) % 2, 0, 0))] * 2
        out = pl.BlockSpec(cell, lambda z, n, p: (0, 0))
        return pl.pallas_call(
            third_send_kernel,
            grid_spec=pltpu.PrefetchScalarGridSpec(num_scalar_prefetch=1, grid=(1, 1), in_specs=specs, out_specs=[out] * layers),
            out_shape=[jax.ShapeDtypeStruct(cell, bf16)] * layers,
            cost_estimate=takes(3),
            name="third_send",
        )(place, *[keep, left, right] * layers)

    def to_layer(value, step):
        pairs = [
            (win * blk_count + blk, win * blk_count + (blk + 2 * step) % blk_count)
            for win in range(win_count)
            for blk in range(blk_count)
        ]
        return lax.ppermute(value, ("win", "blk"), pairs)

    first_left, first_right = first_send()
    first_left, first_right = swap(first_left, 0, 1), swap(first_right, 2, 0)

    grad_parts = []
    for group in range(groups):
        after = []
        if group == 1:
            early_kept, send_left, send_right = second_send(first_left, first_right)
            after = [early_kept]
            second = swap(send_left, 2, 0), swap(send_right, 0, 1)
        if group == 2:
            early_parts = third_send(early_kept, *second)
            after = [early_parts[0]]
            early_parts = [early_parts[0]] + [to_layer(early_parts[n], n) for n in range(1, layers)]

        def column(first):
            return pl.BlockSpec((all_rows, lanes), lambda g, t: (0, first))

        def full(columns):
            return pl.BlockSpec((all_rows, columns), lambda g, t: (0, 0))

        grad_store = pltpu.VMEM((blocks, block_len, lanes), f32)
        glob_store = pltpu.VMEM((2, block_len, lanes), f32)
        dq, own, other = pl.pallas_call(
            partial(attend_back_kernel, sizes, blocks, head_dim, score_scale, group),
            grid_spec=pltpu.PrefetchScalarGridSpec(
                num_scalar_prefetch=1,
                grid=(1,),
                in_specs=[
                    column(group), column(group), column(group), column(groups + group), column(groups + group), column(group),
                    pl.BlockSpec((1, half_blocks, lanes), lambda g, t: (group, 0, 0)),
                    *[any_place] * len(after),
                ],
                out_specs=[full(lanes), full(2 * lanes), full(2 * lanes)],
                scratch_shapes=[store, store, grad_store, grad_store, glob_store, glob_store],
            ),
            out_shape=[jax.ShapeDtypeStruct((all_rows, n * lanes), bf16) for n in (1, 2, 2)],
            compiler_params=params,
            cost_estimate=takes(25),
            name="attend_back",
        )(table, query, key_value, key_value_other, key_value, key_value_other, grad_attended, log_total, *after)
        grad_parts += [dq, own, swap(other, 1, 0)]

    def vmem(*shape):
        return pltpu.VMEM(shape, bf16)

    first_shape, mid_shape = (2, 2, 2), (2, 2)
    chain = lambda size: [vmem(*lead, size, width) for lead in (first_shape, mid_shape, mid_shape, (3,), ())]
    grad_tokens, late, early = pl.pallas_call(
        partial(finish_kernel, groups),
        grid=(layers,),
        in_specs=[by_tile(p.shape[1]) for p in grad_parts]
        + [by_tile(width), by_tile(width), whole(1, width), whole(1, width), whole(width, 3 * width), whole(4, width), whole(1, wide)]
        + [any_place] * layers,
        out_specs=[any_place] * 3,
        out_shape=[
            jax.ShapeDtypeStruct((layers, length, width), bf16),
            jax.ShapeDtypeStruct((win_count, late_size, width), bf16),
            jax.ShapeDtypeStruct((win_count, early_rows, width), bf16),
        ],
        scratch_shapes=[
            vmem(all_rows, 3 * width),
            vmem(layers, width, length),
            pltpu.VMEM((4, width), f32),
            vmem(layers, length, width),
            vmem(2, 2, 2, 2, 2, late_size, width),
            vmem(2, 2, 2, 2, late_size, width),
            chain(late_size),
            [vmem(*lead, early_rows, width) for lead in ((4,), ())],
            pltpu.SemaphoreType.DMA((layers,)),
            pltpu.SemaphoreType.DMA((layers,)),
            pltpu.SemaphoreType.DMA((4,)),
            pltpu.SemaphoreType.DMA((14,)),
            pltpu.SemaphoreType.DMA((14,)),
            pltpu.SemaphoreType.DMA((2,)),
        ],
        compiler_params=pltpu.CompilerParams(vmem_limit_bytes=62 << 20, collective_id=2, has_side_effects=True),
        cost_estimate=takes(90),
        name="finish",
    )(
        *grad_parts, rows_in, grad_resid, row(gain_one), row(shift_one), w_qkv, vec_two, vec_up,
        *early_parts,
    )
    part = width // blk_count
    count = wide // width
    done_qkv, done_out, done_up, done_down = pl.pallas_call(
        unpack_kernel,
        out_shape=[
            jax.ShapeDtypeStruct(shape, f32)
            for shape in ((part, 3 * width), (part, width), (part, wide), (wide // blk_count, width))
        ],
        compiler_params=params,
        cost_estimate=takes(4),
        name="unpack",
    )(early, late)
    late = late.reshape(-1, width)[3 * part :].astype(f32)
    vec = lax.dynamic_slice_in_dim(late[:8], blk_pos * part, part, axis=1)
    vec_wide = lax.dynamic_slice_in_dim(late[8 : 8 + count].reshape(-1), blk_pos * (wide // blk_count), wide // blk_count)
    return (
        out_tokens,
        grad_tokens,
        done_qkv,
        vec[0],
        vec[1],
        done_out,
        vec[4],
        vec[2],
        vec[3],
        vec[5],
        vec[6],
        done_up,
        vec_wide,
        done_down,
        vec[7],
    )


def solution(mesh):
    placed = (
        P("win", "blk", None),
        P("win", "blk", None),
        P(),
        P(),
        P(),
        P(),
        P(),
        P(),
        P(),
        P(),
        P(),
        P(),
        P(),
        P(),
        P(),
        P("win", None, None, None),
        P("win", None, None, None),
        P("win", None),
        P(),
    )
    return jax.shard_map(
        layer_step,
        mesh=mesh,
        in_specs=placed,
        out_specs=(
            P("win", "blk", None),
            P("win", "blk", None),
            P("blk", None),
            P("blk"),
            P("blk"),
            P("blk", None),
            P("blk"),
            P("blk"),
            P("blk"),
            P("blk"),
            P("blk"),
            P("blk", None),
            P("blk"),
            P("blk", None),
            P("blk"),
        ),
        check_vma=False,
    )
```

```python
from functools import partial

import jax
import jax.numpy as jnp
from jax import lax
from jax.experimental import pallas as pl
from jax.experimental.pallas import tpu as pltpu
from jax.sharding import PartitionSpec as P

SPECIES = 4


epsilon = 1e-05
masked_score = -1000000000.0


def padded(cells, sides, width):
    for axis, dim in sides:
        count = lax.axis_size(axis)
        ends = count - 1
        head = lax.slice_in_dim(cells, 0, width, axis=dim)
        tail = lax.slice_in_dim(cells, cells.shape[dim] - width, cells.shape[dim], axis=dim)
        cells = jnp.concatenate(
            [
                lax.ppermute(tail, axis, [(i, (i + 1) % count) for i in range(ends)]),
                cells,
                lax.ppermute(head, axis, [((i + 1) % count, i) for i in range(ends)]),
            ],
            axis=dim,
        )
    return cells


def layer_norm(values, norm_gain, norm_shift):
    average = jnp.mean(values, axis=-1, keepdims=True)
    centred = values - average
    variance = jnp.mean(centred * centred, axis=-1, keepdims=True)
    return centred * lax.rsqrt(variance + epsilon) * norm_gain + norm_shift


def take_rows(source, index_rows):
    return jnp.take(source, index_rows, axis=0)


def add_rows(base, index_rows, update):
    return base.at[index_rows].add(update)


def set_rows(base, index_rows, update):
    return base.at[index_rows].set(update)


HEADS_PER_GROUP = 4


def regroup_pairs(win_count, layers, step):
    pairs = []
    for win in range(win_count):
        for blk in range(2 * layers):
            layer, side = blk // 2, blk % 2
            target = ((layer + step) % layers) * 2 + win % 2
            pairs.append((win * 2 * layers + blk, ((win // 2) * 2 + side) * 2 * layers + target))
    return pairs


def flip_pairs(win_count, blk_count, win_bit, blk_bit):
    return [
        (win * blk_count + blk, (win ^ win_bit) * blk_count + (blk ^ blk_bit))
        for win in range(win_count)
        for blk in range(blk_count)
    ]


def swap(value, win_bit, blk_bit):
    pairs = flip_pairs(lax.axis_size("win"), lax.axis_size("blk"), win_bit, blk_bit)
    return lax.ppermute(value, ("win", "blk"), pairs)


def head_masks(lanes, head_dim, dtype):
    lane = lax.broadcasted_iota(jnp.int32, (1, lanes), 1)
    return [(lane // head_dim == h).astype(dtype) for h in range(lanes // head_dim)]


def block_places(table, slot, group, sizes):
    heads, picks, rand_size, half_blocks = sizes
    block = table[rand_size + 2 + slot]
    near = [table[rand_size + 2 + half_blocks + slot], slot, table[rand_size + 2 + 2 * half_blocks + slot]]
    row = (block * heads + group * HEADS_PER_GROUP) * picks
    rand = [[table[row + h * picks + r] for h in range(HEADS_PER_GROUP)] for r in range(picks)]
    return block, near, rand


def spread_heads(rows, masks):
    return jnp.concatenate([rows * m for m in masks], axis=0)


def pick_heads(square, masks, height):
    total = square[0:height] * masks[0]
    for h in range(1, len(masks)):
        total = total + square[h * height : (h + 1) * height] * masks[h]
    return total


def key_rows(source, near, glob, rand, low_half):
    parts = [source[p] for p in near] + [source[p] for p in glob]
    for places in rand:
        columns = []
        for c in range(len(places) // 2):
            low = source[places[2 * c], :, c * 128 : (c + 1) * 128]
            high = source[places[2 * c + 1], :, c * 128 : (c + 1) * 128]
            columns.append(jnp.where(low_half, low, high))
        parts.append(jnp.concatenate(columns, axis=1))
    return jnp.concatenate(parts, axis=0)


def mask_scores(scores, block, blocks, block_len):
    first = jnp.where(block > 0, scores[:block_len], masked_score)
    last = jnp.where(block < blocks - 1, scores[2 * block_len : 3 * block_len], masked_score)
    return jnp.concatenate([first, scores[block_len : 2 * block_len], last, scores[3 * block_len :]], axis=0)


def across(left, right):
    return lax.dot_general(left, right, (((1,), (1,)), ((), ())), preferred_element_type=jnp.float32)


def down(left, right):
    return lax.dot_general(left, right, (((0,), (0,)), ((), ())), preferred_element_type=jnp.float32)


def load_halves(target, own, other, half_blocks, block_len):
    lanes = own.shape[-1]
    target[0:half_blocks] = own[...].reshape(half_blocks, block_len, lanes)
    target[half_blocks:] = other[...].reshape(half_blocks, block_len, lanes)


def attend_kernel(sizes, blocks, head_dim, table, q_ref, k_own, k_other, v_own, v_other, o_ref, lse_ref, k_all, v_all):
    heads, picks, rand_size, half_blocks = sizes
    block_len = k_all.shape[1]
    lanes = q_ref.shape[1]
    group = pl.program_id(0)
    load_halves(k_all, k_own, k_other, half_blocks, block_len)
    load_halves(v_all, v_own, v_other, half_blocks, block_len)
    low_half = lax.broadcasted_iota(jnp.int32, (block_len, 128), 1) < head_dim
    masks = head_masks(lanes, head_dim, jnp.bfloat16)
    masks_f = head_masks(lanes, head_dim, jnp.float32)
    glob = [table[rand_size], table[rand_size + 1]]

    def one(slot, carry):
        block, near, rand = block_places(table, slot, group, sizes)
        rows = pl.ds(pl.multiple_of(slot * block_len, block_len), block_len)
        queries = spread_heads(q_ref[rows, :], masks)
        keys = key_rows(k_all, near, glob, rand, low_half)
        scores = mask_scores(across(keys, queries), block, blocks, block_len)
        top = jnp.max(scores, axis=0, keepdims=True)
        weights = jnp.exp(scores - top)
        total = jnp.sum(weights, axis=0, keepdims=True)
        probs = (weights * (1.0 / total)).astype(jnp.bfloat16)
        values = key_rows(v_all, near, glob, rand, low_half)
        o_ref[rows, :] = pick_heads(down(probs, values), masks_f, block_len).astype(jnp.bfloat16)
        lse_ref[0, pl.ds(slot, 1), :] = top + jnp.log(total)
        return carry

    lax.fori_loop(0, half_blocks, one, 0, unroll=min(8, half_blocks))


def attend_back_kernel(
    sizes, blocks, head_dim, scale, group,
    table, q_ref, k_own, k_other, v_own, v_other, go_ref, lse_ref, *refs,
):
    dq_ref, own_ref, other_ref, k_all, v_all, dk_all, dv_all, dk_glob, dv_glob = refs[-9:]
    heads, picks, rand_size, half_blocks = sizes
    block_len = k_all.shape[1]
    lanes = q_ref.shape[1]
    f32 = jnp.float32
    load_halves(k_all, k_own, k_other, half_blocks, block_len)
    load_halves(v_all, v_own, v_other, half_blocks, block_len)
    dk_all[...] = jnp.zeros_like(dk_all)
    dv_all[...] = jnp.zeros_like(dv_all)
    dk_glob[...] = jnp.zeros_like(dk_glob)
    dv_glob[...] = jnp.zeros_like(dv_glob)
    low_half = lax.broadcasted_iota(jnp.int32, (block_len, 128), 1) < head_dim
    masks = head_masks(lanes, head_dim, jnp.bfloat16)
    masks_f = head_masks(lanes, head_dim, f32)
    glob = [table[rand_size], table[rand_size + 1]]

    def add_back(grads, near, rand, into, into_glob):
        for n in range(3):
            into[near[n]] += grads[n * block_len : (n + 1) * block_len]
        for n in range(2):
            into_glob[n] += grads[(3 + n) * block_len : (4 + n) * block_len]
        for r in range(picks):
            part = grads[(5 + r) * block_len : (6 + r) * block_len]
            for c in range(lanes // 128):
                cell = part[:, c * 128 : (c + 1) * 128]
                columns = pl.ds(c * 128, 128)
                into[rand[r][2 * c], :, columns] += jnp.where(low_half, cell, 0.0)
                into[rand[r][2 * c + 1], :, columns] += jnp.where(low_half, 0.0, cell)

    def one(slot, carry):
        block, near, rand = block_places(table, slot, group, sizes)
        rows = pl.ds(pl.multiple_of(slot * block_len, block_len), block_len)
        queries = spread_heads(q_ref[rows, :], masks)
        grads_out = spread_heads(go_ref[rows, :], masks)
        keys = key_rows(k_all, near, glob, rand, low_half)
        values = key_rows(v_all, near, glob, rand, low_half)
        scores = mask_scores(across(keys, queries), block, blocks, block_len)
        probs = jnp.exp(scores - lse_ref[0, pl.ds(slot, 1), :])
        grad_probs = across(values, grads_out)
        row_dot = jnp.sum(probs * grad_probs, axis=0, keepdims=True)
        grad_scores = (probs * (grad_probs - row_dot)).astype(jnp.bfloat16)
        add_back(jnp.dot(probs.astype(jnp.bfloat16), grads_out, preferred_element_type=f32), near, rand, dv_all, dv_glob)
        add_back(jnp.dot(grad_scores, queries, preferred_element_type=f32), near, rand, dk_all, dk_glob)
        dq_ref[rows, :] = (pick_heads(down(grad_scores, keys), masks_f, block_len) * scale).astype(jnp.bfloat16)
        return carry

    lax.fori_loop(0, half_blocks, one, 0, unroll=min(8, half_blocks))
    for n in range(2):
        dk_all[glob[n]] += dk_glob[n]
        dv_all[glob[n]] += dv_glob[n]
    for target, start in ((own_ref, 0), (other_ref, half_blocks)):
        for n, source in enumerate((dk_all, dv_all)):
            cells = source[start : start + half_blocks].astype(jnp.bfloat16)
            target[:, n * lanes : (n + 1) * lanes] = cells.reshape(half_blocks * block_len, lanes)


def norm_parts(values):
    average = jnp.mean(values, axis=-1, keepdims=True)
    centred = values - average
    rstd = lax.rsqrt(jnp.mean(centred * centred, axis=-1, keepdims=True) + epsilon)
    return centred * rstd, rstd


def norm_back(grad, normal, rstd, gain):
    scaled = grad * gain
    first = jnp.mean(scaled, axis=-1, keepdims=True)
    second = jnp.mean(scaled * normal, axis=-1, keepdims=True)
    return rstd * (scaled - first - normal * second)


def normal_parts(values):
    cdf = 0.5 + 0.5 * lax.erf(values * 0.5**0.5)
    return cdf, values * jnp.exp(-0.5 * values * values) * 0.3989422804014327


def column_sum(values):
    return jnp.sum(values, axis=0, keepdims=True)


def qkv_kernel(scale, rows_ref, gain, shift, weight, bias, q_ref, kv_ref):
    width = rows_ref.shape[1]
    normal, _ = norm_parts(rows_ref[...].astype(jnp.float32))
    normed = (normal * gain[...] + shift[...]).astype(jnp.bfloat16)

    def part(n):
        columns = slice(n * width, (n + 1) * width)
        return jnp.dot(normed, weight[:, columns], preferred_element_type=jnp.float32)

    q_ref[...] = (part(0) + bias[0:1]).astype(jnp.bfloat16) * jnp.asarray(scale, jnp.bfloat16)
    kv_ref[:, :width] = part(1).astype(jnp.bfloat16)
    kv_ref[:, width:] = (part(2) + bias[1:2]).astype(jnp.bfloat16)


MESH = pl.DeviceIdType.MESH


def tile_order(number):
    return jnp.where(number == 0, 2, jnp.where(number == 2, 3, jnp.where(number == 3, 0, number)))


def position():
    win, blk = lax.axis_index("win"), lax.axis_index("blk")
    return win, blk, win % 2, blk // 2, blk % 2


def owner_of(tile, layers):
    win, blk, core, layer, side = position()
    return (win // 2) * 2 + side, ((layer + layers - tile) % layers) * 2 + core


def greet_owners(layers, peers):
    barrier = pltpu.get_barrier_semaphore()
    others = len(peers)
    for peer in peers:
        pl.semaphore_signal(barrier, inc=1, device_id=peer, device_id_type=MESH)
    _, _, core, _, side = position()
    for tile in range(1, layers):
        pl.semaphore_signal(barrier, inc=1, device_id=owner_of(tile, layers), device_id_type=MESH)

    @pl.when(side != core)
    def _():
        pl.semaphore_signal(barrier, inc=1, device_id=owner_of(0, layers), device_id_type=MESH)
        pl.semaphore_wait(barrier, layers + others)

    @pl.when(side == core)
    def _():
        pl.semaphore_wait(barrier, layers - 1 + others)


def return_tile(tile, source, target, send_sem, recv_sems, start):
    _, _, core, layer, side = position()
    layers = target.shape[0]
    stays = (tile == 0) & (side == core)

    @pl.when(stays)
    def _():
        move = pltpu.make_async_copy(source, target.at[layer], recv_sems.at[tile])
        move.start() if start else move.wait()

    @pl.when(jnp.logical_not(stays))
    def _():
        move = pltpu.make_async_remote_copy(
            src_ref=source, dst_ref=target.at[layer], send_sem=send_sem, recv_sem=recv_sems.at[tile],
            device_id=owner_of(tile, layers), device_id_type=MESH,
        )
        move.start() if start else move.wait()


def ffn_forward_kernel(
    chunk,
    rows_ref, att_ref, w_out, b_out, gain, shift, w_up, b_up, w_down, b_down,
    out_ref, normal_ref, second_ref, att_turned_ref, rstd_ref, active_ref, slope_ref,
):
    f32, bf16 = jnp.float32, jnp.bfloat16
    wide = w_up.shape[1]
    att = att_ref[...]
    residual = rows_ref[...].astype(f32) + (jnp.dot(att, w_out[...], preferred_element_type=f32) + b_out[...])
    normal, rstd = norm_parts(residual)
    second = (normal * gain[...] + shift[...]).astype(bf16)
    normal_ref[...] = normal.astype(bf16)
    second_ref[...] = second.T
    att_turned_ref[...] = att.T
    rstd_ref[...] = jnp.broadcast_to(rstd, rstd_ref.shape)

    def raise_part(first):
        part = slice(first, first + chunk)
        return jnp.dot(second, w_up[:, part], preferred_element_type=f32) + b_up[:, part]

    ahead = raise_part(0)
    for first in range(0, wide, chunk):
        inner = ahead
        if first + chunk < wide:
            ahead = raise_part(first + chunk)
        cdf, slope = normal_parts(inner)
        active_ref[:, first : first + chunk] = (inner * cdf).astype(bf16)
        slope_ref[:, first : first + chunk] = (cdf + slope).astype(bf16)
    total = residual + b_down[...] + jnp.dot(active_ref[...], w_down[...], preferred_element_type=f32)
    out_ref[...] = total.astype(bf16)


def ffn_back_kernel(
    chunks, shards, kept_tiles,
    scale, active_ref, slope_ref, w_up, w_down, second_t, normal_ref, rstd_ref, att_t, w_out, gain,
    cot_a, cot_b, cot_c, cot_d, output,
    resid_ref, go_ref, vec_ref, vec_up_ref, keep_ref, other_ref, out_ref,
    cot_rows, branch, branch_t, grad_inner, grad_second, stage_up, stage_down,
    cot_sems, ship_send, ship_recv, cell_send, cell_recv, done_sems,
):
    f32, bf16 = jnp.float32, jnp.bfloat16
    step = pl.program_id(0)
    slot = step % 2
    width = w_up.shape[0]
    tiles, length = cot_rows.shape[:2]
    part = width // shards
    half = width // 2
    size = keep_ref.shape[2]
    win, blk, core, _, _ = position()
    peer = (win + 1 - 2 * core, blk)

    def rows_of(n):
        return slice(n * length, (n + 1) * length)

    def ship(what):
        for n, tile in enumerate(kept_tiles):
            return_tile(tile, output.at[rows_of(tile)], out_ref, ship_send.at[n], ship_recv, what)

    def moves(c):
        cuts = []
        if c < chunks:
            base = 4 * c
            for first, count, piece, row in span_cuts(c * part, part, size):
                cuts.append((base + len(cuts), stage_up.at[c % 2, :, pl.ds(first, count)], slice(0, shards), piece, row, count))
            mine = slice(2 * c, 2 * c + 2)
            for first, count, piece, row in span_cuts(chunks * part, half, size):
                cuts.append((24 + base + len(cuts), stage_down.at[c % 2, :, pl.ds(first, count)], mine, piece, row, count))
        else:
            start = chunks * part + half
            for first, count, piece, row in span_cuts(start, 4 * size - start, size):
                cuts.append((20 + len(cuts), stage_up.at[0, :, pl.ds(first, count)], slice(0, shards), piece, row, count))
        return cuts

    def act(c, what):
        for number, source, mine, piece, row, count in moves(c):
            cell = (pl.ds(mine.start, mine.stop - mine.start), piece // 2, pl.ds(row, count))
            def far():
                return pltpu.make_async_remote_copy(
                    src_ref=source, dst_ref=other_ref.at[cell], send_sem=cell_send.at[number], recv_sem=cell_recv.at[number],
                    device_id=peer, device_id_type=MESH,
                )

            @pl.when(core == piece % 2)
            def _():
                if what == "receive":
                    far().wait_recv()
                else:
                    near = pltpu.make_async_copy(source, keep_ref.at[cell], cell_send.at[number])
                    near.start() if what == "start" else near.wait()

            if what != "receive":
                @pl.when(core != piece % 2)
                def _():
                    far().start() if what == "start" else far().wait_send()

    def cot_moves():
        return [
            pltpu.make_async_copy(source, cot_rows.at[n], cot_sems.at[n]) for n, source in enumerate((cot_a, cot_b, cot_c, cot_d))
        ]

    @pl.when(step == 0)
    def _():
        for move in cot_moves():
            move.start()
        greet_owners(tiles, [peer])
        ship(True)
        vec_ref[...] = jnp.zeros_like(vec_ref)
        for n, move in enumerate(cot_moves()):
            move.wait()
            upstream = cot_rows[n].astype(f32) * scale[0]
            vec_ref[3:4] += column_sum(upstream)
            branch[rows_of(n), :] = upstream.astype(bf16)
            branch_t[:, rows_of(n)] = upstream.astype(bf16).T
        grad_second[...] = jnp.zeros_like(grad_second)

    for c in range(2, chunks):
        @pl.when(step == c)
        def _():
            act(c - 2, "wait")

    full = jnp.dot(branch_t[...], active_ref[...], preferred_element_type=f32)
    for n in range(2):
        for k in range(2):
            stage_down[slot, n, :, k * half : (k + 1) * half] = full[k * half : (k + 1) * half, n * half : (n + 1) * half].astype(bf16)
    total = jnp.zeros((1, w_up.shape[1]), f32)
    for n in range(tiles):
        grad = across(branch[rows_of(n), :], w_down[...]) * slope_ref[rows_of(n), :].astype(f32)
        total = total + column_sum(grad)
        grad_inner[rows_of(n), :] = grad.astype(bf16)
        grad_second[rows_of(n), :] += across(grad_inner[rows_of(n), :], w_up[...])
    vec_up_ref[pl.ds(step, 1), :] = total
    full = jnp.dot(second_t[...], grad_inner[...], preferred_element_type=f32)
    for b in range(shards):
        stage_up[slot, b, 0:part] = full[b * part : (b + 1) * part].astype(bf16)
    for c in range(chunks):
        @pl.when(step == c)
        def _():
            act(c, "start")

    @pl.when(step == chunks - 1)
    def _():
        for n in range(tiles):
            upstream = cot_rows[n].astype(f32) * scale[0]
            grad = grad_second[rows_of(n), :]
            normal = normal_ref[rows_of(n), :].astype(f32)
            grad_resid = upstream + norm_back(grad, normal, rstd_ref[rows_of(n), 0:1], gain[...])
            grad_proj = grad_resid.astype(bf16)
            grad_inner[rows_of(n), :] = grad_proj
            branch[rows_of(n), :] = across(grad_proj, w_out[...]).astype(bf16)
            vec_ref[0:1] += column_sum(grad_resid)
            vec_ref[1:2] += column_sum(grad * normal)
            vec_ref[2:3] += column_sum(grad)
        results = [
            pltpu.make_async_copy(grad_inner, resid_ref, done_sems.at[0]),
            pltpu.make_async_copy(branch, go_ref, done_sems.at[1]),
        ]
        for move in results:
            move.start()
        full = jnp.dot(att_t[...], grad_inner[...], preferred_element_type=f32)
        act(chunks - 2, "wait")
        for b in range(shards):
            stage_up[0, b, 0:part] = full[b * part : (b + 1) * part].astype(bf16)
            stage_up[0, b, part:] = jnp.zeros((stage_up.shape[2] - part, width), bf16)
        act(chunks, "start")
        act(chunks - 1, "wait")
        act(chunks, "wait")
        for c in range(chunks + 1):
            act(c, "receive")
        for move in results:
            move.wait()
        ship(False)


def span_cuts(start, count, size):
    cuts, at = [], start
    while at < start + count:
        end = min(start + count, (at // size + 1) * size)
        cuts.append((at - start, end - at, at // size, at % size))
        at = end
    return cuts


def row_cuts(count, part, size):
    cuts = []
    for k in range(count):
        start = k * part
        while start < (k + 1) * part:
            end = min((k + 1) * part, (start // size + 1) * size)
            cuts.append((k, start - k * part, end - start, start // size, start % size))
            start = end
    return cuts


def add_into(target, got):
    target[...] = (target[...].astype(jnp.float32) + got[...].astype(jnp.float32)).astype(jnp.bfloat16)


def finish_kernel(groups, *refs):
    f32, bf16 = jnp.float32, jnp.bfloat16
    parts = refs[: 3 * groups - 1]
    (
        last_other, rows_ref, resid_ref, gain, shift, weight, vec_two, vec_up, early_a, early_b, early_c, early_d,
        tok_ref, late_ref, early_ref,
        joined, turned, vec, out_rows, cells, core_got, late_bufs, early_bufs, send_sems, recv_sems, load_sems, chain_send, chain_recv, keep_sems, last_rows, last_send, last_recv,
    ) = refs[3 * groups - 1 :]
    step, steps = pl.program_id(0), pl.num_programs(0)
    length, width = rows_ref.shape
    lanes = width // groups
    part = width // 8
    win, blk, core, layer, side = position()
    pair = win // 2
    core_peer = (win + 1 - 2 * core, blk)
    pair_peer = (win + 2 - 4 * pair, blk)
    side_peer = (win, blk + 1 - 2 * side)
    layer_peers = [(win, ((layer + n) % 4) * 2 + side) for n in (1, 2, 3)]

    def remote(source, target, number, peer):
        return pltpu.make_async_remote_copy(
            src_ref=source, dst_ref=target, send_sem=chain_send.at[number], recv_sem=chain_recv.at[number],
            device_id=peer, device_id_type=MESH,
        )

    early_got, early_final = early_bufs

    def loads():
        return [
            pltpu.make_async_copy(source, early_got.at[n], load_sems.at[n])
            for n, source in enumerate((early_a, early_b, early_c, early_d))
        ]

    def second_step(state, got, base):
        return [
            remote(state.at[0, :, 1 - pair], got.at[0], base, pair_peer),
            remote(state.at[1, :, 1 - side], got.at[1], base + 1, side_peer),
        ]

    def add_second(state, got, mid):
        for z in range(2):
            mid[0, z] = (state[0, z, pair].astype(f32) + got[0, z].astype(f32)).astype(bf16)
            mid[1, z] = (state[1, z, side].astype(f32) + got[1, z].astype(f32)).astype(bf16)

    def layer_step(mid, got, base):
        moves = []
        for n in range(3):
            other = (layer + n + 1) % 4
            moves.append(remote(mid.at[other // 2, other % 2], got.at[n], base + n, layer_peers[n]))
        return moves

    def sum_into(final, parts):
        total = parts[0].astype(f32)
        for one in parts[1:]:
            total = total + one.astype(f32)
        final[...] = total.astype(bf16)

    def share(final, target, base):
        return [
            remote(final, target.at[win], base, core_peer),
            remote(final, target.at[win], base + 1, pair_peer),
        ]

    def pass_on(target, base):
        return [remote(target.at[win + 2 - 4 * pair], target.at[win + 2 - 4 * pair], base, core_peer)]

    def start(moves):
        for move in moves:
            move.start()

    def wait(moves):
        for move in moves:
            move.wait()

    def last_move(number):
        first = pl.multiple_of(tile_order(number) * length, length)
        return pltpu.make_async_remote_copy(
            src_ref=last_other.at[pl.ds(first, length)], dst_ref=last_rows.at[number], send_sem=last_send.at[number],
            recv_sem=last_recv.at[number], device_id=core_peer, device_id_type=MESH,
        )

    late_first, late_second, late_mid, late_got, late_final = late_bufs
    early_base, late_base = 8, 0

    @pl.when(step == 0)
    def _():
        start(loads())
        greet_owners(steps, [core_peer, pair_peer, side_peer] + layer_peers)
        for n in range(4):
            last_move(n).start()
        vec[...] = jnp.zeros_like(vec)

    tile = tile_order(step)
    rows = pl.ds(pl.multiple_of(tile * length, length), length)
    last_move(step).wait()
    for g in range(groups):
        dq, own = parts[3 * g : 3 * g + 2]
        other = parts[3 * g + 2] if g < groups - 1 else last_rows.at[step]
        columns = slice(g * lanes, (g + 1) * lanes)
        joined[rows, columns] = dq[...]
        both = (own[...].astype(f32) + other[...].astype(f32)).astype(bf16)
        joined[rows, width + g * lanes : width + (g + 1) * lanes] = both[:, :lanes]
        joined[rows, 2 * width + g * lanes : 2 * width + (g + 1) * lanes] = both[:, lanes:]
        vec[0:1, columns] += column_sum(dq[...].astype(f32))
        vec[1:2, columns] += column_sum(both[:, lanes:].astype(f32))
    grad = across(joined[rows, :], weight[...])
    normal, rstd = norm_parts(rows_ref[...].astype(f32))
    turned[tile] = (normal * gain[...] + shift[...]).astype(bf16).T
    vec[2:3] += column_sum(grad * normal)
    vec[3:4] += column_sum(grad)
    out_rows[step] = (resid_ref[...].astype(f32) + norm_back(grad, normal, rstd, gain[...])).astype(bf16)
    return_tile(tile, out_rows.at[step], tok_ref, send_sems.at[step], recv_sems, True)

    @pl.when(step == 0)
    def _():
        wait(loads())
        sum_into(early_final, [early_got[n] for n in range(4)])
        start(share(early_final, early_ref, early_base))
        pltpu.make_async_copy(early_final, early_ref.at[win], keep_sems.at[0]).start()

    @pl.when(step == steps - 1)
    def _():
        size = cells.shape[5]
        cuts = row_cuts(3, part, size)
        for k in range(3):
            full = jnp.dot(turned[0], joined[0:length, k * width : (k + 1) * width], preferred_element_type=f32)
            for n in range(1, 4):
                full = full + jnp.dot(
                    turned[n], joined[n * length : (n + 1) * length, k * width : (k + 1) * width], preferred_element_type=f32
                )
            for b in range(8):
                for which, first, count, piece, row in cuts:
                    if which == k:
                        cells[piece % 2, b // 4, b // 2 % 2, b % 2, piece // 2, row : row + count] = full[
                            b * part + first : b * part + first + count
                        ].astype(bf16)
        tail = jnp.concatenate(
            [vec[...], vec_two[...], vec_up[...]]
            + [jnp.zeros((4 * size - 3 * part - 12, width), f32)],
            axis=0,
        ).astype(bf16)
        for b in range(8):
            cells[1, b // 4, b // 2 % 2, b % 2, 1, 3 * part - 3 * size :] = tail
        exchange = [remote(cells.at[1 - core], core_got, late_base, core_peer)]
        start(exchange)
        wait(share(early_final, early_ref, early_base))
        start(pass_on(early_ref, early_base + 2))
        wait(exchange)
        mine = cells.at[core]
        for b in range(8):
            for x in range(2):
                add_into(mine.at[b // 4, b // 2 % 2, b % 2, x], core_got.at[b // 4, b // 2 % 2, b % 2, x])
        first = [
            remote(mine.at[0, :, 1 - side], late_first.at[0], late_base + 1, side_peer),
            remote(mine.at[1, :, :, 1 - pair], late_first.at[1], late_base + 2, pair_peer),
        ]
        start(first)
        wait(first)
        state = core_got.at[0]
        for z in range(2):
            for n in range(2):
                state[0, z, n] = (mine[0, z, side, n].astype(f32) + late_first[0, z, n].astype(f32)).astype(bf16)
                state[1, z, n] = (mine[1, z, n, pair].astype(f32) + late_first[1, z, n].astype(f32)).astype(bf16)
        start(second_step(state, late_second, late_base + 3))
        wait(second_step(state, late_second, late_base + 3))
        add_second(state, late_second, late_mid)
        across_layers = layer_step(late_mid, late_got, late_base + 5)
        start(across_layers)
        wait(across_layers)
        sum_into(late_final, [late_mid[layer // 2, layer % 2]] + [late_got[n] for n in range(3)])
        start(share(late_final, late_ref, early_base + 3))
        keep_late = pltpu.make_async_copy(late_final, late_ref.at[win], keep_sems.at[1])
        keep_late.start()
        wait(share(late_final, late_ref, early_base + 3))
        start(pass_on(late_ref, early_base + 5))
        wait(pass_on(early_ref, early_base + 2))
        wait(pass_on(late_ref, early_base + 5))
        pltpu.make_async_copy(early_final, early_ref.at[win], keep_sems.at[0]).wait()
        keep_late.wait()
        for n in range(4):
            return_tile(tile_order(n), out_rows.at[n], tok_ref, send_sems.at[n], recv_sems, False)


def first_send_kernel(place, keep_left, other_left, keep_right, other_right, left_ref, right_ref):
    for keep, other, target in ((keep_left, other_left, left_ref), (keep_right, other_right, right_ref)):
        target[...] = (keep[...].astype(jnp.float32) + other[...].astype(jnp.float32)).astype(jnp.bfloat16).reshape(target.shape)


def sum_low(target, refs):
    total = refs[0][...].astype(jnp.float32)
    for ref in refs[1:]:
        total = total + ref[...].astype(jnp.float32)
    target[...] = total.astype(jnp.bfloat16).reshape(target.shape)


def second_send_kernel(place, *refs):
    keep, left, right = refs[12:]
    for n, target in enumerate((keep.at[0], keep.at[1], left, right)):
        sum_low(target, refs[3 * n : 3 * n + 3])


def third_send_kernel(place, *refs):
    for n in range(4):
        keep, left, right = refs[3 * n : 3 * n + 3]
        in_left = (place[3] + n) % 4 < 2
        got = jnp.where(in_left, left[...].astype(jnp.float32), right[...].astype(jnp.float32))
        target = refs[12 + n]
        target[...] = (keep[...].reshape(target.shape).astype(jnp.float32) + got.reshape(target.shape)).astype(jnp.bfloat16)


def unpack_kernel(early, late, qkv_ref, out_ref, up_ref, down_ref):
    f32 = jnp.float32
    part, width = out_ref.shape
    count = up_ref.shape[1] // width
    half = width // 2

    def cells(source, first, rows):
        size = source.shape[1]
        parts = []
        while rows > 0:
            take = min(rows, size - first % size)
            parts.append(source[first // size, first % size : first % size + take])
            first, rows = first + take, rows - take
        return (parts[0] if len(parts) == 1 else jnp.concatenate(parts, axis=0)).astype(f32)

    for k in range(3):
        qkv_ref[:, k * width : (k + 1) * width] = cells(late, k * part, part)
    for k in range(count):
        up_ref[:, k * width : (k + 1) * width] = cells(early, k * part, part)
    turned = cells(early, count * part, half)
    down_ref[:, :half] = turned[:, :half].T
    down_ref[:, half:] = turned[:, half:].T
    out_ref[...] = cells(early, count * part + half, part)


def general_body(
    tokens,
    cotangent,
    w_qkv,
    b_q,
    b_v,
    w_out,
    b_out,
    gain_one,
    shift_one,
    gain_two,
    shift_two,
    w_up,
    b_up,
    w_down,
    b_down,
    rand_owner,
    rand_sub,
    global_ids,
    species,
):
    blk_count = lax.axis_size("blk")
    blk_pos = lax.axis_index("blk")
    win_pos = lax.axis_index("win")
    windows, length, model_width = tokens.shape
    blocks = rand_owner.shape[1]
    heads = rand_owner.shape[2]
    picks = rand_owner.shape[3]
    glob_count = global_ids.shape[1]
    own_blocks = blocks // blk_count
    block_len = length // own_blocks
    head_dim = model_width // heads
    pair_width = 2 * head_dim
    all_rows = windows * length
    key_count = 3 + glob_count + picks
    per_device = own_blocks * heads * picks
    slot_cap = max(2, 2 * per_device // blk_count)
    score_scale = head_dim ** (-0.5)
    f32 = jnp.float32
    bf16 = jnp.bfloat16
    tokens_f = tokens.reshape(all_rows, model_width).astype(f32)
    normed_f, norm_one_pull = jax.vjp(layer_norm, tokens_f, gain_one, shift_one)
    normed = normed_f.astype(bf16)
    joined = jnp.dot(normed, w_qkv, preferred_element_type=f32)
    query_vals = (joined[:, :model_width] + b_q).astype(bf16)
    key_vals = joined[:, model_width : 2 * model_width].astype(bf16)
    value_vals = (joined[:, 2 * model_width :] + b_v).astype(bf16)

    def to_heads(tensor):
        return tensor.reshape(windows, own_blocks, block_len, heads, head_dim).transpose(
            0, 1, 3, 2, 4
        )

    def from_heads(tensor):
        return tensor.transpose(0, 1, 3, 2, 4).reshape(all_rows, model_width)

    query_heads = to_heads(query_vals)
    local_pairs = jnp.concatenate([to_heads(key_vals), to_heads(value_vals)], axis=-1)
    rimmed = padded(local_pairs, (("blk", 1),), 1)
    block_ids = blk_pos * own_blocks + jnp.arange(own_blocks, dtype=jnp.int32)
    owned_glob = (global_ids[:, :, None] == block_ids[None, None, :]).astype(bf16)
    glob_terms = jnp.einsum("wgb,wbhsc->wghsc", owned_glob, local_pairs, preferred_element_type=f32)
    glob_pairs = lax.psum(glob_terms.astype(jnp.bfloat16), "blk").astype(jnp.float32).astype(bf16)
    owner_rows = rand_owner.reshape(windows, blk_count, per_device)
    sub_rows = rand_sub.reshape(windows, blk_count, per_device)
    owner_hits = (owner_rows[..., None] == jnp.arange(blk_count, dtype=jnp.int32)).astype(jnp.int32)
    slot_rows = jnp.sum(owner_hits * (jnp.cumsum(owner_hits, axis=2) - 1), axis=-1)
    my_owner = lax.dynamic_index_in_dim(owner_rows, blk_pos, 1, keepdims=False)
    my_slot = lax.dynamic_index_in_dim(slot_rows, blk_pos, 1, keepdims=False)
    fetch_index = my_owner * slot_cap + my_slot
    head_of_row = jnp.arange(per_device, dtype=jnp.int32) // picks % heads
    source_rows = sub_rows * heads + head_of_row[None, None, :]
    requester = jnp.arange(blk_count, dtype=jnp.int32)[None, :, None]
    target_rows = jnp.where(
        owner_rows == blk_pos, requester * slot_cap + slot_rows, blk_count * slot_cap
    )
    send_table = jnp.full((windows, blk_count * slot_cap + 1), own_blocks * heads, jnp.int32)
    send_table = jax.vmap(set_rows)(
        send_table, target_rows.reshape(windows, -1), source_rows.reshape(windows, -1)
    )[:, : blk_count * slot_cap]
    flat_pairs = jnp.concatenate(
        [
            local_pairs.reshape(windows, own_blocks * heads, block_len, pair_width),
            jnp.zeros((windows, 1, block_len, pair_width), bf16),
        ],
        axis=1,
    )
    outgoing = jax.vmap(take_rows)(flat_pairs, send_table).reshape(
        windows, blk_count, slot_cap, block_len, pair_width
    )
    incoming = lax.all_to_all(outgoing, "blk", split_axis=1, concat_axis=1, tiled=True).reshape(
        windows, blk_count * slot_cap, block_len, pair_width
    )
    rand_pairs = jax.vmap(take_rows)(incoming, fetch_index).reshape(
        windows, own_blocks, heads, picks, block_len, pair_width
    )
    near_pairs = jnp.stack(
        [rimmed[:, 0:own_blocks], rimmed[:, 1 : own_blocks + 1], rimmed[:, 2 : own_blocks + 2]],
        axis=3,
    )
    far_pairs = jnp.broadcast_to(
        glob_pairs.transpose(0, 2, 1, 3, 4)[:, None],
        (windows, own_blocks, heads, glob_count, block_len, pair_width),
    )
    gathered_keys = jnp.concatenate([near_pairs, far_pairs, rand_pairs], axis=3).reshape(
        windows, own_blocks, heads, key_count * block_len, pair_width
    )
    set_keys = gathered_keys[..., :head_dim]
    set_values = gathered_keys[..., head_dim:]
    block_flags = jnp.concatenate(
        [
            (block_ids > 0)[:, None],
            jnp.ones((own_blocks, 1), jnp.bool_),
            (block_ids < blocks - 1)[:, None],
            jnp.ones((own_blocks, glob_count + picks), jnp.bool_),
        ],
        axis=1,
    )
    key_valid = jnp.repeat(block_flags, block_len, axis=1)[None, :, None, None, :]

    def score_block():
        raw_scores = (
            jnp.einsum("wbhqe,wbhke->wbhqk", query_heads, set_keys, preferred_element_type=f32)
            * score_scale
        )
        return jnp.where(key_valid, raw_scores, masked_score)

    score_matrix = score_block()
    top_score = jnp.max(score_matrix, axis=-1, keepdims=True)
    log_total = top_score + jnp.log(
        jnp.sum(jnp.exp(score_matrix - top_score), axis=-1, keepdims=True)
    )
    probs_low = jnp.exp(score_matrix - log_total).astype(bf16)
    attended = jnp.einsum(
        "wbhqk,wbhke->wbhqe", probs_low, set_values, preferred_element_type=f32
    ).astype(bf16)
    merged = from_heads(attended)
    residual = tokens_f + (jnp.dot(merged, w_out, preferred_element_type=f32) + b_out)
    second_f, norm_two_pull = jax.vjp(layer_norm, residual, gain_two, shift_two)
    second = second_f.astype(bf16)
    inner_f = jnp.dot(second, w_up, preferred_element_type=f32) + b_up
    active_f, gelu_pull = jax.vjp(partial(jax.nn.gelu, approximate=False), inner_f)
    active = active_f.astype(bf16)
    output = residual + (jnp.dot(active, w_down, preferred_element_type=f32) + b_down)
    species_count = jnp.sum(
        (species[:, None] == jnp.arange(SPECIES, dtype=jnp.int32)[None, :]).astype(f32), axis=0
    )
    my_species = lax.dynamic_slice_in_dim(species, win_pos * windows, windows)
    own_count = jnp.sum(
        (my_species[:, None] == jnp.arange(SPECIES, dtype=jnp.int32)[None, :]).astype(f32)
        * species_count[None, :],
        axis=1,
    )
    window_scale = jnp.sqrt(species.shape[0] / (SPECIES * own_count))
    upstream = (cotangent.astype(f32) * window_scale[:, None, None]).reshape(all_rows, model_width)
    grad_branch = upstream.astype(bf16)
    grad_w_down = jnp.einsum("tf,td->fd", active, grad_branch, preferred_element_type=f32)
    grad_b_down = jnp.sum(grad_branch, axis=0, dtype=f32)
    grad_active = jnp.einsum("td,fd->tf", grad_branch, w_down, preferred_element_type=f32)
    grad_inner = gelu_pull(grad_active)[0].astype(bf16)
    grad_w_up = jnp.einsum("td,tf->df", second, grad_inner, preferred_element_type=f32)
    grad_b_up = jnp.sum(grad_inner, axis=0, dtype=f32)
    grad_second = jnp.einsum("tf,df->td", grad_inner, w_up, preferred_element_type=f32)
    grad_resid_norm, grad_gain_two, grad_shift_two = norm_two_pull(grad_second)
    grad_resid = upstream + grad_resid_norm
    grad_proj = grad_resid.astype(bf16)
    grad_w_out = jnp.einsum("ti,to->io", merged, grad_proj, preferred_element_type=f32)
    grad_b_out = jnp.sum(grad_proj, axis=0, dtype=f32)
    grad_attended = to_heads(
        jnp.einsum("to,io->ti", grad_proj, w_out, preferred_element_type=f32).astype(bf16)
    )
    probs_full = jnp.exp(score_block() - log_total)
    grad_probs = jnp.einsum(
        "wbhqe,wbhke->wbhqk", grad_attended, set_values, preferred_element_type=f32
    )
    grad_set_values = jnp.einsum(
        "wbhqk,wbhqe->wbhke", probs_full.astype(bf16), grad_attended, preferred_element_type=f32
    )
    row_dot = jnp.sum(probs_full * grad_probs, axis=-1, keepdims=True)
    grad_scores = (probs_full * (grad_probs - row_dot)).astype(bf16)
    grad_query = (
        jnp.einsum("wbhqk,wbhke->wbhqe", grad_scores, set_keys, preferred_element_type=f32)
        * score_scale
    )
    grad_set_keys = (
        jnp.einsum("wbhqk,wbhqe->wbhke", grad_scores, query_heads, preferred_element_type=f32)
        * score_scale
    )
    grad_set = jnp.concatenate([grad_set_keys, grad_set_values], axis=-1).reshape(
        windows, own_blocks, heads, key_count, block_len, pair_width
    )
    extended = (
        jnp.pad(grad_set[:, :, :, 1], ((0, 0), (1, 1), (0, 0), (0, 0), (0, 0)))
        + jnp.pad(grad_set[:, :, :, 0], ((0, 0), (0, 2), (0, 0), (0, 0), (0, 0)))
        + jnp.pad(grad_set[:, :, :, 2], ((0, 0), (2, 0), (0, 0), (0, 0), (0, 0)))
    )
    edge_grads = jnp.concatenate([extended[:, :1], extended[:, own_blocks + 1 :]], axis=1)
    edge_back = padded(edge_grads.astype(jnp.bfloat16), (("blk", 1),), 1).astype(edge_grads.dtype)
    pair_grad = extended[:, 1 : own_blocks + 1]
    pair_grad = pair_grad.at[:, 0].add(edge_back[:, 0]).at[:, own_blocks - 1].add(edge_back[:, 3])
    glob_grad = jnp.sum(grad_set[:, :, :, 3 : 3 + glob_count], axis=1).transpose(0, 2, 1, 3, 4)
    glob_total = lax.psum(glob_grad.astype(jnp.bfloat16), "blk").astype(jnp.float32)
    pair_grad = pair_grad + jnp.einsum(
        "wgb,wghsc->wbhsc", owned_glob.astype(f32), glob_total, precision=lax.Precision.HIGHEST
    )
    rand_grad = grad_set[:, :, :, 3 + glob_count :].reshape(
        windows, per_device, block_len, pair_width
    )
    back_out = jax.vmap(add_rows)(
        jnp.zeros((windows, blk_count * slot_cap, block_len, pair_width), f32),
        fetch_index,
        rand_grad,
    )
    back_in = lax.all_to_all(
        back_out.reshape(windows, blk_count, slot_cap, block_len, pair_width).astype(jnp.bfloat16),
        "blk",
        split_axis=1,
        concat_axis=1,
        tiled=True,
    ).astype(jnp.float32)
    owner_sum = jax.vmap(add_rows)(
        jnp.zeros((windows, own_blocks * heads + 1, block_len, pair_width), f32),
        send_table,
        back_in.reshape(windows, blk_count * slot_cap, block_len, pair_width),
    )
    pair_grad = pair_grad + owner_sum[:, : own_blocks * heads].reshape(
        windows, own_blocks, heads, block_len, pair_width
    )
    grad_keys = from_heads(pair_grad[..., :head_dim].astype(bf16))
    grad_values = from_heads(pair_grad[..., head_dim:].astype(bf16))
    grad_joined = jnp.concatenate(
        [from_heads(grad_query.astype(bf16)), grad_keys, grad_values], axis=1
    )
    grad_w_qkv = jnp.einsum("td,tc->dc", normed, grad_joined, preferred_element_type=f32)
    grad_b_q = jnp.sum(grad_joined[:, :model_width], axis=0, dtype=f32)
    grad_b_v = jnp.sum(grad_joined[:, 2 * model_width :], axis=0, dtype=f32)
    grad_normed = jnp.einsum("tc,dc->td", grad_joined, w_qkv, preferred_element_type=f32)
    grad_tok_norm, grad_gain_one, grad_shift_one = norm_one_pull(grad_normed)
    grad_tokens = (grad_resid + grad_tok_norm).astype(bf16).reshape(windows, length, model_width)
    local_grads = (
        grad_w_qkv,
        grad_b_q,
        grad_b_v,
        grad_w_out,
        grad_b_out,
        grad_gain_one,
        grad_shift_one,
        grad_gain_two,
        grad_shift_two,
        grad_w_up,
        grad_b_up,
        grad_w_down,
        grad_b_down,
    )
    packed_grads = jnp.concatenate(
        [grad_item.reshape(blk_count, -1) for grad_item in local_grads], axis=1
    )
    total_cols = packed_grads.shape[1]
    win_count = lax.axis_size("win")
    pad_cols = -total_cols % win_count
    shard_sum = lax.psum_scatter(
        packed_grads.astype(jnp.bfloat16), "blk", scatter_dimension=0, tiled=True
    ).astype(jnp.float32)
    split_shard = jnp.pad(shard_sum, ((0, 0), (0, pad_cols))).reshape(win_count, -1)
    group_piece = lax.psum_scatter(
        split_shard.astype(jnp.bfloat16), "win", scatter_dimension=0, tiled=True
    ).astype(jnp.float32)
    summed = (
        lax.all_gather(group_piece.astype(jnp.bfloat16), "win", axis=0, tiled=True)
        .astype(group_piece.dtype)
        .reshape(1, -1)[:, :total_cols]
    )
    shards = []
    offset = 0
    for grad_item in local_grads:
        entry_count = grad_item.size // blk_count
        shards.append(
            summed[0, offset : offset + entry_count].reshape(
                (grad_item.shape[0] // blk_count,) + grad_item.shape[1:]
            )
        )
        offset = offset + entry_count
    out_tokens = output.astype(bf16).reshape(windows, length, model_width)
    return (
        out_tokens,
        grad_tokens,
        shards[0],
        shards[1],
        shards[2],
        shards[3],
        shards[4],
        shards[5],
        shards[6],
        shards[7],
        shards[8],
        shards[9],
        shards[10],
        shards[11],
        shards[12],
    )


def layer_step(*arguments):
    windows = arguments[0].shape[0]
    paired = lax.axis_size("blk") == 2 * windows and lax.axis_size("win") == 4 and windows == 4
    return (paired_body if paired else general_body)(*arguments)


def paired_body(
    tokens,
    cotangent,
    w_qkv,
    b_q,
    b_v,
    w_out,
    b_out,
    gain_one,
    shift_one,
    gain_two,
    shift_two,
    w_up,
    b_up,
    w_down,
    b_down,
    rand_owner,
    rand_sub,
    global_ids,
    species,
):
    f32 = jnp.float32
    bf16 = jnp.bfloat16
    win_count = lax.axis_size("win")
    blk_count = lax.axis_size("blk")
    win_pos = lax.axis_index("win")
    blk_pos = lax.axis_index("blk")
    layers, length, width = tokens.shape
    core, layer, side = win_pos % 2, blk_pos // 2, blk_pos % 2
    blocks, heads, picks = rand_owner.shape[1:]
    own_blocks = blocks // blk_count
    half_blocks = blocks // 2
    block_len = length // own_blocks
    head_dim = width // heads
    all_rows = layers * length
    lanes = HEADS_PER_GROUP * head_dim
    groups = heads // HEADS_PER_GROUP
    score_scale = head_dim ** (-0.5)

    def regroup(value):
        parts = []
        for step in range(layers):
            part = lax.dynamic_index_in_dim(value, (layer + step) % layers, 0, keepdims=False)
            parts.append(lax.ppermute(part, ("win", "blk"), regroup_pairs(win_count, layers, step)))
        return parts

    def send_back(value):
        parts = []
        for step in range(layers):
            pairs = [(b, a) for a, b in regroup_pairs(win_count, layers, step)]
            parts.append(lax.ppermute(value[step * length : (step + 1) * length], ("win", "blk"), pairs))
        return parts

    def in_order(parts):
        result = jnp.zeros((layers, length, width), parts[0].dtype)
        for step, part in enumerate(parts):
            result = lax.dynamic_update_index_in_dim(result, part, (layer + step) % layers, 0)
        return result

    def takes(micros):
        return pl.CostEstimate(flops=micros * 1_000_000_000, bytes_accessed=micros * 1_000_000, transcendentals=0)

    rows_in = jnp.concatenate(regroup(tokens), axis=0)
    cot_in = regroup(cotangent)

    rand_size = blocks * heads * picks
    named = jnp.concatenate(
        [
            lax.dynamic_index_in_dim((rand_owner * own_blocks + rand_sub).reshape(layers, rand_size), layer, 0, keepdims=False),
            lax.dynamic_index_in_dim(global_ids, layer, 0, keepdims=False),
        ]
    )
    named = jnp.where(side == core, named, swap(named, 1, 0))

    def place_of(block):
        owner = block // own_blocks
        half = jnp.where(owner % 2 == core, 0, half_blocks)
        return half + ((layer - owner // 2) % layers) * own_blocks + block % own_blocks

    slot = jnp.arange(half_blocks, dtype=jnp.int32)
    slot_block = (((layer - slot // own_blocks) % layers) * 2 + core) * own_blocks + slot % own_blocks
    table = jnp.concatenate(
        [
            place_of(named),
            slot_block,
            place_of(jnp.maximum(slot_block - 1, 0)),
            place_of(jnp.minimum(slot_block + 1, blocks - 1)),
        ]
    )
    sizes = (heads, picks, rand_size, half_blocks)

    tile = length

    def by_rows(columns):
        return pl.BlockSpec((tile, columns), lambda i: (i, 0))

    def by_tile(columns):
        return pl.BlockSpec((tile, columns), lambda i: (tile_order(i), 0))

    def whole(*shape, once=True):
        mode = pl.Buffered(1) if once else None
        return pl.BlockSpec(shape, lambda i: (0,) * len(shape), pipeline_mode=mode)

    scalars = pl.BlockSpec(memory_space=pltpu.SMEM)
    wide = w_up.shape[1]
    params = pltpu.CompilerParams(vmem_limit_bytes=60 << 20)
    row = lambda vector: vector.reshape(1, -1)
    query, key_value = pl.pallas_call(
        partial(qkv_kernel, score_scale),
        grid=(all_rows // tile,),
        in_specs=[by_rows(width), whole(1, width), whole(1, width), whole(width, 3 * width), whole(2, width)],
        out_specs=[by_rows(width), by_rows(2 * width)],
        out_shape=[jax.ShapeDtypeStruct((all_rows, width), bf16), jax.ShapeDtypeStruct((all_rows, 2 * width), bf16)],
        compiler_params=params,
        cost_estimate=takes(12),
        name="qkv",
    )(rows_in, row(gain_one), row(shift_one), w_qkv, jnp.stack([b_q, b_v]))
    key_value_other = swap(key_value, 1, 0)

    def lane_block(first):
        return pl.BlockSpec((all_rows, lanes), lambda g, t: (0, first + g))

    store = pltpu.VMEM((blocks, block_len, lanes), bf16)
    attended, log_total = pl.pallas_call(
        partial(attend_kernel, sizes, blocks, head_dim),
        grid_spec=pltpu.PrefetchScalarGridSpec(
            num_scalar_prefetch=1,
            grid=(groups,),
            in_specs=[lane_block(0), lane_block(0), lane_block(0), lane_block(groups), lane_block(groups)],
            out_specs=[lane_block(0), pl.BlockSpec((1, half_blocks, lanes), lambda g, t: (g, 0, 0))],
            scratch_shapes=[store, store],
        ),
        out_shape=[
            jax.ShapeDtypeStruct((all_rows, width), bf16),
            jax.ShapeDtypeStruct((groups, half_blocks, lanes), f32),
        ],
        compiler_params=pltpu.CompilerParams(vmem_limit_bytes=56 << 20),
        cost_estimate=takes(37),
        name="attend",
    )(table, query, key_value, key_value_other, key_value, key_value_other)

    species_count = jnp.sum(
        (species[:, None] == jnp.arange(SPECIES, dtype=jnp.int32)[None, :]).astype(f32), axis=0
    )
    my_window = ((win_pos // 2) * 2 + side) * layers + layer
    my_species = lax.dynamic_index_in_dim(species, my_window, 0, keepdims=False)
    own_count = jnp.sum(
        (my_species == jnp.arange(SPECIES, dtype=jnp.int32)).astype(f32) * species_count
    )
    window_scale = jnp.sqrt(species.shape[0] / (SPECIES * own_count))
    payload = 2 * wide // blk_count + width // blk_count
    payload += -payload % (16 * win_count)
    stays = jax.ShapeDtypeStruct((blk_count, win_count // 2, payload // win_count, width), bf16)
    any_place = pl.BlockSpec(memory_space=pl.ANY)
    def remote_params(number, mib):
        return pltpu.CompilerParams(vmem_limit_bytes=mib << 20, collective_id=number, has_side_effects=True)

    output, normal, second_t, attended_t, rstd, active, slope = pl.pallas_call(
        partial(ffn_forward_kernel, 256),
        grid=(layers,),
        in_specs=[
            by_rows(width), by_rows(width), whole(width, width), whole(1, width), whole(1, width),
            whole(1, width), whole(width, wide), whole(1, wide), whole(wide, width), whole(1, width),
        ],
        out_specs=[
            by_rows(width), by_rows(width), pl.BlockSpec((width, length), lambda i: (0, i)), pl.BlockSpec((width, length), lambda i: (0, i)),
            by_rows(128), by_rows(wide), by_rows(wide),
        ],
        out_shape=[
            jax.ShapeDtypeStruct((all_rows, width), bf16),
            jax.ShapeDtypeStruct((all_rows, width), bf16),
            jax.ShapeDtypeStruct((width, all_rows), bf16),
            jax.ShapeDtypeStruct((width, all_rows), bf16),
            jax.ShapeDtypeStruct((all_rows, 128), f32),
            jax.ShapeDtypeStruct((all_rows, wide), bf16),
            jax.ShapeDtypeStruct((all_rows, wide), bf16),
        ],
        compiler_params=params,
        cost_estimate=takes(35),
        name="ffn_forward",
    )(rows_in, attended, w_out, row(b_out), row(gain_two), row(shift_two), w_up, row(b_up), w_down, row(b_down))

    chunks = wide // width

    def keep(*shape):
        return pltpu.VMEM(shape, bf16)

    grad_resid, grad_attended, vec_two, vec_up, early_keep, early_other, out_tokens = pl.pallas_call(
        partial(ffn_back_kernel, chunks, blk_count, (2, 1, 0)),
        grid=(chunks,),
        in_specs=[
            scalars, pl.BlockSpec((all_rows, width), lambda i: (0, i)), pl.BlockSpec((all_rows, width), lambda i: (0, i)),
            pl.BlockSpec((width, width), lambda i: (0, i)), pl.BlockSpec((width, width), lambda i: (i, 0)),
            whole(width, all_rows), whole(all_rows, width), whole(all_rows, 128), whole(width, all_rows), whole(width, width), whole(1, width),
            *[any_place] * (layers + 1),
        ],
        out_specs=[any_place, any_place, whole(4, width), whole(chunks, width), any_place, any_place, any_place],
        out_shape=[
            jax.ShapeDtypeStruct((all_rows, width), bf16),
            jax.ShapeDtypeStruct((all_rows, width), bf16),
            jax.ShapeDtypeStruct((4, width), f32),
            jax.ShapeDtypeStruct((chunks, width), f32),
            stays,
            stays,
            jax.ShapeDtypeStruct((layers, length, width), bf16),
        ],
        scratch_shapes=[
            keep(layers, length, width),
            keep(all_rows, width),
            keep(width, all_rows),
            keep(all_rows, width),
            pltpu.VMEM((all_rows, width), f32),
            keep(2, blk_count, payload - chunks * width // blk_count - width // 2, width),
            keep(2, 2, width // 2, width),
            pltpu.SemaphoreType.DMA((layers,)),
            pltpu.SemaphoreType.DMA((layers,)),
            pltpu.SemaphoreType.DMA((layers,)),
            pltpu.SemaphoreType.DMA((48,)),
            pltpu.SemaphoreType.DMA((48,)),
            pltpu.SemaphoreType.DMA((2,)),
        ],
        compiler_params=remote_params(3, 63),
        cost_estimate=takes(60),
        name="ffn_back",
    )(
        window_scale.reshape(1), active, slope, w_up, w_down, second_t, normal, rstd, attended_t, w_out, row(gain_two), *cot_in, output,
    )
    last_pairs = [(there, here) for here, there in regroup_pairs(win_count, layers, 3)]
    out_last = lax.ppermute(output[3 * length : 4 * length], ("win", "blk"), last_pairs)

    pair = win_pos // 2
    early_rows = payload // win_count
    late_rows = 3 * width // blk_count + 32
    late_size = late_rows // win_count
    cell = (early_rows, width)
    early_keep = early_keep.reshape((2, 2, 2, 2) + cell)
    early_other = early_other.reshape((2, 2, 2, 2) + cell)
    place = jnp.stack([side, pair, side, layer])

    def picked(index):
        return pl.BlockSpec((1, 1, 1, 1) + cell, lambda z, n, p: index(z, n, p) + (0, 0))

    def listed(index):
        return pl.BlockSpec((1, 1) + cell, lambda z, n, p: index(z, n, p) + (0, 0))

    def cells_of(count):
        return [jax.ShapeDtypeStruct((2, 2) + cell, bf16)] * count

    def first_send():
        left = picked(lambda z, n, p: (0, z, 1 - p[0], n))
        right = picked(lambda z, n, p: (1, z, n, 1 - p[1]))
        return pl.pallas_call(
            first_send_kernel,
            grid_spec=pltpu.PrefetchScalarGridSpec(
                num_scalar_prefetch=1, grid=(2, 2), in_specs=[left, left, right, right], out_specs=[listed(lambda z, n, p: (z, n))] * 2
            ),
            out_shape=cells_of(2),
            cost_estimate=takes(3),
            name="first_send",
        )(place, early_keep, early_other, early_keep, early_other)

    def second_send(got_left, got_right):
        specs, operands = [], []
        for far in (0, 1):
            bit = lambda n, p, f=far: p[n] if f == 0 else 1 - p[n]
            left = picked(lambda z, n, p, bit=bit: (0, z, p[0], bit(1, p)))
            right = picked(lambda z, n, p, bit=bit: (1, z, bit(0, p), p[1]))
            specs += [left, left, listed(lambda z, n, p, bit=bit: (z, bit(1, p)))]
            operands += [early_keep, early_other, got_left]
            specs += [right, right, listed(lambda z, n, p, bit=bit: (z, bit(0, p)))]
            operands += [early_keep, early_other, got_right]
        rows_spec = pl.BlockSpec((1,) + cell, lambda z, n, p: (z, 0, 0))
        both_spec = pl.BlockSpec((2, 1) + cell, lambda z, n, p: (0, z, 0, 0))
        return pl.pallas_call(
            second_send_kernel,
            grid_spec=pltpu.PrefetchScalarGridSpec(num_scalar_prefetch=1, grid=(2, 1), in_specs=specs, out_specs=[both_spec, rows_spec, rows_spec]),
            out_shape=cells_of(1) + [jax.ShapeDtypeStruct((2,) + cell, bf16)] * 2,
            cost_estimate=takes(4),
            name="second_send",
        )(place, *operands)

    def third_send(keep, left, right):
        specs = []
        for step in range(layers):
            goal = lambda p, step=step: (p[3] + step) % layers
            specs.append(listed(lambda z, n, p, goal=goal: (goal(p) // 2, goal(p) % 2)))
            specs += [pl.BlockSpec((1,) + cell, lambda z, n, p, goal=goal: (goal(p) % 2, 0, 0))] * 2
        out = pl.BlockSpec(cell, lambda z, n, p: (0, 0))
        return pl.pallas_call(
            third_send_kernel,
            grid_spec=pltpu.PrefetchScalarGridSpec(num_scalar_prefetch=1, grid=(1, 1), in_specs=specs, out_specs=[out] * layers),
            out_shape=[jax.ShapeDtypeStruct(cell, bf16)] * layers,
            cost_estimate=takes(3),
            name="third_send",
        )(place, *[keep, left, right] * layers)

    def to_layer(value, step):
        pairs = [
            (win * blk_count + blk, win * blk_count + (blk + 2 * step) % blk_count)
            for win in range(win_count)
            for blk in range(blk_count)
        ]
        return lax.ppermute(value, ("win", "blk"), pairs)

    first_left, first_right = first_send()
    first_left, first_right = swap(first_left, 0, 1), swap(first_right, 2, 0)

    grad_parts = []
    for group in range(groups):
        after = []
        if group == 1:
            early_kept, send_left, send_right = second_send(first_left, first_right)
            after = [early_kept, out_last]
            second = swap(send_left, 2, 0), swap(send_right, 0, 1)
        if group == 2:
            early_parts = third_send(early_kept, *second)
            after = [early_parts[0]]
            early_parts = [early_parts[0]] + [to_layer(early_parts[n], n) for n in range(1, layers)]

        def column(first):
            return pl.BlockSpec((all_rows, lanes), lambda g, t: (0, first))

        def full(columns):
            return pl.BlockSpec((all_rows, columns), lambda g, t: (0, 0))

        grad_store = pltpu.VMEM((blocks, block_len, lanes), f32)
        glob_store = pltpu.VMEM((2, block_len, lanes), f32)
        dq, own, other = pl.pallas_call(
            partial(attend_back_kernel, sizes, blocks, head_dim, score_scale, group),
            grid_spec=pltpu.PrefetchScalarGridSpec(
                num_scalar_prefetch=1,
                grid=(1,),
                in_specs=[
                    column(group), column(group), column(group), column(groups + group), column(groups + group), column(group),
                    pl.BlockSpec((1, half_blocks, lanes), lambda g, t: (group, 0, 0)),
                    *[any_place] * len(after),
                ],
                out_specs=[full(lanes), full(2 * lanes), full(2 * lanes)],
                scratch_shapes=[store, store, grad_store, grad_store, glob_store, glob_store],
            ),
            out_shape=[jax.ShapeDtypeStruct((all_rows, n * lanes), bf16) for n in (1, 2, 2)],
            compiler_params=params,
            cost_estimate=takes(25),
            name="attend_back",
        )(table, query, key_value, key_value_other, key_value, key_value_other, grad_attended, log_total, *after)
        grad_parts += [dq, own, swap(other, 1, 0) if group < groups - 1 else other]

    def vmem(*shape):
        return pltpu.VMEM(shape, bf16)

    first_shape, mid_shape = (2, 2, 2), (2, 2)
    chain = lambda size: [vmem(*lead, size, width) for lead in (first_shape, mid_shape, mid_shape, (3,), ())]
    grad_tokens, late, early = pl.pallas_call(
        partial(finish_kernel, groups),
        grid=(layers,),
        in_specs=[by_tile(p.shape[1]) for p in grad_parts[:-1]]
        + [any_place, by_tile(width), by_tile(width), whole(1, width), whole(1, width), whole(width, 3 * width), whole(4, width), whole(chunks, width)]
        + [any_place] * layers,
        out_specs=[any_place] * 3,
        out_shape=[
            jax.ShapeDtypeStruct((layers, length, width), bf16),
            jax.ShapeDtypeStruct((win_count, late_size, width), bf16),
            jax.ShapeDtypeStruct((win_count, early_rows, width), bf16),
        ],
        scratch_shapes=[
            vmem(all_rows, 3 * width),
            vmem(layers, width, length),
            pltpu.VMEM((4, width), f32),
            vmem(layers, length, width),
            vmem(2, 2, 2, 2, 2, late_size, width),
            vmem(2, 2, 2, 2, late_size, width),
            chain(late_size),
            [vmem(*lead, early_rows, width) for lead in ((4,), ())],
            pltpu.SemaphoreType.DMA((layers,)),
            pltpu.SemaphoreType.DMA((layers,)),
            pltpu.SemaphoreType.DMA((4,)),
            pltpu.SemaphoreType.DMA((14,)),
            pltpu.SemaphoreType.DMA((14,)),
            pltpu.SemaphoreType.DMA((2,)),
            vmem(layers, length, 2 * lanes),
            pltpu.SemaphoreType.DMA((layers,)),
            pltpu.SemaphoreType.DMA((layers,)),
        ],
        compiler_params=remote_params(2, 62),
        cost_estimate=takes(90),
        name="finish",
    )(
        *grad_parts, rows_in, grad_resid, row(gain_one), row(shift_one), w_qkv, vec_two, vec_up,
        *early_parts,
    )
    part = width // blk_count
    count = wide // width
    done_qkv, done_out, done_up, done_down = pl.pallas_call(
        unpack_kernel,
        out_shape=[
            jax.ShapeDtypeStruct(shape, f32)
            for shape in ((part, 3 * width), (part, width), (part, wide), (wide // blk_count, width))
        ],
        compiler_params=params,
        cost_estimate=takes(4),
        name="unpack",
    )(early, late)
    late = late.reshape(-1, width)[3 * part :].astype(f32)
    vec = lax.dynamic_slice_in_dim(late[:8], blk_pos * part, part, axis=1)
    vec_wide = lax.dynamic_slice_in_dim(late[8 : 8 + count].reshape(-1), blk_pos * (wide // blk_count), wide // blk_count)
    return (
        lax.dynamic_update_index_in_dim(out_tokens, out_last, (layer + 3) % layers, 0),
        grad_tokens,
        done_qkv,
        vec[0],
        vec[1],
        done_out,
        vec[4],
        vec[2],
        vec[3],
        vec[5],
        vec[6],
        done_up,
        vec_wide,
        done_down,
        vec[7],
    )


def solution(mesh):
    placed = (
        P("win", "blk", None),
        P("win", "blk", None),
        P(),
        P(),
        P(),
        P(),
        P(),
        P(),
        P(),
        P(),
        P(),
        P(),
        P(),
        P(),
        P(),
        P("win", None, None, None),
        P("win", None, None, None),
        P("win", None),
        P(),
    )
    return jax.shard_map(
        layer_step,
        mesh=mesh,
        in_specs=placed,
        out_specs=(
            P("win", "blk", None),
            P("win", "blk", None),
            P("blk", None),
            P("blk"),
            P("blk"),
            P("blk", None),
            P("blk"),
            P("blk"),
            P("blk"),
            P("blk"),
            P("blk"),
            P("blk", None),
            P("blk"),
            P("blk", None),
            P("blk"),
        ),
        check_vma=False,
    )
```

```python
from functools import partial

import jax
import jax.numpy as jnp
from jax import lax
from jax.experimental import pallas as pl
from jax.experimental.pallas import tpu as pltpu
from jax.sharding import PartitionSpec as P

SPECIES = 4


epsilon = 1e-05
masked_score = -1000000000.0


def padded(cells, sides, width):
    for axis, dim in sides:
        count = lax.axis_size(axis)
        ends = count - 1
        head = lax.slice_in_dim(cells, 0, width, axis=dim)
        tail = lax.slice_in_dim(cells, cells.shape[dim] - width, cells.shape[dim], axis=dim)
        cells = jnp.concatenate(
            [
                lax.ppermute(tail, axis, [(i, (i + 1) % count) for i in range(ends)]),
                cells,
                lax.ppermute(head, axis, [((i + 1) % count, i) for i in range(ends)]),
            ],
            axis=dim,
        )
    return cells


def layer_norm(values, norm_gain, norm_shift):
    average = jnp.mean(values, axis=-1, keepdims=True)
    centred = values - average
    variance = jnp.mean(centred * centred, axis=-1, keepdims=True)
    return centred * lax.rsqrt(variance + epsilon) * norm_gain + norm_shift


def take_rows(source, index_rows):
    return jnp.take(source, index_rows, axis=0)


def add_rows(base, index_rows, update):
    return base.at[index_rows].add(update)


def set_rows(base, index_rows, update):
    return base.at[index_rows].set(update)


HEADS_PER_GROUP = 4


def regroup_pairs(win_count, layers, step):
    pairs = []
    for win in range(win_count):
        for blk in range(2 * layers):
            layer, side = blk // 2, blk % 2
            target = ((layer + step) % layers) * 2 + win % 2
            pairs.append((win * 2 * layers + blk, ((win // 2) * 2 + side) * 2 * layers + target))
    return pairs


def flip_pairs(win_count, blk_count, win_bit, blk_bit):
    return [
        (win * blk_count + blk, (win ^ win_bit) * blk_count + (blk ^ blk_bit))
        for win in range(win_count)
        for blk in range(blk_count)
    ]


def swap(value, win_bit, blk_bit):
    pairs = flip_pairs(lax.axis_size("win"), lax.axis_size("blk"), win_bit, blk_bit)
    return lax.ppermute(value, ("win", "blk"), pairs)


def head_masks(lanes, head_dim, dtype):
    lane = lax.broadcasted_iota(jnp.int32, (1, lanes), 1)
    return [(lane // head_dim == h).astype(dtype) for h in range(lanes // head_dim)]


def block_places(table, slot, group, sizes):
    heads, picks, rand_size, half_blocks = sizes
    block = table[rand_size + 2 + slot]
    near = [table[rand_size + 2 + half_blocks + slot], slot, table[rand_size + 2 + 2 * half_blocks + slot]]
    row = (block * heads + group * HEADS_PER_GROUP) * picks
    rand = [[table[row + h * picks + r] for h in range(HEADS_PER_GROUP)] for r in range(picks)]
    return block, near, rand


def spread_heads(rows, masks):
    return jnp.concatenate([rows * m for m in masks], axis=0)


def pick_heads(square, masks, height):
    total = square[0:height] * masks[0]
    for h in range(1, len(masks)):
        total = total + square[h * height : (h + 1) * height] * masks[h]
    return total


def key_rows(source, near, glob, rand, low_half):
    parts = [source[p] for p in near] + [source[p] for p in glob]
    for places in rand:
        columns = []
        for c in range(len(places) // 2):
            low = source[places[2 * c], :, c * 128 : (c + 1) * 128]
            high = source[places[2 * c + 1], :, c * 128 : (c + 1) * 128]
            columns.append(jnp.where(low_half, low, high))
        parts.append(jnp.concatenate(columns, axis=1))
    return jnp.concatenate(parts, axis=0)


def mask_scores(scores, block, blocks, block_len):
    first = jnp.where(block > 0, scores[:block_len], masked_score)
    last = jnp.where(block < blocks - 1, scores[2 * block_len : 3 * block_len], masked_score)
    return jnp.concatenate([first, scores[block_len : 2 * block_len], last, scores[3 * block_len :]], axis=0)


def across(left, right):
    return lax.dot_general(left, right, (((1,), (1,)), ((), ())), preferred_element_type=jnp.float32)


def down(left, right):
    return lax.dot_general(left, right, (((0,), (0,)), ((), ())), preferred_element_type=jnp.float32)


def load_halves(target, own, other, half_blocks, block_len):
    lanes = own.shape[-1]
    target[0:half_blocks] = own[...].reshape(half_blocks, block_len, lanes)
    target[half_blocks:] = other[...].reshape(half_blocks, block_len, lanes)


def attend_kernel(sizes, blocks, head_dim, table, q_ref, k_own, k_other, v_own, v_other, o_ref, lse_ref, k_all, v_all):
    heads, picks, rand_size, half_blocks = sizes
    block_len = k_all.shape[1]
    lanes = q_ref.shape[1]
    group = pl.program_id(0)
    load_halves(k_all, k_own, k_other, half_blocks, block_len)
    load_halves(v_all, v_own, v_other, half_blocks, block_len)
    low_half = lax.broadcasted_iota(jnp.int32, (block_len, 128), 1) < head_dim
    masks = head_masks(lanes, head_dim, jnp.bfloat16)
    masks_f = head_masks(lanes, head_dim, jnp.float32)
    glob = [table[rand_size], table[rand_size + 1]]

    def one(slot, carry):
        block, near, rand = block_places(table, slot, group, sizes)
        rows = pl.ds(pl.multiple_of(slot * block_len, block_len), block_len)
        queries = spread_heads(q_ref[rows, :], masks)
        keys = key_rows(k_all, near, glob, rand, low_half)
        scores = mask_scores(across(keys, queries), block, blocks, block_len)
        top = jnp.max(scores, axis=0, keepdims=True)
        weights = jnp.exp(scores - top)
        total = jnp.sum(weights, axis=0, keepdims=True)
        probs = (weights * (1.0 / total)).astype(jnp.bfloat16)
        values = key_rows(v_all, near, glob, rand, low_half)
        o_ref[rows, :] = pick_heads(down(probs, values), masks_f, block_len).astype(jnp.bfloat16)
        lse_ref[0, pl.ds(slot, 1), :] = top + jnp.log(total)
        return carry

    lax.fori_loop(0, half_blocks, one, 0, unroll=min(8, half_blocks))


def attend_back_kernel(
    sizes, blocks, head_dim, scale, group,
    table, q_ref, k_own, k_other, v_own, v_other, go_ref, lse_ref, *refs,
):
    dq_ref, own_ref, other_ref, k_all, v_all, dk_all, dv_all, dk_glob, dv_glob = refs[-9:]
    heads, picks, rand_size, half_blocks = sizes
    block_len = k_all.shape[1]
    lanes = q_ref.shape[1]
    f32 = jnp.float32
    load_halves(k_all, k_own, k_other, half_blocks, block_len)
    load_halves(v_all, v_own, v_other, half_blocks, block_len)
    dk_all[...] = jnp.zeros_like(dk_all)
    dv_all[...] = jnp.zeros_like(dv_all)
    dk_glob[...] = jnp.zeros_like(dk_glob)
    dv_glob[...] = jnp.zeros_like(dv_glob)
    low_half = lax.broadcasted_iota(jnp.int32, (block_len, 128), 1) < head_dim
    masks = head_masks(lanes, head_dim, jnp.bfloat16)
    masks_f = head_masks(lanes, head_dim, f32)
    glob = [table[rand_size], table[rand_size + 1]]

    def add_back(grads, near, rand, into, into_glob):
        for n in range(3):
            into[near[n]] += grads[n * block_len : (n + 1) * block_len]
        for n in range(2):
            into_glob[n] += grads[(3 + n) * block_len : (4 + n) * block_len]
        for r in range(picks):
            part = grads[(5 + r) * block_len : (6 + r) * block_len]
            for c in range(lanes // 128):
                cell = part[:, c * 128 : (c + 1) * 128]
                columns = pl.ds(c * 128, 128)
                into[rand[r][2 * c], :, columns] += jnp.where(low_half, cell, 0.0)
                into[rand[r][2 * c + 1], :, columns] += jnp.where(low_half, 0.0, cell)

    def one(slot, carry):
        block, near, rand = block_places(table, slot, group, sizes)
        rows = pl.ds(pl.multiple_of(slot * block_len, block_len), block_len)
        queries = spread_heads(q_ref[rows, :], masks)
        grads_out = spread_heads(go_ref[rows, :], masks)
        keys = key_rows(k_all, near, glob, rand, low_half)
        values = key_rows(v_all, near, glob, rand, low_half)
        scores = mask_scores(across(keys, queries), block, blocks, block_len)
        probs = jnp.exp(scores - lse_ref[0, pl.ds(slot, 1), :])
        grad_probs = across(values, grads_out)
        row_dot = jnp.sum(probs * grad_probs, axis=0, keepdims=True)
        grad_scores = (probs * (grad_probs - row_dot)).astype(jnp.bfloat16)
        add_back(jnp.dot(probs.astype(jnp.bfloat16), grads_out, preferred_element_type=f32), near, rand, dv_all, dv_glob)
        add_back(jnp.dot(grad_scores, queries, preferred_element_type=f32), near, rand, dk_all, dk_glob)
        dq_ref[rows, :] = (pick_heads(down(grad_scores, keys), masks_f, block_len) * scale).astype(jnp.bfloat16)
        return carry

    lax.fori_loop(0, half_blocks, one, 0, unroll=min(8, half_blocks))
    for n in range(2):
        dk_all[glob[n]] += dk_glob[n]
        dv_all[glob[n]] += dv_glob[n]
    for target, start in ((own_ref, 0), (other_ref, half_blocks)):
        for n, source in enumerate((dk_all, dv_all)):
            cells = source[start : start + half_blocks].astype(jnp.bfloat16)
            target[:, n * lanes : (n + 1) * lanes] = cells.reshape(half_blocks * block_len, lanes)


def norm_parts(values):
    average = jnp.mean(values, axis=-1, keepdims=True)
    centred = values - average
    rstd = lax.rsqrt(jnp.mean(centred * centred, axis=-1, keepdims=True) + epsilon)
    return centred * rstd, rstd


def norm_back(grad, normal, rstd, gain):
    scaled = grad * gain
    first = jnp.mean(scaled, axis=-1, keepdims=True)
    second = jnp.mean(scaled * normal, axis=-1, keepdims=True)
    return rstd * (scaled - first - normal * second)


def normal_parts(values):
    cdf = 0.5 + 0.5 * lax.erf(values * 0.5**0.5)
    return cdf, values * jnp.exp(-0.5 * values * values) * 0.3989422804014327


def column_sum(values):
    return jnp.sum(values, axis=0, keepdims=True)


MESH = pl.DeviceIdType.MESH


def tile_order(number):
    return jnp.where(number == 0, 2, jnp.where(number == 2, 3, jnp.where(number == 3, 0, number)))


def position():
    win, blk = lax.axis_index("win"), lax.axis_index("blk")
    return win, blk, win % 2, blk // 2, blk % 2


def owner_of(tile, layers):
    win, blk, core, layer, side = position()
    return (win // 2) * 2 + side, ((layer + layers - tile) % layers) * 2 + core


def greet_owners(layers, peers):
    barrier = pltpu.get_barrier_semaphore()
    others = len(peers)
    for peer in peers:
        pl.semaphore_signal(barrier, inc=1, device_id=peer, device_id_type=MESH)
    _, _, core, _, side = position()
    for tile in range(1, layers):
        pl.semaphore_signal(barrier, inc=1, device_id=owner_of(tile, layers), device_id_type=MESH)

    @pl.when(side != core)
    def _():
        pl.semaphore_signal(barrier, inc=1, device_id=owner_of(0, layers), device_id_type=MESH)
        pl.semaphore_wait(barrier, layers + others)

    @pl.when(side == core)
    def _():
        pl.semaphore_wait(barrier, layers - 1 + others)


def return_tile(tile, source, target, send_sem, recv_sems, start):
    _, _, core, layer, side = position()
    layers = target.shape[0]
    stays = (tile == 0) & (side == core)

    @pl.when(stays)
    def _():
        move = pltpu.make_async_copy(source, target.at[layer], recv_sems.at[tile])
        move.start() if start else move.wait()

    @pl.when(jnp.logical_not(stays))
    def _():
        move = pltpu.make_async_remote_copy(
            src_ref=source, dst_ref=target.at[layer], send_sem=send_sem, recv_sem=recv_sems.at[tile],
            device_id=owner_of(tile, layers), device_id_type=MESH,
        )
        move.start() if start else move.wait()


def arrival_order(number):
    return jnp.where(number == 2, 3, jnp.where(number == 3, 2, number))


def front_kernel(
    scale, tokens, gain, shift, weight, bias,
    rows_ref, q_ref, kv_ref, other_ref, ready_ref,
    held, kv_rows, send_sems, recv_sems, kv_sems, kv_send, kv_recv, row_sems,
):
    f32, bf16 = jnp.float32, jnp.bfloat16
    step, steps = pl.program_id(0), pl.num_programs(0)
    length, width = held.shape[1:]
    win, blk, core, layer, side = position()
    layers = held.shape[0]
    peer = (win + 1 - 2 * core, blk)

    def token_move(tile, start):
        goal = (layer + tile) % layers

        def local():
            return pltpu.make_async_copy(tokens.at[goal], held.at[tile], recv_sems.at[tile])

        def far():
            return pltpu.make_async_remote_copy(
                src_ref=tokens.at[goal], dst_ref=held.at[tile], send_sem=send_sems.at[tile], recv_sem=recv_sems.at[tile],
                device_id=((win // 2) * 2 + side, goal * 2 + core), device_id_type=MESH,
            )

        stays = (tile == 0) & (side == core)

        @pl.when(stays)
        def _():
            local().start() if start else local().wait()

        @pl.when(jnp.logical_not(stays))
        def _():
            far().start() if start else far().wait()

    def rows_of(tile):
        return pl.ds(pl.multiple_of(tile * length, length), length)

    def kv_moves(number):
        tile = arrival_order(number)
        return [
            pltpu.make_async_copy(kv_rows.at[number], kv_ref.at[rows_of(tile)], kv_sems.at[number]),
            pltpu.make_async_copy(held.at[tile], rows_ref.at[rows_of(tile)], row_sems.at[number]),
            pltpu.make_async_remote_copy(
                src_ref=kv_rows.at[number], dst_ref=other_ref.at[rows_of(tile)], send_sem=kv_send.at[number], recv_sem=kv_recv.at[number],
                device_id=peer, device_id_type=MESH,
            ),
        ]

    @pl.when(step == 0)
    def _():
        greet_owners(layers, [peer])
        for n in range(4):
            token_move(arrival_order(n), True)
        ready_ref[...] = jnp.zeros_like(ready_ref)

    tile = arrival_order(step)
    token_move(tile, False)
    normal, _ = norm_parts(held[tile].astype(f32))
    normed = (normal * gain[...] + shift[...]).astype(bf16)

    def part(n):
        return jnp.dot(normed, weight[:, n * width : (n + 1) * width], preferred_element_type=f32)

    kv_rows[step, :, :width] = part(1).astype(bf16)
    kv_rows[step, :, width:] = (part(2) + bias[1:2]).astype(bf16)
    for move in kv_moves(step):
        move.start()
    q_ref[...] = (part(0) + bias[0:1]).astype(bf16) * jnp.asarray(scale, bf16)

    @pl.when(step == steps - 1)
    def _():
        for n in range(4):
            for move in kv_moves(n):
                move.wait()


def ffn_forward_kernel(
    chunk,
    rows_ref, att_ref, w_out, b_out, gain, shift, w_up, b_up, w_down, b_down,
    out_ref, normal_ref, second_ref, att_turned_ref, rstd_ref, active_ref, slope_ref,
):
    f32, bf16 = jnp.float32, jnp.bfloat16
    wide = w_up.shape[1]
    att = att_ref[...]
    residual = rows_ref[...].astype(f32) + (jnp.dot(att, w_out[...], preferred_element_type=f32) + b_out[...])
    normal, rstd = norm_parts(residual)
    second = (normal * gain[...] + shift[...]).astype(bf16)
    normal_ref[...] = normal.astype(bf16)
    second_ref[...] = second.T
    att_turned_ref[...] = att.T
    rstd_ref[...] = jnp.broadcast_to(rstd, rstd_ref.shape)

    def raise_part(first):
        part = slice(first, first + chunk)
        return jnp.dot(second, w_up[:, part], preferred_element_type=f32) + b_up[:, part]

    ahead = raise_part(0)
    for first in range(0, wide, chunk):
        inner = ahead
        if first + chunk < wide:
            ahead = raise_part(first + chunk)
        cdf, slope = normal_parts(inner)
        active_ref[:, first : first + chunk] = (inner * cdf).astype(bf16)
        slope_ref[:, first : first + chunk] = (cdf + slope).astype(bf16)
    total = residual + b_down[...] + jnp.dot(active_ref[...], w_down[...], preferred_element_type=f32)
    out_ref[...] = total.astype(bf16)


def ffn_back_kernel(
    chunks, shards, kept_tiles,
    scale, active_ref, slope_ref, w_up, w_down, second_t, normal_ref, rstd_ref, att_t, w_out, gain,
    cot_a, cot_b, cot_c, cot_d, output,
    resid_ref, go_ref, vec_ref, vec_up_ref, keep_ref, other_ref, out_ref,
    cot_rows, branch, branch_t, grad_inner, grad_second, stage_up, stage_down,
    cot_sems, ship_send, ship_recv, cell_send, cell_recv, done_sems,
):
    f32, bf16 = jnp.float32, jnp.bfloat16
    step = pl.program_id(0)
    slot = step % 2
    width = w_up.shape[0]
    tiles, length = cot_rows.shape[:2]
    part = width // shards
    half = width // 2
    size = keep_ref.shape[2]
    win, blk, core, _, _ = position()
    peer = (win + 1 - 2 * core, blk)

    def rows_of(n):
        return slice(n * length, (n + 1) * length)

    def ship(what):
        for n, tile in enumerate(kept_tiles):
            return_tile(tile, output.at[rows_of(tile)], out_ref, ship_send.at[n], ship_recv, what)

    def moves(c):
        cuts = []
        if c < chunks:
            base = 4 * c
            for first, count, piece, row in span_cuts(c * part, part, size):
                cuts.append((base + len(cuts), stage_up.at[c % 2, :, pl.ds(first, count)], slice(0, shards), piece, row, count))
            mine = slice(2 * c, 2 * c + 2)
            for first, count, piece, row in span_cuts(chunks * part, half, size):
                cuts.append((24 + base + len(cuts), stage_down.at[c % 2, :, pl.ds(first, count)], mine, piece, row, count))
        else:
            start = chunks * part + half
            for first, count, piece, row in span_cuts(start, 4 * size - start, size):
                cuts.append((20 + len(cuts), stage_up.at[0, :, pl.ds(first, count)], slice(0, shards), piece, row, count))
        return cuts

    def act(c, what):
        for number, source, mine, piece, row, count in moves(c):
            cell = (pl.ds(mine.start, mine.stop - mine.start), piece // 2, pl.ds(row, count))
            def far():
                return pltpu.make_async_remote_copy(
                    src_ref=source, dst_ref=other_ref.at[cell], send_sem=cell_send.at[number], recv_sem=cell_recv.at[number],
                    device_id=peer, device_id_type=MESH,
                )

            @pl.when(core == piece % 2)
            def _():
                if what == "receive":
                    far().wait_recv()
                else:
                    near = pltpu.make_async_copy(source, keep_ref.at[cell], cell_send.at[number])
                    near.start() if what == "start" else near.wait()

            if what != "receive":
                @pl.when(core != piece % 2)
                def _():
                    far().start() if what == "start" else far().wait_send()

    def cot_moves():
        return [
            pltpu.make_async_copy(source, cot_rows.at[n], cot_sems.at[n]) for n, source in enumerate((cot_a, cot_b, cot_c, cot_d))
        ]

    @pl.when(step == 0)
    def _():
        for move in cot_moves():
            move.start()
        greet_owners(tiles, [peer])
        ship(True)
        vec_ref[...] = jnp.zeros_like(vec_ref)
        for n, move in enumerate(cot_moves()):
            move.wait()
            upstream = cot_rows[n].astype(f32) * scale[0]
            vec_ref[3:4] += column_sum(upstream)
            branch[rows_of(n), :] = upstream.astype(bf16)
            branch_t[:, rows_of(n)] = upstream.astype(bf16).T
        grad_second[...] = jnp.zeros_like(grad_second)

    for c in range(2, chunks):
        @pl.when(step == c)
        def _():
            act(c - 2, "wait")

    full = jnp.dot(branch_t[...], active_ref[...], preferred_element_type=f32)
    for n in range(2):
        for k in range(2):
            stage_down[slot, n, :, k * half : (k + 1) * half] = full[k * half : (k + 1) * half, n * half : (n + 1) * half].astype(bf16)
    total = jnp.zeros((1, w_up.shape[1]), f32)
    for n in range(tiles):
        grad = across(branch[rows_of(n), :], w_down[...]) * slope_ref[rows_of(n), :].astype(f32)
        total = total + column_sum(grad)
        grad_inner[rows_of(n), :] = grad.astype(bf16)
        grad_second[rows_of(n), :] += across(grad_inner[rows_of(n), :], w_up[...])
    vec_up_ref[pl.ds(step, 1), :] = total
    full = jnp.dot(second_t[...], grad_inner[...], preferred_element_type=f32)
    for b in range(shards):
        stage_up[slot, b, 0:part] = full[b * part : (b + 1) * part].astype(bf16)
    for c in range(chunks):
        @pl.when(step == c)
        def _():
            act(c, "start")

    @pl.when(step == chunks - 1)
    def _():
        for n in range(tiles):
            upstream = cot_rows[n].astype(f32) * scale[0]
            grad = grad_second[rows_of(n), :]
            normal = normal_ref[rows_of(n), :].astype(f32)
            grad_resid = upstream + norm_back(grad, normal, rstd_ref[rows_of(n), 0:1], gain[...])
            grad_proj = grad_resid.astype(bf16)
            grad_inner[rows_of(n), :] = grad_proj
            branch[rows_of(n), :] = across(grad_proj, w_out[...]).astype(bf16)
            vec_ref[0:1] += column_sum(grad_resid)
            vec_ref[1:2] += column_sum(grad * normal)
            vec_ref[2:3] += column_sum(grad)
        results = [
            pltpu.make_async_copy(grad_inner, resid_ref, done_sems.at[0]),
            pltpu.make_async_copy(branch, go_ref, done_sems.at[1]),
        ]
        for move in results:
            move.start()
        full = jnp.dot(att_t[...], grad_inner[...], preferred_element_type=f32)
        act(chunks - 2, "wait")
        for b in range(shards):
            stage_up[0, b, 0:part] = full[b * part : (b + 1) * part].astype(bf16)
            stage_up[0, b, part:] = jnp.zeros((stage_up.shape[2] - part, width), bf16)
        act(chunks, "start")
        act(chunks - 1, "wait")
        act(chunks, "wait")
        for c in range(chunks + 1):
            act(c, "receive")
        for move in results:
            move.wait()
        ship(False)


def span_cuts(start, count, size):
    cuts, at = [], start
    while at < start + count:
        end = min(start + count, (at // size + 1) * size)
        cuts.append((at - start, end - at, at // size, at % size))
        at = end
    return cuts


def row_cuts(count, part, size):
    cuts = []
    for k in range(count):
        start = k * part
        while start < (k + 1) * part:
            end = min((k + 1) * part, (start // size + 1) * size)
            cuts.append((k, start - k * part, end - start, start // size, start % size))
            start = end
    return cuts


def add_into(target, got):
    target[...] = (target[...].astype(jnp.float32) + got[...].astype(jnp.float32)).astype(jnp.bfloat16)


def finish_kernel(groups, *refs):
    f32, bf16 = jnp.float32, jnp.bfloat16
    parts = refs[: 3 * groups - 1]
    (
        last_other, rows_ref, resid_ref, gain, shift, weight, vec_two, vec_up, early_a, early_b, early_c, early_d,
        tok_ref, late_ref, early_ref,
        joined, turned, vec, out_rows, cells, core_got, late_bufs, early_bufs, send_sems, recv_sems, load_sems, chain_send, chain_recv, keep_sems, last_rows, last_send, last_recv,
    ) = refs[3 * groups - 1 :]
    step, steps = pl.program_id(0), pl.num_programs(0)
    length, width = rows_ref.shape
    lanes = width // groups
    part = width // 8
    win, blk, core, layer, side = position()
    pair = win // 2
    core_peer = (win + 1 - 2 * core, blk)
    pair_peer = (win + 2 - 4 * pair, blk)
    side_peer = (win, blk + 1 - 2 * side)
    layer_peers = [(win, ((layer + n) % 4) * 2 + side) for n in (1, 2, 3)]

    def remote(source, target, number, peer):
        return pltpu.make_async_remote_copy(
            src_ref=source, dst_ref=target, send_sem=chain_send.at[number], recv_sem=chain_recv.at[number],
            device_id=peer, device_id_type=MESH,
        )

    early_got, early_final = early_bufs

    def loads():
        return [
            pltpu.make_async_copy(source, early_got.at[n], load_sems.at[n])
            for n, source in enumerate((early_a, early_b, early_c, early_d))
        ]

    def second_step(state, got, base):
        return [
            remote(state.at[0, :, 1 - pair], got.at[0], base, pair_peer),
            remote(state.at[1, :, 1 - side], got.at[1], base + 1, side_peer),
        ]

    def add_second(state, got, mid):
        for z in range(2):
            mid[0, z] = (state[0, z, pair].astype(f32) + got[0, z].astype(f32)).astype(bf16)
            mid[1, z] = (state[1, z, side].astype(f32) + got[1, z].astype(f32)).astype(bf16)

    def layer_step(mid, got, base):
        moves = []
        for n in range(3):
            other = (layer + n + 1) % 4
            moves.append(remote(mid.at[other // 2, other % 2], got.at[n], base + n, layer_peers[n]))
        return moves

    def sum_into(final, parts):
        total = parts[0].astype(f32)
        for one in parts[1:]:
            total = total + one.astype(f32)
        final[...] = total.astype(bf16)

    def share(final, target, base):
        return [
            remote(final, target.at[win], base, core_peer),
            remote(final, target.at[win], base + 1, pair_peer),
        ]

    def pass_on(target, base):
        return [remote(target.at[win + 2 - 4 * pair], target.at[win + 2 - 4 * pair], base, core_peer)]

    def start(moves):
        for move in moves:
            move.start()

    def wait(moves):
        for move in moves:
            move.wait()

    def last_move(number):
        first = pl.multiple_of(tile_order(number) * length, length)
        return pltpu.make_async_remote_copy(
            src_ref=last_other.at[pl.ds(first, length)], dst_ref=last_rows.at[number], send_sem=last_send.at[number],
            recv_sem=last_recv.at[number], device_id=core_peer, device_id_type=MESH,
        )

    late_first, late_second, late_mid, late_got, late_final = late_bufs
    early_base, late_base = 8, 0

    @pl.when(step == 0)
    def _():
        start(loads())
        greet_owners(steps, [core_peer, pair_peer, side_peer] + layer_peers)
        for n in range(4):
            last_move(n).start()
        vec[...] = jnp.zeros_like(vec)

    tile = tile_order(step)
    rows = pl.ds(pl.multiple_of(tile * length, length), length)
    last_move(step).wait()
    for g in range(groups):
        dq, own = parts[3 * g : 3 * g + 2]
        other = parts[3 * g + 2] if g < groups - 1 else last_rows.at[step]
        columns = slice(g * lanes, (g + 1) * lanes)
        joined[rows, columns] = dq[...]
        both = (own[...].astype(f32) + other[...].astype(f32)).astype(bf16)
        joined[rows, width + g * lanes : width + (g + 1) * lanes] = both[:, :lanes]
        joined[rows, 2 * width + g * lanes : 2 * width + (g + 1) * lanes] = both[:, lanes:]
        vec[0:1, columns] += column_sum(dq[...].astype(f32))
        vec[1:2, columns] += column_sum(both[:, lanes:].astype(f32))
    grad = across(joined[rows, :], weight[...])
    normal, rstd = norm_parts(rows_ref[...].astype(f32))
    turned[tile] = (normal * gain[...] + shift[...]).astype(bf16).T
    vec[2:3] += column_sum(grad * normal)
    vec[3:4] += column_sum(grad)
    out_rows[step] = (resid_ref[...].astype(f32) + norm_back(grad, normal, rstd, gain[...])).astype(bf16)
    return_tile(tile, out_rows.at[step], tok_ref, send_sems.at[step], recv_sems, True)

    @pl.when(step == 0)
    def _():
        wait(loads())
        sum_into(early_final, [early_got[n] for n in range(4)])
        start(share(early_final, early_ref, early_base))
        pltpu.make_async_copy(early_final, early_ref.at[win], keep_sems.at[0]).start()

    @pl.when(step == steps - 1)
    def _():
        size = cells.shape[5]
        cuts = row_cuts(3, part, size)
        for k in range(3):
            full = jnp.dot(turned[0], joined[0:length, k * width : (k + 1) * width], preferred_element_type=f32)
            for n in range(1, 4):
                full = full + jnp.dot(
                    turned[n], joined[n * length : (n + 1) * length, k * width : (k + 1) * width], preferred_element_type=f32
                )
            for b in range(8):
                for which, first, count, piece, row in cuts:
                    if which == k:
                        cells[piece % 2, b // 4, b // 2 % 2, b % 2, piece // 2, row : row + count] = full[
                            b * part + first : b * part + first + count
                        ].astype(bf16)
        tail = jnp.concatenate(
            [vec[...], vec_two[...], vec_up[...]]
            + [jnp.zeros((4 * size - 3 * part - 12, width), f32)],
            axis=0,
        ).astype(bf16)
        for b in range(8):
            cells[1, b // 4, b // 2 % 2, b % 2, 1, 3 * part - 3 * size :] = tail
        exchange = [remote(cells.at[1 - core], core_got, late_base, core_peer)]
        start(exchange)
        wait(share(early_final, early_ref, early_base))
        start(pass_on(early_ref, early_base + 2))
        wait(exchange)
        mine = cells.at[core]
        for b in range(8):
            for x in range(2):
                add_into(mine.at[b // 4, b // 2 % 2, b % 2, x], core_got.at[b // 4, b // 2 % 2, b % 2, x])
        first = [
            remote(mine.at[0, :, 1 - side], late_first.at[0], late_base + 1, side_peer),
            remote(mine.at[1, :, :, 1 - pair], late_first.at[1], late_base + 2, pair_peer),
        ]
        start(first)
        wait(first)
        state = core_got.at[0]
        for z in range(2):
            for n in range(2):
                state[0, z, n] = (mine[0, z, side, n].astype(f32) + late_first[0, z, n].astype(f32)).astype(bf16)
                state[1, z, n] = (mine[1, z, n, pair].astype(f32) + late_first[1, z, n].astype(f32)).astype(bf16)
        start(second_step(state, late_second, late_base + 3))
        wait(second_step(state, late_second, late_base + 3))
        add_second(state, late_second, late_mid)
        across_layers = layer_step(late_mid, late_got, late_base + 5)
        start(across_layers)
        wait(across_layers)
        sum_into(late_final, [late_mid[layer // 2, layer % 2]] + [late_got[n] for n in range(3)])
        start(share(late_final, late_ref, early_base + 3))
        keep_late = pltpu.make_async_copy(late_final, late_ref.at[win], keep_sems.at[1])
        keep_late.start()
        wait(share(late_final, late_ref, early_base + 3))
        start(pass_on(late_ref, early_base + 5))
        wait(pass_on(early_ref, early_base + 2))
        wait(pass_on(late_ref, early_base + 5))
        pltpu.make_async_copy(early_final, early_ref.at[win], keep_sems.at[0]).wait()
        keep_late.wait()
        for n in range(4):
            return_tile(tile_order(n), out_rows.at[n], tok_ref, send_sems.at[n], recv_sems, False)


def first_send_kernel(place, keep_left, other_left, keep_right, other_right, left_ref, right_ref):
    for keep, other, target in ((keep_left, other_left, left_ref), (keep_right, other_right, right_ref)):
        target[...] = (keep[...].astype(jnp.float32) + other[...].astype(jnp.float32)).astype(jnp.bfloat16).reshape(target.shape)


def sum_low(target, refs):
    total = refs[0][...].astype(jnp.float32)
    for ref in refs[1:]:
        total = total + ref[...].astype(jnp.float32)
    target[...] = total.astype(jnp.bfloat16).reshape(target.shape)


def second_send_kernel(place, *refs):
    keep, left, right = refs[12:]
    for n, target in enumerate((keep.at[0], keep.at[1], left, right)):
        sum_low(target, refs[3 * n : 3 * n + 3])


def third_send_kernel(place, *refs):
    for n in range(4):
        keep, left, right = refs[3 * n : 3 * n + 3]
        in_left = (place[3] + n) % 4 < 2
        got = jnp.where(in_left, left[...].astype(jnp.float32), right[...].astype(jnp.float32))
        target = refs[12 + n]
        target[...] = (keep[...].reshape(target.shape).astype(jnp.float32) + got.reshape(target.shape)).astype(jnp.bfloat16)


def unpack_kernel(early, late, qkv_ref, out_ref, up_ref, down_ref):
    f32 = jnp.float32
    part, width = out_ref.shape
    count = up_ref.shape[1] // width
    half = width // 2

    def cells(source, first, rows):
        size = source.shape[1]
        parts = []
        while rows > 0:
            take = min(rows, size - first % size)
            parts.append(source[first // size, first % size : first % size + take])
            first, rows = first + take, rows - take
        return (parts[0] if len(parts) == 1 else jnp.concatenate(parts, axis=0)).astype(f32)

    for k in range(3):
        qkv_ref[:, k * width : (k + 1) * width] = cells(late, k * part, part)
    for k in range(count):
        up_ref[:, k * width : (k + 1) * width] = cells(early, k * part, part)
    turned = cells(early, count * part, half)
    down_ref[:, :half] = turned[:, :half].T
    down_ref[:, half:] = turned[:, half:].T
    out_ref[...] = cells(early, count * part + half, part)


def general_body(
    tokens,
    cotangent,
    w_qkv,
    b_q,
    b_v,
    w_out,
    b_out,
    gain_one,
    shift_one,
    gain_two,
    shift_two,
    w_up,
    b_up,
    w_down,
    b_down,
    rand_owner,
    rand_sub,
    global_ids,
    species,
):
    blk_count = lax.axis_size("blk")
    blk_pos = lax.axis_index("blk")
    win_pos = lax.axis_index("win")
    windows, length, model_width = tokens.shape
    blocks = rand_owner.shape[1]
    heads = rand_owner.shape[2]
    picks = rand_owner.shape[3]
    glob_count = global_ids.shape[1]
    own_blocks = blocks // blk_count
    block_len = length // own_blocks
    head_dim = model_width // heads
    pair_width = 2 * head_dim
    all_rows = windows * length
    key_count = 3 + glob_count + picks
    per_device = own_blocks * heads * picks
    slot_cap = max(2, 2 * per_device // blk_count)
    score_scale = head_dim ** (-0.5)
    f32 = jnp.float32
    bf16 = jnp.bfloat16
    tokens_f = tokens.reshape(all_rows, model_width).astype(f32)
    normed_f, norm_one_pull = jax.vjp(layer_norm, tokens_f, gain_one, shift_one)
    normed = normed_f.astype(bf16)
    joined = jnp.dot(normed, w_qkv, preferred_element_type=f32)
    query_vals = (joined[:, :model_width] + b_q).astype(bf16)
    key_vals = joined[:, model_width : 2 * model_width].astype(bf16)
    value_vals = (joined[:, 2 * model_width :] + b_v).astype(bf16)

    def to_heads(tensor):
        return tensor.reshape(windows, own_blocks, block_len, heads, head_dim).transpose(
            0, 1, 3, 2, 4
        )

    def from_heads(tensor):
        return tensor.transpose(0, 1, 3, 2, 4).reshape(all_rows, model_width)

    query_heads = to_heads(query_vals)
    local_pairs = jnp.concatenate([to_heads(key_vals), to_heads(value_vals)], axis=-1)
    rimmed = padded(local_pairs, (("blk", 1),), 1)
    block_ids = blk_pos * own_blocks + jnp.arange(own_blocks, dtype=jnp.int32)
    owned_glob = (global_ids[:, :, None] == block_ids[None, None, :]).astype(bf16)
    glob_terms = jnp.einsum("wgb,wbhsc->wghsc", owned_glob, local_pairs, preferred_element_type=f32)
    glob_pairs = lax.psum(glob_terms.astype(jnp.bfloat16), "blk").astype(jnp.float32).astype(bf16)
    owner_rows = rand_owner.reshape(windows, blk_count, per_device)
    sub_rows = rand_sub.reshape(windows, blk_count, per_device)
    owner_hits = (owner_rows[..., None] == jnp.arange(blk_count, dtype=jnp.int32)).astype(jnp.int32)
    slot_rows = jnp.sum(owner_hits * (jnp.cumsum(owner_hits, axis=2) - 1), axis=-1)
    my_owner = lax.dynamic_index_in_dim(owner_rows, blk_pos, 1, keepdims=False)
    my_slot = lax.dynamic_index_in_dim(slot_rows, blk_pos, 1, keepdims=False)
    fetch_index = my_owner * slot_cap + my_slot
    head_of_row = jnp.arange(per_device, dtype=jnp.int32) // picks % heads
    source_rows = sub_rows * heads + head_of_row[None, None, :]
    requester = jnp.arange(blk_count, dtype=jnp.int32)[None, :, None]
    target_rows = jnp.where(
        owner_rows == blk_pos, requester * slot_cap + slot_rows, blk_count * slot_cap
    )
    send_table = jnp.full((windows, blk_count * slot_cap + 1), own_blocks * heads, jnp.int32)
    send_table = jax.vmap(set_rows)(
        send_table, target_rows.reshape(windows, -1), source_rows.reshape(windows, -1)
    )[:, : blk_count * slot_cap]
    flat_pairs = jnp.concatenate(
        [
            local_pairs.reshape(windows, own_blocks * heads, block_len, pair_width),
            jnp.zeros((windows, 1, block_len, pair_width), bf16),
        ],
        axis=1,
    )
    outgoing = jax.vmap(take_rows)(flat_pairs, send_table).reshape(
        windows, blk_count, slot_cap, block_len, pair_width
    )
    incoming = lax.all_to_all(outgoing, "blk", split_axis=1, concat_axis=1, tiled=True).reshape(
        windows, blk_count * slot_cap, block_len, pair_width
    )
    rand_pairs = jax.vmap(take_rows)(incoming, fetch_index).reshape(
        windows, own_blocks, heads, picks, block_len, pair_width
    )
    near_pairs = jnp.stack(
        [rimmed[:, 0:own_blocks], rimmed[:, 1 : own_blocks + 1], rimmed[:, 2 : own_blocks + 2]],
        axis=3,
    )
    far_pairs = jnp.broadcast_to(
        glob_pairs.transpose(0, 2, 1, 3, 4)[:, None],
        (windows, own_blocks, heads, glob_count, block_len, pair_width),
    )
    gathered_keys = jnp.concatenate([near_pairs, far_pairs, rand_pairs], axis=3).reshape(
        windows, own_blocks, heads, key_count * block_len, pair_width
    )
    set_keys = gathered_keys[..., :head_dim]
    set_values = gathered_keys[..., head_dim:]
    block_flags = jnp.concatenate(
        [
            (block_ids > 0)[:, None],
            jnp.ones((own_blocks, 1), jnp.bool_),
            (block_ids < blocks - 1)[:, None],
            jnp.ones((own_blocks, glob_count + picks), jnp.bool_),
        ],
        axis=1,
    )
    key_valid = jnp.repeat(block_flags, block_len, axis=1)[None, :, None, None, :]

    def score_block():
        raw_scores = (
            jnp.einsum("wbhqe,wbhke->wbhqk", query_heads, set_keys, preferred_element_type=f32)
            * score_scale
        )
        return jnp.where(key_valid, raw_scores, masked_score)

    score_matrix = score_block()
    top_score = jnp.max(score_matrix, axis=-1, keepdims=True)
    log_total = top_score + jnp.log(
        jnp.sum(jnp.exp(score_matrix - top_score), axis=-1, keepdims=True)
    )
    probs_low = jnp.exp(score_matrix - log_total).astype(bf16)
    attended = jnp.einsum(
        "wbhqk,wbhke->wbhqe", probs_low, set_values, preferred_element_type=f32
    ).astype(bf16)
    merged = from_heads(attended)
    residual = tokens_f + (jnp.dot(merged, w_out, preferred_element_type=f32) + b_out)
    second_f, norm_two_pull = jax.vjp(layer_norm, residual, gain_two, shift_two)
    second = second_f.astype(bf16)
    inner_f = jnp.dot(second, w_up, preferred_element_type=f32) + b_up
    active_f, gelu_pull = jax.vjp(partial(jax.nn.gelu, approximate=False), inner_f)
    active = active_f.astype(bf16)
    output = residual + (jnp.dot(active, w_down, preferred_element_type=f32) + b_down)
    species_count = jnp.sum(
        (species[:, None] == jnp.arange(SPECIES, dtype=jnp.int32)[None, :]).astype(f32), axis=0
    )
    my_species = lax.dynamic_slice_in_dim(species, win_pos * windows, windows)
    own_count = jnp.sum(
        (my_species[:, None] == jnp.arange(SPECIES, dtype=jnp.int32)[None, :]).astype(f32)
        * species_count[None, :],
        axis=1,
    )
    window_scale = jnp.sqrt(species.shape[0] / (SPECIES * own_count))
    upstream = (cotangent.astype(f32) * window_scale[:, None, None]).reshape(all_rows, model_width)
    grad_branch = upstream.astype(bf16)
    grad_w_down = jnp.einsum("tf,td->fd", active, grad_branch, preferred_element_type=f32)
    grad_b_down = jnp.sum(grad_branch, axis=0, dtype=f32)
    grad_active = jnp.einsum("td,fd->tf", grad_branch, w_down, preferred_element_type=f32)
    grad_inner = gelu_pull(grad_active)[0].astype(bf16)
    grad_w_up = jnp.einsum("td,tf->df", second, grad_inner, preferred_element_type=f32)
    grad_b_up = jnp.sum(grad_inner, axis=0, dtype=f32)
    grad_second = jnp.einsum("tf,df->td", grad_inner, w_up, preferred_element_type=f32)
    grad_resid_norm, grad_gain_two, grad_shift_two = norm_two_pull(grad_second)
    grad_resid = upstream + grad_resid_norm
    grad_proj = grad_resid.astype(bf16)
    grad_w_out = jnp.einsum("ti,to->io", merged, grad_proj, preferred_element_type=f32)
    grad_b_out = jnp.sum(grad_proj, axis=0, dtype=f32)
    grad_attended = to_heads(
        jnp.einsum("to,io->ti", grad_proj, w_out, preferred_element_type=f32).astype(bf16)
    )
    probs_full = jnp.exp(score_block() - log_total)
    grad_probs = jnp.einsum(
        "wbhqe,wbhke->wbhqk", grad_attended, set_values, preferred_element_type=f32
    )
    grad_set_values = jnp.einsum(
        "wbhqk,wbhqe->wbhke", probs_full.astype(bf16), grad_attended, preferred_element_type=f32
    )
    row_dot = jnp.sum(probs_full * grad_probs, axis=-1, keepdims=True)
    grad_scores = (probs_full * (grad_probs - row_dot)).astype(bf16)
    grad_query = (
        jnp.einsum("wbhqk,wbhke->wbhqe", grad_scores, set_keys, preferred_element_type=f32)
        * score_scale
    )
    grad_set_keys = (
        jnp.einsum("wbhqk,wbhqe->wbhke", grad_scores, query_heads, preferred_element_type=f32)
        * score_scale
    )
    grad_set = jnp.concatenate([grad_set_keys, grad_set_values], axis=-1).reshape(
        windows, own_blocks, heads, key_count, block_len, pair_width
    )
    extended = (
        jnp.pad(grad_set[:, :, :, 1], ((0, 0), (1, 1), (0, 0), (0, 0), (0, 0)))
        + jnp.pad(grad_set[:, :, :, 0], ((0, 0), (0, 2), (0, 0), (0, 0), (0, 0)))
        + jnp.pad(grad_set[:, :, :, 2], ((0, 0), (2, 0), (0, 0), (0, 0), (0, 0)))
    )
    edge_grads = jnp.concatenate([extended[:, :1], extended[:, own_blocks + 1 :]], axis=1)
    edge_back = padded(edge_grads.astype(jnp.bfloat16), (("blk", 1),), 1).astype(edge_grads.dtype)
    pair_grad = extended[:, 1 : own_blocks + 1]
    pair_grad = pair_grad.at[:, 0].add(edge_back[:, 0]).at[:, own_blocks - 1].add(edge_back[:, 3])
    glob_grad = jnp.sum(grad_set[:, :, :, 3 : 3 + glob_count], axis=1).transpose(0, 2, 1, 3, 4)
    glob_total = lax.psum(glob_grad.astype(jnp.bfloat16), "blk").astype(jnp.float32)
    pair_grad = pair_grad + jnp.einsum(
        "wgb,wghsc->wbhsc", owned_glob.astype(f32), glob_total, precision=lax.Precision.HIGHEST
    )
    rand_grad = grad_set[:, :, :, 3 + glob_count :].reshape(
        windows, per_device, block_len, pair_width
    )
    back_out = jax.vmap(add_rows)(
        jnp.zeros((windows, blk_count * slot_cap, block_len, pair_width), f32),
        fetch_index,
        rand_grad,
    )
    back_in = lax.all_to_all(
        back_out.reshape(windows, blk_count, slot_cap, block_len, pair_width).astype(jnp.bfloat16),
        "blk",
        split_axis=1,
        concat_axis=1,
        tiled=True,
    ).astype(jnp.float32)
    owner_sum = jax.vmap(add_rows)(
        jnp.zeros((windows, own_blocks * heads + 1, block_len, pair_width), f32),
        send_table,
        back_in.reshape(windows, blk_count * slot_cap, block_len, pair_width),
    )
    pair_grad = pair_grad + owner_sum[:, : own_blocks * heads].reshape(
        windows, own_blocks, heads, block_len, pair_width
    )
    grad_keys = from_heads(pair_grad[..., :head_dim].astype(bf16))
    grad_values = from_heads(pair_grad[..., head_dim:].astype(bf16))
    grad_joined = jnp.concatenate(
        [from_heads(grad_query.astype(bf16)), grad_keys, grad_values], axis=1
    )
    grad_w_qkv = jnp.einsum("td,tc->dc", normed, grad_joined, preferred_element_type=f32)
    grad_b_q = jnp.sum(grad_joined[:, :model_width], axis=0, dtype=f32)
    grad_b_v = jnp.sum(grad_joined[:, 2 * model_width :], axis=0, dtype=f32)
    grad_normed = jnp.einsum("tc,dc->td", grad_joined, w_qkv, preferred_element_type=f32)
    grad_tok_norm, grad_gain_one, grad_shift_one = norm_one_pull(grad_normed)
    grad_tokens = (grad_resid + grad_tok_norm).astype(bf16).reshape(windows, length, model_width)
    local_grads = (
        grad_w_qkv,
        grad_b_q,
        grad_b_v,
        grad_w_out,
        grad_b_out,
        grad_gain_one,
        grad_shift_one,
        grad_gain_two,
        grad_shift_two,
        grad_w_up,
        grad_b_up,
        grad_w_down,
        grad_b_down,
    )
    packed_grads = jnp.concatenate(
        [grad_item.reshape(blk_count, -1) for grad_item in local_grads], axis=1
    )
    total_cols = packed_grads.shape[1]
    win_count = lax.axis_size("win")
    pad_cols = -total_cols % win_count
    shard_sum = lax.psum_scatter(
        packed_grads.astype(jnp.bfloat16), "blk", scatter_dimension=0, tiled=True
    ).astype(jnp.float32)
    split_shard = jnp.pad(shard_sum, ((0, 0), (0, pad_cols))).reshape(win_count, -1)
    group_piece = lax.psum_scatter(
        split_shard.astype(jnp.bfloat16), "win", scatter_dimension=0, tiled=True
    ).astype(jnp.float32)
    summed = (
        lax.all_gather(group_piece.astype(jnp.bfloat16), "win", axis=0, tiled=True)
        .astype(group_piece.dtype)
        .reshape(1, -1)[:, :total_cols]
    )
    shards = []
    offset = 0
    for grad_item in local_grads:
        entry_count = grad_item.size // blk_count
        shards.append(
            summed[0, offset : offset + entry_count].reshape(
                (grad_item.shape[0] // blk_count,) + grad_item.shape[1:]
            )
        )
        offset = offset + entry_count
    out_tokens = output.astype(bf16).reshape(windows, length, model_width)
    return (
        out_tokens,
        grad_tokens,
        shards[0],
        shards[1],
        shards[2],
        shards[3],
        shards[4],
        shards[5],
        shards[6],
        shards[7],
        shards[8],
        shards[9],
        shards[10],
        shards[11],
        shards[12],
    )


def layer_step(*arguments):
    windows = arguments[0].shape[0]
    paired = lax.axis_size("blk") == 2 * windows and lax.axis_size("win") == 4 and windows == 4
    return (paired_body if paired else general_body)(*arguments)


def paired_body(
    tokens,
    cotangent,
    w_qkv,
    b_q,
    b_v,
    w_out,
    b_out,
    gain_one,
    shift_one,
    gain_two,
    shift_two,
    w_up,
    b_up,
    w_down,
    b_down,
    rand_owner,
    rand_sub,
    global_ids,
    species,
):
    f32 = jnp.float32
    bf16 = jnp.bfloat16
    win_count = lax.axis_size("win")
    blk_count = lax.axis_size("blk")
    win_pos = lax.axis_index("win")
    blk_pos = lax.axis_index("blk")
    layers, length, width = tokens.shape
    core, layer, side = win_pos % 2, blk_pos // 2, blk_pos % 2
    blocks, heads, picks = rand_owner.shape[1:]
    own_blocks = blocks // blk_count
    half_blocks = blocks // 2
    block_len = length // own_blocks
    head_dim = width // heads
    all_rows = layers * length
    lanes = HEADS_PER_GROUP * head_dim
    groups = heads // HEADS_PER_GROUP
    score_scale = head_dim ** (-0.5)

    def regroup(value, after):
        parts = []
        for step in range(layers):
            part = lax.dynamic_index_in_dim(value, (layer + step) % layers + after, 0, keepdims=False)
            parts.append(lax.ppermute(part, ("win", "blk"), regroup_pairs(win_count, layers, step)))
        return parts

    def takes(micros):
        return pl.CostEstimate(flops=micros * 1_000_000_000, bytes_accessed=micros * 1_000_000, transcendentals=0)


    rand_size = blocks * heads * picks
    named = jnp.concatenate(
        [
            lax.dynamic_index_in_dim((rand_owner * own_blocks + rand_sub).reshape(layers, rand_size), layer, 0, keepdims=False),
            lax.dynamic_index_in_dim(global_ids, layer, 0, keepdims=False),
        ]
    )
    named = jnp.where(side == core, named, swap(named, 1, 0))

    def place_of(block):
        owner = block // own_blocks
        half = jnp.where(owner % 2 == core, 0, half_blocks)
        return half + ((layer - owner // 2) % layers) * own_blocks + block % own_blocks

    slot = jnp.arange(half_blocks, dtype=jnp.int32)
    slot_block = (((layer - slot // own_blocks) % layers) * 2 + core) * own_blocks + slot % own_blocks
    table = jnp.concatenate(
        [
            place_of(named),
            slot_block,
            place_of(jnp.maximum(slot_block - 1, 0)),
            place_of(jnp.minimum(slot_block + 1, blocks - 1)),
        ]
    )
    sizes = (heads, picks, rand_size, half_blocks)

    tile = length

    def by_rows(columns):
        return pl.BlockSpec((tile, columns), lambda i: (i, 0))

    def by_tile(columns):
        return pl.BlockSpec((tile, columns), lambda i: (tile_order(i), 0))

    def whole(*shape, once=True):
        mode = pl.Buffered(1) if once else None
        return pl.BlockSpec(shape, lambda i: (0,) * len(shape), pipeline_mode=mode)

    scalars = pl.BlockSpec(memory_space=pltpu.SMEM)
    wide = w_up.shape[1]
    params = pltpu.CompilerParams(vmem_limit_bytes=60 << 20)
    row = lambda vector: vector.reshape(1, -1)
    def remote_params(number, mib):
        return pltpu.CompilerParams(vmem_limit_bytes=mib << 20, collective_id=number, has_side_effects=True)

    any_place = pl.BlockSpec(memory_space=pl.ANY)

    def keep(*shape):
        return pltpu.VMEM(shape, bf16)

    copies = pltpu.SemaphoreType.DMA((layers,))
    rows_in, query, key_value, key_value_other, ready = pl.pallas_call(
        partial(front_kernel, score_scale),
        grid=(layers,),
        in_specs=[any_place, whole(1, width), whole(1, width), whole(width, 3 * width), whole(2, width)],
        out_specs=[any_place, pl.BlockSpec((tile, width), lambda i: (arrival_order(i), 0)), any_place, any_place, whole(8, 128)],
        out_shape=[
            jax.ShapeDtypeStruct((all_rows, width), bf16),
            jax.ShapeDtypeStruct((all_rows, width), bf16),
            jax.ShapeDtypeStruct((all_rows, 2 * width), bf16),
            jax.ShapeDtypeStruct((all_rows, 2 * width), bf16),
            jax.ShapeDtypeStruct((8, 128), jnp.int32),
        ],
        scratch_shapes=[keep(layers, length, width), keep(layers, length, 2 * width)] + [copies] * 6,
        compiler_params=remote_params(1, 48),
        cost_estimate=takes(80),
        name="front",
    )(tokens, row(gain_one), row(shift_one), w_qkv, jnp.stack([b_q, b_v]))
    cot_in = regroup(cotangent, ready[0, 0])

    def lane_block(first):
        return pl.BlockSpec((all_rows, lanes), lambda g, t: (0, first + g))

    store = pltpu.VMEM((blocks, block_len, lanes), bf16)
    attended, log_total = pl.pallas_call(
        partial(attend_kernel, sizes, blocks, head_dim),
        grid_spec=pltpu.PrefetchScalarGridSpec(
            num_scalar_prefetch=1,
            grid=(groups,),
            in_specs=[lane_block(0), lane_block(0), lane_block(0), lane_block(groups), lane_block(groups)],
            out_specs=[lane_block(0), pl.BlockSpec((1, half_blocks, lanes), lambda g, t: (g, 0, 0))],
            scratch_shapes=[store, store],
        ),
        out_shape=[
            jax.ShapeDtypeStruct((all_rows, width), bf16),
            jax.ShapeDtypeStruct((groups, half_blocks, lanes), f32),
        ],
        compiler_params=pltpu.CompilerParams(vmem_limit_bytes=56 << 20),
        cost_estimate=takes(37),
        name="attend",
    )(table, query, key_value, key_value_other, key_value, key_value_other)

    species_count = jnp.sum(
        (species[:, None] == jnp.arange(SPECIES, dtype=jnp.int32)[None, :]).astype(f32), axis=0
    )
    my_window = ((win_pos // 2) * 2 + side) * layers + layer
    my_species = lax.dynamic_index_in_dim(species, my_window, 0, keepdims=False)
    own_count = jnp.sum(
        (my_species == jnp.arange(SPECIES, dtype=jnp.int32)).astype(f32) * species_count
    )
    window_scale = jnp.sqrt(species.shape[0] / (SPECIES * own_count))
    payload = 2 * wide // blk_count + width // blk_count
    payload += -payload % (16 * win_count)
    stays = jax.ShapeDtypeStruct((blk_count, win_count // 2, payload // win_count, width), bf16)
    output, normal, second_t, attended_t, rstd, active, slope = pl.pallas_call(
        partial(ffn_forward_kernel, 256),
        grid=(layers,),
        in_specs=[
            by_rows(width), by_rows(width), whole(width, width), whole(1, width), whole(1, width),
            whole(1, width), whole(width, wide), whole(1, wide), whole(wide, width), whole(1, width),
        ],
        out_specs=[
            by_rows(width), by_rows(width), pl.BlockSpec((width, length), lambda i: (0, i)), pl.BlockSpec((width, length), lambda i: (0, i)),
            by_rows(128), by_rows(wide), by_rows(wide),
        ],
        out_shape=[
            jax.ShapeDtypeStruct((all_rows, width), bf16),
            jax.ShapeDtypeStruct((all_rows, width), bf16),
            jax.ShapeDtypeStruct((width, all_rows), bf16),
            jax.ShapeDtypeStruct((width, all_rows), bf16),
            jax.ShapeDtypeStruct((all_rows, 128), f32),
            jax.ShapeDtypeStruct((all_rows, wide), bf16),
            jax.ShapeDtypeStruct((all_rows, wide), bf16),
        ],
        compiler_params=params,
        cost_estimate=takes(35),
        name="ffn_forward",
    )(rows_in, attended, w_out, row(b_out), row(gain_two), row(shift_two), w_up, row(b_up), w_down, row(b_down))

    chunks = wide // width

    grad_resid, grad_attended, vec_two, vec_up, early_keep, early_other, out_tokens = pl.pallas_call(
        partial(ffn_back_kernel, chunks, blk_count, (2, 1, 3, 0)),
        grid=(chunks,),
        in_specs=[
            scalars, pl.BlockSpec((all_rows, width), lambda i: (0, i)), pl.BlockSpec((all_rows, width), lambda i: (0, i)),
            pl.BlockSpec((width, width), lambda i: (0, i)), pl.BlockSpec((width, width), lambda i: (i, 0)),
            whole(width, all_rows), whole(all_rows, width), whole(all_rows, 128), whole(width, all_rows), whole(width, width), whole(1, width),
            *[any_place] * (layers + 1),
        ],
        out_specs=[any_place, any_place, whole(4, width), whole(chunks, width), any_place, any_place, any_place],
        out_shape=[
            jax.ShapeDtypeStruct((all_rows, width), bf16),
            jax.ShapeDtypeStruct((all_rows, width), bf16),
            jax.ShapeDtypeStruct((4, width), f32),
            jax.ShapeDtypeStruct((chunks, width), f32),
            stays,
            stays,
            jax.ShapeDtypeStruct((layers, length, width), bf16),
        ],
        scratch_shapes=[
            keep(layers, length, width),
            keep(all_rows, width),
            keep(width, all_rows),
            keep(all_rows, width),
            pltpu.VMEM((all_rows, width), f32),
            keep(2, blk_count, payload - chunks * width // blk_count - width // 2, width),
            keep(2, 2, width // 2, width),
            pltpu.SemaphoreType.DMA((layers,)),
            pltpu.SemaphoreType.DMA((layers,)),
            pltpu.SemaphoreType.DMA((layers,)),
            pltpu.SemaphoreType.DMA((48,)),
            pltpu.SemaphoreType.DMA((48,)),
            pltpu.SemaphoreType.DMA((2,)),
        ],
        compiler_params=remote_params(3, 63),
        cost_estimate=takes(60),
        name="ffn_back",
    )(
        window_scale.reshape(1), active, slope, w_up, w_down, second_t, normal, rstd, attended_t, w_out, row(gain_two), *cot_in, output,
    )
    pair = win_pos // 2
    early_rows = payload // win_count
    late_rows = 3 * width // blk_count + 32
    late_size = late_rows // win_count
    cell = (early_rows, width)
    early_keep = early_keep.reshape((2, 2, 2, 2) + cell)
    early_other = early_other.reshape((2, 2, 2, 2) + cell)
    place = jnp.stack([side, pair, side, layer])

    def picked(index):
        return pl.BlockSpec((1, 1, 1, 1) + cell, lambda z, n, p: index(z, n, p) + (0, 0))

    def listed(index):
        return pl.BlockSpec((1, 1) + cell, lambda z, n, p: index(z, n, p) + (0, 0))

    def cells_of(count):
        return [jax.ShapeDtypeStruct((2, 2) + cell, bf16)] * count

    def first_send():
        left = picked(lambda z, n, p: (0, z, 1 - p[0], n))
        right = picked(lambda z, n, p: (1, z, n, 1 - p[1]))
        return pl.pallas_call(
            first_send_kernel,
            grid_spec=pltpu.PrefetchScalarGridSpec(
                num_scalar_prefetch=1, grid=(2, 2), in_specs=[left, left, right, right], out_specs=[listed(lambda z, n, p: (z, n))] * 2
            ),
            out_shape=cells_of(2),
            cost_estimate=takes(3),
            name="first_send",
        )(place, early_keep, early_other, early_keep, early_other)

    def second_send(got_left, got_right):
        specs, operands = [], []
        for far in (0, 1):
            bit = lambda n, p, f=far: p[n] if f == 0 else 1 - p[n]
            left = picked(lambda z, n, p, bit=bit: (0, z, p[0], bit(1, p)))
            right = picked(lambda z, n, p, bit=bit: (1, z, bit(0, p), p[1]))
            specs += [left, left, listed(lambda z, n, p, bit=bit: (z, bit(1, p)))]
            operands += [early_keep, early_other, got_left]
            specs += [right, right, listed(lambda z, n, p, bit=bit: (z, bit(0, p)))]
            operands += [early_keep, early_other, got_right]
        rows_spec = pl.BlockSpec((1,) + cell, lambda z, n, p: (z, 0, 0))
        both_spec = pl.BlockSpec((2, 1) + cell, lambda z, n, p: (0, z, 0, 0))
        return pl.pallas_call(
            second_send_kernel,
            grid_spec=pltpu.PrefetchScalarGridSpec(num_scalar_prefetch=1, grid=(2, 1), in_specs=specs, out_specs=[both_spec, rows_spec, rows_spec]),
            out_shape=cells_of(1) + [jax.ShapeDtypeStruct((2,) + cell, bf16)] * 2,
            cost_estimate=takes(4),
            name="second_send",
        )(place, *operands)

    def third_send(keep, left, right):
        specs = []
        for step in range(layers):
            goal = lambda p, step=step: (p[3] + step) % layers
            specs.append(listed(lambda z, n, p, goal=goal: (goal(p) // 2, goal(p) % 2)))
            specs += [pl.BlockSpec((1,) + cell, lambda z, n, p, goal=goal: (goal(p) % 2, 0, 0))] * 2
        out = pl.BlockSpec(cell, lambda z, n, p: (0, 0))
        return pl.pallas_call(
            third_send_kernel,
            grid_spec=pltpu.PrefetchScalarGridSpec(num_scalar_prefetch=1, grid=(1, 1), in_specs=specs, out_specs=[out] * layers),
            out_shape=[jax.ShapeDtypeStruct(cell, bf16)] * layers,
            cost_estimate=takes(3),
            name="third_send",
        )(place, *[keep, left, right] * layers)

    def to_layer(value, step):
        pairs = [
            (win * blk_count + blk, win * blk_count + (blk + 2 * step) % blk_count)
            for win in range(win_count)
            for blk in range(blk_count)
        ]
        return lax.ppermute(value, ("win", "blk"), pairs)

    first_left, first_right = first_send()
    first_left, first_right = swap(first_left, 0, 1), swap(first_right, 2, 0)

    grad_parts = []
    for group in range(groups):
        after = []
        if group == 1:
            early_kept, send_left, send_right = second_send(first_left, first_right)
            after = [early_kept]
            second = swap(send_left, 2, 0), swap(send_right, 0, 1)
        if group == 2:
            early_parts = third_send(early_kept, *second)
            after = [early_parts[0]]
            early_parts = [early_parts[0]] + [to_layer(early_parts[n], n) for n in range(1, layers)]

        def column(first):
            return pl.BlockSpec((all_rows, lanes), lambda g, t: (0, first))

        def full(columns):
            return pl.BlockSpec((all_rows, columns), lambda g, t: (0, 0))

        grad_store = pltpu.VMEM((blocks, block_len, lanes), f32)
        glob_store = pltpu.VMEM((2, block_len, lanes), f32)
        dq, own, other = pl.pallas_call(
            partial(attend_back_kernel, sizes, blocks, head_dim, score_scale, group),
            grid_spec=pltpu.PrefetchScalarGridSpec(
                num_scalar_prefetch=1,
                grid=(1,),
                in_specs=[
                    column(group), column(group), column(group), column(groups + group), column(groups + group), column(group),
                    pl.BlockSpec((1, half_blocks, lanes), lambda g, t: (group, 0, 0)),
                    *[any_place] * len(after),
                ],
                out_specs=[full(lanes), full(2 * lanes), full(2 * lanes)],
                scratch_shapes=[store, store, grad_store, grad_store, glob_store, glob_store],
            ),
            out_shape=[jax.ShapeDtypeStruct((all_rows, n * lanes), bf16) for n in (1, 2, 2)],
            compiler_params=params,
            cost_estimate=takes(25),
            name="attend_back",
        )(table, query, key_value, key_value_other, key_value, key_value_other, grad_attended, log_total, *after)
        grad_parts += [dq, own, swap(other, 1, 0) if group < groups - 1 else other]

    def vmem(*shape):
        return pltpu.VMEM(shape, bf16)

    first_shape, mid_shape = (2, 2, 2), (2, 2)
    chain = lambda size: [vmem(*lead, size, width) for lead in (first_shape, mid_shape, mid_shape, (3,), ())]
    grad_tokens, late, early = pl.pallas_call(
        partial(finish_kernel, groups),
        grid=(layers,),
        in_specs=[by_tile(p.shape[1]) for p in grad_parts[:-1]]
        + [any_place, by_tile(width), by_tile(width), whole(1, width), whole(1, width), whole(width, 3 * width), whole(4, width), whole(chunks, width)]
        + [any_place] * layers,
        out_specs=[any_place] * 3,
        out_shape=[
            jax.ShapeDtypeStruct((layers, length, width), bf16),
            jax.ShapeDtypeStruct((win_count, late_size, width), bf16),
            jax.ShapeDtypeStruct((win_count, early_rows, width), bf16),
        ],
        scratch_shapes=[
            vmem(all_rows, 3 * width),
            vmem(layers, width, length),
            pltpu.VMEM((4, width), f32),
            vmem(layers, length, width),
            vmem(2, 2, 2, 2, 2, late_size, width),
            vmem(2, 2, 2, 2, late_size, width),
            chain(late_size),
            [vmem(*lead, early_rows, width) for lead in ((4,), ())],
            pltpu.SemaphoreType.DMA((layers,)),
            pltpu.SemaphoreType.DMA((layers,)),
            pltpu.SemaphoreType.DMA((4,)),
            pltpu.SemaphoreType.DMA((14,)),
            pltpu.SemaphoreType.DMA((14,)),
            pltpu.SemaphoreType.DMA((2,)),
            vmem(layers, length, 2 * lanes),
            pltpu.SemaphoreType.DMA((layers,)),
            pltpu.SemaphoreType.DMA((layers,)),
        ],
        compiler_params=remote_params(2, 62),
        cost_estimate=takes(90),
        name="finish",
    )(
        *grad_parts, rows_in, grad_resid, row(gain_one), row(shift_one), w_qkv, vec_two, vec_up,
        *early_parts,
    )
    part = width // blk_count
    count = wide // width
    done_qkv, done_out, done_up, done_down = pl.pallas_call(
        unpack_kernel,
        out_shape=[
            jax.ShapeDtypeStruct(shape, f32)
            for shape in ((part, 3 * width), (part, width), (part, wide), (wide // blk_count, width))
        ],
        compiler_params=params,
        cost_estimate=takes(4),
        name="unpack",
    )(early, late)
    late = late.reshape(-1, width)[3 * part :].astype(f32)
    vec = lax.dynamic_slice_in_dim(late[:8], blk_pos * part, part, axis=1)
    vec_wide = lax.dynamic_slice_in_dim(late[8 : 8 + count].reshape(-1), blk_pos * (wide // blk_count), wide // blk_count)
    return (
        out_tokens,
        grad_tokens,
        done_qkv,
        vec[0],
        vec[1],
        done_out,
        vec[4],
        vec[2],
        vec[3],
        vec[5],
        vec[6],
        done_up,
        vec_wide,
        done_down,
        vec[7],
    )


def solution(mesh):
    placed = (
        P("win", "blk", None),
        P("win", "blk", None),
        P(),
        P(),
        P(),
        P(),
        P(),
        P(),
        P(),
        P(),
        P(),
        P(),
        P(),
        P(),
        P(),
        P("win", None, None, None),
        P("win", None, None, None),
        P("win", None),
        P(),
    )
    return jax.shard_map(
        layer_step,
        mesh=mesh,
        in_specs=placed,
        out_specs=(
            P("win", "blk", None),
            P("win", "blk", None),
            P("blk", None),
            P("blk"),
            P("blk"),
            P("blk", None),
            P("blk"),
            P("blk"),
            P("blk"),
            P("blk"),
            P("blk"),
            P("blk", None),
            P("blk"),
            P("blk", None),
            P("blk"),
        ),
        check_vma=False,
    )
```

```python
from functools import partial

import jax
import jax.numpy as jnp
from jax import lax
from jax.experimental import pallas as pl
from jax.experimental.pallas import tpu as pltpu
from jax.sharding import PartitionSpec as P

SPECIES = 4


epsilon = 1e-05
masked_score = -1000000000.0


def padded(cells, sides, width):
    for axis, dim in sides:
        count = lax.axis_size(axis)
        ends = count - 1
        head = lax.slice_in_dim(cells, 0, width, axis=dim)
        tail = lax.slice_in_dim(cells, cells.shape[dim] - width, cells.shape[dim], axis=dim)
        cells = jnp.concatenate(
            [
                lax.ppermute(tail, axis, [(i, (i + 1) % count) for i in range(ends)]),
                cells,
                lax.ppermute(head, axis, [((i + 1) % count, i) for i in range(ends)]),
            ],
            axis=dim,
        )
    return cells


def layer_norm(values, norm_gain, norm_shift):
    average = jnp.mean(values, axis=-1, keepdims=True)
    centred = values - average
    variance = jnp.mean(centred * centred, axis=-1, keepdims=True)
    return centred * lax.rsqrt(variance + epsilon) * norm_gain + norm_shift


def take_rows(source, index_rows):
    return jnp.take(source, index_rows, axis=0)


def add_rows(base, index_rows, update):
    return base.at[index_rows].add(update)


def set_rows(base, index_rows, update):
    return base.at[index_rows].set(update)


HEADS_PER_GROUP = 4


def regroup_pairs(win_count, layers, step):
    pairs = []
    for win in range(win_count):
        for blk in range(2 * layers):
            layer, side = blk // 2, blk % 2
            target = ((layer + step) % layers) * 2 + win % 2
            pairs.append((win * 2 * layers + blk, ((win // 2) * 2 + side) * 2 * layers + target))
    return pairs


def flip_pairs(win_count, blk_count, win_bit, blk_bit):
    return [
        (win * blk_count + blk, (win ^ win_bit) * blk_count + (blk ^ blk_bit))
        for win in range(win_count)
        for blk in range(blk_count)
    ]


def swap(value, win_bit, blk_bit):
    pairs = flip_pairs(lax.axis_size("win"), lax.axis_size("blk"), win_bit, blk_bit)
    return lax.ppermute(value, ("win", "blk"), pairs)


def head_masks(lanes, head_dim, dtype):
    lane = lax.broadcasted_iota(jnp.int32, (1, lanes), 1)
    return [(lane // head_dim == h).astype(dtype) for h in range(lanes // head_dim)]


def block_places(table, slot, group, sizes):
    heads, picks, rand_size, half_blocks = sizes
    block = table[rand_size + 2 + slot]
    near = [table[rand_size + 2 + half_blocks + slot], slot, table[rand_size + 2 + 2 * half_blocks + slot]]
    row = (block * heads + group * HEADS_PER_GROUP) * picks
    rand = [[table[row + h * picks + r] for h in range(HEADS_PER_GROUP)] for r in range(picks)]
    return block, near, rand


def spread_heads(rows, masks):
    return jnp.concatenate([rows * m for m in masks], axis=0)


def pick_heads(square, masks, height):
    total = square[0:height] * masks[0]
    for h in range(1, len(masks)):
        total = total + square[h * height : (h + 1) * height] * masks[h]
    return total


def key_rows(source, near, glob, rand, low_half):
    parts = [source[p] for p in near] + [source[p] for p in glob]
    for places in rand:
        columns = []
        for c in range(len(places) // 2):
            low = source[places[2 * c], :, c * 128 : (c + 1) * 128]
            high = source[places[2 * c + 1], :, c * 128 : (c + 1) * 128]
            columns.append(jnp.where(low_half, low, high))
        parts.append(jnp.concatenate(columns, axis=1))
    return jnp.concatenate(parts, axis=0)


def mask_scores(scores, block, blocks, block_len):
    first = jnp.where(block > 0, scores[:block_len], masked_score)
    last = jnp.where(block < blocks - 1, scores[2 * block_len : 3 * block_len], masked_score)
    return jnp.concatenate([first, scores[block_len : 2 * block_len], last, scores[3 * block_len :]], axis=0)


def across(left, right):
    return lax.dot_general(left, right, (((1,), (1,)), ((), ())), preferred_element_type=jnp.float32)


def down(left, right):
    return lax.dot_general(left, right, (((0,), (0,)), ((), ())), preferred_element_type=jnp.float32)


def load_halves(target, own, other, half_blocks, block_len):
    lanes = own.shape[-1]
    target[0:half_blocks] = own[...].reshape(half_blocks, block_len, lanes)
    target[half_blocks:] = other[...].reshape(half_blocks, block_len, lanes)


def attend_kernel(
    sizes, blocks, head_dim, cot_tiles,
    table, q_ref, k_own, k_other, v_own, v_other, cotangent,
    o_ref, lse_ref, cot_ref,
    k_all, v_all, send_sems, recv_sems,
):
    heads, picks, rand_size, half_blocks = sizes
    block_len = k_all.shape[1]
    lanes = q_ref.shape[1]
    group = pl.program_id(0)
    _, _, core, layer, _ = position()
    own_blocks = blocks // 8

    @pl.when(group == 0)
    def _():
        greet_owners(4, [])
        for n, tile in enumerate(cot_tiles):
            regroup_move(cotangent, cot_ref.at[n], tile, send_sems.at[n], recv_sems.at[n], True)

    load_halves(k_all, k_own, k_other, half_blocks, block_len)
    load_halves(v_all, v_own, v_other, half_blocks, block_len)
    low_half = lax.broadcasted_iota(jnp.int32, (block_len, 128), 1) < head_dim
    masks = head_masks(lanes, head_dim, jnp.bfloat16)
    masks_f = head_masks(lanes, head_dim, jnp.float32)
    glob = [table[rand_size], table[rand_size + 1]]

    def one(slot, carry):
        block = (((layer + 4 - slot // own_blocks) % 4) * 2 + core) * own_blocks + slot % own_blocks
        _, near, rand = block_places(table, slot, group, sizes)
        rows = pl.ds(pl.multiple_of(slot * block_len, block_len), block_len)
        queries = spread_heads(q_ref[rows, :], masks)
        keys = key_rows(k_all, near, glob, rand, low_half)
        scores = mask_scores(across(keys, queries), block, blocks, block_len)
        top = jnp.max(scores, axis=0, keepdims=True)
        weights = jnp.exp(scores - top)
        total = jnp.sum(weights, axis=0, keepdims=True)
        probs = (weights * (1.0 / total)).astype(jnp.bfloat16)
        values = key_rows(v_all, near, glob, rand, low_half)
        o_ref[rows, :] = pick_heads(down(probs, values), masks_f, block_len).astype(jnp.bfloat16)
        lse_ref[0, pl.ds(slot, 1), :] = top + jnp.log(total)
        return carry

    lax.fori_loop(0, half_blocks, one, 0, unroll=min(8, half_blocks))

    @pl.when(group == pl.num_programs(0) - 1)
    def _():
        for n, tile in enumerate(cot_tiles):
            regroup_move(cotangent, cot_ref.at[n], tile, send_sems.at[n], recv_sems.at[n], False)


def attend_back_kernel(
    sizes, blocks, head_dim, scale, group,
    table, q_ref, k_own, k_other, v_own, v_other, go_ref, lse_ref, *refs,
):
    dq_ref, own_ref, other_ref, k_all, v_all, dk_all, dv_all, dk_glob, dv_glob = refs[-9:]
    heads, picks, rand_size, half_blocks = sizes
    block_len = k_all.shape[1]
    lanes = q_ref.shape[1]
    f32 = jnp.float32
    load_halves(k_all, k_own, k_other, half_blocks, block_len)
    load_halves(v_all, v_own, v_other, half_blocks, block_len)
    dk_all[...] = jnp.zeros_like(dk_all)
    dv_all[...] = jnp.zeros_like(dv_all)
    dk_glob[...] = jnp.zeros_like(dk_glob)
    dv_glob[...] = jnp.zeros_like(dv_glob)
    low_half = lax.broadcasted_iota(jnp.int32, (block_len, 128), 1) < head_dim
    masks = head_masks(lanes, head_dim, jnp.bfloat16)
    masks_f = head_masks(lanes, head_dim, f32)
    glob = [table[rand_size], table[rand_size + 1]]

    def add_back(grads, near, rand, into, into_glob):
        for n in range(3):
            into[near[n]] += grads[n * block_len : (n + 1) * block_len]
        for n in range(2):
            into_glob[n] += grads[(3 + n) * block_len : (4 + n) * block_len]
        for r in range(picks):
            part = grads[(5 + r) * block_len : (6 + r) * block_len]
            for c in range(lanes // 128):
                cell = part[:, c * 128 : (c + 1) * 128]
                columns = pl.ds(c * 128, 128)
                into[rand[r][2 * c], :, columns] += jnp.where(low_half, cell, 0.0)
                into[rand[r][2 * c + 1], :, columns] += jnp.where(low_half, 0.0, cell)

    def one(slot, carry):
        block, near, rand = block_places(table, slot, group, sizes)
        rows = pl.ds(pl.multiple_of(slot * block_len, block_len), block_len)
        queries = spread_heads(q_ref[rows, :], masks)
        grads_out = spread_heads(go_ref[rows, :], masks)
        keys = key_rows(k_all, near, glob, rand, low_half)
        values = key_rows(v_all, near, glob, rand, low_half)
        scores = mask_scores(across(keys, queries), block, blocks, block_len)
        probs = jnp.exp(scores - lse_ref[0, pl.ds(slot, 1), :])
        grad_probs = across(values, grads_out)
        row_dot = jnp.sum(probs * grad_probs, axis=0, keepdims=True)
        grad_scores = (probs * (grad_probs - row_dot)).astype(jnp.bfloat16)
        add_back(jnp.dot(probs.astype(jnp.bfloat16), grads_out, preferred_element_type=f32), near, rand, dv_all, dv_glob)
        add_back(jnp.dot(grad_scores, queries, preferred_element_type=f32), near, rand, dk_all, dk_glob)
        dq_ref[rows, :] = (pick_heads(down(grad_scores, keys), masks_f, block_len) * scale).astype(jnp.bfloat16)
        return carry

    lax.fori_loop(0, half_blocks, one, 0, unroll=min(8, half_blocks))
    for n in range(2):
        dk_all[glob[n]] += dk_glob[n]
        dv_all[glob[n]] += dv_glob[n]
    for target, start in ((own_ref, 0), (other_ref, half_blocks)):
        for n, source in enumerate((dk_all, dv_all)):
            cells = source[start : start + half_blocks].astype(jnp.bfloat16)
            target[:, n * lanes : (n + 1) * lanes] = cells.reshape(half_blocks * block_len, lanes)


def norm_parts(values):
    average = jnp.mean(values, axis=-1, keepdims=True)
    centred = values - average
    rstd = lax.rsqrt(jnp.mean(centred * centred, axis=-1, keepdims=True) + epsilon)
    return centred * rstd, rstd


def norm_back(grad, normal, rstd, gain):
    scaled = grad * gain
    first = jnp.mean(scaled, axis=-1, keepdims=True)
    second = jnp.mean(scaled * normal, axis=-1, keepdims=True)
    return rstd * (scaled - first - normal * second)


def normal_parts(values):
    cdf = 0.5 + 0.5 * lax.erf(values * 0.5**0.5)
    return cdf, values * jnp.exp(-0.5 * values * values) * 0.3989422804014327


def column_sum(values):
    return jnp.sum(values, axis=0, keepdims=True)


MESH = pl.DeviceIdType.MESH


def tile_order(number):
    return jnp.where(number == 0, 2, jnp.where(number == 2, 3, jnp.where(number == 3, 0, number)))


def position():
    win, blk = lax.axis_index("win"), lax.axis_index("blk")
    return win, blk, win % 2, blk // 2, blk % 2


def owner_of(tile, layers):
    win, blk, core, layer, side = position()
    return (win // 2) * 2 + side, ((layer + layers - tile) % layers) * 2 + core


def greet_owners(layers, peers):
    barrier = pltpu.get_barrier_semaphore()
    others = len(peers)
    for peer in peers:
        pl.semaphore_signal(barrier, inc=1, device_id=peer, device_id_type=MESH)
    _, _, core, _, side = position()
    for tile in range(1, layers):
        pl.semaphore_signal(barrier, inc=1, device_id=owner_of(tile, layers), device_id_type=MESH)

    @pl.when(side != core)
    def _():
        pl.semaphore_signal(barrier, inc=1, device_id=owner_of(0, layers), device_id_type=MESH)
        pl.semaphore_wait(barrier, layers + others)

    @pl.when(side == core)
    def _():
        pl.semaphore_wait(barrier, layers - 1 + others)


def return_tile(tile, source, target, send_sem, recv_sems, start):
    _, _, core, layer, side = position()
    layers = target.shape[0]
    stays = (tile == 0) & (side == core)

    @pl.when(stays)
    def _():
        move = pltpu.make_async_copy(source, target.at[layer], recv_sems.at[tile])
        move.start() if start else move.wait()

    @pl.when(jnp.logical_not(stays))
    def _():
        move = pltpu.make_async_remote_copy(
            src_ref=source, dst_ref=target.at[layer], send_sem=send_sem, recv_sem=recv_sems.at[tile],
            device_id=owner_of(tile, layers), device_id_type=MESH,
        )
        move.start() if start else move.wait()


def regroup_move(source, target, tile, send_sem, recv_sem, start):
    win, _, core, layer, side = position()
    layers = source.shape[0]
    goal = (layer + tile) % layers
    stays = (tile == 0) & (side == core)

    def local():
        return pltpu.make_async_copy(source.at[goal], target, recv_sem)

    def far():
        return pltpu.make_async_remote_copy(
            src_ref=source.at[goal], dst_ref=target, send_sem=send_sem, recv_sem=recv_sem,
            device_id=((win // 2) * 2 + side, goal * 2 + core), device_id_type=MESH,
        )

    @pl.when(stays)
    def _():
        local().start() if start else local().wait()

    @pl.when(jnp.logical_not(stays))
    def _():
        far().start() if start else far().wait()


def arrival_order(number):
    return jnp.where(number == 2, 3, jnp.where(number == 3, 2, number))


def front_kernel(
    scale, tokens, gain, shift, weight, bias,
    rows_ref, q_ref, kv_ref, other_ref,
    held, kv_rows, send_sems, recv_sems, kv_sems, kv_send, kv_recv, row_sems,
):
    f32, bf16 = jnp.float32, jnp.bfloat16
    step, steps = pl.program_id(0), pl.num_programs(0)
    length, width = held.shape[1:]
    win, blk, core, layer, side = position()
    layers = held.shape[0]
    peer = (win + 1 - 2 * core, blk)

    def token_move(tile, start):
        regroup_move(tokens, held.at[tile], tile, send_sems.at[tile], recv_sems.at[tile], start)

    def rows_of(tile):
        return pl.ds(pl.multiple_of(tile * length, length), length)

    def kv_moves(number):
        tile = arrival_order(number)
        return [
            pltpu.make_async_copy(kv_rows.at[number], kv_ref.at[rows_of(tile)], kv_sems.at[number]),
            pltpu.make_async_copy(held.at[tile], rows_ref.at[rows_of(tile)], row_sems.at[number]),
            pltpu.make_async_remote_copy(
                src_ref=kv_rows.at[number], dst_ref=other_ref.at[rows_of(tile)], send_sem=kv_send.at[number], recv_sem=kv_recv.at[number],
                device_id=peer, device_id_type=MESH,
            ),
        ]

    @pl.when(step == 0)
    def _():
        greet_owners(layers, [peer])
        for n in range(4):
            token_move(arrival_order(n), True)

    tile = arrival_order(step)
    token_move(tile, False)
    normal, _ = norm_parts(held[tile].astype(f32))
    normed = (normal * gain[...] + shift[...]).astype(bf16)

    def part(n):
        return jnp.dot(normed, weight[:, n * width : (n + 1) * width], preferred_element_type=f32)

    kv_rows[step, :, :width] = part(1).astype(bf16)
    kv_rows[step, :, width:] = (part(2) + bias[1:2]).astype(bf16)
    for move in kv_moves(step):
        move.start()
    q_ref[...] = (part(0) + bias[0:1]).astype(bf16) * jnp.asarray(scale, bf16)

    @pl.when(step == steps - 1)
    def _():
        for n in range(4):
            for move in kv_moves(n):
                move.wait()


def ffn_forward_kernel(
    chunk, cot_tiles,
    rows_ref, att_ref, w_out, b_out, gain, shift, w_up, b_up, w_down, b_down, cotangent,
    out_ref, last_ref, normal_ref, second_ref, att_turned_ref, rstd_ref, active_ref, slope_ref, cot_ref,
    send_sems, recv_sems,
):
    f32, bf16 = jnp.float32, jnp.bfloat16
    step, steps = pl.program_id(0), pl.num_programs(0)

    @pl.when(step == 0)
    def _():
        greet_owners(4, [])
        for n, tile in enumerate(cot_tiles):
            regroup_move(cotangent, cot_ref.at[n], tile, send_sems.at[n], recv_sems.at[n], True)

    wide = w_up.shape[1]
    att = att_ref[...]
    residual = rows_ref[...].astype(f32) + (jnp.dot(att, w_out[...], preferred_element_type=f32) + b_out[...])
    normal, rstd = norm_parts(residual)
    second = (normal * gain[...] + shift[...]).astype(bf16)
    normal_ref[...] = normal.astype(bf16)
    second_ref[...] = second.T
    att_turned_ref[...] = att.T
    rstd_ref[...] = jnp.broadcast_to(rstd, rstd_ref.shape)

    def raise_part(first):
        part = slice(first, first + chunk)
        return jnp.dot(second, w_up[:, part], preferred_element_type=f32) + b_up[:, part]

    ahead = raise_part(0)
    for first in range(0, wide, chunk):
        inner = ahead
        if first + chunk < wide:
            ahead = raise_part(first + chunk)
        cdf, slope = normal_parts(inner)
        active_ref[:, first : first + chunk] = (inner * cdf).astype(bf16)
        slope_ref[:, first : first + chunk] = (cdf + slope).astype(bf16)
    total = residual + b_down[...] + jnp.dot(active_ref[...], w_down[...], preferred_element_type=f32)
    out_ref[...] = total.astype(bf16)

    @pl.when(step == steps - 1)
    def _():
        last_ref[...] = total.astype(bf16)
        for n, tile in enumerate(cot_tiles):
            regroup_move(cotangent, cot_ref.at[n], tile, send_sems.at[n], recv_sems.at[n], False)


def ffn_back_kernel(
    chunks, shards, kept_tiles,
    scale, active_ref, slope_ref, w_up, w_down, second_t, normal_ref, rstd_ref, att_t, w_out, gain,
    cot_even, cot_odd, output,
    resid_ref, go_ref, vec_ref, vec_up_ref, keep_ref, other_ref, out_ref,
    cot_rows, branch, branch_t, grad_inner, grad_second, stage_up, stage_down,
    cot_sems, ship_send, ship_recv, cell_send, cell_recv, done_sems,
):
    f32, bf16 = jnp.float32, jnp.bfloat16
    step = pl.program_id(0)
    slot = step % 2
    width = w_up.shape[0]
    tiles, length = cot_rows.shape[:2]
    part = width // shards
    half = width // 2
    size = keep_ref.shape[2]
    win, blk, core, _, _ = position()
    peer = (win + 1 - 2 * core, blk)

    def rows_of(n):
        return slice(n * length, (n + 1) * length)

    def ship(what):
        for n, tile in enumerate(kept_tiles):
            return_tile(tile, output.at[rows_of(tile)], out_ref, ship_send.at[n], ship_recv, what)

    def moves(c):
        cuts = []
        if c < chunks:
            base = 4 * c
            for first, count, piece, row in span_cuts(c * part, part, size):
                cuts.append((base + len(cuts), stage_up.at[c % 2, :, pl.ds(first, count)], slice(0, shards), piece, row, count))
            mine = slice(2 * c, 2 * c + 2)
            for first, count, piece, row in span_cuts(chunks * part, half, size):
                cuts.append((24 + base + len(cuts), stage_down.at[c % 2, :, pl.ds(first, count)], mine, piece, row, count))
        else:
            start = chunks * part + half
            for first, count, piece, row in span_cuts(start, 4 * size - start, size):
                cuts.append((20 + len(cuts), stage_up.at[0, :, pl.ds(first, count)], slice(0, shards), piece, row, count))
        return cuts

    def act(c, what):
        for number, source, mine, piece, row, count in moves(c):
            cell = (pl.ds(mine.start, mine.stop - mine.start), piece // 2, pl.ds(row, count))
            def far():
                return pltpu.make_async_remote_copy(
                    src_ref=source, dst_ref=other_ref.at[cell], send_sem=cell_send.at[number], recv_sem=cell_recv.at[number],
                    device_id=peer, device_id_type=MESH,
                )

            @pl.when(core == piece % 2)
            def _():
                if what == "receive":
                    far().wait_recv()
                else:
                    near = pltpu.make_async_copy(source, keep_ref.at[cell], cell_send.at[number])
                    near.start() if what == "start" else near.wait()

            if what != "receive":
                @pl.when(core != piece % 2)
                def _():
                    far().start() if what == "start" else far().wait_send()

    def cot_moves():
        return [
            pltpu.make_async_copy((cot_even, cot_odd)[n % 2].at[n // 2], cot_rows.at[n], cot_sems.at[n]) for n in range(4)
        ]

    @pl.when(step == 0)
    def _():
        for move in cot_moves():
            move.start()
        greet_owners(tiles, [peer])
        ship(True)
        vec_ref[...] = jnp.zeros_like(vec_ref)
        for n, move in enumerate(cot_moves()):
            move.wait()
            upstream = cot_rows[n].astype(f32) * scale[0]
            vec_ref[3:4] += column_sum(upstream)
            branch[rows_of(n), :] = upstream.astype(bf16)
            branch_t[:, rows_of(n)] = upstream.astype(bf16).T
        grad_second[...] = jnp.zeros_like(grad_second)

    for c in range(2, chunks):
        @pl.when(step == c)
        def _():
            act(c - 2, "wait")

    full = jnp.dot(branch_t[...], active_ref[...], preferred_element_type=f32)
    for n in range(2):
        for k in range(2):
            stage_down[slot, n, :, k * half : (k + 1) * half] = full[k * half : (k + 1) * half, n * half : (n + 1) * half].astype(bf16)
    total = jnp.zeros((1, w_up.shape[1]), f32)
    for n in range(tiles):
        grad = across(branch[rows_of(n), :], w_down[...]) * slope_ref[rows_of(n), :].astype(f32)
        total = total + column_sum(grad)
        grad_inner[rows_of(n), :] = grad.astype(bf16)
        grad_second[rows_of(n), :] += across(grad_inner[rows_of(n), :], w_up[...])
    vec_up_ref[pl.ds(step, 1), :] = total
    full = jnp.dot(second_t[...], grad_inner[...], preferred_element_type=f32)
    for b in range(shards):
        stage_up[slot, b, 0:part] = full[b * part : (b + 1) * part].astype(bf16)
    for c in range(chunks):
        @pl.when(step == c)
        def _():
            act(c, "start")

    @pl.when(step == chunks - 1)
    def _():
        for n in range(tiles):
            upstream = cot_rows[n].astype(f32) * scale[0]
            grad = grad_second[rows_of(n), :]
            normal = normal_ref[rows_of(n), :].astype(f32)
            grad_resid = upstream + norm_back(grad, normal, rstd_ref[rows_of(n), 0:1], gain[...])
            grad_proj = grad_resid.astype(bf16)
            grad_inner[rows_of(n), :] = grad_proj
            branch[rows_of(n), :] = across(grad_proj, w_out[...]).astype(bf16)
            vec_ref[0:1] += column_sum(grad_resid)
            vec_ref[1:2] += column_sum(grad * normal)
            vec_ref[2:3] += column_sum(grad)
        results = [
            pltpu.make_async_copy(grad_inner, resid_ref, done_sems.at[0]),
            pltpu.make_async_copy(branch, go_ref, done_sems.at[1]),
        ]
        for move in results:
            move.start()
        full = jnp.dot(att_t[...], grad_inner[...], preferred_element_type=f32)
        act(chunks - 2, "wait")
        for b in range(shards):
            stage_up[0, b, 0:part] = full[b * part : (b + 1) * part].astype(bf16)
            stage_up[0, b, part:] = jnp.zeros((stage_up.shape[2] - part, width), bf16)
        act(chunks, "start")
        act(chunks - 1, "wait")
        act(chunks, "wait")
        for c in range(chunks + 1):
            act(c, "receive")
        for move in results:
            move.wait()
        ship(False)


def span_cuts(start, count, size):
    cuts, at = [], start
    while at < start + count:
        end = min(start + count, (at // size + 1) * size)
        cuts.append((at - start, end - at, at // size, at % size))
        at = end
    return cuts


def row_cuts(count, part, size):
    cuts = []
    for k in range(count):
        start = k * part
        while start < (k + 1) * part:
            end = min((k + 1) * part, (start // size + 1) * size)
            cuts.append((k, start - k * part, end - start, start // size, start % size))
            start = end
    return cuts


def add_into(target, got):
    target[...] = (target[...].astype(jnp.float32) + got[...].astype(jnp.float32)).astype(jnp.bfloat16)


def finish_kernel(groups, *refs):
    f32, bf16 = jnp.float32, jnp.bfloat16
    parts = refs[: 3 * groups - 1]
    (
        last_other, rows_ref, resid_ref, gain, shift, weight, vec_two, vec_up, early_a, early_b, early_c, early_d,
        tok_ref, late_ref, early_ref,
        joined, turned, vec, out_rows, cells, core_got, late_bufs, early_bufs, send_sems, recv_sems, load_sems, chain_send, chain_recv, keep_sems, last_rows, last_send, last_recv,
    ) = refs[3 * groups - 1 :]
    step, steps = pl.program_id(0), pl.num_programs(0)
    length, width = rows_ref.shape
    lanes = width // groups
    part = width // 8
    win, blk, core, layer, side = position()
    pair = win // 2
    core_peer = (win + 1 - 2 * core, blk)
    pair_peer = (win + 2 - 4 * pair, blk)
    side_peer = (win, blk + 1 - 2 * side)
    layer_peers = [(win, ((layer + n) % 4) * 2 + side) for n in (1, 2, 3)]

    def remote(source, target, number, peer):
        return pltpu.make_async_remote_copy(
            src_ref=source, dst_ref=target, send_sem=chain_send.at[number], recv_sem=chain_recv.at[number],
            device_id=peer, device_id_type=MESH,
        )

    early_got, early_final = early_bufs

    def loads():
        return [
            pltpu.make_async_copy(source, early_got.at[n], load_sems.at[n])
            for n, source in enumerate((early_a, early_b, early_c, early_d))
        ]

    def second_step(state, got, base):
        return [
            remote(state.at[0, :, 1 - pair], got.at[0], base, pair_peer),
            remote(state.at[1, :, 1 - side], got.at[1], base + 1, side_peer),
        ]

    def add_second(state, got, mid):
        for z in range(2):
            mid[0, z] = (state[0, z, pair].astype(f32) + got[0, z].astype(f32)).astype(bf16)
            mid[1, z] = (state[1, z, side].astype(f32) + got[1, z].astype(f32)).astype(bf16)

    def layer_step(mid, got, base):
        moves = []
        for n in range(3):
            other = (layer + n + 1) % 4
            moves.append(remote(mid.at[other // 2, other % 2], got.at[n], base + n, layer_peers[n]))
        return moves

    def sum_into(final, parts):
        total = parts[0].astype(f32)
        for one in parts[1:]:
            total = total + one.astype(f32)
        final[...] = total.astype(bf16)

    def share(final, target, base):
        return [
            remote(final, target.at[win], base, core_peer),
            remote(final, target.at[win], base + 1, pair_peer),
        ]

    def pass_on(target, base):
        return [remote(target.at[win + 2 - 4 * pair], target.at[win + 2 - 4 * pair], base, core_peer)]

    def start(moves):
        for move in moves:
            move.start()

    def wait(moves):
        for move in moves:
            move.wait()

    def last_move(number):
        first = pl.multiple_of(tile_order(number) * length, length)
        return pltpu.make_async_remote_copy(
            src_ref=last_other.at[pl.ds(first, length)], dst_ref=last_rows.at[number], send_sem=last_send.at[number],
            recv_sem=last_recv.at[number], device_id=core_peer, device_id_type=MESH,
        )

    late_first, late_second, late_mid, late_got, late_final = late_bufs
    early_base, late_base = 8, 0

    @pl.when(step == 0)
    def _():
        start(loads())
        greet_owners(steps, [core_peer, pair_peer, side_peer] + layer_peers)
        for n in range(4):
            last_move(n).start()
        vec[...] = jnp.zeros_like(vec)

    tile = tile_order(step)
    rows = pl.ds(pl.multiple_of(tile * length, length), length)
    last_move(step).wait()
    for g in range(groups):
        dq, own = parts[3 * g : 3 * g + 2]
        other = parts[3 * g + 2] if g < groups - 1 else last_rows.at[step]
        columns = slice(g * lanes, (g + 1) * lanes)
        joined[rows, columns] = dq[...]
        both = (own[...].astype(f32) + other[...].astype(f32)).astype(bf16)
        joined[rows, width + g * lanes : width + (g + 1) * lanes] = both[:, :lanes]
        joined[rows, 2 * width + g * lanes : 2 * width + (g + 1) * lanes] = both[:, lanes:]
        vec[0:1, columns] += column_sum(dq[...].astype(f32))
        vec[1:2, columns] += column_sum(both[:, lanes:].astype(f32))
    grad = across(joined[rows, :], weight[...])
    normal, rstd = norm_parts(rows_ref[...].astype(f32))
    turned[tile] = (normal * gain[...] + shift[...]).astype(bf16).T
    vec[2:3] += column_sum(grad * normal)
    vec[3:4] += column_sum(grad)
    out_rows[step] = (resid_ref[...].astype(f32) + norm_back(grad, normal, rstd, gain[...])).astype(bf16)
    return_tile(tile, out_rows.at[step], tok_ref, send_sems.at[step], recv_sems, True)

    @pl.when(step == 0)
    def _():
        wait(loads())
        sum_into(early_final, [early_got[n] for n in range(4)])
        start(share(early_final, early_ref, early_base))
        pltpu.make_async_copy(early_final, early_ref.at[win], keep_sems.at[0]).start()

    @pl.when(step == steps - 1)
    def _():
        size = cells.shape[5]
        cuts = row_cuts(3, part, size)
        for k in range(3):
            full = jnp.dot(turned[0], joined[0:length, k * width : (k + 1) * width], preferred_element_type=f32)
            for n in range(1, 4):
                full = full + jnp.dot(
                    turned[n], joined[n * length : (n + 1) * length, k * width : (k + 1) * width], preferred_element_type=f32
                )
            for b in range(8):
                for which, first, count, piece, row in cuts:
                    if which == k:
                        cells[piece % 2, b // 4, b // 2 % 2, b % 2, piece // 2, row : row + count] = full[
                            b * part + first : b * part + first + count
                        ].astype(bf16)
        tail = jnp.concatenate(
            [vec[...], vec_two[...], vec_up[...]]
            + [jnp.zeros((4 * size - 3 * part - 12, width), f32)],
            axis=0,
        ).astype(bf16)
        for b in range(8):
            cells[1, b // 4, b // 2 % 2, b % 2, 1, 3 * part - 3 * size :] = tail
        exchange = [remote(cells.at[1 - core], core_got, late_base, core_peer)]
        start(exchange)
        wait(share(early_final, early_ref, early_base))
        start(pass_on(early_ref, early_base + 2))
        wait(exchange)
        mine = cells.at[core]
        for b in range(8):
            for x in range(2):
                add_into(mine.at[b // 4, b // 2 % 2, b % 2, x], core_got.at[b // 4, b // 2 % 2, b % 2, x])
        first = [
            remote(mine.at[0, :, 1 - side], late_first.at[0], late_base + 1, side_peer),
            remote(mine.at[1, :, :, 1 - pair], late_first.at[1], late_base + 2, pair_peer),
        ]
        start(first)
        wait(first)
        state = core_got.at[0]
        for z in range(2):
            for n in range(2):
                state[0, z, n] = (mine[0, z, side, n].astype(f32) + late_first[0, z, n].astype(f32)).astype(bf16)
                state[1, z, n] = (mine[1, z, n, pair].astype(f32) + late_first[1, z, n].astype(f32)).astype(bf16)
        start(second_step(state, late_second, late_base + 3))
        wait(second_step(state, late_second, late_base + 3))
        add_second(state, late_second, late_mid)
        across_layers = layer_step(late_mid, late_got, late_base + 5)
        start(across_layers)
        wait(across_layers)
        sum_into(late_final, [late_mid[layer // 2, layer % 2]] + [late_got[n] for n in range(3)])
        start(share(late_final, late_ref, early_base + 3))
        keep_late = pltpu.make_async_copy(late_final, late_ref.at[win], keep_sems.at[1])
        keep_late.start()
        wait(share(late_final, late_ref, early_base + 3))
        start(pass_on(late_ref, early_base + 5))
        wait(pass_on(early_ref, early_base + 2))
        wait(pass_on(late_ref, early_base + 5))
        pltpu.make_async_copy(early_final, early_ref.at[win], keep_sems.at[0]).wait()
        keep_late.wait()
        for n in range(4):
            return_tile(tile_order(n), out_rows.at[n], tok_ref, send_sems.at[n], recv_sems, False)


def first_send_kernel(place, keep_left, other_left, keep_right, other_right, left_ref, right_ref):
    for keep, other, target in ((keep_left, other_left, left_ref), (keep_right, other_right, right_ref)):
        target[...] = (keep[...].astype(jnp.float32) + other[...].astype(jnp.float32)).astype(jnp.bfloat16).reshape(target.shape)


def sum_low(target, refs):
    total = refs[0][...].astype(jnp.float32)
    for ref in refs[1:]:
        total = total + ref[...].astype(jnp.float32)
    target[...] = total.astype(jnp.bfloat16).reshape(target.shape)


def second_send_kernel(place, *refs):
    keep, left, right = refs[12:]
    for n, target in enumerate((keep.at[0], keep.at[1], left, right)):
        sum_low(target, refs[3 * n : 3 * n + 3])


def third_send_kernel(place, *refs):
    for n in range(4):
        keep, left, right = refs[3 * n : 3 * n + 3]
        in_left = (place[3] + n) % 4 < 2
        got = jnp.where(in_left, left[...].astype(jnp.float32), right[...].astype(jnp.float32))
        target = refs[12 + n]
        target[...] = (keep[...].reshape(target.shape).astype(jnp.float32) + got.reshape(target.shape)).astype(jnp.bfloat16)


def unpack_kernel(early, late, qkv_ref, out_ref, up_ref, down_ref):
    f32 = jnp.float32
    part, width = out_ref.shape
    count = up_ref.shape[1] // width
    half = width // 2

    def cells(source, first, rows):
        size = source.shape[1]
        parts = []
        while rows > 0:
            take = min(rows, size - first % size)
            parts.append(source[first // size, first % size : first % size + take])
            first, rows = first + take, rows - take
        return (parts[0] if len(parts) == 1 else jnp.concatenate(parts, axis=0)).astype(f32)

    for k in range(3):
        qkv_ref[:, k * width : (k + 1) * width] = cells(late, k * part, part)
    for k in range(count):
        up_ref[:, k * width : (k + 1) * width] = cells(early, k * part, part)
    turned = cells(early, count * part, half)
    down_ref[:, :half] = turned[:, :half].T
    down_ref[:, half:] = turned[:, half:].T
    out_ref[...] = cells(early, count * part + half, part)


def general_body(
    tokens,
    cotangent,
    w_qkv,
    b_q,
    b_v,
    w_out,
    b_out,
    gain_one,
    shift_one,
    gain_two,
    shift_two,
    w_up,
    b_up,
    w_down,
    b_down,
    rand_owner,
    rand_sub,
    global_ids,
    species,
):
    blk_count = lax.axis_size("blk")
    blk_pos = lax.axis_index("blk")
    win_pos = lax.axis_index("win")
    windows, length, model_width = tokens.shape
    blocks = rand_owner.shape[1]
    heads = rand_owner.shape[2]
    picks = rand_owner.shape[3]
    glob_count = global_ids.shape[1]
    own_blocks = blocks // blk_count
    block_len = length // own_blocks
    head_dim = model_width // heads
    pair_width = 2 * head_dim
    all_rows = windows * length
    key_count = 3 + glob_count + picks
    per_device = own_blocks * heads * picks
    slot_cap = max(2, 2 * per_device // blk_count)
    score_scale = head_dim ** (-0.5)
    f32 = jnp.float32
    bf16 = jnp.bfloat16
    tokens_f = tokens.reshape(all_rows, model_width).astype(f32)
    normed_f, norm_one_pull = jax.vjp(layer_norm, tokens_f, gain_one, shift_one)
    normed = normed_f.astype(bf16)
    joined = jnp.dot(normed, w_qkv, preferred_element_type=f32)
    query_vals = (joined[:, :model_width] + b_q).astype(bf16)
    key_vals = joined[:, model_width : 2 * model_width].astype(bf16)
    value_vals = (joined[:, 2 * model_width :] + b_v).astype(bf16)

    def to_heads(tensor):
        return tensor.reshape(windows, own_blocks, block_len, heads, head_dim).transpose(
            0, 1, 3, 2, 4
        )

    def from_heads(tensor):
        return tensor.transpose(0, 1, 3, 2, 4).reshape(all_rows, model_width)

    query_heads = to_heads(query_vals)
    local_pairs = jnp.concatenate([to_heads(key_vals), to_heads(value_vals)], axis=-1)
    rimmed = padded(local_pairs, (("blk", 1),), 1)
    block_ids = blk_pos * own_blocks + jnp.arange(own_blocks, dtype=jnp.int32)
    owned_glob = (global_ids[:, :, None] == block_ids[None, None, :]).astype(bf16)
    glob_terms = jnp.einsum("wgb,wbhsc->wghsc", owned_glob, local_pairs, preferred_element_type=f32)
    glob_pairs = lax.psum(glob_terms.astype(jnp.bfloat16), "blk").astype(jnp.float32).astype(bf16)
    owner_rows = rand_owner.reshape(windows, blk_count, per_device)
    sub_rows = rand_sub.reshape(windows, blk_count, per_device)
    owner_hits = (owner_rows[..., None] == jnp.arange(blk_count, dtype=jnp.int32)).astype(jnp.int32)
    slot_rows = jnp.sum(owner_hits * (jnp.cumsum(owner_hits, axis=2) - 1), axis=-1)
    my_owner = lax.dynamic_index_in_dim(owner_rows, blk_pos, 1, keepdims=False)
    my_slot = lax.dynamic_index_in_dim(slot_rows, blk_pos, 1, keepdims=False)
    fetch_index = my_owner * slot_cap + my_slot
    head_of_row = jnp.arange(per_device, dtype=jnp.int32) // picks % heads
    source_rows = sub_rows * heads + head_of_row[None, None, :]
    requester = jnp.arange(blk_count, dtype=jnp.int32)[None, :, None]
    target_rows = jnp.where(
        owner_rows == blk_pos, requester * slot_cap + slot_rows, blk_count * slot_cap
    )
    send_table = jnp.full((windows, blk_count * slot_cap + 1), own_blocks * heads, jnp.int32)
    send_table = jax.vmap(set_rows)(
        send_table, target_rows.reshape(windows, -1), source_rows.reshape(windows, -1)
    )[:, : blk_count * slot_cap]
    flat_pairs = jnp.concatenate(
        [
            local_pairs.reshape(windows, own_blocks * heads, block_len, pair_width),
            jnp.zeros((windows, 1, block_len, pair_width), bf16),
        ],
        axis=1,
    )
    outgoing = jax.vmap(take_rows)(flat_pairs, send_table).reshape(
        windows, blk_count, slot_cap, block_len, pair_width
    )
    incoming = lax.all_to_all(outgoing, "blk", split_axis=1, concat_axis=1, tiled=True).reshape(
        windows, blk_count * slot_cap, block_len, pair_width
    )
    rand_pairs = jax.vmap(take_rows)(incoming, fetch_index).reshape(
        windows, own_blocks, heads, picks, block_len, pair_width
    )
    near_pairs = jnp.stack(
        [rimmed[:, 0:own_blocks], rimmed[:, 1 : own_blocks + 1], rimmed[:, 2 : own_blocks + 2]],
        axis=3,
    )
    far_pairs = jnp.broadcast_to(
        glob_pairs.transpose(0, 2, 1, 3, 4)[:, None],
        (windows, own_blocks, heads, glob_count, block_len, pair_width),
    )
    gathered_keys = jnp.concatenate([near_pairs, far_pairs, rand_pairs], axis=3).reshape(
        windows, own_blocks, heads, key_count * block_len, pair_width
    )
    set_keys = gathered_keys[..., :head_dim]
    set_values = gathered_keys[..., head_dim:]
    block_flags = jnp.concatenate(
        [
            (block_ids > 0)[:, None],
            jnp.ones((own_blocks, 1), jnp.bool_),
            (block_ids < blocks - 1)[:, None],
            jnp.ones((own_blocks, glob_count + picks), jnp.bool_),
        ],
        axis=1,
    )
    key_valid = jnp.repeat(block_flags, block_len, axis=1)[None, :, None, None, :]

    def score_block():
        raw_scores = (
            jnp.einsum("wbhqe,wbhke->wbhqk", query_heads, set_keys, preferred_element_type=f32)
            * score_scale
        )
        return jnp.where(key_valid, raw_scores, masked_score)

    score_matrix = score_block()
    top_score = jnp.max(score_matrix, axis=-1, keepdims=True)
    log_total = top_score + jnp.log(
        jnp.sum(jnp.exp(score_matrix - top_score), axis=-1, keepdims=True)
    )
    probs_low = jnp.exp(score_matrix - log_total).astype(bf16)
    attended = jnp.einsum(
        "wbhqk,wbhke->wbhqe", probs_low, set_values, preferred_element_type=f32
    ).astype(bf16)
    merged = from_heads(attended)
    residual = tokens_f + (jnp.dot(merged, w_out, preferred_element_type=f32) + b_out)
    second_f, norm_two_pull = jax.vjp(layer_norm, residual, gain_two, shift_two)
    second = second_f.astype(bf16)
    inner_f = jnp.dot(second, w_up, preferred_element_type=f32) + b_up
    active_f, gelu_pull = jax.vjp(partial(jax.nn.gelu, approximate=False), inner_f)
    active = active_f.astype(bf16)
    output = residual + (jnp.dot(active, w_down, preferred_element_type=f32) + b_down)
    species_count = jnp.sum(
        (species[:, None] == jnp.arange(SPECIES, dtype=jnp.int32)[None, :]).astype(f32), axis=0
    )
    my_species = lax.dynamic_slice_in_dim(species, win_pos * windows, windows)
    own_count = jnp.sum(
        (my_species[:, None] == jnp.arange(SPECIES, dtype=jnp.int32)[None, :]).astype(f32)
        * species_count[None, :],
        axis=1,
    )
    window_scale = jnp.sqrt(species.shape[0] / (SPECIES * own_count))
    upstream = (cotangent.astype(f32) * window_scale[:, None, None]).reshape(all_rows, model_width)
    grad_branch = upstream.astype(bf16)
    grad_w_down = jnp.einsum("tf,td->fd", active, grad_branch, preferred_element_type=f32)
    grad_b_down = jnp.sum(grad_branch, axis=0, dtype=f32)
    grad_active = jnp.einsum("td,fd->tf", grad_branch, w_down, preferred_element_type=f32)
    grad_inner = gelu_pull(grad_active)[0].astype(bf16)
    grad_w_up = jnp.einsum("td,tf->df", second, grad_inner, preferred_element_type=f32)
    grad_b_up = jnp.sum(grad_inner, axis=0, dtype=f32)
    grad_second = jnp.einsum("tf,df->td", grad_inner, w_up, preferred_element_type=f32)
    grad_resid_norm, grad_gain_two, grad_shift_two = norm_two_pull(grad_second)
    grad_resid = upstream + grad_resid_norm
    grad_proj = grad_resid.astype(bf16)
    grad_w_out = jnp.einsum("ti,to->io", merged, grad_proj, preferred_element_type=f32)
    grad_b_out = jnp.sum(grad_proj, axis=0, dtype=f32)
    grad_attended = to_heads(
        jnp.einsum("to,io->ti", grad_proj, w_out, preferred_element_type=f32).astype(bf16)
    )
    probs_full = jnp.exp(score_block() - log_total)
    grad_probs = jnp.einsum(
        "wbhqe,wbhke->wbhqk", grad_attended, set_values, preferred_element_type=f32
    )
    grad_set_values = jnp.einsum(
        "wbhqk,wbhqe->wbhke", probs_full.astype(bf16), grad_attended, preferred_element_type=f32
    )
    row_dot = jnp.sum(probs_full * grad_probs, axis=-1, keepdims=True)
    grad_scores = (probs_full * (grad_probs - row_dot)).astype(bf16)
    grad_query = (
        jnp.einsum("wbhqk,wbhke->wbhqe", grad_scores, set_keys, preferred_element_type=f32)
        * score_scale
    )
    grad_set_keys = (
        jnp.einsum("wbhqk,wbhqe->wbhke", grad_scores, query_heads, preferred_element_type=f32)
        * score_scale
    )
    grad_set = jnp.concatenate([grad_set_keys, grad_set_values], axis=-1).reshape(
        windows, own_blocks, heads, key_count, block_len, pair_width
    )
    extended = (
        jnp.pad(grad_set[:, :, :, 1], ((0, 0), (1, 1), (0, 0), (0, 0), (0, 0)))
        + jnp.pad(grad_set[:, :, :, 0], ((0, 0), (0, 2), (0, 0), (0, 0), (0, 0)))
        + jnp.pad(grad_set[:, :, :, 2], ((0, 0), (2, 0), (0, 0), (0, 0), (0, 0)))
    )
    edge_grads = jnp.concatenate([extended[:, :1], extended[:, own_blocks + 1 :]], axis=1)
    edge_back = padded(edge_grads.astype(jnp.bfloat16), (("blk", 1),), 1).astype(edge_grads.dtype)
    pair_grad = extended[:, 1 : own_blocks + 1]
    pair_grad = pair_grad.at[:, 0].add(edge_back[:, 0]).at[:, own_blocks - 1].add(edge_back[:, 3])
    glob_grad = jnp.sum(grad_set[:, :, :, 3 : 3 + glob_count], axis=1).transpose(0, 2, 1, 3, 4)
    glob_total = lax.psum(glob_grad.astype(jnp.bfloat16), "blk").astype(jnp.float32)
    pair_grad = pair_grad + jnp.einsum(
        "wgb,wghsc->wbhsc", owned_glob.astype(f32), glob_total, precision=lax.Precision.HIGHEST
    )
    rand_grad = grad_set[:, :, :, 3 + glob_count :].reshape(
        windows, per_device, block_len, pair_width
    )
    back_out = jax.vmap(add_rows)(
        jnp.zeros((windows, blk_count * slot_cap, block_len, pair_width), f32),
        fetch_index,
        rand_grad,
    )
    back_in = lax.all_to_all(
        back_out.reshape(windows, blk_count, slot_cap, block_len, pair_width).astype(jnp.bfloat16),
        "blk",
        split_axis=1,
        concat_axis=1,
        tiled=True,
    ).astype(jnp.float32)
    owner_sum = jax.vmap(add_rows)(
        jnp.zeros((windows, own_blocks * heads + 1, block_len, pair_width), f32),
        send_table,
        back_in.reshape(windows, blk_count * slot_cap, block_len, pair_width),
    )
    pair_grad = pair_grad + owner_sum[:, : own_blocks * heads].reshape(
        windows, own_blocks, heads, block_len, pair_width
    )
    grad_keys = from_heads(pair_grad[..., :head_dim].astype(bf16))
    grad_values = from_heads(pair_grad[..., head_dim:].astype(bf16))
    grad_joined = jnp.concatenate(
        [from_heads(grad_query.astype(bf16)), grad_keys, grad_values], axis=1
    )
    grad_w_qkv = jnp.einsum("td,tc->dc", normed, grad_joined, preferred_element_type=f32)
    grad_b_q = jnp.sum(grad_joined[:, :model_width], axis=0, dtype=f32)
    grad_b_v = jnp.sum(grad_joined[:, 2 * model_width :], axis=0, dtype=f32)
    grad_normed = jnp.einsum("tc,dc->td", grad_joined, w_qkv, preferred_element_type=f32)
    grad_tok_norm, grad_gain_one, grad_shift_one = norm_one_pull(grad_normed)
    grad_tokens = (grad_resid + grad_tok_norm).astype(bf16).reshape(windows, length, model_width)
    local_grads = (
        grad_w_qkv,
        grad_b_q,
        grad_b_v,
        grad_w_out,
        grad_b_out,
        grad_gain_one,
        grad_shift_one,
        grad_gain_two,
        grad_shift_two,
        grad_w_up,
        grad_b_up,
        grad_w_down,
        grad_b_down,
    )
    packed_grads = jnp.concatenate(
        [grad_item.reshape(blk_count, -1) for grad_item in local_grads], axis=1
    )
    total_cols = packed_grads.shape[1]
    win_count = lax.axis_size("win")
    pad_cols = -total_cols % win_count
    shard_sum = lax.psum_scatter(
        packed_grads.astype(jnp.bfloat16), "blk", scatter_dimension=0, tiled=True
    ).astype(jnp.float32)
    split_shard = jnp.pad(shard_sum, ((0, 0), (0, pad_cols))).reshape(win_count, -1)
    group_piece = lax.psum_scatter(
        split_shard.astype(jnp.bfloat16), "win", scatter_dimension=0, tiled=True
    ).astype(jnp.float32)
    summed = (
        lax.all_gather(group_piece.astype(jnp.bfloat16), "win", axis=0, tiled=True)
        .astype(group_piece.dtype)
        .reshape(1, -1)[:, :total_cols]
    )
    shards = []
    offset = 0
    for grad_item in local_grads:
        entry_count = grad_item.size // blk_count
        shards.append(
            summed[0, offset : offset + entry_count].reshape(
                (grad_item.shape[0] // blk_count,) + grad_item.shape[1:]
            )
        )
        offset = offset + entry_count
    out_tokens = output.astype(bf16).reshape(windows, length, model_width)
    return (
        out_tokens,
        grad_tokens,
        shards[0],
        shards[1],
        shards[2],
        shards[3],
        shards[4],
        shards[5],
        shards[6],
        shards[7],
        shards[8],
        shards[9],
        shards[10],
        shards[11],
        shards[12],
    )


def layer_step(*arguments):
    windows = arguments[0].shape[0]
    paired = lax.axis_size("blk") == 2 * windows and lax.axis_size("win") == 4 and windows == 4
    return (paired_body if paired else general_body)(*arguments)


def paired_body(
    tokens,
    cotangent,
    w_qkv,
    b_q,
    b_v,
    w_out,
    b_out,
    gain_one,
    shift_one,
    gain_two,
    shift_two,
    w_up,
    b_up,
    w_down,
    b_down,
    rand_owner,
    rand_sub,
    global_ids,
    species,
):
    f32 = jnp.float32
    bf16 = jnp.bfloat16
    win_count = lax.axis_size("win")
    blk_count = lax.axis_size("blk")
    win_pos = lax.axis_index("win")
    blk_pos = lax.axis_index("blk")
    layers, length, width = tokens.shape
    core, layer, side = win_pos % 2, blk_pos // 2, blk_pos % 2
    blocks, heads, picks = rand_owner.shape[1:]
    own_blocks = blocks // blk_count
    half_blocks = blocks // 2
    block_len = length // own_blocks
    head_dim = width // heads
    all_rows = layers * length
    lanes = HEADS_PER_GROUP * head_dim
    groups = heads // HEADS_PER_GROUP
    score_scale = head_dim ** (-0.5)

    def takes(micros):
        return pl.CostEstimate(flops=micros * 1_000_000_000, bytes_accessed=micros * 1_000_000, transcendentals=0)


    rand_size = blocks * heads * picks
    named = jnp.concatenate(
        [
            lax.dynamic_index_in_dim((rand_owner * own_blocks + rand_sub).reshape(layers, rand_size), layer, 0, keepdims=False),
            lax.dynamic_index_in_dim(global_ids, layer, 0, keepdims=False),
        ]
    )
    named = jnp.where(side == core, named, swap(named, 1, 0))

    def place_of(block):
        owner = block // own_blocks
        half = jnp.where(owner % 2 == core, 0, half_blocks)
        return half + ((layer - owner // 2) % layers) * own_blocks + block % own_blocks

    slot = jnp.arange(half_blocks, dtype=jnp.int32)
    slot_block = (((layer - slot // own_blocks) % layers) * 2 + core) * own_blocks + slot % own_blocks
    table = jnp.concatenate(
        [
            place_of(named),
            slot_block,
            place_of(jnp.maximum(slot_block - 1, 0)),
            place_of(jnp.minimum(slot_block + 1, blocks - 1)),
        ]
    )
    sizes = (heads, picks, rand_size, half_blocks)

    tile = length

    def by_rows(columns):
        return pl.BlockSpec((tile, columns), lambda i: (i, 0))

    def by_tile(columns):
        return pl.BlockSpec((tile, columns), lambda i: (tile_order(i), 0))

    def whole(*shape, once=True):
        mode = pl.Buffered(1) if once else None
        return pl.BlockSpec(shape, lambda i: (0,) * len(shape), pipeline_mode=mode)

    scalars = pl.BlockSpec(memory_space=pltpu.SMEM)
    wide = w_up.shape[1]
    params = pltpu.CompilerParams(vmem_limit_bytes=60 << 20)
    row = lambda vector: vector.reshape(1, -1)
    def remote_params(number, mib):
        return pltpu.CompilerParams(vmem_limit_bytes=mib << 20, collective_id=number, has_side_effects=True)

    any_place = pl.BlockSpec(memory_space=pl.ANY)
    hbm = pl.BlockSpec(memory_space=pltpu.HBM)

    def keep(*shape):
        return pltpu.VMEM(shape, bf16)

    copies = pltpu.SemaphoreType.DMA((layers,))
    rows_in, query, key_value, key_value_other = pl.pallas_call(
        partial(front_kernel, score_scale),
        grid=(layers,),
        in_specs=[any_place, whole(1, width), whole(1, width), whole(width, 3 * width), whole(2, width)],
        out_specs=[hbm, pl.BlockSpec((tile, width), lambda i: (arrival_order(i), 0)), hbm, hbm],
        out_shape=[
            jax.ShapeDtypeStruct((all_rows, width), bf16),
            jax.ShapeDtypeStruct((all_rows, width), bf16),
            jax.ShapeDtypeStruct((all_rows, 2 * width), bf16),
            jax.ShapeDtypeStruct((all_rows, 2 * width), bf16),
        ],
        scratch_shapes=[keep(layers, length, width), keep(layers, length, 2 * width)] + [copies] * 6,
        compiler_params=remote_params(1, 48),
        cost_estimate=takes(80),
        name="front",
    )(tokens, row(gain_one), row(shift_one), w_qkv, jnp.stack([b_q, b_v]))

    def lane_group(first):
        return pl.BlockSpec((all_rows, lanes), lambda g: (0, first + g))

    store = pltpu.VMEM((blocks, block_len, lanes), bf16)
    halves = layers // 2
    attended, log_total, cot_even = pl.pallas_call(
        partial(attend_kernel, sizes, blocks, head_dim, (0, 2)),
        grid=(groups,),
        in_specs=[scalars] + [lane_group(0), lane_group(0), lane_group(0), lane_group(groups), lane_group(groups), any_place],
        out_specs=[lane_group(0), pl.BlockSpec((1, half_blocks, lanes), lambda g: (g, 0, 0)), hbm],
        out_shape=[
            jax.ShapeDtypeStruct((all_rows, width), bf16),
            jax.ShapeDtypeStruct((groups, half_blocks, lanes), f32),
            jax.ShapeDtypeStruct((halves, length, width), bf16),
        ],
        scratch_shapes=[store, store] + [pltpu.SemaphoreType.DMA((halves,))] * 2,
        compiler_params=remote_params(4, 56),
        cost_estimate=takes(38),
        name="attend",
    )(table, query, key_value, key_value_other, key_value, key_value_other, cotangent)

    species_count = jnp.sum(
        (species[:, None] == jnp.arange(SPECIES, dtype=jnp.int32)[None, :]).astype(f32), axis=0
    )
    my_window = ((win_pos // 2) * 2 + side) * layers + layer
    my_species = lax.dynamic_index_in_dim(species, my_window, 0, keepdims=False)
    own_count = jnp.sum(
        (my_species == jnp.arange(SPECIES, dtype=jnp.int32)).astype(f32) * species_count
    )
    window_scale = jnp.sqrt(species.shape[0] / (SPECIES * own_count))
    payload = 2 * wide // blk_count + width // blk_count
    payload += -payload % (16 * win_count)
    stays = jax.ShapeDtypeStruct((blk_count, win_count // 2, payload // win_count, width), bf16)
    output, out_last, normal, second_t, attended_t, rstd, active, slope, cot_odd = pl.pallas_call(
        partial(ffn_forward_kernel, 256, (1, 3)),
        grid=(layers,),
        in_specs=[
            by_rows(width), by_rows(width), whole(width, width), whole(1, width), whole(1, width),
            whole(1, width), whole(width, wide), whole(1, wide), whole(wide, width), whole(1, width), any_place,
        ],
        out_specs=[
            by_rows(width), whole(length, width, once=False), by_rows(width), pl.BlockSpec((width, length), lambda i: (0, i)), pl.BlockSpec((width, length), lambda i: (0, i)),
            by_rows(128), by_rows(wide), by_rows(wide), hbm,
        ],
        out_shape=[
            jax.ShapeDtypeStruct((all_rows, width), bf16),
            jax.ShapeDtypeStruct((length, width), bf16),
            jax.ShapeDtypeStruct((all_rows, width), bf16),
            jax.ShapeDtypeStruct((width, all_rows), bf16),
            jax.ShapeDtypeStruct((width, all_rows), bf16),
            jax.ShapeDtypeStruct((all_rows, 128), f32),
            jax.ShapeDtypeStruct((all_rows, wide), bf16),
            jax.ShapeDtypeStruct((all_rows, wide), bf16),
            jax.ShapeDtypeStruct((halves, length, width), bf16),
        ],
        scratch_shapes=[pltpu.SemaphoreType.DMA((halves,))] * 2,
        compiler_params=remote_params(5, 60),
        cost_estimate=takes(35),
        name="ffn_forward",
    )(rows_in, attended, w_out, row(b_out), row(gain_two), row(shift_two), w_up, row(b_up), w_down, row(b_down), cotangent)

    chunks = wide // width

    grad_resid, grad_attended, vec_two, vec_up, early_keep, early_other, out_tokens = pl.pallas_call(
        partial(ffn_back_kernel, chunks, blk_count, (2, 1, 0)),
        grid=(chunks,),
        in_specs=[
            scalars, pl.BlockSpec((all_rows, width), lambda i: (0, i)), pl.BlockSpec((all_rows, width), lambda i: (0, i)),
            pl.BlockSpec((width, width), lambda i: (0, i)), pl.BlockSpec((width, width), lambda i: (i, 0)),
            whole(width, all_rows), whole(all_rows, width), whole(all_rows, 128), whole(width, all_rows), whole(width, width), whole(1, width),
            any_place, any_place, any_place,
        ],
        out_specs=[hbm, hbm, whole(4, width), whole(chunks, width), hbm, hbm, hbm],
        out_shape=[
            jax.ShapeDtypeStruct((all_rows, width), bf16),
            jax.ShapeDtypeStruct((all_rows, width), bf16),
            jax.ShapeDtypeStruct((4, width), f32),
            jax.ShapeDtypeStruct((chunks, width), f32),
            stays,
            stays,
            jax.ShapeDtypeStruct((layers, length, width), bf16),
        ],
        scratch_shapes=[
            keep(layers, length, width),
            keep(all_rows, width),
            keep(width, all_rows),
            keep(all_rows, width),
            pltpu.VMEM((all_rows, width), f32),
            keep(2, blk_count, payload - chunks * width // blk_count - width // 2, width),
            keep(2, 2, width // 2, width),
            pltpu.SemaphoreType.DMA((layers,)),
            pltpu.SemaphoreType.DMA((layers,)),
            pltpu.SemaphoreType.DMA((layers,)),
            pltpu.SemaphoreType.DMA((48,)),
            pltpu.SemaphoreType.DMA((48,)),
            pltpu.SemaphoreType.DMA((2,)),
        ],
        compiler_params=remote_params(3, 63),
        cost_estimate=takes(60),
        name="ffn_back",
    )(
        window_scale.reshape(1), active, slope, w_up, w_down, second_t, normal, rstd, attended_t, w_out, row(gain_two), cot_even, cot_odd, output,
    )
    last_pairs = [(there, here) for here, there in regroup_pairs(win_count, layers, 3)]
    out_last = lax.ppermute(out_last, ("win", "blk"), last_pairs)
    pair = win_pos // 2
    early_rows = payload // win_count
    late_rows = 3 * width // blk_count + 32
    late_size = late_rows // win_count
    cell = (early_rows, width)
    early_keep = early_keep.reshape((2, 2, 2, 2) + cell)
    early_other = early_other.reshape((2, 2, 2, 2) + cell)
    place = jnp.stack([side, pair, side, layer])

    def picked(index):
        return pl.BlockSpec((1, 1, 1, 1) + cell, lambda z, n, p: index(z, n, p) + (0, 0))

    def listed(index):
        return pl.BlockSpec((1, 1) + cell, lambda z, n, p: index(z, n, p) + (0, 0))

    def cells_of(count):
        return [jax.ShapeDtypeStruct((2, 2) + cell, bf16)] * count

    def first_send():
        left = picked(lambda z, n, p: (0, z, 1 - p[0], n))
        right = picked(lambda z, n, p: (1, z, n, 1 - p[1]))
        return pl.pallas_call(
            first_send_kernel,
            grid_spec=pltpu.PrefetchScalarGridSpec(
                num_scalar_prefetch=1, grid=(2, 2), in_specs=[left, left, right, right], out_specs=[listed(lambda z, n, p: (z, n))] * 2
            ),
            out_shape=cells_of(2),
            cost_estimate=takes(3),
            name="first_send",
        )(place, early_keep, early_other, early_keep, early_other)

    def second_send(got_left, got_right):
        specs, operands = [], []
        for far in (0, 1):
            bit = lambda n, p, f=far: p[n] if f == 0 else 1 - p[n]
            left = picked(lambda z, n, p, bit=bit: (0, z, p[0], bit(1, p)))
            right = picked(lambda z, n, p, bit=bit: (1, z, bit(0, p), p[1]))
            specs += [left, left, listed(lambda z, n, p, bit=bit: (z, bit(1, p)))]
            operands += [early_keep, early_other, got_left]
            specs += [right, right, listed(lambda z, n, p, bit=bit: (z, bit(0, p)))]
            operands += [early_keep, early_other, got_right]
        rows_spec = pl.BlockSpec((1,) + cell, lambda z, n, p: (z, 0, 0))
        both_spec = pl.BlockSpec((2, 1) + cell, lambda z, n, p: (0, z, 0, 0))
        return pl.pallas_call(
            second_send_kernel,
            grid_spec=pltpu.PrefetchScalarGridSpec(num_scalar_prefetch=1, grid=(2, 1), in_specs=specs, out_specs=[both_spec, rows_spec, rows_spec]),
            out_shape=cells_of(1) + [jax.ShapeDtypeStruct((2,) + cell, bf16)] * 2,
            cost_estimate=takes(4),
            name="second_send",
        )(place, *operands)

    def third_send(keep, left, right):
        specs = []
        for step in range(layers):
            goal = lambda p, step=step: (p[3] + step) % layers
            specs.append(listed(lambda z, n, p, goal=goal: (goal(p) // 2, goal(p) % 2)))
            specs += [pl.BlockSpec((1,) + cell, lambda z, n, p, goal=goal: (goal(p) % 2, 0, 0))] * 2
        out = pl.BlockSpec(cell, lambda z, n, p: (0, 0))
        return pl.pallas_call(
            third_send_kernel,
            grid_spec=pltpu.PrefetchScalarGridSpec(num_scalar_prefetch=1, grid=(1, 1), in_specs=specs, out_specs=[out] * layers),
            out_shape=[jax.ShapeDtypeStruct(cell, bf16)] * layers,
            cost_estimate=takes(3),
            name="third_send",
        )(place, *[keep, left, right] * layers)

    def to_layer(value, step):
        pairs = [
            (win * blk_count + blk, win * blk_count + (blk + 2 * step) % blk_count)
            for win in range(win_count)
            for blk in range(blk_count)
        ]
        return lax.ppermute(value, ("win", "blk"), pairs)

    first_left, first_right = first_send()
    first_left, first_right = swap(first_left, 0, 1), swap(first_right, 2, 0)

    grad_parts = []
    for group in range(groups):
        after = []
        if group == 1:
            early_kept, send_left, send_right = second_send(first_left, first_right)
            after = [early_kept, out_last]
            second = swap(send_left, 2, 0), swap(send_right, 0, 1)
        if group == 2:
            early_parts = third_send(early_kept, *second)
            after = [early_parts[0]]
            early_parts = [early_parts[0]] + [to_layer(early_parts[n], n) for n in range(1, layers)]

        def column(first):
            return pl.BlockSpec((all_rows, lanes), lambda g, t: (0, first))

        def full(columns):
            return pl.BlockSpec((all_rows, columns), lambda g, t: (0, 0))

        grad_store = pltpu.VMEM((blocks, block_len, lanes), f32)
        glob_store = pltpu.VMEM((2, block_len, lanes), f32)
        dq, own, other = pl.pallas_call(
            partial(attend_back_kernel, sizes, blocks, head_dim, score_scale, group),
            grid_spec=pltpu.PrefetchScalarGridSpec(
                num_scalar_prefetch=1,
                grid=(1,),
                in_specs=[
                    column(group), column(group), column(group), column(groups + group), column(groups + group), column(group),
                    pl.BlockSpec((1, half_blocks, lanes), lambda g, t: (group, 0, 0)),
                    *[any_place] * len(after),
                ],
                out_specs=[full(lanes), full(2 * lanes), full(2 * lanes)],
                scratch_shapes=[store, store, grad_store, grad_store, glob_store, glob_store],
            ),
            out_shape=[jax.ShapeDtypeStruct((all_rows, n * lanes), bf16) for n in (1, 2, 2)],
            compiler_params=params,
            cost_estimate=takes(25),
            name="attend_back",
        )(table, query, key_value, key_value_other, key_value, key_value_other, grad_attended, log_total, *after)
        grad_parts += [dq, own, swap(other, 1, 0) if group < groups - 1 else other]

    def vmem(*shape):
        return pltpu.VMEM(shape, bf16)

    first_shape, mid_shape = (2, 2, 2), (2, 2)
    chain = lambda size: [vmem(*lead, size, width) for lead in (first_shape, mid_shape, mid_shape, (3,), ())]
    grad_tokens, late, early = pl.pallas_call(
        partial(finish_kernel, groups),
        grid=(layers,),
        in_specs=[by_tile(p.shape[1]) for p in grad_parts[:-1]]
        + [any_place, by_tile(width), by_tile(width), whole(1, width), whole(1, width), whole(width, 3 * width), whole(4, width), whole(chunks, width)]
        + [any_place] * layers,
        out_specs=[hbm] * 3,
        out_shape=[
            jax.ShapeDtypeStruct((layers, length, width), bf16),
            jax.ShapeDtypeStruct((win_count, late_size, width), bf16),
            jax.ShapeDtypeStruct((win_count, early_rows, width), bf16),
        ],
        scratch_shapes=[
            vmem(all_rows, 3 * width),
            vmem(layers, width, length),
            pltpu.VMEM((4, width), f32),
            vmem(layers, length, width),
            vmem(2, 2, 2, 2, 2, late_size, width),
            vmem(2, 2, 2, 2, late_size, width),
            chain(late_size),
            [vmem(*lead, early_rows, width) for lead in ((4,), ())],
            pltpu.SemaphoreType.DMA((layers,)),
            pltpu.SemaphoreType.DMA((layers,)),
            pltpu.SemaphoreType.DMA((4,)),
            pltpu.SemaphoreType.DMA((14,)),
            pltpu.SemaphoreType.DMA((14,)),
            pltpu.SemaphoreType.DMA((2,)),
            vmem(layers, length, 2 * lanes),
            pltpu.SemaphoreType.DMA((layers,)),
            pltpu.SemaphoreType.DMA((layers,)),
        ],
        compiler_params=remote_params(2, 62),
        cost_estimate=takes(90),
        name="finish",
    )(
        *grad_parts, rows_in, grad_resid, row(gain_one), row(shift_one), w_qkv, vec_two, vec_up,
        *early_parts,
    )
    part = width // blk_count
    count = wide // width
    done_qkv, done_out, done_up, done_down = pl.pallas_call(
        unpack_kernel,
        out_shape=[
            jax.ShapeDtypeStruct(shape, f32)
            for shape in ((part, 3 * width), (part, width), (part, wide), (wide // blk_count, width))
        ],
        compiler_params=params,
        cost_estimate=takes(4),
        name="unpack",
    )(early, late)
    late = late.reshape(-1, width)[3 * part :].astype(f32)
    vec = lax.dynamic_slice_in_dim(late[:8], blk_pos * part, part, axis=1)
    vec_wide = lax.dynamic_slice_in_dim(late[8 : 8 + count].reshape(-1), blk_pos * (wide // blk_count), wide // blk_count)
    return (
        lax.dynamic_update_index_in_dim(out_tokens, out_last, (layer + 3) % layers, 0),
        grad_tokens,
        done_qkv,
        vec[0],
        vec[1],
        done_out,
        vec[4],
        vec[2],
        vec[3],
        vec[5],
        vec[6],
        done_up,
        vec_wide,
        done_down,
        vec[7],
    )


def solution(mesh):
    placed = (
        P("win", "blk", None),
        P("win", "blk", None),
        P(),
        P(),
        P(),
        P(),
        P(),
        P(),
        P(),
        P(),
        P(),
        P(),
        P(),
        P(),
        P(),
        P("win", None, None, None),
        P("win", None, None, None),
        P("win", None),
        P(),
    )
    return jax.shard_map(
        layer_step,
        mesh=mesh,
        in_specs=placed,
        out_specs=(
            P("win", "blk", None),
            P("win", "blk", None),
            P("blk", None),
            P("blk"),
            P("blk"),
            P("blk", None),
            P("blk"),
            P("blk"),
            P("blk"),
            P("blk"),
            P("blk"),
            P("blk", None),
            P("blk"),
            P("blk", None),
            P("blk"),
        ),
        check_vma=False,
    )
```

```python
from functools import partial

import jax
import jax.numpy as jnp
from jax import lax
from jax.experimental import pallas as pl
from jax.experimental.pallas import tpu as pltpu
from jax.sharding import PartitionSpec as P

SPECIES = 4


epsilon = 1e-05
masked_score = -1000000000.0


def padded(cells, sides, width):
    for axis, dim in sides:
        count = lax.axis_size(axis)
        ends = count - 1
        head = lax.slice_in_dim(cells, 0, width, axis=dim)
        tail = lax.slice_in_dim(cells, cells.shape[dim] - width, cells.shape[dim], axis=dim)
        cells = jnp.concatenate(
            [
                lax.ppermute(tail, axis, [(i, (i + 1) % count) for i in range(ends)]),
                cells,
                lax.ppermute(head, axis, [((i + 1) % count, i) for i in range(ends)]),
            ],
            axis=dim,
        )
    return cells


def layer_norm(values, norm_gain, norm_shift):
    average = jnp.mean(values, axis=-1, keepdims=True)
    centred = values - average
    variance = jnp.mean(centred * centred, axis=-1, keepdims=True)
    return centred * lax.rsqrt(variance + epsilon) * norm_gain + norm_shift


def take_rows(source, index_rows):
    return jnp.take(source, index_rows, axis=0)


def add_rows(base, index_rows, update):
    return base.at[index_rows].add(update)


def set_rows(base, index_rows, update):
    return base.at[index_rows].set(update)


HEADS_PER_GROUP = 4


def regroup_pairs(win_count, layers, step):
    pairs = []
    for win in range(win_count):
        for blk in range(2 * layers):
            layer, side = blk // 2, blk % 2
            target = ((layer + step) % layers) * 2 + win % 2
            pairs.append((win * 2 * layers + blk, ((win // 2) * 2 + side) * 2 * layers + target))
    return pairs


def flip_pairs(win_count, blk_count, win_bit, blk_bit):
    return [
        (win * blk_count + blk, (win ^ win_bit) * blk_count + (blk ^ blk_bit))
        for win in range(win_count)
        for blk in range(blk_count)
    ]


def swap(value, win_bit, blk_bit):
    pairs = flip_pairs(lax.axis_size("win"), lax.axis_size("blk"), win_bit, blk_bit)
    return lax.ppermute(value, ("win", "blk"), pairs)


def head_masks(lanes, head_dim, dtype):
    lane = lax.broadcasted_iota(jnp.int32, (1, lanes), 1)
    return [(lane // head_dim == h).astype(dtype) for h in range(lanes // head_dim)]


def block_places(table, slot, group, sizes):
    heads, picks, rand_size, half_blocks = sizes
    block = table[rand_size + 2 + 2 * half_blocks + slot]
    near = [table[rand_size + 2 + slot], slot, table[rand_size + 2 + half_blocks + slot]]
    row = (block * heads + group * HEADS_PER_GROUP) * picks
    rand = [[table[row + h * picks + r] for h in range(HEADS_PER_GROUP)] for r in range(picks)]
    return block, near, rand


def spread_heads(rows, masks):
    return jnp.concatenate([rows * m for m in masks], axis=0)


def pick_heads(square, masks, height):
    total = square[0:height] * masks[0]
    for h in range(1, len(masks)):
        total = total + square[h * height : (h + 1) * height] * masks[h]
    return total


def key_rows(source, near, glob, rand, low_half):
    parts = [source[p] for p in near] + [source[p] for p in glob]
    for places in rand:
        columns = []
        for c in range(len(places) // 2):
            low = source[places[2 * c], :, c * 128 : (c + 1) * 128]
            high = source[places[2 * c + 1], :, c * 128 : (c + 1) * 128]
            columns.append(jnp.where(low_half, low, high))
        parts.append(jnp.concatenate(columns, axis=1))
    return jnp.concatenate(parts, axis=0)


def mask_scores(scores, block, blocks, block_len):
    first = jnp.where(block > 0, scores[:block_len], masked_score)
    last = jnp.where(block < blocks - 1, scores[2 * block_len : 3 * block_len], masked_score)
    return jnp.concatenate([first, scores[block_len : 2 * block_len], last, scores[3 * block_len :]], axis=0)


def across(left, right):
    return lax.dot_general(left, right, (((1,), (1,)), ((), ())), preferred_element_type=jnp.float32)


def down(left, right):
    return lax.dot_general(left, right, (((0,), (0,)), ((), ())), preferred_element_type=jnp.float32)


def load_halves(target, own, other, half_blocks, block_len):
    lanes = own.shape[-1]
    target[0:half_blocks] = own[...].reshape(half_blocks, block_len, lanes)
    target[half_blocks:] = other[...].reshape(half_blocks, block_len, lanes)


def attend_kernel(
    sizes, blocks, head_dim, cot_tiles,
    table, q_ref, k_own, k_other, v_own, v_other, cotangent,
    o_ref, lse_ref, cot_ref,
    k_all, v_all, send_sems, recv_sems,
):
    heads, picks, rand_size, half_blocks = sizes
    block_len = k_all.shape[1]
    lanes = q_ref.shape[1]
    group = pl.program_id(0)
    _, _, core, layer, _ = position()
    own_blocks = blocks // 8

    @pl.when(group == 0)
    def _():
        greet_owners(4, [])
        for n, tile in enumerate(cot_tiles):
            regroup_move(cotangent, cot_ref.at[n], tile, send_sems.at[n], recv_sems.at[n], True)

    load_halves(k_all, k_own, k_other, half_blocks, block_len)
    load_halves(v_all, v_own, v_other, half_blocks, block_len)
    low_half = lax.broadcasted_iota(jnp.int32, (block_len, 128), 1) < head_dim
    masks = head_masks(lanes, head_dim, jnp.bfloat16)
    masks_f = head_masks(lanes, head_dim, jnp.float32)
    glob = [table[rand_size], table[rand_size + 1]]

    def several(number, carry):
        slots = [number * together + u for u in range(together)]
        places = [block_places(table, slot, group, sizes) for slot in slots]
        numbers = [(((layer + 4 - slot // own_blocks) % 4) * 2 + core) * own_blocks + slot % own_blocks for slot in slots]
        rows = [pl.ds(pl.multiple_of(slot * block_len, block_len), block_len) for slot in slots]
        queries = [spread_heads(q_ref[r, :], masks) for r in rows]
        keys = [key_rows(k_all, near, glob, rand, low_half) for _, near, rand in places]
        scores = [
            mask_scores(across(key, query), block, blocks, block_len) for key, query, block in zip(keys, queries, numbers)
        ]
        tops = [jnp.max(score, axis=0, keepdims=True) for score in scores]
        weights = [jnp.exp(score - top) for score, top in zip(scores, tops)]
        totals = [jnp.sum(weight, axis=0, keepdims=True) for weight in weights]
        probs = [(weight * (1.0 / total)).astype(jnp.bfloat16) for weight, total in zip(weights, totals)]
        values = [key_rows(v_all, near, glob, rand, low_half) for _, near, rand in places]
        for slot, r, prob, value, top, total in zip(slots, rows, probs, values, tops, totals):
            o_ref[r, :] = pick_heads(down(prob, value), masks_f, block_len).astype(jnp.bfloat16)
            lse_ref[0, pl.ds(slot, 1), :] = top + jnp.log(total)
        return carry

    together = 4
    lax.fori_loop(0, half_blocks // together, several, 0, unroll=4)

    @pl.when(group == pl.num_programs(0) - 1)
    def _():
        for n, tile in enumerate(cot_tiles):
            regroup_move(cotangent, cot_ref.at[n], tile, send_sems.at[n], recv_sems.at[n], False)


def attend_back_kernel(
    sizes, blocks, head_dim, scale, group,
    table, q_ref, k_own, k_other, v_own, v_other, go_ref, lse_ref, *refs,
):
    dq_ref, own_ref, other_ref, k_all, v_all, dk_all, dv_all, dk_glob, dv_glob = refs[-9:]
    heads, picks, rand_size, half_blocks = sizes
    block_len = k_all.shape[1]
    lanes = q_ref.shape[1]
    f32 = jnp.float32
    load_halves(k_all, k_own, k_other, half_blocks, block_len)
    load_halves(v_all, v_own, v_other, half_blocks, block_len)
    dk_all[...] = jnp.zeros_like(dk_all)
    dv_all[...] = jnp.zeros_like(dv_all)
    dk_glob[...] = jnp.zeros_like(dk_glob)
    dv_glob[...] = jnp.zeros_like(dv_glob)
    low_half = lax.broadcasted_iota(jnp.int32, (block_len, 128), 1) < head_dim
    masks = head_masks(lanes, head_dim, jnp.bfloat16)
    masks_f = head_masks(lanes, head_dim, f32)
    glob = [table[rand_size], table[rand_size + 1]]

    def add_back(grads, near, rand, into, into_glob):
        for n in range(3):
            into[near[n]] += grads[n * block_len : (n + 1) * block_len]
        for n in range(2):
            into_glob[n] += grads[(3 + n) * block_len : (4 + n) * block_len]
        for r in range(picks):
            part = grads[(5 + r) * block_len : (6 + r) * block_len]
            for c in range(lanes // 128):
                cell = part[:, c * 128 : (c + 1) * 128]
                columns = pl.ds(c * 128, 128)
                into[rand[r][2 * c], :, columns] += jnp.where(low_half, cell, 0.0)
                into[rand[r][2 * c + 1], :, columns] += jnp.where(low_half, 0.0, cell)

    def several(number, carry):
        slots = [number * 2 + u for u in range(2)]
        places = [block_places(table, slot, group, sizes) for slot in slots]
        rows = [pl.ds(pl.multiple_of(slot * block_len, block_len), block_len) for slot in slots]
        queries = [spread_heads(q_ref[r, :], masks) for r in rows]
        keys = [key_rows(k_all, near, glob, rand, low_half) for _, near, rand in places]
        scores = [across(key, query) for key, query in zip(keys, queries)]
        grads_out = [spread_heads(go_ref[r, :], masks) for r in rows]
        values = [key_rows(v_all, near, glob, rand, low_half) for _, near, rand in places]
        grad_probs = [across(value, grad) for value, grad in zip(values, grads_out)]
        probs = [
            jnp.exp(mask_scores(score, block, blocks, block_len) - lse_ref[0, pl.ds(slot, 1), :])
            for score, (block, _, _), slot in zip(scores, places, slots)
        ]
        row_dots = [jnp.sum(prob * grad, axis=0, keepdims=True) for prob, grad in zip(probs, grad_probs)]
        grad_scores = [
            (prob * (grad - dot)).astype(jnp.bfloat16) for prob, grad, dot in zip(probs, grad_probs, row_dots)
        ]
        grad_values = [
            jnp.dot(prob.astype(jnp.bfloat16), grad, preferred_element_type=f32) for prob, grad in zip(probs, grads_out)
        ]
        grad_keys = [jnp.dot(grad, query, preferred_element_type=f32) for grad, query in zip(grad_scores, queries)]
        for r, grad, key in zip(rows, grad_scores, keys):
            dq_ref[r, :] = (pick_heads(down(grad, key), masks_f, block_len) * scale).astype(jnp.bfloat16)
        for grad, key_grad, (_, near, rand) in zip(grad_values, grad_keys, places):
            add_back(grad, near, rand, dv_all, dv_glob)
            add_back(key_grad, near, rand, dk_all, dk_glob)
        return carry

    lax.fori_loop(0, half_blocks // 2, several, 0, unroll=4)
    for n in range(2):
        dk_all[glob[n]] += dk_glob[n]
        dv_all[glob[n]] += dv_glob[n]
    for target, start in ((own_ref, 0), (other_ref, half_blocks)):
        for n, source in enumerate((dk_all, dv_all)):
            cells = source[start : start + half_blocks].astype(jnp.bfloat16)
            target[:, n * lanes : (n + 1) * lanes] = cells.reshape(half_blocks * block_len, lanes)


def norm_parts(values):
    average = jnp.mean(values, axis=-1, keepdims=True)
    centred = values - average
    rstd = lax.rsqrt(jnp.mean(centred * centred, axis=-1, keepdims=True) + epsilon)
    return centred * rstd, rstd


def norm_back(grad, normal, rstd, gain):
    scaled = grad * gain
    first = jnp.mean(scaled, axis=-1, keepdims=True)
    second = jnp.mean(scaled * normal, axis=-1, keepdims=True)
    return rstd * (scaled - first - normal * second)


def normal_parts(values):
    cdf = 0.5 + 0.5 * lax.erf(values * 0.5**0.5)
    return cdf, values * jnp.exp(-0.5 * values * values) * 0.3989422804014327


def column_sum(values):
    return jnp.sum(values, axis=0, keepdims=True)


MESH = pl.DeviceIdType.MESH


def tile_order(number):
    return jnp.where(number == 0, 2, jnp.where(number == 2, 3, jnp.where(number == 3, 0, number)))


def position():
    win, blk = lax.axis_index("win"), lax.axis_index("blk")
    return win, blk, win % 2, blk // 2, blk % 2


def owner_of(tile, layers):
    win, blk, core, layer, side = position()
    return (win // 2) * 2 + side, ((layer + layers - tile) % layers) * 2 + core


def greet_owners(layers, peers):
    barrier = pltpu.get_barrier_semaphore()
    others = len(peers)
    for peer in peers:
        pl.semaphore_signal(barrier, inc=1, device_id=peer, device_id_type=MESH)
    _, _, core, _, side = position()
    for tile in range(1, layers):
        pl.semaphore_signal(barrier, inc=1, device_id=owner_of(tile, layers), device_id_type=MESH)

    @pl.when(side != core)
    def _():
        pl.semaphore_signal(barrier, inc=1, device_id=owner_of(0, layers), device_id_type=MESH)
        pl.semaphore_wait(barrier, layers + others)

    @pl.when(side == core)
    def _():
        pl.semaphore_wait(barrier, layers - 1 + others)


def return_tile(tile, source, target, send_sem, recv_sems, start):
    _, _, core, layer, side = position()
    layers = target.shape[0]
    stays = (tile == 0) & (side == core)

    @pl.when(stays)
    def _():
        move = pltpu.make_async_copy(source, target.at[layer], recv_sems.at[tile])
        move.start() if start else move.wait()

    @pl.when(jnp.logical_not(stays))
    def _():
        move = pltpu.make_async_remote_copy(
            src_ref=source, dst_ref=target.at[layer], send_sem=send_sem, recv_sem=recv_sems.at[tile],
            device_id=owner_of(tile, layers), device_id_type=MESH,
        )
        move.start() if start else move.wait()


def regroup_move(source, target, tile, send_sem, recv_sem, start):
    win, _, core, layer, side = position()
    layers = source.shape[0]
    goal = (layer + tile) % layers
    stays = (tile == 0) & (side == core)

    def local():
        return pltpu.make_async_copy(source.at[goal], target, recv_sem)

    def far():
        return pltpu.make_async_remote_copy(
            src_ref=source.at[goal], dst_ref=target, send_sem=send_sem, recv_sem=recv_sem,
            device_id=((win // 2) * 2 + side, goal * 2 + core), device_id_type=MESH,
        )

    @pl.when(stays)
    def _():
        local().start() if start else local().wait()

    @pl.when(jnp.logical_not(stays))
    def _():
        far().start() if start else far().wait()


def arrival_order(number):
    return jnp.where(number == 2, 3, jnp.where(number == 3, 2, number))


def front_kernel(
    scale, tokens, gain, shift, weight, bias,
    rows_ref, q_ref, kv_ref, other_ref,
    held, kv_rows, send_sems, recv_sems, kv_sems, kv_send, kv_recv, row_sems,
):
    f32, bf16 = jnp.float32, jnp.bfloat16
    step, steps = pl.program_id(0), pl.num_programs(0)
    length, width = held.shape[1:]
    win, blk, core, layer, side = position()
    layers = held.shape[0]
    peer = (win + 1 - 2 * core, blk)

    def token_move(tile, start):
        regroup_move(tokens, held.at[tile], tile, send_sems.at[tile], recv_sems.at[tile], start)

    def rows_of(tile):
        return pl.ds(pl.multiple_of(tile * length, length), length)

    def kv_moves(number):
        tile = arrival_order(number)
        return [
            pltpu.make_async_copy(kv_rows.at[number], kv_ref.at[rows_of(tile)], kv_sems.at[number]),
            pltpu.make_async_copy(held.at[tile], rows_ref.at[rows_of(tile)], row_sems.at[number]),
            pltpu.make_async_remote_copy(
                src_ref=kv_rows.at[number], dst_ref=other_ref.at[rows_of(tile)], send_sem=kv_send.at[number], recv_sem=kv_recv.at[number],
                device_id=peer, device_id_type=MESH,
            ),
        ]

    @pl.when(step == 0)
    def _():
        greet_owners(layers, [peer])
        for n in range(4):
            token_move(arrival_order(n), True)

    tile = arrival_order(step)
    token_move(tile, False)
    normal, _ = norm_parts(held[tile].astype(f32))
    normed = (normal * gain[...] + shift[...]).astype(bf16)

    def part(n):
        return jnp.dot(normed, weight[:, n * width : (n + 1) * width], preferred_element_type=f32)

    kv_rows[step, :, :width] = part(1).astype(bf16)
    kv_rows[step, :, width:] = (part(2) + bias[1:2]).astype(bf16)
    for move in kv_moves(step):
        move.start()
    q_ref[...] = (part(0) + bias[0:1]).astype(bf16) * jnp.asarray(scale, bf16)

    @pl.when(step == steps - 1)
    def _():
        for n in range(4):
            for move in kv_moves(n):
                move.wait()


def ffn_forward_kernel(
    chunk, cot_tiles,
    rows_ref, att_ref, w_out, b_out, gain, shift, w_up, b_up, w_down, b_down, cotangent,
    out_ref, last_ref, normal_ref, second_ref, att_turned_ref, rstd_ref, active_ref, slope_ref, cot_ref,
    send_sems, recv_sems, up_rows, down_rows, load_sems,
):
    f32, bf16 = jnp.float32, jnp.bfloat16
    step, steps = pl.program_id(0), pl.num_programs(0)

    fetch_up = pltpu.make_async_copy(w_up, up_rows, load_sems.at[0])
    fetch_down = pltpu.make_async_copy(w_down, down_rows, load_sems.at[1])

    @pl.when(step == 0)
    def _():
        fetch_up.start()
        fetch_down.start()
        greet_owners(4, [])
        for n, tile in enumerate(cot_tiles):
            regroup_move(cotangent, cot_ref.at[n], tile, send_sems.at[n], recv_sems.at[n], True)

    wide = up_rows.shape[1]
    att = att_ref[...]
    residual = rows_ref[...].astype(f32) + (jnp.dot(att, w_out[...], preferred_element_type=f32) + b_out[...])
    normal, rstd = norm_parts(residual)
    second = (normal * gain[...] + shift[...]).astype(bf16)
    normal_ref[...] = normal.astype(bf16)
    second_ref[...] = second.T
    att_turned_ref[...] = att.T
    rstd_ref[...] = jnp.broadcast_to(rstd, rstd_ref.shape)

    @pl.when(step == 0)
    def _():
        fetch_up.wait()
        fetch_down.wait()

    def raise_part(first):
        part = slice(first, first + chunk)
        return jnp.dot(second, up_rows[:, part], preferred_element_type=f32) + b_up[:, part]

    ahead = raise_part(0)
    for first in range(0, wide, chunk):
        inner = ahead
        if first + chunk < wide:
            ahead = raise_part(first + chunk)
        cdf, slope = normal_parts(inner)
        active_ref[:, first : first + chunk] = (inner * cdf).astype(bf16)
        slope_ref[:, first : first + chunk] = (cdf + slope).astype(bf16)
    total = residual + b_down[...] + jnp.dot(active_ref[...], down_rows[...], preferred_element_type=f32)
    out_ref[...] = total.astype(bf16)

    @pl.when(step == steps - 1)
    def _():
        last_ref[...] = total.astype(bf16)
        for n, tile in enumerate(cot_tiles):
            regroup_move(cotangent, cot_ref.at[n], tile, send_sems.at[n], recv_sems.at[n], False)


def ffn_back_kernel(
    chunks, shards, kept_tiles,
    species, active_ref, slope_ref, w_up, w_down, second_t, gain, normal_in, rstd_in, att_in, w_out_in,
    cot_even, cot_odd, output,
    resid_ref, go_ref, vec_ref, vec_up_ref, keep_ref, other_ref, out_ref,
    cot_rows, branch, branch_t, grad_inner, grad_second, stage_up, stage_down,
    cot_sems, ship_send, ship_recv, cell_send, cell_recv, done_sems, normal_ref, rstd_ref, att_t, w_out, load_sems,
):
    f32, bf16 = jnp.float32, jnp.bfloat16
    step = pl.program_id(0)
    slot = step % 2
    width = w_up.shape[0]
    tiles, length = cot_rows.shape[:2]
    part = width // shards
    half = width // 2
    size = keep_ref.shape[2]
    win, blk, core, _, _ = position()
    peer = (win + 1 - 2 * core, blk)

    def rows_of(n):
        return slice(n * length, (n + 1) * length)

    def ship(what):
        for n, tile in enumerate(kept_tiles):
            return_tile(tile, output.at[rows_of(tile)], out_ref, ship_send.at[n], ship_recv, what)

    def moves(c):
        cuts = []
        if c < chunks:
            base = 4 * c
            for first, count, piece, row in span_cuts(c * part, part, size):
                cuts.append((base + len(cuts), stage_up.at[c % 2, :, pl.ds(first, count)], slice(0, shards), piece, row, count))
            mine = slice(2 * c, 2 * c + 2)
            for first, count, piece, row in span_cuts(chunks * part, half, size):
                cuts.append((24 + base + len(cuts), stage_down.at[c % 2, :, pl.ds(first, count)], mine, piece, row, count))
        else:
            start = chunks * part + half
            for first, count, piece, row in span_cuts(start, 4 * size - start, size):
                cuts.append((20 + len(cuts), stage_up.at[0, :, pl.ds(first, count)], slice(0, shards), piece, row, count))
        return cuts

    def act(c, what):
        for number, source, mine, piece, row, count in moves(c):
            cell = (pl.ds(mine.start, mine.stop - mine.start), piece // 2, pl.ds(row, count))
            def far():
                return pltpu.make_async_remote_copy(
                    src_ref=source, dst_ref=other_ref.at[cell], send_sem=cell_send.at[number], recv_sem=cell_recv.at[number],
                    device_id=peer, device_id_type=MESH,
                )

            @pl.when(core == piece % 2)
            def _():
                if what == "receive":
                    far().wait_recv()
                else:
                    near = pltpu.make_async_copy(source, keep_ref.at[cell], cell_send.at[number])
                    near.start() if what == "start" else near.wait()

            if what != "receive":
                @pl.when(core != piece % 2)
                def _():
                    far().start() if what == "start" else far().wait_send()

    def late_loads():
        pairs = ((normal_in, normal_ref), (rstd_in, rstd_ref), (att_in, att_t), (w_out_in, w_out))
        return [pltpu.make_async_copy(a, b, load_sems.at[n]) for n, (a, b) in enumerate(pairs)]

    windows = species.shape[0]
    mine = species[((win // 2) * 2 + blk % 2) * tiles + blk // 2]
    alike = jnp.zeros((), f32)
    for n in range(windows):
        alike = alike + jnp.where(species[n] == mine, 1.0, 0.0)
    scale = jnp.sqrt(windows / (SPECIES * jnp.full((1, width), alike, f32)))

    def cot_moves():
        return [
            pltpu.make_async_copy((cot_even, cot_odd)[n % 2].at[n // 2], cot_rows.at[n], cot_sems.at[n]) for n in range(4)
        ]

    @pl.when(step == 0)
    def _():
        for move in cot_moves() + late_loads():
            move.start()
        greet_owners(tiles, [peer])
        ship(True)
        vec_ref[...] = jnp.zeros_like(vec_ref)
        for n, move in enumerate(cot_moves()):
            move.wait()
            upstream = cot_rows[n].astype(f32) * scale
            vec_ref[3:4] += column_sum(upstream)
            branch[rows_of(n), :] = upstream.astype(bf16)
            branch_t[:, rows_of(n)] = upstream.astype(bf16).T
        grad_second[...] = jnp.zeros_like(grad_second)

    for c in range(2, chunks):
        @pl.when(step == c)
        def _():
            act(c - 2, "wait")

    full = jnp.dot(branch_t[...], active_ref[...], preferred_element_type=f32)
    for n in range(2):
        for k in range(2):
            stage_down[slot, n, :, k * half : (k + 1) * half] = full[k * half : (k + 1) * half, n * half : (n + 1) * half].astype(bf16)
    total = jnp.zeros((1, w_up.shape[1]), f32)
    for n in range(tiles):
        grad = across(branch[rows_of(n), :], w_down[...]) * slope_ref[rows_of(n), :].astype(f32)
        total = total + column_sum(grad)
        grad_inner[rows_of(n), :] = grad.astype(bf16)
        grad_second[rows_of(n), :] += across(grad_inner[rows_of(n), :], w_up[...])
    vec_up_ref[pl.ds(step, 1), :] = total
    full = jnp.dot(second_t[...], grad_inner[...], preferred_element_type=f32)
    for b in range(shards):
        stage_up[slot, b, 0:part] = full[b * part : (b + 1) * part].astype(bf16)
    for c in range(chunks):
        @pl.when(step == c)
        def _():
            act(c, "start")

    @pl.when(step == chunks - 1)
    def _():
        for move in late_loads():
            move.wait()
        for n in range(tiles):
            upstream = cot_rows[n].astype(f32) * scale
            grad = grad_second[rows_of(n), :]
            normal = normal_ref[rows_of(n), :].astype(f32)
            grad_resid = upstream + norm_back(grad, normal, rstd_ref[rows_of(n), 0:1], gain[...])
            grad_proj = grad_resid.astype(bf16)
            grad_inner[rows_of(n), :] = grad_proj
            branch[rows_of(n), :] = across(grad_proj, w_out[...]).astype(bf16)
            vec_ref[0:1] += column_sum(grad_resid)
            vec_ref[1:2] += column_sum(grad * normal)
            vec_ref[2:3] += column_sum(grad)
        results = [
            pltpu.make_async_copy(grad_inner, resid_ref, done_sems.at[0]),
            pltpu.make_async_copy(branch, go_ref, done_sems.at[1]),
        ]
        for move in results:
            move.start()
        full = jnp.dot(att_t[...], grad_inner[...], preferred_element_type=f32)
        act(chunks - 2, "wait")
        for b in range(shards):
            stage_up[0, b, 0:part] = full[b * part : (b + 1) * part].astype(bf16)
            stage_up[0, b, part:] = jnp.zeros((stage_up.shape[2] - part, width), bf16)
        act(chunks, "start")
        act(chunks - 1, "wait")
        act(chunks, "wait")
        for c in range(chunks + 1):
            act(c, "receive")
        for move in results:
            move.wait()
        ship(False)


def span_cuts(start, count, size):
    cuts, at = [], start
    while at < start + count:
        end = min(start + count, (at // size + 1) * size)
        cuts.append((at - start, end - at, at // size, at % size))
        at = end
    return cuts


def row_cuts(count, part, size):
    cuts = []
    for k in range(count):
        start = k * part
        while start < (k + 1) * part:
            end = min((k + 1) * part, (start // size + 1) * size)
            cuts.append((k, start - k * part, end - start, start // size, start % size))
            start = end
    return cuts


def add_into(target, got):
    target[...] = (target[...].astype(jnp.float32) + got[...].astype(jnp.float32)).astype(jnp.bfloat16)


def finish_kernel(groups, *refs):
    f32, bf16 = jnp.float32, jnp.bfloat16
    parts = refs[: 3 * groups - 1]
    (
        last_other, rows_ref, resid_ref, gain, shift, weight, vec_two, vec_up, early_a, early_b, early_c, early_d,
        tok_ref, late_ref, early_ref,
        joined, turned, vec, out_rows, cells, core_got, late_bufs, early_bufs, send_sems, recv_sems, load_sems, chain_send, chain_recv, keep_sems, last_rows, last_send, last_recv,
    ) = refs[3 * groups - 1 :]
    step, steps = pl.program_id(0), pl.num_programs(0)
    length, width = rows_ref.shape
    lanes = width // groups
    part = width // 8
    win, blk, core, layer, side = position()
    pair = win // 2
    core_peer = (win + 1 - 2 * core, blk)
    pair_peer = (win + 2 - 4 * pair, blk)
    side_peer = (win, blk + 1 - 2 * side)
    layer_peers = [(win, ((layer + n) % 4) * 2 + side) for n in (1, 2, 3)]

    def remote(source, target, number, peer):
        return pltpu.make_async_remote_copy(
            src_ref=source, dst_ref=target, send_sem=chain_send.at[number], recv_sem=chain_recv.at[number],
            device_id=peer, device_id_type=MESH,
        )

    early_got, early_final = early_bufs

    def loads():
        return [
            pltpu.make_async_copy(source, early_got.at[n], load_sems.at[n])
            for n, source in enumerate((early_a, early_b, early_c, early_d))
        ]

    def second_step(state, got, base):
        return [
            remote(state.at[0, :, 1 - pair], got.at[0], base, pair_peer),
            remote(state.at[1, :, 1 - side], got.at[1], base + 1, side_peer),
        ]

    def add_second(state, got, mid):
        for z in range(2):
            mid[0, z] = (state[0, z, pair].astype(f32) + got[0, z].astype(f32)).astype(bf16)
            mid[1, z] = (state[1, z, side].astype(f32) + got[1, z].astype(f32)).astype(bf16)

    def layer_step(mid, got, base):
        moves = []
        for n in range(3):
            other = (layer + n + 1) % 4
            moves.append(remote(mid.at[other // 2, other % 2], got.at[n], base + n, layer_peers[n]))
        return moves

    def sum_into(final, parts):
        total = parts[0].astype(f32)
        for one in parts[1:]:
            total = total + one.astype(f32)
        final[...] = total.astype(bf16)

    def share(final, target, base):
        return [
            remote(final, target.at[win], base, core_peer),
            remote(final, target.at[win], base + 1, pair_peer),
        ]

    def pass_on(target, base):
        return [remote(target.at[win + 2 - 4 * pair], target.at[win + 2 - 4 * pair], base, core_peer)]

    def start(moves):
        for move in moves:
            move.start()

    def wait(moves):
        for move in moves:
            move.wait()

    def last_move(number):
        first = pl.multiple_of(tile_order(number) * length, length)
        return pltpu.make_async_remote_copy(
            src_ref=last_other.at[pl.ds(first, length)], dst_ref=last_rows.at[number], send_sem=last_send.at[number],
            recv_sem=last_recv.at[number], device_id=core_peer, device_id_type=MESH,
        )

    late_first, late_second, late_mid, late_got, late_final = late_bufs
    early_base, late_base = 8, 0

    @pl.when(step == 0)
    def _():
        start(loads())
        greet_owners(steps, [core_peer, pair_peer, side_peer] + layer_peers)
        for n in range(4):
            last_move(n).start()
        vec[...] = jnp.zeros_like(vec)

    tile = tile_order(step)
    rows = pl.ds(pl.multiple_of(tile * length, length), length)
    last_move(step).wait()
    for g in range(groups):
        dq, own = parts[3 * g : 3 * g + 2]
        other = parts[3 * g + 2] if g < groups - 1 else last_rows.at[step]
        columns = slice(g * lanes, (g + 1) * lanes)
        joined[rows, columns] = dq[...]
        both = (own[...].astype(f32) + other[...].astype(f32)).astype(bf16)
        joined[rows, width + g * lanes : width + (g + 1) * lanes] = both[:, :lanes]
        joined[rows, 2 * width + g * lanes : 2 * width + (g + 1) * lanes] = both[:, lanes:]
        vec[0:1, columns] += column_sum(dq[...].astype(f32))
        vec[1:2, columns] += column_sum(both[:, lanes:].astype(f32))
    grad = across(joined[rows, :], weight[...])
    normal, rstd = norm_parts(rows_ref[...].astype(f32))
    turned[tile] = (normal * gain[...] + shift[...]).astype(bf16).T
    vec[2:3] += column_sum(grad * normal)
    vec[3:4] += column_sum(grad)
    out_rows[step] = (resid_ref[...].astype(f32) + norm_back(grad, normal, rstd, gain[...])).astype(bf16)
    return_tile(tile, out_rows.at[step], tok_ref, send_sems.at[step], recv_sems, True)

    @pl.when(step == 0)
    def _():
        wait(loads())
        sum_into(early_final, [early_got[n] for n in range(4)])
        start(share(early_final, early_ref, early_base))
        pltpu.make_async_copy(early_final, early_ref.at[win], keep_sems.at[0]).start()

    @pl.when(step == steps - 1)
    def _():
        size = cells.shape[5]
        cuts = row_cuts(3, part, size)
        for k in range(3):
            full = jnp.dot(turned[0], joined[0:length, k * width : (k + 1) * width], preferred_element_type=f32)
            for n in range(1, 4):
                full = full + jnp.dot(
                    turned[n], joined[n * length : (n + 1) * length, k * width : (k + 1) * width], preferred_element_type=f32
                )
            for b in range(8):
                for which, first, count, piece, row in cuts:
                    if which == k:
                        cells[piece % 2, b // 4, b // 2 % 2, b % 2, piece // 2, row : row + count] = full[
                            b * part + first : b * part + first + count
                        ].astype(bf16)
        tail = jnp.concatenate(
            [vec[...], vec_two[...], vec_up[...]]
            + [jnp.zeros((4 * size - 3 * part - 12, width), f32)],
            axis=0,
        ).astype(bf16)
        for b in range(8):
            cells[1, b // 4, b // 2 % 2, b % 2, 1, 3 * part - 3 * size :] = tail
        exchange = [remote(cells.at[1 - core], core_got, late_base, core_peer)]
        start(exchange)
        wait(share(early_final, early_ref, early_base))
        start(pass_on(early_ref, early_base + 2))
        wait(exchange)
        mine = cells.at[core]
        for b in range(8):
            for x in range(2):
                add_into(mine.at[b // 4, b // 2 % 2, b % 2, x], core_got.at[b // 4, b // 2 % 2, b % 2, x])
        first = [
            remote(mine.at[0, :, 1 - side], late_first.at[0], late_base + 1, side_peer),
            remote(mine.at[1, :, :, 1 - pair], late_first.at[1], late_base + 2, pair_peer),
        ]
        start(first)
        wait(first)
        state = core_got.at[0]
        for z in range(2):
            for n in range(2):
                state[0, z, n] = (mine[0, z, side, n].astype(f32) + late_first[0, z, n].astype(f32)).astype(bf16)
                state[1, z, n] = (mine[1, z, n, pair].astype(f32) + late_first[1, z, n].astype(f32)).astype(bf16)
        start(second_step(state, late_second, late_base + 3))
        wait(second_step(state, late_second, late_base + 3))
        add_second(state, late_second, late_mid)
        across_layers = layer_step(late_mid, late_got, late_base + 5)
        start(across_layers)
        wait(across_layers)
        sum_into(late_final, [late_mid[layer // 2, layer % 2]] + [late_got[n] for n in range(3)])
        start(share(late_final, late_ref, early_base + 3))
        keep_late = pltpu.make_async_copy(late_final, late_ref.at[win], keep_sems.at[1])
        keep_late.start()
        wait(share(late_final, late_ref, early_base + 3))
        start(pass_on(late_ref, early_base + 5))
        wait(pass_on(early_ref, early_base + 2))
        wait(pass_on(late_ref, early_base + 5))
        pltpu.make_async_copy(early_final, early_ref.at[win], keep_sems.at[0]).wait()
        keep_late.wait()
        for n in range(4):
            return_tile(tile_order(n), out_rows.at[n], tok_ref, send_sems.at[n], recv_sems, False)


def first_send_kernel(place, keep_left, other_left, keep_right, other_right, left_ref, right_ref):
    for keep, other, target in ((keep_left, other_left, left_ref), (keep_right, other_right, right_ref)):
        target[...] = (keep[...].astype(jnp.float32) + other[...].astype(jnp.float32)).astype(jnp.bfloat16).reshape(target.shape)


def sum_low(target, refs):
    total = refs[0][...].astype(jnp.float32)
    for ref in refs[1:]:
        total = total + ref[...].astype(jnp.float32)
    target[...] = total.astype(jnp.bfloat16).reshape(target.shape)


def second_send_kernel(place, *refs):
    keep, left, right = refs[12:]
    for n, target in enumerate((keep.at[0], keep.at[1], left, right)):
        sum_low(target, refs[3 * n : 3 * n + 3])


def third_send_kernel(place, *refs):
    for n in range(4):
        keep, left, right = refs[3 * n : 3 * n + 3]
        in_left = (place[3] + n) % 4 < 2
        got = jnp.where(in_left, left[...].astype(jnp.float32), right[...].astype(jnp.float32))
        target = refs[12 + n]
        target[...] = (keep[...].reshape(target.shape).astype(jnp.float32) + got.reshape(target.shape)).astype(jnp.bfloat16)


def unpack_kernel(early, late, qkv_ref, out_ref, up_ref, down_ref):
    f32 = jnp.float32
    part, width = out_ref.shape
    count = up_ref.shape[1] // width
    half = width // 2

    def cells(source, first, rows):
        size = source.shape[1]
        parts = []
        while rows > 0:
            take = min(rows, size - first % size)
            parts.append(source[first // size, first % size : first % size + take])
            first, rows = first + take, rows - take
        return (parts[0] if len(parts) == 1 else jnp.concatenate(parts, axis=0)).astype(f32)

    for k in range(3):
        qkv_ref[:, k * width : (k + 1) * width] = cells(late, k * part, part)
    for k in range(count):
        up_ref[:, k * width : (k + 1) * width] = cells(early, k * part, part)
    turned = cells(early, count * part, half)
    down_ref[:, :half] = turned[:, :half].T
    down_ref[:, half:] = turned[:, half:].T
    out_ref[...] = cells(early, count * part + half, part)


def general_body(
    tokens,
    cotangent,
    w_qkv,
    b_q,
    b_v,
    w_out,
    b_out,
    gain_one,
    shift_one,
    gain_two,
    shift_two,
    w_up,
    b_up,
    w_down,
    b_down,
    rand_owner,
    rand_sub,
    global_ids,
    species,
):
    blk_count = lax.axis_size("blk")
    blk_pos = lax.axis_index("blk")
    win_pos = lax.axis_index("win")
    windows, length, model_width = tokens.shape
    blocks = rand_owner.shape[1]
    heads = rand_owner.shape[2]
    picks = rand_owner.shape[3]
    glob_count = global_ids.shape[1]
    own_blocks = blocks // blk_count
    block_len = length // own_blocks
    head_dim = model_width // heads
    pair_width = 2 * head_dim
    all_rows = windows * length
    key_count = 3 + glob_count + picks
    per_device = own_blocks * heads * picks
    slot_cap = max(2, 2 * per_device // blk_count)
    score_scale = head_dim ** (-0.5)
    f32 = jnp.float32
    bf16 = jnp.bfloat16
    tokens_f = tokens.reshape(all_rows, model_width).astype(f32)
    normed_f, norm_one_pull = jax.vjp(layer_norm, tokens_f, gain_one, shift_one)
    normed = normed_f.astype(bf16)
    joined = jnp.dot(normed, w_qkv, preferred_element_type=f32)
    query_vals = (joined[:, :model_width] + b_q).astype(bf16)
    key_vals = joined[:, model_width : 2 * model_width].astype(bf16)
    value_vals = (joined[:, 2 * model_width :] + b_v).astype(bf16)

    def to_heads(tensor):
        return tensor.reshape(windows, own_blocks, block_len, heads, head_dim).transpose(
            0, 1, 3, 2, 4
        )

    def from_heads(tensor):
        return tensor.transpose(0, 1, 3, 2, 4).reshape(all_rows, model_width)

    query_heads = to_heads(query_vals)
    local_pairs = jnp.concatenate([to_heads(key_vals), to_heads(value_vals)], axis=-1)
    rimmed = padded(local_pairs, (("blk", 1),), 1)
    block_ids = blk_pos * own_blocks + jnp.arange(own_blocks, dtype=jnp.int32)
    owned_glob = (global_ids[:, :, None] == block_ids[None, None, :]).astype(bf16)
    glob_terms = jnp.einsum("wgb,wbhsc->wghsc", owned_glob, local_pairs, preferred_element_type=f32)
    glob_pairs = lax.psum(glob_terms.astype(jnp.bfloat16), "blk").astype(jnp.float32).astype(bf16)
    owner_rows = rand_owner.reshape(windows, blk_count, per_device)
    sub_rows = rand_sub.reshape(windows, blk_count, per_device)
    owner_hits = (owner_rows[..., None] == jnp.arange(blk_count, dtype=jnp.int32)).astype(jnp.int32)
    slot_rows = jnp.sum(owner_hits * (jnp.cumsum(owner_hits, axis=2) - 1), axis=-1)
    my_owner = lax.dynamic_index_in_dim(owner_rows, blk_pos, 1, keepdims=False)
    my_slot = lax.dynamic_index_in_dim(slot_rows, blk_pos, 1, keepdims=False)
    fetch_index = my_owner * slot_cap + my_slot
    head_of_row = jnp.arange(per_device, dtype=jnp.int32) // picks % heads
    source_rows = sub_rows * heads + head_of_row[None, None, :]
    requester = jnp.arange(blk_count, dtype=jnp.int32)[None, :, None]
    target_rows = jnp.where(
        owner_rows == blk_pos, requester * slot_cap + slot_rows, blk_count * slot_cap
    )
    send_table = jnp.full((windows, blk_count * slot_cap + 1), own_blocks * heads, jnp.int32)
    send_table = jax.vmap(set_rows)(
        send_table, target_rows.reshape(windows, -1), source_rows.reshape(windows, -1)
    )[:, : blk_count * slot_cap]
    flat_pairs = jnp.concatenate(
        [
            local_pairs.reshape(windows, own_blocks * heads, block_len, pair_width),
            jnp.zeros((windows, 1, block_len, pair_width), bf16),
        ],
        axis=1,
    )
    outgoing = jax.vmap(take_rows)(flat_pairs, send_table).reshape(
        windows, blk_count, slot_cap, block_len, pair_width
    )
    incoming = lax.all_to_all(outgoing, "blk", split_axis=1, concat_axis=1, tiled=True).reshape(
        windows, blk_count * slot_cap, block_len, pair_width
    )
    rand_pairs = jax.vmap(take_rows)(incoming, fetch_index).reshape(
        windows, own_blocks, heads, picks, block_len, pair_width
    )
    near_pairs = jnp.stack(
        [rimmed[:, 0:own_blocks], rimmed[:, 1 : own_blocks + 1], rimmed[:, 2 : own_blocks + 2]],
        axis=3,
    )
    far_pairs = jnp.broadcast_to(
        glob_pairs.transpose(0, 2, 1, 3, 4)[:, None],
        (windows, own_blocks, heads, glob_count, block_len, pair_width),
    )
    gathered_keys = jnp.concatenate([near_pairs, far_pairs, rand_pairs], axis=3).reshape(
        windows, own_blocks, heads, key_count * block_len, pair_width
    )
    set_keys = gathered_keys[..., :head_dim]
    set_values = gathered_keys[..., head_dim:]
    block_flags = jnp.concatenate(
        [
            (block_ids > 0)[:, None],
            jnp.ones((own_blocks, 1), jnp.bool_),
            (block_ids < blocks - 1)[:, None],
            jnp.ones((own_blocks, glob_count + picks), jnp.bool_),
        ],
        axis=1,
    )
    key_valid = jnp.repeat(block_flags, block_len, axis=1)[None, :, None, None, :]

    def score_block():
        raw_scores = (
            jnp.einsum("wbhqe,wbhke->wbhqk", query_heads, set_keys, preferred_element_type=f32)
            * score_scale
        )
        return jnp.where(key_valid, raw_scores, masked_score)

    score_matrix = score_block()
    top_score = jnp.max(score_matrix, axis=-1, keepdims=True)
    log_total = top_score + jnp.log(
        jnp.sum(jnp.exp(score_matrix - top_score), axis=-1, keepdims=True)
    )
    probs_low = jnp.exp(score_matrix - log_total).astype(bf16)
    attended = jnp.einsum(
        "wbhqk,wbhke->wbhqe", probs_low, set_values, preferred_element_type=f32
    ).astype(bf16)
    merged = from_heads(attended)
    residual = tokens_f + (jnp.dot(merged, w_out, preferred_element_type=f32) + b_out)
    second_f, norm_two_pull = jax.vjp(layer_norm, residual, gain_two, shift_two)
    second = second_f.astype(bf16)
    inner_f = jnp.dot(second, w_up, preferred_element_type=f32) + b_up
    active_f, gelu_pull = jax.vjp(partial(jax.nn.gelu, approximate=False), inner_f)
    active = active_f.astype(bf16)
    output = residual + (jnp.dot(active, w_down, preferred_element_type=f32) + b_down)
    species_count = jnp.sum(
        (species[:, None] == jnp.arange(SPECIES, dtype=jnp.int32)[None, :]).astype(f32), axis=0
    )
    my_species = lax.dynamic_slice_in_dim(species, win_pos * windows, windows)
    own_count = jnp.sum(
        (my_species[:, None] == jnp.arange(SPECIES, dtype=jnp.int32)[None, :]).astype(f32)
        * species_count[None, :],
        axis=1,
    )
    window_scale = jnp.sqrt(species.shape[0] / (SPECIES * own_count))
    upstream = (cotangent.astype(f32) * window_scale[:, None, None]).reshape(all_rows, model_width)
    grad_branch = upstream.astype(bf16)
    grad_w_down = jnp.einsum("tf,td->fd", active, grad_branch, preferred_element_type=f32)
    grad_b_down = jnp.sum(grad_branch, axis=0, dtype=f32)
    grad_active = jnp.einsum("td,fd->tf", grad_branch, w_down, preferred_element_type=f32)
    grad_inner = gelu_pull(grad_active)[0].astype(bf16)
    grad_w_up = jnp.einsum("td,tf->df", second, grad_inner, preferred_element_type=f32)
    grad_b_up = jnp.sum(grad_inner, axis=0, dtype=f32)
    grad_second = jnp.einsum("tf,df->td", grad_inner, w_up, preferred_element_type=f32)
    grad_resid_norm, grad_gain_two, grad_shift_two = norm_two_pull(grad_second)
    grad_resid = upstream + grad_resid_norm
    grad_proj = grad_resid.astype(bf16)
    grad_w_out = jnp.einsum("ti,to->io", merged, grad_proj, preferred_element_type=f32)
    grad_b_out = jnp.sum(grad_proj, axis=0, dtype=f32)
    grad_attended = to_heads(
        jnp.einsum("to,io->ti", grad_proj, w_out, preferred_element_type=f32).astype(bf16)
    )
    probs_full = jnp.exp(score_block() - log_total)
    grad_probs = jnp.einsum(
        "wbhqe,wbhke->wbhqk", grad_attended, set_values, preferred_element_type=f32
    )
    grad_set_values = jnp.einsum(
        "wbhqk,wbhqe->wbhke", probs_full.astype(bf16), grad_attended, preferred_element_type=f32
    )
    row_dot = jnp.sum(probs_full * grad_probs, axis=-1, keepdims=True)
    grad_scores = (probs_full * (grad_probs - row_dot)).astype(bf16)
    grad_query = (
        jnp.einsum("wbhqk,wbhke->wbhqe", grad_scores, set_keys, preferred_element_type=f32)
        * score_scale
    )
    grad_set_keys = (
        jnp.einsum("wbhqk,wbhqe->wbhke", grad_scores, query_heads, preferred_element_type=f32)
        * score_scale
    )
    grad_set = jnp.concatenate([grad_set_keys, grad_set_values], axis=-1).reshape(
        windows, own_blocks, heads, key_count, block_len, pair_width
    )
    extended = (
        jnp.pad(grad_set[:, :, :, 1], ((0, 0), (1, 1), (0, 0), (0, 0), (0, 0)))
        + jnp.pad(grad_set[:, :, :, 0], ((0, 0), (0, 2), (0, 0), (0, 0), (0, 0)))
        + jnp.pad(grad_set[:, :, :, 2], ((0, 0), (2, 0), (0, 0), (0, 0), (0, 0)))
    )
    edge_grads = jnp.concatenate([extended[:, :1], extended[:, own_blocks + 1 :]], axis=1)
    edge_back = padded(edge_grads.astype(jnp.bfloat16), (("blk", 1),), 1).astype(edge_grads.dtype)
    pair_grad = extended[:, 1 : own_blocks + 1]
    pair_grad = pair_grad.at[:, 0].add(edge_back[:, 0]).at[:, own_blocks - 1].add(edge_back[:, 3])
    glob_grad = jnp.sum(grad_set[:, :, :, 3 : 3 + glob_count], axis=1).transpose(0, 2, 1, 3, 4)
    glob_total = lax.psum(glob_grad.astype(jnp.bfloat16), "blk").astype(jnp.float32)
    pair_grad = pair_grad + jnp.einsum(
        "wgb,wghsc->wbhsc", owned_glob.astype(f32), glob_total, precision=lax.Precision.HIGHEST
    )
    rand_grad = grad_set[:, :, :, 3 + glob_count :].reshape(
        windows, per_device, block_len, pair_width
    )
    back_out = jax.vmap(add_rows)(
        jnp.zeros((windows, blk_count * slot_cap, block_len, pair_width), f32),
        fetch_index,
        rand_grad,
    )
    back_in = lax.all_to_all(
        back_out.reshape(windows, blk_count, slot_cap, block_len, pair_width).astype(jnp.bfloat16),
        "blk",
        split_axis=1,
        concat_axis=1,
        tiled=True,
    ).astype(jnp.float32)
    owner_sum = jax.vmap(add_rows)(
        jnp.zeros((windows, own_blocks * heads + 1, block_len, pair_width), f32),
        send_table,
        back_in.reshape(windows, blk_count * slot_cap, block_len, pair_width),
    )
    pair_grad = pair_grad + owner_sum[:, : own_blocks * heads].reshape(
        windows, own_blocks, heads, block_len, pair_width
    )
    grad_keys = from_heads(pair_grad[..., :head_dim].astype(bf16))
    grad_values = from_heads(pair_grad[..., head_dim:].astype(bf16))
    grad_joined = jnp.concatenate(
        [from_heads(grad_query.astype(bf16)), grad_keys, grad_values], axis=1
    )
    grad_w_qkv = jnp.einsum("td,tc->dc", normed, grad_joined, preferred_element_type=f32)
    grad_b_q = jnp.sum(grad_joined[:, :model_width], axis=0, dtype=f32)
    grad_b_v = jnp.sum(grad_joined[:, 2 * model_width :], axis=0, dtype=f32)
    grad_normed = jnp.einsum("tc,dc->td", grad_joined, w_qkv, preferred_element_type=f32)
    grad_tok_norm, grad_gain_one, grad_shift_one = norm_one_pull(grad_normed)
    grad_tokens = (grad_resid + grad_tok_norm).astype(bf16).reshape(windows, length, model_width)
    local_grads = (
        grad_w_qkv,
        grad_b_q,
        grad_b_v,
        grad_w_out,
        grad_b_out,
        grad_gain_one,
        grad_shift_one,
        grad_gain_two,
        grad_shift_two,
        grad_w_up,
        grad_b_up,
        grad_w_down,
        grad_b_down,
    )
    packed_grads = jnp.concatenate(
        [grad_item.reshape(blk_count, -1) for grad_item in local_grads], axis=1
    )
    total_cols = packed_grads.shape[1]
    win_count = lax.axis_size("win")
    pad_cols = -total_cols % win_count
    shard_sum = lax.psum_scatter(
        packed_grads.astype(jnp.bfloat16), "blk", scatter_dimension=0, tiled=True
    ).astype(jnp.float32)
    split_shard = jnp.pad(shard_sum, ((0, 0), (0, pad_cols))).reshape(win_count, -1)
    group_piece = lax.psum_scatter(
        split_shard.astype(jnp.bfloat16), "win", scatter_dimension=0, tiled=True
    ).astype(jnp.float32)
    summed = (
        lax.all_gather(group_piece.astype(jnp.bfloat16), "win", axis=0, tiled=True)
        .astype(group_piece.dtype)
        .reshape(1, -1)[:, :total_cols]
    )
    shards = []
    offset = 0
    for grad_item in local_grads:
        entry_count = grad_item.size // blk_count
        shards.append(
            summed[0, offset : offset + entry_count].reshape(
                (grad_item.shape[0] // blk_count,) + grad_item.shape[1:]
            )
        )
        offset = offset + entry_count
    out_tokens = output.astype(bf16).reshape(windows, length, model_width)
    return (
        out_tokens,
        grad_tokens,
        shards[0],
        shards[1],
        shards[2],
        shards[3],
        shards[4],
        shards[5],
        shards[6],
        shards[7],
        shards[8],
        shards[9],
        shards[10],
        shards[11],
        shards[12],
    )


def layer_step(*arguments):
    windows = arguments[0].shape[0]
    paired = lax.axis_size("blk") == 2 * windows and lax.axis_size("win") == 4 and windows == 4
    return (paired_body if paired else general_body)(*arguments)


def paired_body(
    tokens,
    cotangent,
    w_qkv,
    b_q,
    b_v,
    w_out,
    b_out,
    gain_one,
    shift_one,
    gain_two,
    shift_two,
    w_up,
    b_up,
    w_down,
    b_down,
    rand_owner,
    rand_sub,
    global_ids,
    species,
):
    f32 = jnp.float32
    bf16 = jnp.bfloat16
    win_count = lax.axis_size("win")
    blk_count = lax.axis_size("blk")
    win_pos = lax.axis_index("win")
    blk_pos = lax.axis_index("blk")
    layers, length, width = tokens.shape
    core, layer, side = win_pos % 2, blk_pos // 2, blk_pos % 2
    blocks, heads, picks = rand_owner.shape[1:]
    own_blocks = blocks // blk_count
    half_blocks = blocks // 2
    block_len = length // own_blocks
    head_dim = width // heads
    all_rows = layers * length
    lanes = HEADS_PER_GROUP * head_dim
    groups = heads // HEADS_PER_GROUP
    score_scale = head_dim ** (-0.5)

    def takes(micros):
        return pl.CostEstimate(flops=micros * 1_000_000_000, bytes_accessed=micros * 1_000_000, transcendentals=0)


    rand_size = blocks * heads * picks
    named = jnp.concatenate(
        [
            lax.dynamic_index_in_dim((rand_owner * own_blocks + rand_sub).reshape(layers, rand_size), layer, 0, keepdims=False),
            lax.dynamic_index_in_dim(global_ids, layer, 0, keepdims=False),
        ]
    )
    slot = jnp.arange(half_blocks, dtype=jnp.int32)

    def table_for(which):
        block = (((layer - slot // own_blocks) % layers) * 2 + which) * own_blocks + slot % own_blocks
        reads = jnp.concatenate([named, jnp.maximum(block - 1, 0), jnp.minimum(block + 1, blocks - 1)])
        owner = reads // own_blocks
        half = jnp.where(owner % 2 == which, 0, half_blocks)
        places = half + ((layer - owner // 2) % layers) * own_blocks + reads % own_blocks
        return jnp.concatenate([places, block])

    table = jnp.where(side == core, table_for(core), swap(table_for(1 - core), 1, 0))
    sizes = (heads, picks, rand_size, half_blocks)

    tile = length

    def by_rows(columns):
        return pl.BlockSpec((tile, columns), lambda i: (i, 0))

    def by_tile(columns):
        return pl.BlockSpec((tile, columns), lambda i: (tile_order(i), 0))

    def whole(*shape, once=True):
        mode = pl.Buffered(1) if once else None
        return pl.BlockSpec(shape, lambda i: (0,) * len(shape), pipeline_mode=mode)

    scalars = pl.BlockSpec(memory_space=pltpu.SMEM)
    wide = w_up.shape[1]
    params = pltpu.CompilerParams(vmem_limit_bytes=60 << 20)
    row = lambda vector: vector.reshape(1, -1)
    def remote_params(number, mib):
        return pltpu.CompilerParams(vmem_limit_bytes=mib << 20, collective_id=number, has_side_effects=True)

    any_place = pl.BlockSpec(memory_space=pl.ANY)
    hbm = pl.BlockSpec(memory_space=pltpu.HBM)

    def keep(*shape):
        return pltpu.VMEM(shape, bf16)

    copies = pltpu.SemaphoreType.DMA((layers,))
    rows_in, query, key_value, key_value_other = pl.pallas_call(
        partial(front_kernel, score_scale),
        grid=(layers,),
        in_specs=[any_place, whole(1, width), whole(1, width), whole(width, 3 * width), whole(2, width)],
        out_specs=[hbm, pl.BlockSpec((tile, width), lambda i: (arrival_order(i), 0)), hbm, hbm],
        out_shape=[
            jax.ShapeDtypeStruct((all_rows, width), bf16),
            jax.ShapeDtypeStruct((all_rows, width), bf16),
            jax.ShapeDtypeStruct((all_rows, 2 * width), bf16),
            jax.ShapeDtypeStruct((all_rows, 2 * width), bf16),
        ],
        scratch_shapes=[keep(layers, length, width), keep(layers, length, 2 * width)] + [copies] * 6,
        compiler_params=remote_params(1, 48),
        cost_estimate=takes(80),
        name="front",
    )(tokens, row(gain_one), row(shift_one), w_qkv, jnp.stack([b_q, b_v]))

    def lane_group(first):
        return pl.BlockSpec((all_rows, lanes), lambda g: (0, first + g))

    store = pltpu.VMEM((blocks, block_len, lanes), bf16)
    halves = layers // 2
    attended, log_total, cot_even = pl.pallas_call(
        partial(attend_kernel, sizes, blocks, head_dim, (0, 2)),
        grid=(groups,),
        in_specs=[scalars] + [lane_group(0), lane_group(0), lane_group(0), lane_group(groups), lane_group(groups), any_place],
        out_specs=[lane_group(0), pl.BlockSpec((1, half_blocks, lanes), lambda g: (g, 0, 0)), hbm],
        out_shape=[
            jax.ShapeDtypeStruct((all_rows, width), bf16),
            jax.ShapeDtypeStruct((groups, half_blocks, lanes), f32),
            jax.ShapeDtypeStruct((halves, length, width), bf16),
        ],
        scratch_shapes=[store, store] + [pltpu.SemaphoreType.DMA((halves,))] * 2,
        compiler_params=remote_params(4, 56),
        cost_estimate=takes(38),
        name="attend",
    )(table, query, key_value, key_value_other, key_value, key_value_other, cotangent)

    payload = 2 * wide // blk_count + width // blk_count
    payload += -payload % (16 * win_count)
    stays = jax.ShapeDtypeStruct((blk_count, win_count // 2, payload // win_count, width), bf16)
    output, out_last, normal, second_t, attended_t, rstd, active, slope, cot_odd = pl.pallas_call(
        partial(ffn_forward_kernel, 256, (1, 3)),
        grid=(layers,),
        in_specs=[
            by_rows(width), by_rows(width), whole(width, width), whole(1, width), whole(1, width),
            whole(1, width), any_place, whole(1, wide), any_place, whole(1, width), any_place,
        ],
        out_specs=[
            by_rows(width), whole(length, width, once=False), by_rows(width), pl.BlockSpec((width, length), lambda i: (0, i)), pl.BlockSpec((width, length), lambda i: (0, i)),
            by_rows(128), by_rows(wide), by_rows(wide), hbm,
        ],
        out_shape=[
            jax.ShapeDtypeStruct((all_rows, width), bf16),
            jax.ShapeDtypeStruct((length, width), bf16),
            jax.ShapeDtypeStruct((all_rows, width), bf16),
            jax.ShapeDtypeStruct((width, all_rows), bf16),
            jax.ShapeDtypeStruct((width, all_rows), bf16),
            jax.ShapeDtypeStruct((all_rows, 128), f32),
            jax.ShapeDtypeStruct((all_rows, wide), bf16),
            jax.ShapeDtypeStruct((all_rows, wide), bf16),
            jax.ShapeDtypeStruct((halves, length, width), bf16),
        ],
        scratch_shapes=[pltpu.SemaphoreType.DMA((halves,))] * 2 + [keep(width, wide), keep(wide, width), pltpu.SemaphoreType.DMA((2,))],
        compiler_params=remote_params(5, 60),
        cost_estimate=takes(35),
        name="ffn_forward",
    )(rows_in, attended, w_out, row(b_out), row(gain_two), row(shift_two), w_up, row(b_up), w_down, row(b_down), cotangent)

    chunks = wide // width

    grad_resid, grad_attended, vec_two, vec_up, early_keep, early_other, out_tokens = pl.pallas_call(
        partial(ffn_back_kernel, chunks, blk_count, (2, 1, 0)),
        grid=(chunks,),
        in_specs=[
            scalars, pl.BlockSpec((all_rows, width), lambda i: (0, i)), pl.BlockSpec((all_rows, width), lambda i: (0, i)),
            pl.BlockSpec((width, width), lambda i: (0, i)), pl.BlockSpec((width, width), lambda i: (i, 0)),
            whole(width, all_rows), whole(1, width), *[any_place] * 7,
        ],
        out_specs=[hbm, hbm, whole(4, width), whole(chunks, width), hbm, hbm, hbm],
        out_shape=[
            jax.ShapeDtypeStruct((all_rows, width), bf16),
            jax.ShapeDtypeStruct((all_rows, width), bf16),
            jax.ShapeDtypeStruct((4, width), f32),
            jax.ShapeDtypeStruct((chunks, width), f32),
            stays,
            stays,
            jax.ShapeDtypeStruct((layers, length, width), bf16),
        ],
        scratch_shapes=[
            keep(layers, length, width),
            keep(all_rows, width),
            keep(width, all_rows),
            keep(all_rows, width),
            pltpu.VMEM((all_rows, width), f32),
            keep(2, blk_count, payload - chunks * width // blk_count - width // 2, width),
            keep(2, 2, width // 2, width),
            pltpu.SemaphoreType.DMA((layers,)),
            pltpu.SemaphoreType.DMA((layers,)),
            pltpu.SemaphoreType.DMA((layers,)),
            pltpu.SemaphoreType.DMA((48,)),
            pltpu.SemaphoreType.DMA((48,)),
            pltpu.SemaphoreType.DMA((2,)),
            keep(all_rows, width),
            pltpu.VMEM((all_rows, 128), f32),
            keep(width, all_rows),
            keep(width, width),
            pltpu.SemaphoreType.DMA((4,)),
        ],
        compiler_params=remote_params(3, 63),
        cost_estimate=takes(60),
        name="ffn_back",
    )(
        species, active, slope, w_up, w_down, second_t, row(gain_two), normal, rstd, attended_t, w_out, cot_even, cot_odd, output,
    )
    last_pairs = [(there, here) for here, there in regroup_pairs(win_count, layers, 3)]
    out_last = lax.ppermute(out_last, ("win", "blk"), last_pairs)
    pair = win_pos // 2
    early_rows = payload // win_count
    late_rows = 3 * width // blk_count + 32
    late_size = late_rows // win_count
    cell = (early_rows, width)
    early_keep = early_keep.reshape((2, 2, 2, 2) + cell)
    early_other = early_other.reshape((2, 2, 2, 2) + cell)
    place = jnp.stack([side, pair, side, layer])

    def picked(index):
        return pl.BlockSpec((1, 1, 1, 1) + cell, lambda z, n, p: index(z, n, p) + (0, 0))

    def listed(index):
        return pl.BlockSpec((1, 1) + cell, lambda z, n, p: index(z, n, p) + (0, 0))

    def cells_of(count):
        return [jax.ShapeDtypeStruct((2, 2) + cell, bf16)] * count

    def first_send():
        left = picked(lambda z, n, p: (0, z, 1 - p[0], n))
        right = picked(lambda z, n, p: (1, z, n, 1 - p[1]))
        return pl.pallas_call(
            first_send_kernel,
            grid_spec=pltpu.PrefetchScalarGridSpec(
                num_scalar_prefetch=1, grid=(2, 2), in_specs=[left, left, right, right], out_specs=[listed(lambda z, n, p: (z, n))] * 2
            ),
            out_shape=cells_of(2),
            cost_estimate=takes(3),
            name="first_send",
        )(place, early_keep, early_other, early_keep, early_other)

    def second_send(got_left, got_right):
        specs, operands = [], []
        for far in (0, 1):
            bit = lambda n, p, f=far: p[n] if f == 0 else 1 - p[n]
            left = picked(lambda z, n, p, bit=bit: (0, z, p[0], bit(1, p)))
            right = picked(lambda z, n, p, bit=bit: (1, z, bit(0, p), p[1]))
            specs += [left, left, listed(lambda z, n, p, bit=bit: (z, bit(1, p)))]
            operands += [early_keep, early_other, got_left]
            specs += [right, right, listed(lambda z, n, p, bit=bit: (z, bit(0, p)))]
            operands += [early_keep, early_other, got_right]
        rows_spec = pl.BlockSpec((1,) + cell, lambda z, n, p: (z, 0, 0))
        both_spec = pl.BlockSpec((2, 1) + cell, lambda z, n, p: (0, z, 0, 0))
        return pl.pallas_call(
            second_send_kernel,
            grid_spec=pltpu.PrefetchScalarGridSpec(num_scalar_prefetch=1, grid=(2, 1), in_specs=specs, out_specs=[both_spec, rows_spec, rows_spec]),
            out_shape=cells_of(1) + [jax.ShapeDtypeStruct((2,) + cell, bf16)] * 2,
            cost_estimate=takes(4),
            name="second_send",
        )(place, *operands)

    def third_send(keep, left, right):
        specs = []
        for step in range(layers):
            goal = lambda p, step=step: (p[3] + step) % layers
            specs.append(listed(lambda z, n, p, goal=goal: (goal(p) // 2, goal(p) % 2)))
            specs += [pl.BlockSpec((1,) + cell, lambda z, n, p, goal=goal: (goal(p) % 2, 0, 0))] * 2
        out = pl.BlockSpec(cell, lambda z, n, p: (0, 0))
        return pl.pallas_call(
            third_send_kernel,
            grid_spec=pltpu.PrefetchScalarGridSpec(num_scalar_prefetch=1, grid=(1, 1), in_specs=specs, out_specs=[out] * layers),
            out_shape=[jax.ShapeDtypeStruct(cell, bf16)] * layers,
            cost_estimate=takes(3),
            name="third_send",
        )(place, *[keep, left, right] * layers)

    def to_layer(value, step):
        pairs = [
            (win * blk_count + blk, win * blk_count + (blk + 2 * step) % blk_count)
            for win in range(win_count)
            for blk in range(blk_count)
        ]
        return lax.ppermute(value, ("win", "blk"), pairs)

    first_left, first_right = first_send()
    first_left, first_right = swap(first_left, 0, 1), swap(first_right, 2, 0)

    grad_parts = []
    for group in range(groups):
        after = []
        if group == 1:
            early_kept, send_left, send_right = second_send(first_left, first_right)
            after = [early_kept, out_last]
            second = swap(send_left, 2, 0), swap(send_right, 0, 1)
        if group == 2:
            early_parts = third_send(early_kept, *second)
            after = [early_parts[0]]
            early_parts = [early_parts[0]] + [to_layer(early_parts[n], n) for n in range(1, layers)]

        def column(first):
            return pl.BlockSpec((all_rows, lanes), lambda g, t: (0, first))

        def full(columns):
            return pl.BlockSpec((all_rows, columns), lambda g, t: (0, 0))

        grad_store = pltpu.VMEM((blocks, block_len, lanes), f32)
        glob_store = pltpu.VMEM((2, block_len, lanes), f32)
        dq, own, other = pl.pallas_call(
            partial(attend_back_kernel, sizes, blocks, head_dim, score_scale, group),
            grid_spec=pltpu.PrefetchScalarGridSpec(
                num_scalar_prefetch=1,
                grid=(1,),
                in_specs=[
                    column(group), column(group), column(group), column(groups + group), column(groups + group), column(group),
                    pl.BlockSpec((1, half_blocks, lanes), lambda g, t: (group, 0, 0)),
                    *[any_place] * len(after),
                ],
                out_specs=[full(lanes), full(2 * lanes), full(2 * lanes)],
                scratch_shapes=[store, store, grad_store, grad_store, glob_store, glob_store],
            ),
            out_shape=[jax.ShapeDtypeStruct((all_rows, n * lanes), bf16) for n in (1, 2, 2)],
            compiler_params=params,
            cost_estimate=takes(25),
            name="attend_back",
        )(table, query, key_value, key_value_other, key_value, key_value_other, grad_attended, log_total, *after)
        grad_parts += [dq, own, swap(other, 1, 0) if group < groups - 1 else other]

    def vmem(*shape):
        return pltpu.VMEM(shape, bf16)

    first_shape, mid_shape = (2, 2, 2), (2, 2)
    chain = lambda size: [vmem(*lead, size, width) for lead in (first_shape, mid_shape, mid_shape, (3,), ())]
    grad_tokens, late, early = pl.pallas_call(
        partial(finish_kernel, groups),
        grid=(layers,),
        in_specs=[by_tile(p.shape[1]) for p in grad_parts[:-1]]
        + [any_place, by_tile(width), by_tile(width), whole(1, width), whole(1, width), whole(width, 3 * width), whole(4, width), whole(chunks, width)]
        + [any_place] * layers,
        out_specs=[hbm] * 3,
        out_shape=[
            jax.ShapeDtypeStruct((layers, length, width), bf16),
            jax.ShapeDtypeStruct((win_count, late_size, width), bf16),
            jax.ShapeDtypeStruct((win_count, early_rows, width), bf16),
        ],
        scratch_shapes=[
            vmem(all_rows, 3 * width),
            vmem(layers, width, length),
            pltpu.VMEM((4, width), f32),
            vmem(layers, length, width),
            vmem(2, 2, 2, 2, 2, late_size, width),
            vmem(2, 2, 2, 2, late_size, width),
            chain(late_size),
            [vmem(*lead, early_rows, width) for lead in ((4,), ())],
            pltpu.SemaphoreType.DMA((layers,)),
            pltpu.SemaphoreType.DMA((layers,)),
            pltpu.SemaphoreType.DMA((4,)),
            pltpu.SemaphoreType.DMA((14,)),
            pltpu.SemaphoreType.DMA((14,)),
            pltpu.SemaphoreType.DMA((2,)),
            vmem(layers, length, 2 * lanes),
            pltpu.SemaphoreType.DMA((layers,)),
            pltpu.SemaphoreType.DMA((layers,)),
        ],
        compiler_params=remote_params(2, 62),
        cost_estimate=takes(90),
        name="finish",
    )(
        *grad_parts, rows_in, grad_resid, row(gain_one), row(shift_one), w_qkv, vec_two, vec_up,
        *early_parts,
    )
    part = width // blk_count
    count = wide // width
    done_qkv, done_out, done_up, done_down = pl.pallas_call(
        unpack_kernel,
        out_shape=[
            jax.ShapeDtypeStruct(shape, f32)
            for shape in ((part, 3 * width), (part, width), (part, wide), (wide // blk_count, width))
        ],
        compiler_params=params,
        cost_estimate=takes(4),
        name="unpack",
    )(early, late)
    late = late.reshape(-1, width)[3 * part :].astype(f32)
    vec = lax.dynamic_slice_in_dim(late[:8], blk_pos * part, part, axis=1)
    vec_wide = lax.dynamic_slice_in_dim(late[8 : 8 + count].reshape(-1), blk_pos * (wide // blk_count), wide // blk_count)
    return (
        lax.dynamic_update_index_in_dim(out_tokens, out_last, (layer + 3) % layers, 0),
        grad_tokens,
        done_qkv,
        vec[0],
        vec[1],
        done_out,
        vec[4],
        vec[2],
        vec[3],
        vec[5],
        vec[6],
        done_up,
        vec_wide,
        done_down,
        vec[7],
    )


def solution(mesh):
    placed = (
        P("win", "blk", None),
        P("win", "blk", None),
        P(),
        P(),
        P(),
        P(),
        P(),
        P(),
        P(),
        P(),
        P(),
        P(),
        P(),
        P(),
        P(),
        P("win", None, None, None),
        P("win", None, None, None),
        P("win", None),
        P(),
    )
    return jax.shard_map(
        layer_step,
        mesh=mesh,
        in_specs=placed,
        out_specs=(
            P("win", "blk", None),
            P("win", "blk", None),
            P("blk", None),
            P("blk"),
            P("blk"),
            P("blk", None),
            P("blk"),
            P("blk"),
            P("blk"),
            P("blk"),
            P("blk"),
            P("blk", None),
            P("blk"),
            P("blk", None),
            P("blk"),
        ),
        check_vma=False,
    )
```

```python
from functools import partial

import jax
import jax.numpy as jnp
from jax import lax
from jax.experimental import pallas as pl
from jax.experimental.pallas import tpu as pltpu
from jax.sharding import PartitionSpec as P

SPECIES = 4


epsilon = 1e-05
masked_score = -1000000000.0


def padded(cells, sides, width):
    for axis, dim in sides:
        count = lax.axis_size(axis)
        ends = count - 1
        head = lax.slice_in_dim(cells, 0, width, axis=dim)
        tail = lax.slice_in_dim(cells, cells.shape[dim] - width, cells.shape[dim], axis=dim)
        cells = jnp.concatenate(
            [
                lax.ppermute(tail, axis, [(i, (i + 1) % count) for i in range(ends)]),
                cells,
                lax.ppermute(head, axis, [((i + 1) % count, i) for i in range(ends)]),
            ],
            axis=dim,
        )
    return cells


def layer_norm(values, norm_gain, norm_shift):
    average = jnp.mean(values, axis=-1, keepdims=True)
    centred = values - average
    variance = jnp.mean(centred * centred, axis=-1, keepdims=True)
    return centred * lax.rsqrt(variance + epsilon) * norm_gain + norm_shift


def take_rows(source, index_rows):
    return jnp.take(source, index_rows, axis=0)


def add_rows(base, index_rows, update):
    return base.at[index_rows].add(update)


def set_rows(base, index_rows, update):
    return base.at[index_rows].set(update)


HEADS_PER_GROUP = 4


def regroup_pairs(win_count, layers, step):
    pairs = []
    for win in range(win_count):
        for blk in range(2 * layers):
            layer, side = blk // 2, blk % 2
            target = ((layer + step) % layers) * 2 + win % 2
            pairs.append((win * 2 * layers + blk, ((win // 2) * 2 + side) * 2 * layers + target))
    return pairs


def flip_pairs(win_count, blk_count, win_bit, blk_bit):
    return [
        (win * blk_count + blk, (win ^ win_bit) * blk_count + (blk ^ blk_bit))
        for win in range(win_count)
        for blk in range(blk_count)
    ]


def swap(value, win_bit, blk_bit):
    pairs = flip_pairs(lax.axis_size("win"), lax.axis_size("blk"), win_bit, blk_bit)
    return lax.ppermute(value, ("win", "blk"), pairs)


def head_masks(lanes, head_dim, dtype):
    lane = lax.broadcasted_iota(jnp.int32, (1, lanes), 1)
    return [(lane // head_dim == h).astype(dtype) for h in range(lanes // head_dim)]


def block_places(table, slot, group, sizes):
    heads, picks, rand_size, half_blocks = sizes
    block = table[rand_size + 2 + 2 * half_blocks + slot]
    near = [table[rand_size + 2 + slot], slot, table[rand_size + 2 + half_blocks + slot]]
    row = (block * heads + group * HEADS_PER_GROUP) * picks
    rand = [[table[row + h * picks + r] for h in range(HEADS_PER_GROUP)] for r in range(picks)]
    return block, near, rand


def spread_heads(rows, masks):
    return jnp.concatenate([rows * m for m in masks], axis=0)


def pick_heads(square, masks, height):
    total = square[0:height] * masks[0]
    for h in range(1, len(masks)):
        total = total + square[h * height : (h + 1) * height] * masks[h]
    return total


def key_rows(source, near, glob, rand, low_half):
    parts = [source[p] for p in near] + [source[p] for p in glob]
    for places in rand:
        columns = []
        for c in range(len(places) // 2):
            low = source[places[2 * c], :, c * 128 : (c + 1) * 128]
            high = source[places[2 * c + 1], :, c * 128 : (c + 1) * 128]
            columns.append(jnp.where(low_half, low, high))
        parts.append(jnp.concatenate(columns, axis=1))
    return jnp.concatenate(parts, axis=0)


def mask_scores(scores, block, blocks, block_len):
    first = jnp.where(block > 0, scores[:block_len], masked_score)
    last = jnp.where(block < blocks - 1, scores[2 * block_len : 3 * block_len], masked_score)
    return jnp.concatenate([first, scores[block_len : 2 * block_len], last, scores[3 * block_len :]], axis=0)


def across(left, right):
    return lax.dot_general(left, right, (((1,), (1,)), ((), ())), preferred_element_type=jnp.float32)


def down(left, right):
    return lax.dot_general(left, right, (((0,), (0,)), ((), ())), preferred_element_type=jnp.float32)


def load_halves(target, own, other, half_blocks, block_len):
    lanes = own.shape[-1]
    target[0:half_blocks] = own[...].reshape(half_blocks, block_len, lanes)
    target[half_blocks:] = other[...].reshape(half_blocks, block_len, lanes)


def attend_kernel(
    sizes, blocks, head_dim, cot_tiles,
    table, q_ref, k_own, k_other, v_own, v_other, cotangent,
    o_ref, lse_ref, cot_ref,
    k_all, v_all, send_sems, recv_sems,
):
    heads, picks, rand_size, half_blocks = sizes
    block_len = k_all.shape[1]
    lanes = q_ref.shape[1]
    group = pl.program_id(0)
    _, _, core, layer, _ = position()
    own_blocks = blocks // 8

    @pl.when(group == 0)
    def _():
        greet_owners(4, [])
        for n, tile in enumerate(cot_tiles):
            regroup_move(cotangent, cot_ref.at[n], tile, send_sems.at[n], recv_sems.at[n], True)

    load_halves(k_all, k_own, k_other, half_blocks, block_len)
    load_halves(v_all, v_own, v_other, half_blocks, block_len)
    low_half = lax.broadcasted_iota(jnp.int32, (block_len, 128), 1) < head_dim
    masks = head_masks(lanes, head_dim, jnp.bfloat16)
    masks_f = head_masks(lanes, head_dim, jnp.float32)
    glob = [table[rand_size], table[rand_size + 1]]

    def several(number, carry):
        slots = [number * together + u for u in range(together)]
        places = [block_places(table, slot, group, sizes) for slot in slots]
        numbers = [(((layer + 4 - slot // own_blocks) % 4) * 2 + core) * own_blocks + slot % own_blocks for slot in slots]
        rows = [pl.ds(pl.multiple_of(slot * block_len, block_len), block_len) for slot in slots]
        queries = [spread_heads(q_ref[r, :], masks) for r in rows]
        keys = [key_rows(k_all, near, glob, rand, low_half) for _, near, rand in places]
        scores = [
            mask_scores(across(key, query), block, blocks, block_len) for key, query, block in zip(keys, queries, numbers)
        ]
        tops = [jnp.max(score, axis=0, keepdims=True) for score in scores]
        weights = [jnp.exp(score - top) for score, top in zip(scores, tops)]
        totals = [jnp.sum(weight, axis=0, keepdims=True) for weight in weights]
        probs = [(weight * (1.0 / total)).astype(jnp.bfloat16) for weight, total in zip(weights, totals)]
        values = [key_rows(v_all, near, glob, rand, low_half) for _, near, rand in places]
        for slot, r, prob, value, top, total in zip(slots, rows, probs, values, tops, totals):
            o_ref[r, :] = pick_heads(down(prob, value), masks_f, block_len).astype(jnp.bfloat16)
            lse_ref[0, pl.ds(slot, 1), :] = top + jnp.log(total)
        return carry

    together = 4
    lax.fori_loop(0, half_blocks // together, several, 0, unroll=4)

    @pl.when(group == pl.num_programs(0) - 1)
    def _():
        for n, tile in enumerate(cot_tiles):
            regroup_move(cotangent, cot_ref.at[n], tile, send_sems.at[n], recv_sems.at[n], False)


def attend_back_kernel(
    sizes, blocks, head_dim, scale, group,
    table, q_ref, k_own, k_other, v_own, v_other, go_ref, lse_ref, *refs,
):
    dq_ref, own_ref, other_ref, k_all, v_all, dk_all, dv_all, dk_glob, dv_glob = refs[-9:]
    heads, picks, rand_size, half_blocks = sizes
    block_len = k_all.shape[1]
    lanes = q_ref.shape[1]
    f32 = jnp.float32
    load_halves(k_all, k_own, k_other, half_blocks, block_len)
    load_halves(v_all, v_own, v_other, half_blocks, block_len)
    dk_all[...] = jnp.zeros_like(dk_all)
    dv_all[...] = jnp.zeros_like(dv_all)
    dk_glob[...] = jnp.zeros_like(dk_glob)
    dv_glob[...] = jnp.zeros_like(dv_glob)
    low_half = lax.broadcasted_iota(jnp.int32, (block_len, 128), 1) < head_dim
    masks = head_masks(lanes, head_dim, jnp.bfloat16)
    masks_f = head_masks(lanes, head_dim, f32)
    glob = [table[rand_size], table[rand_size + 1]]

    def add_back(grads, near, rand, into, into_glob):
        for n in range(3):
            into[near[n]] += grads[n * block_len : (n + 1) * block_len]
        for n in range(2):
            into_glob[n] += grads[(3 + n) * block_len : (4 + n) * block_len]
        for r in range(picks):
            part = grads[(5 + r) * block_len : (6 + r) * block_len]
            for c in range(lanes // 128):
                cell = part[:, c * 128 : (c + 1) * 128]
                columns = pl.ds(c * 128, 128)
                into[rand[r][2 * c], :, columns] += jnp.where(low_half, cell, 0.0)
                into[rand[r][2 * c + 1], :, columns] += jnp.where(low_half, 0.0, cell)

    def several(number, carry):
        slots = [number * 2 + u for u in range(2)]
        places = [block_places(table, slot, group, sizes) for slot in slots]
        rows = [pl.ds(pl.multiple_of(slot * block_len, block_len), block_len) for slot in slots]
        queries = [spread_heads(q_ref[r, :], masks) for r in rows]
        keys = [key_rows(k_all, near, glob, rand, low_half) for _, near, rand in places]
        scores = [across(key, query) for key, query in zip(keys, queries)]
        grads_out = [spread_heads(go_ref[r, :], masks) for r in rows]
        values = [key_rows(v_all, near, glob, rand, low_half) for _, near, rand in places]
        grad_probs = [across(value, grad) for value, grad in zip(values, grads_out)]
        probs = [
            jnp.exp(mask_scores(score, block, blocks, block_len) - lse_ref[0, pl.ds(slot, 1), :])
            for score, (block, _, _), slot in zip(scores, places, slots)
        ]
        row_dots = [jnp.sum(prob * grad, axis=0, keepdims=True) for prob, grad in zip(probs, grad_probs)]
        grad_scores = [
            (prob * (grad - dot)).astype(jnp.bfloat16) for prob, grad, dot in zip(probs, grad_probs, row_dots)
        ]
        grad_values = [
            jnp.dot(prob.astype(jnp.bfloat16), grad, preferred_element_type=f32) for prob, grad in zip(probs, grads_out)
        ]
        grad_keys = [jnp.dot(grad, query, preferred_element_type=f32) for grad, query in zip(grad_scores, queries)]
        for r, grad, key in zip(rows, grad_scores, keys):
            dq_ref[r, :] = (pick_heads(down(grad, key), masks_f, block_len) * scale).astype(jnp.bfloat16)
        for grad, key_grad, (_, near, rand) in zip(grad_values, grad_keys, places):
            add_back(grad, near, rand, dv_all, dv_glob)
            add_back(key_grad, near, rand, dk_all, dk_glob)
        return carry

    lax.fori_loop(0, half_blocks // 2, several, 0, unroll=4)
    for n in range(2):
        dk_all[glob[n]] += dk_glob[n]
        dv_all[glob[n]] += dv_glob[n]
    for target, start in ((own_ref, 0), (other_ref, half_blocks)):
        for n, source in enumerate((dk_all, dv_all)):
            cells = source[start : start + half_blocks].astype(jnp.bfloat16)
            target[:, n * lanes : (n + 1) * lanes] = cells.reshape(half_blocks * block_len, lanes)


def norm_parts(values):
    average = jnp.mean(values, axis=-1, keepdims=True)
    centred = values - average
    rstd = lax.rsqrt(jnp.mean(centred * centred, axis=-1, keepdims=True) + epsilon)
    return centred * rstd, rstd


def norm_back(grad, normal, rstd, gain):
    scaled = grad * gain
    first = jnp.mean(scaled, axis=-1, keepdims=True)
    second = jnp.mean(scaled * normal, axis=-1, keepdims=True)
    return rstd * (scaled - first - normal * second)


def normal_parts(values):
    cdf = 0.5 + 0.5 * lax.erf(values * 0.5**0.5)
    return cdf, values * jnp.exp(-0.5 * values * values) * 0.3989422804014327


def column_sum(values):
    return jnp.sum(values, axis=0, keepdims=True)


MESH = pl.DeviceIdType.MESH


def tile_order(number):
    return jnp.where(number == 0, 2, jnp.where(number == 2, 3, jnp.where(number == 3, 0, number)))


def position():
    win, blk = lax.axis_index("win"), lax.axis_index("blk")
    return win, blk, win % 2, blk // 2, blk % 2


def owner_of(tile, layers):
    win, blk, core, layer, side = position()
    return (win // 2) * 2 + side, ((layer + layers - tile) % layers) * 2 + core


def greet_owners(layers, peers):
    barrier = pltpu.get_barrier_semaphore()
    others = len(peers)
    for peer in peers:
        pl.semaphore_signal(barrier, inc=1, device_id=peer, device_id_type=MESH)
    _, _, core, _, side = position()
    for tile in range(1, layers):
        pl.semaphore_signal(barrier, inc=1, device_id=owner_of(tile, layers), device_id_type=MESH)

    @pl.when(side != core)
    def _():
        pl.semaphore_signal(barrier, inc=1, device_id=owner_of(0, layers), device_id_type=MESH)
        pl.semaphore_wait(barrier, layers + others)

    @pl.when(side == core)
    def _():
        pl.semaphore_wait(barrier, layers - 1 + others)


def return_tile(tile, source, target, send_sem, recv_sems, start):
    _, _, core, layer, side = position()
    layers = target.shape[0]
    stays = (tile == 0) & (side == core)

    @pl.when(stays)
    def _():
        move = pltpu.make_async_copy(source, target.at[layer], recv_sems.at[tile])
        move.start() if start else move.wait()

    @pl.when(jnp.logical_not(stays))
    def _():
        move = pltpu.make_async_remote_copy(
            src_ref=source, dst_ref=target.at[layer], send_sem=send_sem, recv_sem=recv_sems.at[tile],
            device_id=owner_of(tile, layers), device_id_type=MESH,
        )
        move.start() if start else move.wait()


def regroup_move(source, target, tile, send_sem, recv_sem, start):
    win, _, core, layer, side = position()
    layers = source.shape[0]
    goal = (layer + tile) % layers
    stays = (tile == 0) & (side == core)

    def local():
        return pltpu.make_async_copy(source.at[goal], target, recv_sem)

    def far():
        return pltpu.make_async_remote_copy(
            src_ref=source.at[goal], dst_ref=target, send_sem=send_sem, recv_sem=recv_sem,
            device_id=((win // 2) * 2 + side, goal * 2 + core), device_id_type=MESH,
        )

    @pl.when(stays)
    def _():
        local().start() if start else local().wait()

    @pl.when(jnp.logical_not(stays))
    def _():
        far().start() if start else far().wait()


def arrival_order(number):
    return jnp.where(number == 2, 3, jnp.where(number == 3, 2, number))


def front_kernel(
    scale, tokens, vectors, weight,
    rows_ref, q_ref, kv_ref, other_ref,
    held, kv_rows, send_sems, recv_sems, kv_sems, kv_send, kv_recv, row_sems,
):
    f32, bf16 = jnp.float32, jnp.bfloat16
    step, steps = pl.program_id(0), pl.num_programs(0)
    length, width = held.shape[1:]
    win, blk, core, layer, side = position()
    layers = held.shape[0]
    peer = (win + 1 - 2 * core, blk)

    def token_move(tile, start):
        regroup_move(tokens, held.at[tile], tile, send_sems.at[tile], recv_sems.at[tile], start)

    def rows_of(tile):
        return pl.ds(pl.multiple_of(tile * length, length), length)

    def kv_moves(number):
        tile = arrival_order(number)
        return [
            pltpu.make_async_copy(kv_rows.at[number], kv_ref.at[rows_of(tile)], kv_sems.at[number]),
            pltpu.make_async_copy(held.at[tile], rows_ref.at[rows_of(tile)], row_sems.at[number]),
            pltpu.make_async_remote_copy(
                src_ref=kv_rows.at[number], dst_ref=other_ref.at[rows_of(tile)], send_sem=kv_send.at[number], recv_sem=kv_recv.at[number],
                device_id=peer, device_id_type=MESH,
            ),
        ]

    @pl.when(step == 0)
    def _():
        greet_owners(layers, [peer])
        for n in range(4):
            token_move(arrival_order(n), True)

    tile = arrival_order(step)
    token_move(tile, False)
    normal, _ = norm_parts(held[tile].astype(f32))
    normed = (normal * vectors[0:1] + vectors[1:2]).astype(bf16)

    def part(n):
        return jnp.dot(normed, weight[:, n * width : (n + 1) * width], preferred_element_type=f32)

    kv_rows[step, :, :width] = part(1).astype(bf16)
    kv_rows[step, :, width:] = (part(2) + vectors[3:4]).astype(bf16)
    for move in kv_moves(step):
        move.start()
    q_ref[...] = (part(0) + vectors[2:3]).astype(bf16) * jnp.asarray(scale, bf16)

    @pl.when(step == steps - 1)
    def _():
        for n in range(4):
            for move in kv_moves(n):
                move.wait()


def ffn_forward_kernel(
    chunk, cot_tiles,
    rows_ref, att_ref, w_out, vectors, w_up, b_up, w_down, cotangent,
    out_ref, last_ref, normal_ref, second_ref, att_turned_ref, rstd_ref, active_ref, slope_ref, cot_ref,
    send_sems, recv_sems, up_rows, down_rows, load_sems,
):
    f32, bf16 = jnp.float32, jnp.bfloat16
    step, steps = pl.program_id(0), pl.num_programs(0)

    fetch_up = pltpu.make_async_copy(w_up, up_rows, load_sems.at[0])
    fetch_down = pltpu.make_async_copy(w_down, down_rows, load_sems.at[1])

    @pl.when(step == 0)
    def _():
        fetch_up.start()
        fetch_down.start()
        greet_owners(4, [])
        for n, tile in enumerate(cot_tiles):
            regroup_move(cotangent, cot_ref.at[n], tile, send_sems.at[n], recv_sems.at[n], True)

    wide = up_rows.shape[1]
    b_out, gain, shift, b_down = (vectors.at[n : n + 1] for n in range(4))
    att = att_ref[...]
    residual = rows_ref[...].astype(f32) + (jnp.dot(att, w_out[...], preferred_element_type=f32) + b_out[...])
    normal, rstd = norm_parts(residual)
    second = (normal * gain[...] + shift[...]).astype(bf16)
    normal_ref[...] = normal.astype(bf16)
    second_ref[...] = second.T
    att_turned_ref[...] = att.T
    rstd_ref[...] = jnp.broadcast_to(rstd, rstd_ref.shape)

    @pl.when(step == 0)
    def _():
        fetch_up.wait()
        fetch_down.wait()

    def raise_part(first):
        part = slice(first, first + chunk)
        return jnp.dot(second, up_rows[:, part], preferred_element_type=f32) + b_up[:, part]

    ahead = raise_part(0)
    for first in range(0, wide, chunk):
        inner = ahead
        if first + chunk < wide:
            ahead = raise_part(first + chunk)
        cdf, slope = normal_parts(inner)
        active_ref[:, first : first + chunk] = (inner * cdf).astype(bf16)
        slope_ref[:, first : first + chunk] = (cdf + slope).astype(bf16)
    total = residual + b_down[...] + jnp.dot(active_ref[...], down_rows[...], preferred_element_type=f32)
    out_ref[...] = total.astype(bf16)

    @pl.when(step == steps - 1)
    def _():
        last_ref[...] = total.astype(bf16)
        for n, tile in enumerate(cot_tiles):
            regroup_move(cotangent, cot_ref.at[n], tile, send_sems.at[n], recv_sems.at[n], False)


def ffn_back_kernel(
    chunks, shards, kept_tiles,
    species, active_ref, slope_ref, w_up, w_down, second_t, vectors, normal_in, rstd_in, att_in, w_out_in,
    cot_even, cot_odd, output,
    resid_ref, go_ref, vec_ref, vec_up_ref, keep_ref, other_ref, out_ref,
    cot_rows, branch, branch_t, grad_inner, grad_second, stage_up, stage_down,
    cot_sems, ship_send, ship_recv, cell_send, cell_recv, done_sems, normal_ref, rstd_ref, att_t, w_out, load_sems,
):
    f32, bf16 = jnp.float32, jnp.bfloat16
    step = pl.program_id(0)
    slot = step % 2
    width = w_up.shape[0]
    tiles, length = cot_rows.shape[:2]
    part = width // shards
    half = width // 2
    size = keep_ref.shape[2]
    win, blk, core, _, _ = position()
    peer = (win + 1 - 2 * core, blk)

    def rows_of(n):
        return slice(n * length, (n + 1) * length)

    def ship(what):
        for n, tile in enumerate(kept_tiles):
            return_tile(tile, output.at[rows_of(tile)], out_ref, ship_send.at[n], ship_recv, what)

    def moves(c):
        cuts = []
        if c < chunks:
            base = 4 * c
            for first, count, piece, row in span_cuts(c * part, part, size):
                cuts.append((base + len(cuts), stage_up.at[c % 2, :, pl.ds(first, count)], slice(0, shards), piece, row, count))
            mine = slice(2 * c, 2 * c + 2)
            for first, count, piece, row in span_cuts(chunks * part, half, size):
                cuts.append((24 + base + len(cuts), stage_down.at[c % 2, :, pl.ds(first, count)], mine, piece, row, count))
        else:
            start = chunks * part + half
            for first, count, piece, row in span_cuts(start, 4 * size - start, size):
                cuts.append((20 + len(cuts), stage_up.at[0, :, pl.ds(first, count)], slice(0, shards), piece, row, count))
        return cuts

    def act(c, what):
        for number, source, mine, piece, row, count in moves(c):
            cell = (pl.ds(mine.start, mine.stop - mine.start), piece // 2, pl.ds(row, count))
            def far():
                return pltpu.make_async_remote_copy(
                    src_ref=source, dst_ref=other_ref.at[cell], send_sem=cell_send.at[number], recv_sem=cell_recv.at[number],
                    device_id=peer, device_id_type=MESH,
                )

            @pl.when(core == piece % 2)
            def _():
                if what == "receive":
                    far().wait_recv()
                else:
                    near = pltpu.make_async_copy(source, keep_ref.at[cell], cell_send.at[number])
                    near.start() if what == "start" else near.wait()

            if what != "receive":
                @pl.when(core != piece % 2)
                def _():
                    far().start() if what == "start" else far().wait_send()

    def late_loads():
        pairs = ((normal_in, normal_ref), (rstd_in, rstd_ref), (att_in, att_t), (w_out_in, w_out))
        return [pltpu.make_async_copy(a, b, load_sems.at[n]) for n, (a, b) in enumerate(pairs)]

    windows = species.shape[0]
    mine = species[((win // 2) * 2 + blk % 2) * tiles + blk // 2]
    alike = jnp.zeros((), f32)
    for n in range(windows):
        alike = alike + jnp.where(species[n] == mine, 1.0, 0.0)
    scale = jnp.sqrt(windows / (SPECIES * jnp.full((1, width), alike, f32)))

    def cot_moves():
        return [
            pltpu.make_async_copy((cot_even, cot_odd)[n % 2].at[n // 2], cot_rows.at[n], cot_sems.at[n]) for n in range(4)
        ]

    @pl.when(step == 0)
    def _():
        for move in cot_moves() + late_loads():
            move.start()
        greet_owners(tiles, [peer])
        ship(True)
        vec_ref[...] = jnp.zeros_like(vec_ref)
        for n, move in enumerate(cot_moves()):
            move.wait()
            upstream = cot_rows[n].astype(f32) * scale
            vec_ref[3:4] += column_sum(upstream)
            branch[rows_of(n), :] = upstream.astype(bf16)
            branch_t[:, rows_of(n)] = upstream.astype(bf16).T
        grad_second[...] = jnp.zeros_like(grad_second)

    for c in range(2, chunks):
        @pl.when(step == c)
        def _():
            act(c - 2, "wait")

    full = jnp.dot(branch_t[...], active_ref[...], preferred_element_type=f32)
    for n in range(2):
        for k in range(2):
            stage_down[slot, n, :, k * half : (k + 1) * half] = full[k * half : (k + 1) * half, n * half : (n + 1) * half].astype(bf16)
    total = jnp.zeros((1, w_up.shape[1]), f32)
    for n in range(tiles):
        grad = across(branch[rows_of(n), :], w_down[...]) * slope_ref[rows_of(n), :].astype(f32)
        total = total + column_sum(grad)
        grad_inner[rows_of(n), :] = grad.astype(bf16)
        grad_second[rows_of(n), :] += across(grad_inner[rows_of(n), :], w_up[...])
    vec_up_ref[pl.ds(step, 1), :] = total
    full = jnp.dot(second_t[...], grad_inner[...], preferred_element_type=f32)
    for b in range(shards):
        stage_up[slot, b, 0:part] = full[b * part : (b + 1) * part].astype(bf16)
    for c in range(chunks):
        @pl.when(step == c)
        def _():
            act(c, "start")

    @pl.when(step == chunks - 1)
    def _():
        for move in late_loads():
            move.wait()
        for n in range(tiles):
            upstream = cot_rows[n].astype(f32) * scale
            grad = grad_second[rows_of(n), :]
            normal = normal_ref[rows_of(n), :].astype(f32)
            grad_resid = upstream + norm_back(grad, normal, rstd_ref[rows_of(n), 0:1], vectors[1:2])
            grad_proj = grad_resid.astype(bf16)
            grad_inner[rows_of(n), :] = grad_proj
            branch[rows_of(n), :] = across(grad_proj, w_out[...]).astype(bf16)
            vec_ref[0:1] += column_sum(grad_resid)
            vec_ref[1:2] += column_sum(grad * normal)
            vec_ref[2:3] += column_sum(grad)
        results = [
            pltpu.make_async_copy(grad_inner, resid_ref, done_sems.at[0]),
            pltpu.make_async_copy(branch, go_ref, done_sems.at[1]),
        ]
        for move in results:
            move.start()
        full = jnp.dot(att_t[...], grad_inner[...], preferred_element_type=f32)
        act(chunks - 2, "wait")
        for b in range(shards):
            stage_up[0, b, 0:part] = full[b * part : (b + 1) * part].astype(bf16)
            stage_up[0, b, part:] = jnp.zeros((stage_up.shape[2] - part, width), bf16)
        act(chunks, "start")
        act(chunks - 1, "wait")
        act(chunks, "wait")
        for c in range(chunks + 1):
            act(c, "receive")
        for move in results:
            move.wait()
        ship(False)


def span_cuts(start, count, size):
    cuts, at = [], start
    while at < start + count:
        end = min(start + count, (at // size + 1) * size)
        cuts.append((at - start, end - at, at // size, at % size))
        at = end
    return cuts


def row_cuts(count, part, size):
    cuts = []
    for k in range(count):
        start = k * part
        while start < (k + 1) * part:
            end = min((k + 1) * part, (start // size + 1) * size)
            cuts.append((k, start - k * part, end - start, start // size, start % size))
            start = end
    return cuts


def add_into(target, got):
    target[...] = (target[...].astype(jnp.float32) + got[...].astype(jnp.float32)).astype(jnp.bfloat16)


def finish_kernel(groups, *refs):
    f32, bf16 = jnp.float32, jnp.bfloat16
    parts, others = refs[: 2 * groups], refs[2 * groups : 3 * groups]
    (
        rows_ref, resid_ref, vectors, weight, vec_two, vec_up, early_a, early_b, early_c, early_d,
        tok_ref, late_ref, early_ref,
        joined, turned, vec, out_rows, cells, core_got, late_bufs, early_bufs, send_sems, recv_sems, load_sems, chain_send, chain_recv, keep_sems, last_rows, last_send, last_recv,
    ) = refs[3 * groups :]
    step, steps = pl.program_id(0), pl.num_programs(0)
    length, width = rows_ref.shape
    lanes = width // groups
    part = width // 8
    win, blk, core, layer, side = position()
    pair = win // 2
    core_peer = (win + 1 - 2 * core, blk)
    pair_peer = (win + 2 - 4 * pair, blk)
    side_peer = (win, blk + 1 - 2 * side)
    layer_peers = [(win, ((layer + n) % 4) * 2 + side) for n in (1, 2, 3)]

    def remote(source, target, number, peer):
        return pltpu.make_async_remote_copy(
            src_ref=source, dst_ref=target, send_sem=chain_send.at[number], recv_sem=chain_recv.at[number],
            device_id=peer, device_id_type=MESH,
        )

    early_got, early_final = early_bufs

    def loads():
        return [
            pltpu.make_async_copy(source, early_got.at[n], load_sems.at[n])
            for n, source in enumerate((early_a, early_b, early_c, early_d))
        ]

    def second_step(state, got, base):
        return [
            remote(state.at[0, :, 1 - pair], got.at[0], base, pair_peer),
            remote(state.at[1, :, 1 - side], got.at[1], base + 1, side_peer),
        ]

    def add_second(state, got, mid):
        for z in range(2):
            mid[0, z] = (state[0, z, pair].astype(f32) + got[0, z].astype(f32)).astype(bf16)
            mid[1, z] = (state[1, z, side].astype(f32) + got[1, z].astype(f32)).astype(bf16)

    def layer_step(mid, got, base):
        moves = []
        for n in range(3):
            other = (layer + n + 1) % 4
            moves.append(remote(mid.at[other // 2, other % 2], got.at[n], base + n, layer_peers[n]))
        return moves

    def sum_into(final, parts):
        total = parts[0].astype(f32)
        for one in parts[1:]:
            total = total + one.astype(f32)
        final[...] = total.astype(bf16)

    def share(final, target, base):
        return [
            remote(final, target.at[win], base, core_peer),
            remote(final, target.at[win], base + 1, pair_peer),
        ]

    def pass_on(target, base):
        return [remote(target.at[win + 2 - 4 * pair], target.at[win + 2 - 4 * pair], base, core_peer)]

    def start(moves):
        for move in moves:
            move.start()

    def wait(moves):
        for move in moves:
            move.wait()

    def swap_moves(number):
        first = pl.multiple_of(tile_order(number) * length, length)
        return [
            pltpu.make_async_remote_copy(
                src_ref=others[g].at[pl.ds(first, length)], dst_ref=last_rows.at[g, number], send_sem=last_send.at[g, number],
                recv_sem=last_recv.at[g, number], device_id=core_peer, device_id_type=MESH,
            )
            for g in range(groups)
        ]

    late_first, late_second, late_mid, late_got, late_final = late_bufs
    early_base, late_base = 8, 0
    held = 1

    @pl.when(step == 0)
    def _():
        start(loads())
        greet_owners(steps, [core_peer, pair_peer, side_peer] + layer_peers)
        for n in range(4):
            start(swap_moves(n))
        vec[...] = jnp.zeros_like(vec)

    tile = tile_order(step)
    rows = pl.ds(pl.multiple_of(tile * length, length), length)
    wait(swap_moves(step))
    for g in range(groups):
        dq, own = parts[2 * g : 2 * g + 2]
        other = last_rows.at[g, step]
        columns = slice(g * lanes, (g + 1) * lanes)
        joined[rows, columns] = dq[...]
        both = (own[...].astype(f32) + other[...].astype(f32)).astype(bf16)
        joined[rows, width + g * lanes : width + (g + 1) * lanes] = both[:, :lanes]
        joined[rows, 2 * width + g * lanes : 2 * width + (g + 1) * lanes] = both[:, lanes:]
        vec[0:1, columns] += column_sum(dq[...].astype(f32))
        vec[1:2, columns] += column_sum(both[:, lanes:].astype(f32))
    grad = across(joined[rows, :], weight[...])
    normal, rstd = norm_parts(rows_ref[...].astype(f32))
    turned[tile] = (normal * vectors[0:1] + vectors[1:2]).astype(bf16).T
    vec[2:3] += column_sum(grad * normal)
    vec[3:4] += column_sum(grad)
    out_rows[step] = (resid_ref[...].astype(f32) + norm_back(grad, normal, rstd, vectors[0:1])).astype(bf16)

    @pl.when(step != held)
    def _():
        return_tile(tile, out_rows.at[step], tok_ref, send_sems.at[step], recv_sems, True)


    @pl.when(step == 0)
    def _():
        wait(loads())
        sum_into(early_final, [early_got[n] for n in range(4)])
        start(share(early_final, early_ref, early_base))
        pltpu.make_async_copy(early_final, early_ref.at[win], keep_sems.at[0]).start()

    @pl.when(step == steps - 1)
    def _():
        size = cells.shape[5]
        cuts = row_cuts(3, part, size)
        for k in range(3):
            full = jnp.dot(turned[0], joined[0:length, k * width : (k + 1) * width], preferred_element_type=f32)
            for n in range(1, 4):
                full = full + jnp.dot(
                    turned[n], joined[n * length : (n + 1) * length, k * width : (k + 1) * width], preferred_element_type=f32
                )
            for b in range(8):
                for which, first, count, piece, row in cuts:
                    if which == k:
                        cells[piece % 2, b // 4, b // 2 % 2, b % 2, piece // 2, row : row + count] = full[
                            b * part + first : b * part + first + count
                        ].astype(bf16)
        tail = jnp.concatenate(
            [vec[...], vec_two[...], vec_up[...]]
            + [jnp.zeros((4 * size - 3 * part - 12, width), f32)],
            axis=0,
        ).astype(bf16)
        for b in range(8):
            cells[1, b // 4, b // 2 % 2, b % 2, 1, 3 * part - 3 * size :] = tail
        exchange = [remote(cells.at[1 - core], core_got, late_base, core_peer)]
        start(exchange)
        wait(share(early_final, early_ref, early_base))
        start(pass_on(early_ref, early_base + 2))
        wait(exchange)
        mine = cells.at[core]
        for b in range(8):
            for x in range(2):
                add_into(mine.at[b // 4, b // 2 % 2, b % 2, x], core_got.at[b // 4, b // 2 % 2, b % 2, x])
        first = [
            remote(mine.at[0, :, 1 - side], late_first.at[0], late_base + 1, side_peer),
            remote(mine.at[1, :, :, 1 - pair], late_first.at[1], late_base + 2, pair_peer),
        ]
        start(first)
        wait(first)
        state = core_got.at[0]
        for z in range(2):
            for n in range(2):
                state[0, z, n] = (mine[0, z, side, n].astype(f32) + late_first[0, z, n].astype(f32)).astype(bf16)
                state[1, z, n] = (mine[1, z, n, pair].astype(f32) + late_first[1, z, n].astype(f32)).astype(bf16)
        start(second_step(state, late_second, late_base + 3))
        wait(second_step(state, late_second, late_base + 3))
        add_second(state, late_second, late_mid)
        across_layers = layer_step(late_mid, late_got, late_base + 5)
        start(across_layers)
        return_tile(tile_order(held), out_rows.at[held], tok_ref, send_sems.at[held], recv_sems, True)
        wait(across_layers)
        sum_into(late_final, [late_mid[layer // 2, layer % 2]] + [late_got[n] for n in range(3)])
        start(share(late_final, late_ref, early_base + 3))
        keep_late = pltpu.make_async_copy(late_final, late_ref.at[win], keep_sems.at[1])
        keep_late.start()
        wait(share(late_final, late_ref, early_base + 3))
        start(pass_on(late_ref, early_base + 5))
        wait(pass_on(early_ref, early_base + 2))
        wait(pass_on(late_ref, early_base + 5))
        pltpu.make_async_copy(early_final, early_ref.at[win], keep_sems.at[0]).wait()
        keep_late.wait()
        for n in range(4):
            return_tile(tile_order(n), out_rows.at[n], tok_ref, send_sems.at[n], recv_sems, False)


def first_send_kernel(place, keep_left, other_left, keep_right, other_right, left_ref, right_ref):
    for keep, other, target in ((keep_left, other_left, left_ref), (keep_right, other_right, right_ref)):
        target[...] = (keep[...].astype(jnp.float32) + other[...].astype(jnp.float32)).astype(jnp.bfloat16).reshape(target.shape)


def sum_low(target, refs):
    total = refs[0][...].astype(jnp.float32)
    for ref in refs[1:]:
        total = total + ref[...].astype(jnp.float32)
    target[...] = total.astype(jnp.bfloat16).reshape(target.shape)


def second_send_kernel(place, keep_left, other_left, got_left, keep_right, other_right, got_right, kept, left, right):
    side, pair = place[0], place[1]

    def total(refs, index):
        return sum(ref[index].astype(jnp.float32) for ref in refs).astype(jnp.bfloat16)

    for bit, first, second in ((0, kept.at[0, 0], kept.at[1, 0]), (1, left.at[0], right.at[0])):
        across_pair = pair if bit == 0 else 1 - pair
        across_side = side if bit == 0 else 1 - side
        first[...] = total((keep_left.at[0, 0, 0], other_left.at[0, 0, 0], got_left.at[0]), across_pair)
        second[...] = total((keep_right.at[0, 0, :, 0], other_right.at[0, 0, :, 0], got_right.at[0]), across_side)


def third_send_kernel(place, *refs):
    for n in range(4):
        keep, left, right = refs[3 * n : 3 * n + 3]
        in_left = (place[3] + n) % 4 < 2
        got = jnp.where(in_left, left[...].astype(jnp.float32), right[...].astype(jnp.float32))
        target = refs[12 + n]
        target[...] = (keep[...].reshape(target.shape).astype(jnp.float32) + got.reshape(target.shape)).astype(jnp.bfloat16)


def unpack_kernel(early, late, qkv_ref, out_ref, up_ref, down_ref):
    f32 = jnp.float32
    part, width = out_ref.shape
    count = up_ref.shape[1] // width
    half = width // 2

    def cells(source, first, rows):
        size = source.shape[1]
        parts = []
        while rows > 0:
            take = min(rows, size - first % size)
            parts.append(source[first // size, first % size : first % size + take])
            first, rows = first + take, rows - take
        return (parts[0] if len(parts) == 1 else jnp.concatenate(parts, axis=0)).astype(f32)

    for k in range(3):
        qkv_ref[:, k * width : (k + 1) * width] = cells(late, k * part, part)
    for k in range(count):
        up_ref[:, k * width : (k + 1) * width] = cells(early, k * part, part)
    turned = cells(early, count * part, half)
    down_ref[:, :half] = turned[:, :half].T
    down_ref[:, half:] = turned[:, half:].T
    out_ref[...] = cells(early, count * part + half, part)


def general_body(
    tokens,
    cotangent,
    w_qkv,
    b_q,
    b_v,
    w_out,
    b_out,
    gain_one,
    shift_one,
    gain_two,
    shift_two,
    w_up,
    b_up,
    w_down,
    b_down,
    rand_owner,
    rand_sub,
    global_ids,
    species,
):
    blk_count = lax.axis_size("blk")
    blk_pos = lax.axis_index("blk")
    win_pos = lax.axis_index("win")
    windows, length, model_width = tokens.shape
    blocks = rand_owner.shape[1]
    heads = rand_owner.shape[2]
    picks = rand_owner.shape[3]
    glob_count = global_ids.shape[1]
    own_blocks = blocks // blk_count
    block_len = length // own_blocks
    head_dim = model_width // heads
    pair_width = 2 * head_dim
    all_rows = windows * length
    key_count = 3 + glob_count + picks
    per_device = own_blocks * heads * picks
    slot_cap = max(2, 2 * per_device // blk_count)
    score_scale = head_dim ** (-0.5)
    f32 = jnp.float32
    bf16 = jnp.bfloat16
    tokens_f = tokens.reshape(all_rows, model_width).astype(f32)
    normed_f, norm_one_pull = jax.vjp(layer_norm, tokens_f, gain_one, shift_one)
    normed = normed_f.astype(bf16)
    joined = jnp.dot(normed, w_qkv, preferred_element_type=f32)
    query_vals = (joined[:, :model_width] + b_q).astype(bf16)
    key_vals = joined[:, model_width : 2 * model_width].astype(bf16)
    value_vals = (joined[:, 2 * model_width :] + b_v).astype(bf16)

    def to_heads(tensor):
        return tensor.reshape(windows, own_blocks, block_len, heads, head_dim).transpose(
            0, 1, 3, 2, 4
        )

    def from_heads(tensor):
        return tensor.transpose(0, 1, 3, 2, 4).reshape(all_rows, model_width)

    query_heads = to_heads(query_vals)
    local_pairs = jnp.concatenate([to_heads(key_vals), to_heads(value_vals)], axis=-1)
    rimmed = padded(local_pairs, (("blk", 1),), 1)
    block_ids = blk_pos * own_blocks + jnp.arange(own_blocks, dtype=jnp.int32)
    owned_glob = (global_ids[:, :, None] == block_ids[None, None, :]).astype(bf16)
    glob_terms = jnp.einsum("wgb,wbhsc->wghsc", owned_glob, local_pairs, preferred_element_type=f32)
    glob_pairs = lax.psum(glob_terms.astype(jnp.bfloat16), "blk").astype(jnp.float32).astype(bf16)
    owner_rows = rand_owner.reshape(windows, blk_count, per_device)
    sub_rows = rand_sub.reshape(windows, blk_count, per_device)
    owner_hits = (owner_rows[..., None] == jnp.arange(blk_count, dtype=jnp.int32)).astype(jnp.int32)
    slot_rows = jnp.sum(owner_hits * (jnp.cumsum(owner_hits, axis=2) - 1), axis=-1)
    my_owner = lax.dynamic_index_in_dim(owner_rows, blk_pos, 1, keepdims=False)
    my_slot = lax.dynamic_index_in_dim(slot_rows, blk_pos, 1, keepdims=False)
    fetch_index = my_owner * slot_cap + my_slot
    head_of_row = jnp.arange(per_device, dtype=jnp.int32) // picks % heads
    source_rows = sub_rows * heads + head_of_row[None, None, :]
    requester = jnp.arange(blk_count, dtype=jnp.int32)[None, :, None]
    target_rows = jnp.where(
        owner_rows == blk_pos, requester * slot_cap + slot_rows, blk_count * slot_cap
    )
    send_table = jnp.full((windows, blk_count * slot_cap + 1), own_blocks * heads, jnp.int32)
    send_table = jax.vmap(set_rows)(
        send_table, target_rows.reshape(windows, -1), source_rows.reshape(windows, -1)
    )[:, : blk_count * slot_cap]
    flat_pairs = jnp.concatenate(
        [
            local_pairs.reshape(windows, own_blocks * heads, block_len, pair_width),
            jnp.zeros((windows, 1, block_len, pair_width), bf16),
        ],
        axis=1,
    )
    outgoing = jax.vmap(take_rows)(flat_pairs, send_table).reshape(
        windows, blk_count, slot_cap, block_len, pair_width
    )
    incoming = lax.all_to_all(outgoing, "blk", split_axis=1, concat_axis=1, tiled=True).reshape(
        windows, blk_count * slot_cap, block_len, pair_width
    )
    rand_pairs = jax.vmap(take_rows)(incoming, fetch_index).reshape(
        windows, own_blocks, heads, picks, block_len, pair_width
    )
    near_pairs = jnp.stack(
        [rimmed[:, 0:own_blocks], rimmed[:, 1 : own_blocks + 1], rimmed[:, 2 : own_blocks + 2]],
        axis=3,
    )
    far_pairs = jnp.broadcast_to(
        glob_pairs.transpose(0, 2, 1, 3, 4)[:, None],
        (windows, own_blocks, heads, glob_count, block_len, pair_width),
    )
    gathered_keys = jnp.concatenate([near_pairs, far_pairs, rand_pairs], axis=3).reshape(
        windows, own_blocks, heads, key_count * block_len, pair_width
    )
    set_keys = gathered_keys[..., :head_dim]
    set_values = gathered_keys[..., head_dim:]
    block_flags = jnp.concatenate(
        [
            (block_ids > 0)[:, None],
            jnp.ones((own_blocks, 1), jnp.bool_),
            (block_ids < blocks - 1)[:, None],
            jnp.ones((own_blocks, glob_count + picks), jnp.bool_),
        ],
        axis=1,
    )
    key_valid = jnp.repeat(block_flags, block_len, axis=1)[None, :, None, None, :]

    def score_block():
        raw_scores = (
            jnp.einsum("wbhqe,wbhke->wbhqk", query_heads, set_keys, preferred_element_type=f32)
            * score_scale
        )
        return jnp.where(key_valid, raw_scores, masked_score)

    score_matrix = score_block()
    top_score = jnp.max(score_matrix, axis=-1, keepdims=True)
    log_total = top_score + jnp.log(
        jnp.sum(jnp.exp(score_matrix - top_score), axis=-1, keepdims=True)
    )
    probs_low = jnp.exp(score_matrix - log_total).astype(bf16)
    attended = jnp.einsum(
        "wbhqk,wbhke->wbhqe", probs_low, set_values, preferred_element_type=f32
    ).astype(bf16)
    merged = from_heads(attended)
    residual = tokens_f + (jnp.dot(merged, w_out, preferred_element_type=f32) + b_out)
    second_f, norm_two_pull = jax.vjp(layer_norm, residual, gain_two, shift_two)
    second = second_f.astype(bf16)
    inner_f = jnp.dot(second, w_up, preferred_element_type=f32) + b_up
    active_f, gelu_pull = jax.vjp(partial(jax.nn.gelu, approximate=False), inner_f)
    active = active_f.astype(bf16)
    output = residual + (jnp.dot(active, w_down, preferred_element_type=f32) + b_down)
    species_count = jnp.sum(
        (species[:, None] == jnp.arange(SPECIES, dtype=jnp.int32)[None, :]).astype(f32), axis=0
    )
    my_species = lax.dynamic_slice_in_dim(species, win_pos * windows, windows)
    own_count = jnp.sum(
        (my_species[:, None] == jnp.arange(SPECIES, dtype=jnp.int32)[None, :]).astype(f32)
        * species_count[None, :],
        axis=1,
    )
    window_scale = jnp.sqrt(species.shape[0] / (SPECIES * own_count))
    upstream = (cotangent.astype(f32) * window_scale[:, None, None]).reshape(all_rows, model_width)
    grad_branch = upstream.astype(bf16)
    grad_w_down = jnp.einsum("tf,td->fd", active, grad_branch, preferred_element_type=f32)
    grad_b_down = jnp.sum(grad_branch, axis=0, dtype=f32)
    grad_active = jnp.einsum("td,fd->tf", grad_branch, w_down, preferred_element_type=f32)
    grad_inner = gelu_pull(grad_active)[0].astype(bf16)
    grad_w_up = jnp.einsum("td,tf->df", second, grad_inner, preferred_element_type=f32)
    grad_b_up = jnp.sum(grad_inner, axis=0, dtype=f32)
    grad_second = jnp.einsum("tf,df->td", grad_inner, w_up, preferred_element_type=f32)
    grad_resid_norm, grad_gain_two, grad_shift_two = norm_two_pull(grad_second)
    grad_resid = upstream + grad_resid_norm
    grad_proj = grad_resid.astype(bf16)
    grad_w_out = jnp.einsum("ti,to->io", merged, grad_proj, preferred_element_type=f32)
    grad_b_out = jnp.sum(grad_proj, axis=0, dtype=f32)
    grad_attended = to_heads(
        jnp.einsum("to,io->ti", grad_proj, w_out, preferred_element_type=f32).astype(bf16)
    )
    probs_full = jnp.exp(score_block() - log_total)
    grad_probs = jnp.einsum(
        "wbhqe,wbhke->wbhqk", grad_attended, set_values, preferred_element_type=f32
    )
    grad_set_values = jnp.einsum(
        "wbhqk,wbhqe->wbhke", probs_full.astype(bf16), grad_attended, preferred_element_type=f32
    )
    row_dot = jnp.sum(probs_full * grad_probs, axis=-1, keepdims=True)
    grad_scores = (probs_full * (grad_probs - row_dot)).astype(bf16)
    grad_query = (
        jnp.einsum("wbhqk,wbhke->wbhqe", grad_scores, set_keys, preferred_element_type=f32)
        * score_scale
    )
    grad_set_keys = (
        jnp.einsum("wbhqk,wbhqe->wbhke", grad_scores, query_heads, preferred_element_type=f32)
        * score_scale
    )
    grad_set = jnp.concatenate([grad_set_keys, grad_set_values], axis=-1).reshape(
        windows, own_blocks, heads, key_count, block_len, pair_width
    )
    extended = (
        jnp.pad(grad_set[:, :, :, 1], ((0, 0), (1, 1), (0, 0), (0, 0), (0, 0)))
        + jnp.pad(grad_set[:, :, :, 0], ((0, 0), (0, 2), (0, 0), (0, 0), (0, 0)))
        + jnp.pad(grad_set[:, :, :, 2], ((0, 0), (2, 0), (0, 0), (0, 0), (0, 0)))
    )
    edge_grads = jnp.concatenate([extended[:, :1], extended[:, own_blocks + 1 :]], axis=1)
    edge_back = padded(edge_grads.astype(jnp.bfloat16), (("blk", 1),), 1).astype(edge_grads.dtype)
    pair_grad = extended[:, 1 : own_blocks + 1]
    pair_grad = pair_grad.at[:, 0].add(edge_back[:, 0]).at[:, own_blocks - 1].add(edge_back[:, 3])
    glob_grad = jnp.sum(grad_set[:, :, :, 3 : 3 + glob_count], axis=1).transpose(0, 2, 1, 3, 4)
    glob_total = lax.psum(glob_grad.astype(jnp.bfloat16), "blk").astype(jnp.float32)
    pair_grad = pair_grad + jnp.einsum(
        "wgb,wghsc->wbhsc", owned_glob.astype(f32), glob_total, precision=lax.Precision.HIGHEST
    )
    rand_grad = grad_set[:, :, :, 3 + glob_count :].reshape(
        windows, per_device, block_len, pair_width
    )
    back_out = jax.vmap(add_rows)(
        jnp.zeros((windows, blk_count * slot_cap, block_len, pair_width), f32),
        fetch_index,
        rand_grad,
    )
    back_in = lax.all_to_all(
        back_out.reshape(windows, blk_count, slot_cap, block_len, pair_width).astype(jnp.bfloat16),
        "blk",
        split_axis=1,
        concat_axis=1,
        tiled=True,
    ).astype(jnp.float32)
    owner_sum = jax.vmap(add_rows)(
        jnp.zeros((windows, own_blocks * heads + 1, block_len, pair_width), f32),
        send_table,
        back_in.reshape(windows, blk_count * slot_cap, block_len, pair_width),
    )
    pair_grad = pair_grad + owner_sum[:, : own_blocks * heads].reshape(
        windows, own_blocks, heads, block_len, pair_width
    )
    grad_keys = from_heads(pair_grad[..., :head_dim].astype(bf16))
    grad_values = from_heads(pair_grad[..., head_dim:].astype(bf16))
    grad_joined = jnp.concatenate(
        [from_heads(grad_query.astype(bf16)), grad_keys, grad_values], axis=1
    )
    grad_w_qkv = jnp.einsum("td,tc->dc", normed, grad_joined, preferred_element_type=f32)
    grad_b_q = jnp.sum(grad_joined[:, :model_width], axis=0, dtype=f32)
    grad_b_v = jnp.sum(grad_joined[:, 2 * model_width :], axis=0, dtype=f32)
    grad_normed = jnp.einsum("tc,dc->td", grad_joined, w_qkv, preferred_element_type=f32)
    grad_tok_norm, grad_gain_one, grad_shift_one = norm_one_pull(grad_normed)
    grad_tokens = (grad_resid + grad_tok_norm).astype(bf16).reshape(windows, length, model_width)
    local_grads = (
        grad_w_qkv,
        grad_b_q,
        grad_b_v,
        grad_w_out,
        grad_b_out,
        grad_gain_one,
        grad_shift_one,
        grad_gain_two,
        grad_shift_two,
        grad_w_up,
        grad_b_up,
        grad_w_down,
        grad_b_down,
    )
    packed_grads = jnp.concatenate(
        [grad_item.reshape(blk_count, -1) for grad_item in local_grads], axis=1
    )
    total_cols = packed_grads.shape[1]
    win_count = lax.axis_size("win")
    pad_cols = -total_cols % win_count
    shard_sum = lax.psum_scatter(
        packed_grads.astype(jnp.bfloat16), "blk", scatter_dimension=0, tiled=True
    ).astype(jnp.float32)
    split_shard = jnp.pad(shard_sum, ((0, 0), (0, pad_cols))).reshape(win_count, -1)
    group_piece = lax.psum_scatter(
        split_shard.astype(jnp.bfloat16), "win", scatter_dimension=0, tiled=True
    ).astype(jnp.float32)
    summed = (
        lax.all_gather(group_piece.astype(jnp.bfloat16), "win", axis=0, tiled=True)
        .astype(group_piece.dtype)
        .reshape(1, -1)[:, :total_cols]
    )
    shards = []
    offset = 0
    for grad_item in local_grads:
        entry_count = grad_item.size // blk_count
        shards.append(
            summed[0, offset : offset + entry_count].reshape(
                (grad_item.shape[0] // blk_count,) + grad_item.shape[1:]
            )
        )
        offset = offset + entry_count
    out_tokens = output.astype(bf16).reshape(windows, length, model_width)
    return (
        out_tokens,
        grad_tokens,
        shards[0],
        shards[1],
        shards[2],
        shards[3],
        shards[4],
        shards[5],
        shards[6],
        shards[7],
        shards[8],
        shards[9],
        shards[10],
        shards[11],
        shards[12],
    )


def layer_step(*arguments):
    windows = arguments[0].shape[0]
    paired = lax.axis_size("blk") == 2 * windows and lax.axis_size("win") == 4 and windows == 4
    return (paired_body if paired else general_body)(*arguments)


def paired_body(
    tokens,
    cotangent,
    w_qkv,
    b_q,
    b_v,
    w_out,
    b_out,
    gain_one,
    shift_one,
    gain_two,
    shift_two,
    w_up,
    b_up,
    w_down,
    b_down,
    rand_owner,
    rand_sub,
    global_ids,
    species,
):
    f32 = jnp.float32
    bf16 = jnp.bfloat16
    win_count = lax.axis_size("win")
    blk_count = lax.axis_size("blk")
    win_pos = lax.axis_index("win")
    blk_pos = lax.axis_index("blk")
    layers, length, width = tokens.shape
    core, layer, side = win_pos % 2, blk_pos // 2, blk_pos % 2
    blocks, heads, picks = rand_owner.shape[1:]
    own_blocks = blocks // blk_count
    half_blocks = blocks // 2
    block_len = length // own_blocks
    head_dim = width // heads
    all_rows = layers * length
    lanes = HEADS_PER_GROUP * head_dim
    groups = heads // HEADS_PER_GROUP
    score_scale = head_dim ** (-0.5)

    def takes(micros):
        return pl.CostEstimate(flops=micros * 1_000_000_000, bytes_accessed=micros * 1_000_000, transcendentals=0)


    rand_size = blocks * heads * picks
    named = jnp.concatenate(
        [
            lax.dynamic_index_in_dim((rand_owner * own_blocks + rand_sub).reshape(layers, rand_size), layer, 0, keepdims=False),
            lax.dynamic_index_in_dim(global_ids, layer, 0, keepdims=False),
        ]
    )
    slot = jnp.arange(half_blocks, dtype=jnp.int32)

    def table_for(which):
        block = (((layer - slot // own_blocks) % layers) * 2 + which) * own_blocks + slot % own_blocks
        reads = jnp.concatenate([named, jnp.maximum(block - 1, 0), jnp.minimum(block + 1, blocks - 1)])
        owner = reads // own_blocks
        half = jnp.where(owner % 2 == which, 0, half_blocks)
        places = half + ((layer - owner // 2) % layers) * own_blocks + reads % own_blocks
        return jnp.concatenate([places, block])

    table = jnp.where(side == core, table_for(core), swap(table_for(1 - core), 1, 0))
    sizes = (heads, picks, rand_size, half_blocks)

    tile = length

    def by_rows(columns):
        return pl.BlockSpec((tile, columns), lambda i: (i, 0))

    def by_tile(columns):
        return pl.BlockSpec((tile, columns), lambda i: (tile_order(i), 0))

    def whole(*shape, once=True):
        mode = pl.Buffered(1) if once else None
        return pl.BlockSpec(shape, lambda i: (0,) * len(shape), pipeline_mode=mode)

    scalars = pl.BlockSpec(memory_space=pltpu.SMEM)
    wide = w_up.shape[1]
    params = pltpu.CompilerParams(vmem_limit_bytes=60 << 20)
    row = lambda vector: vector.reshape(1, -1)
    def remote_params(number, mib):
        return pltpu.CompilerParams(vmem_limit_bytes=mib << 20, collective_id=number, has_side_effects=True)

    any_place = pl.BlockSpec(memory_space=pl.ANY)
    hbm = pl.BlockSpec(memory_space=pltpu.HBM)

    def keep(*shape):
        return pltpu.VMEM(shape, bf16)

    copies = pltpu.SemaphoreType.DMA((layers,))
    vectors_one = jnp.stack([gain_one, shift_one, b_q, b_v])
    vectors_two = jnp.stack([b_out, gain_two, shift_two, b_down])
    rows_in, query, key_value, key_value_other = pl.pallas_call(
        partial(front_kernel, score_scale),
        grid=(layers,),
        in_specs=[any_place, whole(4, width), whole(width, 3 * width)],
        out_specs=[hbm, pl.BlockSpec((tile, width), lambda i: (arrival_order(i), 0)), hbm, hbm],
        out_shape=[
            jax.ShapeDtypeStruct((all_rows, width), bf16),
            jax.ShapeDtypeStruct((all_rows, width), bf16),
            jax.ShapeDtypeStruct((all_rows, 2 * width), bf16),
            jax.ShapeDtypeStruct((all_rows, 2 * width), bf16),
        ],
        scratch_shapes=[keep(layers, length, width), keep(layers, length, 2 * width)] + [copies] * 6,
        compiler_params=remote_params(1, 48),
        cost_estimate=takes(80),
        name="front",
    )(tokens, vectors_one, w_qkv)

    def lane_group(first):
        return pl.BlockSpec((all_rows, lanes), lambda g: (0, first + g))

    store = pltpu.VMEM((blocks, block_len, lanes), bf16)
    halves = layers // 2
    attended, log_total, cot_even = pl.pallas_call(
        partial(attend_kernel, sizes, blocks, head_dim, (0, 2)),
        grid=(groups,),
        in_specs=[scalars] + [lane_group(0), lane_group(0), lane_group(0), lane_group(groups), lane_group(groups), any_place],
        out_specs=[lane_group(0), pl.BlockSpec((1, half_blocks, lanes), lambda g: (g, 0, 0)), hbm],
        out_shape=[
            jax.ShapeDtypeStruct((all_rows, width), bf16),
            jax.ShapeDtypeStruct((groups, half_blocks, lanes), f32),
            jax.ShapeDtypeStruct((halves, length, width), bf16),
        ],
        scratch_shapes=[store, store] + [pltpu.SemaphoreType.DMA((halves,))] * 2,
        compiler_params=remote_params(4, 56),
        cost_estimate=takes(38),
        name="attend",
    )(table, query, key_value, key_value_other, key_value, key_value_other, cotangent)

    payload = 2 * wide // blk_count + width // blk_count
    payload += -payload % (16 * win_count)
    stays = jax.ShapeDtypeStruct((blk_count, win_count // 2, payload // win_count, width), bf16)
    output, out_last, normal, second_t, attended_t, rstd, active, slope, cot_odd = pl.pallas_call(
        partial(ffn_forward_kernel, 256, (1, 3)),
        grid=(layers,),
        in_specs=[
            by_rows(width), by_rows(width), whole(width, width), whole(4, width), any_place, whole(1, wide), any_place, any_place,
        ],
        out_specs=[
            by_rows(width), whole(length, width, once=False), by_rows(width), pl.BlockSpec((width, length), lambda i: (0, i)), pl.BlockSpec((width, length), lambda i: (0, i)),
            by_rows(128), by_rows(wide), by_rows(wide), hbm,
        ],
        out_shape=[
            jax.ShapeDtypeStruct((all_rows, width), bf16),
            jax.ShapeDtypeStruct((length, width), bf16),
            jax.ShapeDtypeStruct((all_rows, width), bf16),
            jax.ShapeDtypeStruct((width, all_rows), bf16),
            jax.ShapeDtypeStruct((width, all_rows), bf16),
            jax.ShapeDtypeStruct((all_rows, 128), f32),
            jax.ShapeDtypeStruct((all_rows, wide), bf16),
            jax.ShapeDtypeStruct((all_rows, wide), bf16),
            jax.ShapeDtypeStruct((halves, length, width), bf16),
        ],
        scratch_shapes=[pltpu.SemaphoreType.DMA((halves,))] * 2 + [keep(width, wide), keep(wide, width), pltpu.SemaphoreType.DMA((2,))],
        compiler_params=remote_params(5, 60),
        cost_estimate=takes(35),
        name="ffn_forward",
    )(rows_in, attended, w_out, vectors_two, w_up, row(b_up), w_down, cotangent)

    chunks = wide // width

    grad_resid, grad_attended, vec_two, vec_up, early_keep, early_other, out_tokens = pl.pallas_call(
        partial(ffn_back_kernel, chunks, blk_count, (2, 1, 0)),
        grid=(chunks,),
        in_specs=[
            scalars, pl.BlockSpec((all_rows, width), lambda i: (0, i)), pl.BlockSpec((all_rows, width), lambda i: (0, i)),
            pl.BlockSpec((width, width), lambda i: (0, i)), pl.BlockSpec((width, width), lambda i: (i, 0)),
            whole(width, all_rows), whole(4, width), *[any_place] * 7,
        ],
        out_specs=[hbm, hbm, whole(4, width), whole(chunks, width), hbm, hbm, hbm],
        out_shape=[
            jax.ShapeDtypeStruct((all_rows, width), bf16),
            jax.ShapeDtypeStruct((all_rows, width), bf16),
            jax.ShapeDtypeStruct((4, width), f32),
            jax.ShapeDtypeStruct((chunks, width), f32),
            stays,
            stays,
            jax.ShapeDtypeStruct((layers, length, width), bf16),
        ],
        scratch_shapes=[
            keep(layers, length, width),
            keep(all_rows, width),
            keep(width, all_rows),
            keep(all_rows, width),
            pltpu.VMEM((all_rows, width), f32),
            keep(2, blk_count, payload - chunks * width // blk_count - width // 2, width),
            keep(2, 2, width // 2, width),
            pltpu.SemaphoreType.DMA((layers,)),
            pltpu.SemaphoreType.DMA((layers,)),
            pltpu.SemaphoreType.DMA((layers,)),
            pltpu.SemaphoreType.DMA((48,)),
            pltpu.SemaphoreType.DMA((48,)),
            pltpu.SemaphoreType.DMA((2,)),
            keep(all_rows, width),
            pltpu.VMEM((all_rows, 128), f32),
            keep(width, all_rows),
            keep(width, width),
            pltpu.SemaphoreType.DMA((4,)),
        ],
        compiler_params=remote_params(3, 63),
        cost_estimate=takes(60),
        name="ffn_back",
    )(
        species, active, slope, w_up, w_down, second_t, vectors_two, normal, rstd, attended_t, w_out, cot_even, cot_odd, output,
    )
    last_pairs = [(there, here) for here, there in regroup_pairs(win_count, layers, 3)]
    out_last = lax.ppermute(out_last, ("win", "blk"), last_pairs)
    pair = win_pos // 2
    early_rows = payload // win_count
    late_rows = 3 * width // blk_count + 32
    late_size = late_rows // win_count
    cell = (early_rows, width)
    early_keep = early_keep.reshape((2, 2, 2, 2) + cell)
    early_other = early_other.reshape((2, 2, 2, 2) + cell)
    place = jnp.stack([side, pair, side, layer])

    def picked(index):
        return pl.BlockSpec((1, 1, 1, 1) + cell, lambda z, n, p: index(z, n, p) + (0, 0))

    def listed(index):
        return pl.BlockSpec((1, 1) + cell, lambda z, n, p: index(z, n, p) + (0, 0))

    def cells_of(count):
        return [jax.ShapeDtypeStruct((2, 2) + cell, bf16)] * count

    def first_send():
        left = picked(lambda z, n, p: (0, z, 1 - p[0], n))
        right = picked(lambda z, n, p: (1, z, n, 1 - p[1]))
        return pl.pallas_call(
            first_send_kernel,
            grid_spec=pltpu.PrefetchScalarGridSpec(
                num_scalar_prefetch=1, grid=(2, 2), in_specs=[left, left, right, right], out_specs=[listed(lambda z, n, p: (z, n))] * 2
            ),
            out_shape=cells_of(2),
            cost_estimate=takes(3),
            name="first_send",
        )(place, early_keep, early_other, early_keep, early_other)

    def second_send(got_left, got_right):
        left = pl.BlockSpec((1, 1, 1, 2) + cell, lambda z, p: (0, z, p[0], 0, 0, 0))
        right = pl.BlockSpec((1, 1, 2, 1) + cell, lambda z, p: (1, z, 0, p[1], 0, 0))
        got = pl.BlockSpec((1, 2) + cell, lambda z, p: (z, 0, 0, 0))
        rows_spec = pl.BlockSpec((1,) + cell, lambda z, p: (z, 0, 0))
        both_spec = pl.BlockSpec((2, 1) + cell, lambda z, p: (0, z, 0, 0))
        return pl.pallas_call(
            second_send_kernel,
            grid_spec=pltpu.PrefetchScalarGridSpec(
                num_scalar_prefetch=1, grid=(2,), in_specs=[left, left, got, right, right, got], out_specs=[both_spec, rows_spec, rows_spec]
            ),
            out_shape=cells_of(1) + [jax.ShapeDtypeStruct((2,) + cell, bf16)] * 2,
            compiler_params=params,
            cost_estimate=takes(4),
            name="second_send",
        )(place, early_keep, early_other, got_left, early_keep, early_other, got_right)

    def third_send(keep, left, right):
        specs = []
        for step in range(layers):
            goal = lambda p, step=step: (p[3] + step) % layers
            specs.append(listed(lambda z, n, p, goal=goal: (goal(p) // 2, goal(p) % 2)))
            specs += [pl.BlockSpec((1,) + cell, lambda z, n, p, goal=goal: (goal(p) % 2, 0, 0))] * 2
        out = pl.BlockSpec(cell, lambda z, n, p: (0, 0))
        return pl.pallas_call(
            third_send_kernel,
            grid_spec=pltpu.PrefetchScalarGridSpec(num_scalar_prefetch=1, grid=(1, 1), in_specs=specs, out_specs=[out] * layers),
            out_shape=[jax.ShapeDtypeStruct(cell, bf16)] * layers,
            cost_estimate=takes(3),
            name="third_send",
        )(place, *[keep, left, right] * layers)

    def to_layer(value, step):
        pairs = [
            (win * blk_count + blk, win * blk_count + (blk + 2 * step) % blk_count)
            for win in range(win_count)
            for blk in range(blk_count)
        ]
        return lax.ppermute(value, ("win", "blk"), pairs)

    first_left, first_right = first_send()
    first_left, first_right = swap(first_left, 0, 1), swap(first_right, 2, 0)

    grad_parts, grad_others = [], []
    for group in range(groups):
        after = []
        if group == 1:
            early_kept, send_left, send_right = second_send(first_left, first_right)
            after = [early_kept, out_last]
            second = swap(send_left, 2, 0), swap(send_right, 0, 1)
        if group == 2:
            early_parts = third_send(early_kept, *second)
            after = [early_parts[0]]
            early_parts = [early_parts[0]] + [to_layer(early_parts[n], n) for n in range(1, layers)]

        def column(first):
            return pl.BlockSpec((all_rows, lanes), lambda g, t: (0, first))

        def full(columns):
            return pl.BlockSpec((all_rows, columns), lambda g, t: (0, 0))

        grad_store = pltpu.VMEM((blocks, block_len, lanes), f32)
        glob_store = pltpu.VMEM((2, block_len, lanes), f32)
        dq, own, other = pl.pallas_call(
            partial(attend_back_kernel, sizes, blocks, head_dim, score_scale, group),
            grid_spec=pltpu.PrefetchScalarGridSpec(
                num_scalar_prefetch=1,
                grid=(1,),
                in_specs=[
                    column(group), column(group), column(group), column(groups + group), column(groups + group), column(group),
                    pl.BlockSpec((1, half_blocks, lanes), lambda g, t: (group, 0, 0)),
                    *[any_place] * len(after),
                ],
                out_specs=[full(lanes), full(2 * lanes), full(2 * lanes)],
                scratch_shapes=[store, store, grad_store, grad_store, glob_store, glob_store],
            ),
            out_shape=[jax.ShapeDtypeStruct((all_rows, n * lanes), bf16) for n in (1, 2, 2)],
            compiler_params=params,
            cost_estimate=takes(25),
            name="attend_back",
        )(table, query, key_value, key_value_other, key_value, key_value_other, grad_attended, log_total, *after)
        grad_parts += [dq, own]
        grad_others.append(other)

    def vmem(*shape):
        return pltpu.VMEM(shape, bf16)

    first_shape, mid_shape = (2, 2, 2), (2, 2)
    chain = lambda size: [vmem(*lead, size, width) for lead in (first_shape, mid_shape, mid_shape, (3,), ())]
    grad_tokens, late, early = pl.pallas_call(
        partial(finish_kernel, groups),
        grid=(layers,),
        in_specs=[by_tile(p.shape[1]) for p in grad_parts]
        + [any_place] * groups
        + [by_tile(width), by_tile(width), whole(4, width), whole(width, 3 * width), whole(4, width), whole(chunks, width)]
        + [any_place] * layers,
        out_specs=[hbm] * 3,
        out_shape=[
            jax.ShapeDtypeStruct((layers, length, width), bf16),
            jax.ShapeDtypeStruct((win_count, late_size, width), bf16),
            jax.ShapeDtypeStruct((win_count, early_rows, width), bf16),
        ],
        scratch_shapes=[
            vmem(all_rows, 3 * width),
            vmem(layers, width, length),
            pltpu.VMEM((4, width), f32),
            vmem(layers, length, width),
            vmem(2, 2, 2, 2, 2, late_size, width),
            vmem(2, 2, 2, 2, late_size, width),
            chain(late_size),
            [vmem(*lead, early_rows, width) for lead in ((4,), ())],
            pltpu.SemaphoreType.DMA((layers,)),
            pltpu.SemaphoreType.DMA((layers,)),
            pltpu.SemaphoreType.DMA((4,)),
            pltpu.SemaphoreType.DMA((14,)),
            pltpu.SemaphoreType.DMA((14,)),
            pltpu.SemaphoreType.DMA((2,)),
            vmem(groups, layers, length, 2 * lanes),
            pltpu.SemaphoreType.DMA((groups, layers)),
            pltpu.SemaphoreType.DMA((groups, layers)),
        ],
        compiler_params=remote_params(2, 62),
        cost_estimate=takes(90),
        name="finish",
    )(
        *grad_parts, *grad_others, rows_in, grad_resid, vectors_one, w_qkv, vec_two, vec_up,
        *early_parts,
    )
    part = width // blk_count
    count = wide // width
    done_qkv, done_out, done_up, done_down = pl.pallas_call(
        unpack_kernel,
        out_shape=[
            jax.ShapeDtypeStruct(shape, f32)
            for shape in ((part, 3 * width), (part, width), (part, wide), (wide // blk_count, width))
        ],
        compiler_params=params,
        cost_estimate=takes(4),
        name="unpack",
    )(early, late)
    late = late.reshape(-1, width)[3 * part :].astype(f32)
    vec = lax.dynamic_slice_in_dim(late[:8], blk_pos * part, part, axis=1)
    vec_wide = lax.dynamic_slice_in_dim(late[8 : 8 + count].reshape(-1), blk_pos * (wide // blk_count), wide // blk_count)
    return (
        lax.dynamic_update_index_in_dim(out_tokens, out_last, (layer + 3) % layers, 0),
        grad_tokens,
        done_qkv,
        vec[0],
        vec[1],
        done_out,
        vec[4],
        vec[2],
        vec[3],
        vec[5],
        vec[6],
        done_up,
        vec_wide,
        done_down,
        vec[7],
    )


def solution(mesh):
    placed = (
        P("win", "blk", None),
        P("win", "blk", None),
        P(),
        P(),
        P(),
        P(),
        P(),
        P(),
        P(),
        P(),
        P(),
        P(),
        P(),
        P(),
        P(),
        P("win", None, None, None),
        P("win", None, None, None),
        P("win", None),
        P(),
    )
    return jax.shard_map(
        layer_step,
        mesh=mesh,
        in_specs=placed,
        out_specs=(
            P("win", "blk", None),
            P("win", "blk", None),
            P("blk", None),
            P("blk"),
            P("blk"),
            P("blk", None),
            P("blk"),
            P("blk"),
            P("blk"),
            P("blk"),
            P("blk"),
            P("blk", None),
            P("blk"),
            P("blk", None),
            P("blk"),
        ),
        check_vma=False,
    )
```

```python
from functools import partial

import jax
import jax.numpy as jnp
from jax import lax
from jax.experimental import pallas as pl
from jax.experimental.pallas import tpu as pltpu
from jax.sharding import PartitionSpec as P

SPECIES = 4


epsilon = 1e-05
masked_score = -1000000000.0


def padded(cells, sides, width):
    for axis, dim in sides:
        count = lax.axis_size(axis)
        ends = count - 1
        head = lax.slice_in_dim(cells, 0, width, axis=dim)
        tail = lax.slice_in_dim(cells, cells.shape[dim] - width, cells.shape[dim], axis=dim)
        cells = jnp.concatenate(
            [
                lax.ppermute(tail, axis, [(i, (i + 1) % count) for i in range(ends)]),
                cells,
                lax.ppermute(head, axis, [((i + 1) % count, i) for i in range(ends)]),
            ],
            axis=dim,
        )
    return cells


def layer_norm(values, norm_gain, norm_shift):
    average = jnp.mean(values, axis=-1, keepdims=True)
    centred = values - average
    variance = jnp.mean(centred * centred, axis=-1, keepdims=True)
    return centred * lax.rsqrt(variance + epsilon) * norm_gain + norm_shift


def take_rows(source, index_rows):
    return jnp.take(source, index_rows, axis=0)


def add_rows(base, index_rows, update):
    return base.at[index_rows].add(update)


def set_rows(base, index_rows, update):
    return base.at[index_rows].set(update)


HEADS_PER_GROUP = 4


def regroup_pairs(win_count, layers, step):
    pairs = []
    for win in range(win_count):
        for blk in range(2 * layers):
            layer, side = blk // 2, blk % 2
            target = ((layer + step) % layers) * 2 + win % 2
            pairs.append((win * 2 * layers + blk, ((win // 2) * 2 + side) * 2 * layers + target))
    return pairs


def flip_pairs(win_count, blk_count, win_bit, blk_bit):
    return [
        (win * blk_count + blk, (win ^ win_bit) * blk_count + (blk ^ blk_bit))
        for win in range(win_count)
        for blk in range(blk_count)
    ]


def swap(value, win_bit, blk_bit):
    pairs = flip_pairs(lax.axis_size("win"), lax.axis_size("blk"), win_bit, blk_bit)
    return lax.ppermute(value, ("win", "blk"), pairs)


def head_masks(lanes, head_dim, dtype):
    lane = lax.broadcasted_iota(jnp.int32, (1, lanes), 1)
    return [(lane // head_dim == h).astype(dtype) for h in range(lanes // head_dim)]


def block_places(table, slot, group, sizes):
    heads, picks, rand_size, half_blocks = sizes
    block = table[rand_size + 2 + 2 * half_blocks + slot]
    near = [table[rand_size + 2 + slot], slot, table[rand_size + 2 + half_blocks + slot]]
    row = (block * heads + group * HEADS_PER_GROUP) * picks
    rand = [[table[row + h * picks + r] for h in range(HEADS_PER_GROUP)] for r in range(picks)]
    return block, near, rand


def spread_heads(rows, masks):
    return jnp.concatenate([rows * m for m in masks], axis=0)


def pick_heads(square, masks, height):
    total = square[0:height] * masks[0]
    for h in range(1, len(masks)):
        total = total + square[h * height : (h + 1) * height] * masks[h]
    return total


def key_rows(source, near, glob, rand, low_half):
    parts = [source[p] for p in near] + [source[p] for p in glob]
    for places in rand:
        columns = []
        for c in range(len(places) // 2):
            low = source[places[2 * c], :, c * 128 : (c + 1) * 128]
            high = source[places[2 * c + 1], :, c * 128 : (c + 1) * 128]
            columns.append(jnp.where(low_half, low, high))
        parts.append(jnp.concatenate(columns, axis=1))
    return jnp.concatenate(parts, axis=0)


def mask_scores(scores, block, blocks, block_len):
    first = jnp.where(block > 0, scores[:block_len], masked_score)
    last = jnp.where(block < blocks - 1, scores[2 * block_len : 3 * block_len], masked_score)
    return jnp.concatenate([first, scores[block_len : 2 * block_len], last, scores[3 * block_len :]], axis=0)


def across(left, right):
    return lax.dot_general(left, right, (((1,), (1,)), ((), ())), preferred_element_type=jnp.float32)


def down(left, right):
    return lax.dot_general(left, right, (((0,), (0,)), ((), ())), preferred_element_type=jnp.float32)


def load_halves(target, own, other, half_blocks, block_len):
    lanes = own.shape[-1]
    target[0:half_blocks] = own[...].reshape(half_blocks, block_len, lanes)
    target[half_blocks:] = other[...].reshape(half_blocks, block_len, lanes)


def attend_kernel(
    sizes, blocks, head_dim, cot_tiles,
    table, q_ref, k_own, k_other, v_own, v_other, cotangent,
    o_ref, lse_ref, cot_ref,
    k_all, v_all, send_sems, recv_sems,
):
    heads, picks, rand_size, half_blocks = sizes
    block_len = k_all.shape[1]
    lanes = q_ref.shape[1]
    group = pl.program_id(0)
    _, _, core, layer, _ = position()
    own_blocks = blocks // 8

    @pl.when(group == 0)
    def _():
        greet_owners(4, [])
        for n, tile in enumerate(cot_tiles):
            regroup_move(cotangent, cot_ref.at[n], tile, send_sems.at[n], recv_sems.at[n], True)

    load_halves(k_all, k_own, k_other, half_blocks, block_len)
    load_halves(v_all, v_own, v_other, half_blocks, block_len)
    low_half = lax.broadcasted_iota(jnp.int32, (block_len, 128), 1) < head_dim
    masks = head_masks(lanes, head_dim, jnp.bfloat16)
    masks_f = head_masks(lanes, head_dim, jnp.float32)
    glob = [table[rand_size], table[rand_size + 1]]

    def several(number, carry):
        slots = [number * together + u for u in range(together)]
        places = [block_places(table, slot, group, sizes) for slot in slots]
        numbers = [(((layer + 4 - slot // own_blocks) % 4) * 2 + core) * own_blocks + slot % own_blocks for slot in slots]
        rows = [pl.ds(pl.multiple_of(slot * block_len, block_len), block_len) for slot in slots]
        queries = [spread_heads(q_ref[r, :], masks) for r in rows]
        keys = [key_rows(k_all, near, glob, rand, low_half) for _, near, rand in places]
        scores = [
            mask_scores(across(key, query), block, blocks, block_len) for key, query, block in zip(keys, queries, numbers)
        ]
        tops = [jnp.max(score, axis=0, keepdims=True) for score in scores]
        weights = [jnp.exp(score - top) for score, top in zip(scores, tops)]
        totals = [jnp.sum(weight, axis=0, keepdims=True) for weight in weights]
        probs = [(weight * (1.0 / total)).astype(jnp.bfloat16) for weight, total in zip(weights, totals)]
        values = [key_rows(v_all, near, glob, rand, low_half) for _, near, rand in places]
        for slot, r, prob, value, top, total in zip(slots, rows, probs, values, tops, totals):
            o_ref[r, :] = pick_heads(down(prob, value), masks_f, block_len).astype(jnp.bfloat16)
            lse_ref[0, pl.ds(slot, 1), :] = top + jnp.log(total)
        return carry

    together = 4
    lax.fori_loop(0, half_blocks // together, several, 0, unroll=4)

    @pl.when(group == pl.num_programs(0) - 1)
    def _():
        for n, tile in enumerate(cot_tiles):
            regroup_move(cotangent, cot_ref.at[n], tile, send_sems.at[n], recv_sems.at[n], False)


def attend_back_kernel(
    sizes, blocks, head_dim, scale, group,
    table, q_ref, k_own, k_other, v_own, v_other, go_ref, lse_ref, *refs,
):
    dq_ref, own_ref, other_ref, k_all, v_all, dk_all, dv_all, dk_glob, dv_glob = refs[-9:]
    heads, picks, rand_size, half_blocks = sizes
    block_len = k_all.shape[1]
    lanes = q_ref.shape[1]
    f32 = jnp.float32
    load_halves(k_all, k_own, k_other, half_blocks, block_len)
    load_halves(v_all, v_own, v_other, half_blocks, block_len)
    dk_all[...] = jnp.zeros_like(dk_all)
    dv_all[...] = jnp.zeros_like(dv_all)
    dk_glob[...] = jnp.zeros_like(dk_glob)
    dv_glob[...] = jnp.zeros_like(dv_glob)
    low_half = lax.broadcasted_iota(jnp.int32, (block_len, 128), 1) < head_dim
    masks = head_masks(lanes, head_dim, jnp.bfloat16)
    masks_f = head_masks(lanes, head_dim, f32)
    glob = [table[rand_size], table[rand_size + 1]]

    def add_back(grads, near, rand, into, into_glob):
        for n in range(3):
            into[near[n]] += grads[n * block_len : (n + 1) * block_len]
        for n in range(2):
            into_glob[n] += grads[(3 + n) * block_len : (4 + n) * block_len]
        for r in range(picks):
            part = grads[(5 + r) * block_len : (6 + r) * block_len]
            for c in range(lanes // 128):
                cell = part[:, c * 128 : (c + 1) * 128]
                columns = pl.ds(c * 128, 128)
                into[rand[r][2 * c], :, columns] += jnp.where(low_half, cell, 0.0)
                into[rand[r][2 * c + 1], :, columns] += jnp.where(low_half, 0.0, cell)

    def several(number, carry):
        slots = [number * 2 + u for u in range(2)]
        places = [block_places(table, slot, group, sizes) for slot in slots]
        rows = [pl.ds(pl.multiple_of(slot * block_len, block_len), block_len) for slot in slots]
        queries = [spread_heads(q_ref[r, :], masks) for r in rows]
        keys = [key_rows(k_all, near, glob, rand, low_half) for _, near, rand in places]
        scores = [across(key, query) for key, query in zip(keys, queries)]
        grads_out = [spread_heads(go_ref[r, :], masks) for r in rows]
        values = [key_rows(v_all, near, glob, rand, low_half) for _, near, rand in places]
        grad_probs = [across(value, grad) for value, grad in zip(values, grads_out)]
        probs = [
            jnp.exp(mask_scores(score, block, blocks, block_len) - lse_ref[0, pl.ds(slot, 1), :])
            for score, (block, _, _), slot in zip(scores, places, slots)
        ]
        row_dots = [jnp.sum(prob * grad, axis=0, keepdims=True) for prob, grad in zip(probs, grad_probs)]
        grad_scores = [
            (prob * (grad - dot)).astype(jnp.bfloat16) for prob, grad, dot in zip(probs, grad_probs, row_dots)
        ]
        grad_values = [
            jnp.dot(prob.astype(jnp.bfloat16), grad, preferred_element_type=f32) for prob, grad in zip(probs, grads_out)
        ]
        grad_keys = [jnp.dot(grad, query, preferred_element_type=f32) for grad, query in zip(grad_scores, queries)]
        for r, grad, key in zip(rows, grad_scores, keys):
            dq_ref[r, :] = (pick_heads(down(grad, key), masks_f, block_len) * scale).astype(jnp.bfloat16)
        for grad, key_grad, (_, near, rand) in zip(grad_values, grad_keys, places):
            add_back(grad, near, rand, dv_all, dv_glob)
            add_back(key_grad, near, rand, dk_all, dk_glob)
        return carry

    lax.fori_loop(0, half_blocks // 2, several, 0, unroll=4)
    for n in range(2):
        dk_all[glob[n]] += dk_glob[n]
        dv_all[glob[n]] += dv_glob[n]
    for target, start in ((own_ref, 0), (other_ref, half_blocks)):
        for n, source in enumerate((dk_all, dv_all)):
            cells = source[start : start + half_blocks].astype(jnp.bfloat16)
            target[:, n * lanes : (n + 1) * lanes] = cells.reshape(half_blocks * block_len, lanes)


def norm_parts(values):
    average = jnp.mean(values, axis=-1, keepdims=True)
    centred = values - average
    rstd = lax.rsqrt(jnp.mean(centred * centred, axis=-1, keepdims=True) + epsilon)
    return centred * rstd, rstd


def norm_back(grad, normal, rstd, gain):
    scaled = grad * gain
    first = jnp.mean(scaled, axis=-1, keepdims=True)
    second = jnp.mean(scaled * normal, axis=-1, keepdims=True)
    return rstd * (scaled - first - normal * second)


def normal_parts(values):
    cdf = 0.5 + 0.5 * lax.erf(values * 0.5**0.5)
    return cdf, values * jnp.exp(-0.5 * values * values) * 0.3989422804014327


def column_sum(values):
    return jnp.sum(values, axis=0, keepdims=True)


MESH = pl.DeviceIdType.MESH


def tile_order(number):
    return jnp.where(number == 0, 2, jnp.where(number == 2, 3, jnp.where(number == 3, 0, number)))


def position():
    win, blk = lax.axis_index("win"), lax.axis_index("blk")
    return win, blk, win % 2, blk // 2, blk % 2


def owner_of(tile, layers):
    win, blk, core, layer, side = position()
    return (win // 2) * 2 + side, ((layer + layers - tile) % layers) * 2 + core


def greet_owners(layers, peers):
    barrier = pltpu.get_barrier_semaphore()
    others = len(peers)
    for peer in peers:
        pl.semaphore_signal(barrier, inc=1, device_id=peer, device_id_type=MESH)
    _, _, core, _, side = position()
    for tile in range(1, layers):
        pl.semaphore_signal(barrier, inc=1, device_id=owner_of(tile, layers), device_id_type=MESH)

    @pl.when(side != core)
    def _():
        pl.semaphore_signal(barrier, inc=1, device_id=owner_of(0, layers), device_id_type=MESH)
        pl.semaphore_wait(barrier, layers + others)

    @pl.when(side == core)
    def _():
        pl.semaphore_wait(barrier, layers - 1 + others)


def return_tile(tile, source, target, send_sem, recv_sems, start):
    _, _, core, layer, side = position()
    layers = target.shape[0]
    stays = (tile == 0) & (side == core)

    @pl.when(stays)
    def _():
        move = pltpu.make_async_copy(source, target.at[layer], recv_sems.at[tile])
        move.start() if start else move.wait()

    @pl.when(jnp.logical_not(stays))
    def _():
        move = pltpu.make_async_remote_copy(
            src_ref=source, dst_ref=target.at[layer], send_sem=send_sem, recv_sem=recv_sems.at[tile],
            device_id=owner_of(tile, layers), device_id_type=MESH,
        )
        move.start() if start else move.wait()


def regroup_move(source, target, tile, send_sem, recv_sem, start):
    win, _, core, layer, side = position()
    layers = source.shape[0]
    goal = (layer + tile) % layers
    stays = (tile == 0) & (side == core)

    def local():
        return pltpu.make_async_copy(source.at[goal], target, recv_sem)

    def far():
        return pltpu.make_async_remote_copy(
            src_ref=source.at[goal], dst_ref=target, send_sem=send_sem, recv_sem=recv_sem,
            device_id=((win // 2) * 2 + side, goal * 2 + core), device_id_type=MESH,
        )

    @pl.when(stays)
    def _():
        local().start() if start else local().wait()

    @pl.when(jnp.logical_not(stays))
    def _():
        far().start() if start else far().wait()


def arrival_order(number):
    return jnp.where(number == 2, 3, jnp.where(number == 3, 2, number))


def front_kernel(
    scale, tokens, vectors, weight,
    rows_ref, q_ref, kv_ref, other_ref,
    held, kv_rows, send_sems, recv_sems, kv_sems, kv_send, kv_recv, row_sems,
):
    f32, bf16 = jnp.float32, jnp.bfloat16
    step, steps = pl.program_id(0), pl.num_programs(0)
    length, width = held.shape[1:]
    win, blk, core, layer, side = position()
    layers = held.shape[0]
    peer = (win + 1 - 2 * core, blk)

    def token_move(tile, start):
        regroup_move(tokens, held.at[tile], tile, send_sems.at[tile], recv_sems.at[tile], start)

    def rows_of(tile):
        return pl.ds(pl.multiple_of(tile * length, length), length)

    def kv_moves(number):
        tile = arrival_order(number)
        return [
            pltpu.make_async_copy(kv_rows.at[number], kv_ref.at[rows_of(tile)], kv_sems.at[number]),
            pltpu.make_async_copy(held.at[tile], rows_ref.at[rows_of(tile)], row_sems.at[number]),
            pltpu.make_async_remote_copy(
                src_ref=kv_rows.at[number], dst_ref=other_ref.at[rows_of(tile)], send_sem=kv_send.at[number], recv_sem=kv_recv.at[number],
                device_id=peer, device_id_type=MESH,
            ),
        ]

    @pl.when(step == 0)
    def _():
        greet_owners(layers, [peer])
        for n in range(4):
            token_move(arrival_order(n), True)

    tile = arrival_order(step)
    token_move(tile, False)
    normal, _ = norm_parts(held[tile].astype(f32))
    normed = (normal * vectors[0:1] + vectors[1:2]).astype(bf16)

    def part(n):
        return jnp.dot(normed, weight[:, n * width : (n + 1) * width], preferred_element_type=f32)

    kv_rows[step, :, :width] = part(1).astype(bf16)
    kv_rows[step, :, width:] = (part(2) + vectors[3:4]).astype(bf16)
    for move in kv_moves(step):
        move.start()
    q_ref[...] = (part(0) + vectors[2:3]).astype(bf16) * jnp.asarray(scale, bf16)

    @pl.when(step == steps - 1)
    def _():
        for n in range(4):
            for move in kv_moves(n):
                move.wait()


def ffn_forward_kernel(
    chunk, cot_tiles,
    rows_ref, att_ref, w_out, vectors, w_up, b_up, w_down, cotangent,
    out_ref, last_ref, normal_ref, second_ref, att_turned_ref, rstd_ref, active_ref, slope_ref, cot_ref,
    send_sems, recv_sems, up_rows, down_rows, load_sems,
):
    f32, bf16 = jnp.float32, jnp.bfloat16
    step, steps = pl.program_id(0), pl.num_programs(0)

    fetch_up = pltpu.make_async_copy(w_up, up_rows, load_sems.at[0])
    fetch_down = pltpu.make_async_copy(w_down, down_rows, load_sems.at[1])

    @pl.when(step == 0)
    def _():
        fetch_up.start()
        fetch_down.start()
        greet_owners(4, [])
        for n, tile in enumerate(cot_tiles):
            regroup_move(cotangent, cot_ref.at[n], tile, send_sems.at[n], recv_sems.at[n], True)

    wide = up_rows.shape[1]
    b_out, gain, shift, b_down = (vectors.at[n : n + 1] for n in range(4))
    att = att_ref[...]
    residual = rows_ref[...].astype(f32) + (jnp.dot(att, w_out[...], preferred_element_type=f32) + b_out[...])
    normal, rstd = norm_parts(residual)
    second = (normal * gain[...] + shift[...]).astype(bf16)
    normal_ref[...] = normal.astype(bf16)
    second_ref[...] = second.T
    att_turned_ref[...] = att.T
    rstd_ref[...] = jnp.broadcast_to(rstd, rstd_ref.shape)

    @pl.when(step == 0)
    def _():
        fetch_up.wait()
        fetch_down.wait()

    def raise_part(first):
        part = slice(first, first + chunk)
        return jnp.dot(second, up_rows[:, part], preferred_element_type=f32) + b_up[:, part]

    ahead = raise_part(0)
    for first in range(0, wide, chunk):
        inner = ahead
        if first + chunk < wide:
            ahead = raise_part(first + chunk)
        cdf, slope = normal_parts(inner)
        active_ref[:, first : first + chunk] = (inner * cdf).astype(bf16)
        slope_ref[:, first : first + chunk] = (cdf + slope).astype(bf16)
    total = residual + b_down[...] + jnp.dot(active_ref[...], down_rows[...], preferred_element_type=f32)
    out_ref[...] = total.astype(bf16)

    @pl.when(step == steps - 1)
    def _():
        last_ref[...] = total.astype(bf16)
        for n, tile in enumerate(cot_tiles):
            regroup_move(cotangent, cot_ref.at[n], tile, send_sems.at[n], recv_sems.at[n], False)


def ffn_back_kernel(
    chunks, shards, kept_tiles,
    species, active_ref, slope_ref, w_up, w_down, second_t, vectors, normal_in, rstd_in, att_in, w_out_in,
    cot_even, cot_odd, output,
    resid_ref, go_ref, vec_ref, vec_up_ref, keep_ref, other_ref, out_ref,
    cot_rows, branch, branch_t, grad_inner, grad_second, stage_up, stage_down,
    cot_sems, ship_send, ship_recv, cell_send, cell_recv, done_sems, normal_ref, rstd_ref, att_t, w_out, load_sems,
):
    f32, bf16 = jnp.float32, jnp.bfloat16
    step = pl.program_id(0)
    slot = step % 2
    width = w_up.shape[0]
    tiles, length = cot_rows.shape[:2]
    part = width // shards
    half = width // 2
    size = keep_ref.shape[2]
    win, blk, core, _, _ = position()
    peer = (win + 1 - 2 * core, blk)

    def rows_of(n):
        return slice(n * length, (n + 1) * length)

    def ship(what):
        for n, tile in enumerate(kept_tiles):
            return_tile(tile, output.at[rows_of(tile)], out_ref, ship_send.at[n], ship_recv, what)

    def moves(c):
        cuts = []
        if c < chunks:
            base = 4 * c
            for first, count, piece, row in span_cuts(c * part, part, size):
                cuts.append((base + len(cuts), stage_up.at[c % 2, :, pl.ds(first, count)], slice(0, shards), piece, row, count))
            mine = slice(2 * c, 2 * c + 2)
            for first, count, piece, row in span_cuts(chunks * part, half, size):
                cuts.append((24 + base + len(cuts), stage_down.at[c % 2, :, pl.ds(first, count)], mine, piece, row, count))
        else:
            start = chunks * part + half
            for first, count, piece, row in span_cuts(start, 4 * size - start, size):
                cuts.append((20 + len(cuts), stage_up.at[0, :, pl.ds(first, count)], slice(0, shards), piece, row, count))
        return cuts

    def act(c, what):
        for number, source, mine, piece, row, count in moves(c):
            cell = (pl.ds(mine.start, mine.stop - mine.start), piece // 2, pl.ds(row, count))
            def far():
                return pltpu.make_async_remote_copy(
                    src_ref=source, dst_ref=other_ref.at[cell], send_sem=cell_send.at[number], recv_sem=cell_recv.at[number],
                    device_id=peer, device_id_type=MESH,
                )

            @pl.when(core == piece % 2)
            def _():
                if what == "receive":
                    far().wait_recv()
                else:
                    near = pltpu.make_async_copy(source, keep_ref.at[cell], cell_send.at[number])
                    near.start() if what == "start" else near.wait()

            if what != "receive":
                @pl.when(core != piece % 2)
                def _():
                    far().start() if what == "start" else far().wait_send()

    def late_loads():
        pairs = ((normal_in, normal_ref), (rstd_in, rstd_ref), (att_in, att_t), (w_out_in, w_out))
        return [pltpu.make_async_copy(a, b, load_sems.at[n]) for n, (a, b) in enumerate(pairs)]

    windows = species.shape[0]
    mine = species[((win // 2) * 2 + blk % 2) * tiles + blk // 2]
    alike = jnp.zeros((), f32)
    for n in range(windows):
        alike = alike + jnp.where(species[n] == mine, 1.0, 0.0)
    scale = jnp.sqrt(windows / (SPECIES * jnp.full((1, width), alike, f32)))

    def cot_moves():
        return [
            pltpu.make_async_copy((cot_even, cot_odd)[n % 2].at[n // 2], cot_rows.at[n], cot_sems.at[n]) for n in range(4)
        ]

    @pl.when(step == 0)
    def _():
        for move in cot_moves() + late_loads():
            move.start()
        greet_owners(tiles, [peer])
        ship(True)
        vec_ref[...] = jnp.zeros_like(vec_ref)
        for n, move in enumerate(cot_moves()):
            move.wait()
            upstream = cot_rows[n].astype(f32) * scale
            vec_ref[3:4] += column_sum(upstream)
            branch[rows_of(n), :] = upstream.astype(bf16)
            branch_t[:, rows_of(n)] = upstream.astype(bf16).T
        grad_second[...] = jnp.zeros_like(grad_second)

    for c in range(2, chunks):
        @pl.when(step == c)
        def _():
            act(c - 2, "wait")

    full = jnp.dot(branch_t[...], active_ref[...], preferred_element_type=f32)
    for n in range(2):
        for k in range(2):
            stage_down[slot, n, :, k * half : (k + 1) * half] = full[k * half : (k + 1) * half, n * half : (n + 1) * half].astype(bf16)
    total = jnp.zeros((1, w_up.shape[1]), f32)
    for n in range(tiles):
        grad = across(branch[rows_of(n), :], w_down[...]) * slope_ref[rows_of(n), :].astype(f32)
        total = total + column_sum(grad)
        grad_inner[rows_of(n), :] = grad.astype(bf16)
        grad_second[rows_of(n), :] += across(grad_inner[rows_of(n), :], w_up[...])
    vec_up_ref[pl.ds(step, 1), :] = total
    full = jnp.dot(second_t[...], grad_inner[...], preferred_element_type=f32)
    for b in range(shards):
        stage_up[slot, b, 0:part] = full[b * part : (b + 1) * part].astype(bf16)
    for c in range(chunks):
        @pl.when(step == c)
        def _():
            act(c, "start")

    @pl.when(step == chunks - 1)
    def _():
        for move in late_loads():
            move.wait()
        for n in range(tiles):
            upstream = cot_rows[n].astype(f32) * scale
            grad = grad_second[rows_of(n), :]
            normal = normal_ref[rows_of(n), :].astype(f32)
            grad_resid = upstream + norm_back(grad, normal, rstd_ref[rows_of(n), 0:1], vectors[1:2])
            grad_proj = grad_resid.astype(bf16)
            grad_inner[rows_of(n), :] = grad_proj
            branch[rows_of(n), :] = across(grad_proj, w_out[...]).astype(bf16)
            vec_ref[0:1] += column_sum(grad_resid)
            vec_ref[1:2] += column_sum(grad * normal)
            vec_ref[2:3] += column_sum(grad)
        results = [
            pltpu.make_async_copy(grad_inner, resid_ref, done_sems.at[0]),
            pltpu.make_async_copy(branch, go_ref, done_sems.at[1]),
        ]
        for move in results:
            move.start()
        full = jnp.dot(att_t[...], grad_inner[...], preferred_element_type=f32)
        act(chunks - 2, "wait")
        for b in range(shards):
            stage_up[0, b, 0:part] = full[b * part : (b + 1) * part].astype(bf16)
            stage_up[0, b, part:] = jnp.zeros((stage_up.shape[2] - part, width), bf16)
        act(chunks, "start")
        act(chunks - 1, "wait")
        act(chunks, "wait")
        for c in range(chunks + 1):
            act(c, "receive")
        for move in results:
            move.wait()
        ship(False)


def span_cuts(start, count, size):
    cuts, at = [], start
    while at < start + count:
        end = min(start + count, (at // size + 1) * size)
        cuts.append((at - start, end - at, at // size, at % size))
        at = end
    return cuts


def row_cuts(count, part, size):
    cuts = []
    for k in range(count):
        start = k * part
        while start < (k + 1) * part:
            end = min((k + 1) * part, (start // size + 1) * size)
            cuts.append((k, start - k * part, end - start, start // size, start % size))
            start = end
    return cuts


def add_into(target, got):
    target[...] = (target[...].astype(jnp.float32) + got[...].astype(jnp.float32)).astype(jnp.bfloat16)


def finish_kernel(groups, *refs):
    f32, bf16 = jnp.float32, jnp.bfloat16
    parts, others = refs[: 2 * groups], refs[2 * groups : 3 * groups]
    (
        rows_ref, resid_ref, vectors, weight, vec_two, vec_up, early_a, early_b, early_c, early_d,
        tok_ref, late_ref, early_ref,
        joined, turned, vec, out_rows, cells, core_got, late_bufs, early_bufs, send_sems, recv_sems, load_sems, chain_send, chain_recv, keep_sems, last_rows, last_send, last_recv,
    ) = refs[3 * groups :]
    step, steps = pl.program_id(0), pl.num_programs(0)
    length, width = rows_ref.shape
    lanes = width // groups
    part = width // 8
    win, blk, core, layer, side = position()
    pair = win // 2
    core_peer = (win + 1 - 2 * core, blk)
    pair_peer = (win + 2 - 4 * pair, blk)
    side_peer = (win, blk + 1 - 2 * side)
    layer_peers = [(win, ((layer + n) % 4) * 2 + side) for n in (1, 2, 3)]

    def remote(source, target, number, peer):
        return pltpu.make_async_remote_copy(
            src_ref=source, dst_ref=target, send_sem=chain_send.at[number], recv_sem=chain_recv.at[number],
            device_id=peer, device_id_type=MESH,
        )

    early_got, early_final = early_bufs

    def loads():
        return [
            pltpu.make_async_copy(source, early_got.at[n], load_sems.at[n])
            for n, source in enumerate((early_a, early_b, early_c, early_d))
        ]

    def second_step(state, got, base):
        return [
            remote(state.at[0, :, 1 - pair], got.at[0], base, pair_peer),
            remote(state.at[1, :, 1 - side], got.at[1], base + 1, side_peer),
        ]

    def add_second(state, got, mid):
        for z in range(2):
            mid[0, z] = (state[0, z, pair].astype(f32) + got[0, z].astype(f32)).astype(bf16)
            mid[1, z] = (state[1, z, side].astype(f32) + got[1, z].astype(f32)).astype(bf16)

    def layer_step(mid, got, base):
        moves = []
        for n in range(3):
            other = (layer + n + 1) % 4
            moves.append(remote(mid.at[other // 2, other % 2], got.at[n], base + n, layer_peers[n]))
        return moves

    def sum_into(final, parts):
        total = parts[0].astype(f32)
        for one in parts[1:]:
            total = total + one.astype(f32)
        final[...] = total.astype(bf16)

    def share(final, target, base):
        return [
            remote(final, target.at[win], base, core_peer),
            remote(final, target.at[win], base + 1, pair_peer),
        ]

    def pass_on(target, base):
        return [remote(target.at[win + 2 - 4 * pair], target.at[win + 2 - 4 * pair], base, core_peer)]

    def start(moves):
        for move in moves:
            move.start()

    def wait(moves):
        for move in moves:
            move.wait()

    def swap_moves(number):
        first = pl.multiple_of(tile_order(number) * length, length)
        return [
            pltpu.make_async_remote_copy(
                src_ref=others[g].at[pl.ds(first, length)], dst_ref=last_rows.at[g, number], send_sem=last_send.at[g, number],
                recv_sem=last_recv.at[g, number], device_id=core_peer, device_id_type=MESH,
            )
            for g in range(groups)
        ]

    late_first, late_second, late_mid, late_got, late_final = late_bufs
    early_base, late_base = 8, 0
    held = 1

    @pl.when(step == 0)
    def _():
        start(loads())
        greet_owners(steps, [core_peer, pair_peer, side_peer] + layer_peers)
        for n in range(4):
            start(swap_moves(n))
        vec[...] = jnp.zeros_like(vec)

    tile = tile_order(step)
    rows = pl.ds(pl.multiple_of(tile * length, length), length)
    wait(swap_moves(step))
    for g in range(groups):
        dq, own = parts[2 * g : 2 * g + 2]
        other = last_rows.at[g, step]
        columns = slice(g * lanes, (g + 1) * lanes)
        joined[rows, columns] = dq[...]
        both = (own[...].astype(f32) + other[...].astype(f32)).astype(bf16)
        joined[rows, width + g * lanes : width + (g + 1) * lanes] = both[:, :lanes]
        joined[rows, 2 * width + g * lanes : 2 * width + (g + 1) * lanes] = both[:, lanes:]
        vec[0:1, columns] += column_sum(dq[...].astype(f32))
        vec[1:2, columns] += column_sum(both[:, lanes:].astype(f32))
    grad = across(joined[rows, :], weight[...])
    normal, rstd = norm_parts(rows_ref[...].astype(f32))
    turned[tile] = (normal * vectors[0:1] + vectors[1:2]).astype(bf16).T
    vec[2:3] += column_sum(grad * normal)
    vec[3:4] += column_sum(grad)
    out_rows[step] = (resid_ref[...].astype(f32) + norm_back(grad, normal, rstd, vectors[0:1])).astype(bf16)

    @pl.when(step != held)
    def _():
        return_tile(tile, out_rows.at[step], tok_ref, send_sems.at[step], recv_sems, True)


    @pl.when(step == 0)
    def _():
        wait(loads())
        sum_into(early_final, [early_got[n] for n in range(4)])
        start(share(early_final, early_ref, early_base))
        pltpu.make_async_copy(early_final, early_ref.at[win], keep_sems.at[0]).start()

    @pl.when(step == steps - 1)
    def _():
        size = cells.shape[5]
        cuts = row_cuts(3, part, size)
        for k in range(3):
            full = jnp.dot(turned[0], joined[0:length, k * width : (k + 1) * width], preferred_element_type=f32)
            for n in range(1, 4):
                full = full + jnp.dot(
                    turned[n], joined[n * length : (n + 1) * length, k * width : (k + 1) * width], preferred_element_type=f32
                )
            for b in range(8):
                for which, first, count, piece, row in cuts:
                    if which == k:
                        cells[piece % 2, b // 4, b // 2 % 2, b % 2, piece // 2, row : row + count] = full[
                            b * part + first : b * part + first + count
                        ].astype(bf16)
        tail = jnp.concatenate(
            [vec[...], vec_two[...], vec_up[...]]
            + [jnp.zeros((4 * size - 3 * part - 12, width), f32)],
            axis=0,
        ).astype(bf16)
        for b in range(8):
            cells[1, b // 4, b // 2 % 2, b % 2, 1, 3 * part - 3 * size :] = tail
        exchange = [remote(cells.at[1 - core], core_got, late_base, core_peer)]
        start(exchange)
        wait(share(early_final, early_ref, early_base))
        start(pass_on(early_ref, early_base + 2))
        wait(exchange)
        mine = cells.at[core]
        for b in range(8):
            for x in range(2):
                add_into(mine.at[b // 4, b // 2 % 2, b % 2, x], core_got.at[b // 4, b // 2 % 2, b % 2, x])
        first = [
            remote(mine.at[0, :, 1 - side], late_first.at[0], late_base + 1, side_peer),
            remote(mine.at[1, :, :, 1 - pair], late_first.at[1], late_base + 2, pair_peer),
        ]
        start(first)
        wait(first)
        state = core_got.at[0]
        for z in range(2):
            for n in range(2):
                state[0, z, n] = (mine[0, z, side, n].astype(f32) + late_first[0, z, n].astype(f32)).astype(bf16)
                state[1, z, n] = (mine[1, z, n, pair].astype(f32) + late_first[1, z, n].astype(f32)).astype(bf16)
        start(second_step(state, late_second, late_base + 3))
        wait(second_step(state, late_second, late_base + 3))
        add_second(state, late_second, late_mid)
        across_layers = layer_step(late_mid, late_got, late_base + 5)
        start(across_layers)
        return_tile(tile_order(held), out_rows.at[held], tok_ref, send_sems.at[held], recv_sems, True)
        wait(across_layers)
        sum_into(late_final, [late_mid[layer // 2, layer % 2]] + [late_got[n] for n in range(3)])
        start(share(late_final, late_ref, early_base + 3))
        keep_late = pltpu.make_async_copy(late_final, late_ref.at[win], keep_sems.at[1])
        keep_late.start()
        wait(share(late_final, late_ref, early_base + 3))
        start(pass_on(late_ref, early_base + 5))
        wait(pass_on(early_ref, early_base + 2))
        wait(pass_on(late_ref, early_base + 5))
        pltpu.make_async_copy(early_final, early_ref.at[win], keep_sems.at[0]).wait()
        keep_late.wait()
        for n in range(4):
            return_tile(tile_order(n), out_rows.at[n], tok_ref, send_sems.at[n], recv_sems, False)


def first_send_kernel(place, keep_left, other_left, keep_right, other_right, left_ref, right_ref):
    for keep, other, target in ((keep_left, other_left, left_ref), (keep_right, other_right, right_ref)):
        target[...] = (keep[...] + other[...]).reshape(target.shape)


def sum_low(target, refs):
    total = refs[0][...].astype(jnp.float32)
    for ref in refs[1:]:
        total = total + ref[...].astype(jnp.float32)
    target[...] = total.astype(jnp.bfloat16).reshape(target.shape)


def second_send_kernel(place, keep_left, other_left, got_left, keep_right, other_right, got_right, kept, left, right):
    side, pair = place[0], place[1]

    def total(refs, index):
        return sum(ref[index].astype(jnp.float32) for ref in refs).astype(jnp.bfloat16)

    for bit, first, second in ((0, kept.at[0, 0], kept.at[1, 0]), (1, left.at[0], right.at[0])):
        across_pair = pair if bit == 0 else 1 - pair
        across_side = side if bit == 0 else 1 - side
        first[...] = total((keep_left.at[0, 0, 0], other_left.at[0, 0, 0], got_left.at[0]), across_pair)
        second[...] = total((keep_right.at[0, 0, :, 0], other_right.at[0, 0, :, 0], got_right.at[0]), across_side)


def third_send_kernel(place, *refs):
    for n in range(4):
        keep, left, right = refs[3 * n : 3 * n + 3]
        in_left = (place[3] + n) % 4 < 2
        got = jnp.where(in_left, left[...].astype(jnp.float32), right[...].astype(jnp.float32))
        target = refs[12 + n]
        target[...] = (keep[...].reshape(target.shape).astype(jnp.float32) + got.reshape(target.shape)).astype(jnp.bfloat16)


def unpack_kernel(
    early, late, out_tokens, grad_tokens,
    qkv_ref, out_ref, up_ref, down_ref, vec_ref, vec_up_ref, out_tokens_ref, grad_tokens_ref,
    sems,
):
    f32 = jnp.float32
    copies = [
        pltpu.make_async_copy(out_tokens, out_tokens_ref, sems.at[0]),
        pltpu.make_async_copy(grad_tokens, grad_tokens_ref, sems.at[1]),
    ]
    for move in copies:
        move.start()
    part, width = out_ref.shape
    count = up_ref.shape[1] // width
    half = width // 2

    def cells(source, first, rows):
        size = source.shape[1]
        parts = []
        while rows > 0:
            take = min(rows, size - first % size)
            parts.append(source[first // size, first % size : first % size + take])
            first, rows = first + take, rows - take
        return (parts[0] if len(parts) == 1 else jnp.concatenate(parts, axis=0)).astype(f32)

    for k in range(3):
        qkv_ref[:, k * width : (k + 1) * width] = cells(late, k * part, part)
    for k in range(count):
        up_ref[:, k * width : (k + 1) * width] = cells(early, k * part, part)
    turned = cells(early, count * part, half)
    down_ref[:, :half] = turned[:, :half].T
    down_ref[:, half:] = turned[:, half:].T
    out_ref[...] = cells(early, count * part + half, part)
    sums = cells(late, 3 * part, 16)
    blk = lax.axis_index("blk")
    for b in range(width // part):
        @pl.when(blk == b)
        def _():
            vec_ref[...] = sums[0:8, b * part : (b + 1) * part]
            first = b * count * part
            vec_up_ref[...] = sums[8 + first // width : 9 + first // width, first % width : first % width + count * part]

    for move in copies:
        move.wait()


def general_body(
    tokens,
    cotangent,
    w_qkv,
    b_q,
    b_v,
    w_out,
    b_out,
    gain_one,
    shift_one,
    gain_two,
    shift_two,
    w_up,
    b_up,
    w_down,
    b_down,
    rand_owner,
    rand_sub,
    global_ids,
    species,
):
    blk_count = lax.axis_size("blk")
    blk_pos = lax.axis_index("blk")
    win_pos = lax.axis_index("win")
    windows, length, model_width = tokens.shape
    blocks = rand_owner.shape[1]
    heads = rand_owner.shape[2]
    picks = rand_owner.shape[3]
    glob_count = global_ids.shape[1]
    own_blocks = blocks // blk_count
    block_len = length // own_blocks
    head_dim = model_width // heads
    pair_width = 2 * head_dim
    all_rows = windows * length
    key_count = 3 + glob_count + picks
    per_device = own_blocks * heads * picks
    slot_cap = max(2, 2 * per_device // blk_count)
    score_scale = head_dim ** (-0.5)
    f32 = jnp.float32
    bf16 = jnp.bfloat16
    tokens_f = tokens.reshape(all_rows, model_width).astype(f32)
    normed_f, norm_one_pull = jax.vjp(layer_norm, tokens_f, gain_one, shift_one)
    normed = normed_f.astype(bf16)
    joined = jnp.dot(normed, w_qkv, preferred_element_type=f32)
    query_vals = (joined[:, :model_width] + b_q).astype(bf16)
    key_vals = joined[:, model_width : 2 * model_width].astype(bf16)
    value_vals = (joined[:, 2 * model_width :] + b_v).astype(bf16)

    def to_heads(tensor):
        return tensor.reshape(windows, own_blocks, block_len, heads, head_dim).transpose(
            0, 1, 3, 2, 4
        )

    def from_heads(tensor):
        return tensor.transpose(0, 1, 3, 2, 4).reshape(all_rows, model_width)

    query_heads = to_heads(query_vals)
    local_pairs = jnp.concatenate([to_heads(key_vals), to_heads(value_vals)], axis=-1)
    rimmed = padded(local_pairs, (("blk", 1),), 1)
    block_ids = blk_pos * own_blocks + jnp.arange(own_blocks, dtype=jnp.int32)
    owned_glob = (global_ids[:, :, None] == block_ids[None, None, :]).astype(bf16)
    glob_terms = jnp.einsum("wgb,wbhsc->wghsc", owned_glob, local_pairs, preferred_element_type=f32)
    glob_pairs = lax.psum(glob_terms.astype(jnp.bfloat16), "blk").astype(jnp.float32).astype(bf16)
    owner_rows = rand_owner.reshape(windows, blk_count, per_device)
    sub_rows = rand_sub.reshape(windows, blk_count, per_device)
    owner_hits = (owner_rows[..., None] == jnp.arange(blk_count, dtype=jnp.int32)).astype(jnp.int32)
    slot_rows = jnp.sum(owner_hits * (jnp.cumsum(owner_hits, axis=2) - 1), axis=-1)
    my_owner = lax.dynamic_index_in_dim(owner_rows, blk_pos, 1, keepdims=False)
    my_slot = lax.dynamic_index_in_dim(slot_rows, blk_pos, 1, keepdims=False)
    fetch_index = my_owner * slot_cap + my_slot
    head_of_row = jnp.arange(per_device, dtype=jnp.int32) // picks % heads
    source_rows = sub_rows * heads + head_of_row[None, None, :]
    requester = jnp.arange(blk_count, dtype=jnp.int32)[None, :, None]
    target_rows = jnp.where(
        owner_rows == blk_pos, requester * slot_cap + slot_rows, blk_count * slot_cap
    )
    send_table = jnp.full((windows, blk_count * slot_cap + 1), own_blocks * heads, jnp.int32)
    send_table = jax.vmap(set_rows)(
        send_table, target_rows.reshape(windows, -1), source_rows.reshape(windows, -1)
    )[:, : blk_count * slot_cap]
    flat_pairs = jnp.concatenate(
        [
            local_pairs.reshape(windows, own_blocks * heads, block_len, pair_width),
            jnp.zeros((windows, 1, block_len, pair_width), bf16),
        ],
        axis=1,
    )
    outgoing = jax.vmap(take_rows)(flat_pairs, send_table).reshape(
        windows, blk_count, slot_cap, block_len, pair_width
    )
    incoming = lax.all_to_all(outgoing, "blk", split_axis=1, concat_axis=1, tiled=True).reshape(
        windows, blk_count * slot_cap, block_len, pair_width
    )
    rand_pairs = jax.vmap(take_rows)(incoming, fetch_index).reshape(
        windows, own_blocks, heads, picks, block_len, pair_width
    )
    near_pairs = jnp.stack(
        [rimmed[:, 0:own_blocks], rimmed[:, 1 : own_blocks + 1], rimmed[:, 2 : own_blocks + 2]],
        axis=3,
    )
    far_pairs = jnp.broadcast_to(
        glob_pairs.transpose(0, 2, 1, 3, 4)[:, None],
        (windows, own_blocks, heads, glob_count, block_len, pair_width),
    )
    gathered_keys = jnp.concatenate([near_pairs, far_pairs, rand_pairs], axis=3).reshape(
        windows, own_blocks, heads, key_count * block_len, pair_width
    )
    set_keys = gathered_keys[..., :head_dim]
    set_values = gathered_keys[..., head_dim:]
    block_flags = jnp.concatenate(
        [
            (block_ids > 0)[:, None],
            jnp.ones((own_blocks, 1), jnp.bool_),
            (block_ids < blocks - 1)[:, None],
            jnp.ones((own_blocks, glob_count + picks), jnp.bool_),
        ],
        axis=1,
    )
    key_valid = jnp.repeat(block_flags, block_len, axis=1)[None, :, None, None, :]

    def score_block():
        raw_scores = (
            jnp.einsum("wbhqe,wbhke->wbhqk", query_heads, set_keys, preferred_element_type=f32)
            * score_scale
        )
        return jnp.where(key_valid, raw_scores, masked_score)

    score_matrix = score_block()
    top_score = jnp.max(score_matrix, axis=-1, keepdims=True)
    log_total = top_score + jnp.log(
        jnp.sum(jnp.exp(score_matrix - top_score), axis=-1, keepdims=True)
    )
    probs_low = jnp.exp(score_matrix - log_total).astype(bf16)
    attended = jnp.einsum(
        "wbhqk,wbhke->wbhqe", probs_low, set_values, preferred_element_type=f32
    ).astype(bf16)
    merged = from_heads(attended)
    residual = tokens_f + (jnp.dot(merged, w_out, preferred_element_type=f32) + b_out)
    second_f, norm_two_pull = jax.vjp(layer_norm, residual, gain_two, shift_two)
    second = second_f.astype(bf16)
    inner_f = jnp.dot(second, w_up, preferred_element_type=f32) + b_up
    active_f, gelu_pull = jax.vjp(partial(jax.nn.gelu, approximate=False), inner_f)
    active = active_f.astype(bf16)
    output = residual + (jnp.dot(active, w_down, preferred_element_type=f32) + b_down)
    species_count = jnp.sum(
        (species[:, None] == jnp.arange(SPECIES, dtype=jnp.int32)[None, :]).astype(f32), axis=0
    )
    my_species = lax.dynamic_slice_in_dim(species, win_pos * windows, windows)
    own_count = jnp.sum(
        (my_species[:, None] == jnp.arange(SPECIES, dtype=jnp.int32)[None, :]).astype(f32)
        * species_count[None, :],
        axis=1,
    )
    window_scale = jnp.sqrt(species.shape[0] / (SPECIES * own_count))
    upstream = (cotangent.astype(f32) * window_scale[:, None, None]).reshape(all_rows, model_width)
    grad_branch = upstream.astype(bf16)
    grad_w_down = jnp.einsum("tf,td->fd", active, grad_branch, preferred_element_type=f32)
    grad_b_down = jnp.sum(grad_branch, axis=0, dtype=f32)
    grad_active = jnp.einsum("td,fd->tf", grad_branch, w_down, preferred_element_type=f32)
    grad_inner = gelu_pull(grad_active)[0].astype(bf16)
    grad_w_up = jnp.einsum("td,tf->df", second, grad_inner, preferred_element_type=f32)
    grad_b_up = jnp.sum(grad_inner, axis=0, dtype=f32)
    grad_second = jnp.einsum("tf,df->td", grad_inner, w_up, preferred_element_type=f32)
    grad_resid_norm, grad_gain_two, grad_shift_two = norm_two_pull(grad_second)
    grad_resid = upstream + grad_resid_norm
    grad_proj = grad_resid.astype(bf16)
    grad_w_out = jnp.einsum("ti,to->io", merged, grad_proj, preferred_element_type=f32)
    grad_b_out = jnp.sum(grad_proj, axis=0, dtype=f32)
    grad_attended = to_heads(
        jnp.einsum("to,io->ti", grad_proj, w_out, preferred_element_type=f32).astype(bf16)
    )
    probs_full = jnp.exp(score_block() - log_total)
    grad_probs = jnp.einsum(
        "wbhqe,wbhke->wbhqk", grad_attended, set_values, preferred_element_type=f32
    )
    grad_set_values = jnp.einsum(
        "wbhqk,wbhqe->wbhke", probs_full.astype(bf16), grad_attended, preferred_element_type=f32
    )
    row_dot = jnp.sum(probs_full * grad_probs, axis=-1, keepdims=True)
    grad_scores = (probs_full * (grad_probs - row_dot)).astype(bf16)
    grad_query = (
        jnp.einsum("wbhqk,wbhke->wbhqe", grad_scores, set_keys, preferred_element_type=f32)
        * score_scale
    )
    grad_set_keys = (
        jnp.einsum("wbhqk,wbhqe->wbhke", grad_scores, query_heads, preferred_element_type=f32)
        * score_scale
    )
    grad_set = jnp.concatenate([grad_set_keys, grad_set_values], axis=-1).reshape(
        windows, own_blocks, heads, key_count, block_len, pair_width
    )
    extended = (
        jnp.pad(grad_set[:, :, :, 1], ((0, 0), (1, 1), (0, 0), (0, 0), (0, 0)))
        + jnp.pad(grad_set[:, :, :, 0], ((0, 0), (0, 2), (0, 0), (0, 0), (0, 0)))
        + jnp.pad(grad_set[:, :, :, 2], ((0, 0), (2, 0), (0, 0), (0, 0), (0, 0)))
    )
    edge_grads = jnp.concatenate([extended[:, :1], extended[:, own_blocks + 1 :]], axis=1)
    edge_back = padded(edge_grads.astype(jnp.bfloat16), (("blk", 1),), 1).astype(edge_grads.dtype)
    pair_grad = extended[:, 1 : own_blocks + 1]
    pair_grad = pair_grad.at[:, 0].add(edge_back[:, 0]).at[:, own_blocks - 1].add(edge_back[:, 3])
    glob_grad = jnp.sum(grad_set[:, :, :, 3 : 3 + glob_count], axis=1).transpose(0, 2, 1, 3, 4)
    glob_total = lax.psum(glob_grad.astype(jnp.bfloat16), "blk").astype(jnp.float32)
    pair_grad = pair_grad + jnp.einsum(
        "wgb,wghsc->wbhsc", owned_glob.astype(f32), glob_total, precision=lax.Precision.HIGHEST
    )
    rand_grad = grad_set[:, :, :, 3 + glob_count :].reshape(
        windows, per_device, block_len, pair_width
    )
    back_out = jax.vmap(add_rows)(
        jnp.zeros((windows, blk_count * slot_cap, block_len, pair_width), f32),
        fetch_index,
        rand_grad,
    )
    back_in = lax.all_to_all(
        back_out.reshape(windows, blk_count, slot_cap, block_len, pair_width).astype(jnp.bfloat16),
        "blk",
        split_axis=1,
        concat_axis=1,
        tiled=True,
    ).astype(jnp.float32)
    owner_sum = jax.vmap(add_rows)(
        jnp.zeros((windows, own_blocks * heads + 1, block_len, pair_width), f32),
        send_table,
        back_in.reshape(windows, blk_count * slot_cap, block_len, pair_width),
    )
    pair_grad = pair_grad + owner_sum[:, : own_blocks * heads].reshape(
        windows, own_blocks, heads, block_len, pair_width
    )
    grad_keys = from_heads(pair_grad[..., :head_dim].astype(bf16))
    grad_values = from_heads(pair_grad[..., head_dim:].astype(bf16))
    grad_joined = jnp.concatenate(
        [from_heads(grad_query.astype(bf16)), grad_keys, grad_values], axis=1
    )
    grad_w_qkv = jnp.einsum("td,tc->dc", normed, grad_joined, preferred_element_type=f32)
    grad_b_q = jnp.sum(grad_joined[:, :model_width], axis=0, dtype=f32)
    grad_b_v = jnp.sum(grad_joined[:, 2 * model_width :], axis=0, dtype=f32)
    grad_normed = jnp.einsum("tc,dc->td", grad_joined, w_qkv, preferred_element_type=f32)
    grad_tok_norm, grad_gain_one, grad_shift_one = norm_one_pull(grad_normed)
    grad_tokens = (grad_resid + grad_tok_norm).astype(bf16).reshape(windows, length, model_width)
    local_grads = (
        grad_w_qkv,
        grad_b_q,
        grad_b_v,
        grad_w_out,
        grad_b_out,
        grad_gain_one,
        grad_shift_one,
        grad_gain_two,
        grad_shift_two,
        grad_w_up,
        grad_b_up,
        grad_w_down,
        grad_b_down,
    )
    packed_grads = jnp.concatenate(
        [grad_item.reshape(blk_count, -1) for grad_item in local_grads], axis=1
    )
    total_cols = packed_grads.shape[1]
    win_count = lax.axis_size("win")
    pad_cols = -total_cols % win_count
    shard_sum = lax.psum_scatter(
        packed_grads.astype(jnp.bfloat16), "blk", scatter_dimension=0, tiled=True
    ).astype(jnp.float32)
    split_shard = jnp.pad(shard_sum, ((0, 0), (0, pad_cols))).reshape(win_count, -1)
    group_piece = lax.psum_scatter(
        split_shard.astype(jnp.bfloat16), "win", scatter_dimension=0, tiled=True
    ).astype(jnp.float32)
    summed = (
        lax.all_gather(group_piece.astype(jnp.bfloat16), "win", axis=0, tiled=True)
        .astype(group_piece.dtype)
        .reshape(1, -1)[:, :total_cols]
    )
    shards = []
    offset = 0
    for grad_item in local_grads:
        entry_count = grad_item.size // blk_count
        shards.append(
            summed[0, offset : offset + entry_count].reshape(
                (grad_item.shape[0] // blk_count,) + grad_item.shape[1:]
            )
        )
        offset = offset + entry_count
    out_tokens = output.astype(bf16).reshape(windows, length, model_width)
    return (
        out_tokens,
        grad_tokens,
        shards[0],
        shards[1],
        shards[2],
        shards[3],
        shards[4],
        shards[5],
        shards[6],
        shards[7],
        shards[8],
        shards[9],
        shards[10],
        shards[11],
        shards[12],
    )


def layer_step(*arguments):
    windows = arguments[0].shape[0]
    paired = lax.axis_size("blk") == 2 * windows and lax.axis_size("win") == 4 and windows == 4
    return (paired_body if paired else general_body)(*arguments)


def paired_body(
    tokens,
    cotangent,
    w_qkv,
    b_q,
    b_v,
    w_out,
    b_out,
    gain_one,
    shift_one,
    gain_two,
    shift_two,
    w_up,
    b_up,
    w_down,
    b_down,
    rand_owner,
    rand_sub,
    global_ids,
    species,
):
    f32 = jnp.float32
    bf16 = jnp.bfloat16
    win_count = lax.axis_size("win")
    blk_count = lax.axis_size("blk")
    win_pos = lax.axis_index("win")
    blk_pos = lax.axis_index("blk")
    layers, length, width = tokens.shape
    core, layer, side = win_pos % 2, blk_pos // 2, blk_pos % 2
    blocks, heads, picks = rand_owner.shape[1:]
    own_blocks = blocks // blk_count
    half_blocks = blocks // 2
    block_len = length // own_blocks
    head_dim = width // heads
    all_rows = layers * length
    lanes = HEADS_PER_GROUP * head_dim
    groups = heads // HEADS_PER_GROUP
    score_scale = head_dim ** (-0.5)

    def takes(micros):
        return pl.CostEstimate(flops=micros * 1_000_000_000, bytes_accessed=micros * 1_000_000, transcendentals=0)


    rand_size = blocks * heads * picks
    named = jnp.concatenate(
        [
            lax.dynamic_index_in_dim((rand_owner * own_blocks + rand_sub).reshape(layers, rand_size), layer, 0, keepdims=False),
            lax.dynamic_index_in_dim(global_ids, layer, 0, keepdims=False),
        ]
    )
    slot = jnp.arange(half_blocks, dtype=jnp.int32)

    def table_for(which):
        block = (((layer - slot // own_blocks) % layers) * 2 + which) * own_blocks + slot % own_blocks
        reads = jnp.concatenate([named, jnp.maximum(block - 1, 0), jnp.minimum(block + 1, blocks - 1)])
        owner = reads // own_blocks
        half = jnp.where(owner % 2 == which, 0, half_blocks)
        places = half + ((layer - owner // 2) % layers) * own_blocks + reads % own_blocks
        return jnp.concatenate([places, block])

    table = jnp.where(side == core, table_for(core), swap(table_for(1 - core), 1, 0))
    sizes = (heads, picks, rand_size, half_blocks)

    tile = length

    def by_rows(columns):
        return pl.BlockSpec((tile, columns), lambda i: (i, 0))

    def by_tile(columns):
        return pl.BlockSpec((tile, columns), lambda i: (tile_order(i), 0))

    def whole(*shape, once=True):
        mode = pl.Buffered(1) if once else None
        return pl.BlockSpec(shape, lambda i: (0,) * len(shape), pipeline_mode=mode)

    scalars = pl.BlockSpec(memory_space=pltpu.SMEM)
    wide = w_up.shape[1]
    params = pltpu.CompilerParams(vmem_limit_bytes=60 << 20)
    row = lambda vector: vector.reshape(1, -1)
    def remote_params(number, mib):
        return pltpu.CompilerParams(vmem_limit_bytes=mib << 20, collective_id=number, has_side_effects=True)

    any_place = pl.BlockSpec(memory_space=pl.ANY)
    hbm = pl.BlockSpec(memory_space=pltpu.HBM)

    def keep(*shape):
        return pltpu.VMEM(shape, bf16)

    copies = pltpu.SemaphoreType.DMA((layers,))
    vectors_one = jnp.stack([gain_one, shift_one, b_q, b_v])
    vectors_two = jnp.stack([b_out, gain_two, shift_two, b_down])
    rows_in, query, key_value, key_value_other = pl.pallas_call(
        partial(front_kernel, score_scale),
        grid=(layers,),
        in_specs=[any_place, whole(4, width), whole(width, 3 * width)],
        out_specs=[hbm, pl.BlockSpec((tile, width), lambda i: (arrival_order(i), 0)), hbm, hbm],
        out_shape=[
            jax.ShapeDtypeStruct((all_rows, width), bf16),
            jax.ShapeDtypeStruct((all_rows, width), bf16),
            jax.ShapeDtypeStruct((all_rows, 2 * width), bf16),
            jax.ShapeDtypeStruct((all_rows, 2 * width), bf16),
        ],
        scratch_shapes=[keep(layers, length, width), keep(layers, length, 2 * width)] + [copies] * 6,
        compiler_params=remote_params(1, 48),
        cost_estimate=takes(80),
        name="front",
    )(tokens, vectors_one, w_qkv)

    def lane_group(first):
        return pl.BlockSpec((all_rows, lanes), lambda g: (0, first + g))

    store = pltpu.VMEM((blocks, block_len, lanes), bf16)
    halves = layers // 2
    attended, log_total, cot_even = pl.pallas_call(
        partial(attend_kernel, sizes, blocks, head_dim, (0, 2)),
        grid=(groups,),
        in_specs=[scalars] + [lane_group(0), lane_group(0), lane_group(0), lane_group(groups), lane_group(groups), any_place],
        out_specs=[lane_group(0), pl.BlockSpec((1, half_blocks, lanes), lambda g: (g, 0, 0)), hbm],
        out_shape=[
            jax.ShapeDtypeStruct((all_rows, width), bf16),
            jax.ShapeDtypeStruct((groups, half_blocks, lanes), f32),
            jax.ShapeDtypeStruct((halves, length, width), bf16),
        ],
        scratch_shapes=[store, store] + [pltpu.SemaphoreType.DMA((halves,))] * 2,
        compiler_params=remote_params(4, 56),
        cost_estimate=takes(38),
        name="attend",
    )(table, query, key_value, key_value_other, key_value, key_value_other, cotangent)

    payload = 2 * wide // blk_count + width // blk_count
    payload += -payload % (16 * win_count)
    stays = jax.ShapeDtypeStruct((blk_count, win_count // 2, payload // win_count, width), bf16)
    output, out_last, normal, second_t, attended_t, rstd, active, slope, cot_odd = pl.pallas_call(
        partial(ffn_forward_kernel, 256, (1, 3)),
        grid=(layers,),
        in_specs=[
            by_rows(width), by_rows(width), whole(width, width), whole(4, width), any_place, whole(1, wide), any_place, any_place,
        ],
        out_specs=[
            by_rows(width), whole(length, width, once=False), by_rows(width), pl.BlockSpec((width, length), lambda i: (0, i)), pl.BlockSpec((width, length), lambda i: (0, i)),
            by_rows(128), by_rows(wide), by_rows(wide), hbm,
        ],
        out_shape=[
            jax.ShapeDtypeStruct((all_rows, width), bf16),
            jax.ShapeDtypeStruct((length, width), bf16),
            jax.ShapeDtypeStruct((all_rows, width), bf16),
            jax.ShapeDtypeStruct((width, all_rows), bf16),
            jax.ShapeDtypeStruct((width, all_rows), bf16),
            jax.ShapeDtypeStruct((all_rows, 128), f32),
            jax.ShapeDtypeStruct((all_rows, wide), bf16),
            jax.ShapeDtypeStruct((all_rows, wide), bf16),
            jax.ShapeDtypeStruct((halves, length, width), bf16),
        ],
        scratch_shapes=[pltpu.SemaphoreType.DMA((halves,))] * 2 + [keep(width, wide), keep(wide, width), pltpu.SemaphoreType.DMA((2,))],
        compiler_params=remote_params(5, 60),
        cost_estimate=takes(35),
        name="ffn_forward",
    )(rows_in, attended, w_out, vectors_two, w_up, row(b_up), w_down, cotangent)

    chunks = wide // width

    grad_resid, grad_attended, vec_two, vec_up, early_keep, early_other, out_tokens = pl.pallas_call(
        partial(ffn_back_kernel, chunks, blk_count, (2, 1, 0)),
        grid=(chunks,),
        in_specs=[
            scalars, pl.BlockSpec((all_rows, width), lambda i: (0, i)), pl.BlockSpec((all_rows, width), lambda i: (0, i)),
            pl.BlockSpec((width, width), lambda i: (0, i)), pl.BlockSpec((width, width), lambda i: (i, 0)),
            whole(width, all_rows), whole(4, width), *[any_place] * 7,
        ],
        out_specs=[hbm, hbm, whole(4, width), whole(chunks, width), hbm, hbm, hbm],
        out_shape=[
            jax.ShapeDtypeStruct((all_rows, width), bf16),
            jax.ShapeDtypeStruct((all_rows, width), bf16),
            jax.ShapeDtypeStruct((4, width), f32),
            jax.ShapeDtypeStruct((chunks, width), f32),
            stays,
            stays,
            jax.ShapeDtypeStruct((layers, length, width), bf16),
        ],
        scratch_shapes=[
            keep(layers, length, width),
            keep(all_rows, width),
            keep(width, all_rows),
            keep(all_rows, width),
            pltpu.VMEM((all_rows, width), f32),
            keep(2, blk_count, payload - chunks * width // blk_count - width // 2, width),
            keep(2, 2, width // 2, width),
            pltpu.SemaphoreType.DMA((layers,)),
            pltpu.SemaphoreType.DMA((layers,)),
            pltpu.SemaphoreType.DMA((layers,)),
            pltpu.SemaphoreType.DMA((48,)),
            pltpu.SemaphoreType.DMA((48,)),
            pltpu.SemaphoreType.DMA((2,)),
            keep(all_rows, width),
            pltpu.VMEM((all_rows, 128), f32),
            keep(width, all_rows),
            keep(width, width),
            pltpu.SemaphoreType.DMA((4,)),
        ],
        compiler_params=remote_params(3, 63),
        cost_estimate=takes(60),
        name="ffn_back",
    )(
        species, active, slope, w_up, w_down, second_t, vectors_two, normal, rstd, attended_t, w_out, cot_even, cot_odd, output,
    )
    last_pairs = [(there, here) for here, there in regroup_pairs(win_count, layers, 3)]
    out_last = lax.ppermute(out_last, ("win", "blk"), last_pairs)
    pair = win_pos // 2
    early_rows = payload // win_count
    late_rows = 3 * width // blk_count + 32
    late_size = late_rows // win_count
    cell = (early_rows, width)
    early_keep = early_keep.reshape((2, 2, 2, 2) + cell)
    early_other = early_other.reshape((2, 2, 2, 2) + cell)
    place = jnp.stack([side, pair, side, layer])

    def picked(index):
        return pl.BlockSpec((1, 1, 1, 1) + cell, lambda z, n, p: index(z, n, p) + (0, 0))

    def listed(index):
        return pl.BlockSpec((1, 1) + cell, lambda z, n, p: index(z, n, p) + (0, 0))

    def cells_of(count):
        return [jax.ShapeDtypeStruct((2, 2) + cell, bf16)] * count

    def first_send():
        left = picked(lambda z, n, p: (0, z, 1 - p[0], n))
        right = picked(lambda z, n, p: (1, z, n, 1 - p[1]))
        return pl.pallas_call(
            first_send_kernel,
            grid_spec=pltpu.PrefetchScalarGridSpec(
                num_scalar_prefetch=1, grid=(2, 2), in_specs=[left, left, right, right], out_specs=[listed(lambda z, n, p: (z, n))] * 2
            ),
            out_shape=cells_of(2),
            cost_estimate=takes(3),
            name="first_send",
        )(place, early_keep, early_other, early_keep, early_other)

    def second_send(got_left, got_right):
        left = pl.BlockSpec((1, 1, 1, 2) + cell, lambda z, p: (0, z, p[0], 0, 0, 0))
        right = pl.BlockSpec((1, 1, 2, 1) + cell, lambda z, p: (1, z, 0, p[1], 0, 0))
        got = pl.BlockSpec((1, 2) + cell, lambda z, p: (z, 0, 0, 0))
        rows_spec = pl.BlockSpec((1,) + cell, lambda z, p: (z, 0, 0))
        both_spec = pl.BlockSpec((2, 1) + cell, lambda z, p: (0, z, 0, 0))
        return pl.pallas_call(
            second_send_kernel,
            grid_spec=pltpu.PrefetchScalarGridSpec(
                num_scalar_prefetch=1, grid=(2,), in_specs=[left, left, got, right, right, got], out_specs=[both_spec, rows_spec, rows_spec]
            ),
            out_shape=cells_of(1) + [jax.ShapeDtypeStruct((2,) + cell, bf16)] * 2,
            compiler_params=params,
            cost_estimate=takes(4),
            name="second_send",
        )(place, early_keep, early_other, got_left, early_keep, early_other, got_right)

    def third_send(keep, left, right):
        specs = []
        for step in range(layers):
            goal = lambda p, step=step: (p[3] + step) % layers
            specs.append(listed(lambda z, n, p, goal=goal: (goal(p) // 2, goal(p) % 2)))
            specs += [pl.BlockSpec((1,) + cell, lambda z, n, p, goal=goal: (goal(p) % 2, 0, 0))] * 2
        out = pl.BlockSpec(cell, lambda z, n, p: (0, 0))
        return pl.pallas_call(
            third_send_kernel,
            grid_spec=pltpu.PrefetchScalarGridSpec(num_scalar_prefetch=1, grid=(1, 1), in_specs=specs, out_specs=[out] * layers),
            out_shape=[jax.ShapeDtypeStruct(cell, bf16)] * layers,
            cost_estimate=takes(3),
            name="third_send",
        )(place, *[keep, left, right] * layers)

    def to_layer(value, step):
        pairs = [
            (win * blk_count + blk, win * blk_count + (blk + 2 * step) % blk_count)
            for win in range(win_count)
            for blk in range(blk_count)
        ]
        return lax.ppermute(value, ("win", "blk"), pairs)

    first_left, first_right = first_send()
    first_left, first_right = swap(first_left, 0, 1), swap(first_right, 2, 0)

    grad_parts, grad_others = [], []
    for group in range(groups):
        after = []
        if group == 1:
            early_kept, send_left, send_right = second_send(first_left, first_right)
            after = [early_kept, out_last]
            second = swap(send_left, 2, 0), swap(send_right, 0, 1)
        if group == 2:
            early_parts = third_send(early_kept, *second)
            after = [early_parts[0]]
            early_parts = [early_parts[0]] + [to_layer(early_parts[n], n) for n in range(1, layers)]

        def column(first):
            return pl.BlockSpec((all_rows, lanes), lambda g, t: (0, first))

        def full(columns):
            return pl.BlockSpec((all_rows, columns), lambda g, t: (0, 0))

        grad_store = pltpu.VMEM((blocks, block_len, lanes), f32)
        glob_store = pltpu.VMEM((2, block_len, lanes), f32)
        dq, own, other = pl.pallas_call(
            partial(attend_back_kernel, sizes, blocks, head_dim, score_scale, group),
            grid_spec=pltpu.PrefetchScalarGridSpec(
                num_scalar_prefetch=1,
                grid=(1,),
                in_specs=[
                    column(group), column(group), column(group), column(groups + group), column(groups + group), column(group),
                    pl.BlockSpec((1, half_blocks, lanes), lambda g, t: (group, 0, 0)),
                    *[any_place] * len(after),
                ],
                out_specs=[full(lanes), full(2 * lanes), full(2 * lanes)],
                scratch_shapes=[store, store, grad_store, grad_store, glob_store, glob_store],
            ),
            out_shape=[jax.ShapeDtypeStruct((all_rows, n * lanes), bf16) for n in (1, 2, 2)],
            compiler_params=params,
            cost_estimate=takes(25),
            name="attend_back",
        )(table, query, key_value, key_value_other, key_value, key_value_other, grad_attended, log_total, *after)
        grad_parts += [dq, own]
        grad_others.append(other)

    def vmem(*shape):
        return pltpu.VMEM(shape, bf16)

    first_shape, mid_shape = (2, 2, 2), (2, 2)
    chain = lambda size: [vmem(*lead, size, width) for lead in (first_shape, mid_shape, mid_shape, (3,), ())]
    grad_tokens, late, early = pl.pallas_call(
        partial(finish_kernel, groups),
        grid=(layers,),
        in_specs=[by_tile(p.shape[1]) for p in grad_parts]
        + [any_place] * groups
        + [by_tile(width), by_tile(width), whole(4, width), whole(width, 3 * width), whole(4, width), whole(chunks, width)]
        + [any_place] * layers,
        out_specs=[hbm] * 3,
        out_shape=[
            jax.ShapeDtypeStruct((layers, length, width), bf16),
            jax.ShapeDtypeStruct((win_count, late_size, width), bf16),
            jax.ShapeDtypeStruct((win_count, early_rows, width), bf16),
        ],
        scratch_shapes=[
            vmem(all_rows, 3 * width),
            vmem(layers, width, length),
            pltpu.VMEM((4, width), f32),
            vmem(layers, length, width),
            vmem(2, 2, 2, 2, 2, late_size, width),
            vmem(2, 2, 2, 2, late_size, width),
            chain(late_size),
            [vmem(*lead, early_rows, width) for lead in ((4,), ())],
            pltpu.SemaphoreType.DMA((layers,)),
            pltpu.SemaphoreType.DMA((layers,)),
            pltpu.SemaphoreType.DMA((4,)),
            pltpu.SemaphoreType.DMA((14,)),
            pltpu.SemaphoreType.DMA((14,)),
            pltpu.SemaphoreType.DMA((2,)),
            vmem(groups, layers, length, 2 * lanes),
            pltpu.SemaphoreType.DMA((groups, layers)),
            pltpu.SemaphoreType.DMA((groups, layers)),
        ],
        compiler_params=remote_params(2, 62),
        cost_estimate=takes(90),
        name="finish",
    )(
        *grad_parts, *grad_others, rows_in, grad_resid, vectors_one, w_qkv, vec_two, vec_up,
        *early_parts,
    )
    part = width // blk_count
    count = wide // width
    in_vmem = pl.BlockSpec(memory_space=pltpu.VMEM)
    done_qkv, done_out, done_up, done_down, vec, vec_wide, out_tokens, grad_tokens = pl.pallas_call(
        unpack_kernel,
        in_specs=[in_vmem, in_vmem, any_place, any_place],
        out_specs=[in_vmem] * 6 + [hbm] * 2,
        out_shape=[
            jax.ShapeDtypeStruct(shape, f32)
            for shape in ((part, 3 * width), (part, width), (part, wide), (wide // blk_count, width), (8, part), (1, wide // blk_count))
        ]
        + [jax.ShapeDtypeStruct((layers, length, width), bf16)] * 2,
        scratch_shapes=[pltpu.SemaphoreType.DMA((2,))],
        compiler_params=params,
        cost_estimate=takes(4),
        name="unpack",
    )(early, late, lax.dynamic_update_index_in_dim(out_tokens, out_last, (layer + 3) % layers, 0), grad_tokens)
    return (
        out_tokens,
        grad_tokens,
        done_qkv,
        vec[0],
        vec[1],
        done_out,
        vec[4],
        vec[2],
        vec[3],
        vec[5],
        vec[6],
        done_up,
        vec_wide.reshape(-1),
        done_down,
        vec[7],
    )


def solution(mesh):
    placed = (
        P("win", "blk", None),
        P("win", "blk", None),
        P(),
        P(),
        P(),
        P(),
        P(),
        P(),
        P(),
        P(),
        P(),
        P(),
        P(),
        P(),
        P(),
        P("win", None, None, None),
        P("win", None, None, None),
        P("win", None),
        P(),
    )
    return jax.shard_map(
        layer_step,
        mesh=mesh,
        in_specs=placed,
        out_specs=(
            P("win", "blk", None),
            P("win", "blk", None),
            P("blk", None),
            P("blk"),
            P("blk"),
            P("blk", None),
            P("blk"),
            P("blk"),
            P("blk"),
            P("blk"),
            P("blk"),
            P("blk", None),
            P("blk"),
            P("blk", None),
            P("blk"),
        ),
        check_vma=False,
    )
```

```python
from functools import partial

import jax
import jax.numpy as jnp
from jax import lax
from jax.experimental import pallas as pl
from jax.experimental.pallas import tpu as pltpu
from jax.sharding import PartitionSpec as P

SPECIES = 4


epsilon = 1e-05
masked_score = -1000000000.0


def padded(cells, sides, width):
    for axis, dim in sides:
        count = lax.axis_size(axis)
        ends = count - 1
        head = lax.slice_in_dim(cells, 0, width, axis=dim)
        tail = lax.slice_in_dim(cells, cells.shape[dim] - width, cells.shape[dim], axis=dim)
        cells = jnp.concatenate(
            [
                lax.ppermute(tail, axis, [(i, (i + 1) % count) for i in range(ends)]),
                cells,
                lax.ppermute(head, axis, [((i + 1) % count, i) for i in range(ends)]),
            ],
            axis=dim,
        )
    return cells


def layer_norm(values, norm_gain, norm_shift):
    average = jnp.mean(values, axis=-1, keepdims=True)
    centred = values - average
    variance = jnp.mean(centred * centred, axis=-1, keepdims=True)
    return centred * lax.rsqrt(variance + epsilon) * norm_gain + norm_shift


def take_rows(source, index_rows):
    return jnp.take(source, index_rows, axis=0)


def add_rows(base, index_rows, update):
    return base.at[index_rows].add(update)


def set_rows(base, index_rows, update):
    return base.at[index_rows].set(update)


HEADS_PER_GROUP = 4


def regroup_pairs(win_count, layers, step):
    pairs = []
    for win in range(win_count):
        for blk in range(2 * layers):
            layer, side = blk // 2, blk % 2
            target = ((layer + step) % layers) * 2 + win % 2
            pairs.append((win * 2 * layers + blk, ((win // 2) * 2 + side) * 2 * layers + target))
    return pairs


def flip_pairs(win_count, blk_count, win_bit, blk_bit):
    return [
        (win * blk_count + blk, (win ^ win_bit) * blk_count + (blk ^ blk_bit))
        for win in range(win_count)
        for blk in range(blk_count)
    ]


def swap(value, win_bit, blk_bit):
    pairs = flip_pairs(lax.axis_size("win"), lax.axis_size("blk"), win_bit, blk_bit)
    return lax.ppermute(value, ("win", "blk"), pairs)


def head_masks(lanes, head_dim, dtype):
    lane = lax.broadcasted_iota(jnp.int32, (1, lanes), 1)
    return [(lane // head_dim == h).astype(dtype) for h in range(lanes // head_dim)]


def block_places(table, slot, group, sizes):
    heads, picks, rand_size, half_blocks = sizes
    block = table[rand_size + 2 + 2 * half_blocks + slot]
    near = [table[rand_size + 2 + slot], slot, table[rand_size + 2 + half_blocks + slot]]
    row = (block * heads + group * HEADS_PER_GROUP) * picks
    rand = [[table[row + h * picks + r] for h in range(HEADS_PER_GROUP)] for r in range(picks)]
    return block, near, rand


def spread_heads(rows, masks):
    return jnp.concatenate([rows * m for m in masks], axis=0)


def pick_heads(square, masks, height):
    total = square[0:height] * masks[0]
    for h in range(1, len(masks)):
        total = total + square[h * height : (h + 1) * height] * masks[h]
    return total


def key_rows(source, near, glob, rand, low_half):
    parts = [source[p] for p in near] + [source[p] for p in glob]
    for places in rand:
        columns = []
        for c in range(len(places) // 2):
            low = source[places[2 * c], :, c * 128 : (c + 1) * 128]
            high = source[places[2 * c + 1], :, c * 128 : (c + 1) * 128]
            columns.append(jnp.where(low_half, low, high))
        parts.append(jnp.concatenate(columns, axis=1))
    return jnp.concatenate(parts, axis=0)


def mask_scores(scores, block, blocks, block_len):
    first = jnp.where(block > 0, scores[:block_len], masked_score)
    last = jnp.where(block < blocks - 1, scores[2 * block_len : 3 * block_len], masked_score)
    return jnp.concatenate([first, scores[block_len : 2 * block_len], last, scores[3 * block_len :]], axis=0)


def across(left, right):
    return lax.dot_general(left, right, (((1,), (1,)), ((), ())), preferred_element_type=jnp.float32)


def down(left, right):
    return lax.dot_general(left, right, (((0,), (0,)), ((), ())), preferred_element_type=jnp.float32)


def load_halves(target, own, other, half_blocks, block_len):
    lanes = own.shape[-1]
    target[0:half_blocks] = own[...].reshape(half_blocks, block_len, lanes)
    target[half_blocks:] = other[...].reshape(half_blocks, block_len, lanes)


def attend_kernel(
    sizes, blocks, head_dim, cot_tiles,
    table, q_ref, k_own, k_other, v_own, v_other, cotangent,
    o_ref, lse_ref, cot_ref,
    k_all, v_all, send_sems, recv_sems,
):
    heads, picks, rand_size, half_blocks = sizes
    block_len = k_all.shape[1]
    lanes = q_ref.shape[1]
    group = pl.program_id(0)
    _, _, core, layer, _ = position()
    own_blocks = blocks // 8

    @pl.when(group == 0)
    def _():
        greet_owners(4, [])
        for n, tile in enumerate(cot_tiles):
            regroup_move(cotangent, cot_ref.at[n], tile, send_sems.at[n], recv_sems.at[n], True)

    load_halves(k_all, k_own, k_other, half_blocks, block_len)
    load_halves(v_all, v_own, v_other, half_blocks, block_len)
    low_half = lax.broadcasted_iota(jnp.int32, (block_len, 128), 1) < head_dim
    masks = head_masks(lanes, head_dim, jnp.bfloat16)
    masks_f = head_masks(lanes, head_dim, jnp.float32)
    glob = [table[rand_size], table[rand_size + 1]]

    def several(number, carry):
        slots = [number * together + u for u in range(together)]
        places = [block_places(table, slot, group, sizes) for slot in slots]
        numbers = [(((layer + 4 - slot // own_blocks) % 4) * 2 + core) * own_blocks + slot % own_blocks for slot in slots]
        rows = [pl.ds(pl.multiple_of(slot * block_len, block_len), block_len) for slot in slots]
        queries = [spread_heads(q_ref[r, :], masks) for r in rows]
        keys = [key_rows(k_all, near, glob, rand, low_half) for _, near, rand in places]
        scores = [
            mask_scores(across(key, query), block, blocks, block_len) for key, query, block in zip(keys, queries, numbers)
        ]
        tops = [jnp.max(score, axis=0, keepdims=True) for score in scores]
        weights = [jnp.exp(score - top) for score, top in zip(scores, tops)]
        totals = [jnp.sum(weight, axis=0, keepdims=True) for weight in weights]
        probs = [(weight * (1.0 / total)).astype(jnp.bfloat16) for weight, total in zip(weights, totals)]
        values = [key_rows(v_all, near, glob, rand, low_half) for _, near, rand in places]
        for slot, r, prob, value, top, total in zip(slots, rows, probs, values, tops, totals):
            o_ref[r, :] = pick_heads(down(prob, value), masks_f, block_len).astype(jnp.bfloat16)
            lse_ref[0, pl.ds(slot, 1), :] = top + jnp.log(total)
        return carry

    together = 4
    lax.fori_loop(0, half_blocks // together, several, 0, unroll=4)

    @pl.when(group == pl.num_programs(0) - 1)
    def _():
        for n, tile in enumerate(cot_tiles):
            regroup_move(cotangent, cot_ref.at[n], tile, send_sems.at[n], recv_sems.at[n], False)


def attend_back_kernel(
    sizes, blocks, head_dim, scale, group,
    table, q_ref, k_own, k_other, v_own, v_other, go_ref, lse_ref, *refs,
):
    dq_ref, own_ref, other_ref, k_all, v_all, dk_all, dv_all, dk_glob, dv_glob = refs[-9:]
    heads, picks, rand_size, half_blocks = sizes
    block_len = k_all.shape[1]
    lanes = q_ref.shape[1]
    f32 = jnp.float32
    load_halves(k_all, k_own, k_other, half_blocks, block_len)
    load_halves(v_all, v_own, v_other, half_blocks, block_len)
    dk_all[...] = jnp.zeros_like(dk_all)
    dv_all[...] = jnp.zeros_like(dv_all)
    dk_glob[...] = jnp.zeros_like(dk_glob)
    dv_glob[...] = jnp.zeros_like(dv_glob)
    low_half = lax.broadcasted_iota(jnp.int32, (block_len, 128), 1) < head_dim
    masks = head_masks(lanes, head_dim, jnp.bfloat16)
    masks_f = head_masks(lanes, head_dim, f32)
    glob = [table[rand_size], table[rand_size + 1]]

    def add_back(grads, near, rand, into, into_glob):
        for n in range(3):
            into[near[n]] += grads[n * block_len : (n + 1) * block_len]
        for n in range(2):
            into_glob[n] += grads[(3 + n) * block_len : (4 + n) * block_len]
        for r in range(picks):
            part = grads[(5 + r) * block_len : (6 + r) * block_len]
            for c in range(lanes // 128):
                cell = part[:, c * 128 : (c + 1) * 128]
                columns = pl.ds(c * 128, 128)
                into[rand[r][2 * c], :, columns] += jnp.where(low_half, cell, 0.0)
                into[rand[r][2 * c + 1], :, columns] += jnp.where(low_half, 0.0, cell)

    def several(number, carry):
        slots = [number * 2 + u for u in range(2)]
        places = [block_places(table, slot, group, sizes) for slot in slots]
        rows = [pl.ds(pl.multiple_of(slot * block_len, block_len), block_len) for slot in slots]
        queries = [spread_heads(q_ref[r, :], masks) for r in rows]
        keys = [key_rows(k_all, near, glob, rand, low_half) for _, near, rand in places]
        scores = [across(key, query) for key, query in zip(keys, queries)]
        grads_out = [spread_heads(go_ref[r, :], masks) for r in rows]
        values = [key_rows(v_all, near, glob, rand, low_half) for _, near, rand in places]
        grad_probs = [across(value, grad) for value, grad in zip(values, grads_out)]
        probs = [
            jnp.exp(mask_scores(score, block, blocks, block_len) - lse_ref[0, pl.ds(slot, 1), :])
            for score, (block, _, _), slot in zip(scores, places, slots)
        ]
        row_dots = [jnp.sum(prob * grad, axis=0, keepdims=True) for prob, grad in zip(probs, grad_probs)]
        grad_scores = [
            (prob * (grad - dot)).astype(jnp.bfloat16) for prob, grad, dot in zip(probs, grad_probs, row_dots)
        ]
        grad_values = [
            jnp.dot(prob.astype(jnp.bfloat16), grad, preferred_element_type=f32) for prob, grad in zip(probs, grads_out)
        ]
        grad_keys = [jnp.dot(grad, query, preferred_element_type=f32) for grad, query in zip(grad_scores, queries)]
        for r, grad, key in zip(rows, grad_scores, keys):
            dq_ref[r, :] = (pick_heads(down(grad, key), masks_f, block_len) * scale).astype(jnp.bfloat16)
        for grad, key_grad, (_, near, rand) in zip(grad_values, grad_keys, places):
            add_back(grad, near, rand, dv_all, dv_glob)
            add_back(key_grad, near, rand, dk_all, dk_glob)
        return carry

    lax.fori_loop(0, half_blocks // 2, several, 0, unroll=4)
    for n in range(2):
        dk_all[glob[n]] += dk_glob[n]
        dv_all[glob[n]] += dv_glob[n]
    for target, start in ((own_ref, 0), (other_ref, half_blocks)):
        for n, source in enumerate((dk_all, dv_all)):
            cells = source[start : start + half_blocks].astype(jnp.bfloat16)
            target[:, n * lanes : (n + 1) * lanes] = cells.reshape(half_blocks * block_len, lanes)


def norm_parts(values):
    average = jnp.mean(values, axis=-1, keepdims=True)
    centred = values - average
    rstd = lax.rsqrt(jnp.mean(centred * centred, axis=-1, keepdims=True) + epsilon)
    return centred * rstd, rstd


def norm_back(grad, normal, rstd, gain):
    scaled = grad * gain
    first = jnp.mean(scaled, axis=-1, keepdims=True)
    second = jnp.mean(scaled * normal, axis=-1, keepdims=True)
    return rstd * (scaled - first - normal * second)


def normal_parts(values):
    cdf = 0.5 + 0.5 * lax.erf(values * 0.5**0.5)
    return cdf, values * jnp.exp(-0.5 * values * values) * 0.3989422804014327


def column_sum(values):
    return jnp.sum(values, axis=0, keepdims=True)


MESH = pl.DeviceIdType.MESH


def tile_order(number):
    return jnp.where(number == 0, 2, jnp.where(number == 2, 3, jnp.where(number == 3, 0, number)))


def position():
    win, blk = lax.axis_index("win"), lax.axis_index("blk")
    return win, blk, win % 2, blk // 2, blk % 2


def owner_of(tile, layers):
    win, blk, core, layer, side = position()
    return (win // 2) * 2 + side, ((layer + layers - tile) % layers) * 2 + core


def greet_owners(layers, peers):
    barrier = pltpu.get_barrier_semaphore()
    others = len(peers)
    for peer in peers:
        pl.semaphore_signal(barrier, inc=1, device_id=peer, device_id_type=MESH)
    _, _, core, _, side = position()
    for tile in range(1, layers):
        pl.semaphore_signal(barrier, inc=1, device_id=owner_of(tile, layers), device_id_type=MESH)

    @pl.when(side != core)
    def _():
        pl.semaphore_signal(barrier, inc=1, device_id=owner_of(0, layers), device_id_type=MESH)
        pl.semaphore_wait(barrier, layers + others)

    @pl.when(side == core)
    def _():
        pl.semaphore_wait(barrier, layers - 1 + others)


def return_tile(tile, source, target, send_sem, recv_sems, start):
    _, _, core, layer, side = position()
    layers = target.shape[0]
    stays = (tile == 0) & (side == core)

    @pl.when(stays)
    def _():
        move = pltpu.make_async_copy(source, target.at[layer], recv_sems.at[tile])
        move.start() if start else move.wait()

    @pl.when(jnp.logical_not(stays))
    def _():
        move = pltpu.make_async_remote_copy(
            src_ref=source, dst_ref=target.at[layer], send_sem=send_sem, recv_sem=recv_sems.at[tile],
            device_id=owner_of(tile, layers), device_id_type=MESH,
        )
        move.start() if start else move.wait()


def regroup_move(source, target, tile, send_sem, recv_sem, start):
    win, _, core, layer, side = position()
    layers = source.shape[0]
    goal = (layer + tile) % layers
    stays = (tile == 0) & (side == core)

    def local():
        return pltpu.make_async_copy(source.at[goal], target, recv_sem)

    def far():
        return pltpu.make_async_remote_copy(
            src_ref=source.at[goal], dst_ref=target, send_sem=send_sem, recv_sem=recv_sem,
            device_id=((win // 2) * 2 + side, goal * 2 + core), device_id_type=MESH,
        )

    @pl.when(stays)
    def _():
        local().start() if start else local().wait()

    @pl.when(jnp.logical_not(stays))
    def _():
        far().start() if start else far().wait()


def arrival_order(number):
    return jnp.where(number == 2, 3, jnp.where(number == 3, 2, number))


def front_kernel(
    scale, tokens, vectors, weight,
    rows_ref, q_ref, kv_ref, other_ref,
    held, kv_rows, send_sems, recv_sems, kv_sems, kv_send, kv_recv, row_sems,
):
    f32, bf16 = jnp.float32, jnp.bfloat16
    step, steps = pl.program_id(0), pl.num_programs(0)
    length, width = held.shape[1:]
    win, blk, core, layer, side = position()
    layers = held.shape[0]
    peer = (win + 1 - 2 * core, blk)

    def token_move(tile, start):
        regroup_move(tokens, held.at[tile], tile, send_sems.at[tile], recv_sems.at[tile], start)

    def rows_of(tile):
        return pl.ds(pl.multiple_of(tile * length, length), length)

    def kv_moves(number):
        tile = arrival_order(number)
        return [
            pltpu.make_async_copy(kv_rows.at[number], kv_ref.at[rows_of(tile)], kv_sems.at[number]),
            pltpu.make_async_copy(held.at[tile], rows_ref.at[rows_of(tile)], row_sems.at[number]),
            pltpu.make_async_remote_copy(
                src_ref=kv_rows.at[number], dst_ref=other_ref.at[rows_of(tile)], send_sem=kv_send.at[number], recv_sem=kv_recv.at[number],
                device_id=peer, device_id_type=MESH,
            ),
        ]

    @pl.when(step == 0)
    def _():
        greet_owners(layers, [peer])
        for n in range(4):
            token_move(arrival_order(n), True)

    tile = arrival_order(step)
    token_move(tile, False)
    normal, _ = norm_parts(held[tile].astype(f32))
    normed = (normal * vectors[0:1] + vectors[1:2]).astype(bf16)

    def part(n):
        return jnp.dot(normed, weight[:, n * width : (n + 1) * width], preferred_element_type=f32)

    kv_rows[step, :, :width] = part(1).astype(bf16)
    kv_rows[step, :, width:] = (part(2) + vectors[3:4]).astype(bf16)
    for move in kv_moves(step):
        move.start()
    q_ref[...] = (part(0) + vectors[2:3]).astype(bf16) * jnp.asarray(scale, bf16)

    @pl.when(step == steps - 1)
    def _():
        for n in range(4):
            for move in kv_moves(n):
                move.wait()


def ffn_forward_kernel(
    chunk, cot_tiles,
    rows_ref, att_ref, w_out, vectors, w_up, b_up, w_down, cotangent,
    out_ref, last_ref, normal_ref, second_ref, att_turned_ref, rstd_ref, active_ref, slope_ref, cot_ref,
    send_sems, recv_sems, up_rows, down_rows, load_sems,
):
    f32, bf16 = jnp.float32, jnp.bfloat16
    step, steps = pl.program_id(0), pl.num_programs(0)

    fetch_up = pltpu.make_async_copy(w_up, up_rows, load_sems.at[0])
    fetch_down = pltpu.make_async_copy(w_down, down_rows, load_sems.at[1])

    @pl.when(step == 0)
    def _():
        fetch_up.start()
        fetch_down.start()
        greet_owners(4, [])
        for n, tile in enumerate(cot_tiles):
            regroup_move(cotangent, cot_ref.at[n], tile, send_sems.at[n], recv_sems.at[n], True)

    wide = up_rows.shape[1]
    b_out, gain, shift, b_down = (vectors.at[n : n + 1] for n in range(4))
    att = att_ref[...]
    residual = rows_ref[...].astype(f32) + (jnp.dot(att, w_out[...], preferred_element_type=f32) + b_out[...])
    normal, rstd = norm_parts(residual)
    second = (normal * gain[...] + shift[...]).astype(bf16)
    normal_ref[...] = normal.astype(bf16)
    second_ref[...] = second.T
    att_turned_ref[...] = att.T
    rstd_ref[...] = jnp.broadcast_to(rstd, rstd_ref.shape)

    @pl.when(step == 0)
    def _():
        fetch_up.wait()
        fetch_down.wait()

    def raise_part(first):
        part = slice(first, first + chunk)
        return jnp.dot(second, up_rows[:, part], preferred_element_type=f32) + b_up[:, part]

    ahead = raise_part(0)
    for first in range(0, wide, chunk):
        inner = ahead
        if first + chunk < wide:
            ahead = raise_part(first + chunk)
        cdf, slope = normal_parts(inner)
        active_ref[:, first : first + chunk] = (inner * cdf).astype(bf16)
        slope_ref[:, first : first + chunk] = (cdf + slope).astype(bf16)
    total = residual + b_down[...] + jnp.dot(active_ref[...], down_rows[...], preferred_element_type=f32)
    out_ref[...] = total.astype(bf16)

    @pl.when(step == steps - 1)
    def _():
        last_ref[...] = total.astype(bf16)
        for n, tile in enumerate(cot_tiles):
            regroup_move(cotangent, cot_ref.at[n], tile, send_sems.at[n], recv_sems.at[n], False)


def ffn_back_kernel(
    chunks, shards, kept_tiles,
    species, active_ref, slope_ref, w_up, w_down, second_t, vectors, normal_in, rstd_in, att_in, w_out_in,
    cot_even, cot_odd, output,
    resid_ref, go_ref, vec_ref, vec_up_ref, keep_ref, other_ref, out_ref,
    cot_rows, branch, branch_t, grad_inner, grad_second, stage_up, stage_down,
    cot_sems, ship_send, ship_recv, cell_send, cell_recv, done_sems, normal_ref, rstd_ref, att_t, w_out, load_sems,
):
    f32, bf16 = jnp.float32, jnp.bfloat16
    step = pl.program_id(0)
    slot = step % 2
    width = w_up.shape[0]
    tiles, length = cot_rows.shape[:2]
    part = width // shards
    half = width // 2
    size = keep_ref.shape[2]
    win, blk, core, _, _ = position()
    peer = (win + 1 - 2 * core, blk)

    def rows_of(n):
        return slice(n * length, (n + 1) * length)

    def ship(what):
        for n, tile in enumerate(kept_tiles):
            return_tile(tile, output.at[rows_of(tile)], out_ref, ship_send.at[n], ship_recv, what)

    def moves(c):
        cuts = []
        if c < chunks:
            base = 4 * c
            for first, count, piece, row in span_cuts(c * part, part, size):
                cuts.append((base + len(cuts), stage_up.at[c % 2, :, pl.ds(first, count)], slice(0, shards), piece, row, count))
            mine = slice(2 * c, 2 * c + 2)
            for first, count, piece, row in span_cuts(chunks * part, half, size):
                cuts.append((24 + base + len(cuts), stage_down.at[c % 2, :, pl.ds(first, count)], mine, piece, row, count))
        else:
            start = chunks * part + half
            for first, count, piece, row in span_cuts(start, 4 * size - start, size):
                cuts.append((20 + len(cuts), stage_up.at[0, :, pl.ds(first, count)], slice(0, shards), piece, row, count))
        return cuts

    def act(c, what):
        for number, source, mine, piece, row, count in moves(c):
            cell = (pl.ds(mine.start, mine.stop - mine.start), piece // 2, pl.ds(row, count))
            def far():
                return pltpu.make_async_remote_copy(
                    src_ref=source, dst_ref=other_ref.at[cell], send_sem=cell_send.at[number], recv_sem=cell_recv.at[number],
                    device_id=peer, device_id_type=MESH,
                )

            @pl.when(core == piece % 2)
            def _():
                if what == "receive":
                    far().wait_recv()
                else:
                    near = pltpu.make_async_copy(source, keep_ref.at[cell], cell_send.at[number])
                    near.start() if what == "start" else near.wait()

            if what != "receive":
                @pl.when(core != piece % 2)
                def _():
                    far().start() if what == "start" else far().wait_send()

    def late_loads():
        pairs = ((normal_in, normal_ref), (rstd_in, rstd_ref), (att_in, att_t), (w_out_in, w_out))
        return [pltpu.make_async_copy(a, b, load_sems.at[n]) for n, (a, b) in enumerate(pairs)]

    windows = species.shape[0]
    mine = species[((win // 2) * 2 + blk % 2) * tiles + blk // 2]
    alike = jnp.zeros((), f32)
    for n in range(windows):
        alike = alike + jnp.where(species[n] == mine, 1.0, 0.0)
    scale = jnp.sqrt(windows / (SPECIES * jnp.full((1, width), alike, f32)))

    def cot_moves():
        return [
            pltpu.make_async_copy((cot_even, cot_odd)[n % 2].at[n // 2], cot_rows.at[n], cot_sems.at[n]) for n in range(4)
        ]

    @pl.when(step == 0)
    def _():
        for move in cot_moves() + late_loads():
            move.start()
        greet_owners(tiles, [peer])
        ship(True)
        vec_ref[...] = jnp.zeros_like(vec_ref)
        for n, move in enumerate(cot_moves()):
            move.wait()
            upstream = cot_rows[n].astype(f32) * scale
            vec_ref[3:4] += column_sum(upstream)
            branch[rows_of(n), :] = upstream.astype(bf16)
            branch_t[:, rows_of(n)] = upstream.astype(bf16).T
        grad_second[...] = jnp.zeros_like(grad_second)

    for c in range(2, chunks):
        @pl.when(step == c)
        def _():
            act(c - 2, "wait")

    full = jnp.dot(branch_t[...], active_ref[...], preferred_element_type=f32)
    for n in range(2):
        for k in range(2):
            stage_down[slot, n, :, k * half : (k + 1) * half] = full[k * half : (k + 1) * half, n * half : (n + 1) * half].astype(bf16)
    total = jnp.zeros((1, w_up.shape[1]), f32)
    for n in range(tiles):
        grad = across(branch[rows_of(n), :], w_down[...]) * slope_ref[rows_of(n), :].astype(f32)
        total = total + column_sum(grad)
        grad_inner[rows_of(n), :] = grad.astype(bf16)
        grad_second[rows_of(n), :] += across(grad_inner[rows_of(n), :], w_up[...])
    vec_up_ref[pl.ds(step, 1), :] = total
    full = jnp.dot(second_t[...], grad_inner[...], preferred_element_type=f32)
    for b in range(shards):
        stage_up[slot, b, 0:part] = full[b * part : (b + 1) * part].astype(bf16)
    for c in range(chunks):
        @pl.when(step == c)
        def _():
            act(c, "start")

    @pl.when(step == chunks - 1)
    def _():
        for move in late_loads():
            move.wait()
        for n in range(tiles):
            upstream = cot_rows[n].astype(f32) * scale
            grad = grad_second[rows_of(n), :]
            normal = normal_ref[rows_of(n), :].astype(f32)
            grad_resid = upstream + norm_back(grad, normal, rstd_ref[rows_of(n), 0:1], vectors[1:2])
            grad_proj = grad_resid.astype(bf16)
            grad_inner[rows_of(n), :] = grad_proj
            branch[rows_of(n), :] = across(grad_proj, w_out[...]).astype(bf16)
            vec_ref[0:1] += column_sum(grad_resid)
            vec_ref[1:2] += column_sum(grad * normal)
            vec_ref[2:3] += column_sum(grad)
        results = [
            pltpu.make_async_copy(grad_inner, resid_ref, done_sems.at[0]),
            pltpu.make_async_copy(branch, go_ref, done_sems.at[1]),
        ]
        for move in results:
            move.start()
        full = jnp.dot(att_t[...], grad_inner[...], preferred_element_type=f32)
        act(chunks - 2, "wait")
        for b in range(shards):
            stage_up[0, b, 0:part] = full[b * part : (b + 1) * part].astype(bf16)
            stage_up[0, b, part:] = jnp.zeros((stage_up.shape[2] - part, width), bf16)
        act(chunks, "start")
        act(chunks - 1, "wait")
        act(chunks, "wait")
        for c in range(chunks + 1):
            act(c, "receive")
        for move in results:
            move.wait()
        ship(False)


def span_cuts(start, count, size):
    cuts, at = [], start
    while at < start + count:
        end = min(start + count, (at // size + 1) * size)
        cuts.append((at - start, end - at, at // size, at % size))
        at = end
    return cuts


def row_cuts(count, part, size):
    cuts = []
    for k in range(count):
        start = k * part
        while start < (k + 1) * part:
            end = min((k + 1) * part, (start // size + 1) * size)
            cuts.append((k, start - k * part, end - start, start // size, start % size))
            start = end
    return cuts


def add_into(target, got):
    target[...] = (target[...].astype(jnp.float32) + got[...].astype(jnp.float32)).astype(jnp.bfloat16)


def finish_kernel(groups, *refs):
    f32, bf16 = jnp.float32, jnp.bfloat16
    parts, others = refs[: 2 * groups], refs[2 * groups : 3 * groups]
    (
        rows_ref, resid_ref, vectors, weight, vec_two, vec_up, early_a, early_b, early_c, early_d,
        tok_ref, late_ref, early_ref,
        joined, turned, vec, out_rows, cells, core_got, late_bufs, early_bufs, send_sems, recv_sems, load_sems, chain_send, chain_recv, keep_sems, last_rows, last_send, last_recv,
    ) = refs[3 * groups :]
    step, steps = pl.program_id(0), pl.num_programs(0)
    length, width = rows_ref.shape
    lanes = width // groups
    part = width // 8
    win, blk, core, layer, side = position()
    pair = win // 2
    core_peer = (win + 1 - 2 * core, blk)
    pair_peer = (win + 2 - 4 * pair, blk)
    side_peer = (win, blk + 1 - 2 * side)
    layer_peers = [(win, ((layer + n) % 4) * 2 + side) for n in (1, 2, 3)]

    def remote(source, target, number, peer):
        return pltpu.make_async_remote_copy(
            src_ref=source, dst_ref=target, send_sem=chain_send.at[number], recv_sem=chain_recv.at[number],
            device_id=peer, device_id_type=MESH,
        )

    early_got, early_final = early_bufs

    def loads():
        return [
            pltpu.make_async_copy(source, early_got.at[n], load_sems.at[n])
            for n, source in enumerate((early_a, early_b, early_c, early_d))
        ]

    def second_step(state, got, base):
        return [
            remote(state.at[0, :, 1 - pair], got.at[0], base, pair_peer),
            remote(state.at[1, :, 1 - side], got.at[1], base + 1, side_peer),
        ]

    def add_second(state, got, mid):
        for z in range(2):
            mid[0, z] = (state[0, z, pair].astype(f32) + got[0, z].astype(f32)).astype(bf16)
            mid[1, z] = (state[1, z, side].astype(f32) + got[1, z].astype(f32)).astype(bf16)

    def layer_step(mid, got, base):
        moves = []
        for n in range(3):
            other = (layer + n + 1) % 4
            moves.append(remote(mid.at[other // 2, other % 2], got.at[n], base + n, layer_peers[n]))
        return moves

    def sum_into(final, parts):
        total = parts[0].astype(f32)
        for one in parts[1:]:
            total = total + one.astype(f32)
        final[...] = total.astype(bf16)

    def share(final, target, base):
        return [
            remote(final, target.at[win], base, core_peer),
            remote(final, target.at[win], base + 1, pair_peer),
        ]

    def pass_on(target, base):
        return [remote(target.at[win + 2 - 4 * pair], target.at[win + 2 - 4 * pair], base, core_peer)]

    def start(moves):
        for move in moves:
            move.start()

    def wait(moves):
        for move in moves:
            move.wait()

    def swap_moves(number):
        first = pl.multiple_of(tile_order(number) * length, length)
        return [
            pltpu.make_async_remote_copy(
                src_ref=others[g].at[pl.ds(first, length)], dst_ref=last_rows.at[g, number], send_sem=last_send.at[g, number],
                recv_sem=last_recv.at[g, number], device_id=core_peer, device_id_type=MESH,
            )
            for g in range(groups)
        ]

    late_first, late_second, late_mid, late_got, late_final = late_bufs
    early_base, late_base = 8, 0
    held = 1

    @pl.when(step == 0)
    def _():
        start(loads())
        greet_owners(steps, [core_peer, pair_peer, side_peer] + layer_peers)
        for n in range(4):
            start(swap_moves(n))
        vec[...] = jnp.zeros_like(vec)

    tile = tile_order(step)
    rows = pl.ds(pl.multiple_of(tile * length, length), length)
    wait(swap_moves(step))
    for g in range(groups):
        dq, own = parts[2 * g : 2 * g + 2]
        other = last_rows.at[g, step]
        columns = slice(g * lanes, (g + 1) * lanes)
        joined[rows, columns] = dq[...]
        both = (own[...].astype(f32) + other[...].astype(f32)).astype(bf16)
        joined[rows, width + g * lanes : width + (g + 1) * lanes] = both[:, :lanes]
        joined[rows, 2 * width + g * lanes : 2 * width + (g + 1) * lanes] = both[:, lanes:]
        vec[0:1, columns] += column_sum(dq[...].astype(f32))
        vec[1:2, columns] += column_sum(both[:, lanes:].astype(f32))
    grad = across(joined[rows, :], weight[...])
    normal, rstd = norm_parts(rows_ref[...].astype(f32))
    turned[tile] = (normal * vectors[0:1] + vectors[1:2]).astype(bf16).T
    vec[2:3] += column_sum(grad * normal)
    vec[3:4] += column_sum(grad)
    out_rows[step] = (resid_ref[...].astype(f32) + norm_back(grad, normal, rstd, vectors[0:1])).astype(bf16)

    @pl.when(step != held)
    def _():
        return_tile(tile, out_rows.at[step], tok_ref, send_sems.at[step], recv_sems, True)


    @pl.when(step == 0)
    def _():
        wait(loads())
        sum_into(early_final, [early_got[n] for n in range(4)])
        start(share(early_final, early_ref, early_base))
        pltpu.make_async_copy(early_final, early_ref.at[win], keep_sems.at[0]).start()

    @pl.when(step == steps - 1)
    def _():
        size = cells.shape[5]
        cuts = row_cuts(3, part, size)
        for k in range(3):
            full = jnp.dot(turned[0], joined[0:length, k * width : (k + 1) * width], preferred_element_type=f32)
            for n in range(1, 4):
                full = full + jnp.dot(
                    turned[n], joined[n * length : (n + 1) * length, k * width : (k + 1) * width], preferred_element_type=f32
                )
            for b in range(8):
                for which, first, count, piece, row in cuts:
                    if which == k:
                        cells[piece % 2, b // 4, b // 2 % 2, b % 2, piece // 2, row : row + count] = full[
                            b * part + first : b * part + first + count
                        ].astype(bf16)
        tail = jnp.concatenate(
            [vec[...], vec_two[...], vec_up[...]]
            + [jnp.zeros((4 * size - 3 * part - 12, width), f32)],
            axis=0,
        ).astype(bf16)
        for b in range(8):
            cells[1, b // 4, b // 2 % 2, b % 2, 1, 3 * part - 3 * size :] = tail
        exchange = [remote(cells.at[1 - core], core_got, late_base, core_peer)]
        start(exchange)
        wait(share(early_final, early_ref, early_base))
        start(pass_on(early_ref, early_base + 2))
        wait(exchange)
        mine = cells.at[core]
        for b in range(8):
            for x in range(2):
                add_into(mine.at[b // 4, b // 2 % 2, b % 2, x], core_got.at[b // 4, b // 2 % 2, b % 2, x])
        first = [
            remote(mine.at[0, :, 1 - side], late_first.at[0], late_base + 1, side_peer),
            remote(mine.at[1, :, :, 1 - pair], late_first.at[1], late_base + 2, pair_peer),
        ]
        start(first)
        wait(first)
        state = core_got.at[0]
        for z in range(2):
            for n in range(2):
                state[0, z, n] = (mine[0, z, side, n].astype(f32) + late_first[0, z, n].astype(f32)).astype(bf16)
                state[1, z, n] = (mine[1, z, n, pair].astype(f32) + late_first[1, z, n].astype(f32)).astype(bf16)
        start(second_step(state, late_second, late_base + 3))
        wait(second_step(state, late_second, late_base + 3))
        add_second(state, late_second, late_mid)
        across_layers = layer_step(late_mid, late_got, late_base + 5)
        start(across_layers)
        return_tile(tile_order(held), out_rows.at[held], tok_ref, send_sems.at[held], recv_sems, True)
        wait(across_layers)
        sum_into(late_final, [late_mid[layer // 2, layer % 2]] + [late_got[n] for n in range(3)])
        start(share(late_final, late_ref, early_base + 3))
        keep_late = pltpu.make_async_copy(late_final, late_ref.at[win], keep_sems.at[1])
        keep_late.start()
        wait(share(late_final, late_ref, early_base + 3))
        start(pass_on(late_ref, early_base + 5))
        wait(pass_on(early_ref, early_base + 2))
        wait(pass_on(late_ref, early_base + 5))
        pltpu.make_async_copy(early_final, early_ref.at[win], keep_sems.at[0]).wait()
        keep_late.wait()
        for n in range(4):
            return_tile(tile_order(n), out_rows.at[n], tok_ref, send_sems.at[n], recv_sems, False)


def first_send_kernel(place, keep_left, other_left, keep_right, other_right, left_ref, right_ref):
    for keep, other, target in ((keep_left, other_left, left_ref), (keep_right, other_right, right_ref)):
        target[...] = (keep[...] + other[...]).reshape(target.shape)


def sum_low(target, refs):
    total = refs[0][...].astype(jnp.float32)
    for ref in refs[1:]:
        total = total + ref[...].astype(jnp.float32)
    target[...] = total.astype(jnp.bfloat16).reshape(target.shape)


def second_send_kernel(place, keep_left, other_left, got_left, keep_right, other_right, got_right, kept, left, right):
    side, pair = place[0], place[1]

    def total(refs, index):
        return sum(ref[index].astype(jnp.float32) for ref in refs).astype(jnp.bfloat16)

    for bit, first, second in ((0, kept.at[0, 0], kept.at[1, 0]), (1, left.at[0], right.at[0])):
        across_pair = pair if bit == 0 else 1 - pair
        across_side = side if bit == 0 else 1 - side
        first[...] = total((keep_left.at[0, 0, 0], other_left.at[0, 0, 0], got_left.at[0]), across_pair)
        second[...] = total((keep_right.at[0, 0, :, 0], other_right.at[0, 0, :, 0], got_right.at[0]), across_side)


def third_send_kernel(place, *refs):
    for n in range(4):
        keep, left, right = refs[3 * n : 3 * n + 3]
        in_left = (place[3] + n) % 4 < 2
        got = jnp.where(in_left, left[...].astype(jnp.float32), right[...].astype(jnp.float32))
        target = refs[12 + n]
        target[...] = (keep[...].reshape(target.shape).astype(jnp.float32) + got.reshape(target.shape)).astype(jnp.bfloat16)


def unpack_kernel(
    early, late, out_tokens, grad_tokens,
    qkv_ref, out_ref, up_ref, down_ref, vec_ref, vec_up_ref, out_tokens_ref, grad_tokens_ref,
    held, in_sems, out_sems,
):
    f32 = jnp.float32
    layers = out_tokens.shape[0]
    places = [(n, j) for j in range(layers) for n in range(2)]

    def bring(n, j):
        return pltpu.make_async_copy((out_tokens, grad_tokens)[n].at[j], held.at[n, j], in_sems.at[n, j])

    def take(n, j):
        return pltpu.make_async_copy(held.at[n, j], (out_tokens_ref, grad_tokens_ref)[n].at[j], out_sems.at[n, j])

    for place in places:
        bring(*place).start()
    part, width = out_ref.shape
    count = up_ref.shape[1] // width
    half = width // 2

    def cells(source, first, rows):
        size = source.shape[1]
        parts = []
        while rows > 0:
            take = min(rows, size - first % size)
            parts.append(source[first // size, first % size : first % size + take])
            first, rows = first + take, rows - take
        return (parts[0] if len(parts) == 1 else jnp.concatenate(parts, axis=0)).astype(f32)

    for k in range(3):
        qkv_ref[:, k * width : (k + 1) * width] = cells(late, k * part, part)
    for place in places:
        bring(*place).wait()
        take(*place).start()
    for k in range(count):
        up_ref[:, k * width : (k + 1) * width] = cells(early, k * part, part)
    turned = cells(early, count * part, half)
    down_ref[:, :half] = turned[:, :half].T
    down_ref[:, half:] = turned[:, half:].T
    out_ref[...] = cells(early, count * part + half, part)
    sums = cells(late, 3 * part, 16)
    blk = lax.axis_index("blk")
    for b in range(width // part):
        @pl.when(blk == b)
        def _():
            vec_ref[...] = sums[0:8, b * part : (b + 1) * part]
            first = b * count * part
            vec_up_ref[...] = sums[8 + first // width : 9 + first // width, first % width : first % width + count * part]

    for place in places:
        take(*place).wait()


def general_body(
    tokens,
    cotangent,
    w_qkv,
    b_q,
    b_v,
    w_out,
    b_out,
    gain_one,
    shift_one,
    gain_two,
    shift_two,
    w_up,
    b_up,
    w_down,
    b_down,
    rand_owner,
    rand_sub,
    global_ids,
    species,
):
    blk_count = lax.axis_size("blk")
    blk_pos = lax.axis_index("blk")
    win_pos = lax.axis_index("win")
    windows, length, model_width = tokens.shape
    blocks = rand_owner.shape[1]
    heads = rand_owner.shape[2]
    picks = rand_owner.shape[3]
    glob_count = global_ids.shape[1]
    own_blocks = blocks // blk_count
    block_len = length // own_blocks
    head_dim = model_width // heads
    pair_width = 2 * head_dim
    all_rows = windows * length
    key_count = 3 + glob_count + picks
    per_device = own_blocks * heads * picks
    slot_cap = max(2, 2 * per_device // blk_count)
    score_scale = head_dim ** (-0.5)
    f32 = jnp.float32
    bf16 = jnp.bfloat16
    tokens_f = tokens.reshape(all_rows, model_width).astype(f32)
    normed_f, norm_one_pull = jax.vjp(layer_norm, tokens_f, gain_one, shift_one)
    normed = normed_f.astype(bf16)
    joined = jnp.dot(normed, w_qkv, preferred_element_type=f32)
    query_vals = (joined[:, :model_width] + b_q).astype(bf16)
    key_vals = joined[:, model_width : 2 * model_width].astype(bf16)
    value_vals = (joined[:, 2 * model_width :] + b_v).astype(bf16)

    def to_heads(tensor):
        return tensor.reshape(windows, own_blocks, block_len, heads, head_dim).transpose(
            0, 1, 3, 2, 4
        )

    def from_heads(tensor):
        return tensor.transpose(0, 1, 3, 2, 4).reshape(all_rows, model_width)

    query_heads = to_heads(query_vals)
    local_pairs = jnp.concatenate([to_heads(key_vals), to_heads(value_vals)], axis=-1)
    rimmed = padded(local_pairs, (("blk", 1),), 1)
    block_ids = blk_pos * own_blocks + jnp.arange(own_blocks, dtype=jnp.int32)
    owned_glob = (global_ids[:, :, None] == block_ids[None, None, :]).astype(bf16)
    glob_terms = jnp.einsum("wgb,wbhsc->wghsc", owned_glob, local_pairs, preferred_element_type=f32)
    glob_pairs = lax.psum(glob_terms.astype(jnp.bfloat16), "blk").astype(jnp.float32).astype(bf16)
    owner_rows = rand_owner.reshape(windows, blk_count, per_device)
    sub_rows = rand_sub.reshape(windows, blk_count, per_device)
    owner_hits = (owner_rows[..., None] == jnp.arange(blk_count, dtype=jnp.int32)).astype(jnp.int32)
    slot_rows = jnp.sum(owner_hits * (jnp.cumsum(owner_hits, axis=2) - 1), axis=-1)
    my_owner = lax.dynamic_index_in_dim(owner_rows, blk_pos, 1, keepdims=False)
    my_slot = lax.dynamic_index_in_dim(slot_rows, blk_pos, 1, keepdims=False)
    fetch_index = my_owner * slot_cap + my_slot
    head_of_row = jnp.arange(per_device, dtype=jnp.int32) // picks % heads
    source_rows = sub_rows * heads + head_of_row[None, None, :]
    requester = jnp.arange(blk_count, dtype=jnp.int32)[None, :, None]
    target_rows = jnp.where(
        owner_rows == blk_pos, requester * slot_cap + slot_rows, blk_count * slot_cap
    )
    send_table = jnp.full((windows, blk_count * slot_cap + 1), own_blocks * heads, jnp.int32)
    send_table = jax.vmap(set_rows)(
        send_table, target_rows.reshape(windows, -1), source_rows.reshape(windows, -1)
    )[:, : blk_count * slot_cap]
    flat_pairs = jnp.concatenate(
        [
            local_pairs.reshape(windows, own_blocks * heads, block_len, pair_width),
            jnp.zeros((windows, 1, block_len, pair_width), bf16),
        ],
        axis=1,
    )
    outgoing = jax.vmap(take_rows)(flat_pairs, send_table).reshape(
        windows, blk_count, slot_cap, block_len, pair_width
    )
    incoming = lax.all_to_all(outgoing, "blk", split_axis=1, concat_axis=1, tiled=True).reshape(
        windows, blk_count * slot_cap, block_len, pair_width
    )
    rand_pairs = jax.vmap(take_rows)(incoming, fetch_index).reshape(
        windows, own_blocks, heads, picks, block_len, pair_width
    )
    near_pairs = jnp.stack(
        [rimmed[:, 0:own_blocks], rimmed[:, 1 : own_blocks + 1], rimmed[:, 2 : own_blocks + 2]],
        axis=3,
    )
    far_pairs = jnp.broadcast_to(
        glob_pairs.transpose(0, 2, 1, 3, 4)[:, None],
        (windows, own_blocks, heads, glob_count, block_len, pair_width),
    )
    gathered_keys = jnp.concatenate([near_pairs, far_pairs, rand_pairs], axis=3).reshape(
        windows, own_blocks, heads, key_count * block_len, pair_width
    )
    set_keys = gathered_keys[..., :head_dim]
    set_values = gathered_keys[..., head_dim:]
    block_flags = jnp.concatenate(
        [
            (block_ids > 0)[:, None],
            jnp.ones((own_blocks, 1), jnp.bool_),
            (block_ids < blocks - 1)[:, None],
            jnp.ones((own_blocks, glob_count + picks), jnp.bool_),
        ],
        axis=1,
    )
    key_valid = jnp.repeat(block_flags, block_len, axis=1)[None, :, None, None, :]

    def score_block():
        raw_scores = (
            jnp.einsum("wbhqe,wbhke->wbhqk", query_heads, set_keys, preferred_element_type=f32)
            * score_scale
        )
        return jnp.where(key_valid, raw_scores, masked_score)

    score_matrix = score_block()
    top_score = jnp.max(score_matrix, axis=-1, keepdims=True)
    log_total = top_score + jnp.log(
        jnp.sum(jnp.exp(score_matrix - top_score), axis=-1, keepdims=True)
    )
    probs_low = jnp.exp(score_matrix - log_total).astype(bf16)
    attended = jnp.einsum(
        "wbhqk,wbhke->wbhqe", probs_low, set_values, preferred_element_type=f32
    ).astype(bf16)
    merged = from_heads(attended)
    residual = tokens_f + (jnp.dot(merged, w_out, preferred_element_type=f32) + b_out)
    second_f, norm_two_pull = jax.vjp(layer_norm, residual, gain_two, shift_two)
    second = second_f.astype(bf16)
    inner_f = jnp.dot(second, w_up, preferred_element_type=f32) + b_up
    active_f, gelu_pull = jax.vjp(partial(jax.nn.gelu, approximate=False), inner_f)
    active = active_f.astype(bf16)
    output = residual + (jnp.dot(active, w_down, preferred_element_type=f32) + b_down)
    species_count = jnp.sum(
        (species[:, None] == jnp.arange(SPECIES, dtype=jnp.int32)[None, :]).astype(f32), axis=0
    )
    my_species = lax.dynamic_slice_in_dim(species, win_pos * windows, windows)
    own_count = jnp.sum(
        (my_species[:, None] == jnp.arange(SPECIES, dtype=jnp.int32)[None, :]).astype(f32)
        * species_count[None, :],
        axis=1,
    )
    window_scale = jnp.sqrt(species.shape[0] / (SPECIES * own_count))
    upstream = (cotangent.astype(f32) * window_scale[:, None, None]).reshape(all_rows, model_width)
    grad_branch = upstream.astype(bf16)
    grad_w_down = jnp.einsum("tf,td->fd", active, grad_branch, preferred_element_type=f32)
    grad_b_down = jnp.sum(grad_branch, axis=0, dtype=f32)
    grad_active = jnp.einsum("td,fd->tf", grad_branch, w_down, preferred_element_type=f32)
    grad_inner = gelu_pull(grad_active)[0].astype(bf16)
    grad_w_up = jnp.einsum("td,tf->df", second, grad_inner, preferred_element_type=f32)
    grad_b_up = jnp.sum(grad_inner, axis=0, dtype=f32)
    grad_second = jnp.einsum("tf,df->td", grad_inner, w_up, preferred_element_type=f32)
    grad_resid_norm, grad_gain_two, grad_shift_two = norm_two_pull(grad_second)
    grad_resid = upstream + grad_resid_norm
    grad_proj = grad_resid.astype(bf16)
    grad_w_out = jnp.einsum("ti,to->io", merged, grad_proj, preferred_element_type=f32)
    grad_b_out = jnp.sum(grad_proj, axis=0, dtype=f32)
    grad_attended = to_heads(
        jnp.einsum("to,io->ti", grad_proj, w_out, preferred_element_type=f32).astype(bf16)
    )
    probs_full = jnp.exp(score_block() - log_total)
    grad_probs = jnp.einsum(
        "wbhqe,wbhke->wbhqk", grad_attended, set_values, preferred_element_type=f32
    )
    grad_set_values = jnp.einsum(
        "wbhqk,wbhqe->wbhke", probs_full.astype(bf16), grad_attended, preferred_element_type=f32
    )
    row_dot = jnp.sum(probs_full * grad_probs, axis=-1, keepdims=True)
    grad_scores = (probs_full * (grad_probs - row_dot)).astype(bf16)
    grad_query = (
        jnp.einsum("wbhqk,wbhke->wbhqe", grad_scores, set_keys, preferred_element_type=f32)
        * score_scale
    )
    grad_set_keys = (
        jnp.einsum("wbhqk,wbhqe->wbhke", grad_scores, query_heads, preferred_element_type=f32)
        * score_scale
    )
    grad_set = jnp.concatenate([grad_set_keys, grad_set_values], axis=-1).reshape(
        windows, own_blocks, heads, key_count, block_len, pair_width
    )
    extended = (
        jnp.pad(grad_set[:, :, :, 1], ((0, 0), (1, 1), (0, 0), (0, 0), (0, 0)))
        + jnp.pad(grad_set[:, :, :, 0], ((0, 0), (0, 2), (0, 0), (0, 0), (0, 0)))
        + jnp.pad(grad_set[:, :, :, 2], ((0, 0), (2, 0), (0, 0), (0, 0), (0, 0)))
    )
    edge_grads = jnp.concatenate([extended[:, :1], extended[:, own_blocks + 1 :]], axis=1)
    edge_back = padded(edge_grads.astype(jnp.bfloat16), (("blk", 1),), 1).astype(edge_grads.dtype)
    pair_grad = extended[:, 1 : own_blocks + 1]
    pair_grad = pair_grad.at[:, 0].add(edge_back[:, 0]).at[:, own_blocks - 1].add(edge_back[:, 3])
    glob_grad = jnp.sum(grad_set[:, :, :, 3 : 3 + glob_count], axis=1).transpose(0, 2, 1, 3, 4)
    glob_total = lax.psum(glob_grad.astype(jnp.bfloat16), "blk").astype(jnp.float32)
    pair_grad = pair_grad + jnp.einsum(
        "wgb,wghsc->wbhsc", owned_glob.astype(f32), glob_total, precision=lax.Precision.HIGHEST
    )
    rand_grad = grad_set[:, :, :, 3 + glob_count :].reshape(
        windows, per_device, block_len, pair_width
    )
    back_out = jax.vmap(add_rows)(
        jnp.zeros((windows, blk_count * slot_cap, block_len, pair_width), f32),
        fetch_index,
        rand_grad,
    )
    back_in = lax.all_to_all(
        back_out.reshape(windows, blk_count, slot_cap, block_len, pair_width).astype(jnp.bfloat16),
        "blk",
        split_axis=1,
        concat_axis=1,
        tiled=True,
    ).astype(jnp.float32)
    owner_sum = jax.vmap(add_rows)(
        jnp.zeros((windows, own_blocks * heads + 1, block_len, pair_width), f32),
        send_table,
        back_in.reshape(windows, blk_count * slot_cap, block_len, pair_width),
    )
    pair_grad = pair_grad + owner_sum[:, : own_blocks * heads].reshape(
        windows, own_blocks, heads, block_len, pair_width
    )
    grad_keys = from_heads(pair_grad[..., :head_dim].astype(bf16))
    grad_values = from_heads(pair_grad[..., head_dim:].astype(bf16))
    grad_joined = jnp.concatenate(
        [from_heads(grad_query.astype(bf16)), grad_keys, grad_values], axis=1
    )
    grad_w_qkv = jnp.einsum("td,tc->dc", normed, grad_joined, preferred_element_type=f32)
    grad_b_q = jnp.sum(grad_joined[:, :model_width], axis=0, dtype=f32)
    grad_b_v = jnp.sum(grad_joined[:, 2 * model_width :], axis=0, dtype=f32)
    grad_normed = jnp.einsum("tc,dc->td", grad_joined, w_qkv, preferred_element_type=f32)
    grad_tok_norm, grad_gain_one, grad_shift_one = norm_one_pull(grad_normed)
    grad_tokens = (grad_resid + grad_tok_norm).astype(bf16).reshape(windows, length, model_width)
    local_grads = (
        grad_w_qkv,
        grad_b_q,
        grad_b_v,
        grad_w_out,
        grad_b_out,
        grad_gain_one,
        grad_shift_one,
        grad_gain_two,
        grad_shift_two,
        grad_w_up,
        grad_b_up,
        grad_w_down,
        grad_b_down,
    )
    packed_grads = jnp.concatenate(
        [grad_item.reshape(blk_count, -1) for grad_item in local_grads], axis=1
    )
    total_cols = packed_grads.shape[1]
    win_count = lax.axis_size("win")
    pad_cols = -total_cols % win_count
    shard_sum = lax.psum_scatter(
        packed_grads.astype(jnp.bfloat16), "blk", scatter_dimension=0, tiled=True
    ).astype(jnp.float32)
    split_shard = jnp.pad(shard_sum, ((0, 0), (0, pad_cols))).reshape(win_count, -1)
    group_piece = lax.psum_scatter(
        split_shard.astype(jnp.bfloat16), "win", scatter_dimension=0, tiled=True
    ).astype(jnp.float32)
    summed = (
        lax.all_gather(group_piece.astype(jnp.bfloat16), "win", axis=0, tiled=True)
        .astype(group_piece.dtype)
        .reshape(1, -1)[:, :total_cols]
    )
    shards = []
    offset = 0
    for grad_item in local_grads:
        entry_count = grad_item.size // blk_count
        shards.append(
            summed[0, offset : offset + entry_count].reshape(
                (grad_item.shape[0] // blk_count,) + grad_item.shape[1:]
            )
        )
        offset = offset + entry_count
    out_tokens = output.astype(bf16).reshape(windows, length, model_width)
    return (
        out_tokens,
        grad_tokens,
        shards[0],
        shards[1],
        shards[2],
        shards[3],
        shards[4],
        shards[5],
        shards[6],
        shards[7],
        shards[8],
        shards[9],
        shards[10],
        shards[11],
        shards[12],
    )


def layer_step(*arguments):
    windows = arguments[0].shape[0]
    paired = lax.axis_size("blk") == 2 * windows and lax.axis_size("win") == 4 and windows == 4
    return (paired_body if paired else general_body)(*arguments)


def paired_body(
    tokens,
    cotangent,
    w_qkv,
    b_q,
    b_v,
    w_out,
    b_out,
    gain_one,
    shift_one,
    gain_two,
    shift_two,
    w_up,
    b_up,
    w_down,
    b_down,
    rand_owner,
    rand_sub,
    global_ids,
    species,
):
    f32 = jnp.float32
    bf16 = jnp.bfloat16
    win_count = lax.axis_size("win")
    blk_count = lax.axis_size("blk")
    win_pos = lax.axis_index("win")
    blk_pos = lax.axis_index("blk")
    layers, length, width = tokens.shape
    core, layer, side = win_pos % 2, blk_pos // 2, blk_pos % 2
    blocks, heads, picks = rand_owner.shape[1:]
    own_blocks = blocks // blk_count
    half_blocks = blocks // 2
    block_len = length // own_blocks
    head_dim = width // heads
    all_rows = layers * length
    lanes = HEADS_PER_GROUP * head_dim
    groups = heads // HEADS_PER_GROUP
    score_scale = head_dim ** (-0.5)

    def takes(micros):
        return pl.CostEstimate(flops=micros * 1_000_000_000, bytes_accessed=micros * 1_000_000, transcendentals=0)


    rand_size = blocks * heads * picks
    named = jnp.concatenate(
        [
            lax.dynamic_index_in_dim((rand_owner * own_blocks + rand_sub).reshape(layers, rand_size), layer, 0, keepdims=False),
            lax.dynamic_index_in_dim(global_ids, layer, 0, keepdims=False),
        ]
    )
    slot = jnp.arange(half_blocks, dtype=jnp.int32)

    def table_for(which):
        block = (((layer - slot // own_blocks) % layers) * 2 + which) * own_blocks + slot % own_blocks
        reads = jnp.concatenate([named, jnp.maximum(block - 1, 0), jnp.minimum(block + 1, blocks - 1)])
        owner = reads // own_blocks
        half = jnp.where(owner % 2 == which, 0, half_blocks)
        places = half + ((layer - owner // 2) % layers) * own_blocks + reads % own_blocks
        return jnp.concatenate([places, block])

    table = jnp.where(side == core, table_for(core), swap(table_for(1 - core), 1, 0))
    sizes = (heads, picks, rand_size, half_blocks)

    tile = length

    def by_rows(columns):
        return pl.BlockSpec((tile, columns), lambda i: (i, 0))

    def by_tile(columns):
        return pl.BlockSpec((tile, columns), lambda i: (tile_order(i), 0))

    def whole(*shape, once=True):
        mode = pl.Buffered(1) if once else None
        return pl.BlockSpec(shape, lambda i: (0,) * len(shape), pipeline_mode=mode)

    scalars = pl.BlockSpec(memory_space=pltpu.SMEM)
    wide = w_up.shape[1]
    params = pltpu.CompilerParams(vmem_limit_bytes=60 << 20)
    row = lambda vector: vector.reshape(1, -1)
    def remote_params(number, mib):
        return pltpu.CompilerParams(vmem_limit_bytes=mib << 20, collective_id=number, has_side_effects=True)

    any_place = pl.BlockSpec(memory_space=pl.ANY)
    hbm = pl.BlockSpec(memory_space=pltpu.HBM)

    def keep(*shape):
        return pltpu.VMEM(shape, bf16)

    copies = pltpu.SemaphoreType.DMA((layers,))
    vectors_one = jnp.stack([gain_one, shift_one, b_q, b_v])
    vectors_two = jnp.stack([b_out, gain_two, shift_two, b_down])
    rows_in, query, key_value, key_value_other = pl.pallas_call(
        partial(front_kernel, score_scale),
        grid=(layers,),
        in_specs=[any_place, whole(4, width), whole(width, 3 * width)],
        out_specs=[hbm, pl.BlockSpec((tile, width), lambda i: (arrival_order(i), 0)), hbm, hbm],
        out_shape=[
            jax.ShapeDtypeStruct((all_rows, width), bf16),
            jax.ShapeDtypeStruct((all_rows, width), bf16),
            jax.ShapeDtypeStruct((all_rows, 2 * width), bf16),
            jax.ShapeDtypeStruct((all_rows, 2 * width), bf16),
        ],
        scratch_shapes=[keep(layers, length, width), keep(layers, length, 2 * width)] + [copies] * 6,
        compiler_params=remote_params(1, 48),
        cost_estimate=takes(80),
        name="front",
    )(tokens, vectors_one, w_qkv)

    def lane_group(first):
        return pl.BlockSpec((all_rows, lanes), lambda g: (0, first + g))

    store = pltpu.VMEM((blocks, block_len, lanes), bf16)
    halves = layers // 2
    attended, log_total, cot_even = pl.pallas_call(
        partial(attend_kernel, sizes, blocks, head_dim, (0, 2)),
        grid=(groups,),
        in_specs=[scalars] + [lane_group(0), lane_group(0), lane_group(0), lane_group(groups), lane_group(groups), any_place],
        out_specs=[lane_group(0), pl.BlockSpec((1, half_blocks, lanes), lambda g: (g, 0, 0)), hbm],
        out_shape=[
            jax.ShapeDtypeStruct((all_rows, width), bf16),
            jax.ShapeDtypeStruct((groups, half_blocks, lanes), f32),
            jax.ShapeDtypeStruct((halves, length, width), bf16),
        ],
        scratch_shapes=[store, store] + [pltpu.SemaphoreType.DMA((halves,))] * 2,
        compiler_params=remote_params(4, 56),
        cost_estimate=takes(38),
        name="attend",
    )(table, query, key_value, key_value_other, key_value, key_value_other, cotangent)

    payload = 2 * wide // blk_count + width // blk_count
    payload += -payload % (16 * win_count)
    stays = jax.ShapeDtypeStruct((blk_count, win_count // 2, payload // win_count, width), bf16)
    output, out_last, normal, second_t, attended_t, rstd, active, slope, cot_odd = pl.pallas_call(
        partial(ffn_forward_kernel, 256, (1, 3)),
        grid=(layers,),
        in_specs=[
            by_rows(width), by_rows(width), whole(width, width), whole(4, width), any_place, whole(1, wide), any_place, any_place,
        ],
        out_specs=[
            by_rows(width), whole(length, width, once=False), by_rows(width), pl.BlockSpec((width, length), lambda i: (0, i)), pl.BlockSpec((width, length), lambda i: (0, i)),
            by_rows(128), by_rows(wide), by_rows(wide), hbm,
        ],
        out_shape=[
            jax.ShapeDtypeStruct((all_rows, width), bf16),
            jax.ShapeDtypeStruct((length, width), bf16),
            jax.ShapeDtypeStruct((all_rows, width), bf16),
            jax.ShapeDtypeStruct((width, all_rows), bf16),
            jax.ShapeDtypeStruct((width, all_rows), bf16),
            jax.ShapeDtypeStruct((all_rows, 128), f32),
            jax.ShapeDtypeStruct((all_rows, wide), bf16),
            jax.ShapeDtypeStruct((all_rows, wide), bf16),
            jax.ShapeDtypeStruct((halves, length, width), bf16),
        ],
        scratch_shapes=[pltpu.SemaphoreType.DMA((halves,))] * 2 + [keep(width, wide), keep(wide, width), pltpu.SemaphoreType.DMA((2,))],
        compiler_params=remote_params(5, 60),
        cost_estimate=takes(35),
        name="ffn_forward",
    )(rows_in, attended, w_out, vectors_two, w_up, row(b_up), w_down, cotangent)

    chunks = wide // width

    grad_resid, grad_attended, vec_two, vec_up, early_keep, early_other, out_tokens = pl.pallas_call(
        partial(ffn_back_kernel, chunks, blk_count, (2, 1, 0)),
        grid=(chunks,),
        in_specs=[
            scalars, pl.BlockSpec((all_rows, width), lambda i: (0, i)), pl.BlockSpec((all_rows, width), lambda i: (0, i)),
            pl.BlockSpec((width, width), lambda i: (0, i)), pl.BlockSpec((width, width), lambda i: (i, 0)),
            whole(width, all_rows), whole(4, width), *[any_place] * 7,
        ],
        out_specs=[hbm, hbm, whole(4, width), whole(chunks, width), hbm, hbm, hbm],
        out_shape=[
            jax.ShapeDtypeStruct((all_rows, width), bf16),
            jax.ShapeDtypeStruct((all_rows, width), bf16),
            jax.ShapeDtypeStruct((4, width), f32),
            jax.ShapeDtypeStruct((chunks, width), f32),
            stays,
            stays,
            jax.ShapeDtypeStruct((layers, length, width), bf16),
        ],
        scratch_shapes=[
            keep(layers, length, width),
            keep(all_rows, width),
            keep(width, all_rows),
            keep(all_rows, width),
            pltpu.VMEM((all_rows, width), f32),
            keep(2, blk_count, payload - chunks * width // blk_count - width // 2, width),
            keep(2, 2, width // 2, width),
            pltpu.SemaphoreType.DMA((layers,)),
            pltpu.SemaphoreType.DMA((layers,)),
            pltpu.SemaphoreType.DMA((layers,)),
            pltpu.SemaphoreType.DMA((48,)),
            pltpu.SemaphoreType.DMA((48,)),
            pltpu.SemaphoreType.DMA((2,)),
            keep(all_rows, width),
            pltpu.VMEM((all_rows, 128), f32),
            keep(width, all_rows),
            keep(width, width),
            pltpu.SemaphoreType.DMA((4,)),
        ],
        compiler_params=remote_params(3, 63),
        cost_estimate=takes(60),
        name="ffn_back",
    )(
        species, active, slope, w_up, w_down, second_t, vectors_two, normal, rstd, attended_t, w_out, cot_even, cot_odd, output,
    )
    last_pairs = [(there, here) for here, there in regroup_pairs(win_count, layers, 3)]
    out_last = lax.ppermute(out_last, ("win", "blk"), last_pairs)
    pair = win_pos // 2
    early_rows = payload // win_count
    late_rows = 3 * width // blk_count + 32
    late_size = late_rows // win_count
    cell = (early_rows, width)
    early_keep = early_keep.reshape((2, 2, 2, 2) + cell)
    early_other = early_other.reshape((2, 2, 2, 2) + cell)
    place = jnp.stack([side, pair, side, layer])

    def picked(index):
        return pl.BlockSpec((1, 1, 1, 1) + cell, lambda z, n, p: index(z, n, p) + (0, 0))

    def listed(index):
        return pl.BlockSpec((1, 1) + cell, lambda z, n, p: index(z, n, p) + (0, 0))

    def cells_of(count):
        return [jax.ShapeDtypeStruct((2, 2) + cell, bf16)] * count

    def first_send():
        left = picked(lambda z, n, p: (0, z, 1 - p[0], n))
        right = picked(lambda z, n, p: (1, z, n, 1 - p[1]))
        return pl.pallas_call(
            first_send_kernel,
            grid_spec=pltpu.PrefetchScalarGridSpec(
                num_scalar_prefetch=1, grid=(2, 2), in_specs=[left, left, right, right], out_specs=[listed(lambda z, n, p: (z, n))] * 2
            ),
            out_shape=cells_of(2),
            cost_estimate=takes(3),
            name="first_send",
        )(place, early_keep, early_other, early_keep, early_other)

    def second_send(got_left, got_right):
        left = pl.BlockSpec((1, 1, 1, 2) + cell, lambda z, p: (0, z, p[0], 0, 0, 0))
        right = pl.BlockSpec((1, 1, 2, 1) + cell, lambda z, p: (1, z, 0, p[1], 0, 0))
        got = pl.BlockSpec((1, 2) + cell, lambda z, p: (z, 0, 0, 0))
        rows_spec = pl.BlockSpec((1,) + cell, lambda z, p: (z, 0, 0))
        both_spec = pl.BlockSpec((2, 1) + cell, lambda z, p: (0, z, 0, 0))
        return pl.pallas_call(
            second_send_kernel,
            grid_spec=pltpu.PrefetchScalarGridSpec(
                num_scalar_prefetch=1, grid=(2,), in_specs=[left, left, got, right, right, got], out_specs=[both_spec, rows_spec, rows_spec]
            ),
            out_shape=cells_of(1) + [jax.ShapeDtypeStruct((2,) + cell, bf16)] * 2,
            compiler_params=params,
            cost_estimate=takes(4),
            name="second_send",
        )(place, early_keep, early_other, got_left, early_keep, early_other, got_right)

    def third_send(keep, left, right):
        specs = []
        for step in range(layers):
            goal = lambda p, step=step: (p[3] + step) % layers
            specs.append(listed(lambda z, n, p, goal=goal: (goal(p) // 2, goal(p) % 2)))
            specs += [pl.BlockSpec((1,) + cell, lambda z, n, p, goal=goal: (goal(p) % 2, 0, 0))] * 2
        out = pl.BlockSpec(cell, lambda z, n, p: (0, 0))
        return pl.pallas_call(
            third_send_kernel,
            grid_spec=pltpu.PrefetchScalarGridSpec(num_scalar_prefetch=1, grid=(1, 1), in_specs=specs, out_specs=[out] * layers),
            out_shape=[jax.ShapeDtypeStruct(cell, bf16)] * layers,
            cost_estimate=takes(3),
            name="third_send",
        )(place, *[keep, left, right] * layers)

    def to_layer(value, step):
        pairs = [
            (win * blk_count + blk, win * blk_count + (blk + 2 * step) % blk_count)
            for win in range(win_count)
            for blk in range(blk_count)
        ]
        return lax.ppermute(value, ("win", "blk"), pairs)

    first_left, first_right = first_send()
    first_left, first_right = swap(first_left, 0, 1), swap(first_right, 2, 0)

    grad_parts, grad_others = [], []
    for group in range(groups):
        after = []
        if group == 1:
            early_kept, send_left, send_right = second_send(first_left, first_right)
            after = [early_kept, out_last]
            second = swap(send_left, 2, 0), swap(send_right, 0, 1)
        if group == 2:
            early_parts = third_send(early_kept, *second)
            after = [early_parts[0]]
            early_parts = [early_parts[0]] + [to_layer(early_parts[n], n) for n in range(1, layers)]

        def column(first):
            return pl.BlockSpec((all_rows, lanes), lambda g, t: (0, first))

        def full(columns):
            return pl.BlockSpec((all_rows, columns), lambda g, t: (0, 0))

        grad_store = pltpu.VMEM((blocks, block_len, lanes), f32)
        glob_store = pltpu.VMEM((2, block_len, lanes), f32)
        dq, own, other = pl.pallas_call(
            partial(attend_back_kernel, sizes, blocks, head_dim, score_scale, group),
            grid_spec=pltpu.PrefetchScalarGridSpec(
                num_scalar_prefetch=1,
                grid=(1,),
                in_specs=[
                    column(group), column(group), column(group), column(groups + group), column(groups + group), column(group),
                    pl.BlockSpec((1, half_blocks, lanes), lambda g, t: (group, 0, 0)),
                    *[any_place] * len(after),
                ],
                out_specs=[full(lanes), full(2 * lanes), full(2 * lanes)],
                scratch_shapes=[store, store, grad_store, grad_store, glob_store, glob_store],
            ),
            out_shape=[jax.ShapeDtypeStruct((all_rows, n * lanes), bf16) for n in (1, 2, 2)],
            compiler_params=params,
            cost_estimate=takes(25),
            name="attend_back",
        )(table, query, key_value, key_value_other, key_value, key_value_other, grad_attended, log_total, *after)
        grad_parts += [dq, own]
        grad_others.append(other)

    def vmem(*shape):
        return pltpu.VMEM(shape, bf16)

    first_shape, mid_shape = (2, 2, 2), (2, 2)
    chain = lambda size: [vmem(*lead, size, width) for lead in (first_shape, mid_shape, mid_shape, (3,), ())]
    grad_tokens, late, early = pl.pallas_call(
        partial(finish_kernel, groups),
        grid=(layers,),
        in_specs=[by_tile(p.shape[1]) for p in grad_parts]
        + [any_place] * groups
        + [by_tile(width), by_tile(width), whole(4, width), whole(width, 3 * width), whole(4, width), whole(chunks, width)]
        + [any_place] * layers,
        out_specs=[hbm] * 3,
        out_shape=[
            jax.ShapeDtypeStruct((layers, length, width), bf16),
            jax.ShapeDtypeStruct((win_count, late_size, width), bf16),
            jax.ShapeDtypeStruct((win_count, early_rows, width), bf16),
        ],
        scratch_shapes=[
            vmem(all_rows, 3 * width),
            vmem(layers, width, length),
            pltpu.VMEM((4, width), f32),
            vmem(layers, length, width),
            vmem(2, 2, 2, 2, 2, late_size, width),
            vmem(2, 2, 2, 2, late_size, width),
            chain(late_size),
            [vmem(*lead, early_rows, width) for lead in ((4,), ())],
            pltpu.SemaphoreType.DMA((layers,)),
            pltpu.SemaphoreType.DMA((layers,)),
            pltpu.SemaphoreType.DMA((4,)),
            pltpu.SemaphoreType.DMA((14,)),
            pltpu.SemaphoreType.DMA((14,)),
            pltpu.SemaphoreType.DMA((2,)),
            vmem(groups, layers, length, 2 * lanes),
            pltpu.SemaphoreType.DMA((groups, layers)),
            pltpu.SemaphoreType.DMA((groups, layers)),
        ],
        compiler_params=remote_params(2, 62),
        cost_estimate=takes(90),
        name="finish",
    )(
        *grad_parts, *grad_others, rows_in, grad_resid, vectors_one, w_qkv, vec_two, vec_up,
        *early_parts,
    )
    part = width // blk_count
    count = wide // width
    in_vmem = pl.BlockSpec(memory_space=pltpu.VMEM)
    done_qkv, done_out, done_up, done_down, vec, vec_wide, out_tokens, grad_tokens = pl.pallas_call(
        unpack_kernel,
        in_specs=[in_vmem, in_vmem, any_place, any_place],
        out_specs=[in_vmem] * 6 + [hbm] * 2,
        out_shape=[
            jax.ShapeDtypeStruct(shape, f32)
            for shape in ((part, 3 * width), (part, width), (part, wide), (wide // blk_count, width), (8, part), (1, wide // blk_count))
        ]
        + [jax.ShapeDtypeStruct((layers, length, width), bf16)] * 2,
        scratch_shapes=[keep(2, layers, length, width), pltpu.SemaphoreType.DMA((2, layers)), pltpu.SemaphoreType.DMA((2, layers))],
        compiler_params=params,
        cost_estimate=takes(4),
        name="unpack",
    )(early, late, lax.dynamic_update_index_in_dim(out_tokens, out_last, (layer + 3) % layers, 0), grad_tokens)
    return (
        out_tokens,
        grad_tokens,
        done_qkv,
        vec[0],
        vec[1],
        done_out,
        vec[4],
        vec[2],
        vec[3],
        vec[5],
        vec[6],
        done_up,
        vec_wide[0],
        done_down,
        vec[7],
    )


def solution(mesh):
    placed = (
        P("win", "blk", None),
        P("win", "blk", None),
        P(),
        P(),
        P(),
        P(),
        P(),
        P(),
        P(),
        P(),
        P(),
        P(),
        P(),
        P(),
        P(),
        P("win", None, None, None),
        P("win", None, None, None),
        P("win", None),
        P(),
    )
    return jax.shard_map(
        layer_step,
        mesh=mesh,
        in_specs=placed,
        out_specs=(
            P("win", "blk", None),
            P("win", "blk", None),
            P("blk", None),
            P("blk"),
            P("blk"),
            P("blk", None),
            P("blk"),
            P("blk"),
            P("blk"),
            P("blk"),
            P("blk"),
            P("blk", None),
            P("blk"),
            P("blk", None),
            P("blk"),
        ),
        check_vma=False,
    )
```

```python
from functools import partial

import jax
import jax.numpy as jnp
from jax import lax
from jax.experimental import pallas as pl
from jax.experimental.pallas import tpu as pltpu
from jax.sharding import PartitionSpec as P

SPECIES = 4


epsilon = 1e-05
masked_score = -1000000000.0


def padded(cells, sides, width):
    for axis, dim in sides:
        count = lax.axis_size(axis)
        ends = count - 1
        head = lax.slice_in_dim(cells, 0, width, axis=dim)
        tail = lax.slice_in_dim(cells, cells.shape[dim] - width, cells.shape[dim], axis=dim)
        cells = jnp.concatenate(
            [
                lax.ppermute(tail, axis, [(i, (i + 1) % count) for i in range(ends)]),
                cells,
                lax.ppermute(head, axis, [((i + 1) % count, i) for i in range(ends)]),
            ],
            axis=dim,
        )
    return cells


def layer_norm(values, norm_gain, norm_shift):
    average = jnp.mean(values, axis=-1, keepdims=True)
    centred = values - average
    variance = jnp.mean(centred * centred, axis=-1, keepdims=True)
    return centred * lax.rsqrt(variance + epsilon) * norm_gain + norm_shift


def take_rows(source, index_rows):
    return jnp.take(source, index_rows, axis=0)


def add_rows(base, index_rows, update):
    return base.at[index_rows].add(update)


def set_rows(base, index_rows, update):
    return base.at[index_rows].set(update)


HEADS_PER_GROUP = 4


def regroup_pairs(win_count, layers, step):
    pairs = []
    for win in range(win_count):
        for blk in range(2 * layers):
            layer, side = blk // 2, blk % 2
            target = ((layer + step) % layers) * 2 + win % 2
            pairs.append((win * 2 * layers + blk, ((win // 2) * 2 + side) * 2 * layers + target))
    return pairs


def flip_pairs(win_count, blk_count, win_bit, blk_bit):
    return [
        (win * blk_count + blk, (win ^ win_bit) * blk_count + (blk ^ blk_bit))
        for win in range(win_count)
        for blk in range(blk_count)
    ]


def swap(value, win_bit, blk_bit):
    pairs = flip_pairs(lax.axis_size("win"), lax.axis_size("blk"), win_bit, blk_bit)
    return lax.ppermute(value, ("win", "blk"), pairs)


def head_masks(lanes, head_dim, dtype):
    lane = lax.broadcasted_iota(jnp.int32, (1, lanes), 1)
    return [(lane // head_dim == h).astype(dtype) for h in range(lanes // head_dim)]


def block_places(table, slot, group, sizes):
    heads, picks, rand_size, half_blocks = sizes
    block = table[rand_size + 2 + 2 * half_blocks + slot]
    near = [table[rand_size + 2 + slot], slot, table[rand_size + 2 + half_blocks + slot]]
    row = (block * heads + group * HEADS_PER_GROUP) * picks
    rand = [[table[row + h * picks + r] for h in range(HEADS_PER_GROUP)] for r in range(picks)]
    return block, near, rand


def spread_heads(rows, masks):
    return jnp.concatenate([rows * m for m in masks], axis=0)


def pick_heads(square, masks, height):
    total = square[0:height] * masks[0]
    for h in range(1, len(masks)):
        total = total + square[h * height : (h + 1) * height] * masks[h]
    return total


def key_rows(source, near, glob, rand, low_half):
    parts = [source[p] for p in near] + [source[p] for p in glob]
    for places in rand:
        columns = []
        for c in range(len(places) // 2):
            low = source[places[2 * c], :, c * 128 : (c + 1) * 128]
            high = source[places[2 * c + 1], :, c * 128 : (c + 1) * 128]
            columns.append(jnp.where(low_half, low, high))
        parts.append(jnp.concatenate(columns, axis=1))
    return jnp.concatenate(parts, axis=0)


def mask_scores(scores, block, blocks, block_len):
    first = jnp.where(block > 0, scores[:block_len], masked_score)
    last = jnp.where(block < blocks - 1, scores[2 * block_len : 3 * block_len], masked_score)
    return jnp.concatenate([first, scores[block_len : 2 * block_len], last, scores[3 * block_len :]], axis=0)


def across(left, right):
    return lax.dot_general(left, right, (((1,), (1,)), ((), ())), preferred_element_type=jnp.float32)


def down(left, right):
    return lax.dot_general(left, right, (((0,), (0,)), ((), ())), preferred_element_type=jnp.float32)


def load_halves(target, own, other, half_blocks, block_len):
    lanes = own.shape[-1]
    target[0:half_blocks] = own[...].reshape(half_blocks, block_len, lanes)
    target[half_blocks:] = other[...].reshape(half_blocks, block_len, lanes)


def attend_kernel(
    sizes, blocks, head_dim, cot_tiles,
    table, q_ref, k_own, k_other, v_own, v_other, cotangent,
    o_ref, lse_ref, cot_ref,
    k_all, v_all, send_sems, recv_sems,
):
    heads, picks, rand_size, half_blocks = sizes
    block_len = k_all.shape[1]
    lanes = q_ref.shape[1]
    group = pl.program_id(0)
    _, _, core, layer, _ = position()
    own_blocks = blocks // 8

    @pl.when(group == 0)
    def _():
        greet_owners(4, [])
        for n, tile in reversed(list(enumerate(cot_tiles))):
            regroup_move(cotangent, cot_ref.at[n], tile, send_sems.at[n], recv_sems.at[n], True)

    load_halves(k_all, k_own, k_other, half_blocks, block_len)
    load_halves(v_all, v_own, v_other, half_blocks, block_len)
    low_half = lax.broadcasted_iota(jnp.int32, (block_len, 128), 1) < head_dim
    masks = head_masks(lanes, head_dim, jnp.bfloat16)
    masks_f = head_masks(lanes, head_dim, jnp.float32)
    glob = [table[rand_size], table[rand_size + 1]]

    def several(number, carry):
        slots = [number * together + u for u in range(together)]
        places = [block_places(table, slot, group, sizes) for slot in slots]
        numbers = [(((layer + 4 - slot // own_blocks) % 4) * 2 + core) * own_blocks + slot % own_blocks for slot in slots]
        rows = [pl.ds(pl.multiple_of(slot * block_len, block_len), block_len) for slot in slots]
        queries = [spread_heads(q_ref[r, :], masks) for r in rows]
        keys = [key_rows(k_all, near, glob, rand, low_half) for _, near, rand in places]
        scores = [
            mask_scores(across(key, query), block, blocks, block_len) for key, query, block in zip(keys, queries, numbers)
        ]
        tops = [jnp.max(score, axis=0, keepdims=True) for score in scores]
        weights = [jnp.exp(score - top) for score, top in zip(scores, tops)]
        totals = [jnp.sum(weight, axis=0, keepdims=True) for weight in weights]
        probs = [(weight * (1.0 / total)).astype(jnp.bfloat16) for weight, total in zip(weights, totals)]
        values = [key_rows(v_all, near, glob, rand, low_half) for _, near, rand in places]
        for slot, r, prob, value, top, total in zip(slots, rows, probs, values, tops, totals):
            o_ref[r, :] = pick_heads(down(prob, value), masks_f, block_len).astype(jnp.bfloat16)
            lse_ref[0, pl.ds(slot, 1), :] = top + jnp.log(total)
        return carry

    together = 4
    lax.fori_loop(0, half_blocks // together, several, 0, unroll=4)

    @pl.when(group == pl.num_programs(0) - 1)
    def _():
        for n, tile in enumerate(cot_tiles):
            regroup_move(cotangent, cot_ref.at[n], tile, send_sems.at[n], recv_sems.at[n], False)


def attend_back_kernel(
    sizes, blocks, head_dim, scale, group,
    table, q_ref, k_own, k_other, v_own, v_other, go_ref, lse_ref, *refs,
):
    dq_ref, own_ref, other_ref, k_all, v_all, dk_all, dv_all, dk_glob, dv_glob = refs[-9:]
    heads, picks, rand_size, half_blocks = sizes
    block_len = k_all.shape[1]
    lanes = q_ref.shape[1]
    f32 = jnp.float32
    load_halves(k_all, k_own, k_other, half_blocks, block_len)
    load_halves(v_all, v_own, v_other, half_blocks, block_len)
    dk_all[...] = jnp.zeros_like(dk_all)
    dv_all[...] = jnp.zeros_like(dv_all)
    dk_glob[...] = jnp.zeros_like(dk_glob)
    dv_glob[...] = jnp.zeros_like(dv_glob)
    low_half = lax.broadcasted_iota(jnp.int32, (block_len, 128), 1) < head_dim
    masks = head_masks(lanes, head_dim, jnp.bfloat16)
    masks_f = head_masks(lanes, head_dim, f32)
    glob = [table[rand_size], table[rand_size + 1]]

    def add_back(grads, near, rand, into, into_glob):
        for n in range(3):
            into[near[n]] += grads[n * block_len : (n + 1) * block_len]
        for n in range(2):
            into_glob[n] += grads[(3 + n) * block_len : (4 + n) * block_len]
        for r in range(picks):
            part = grads[(5 + r) * block_len : (6 + r) * block_len]
            for c in range(lanes // 128):
                cell = part[:, c * 128 : (c + 1) * 128]
                columns = pl.ds(c * 128, 128)
                into[rand[r][2 * c], :, columns] += jnp.where(low_half, cell, 0.0)
                into[rand[r][2 * c + 1], :, columns] += jnp.where(low_half, 0.0, cell)

    def several(number, carry):
        slots = [number * 2 + u for u in range(2)]
        places = [block_places(table, slot, group, sizes) for slot in slots]
        rows = [pl.ds(pl.multiple_of(slot * block_len, block_len), block_len) for slot in slots]
        queries = [spread_heads(q_ref[r, :], masks) for r in rows]
        keys = [key_rows(k_all, near, glob, rand, low_half) for _, near, rand in places]
        scores = [across(key, query) for key, query in zip(keys, queries)]
        grads_out = [spread_heads(go_ref[r, :], masks) for r in rows]
        values = [key_rows(v_all, near, glob, rand, low_half) for _, near, rand in places]
        grad_probs = [across(value, grad) for value, grad in zip(values, grads_out)]
        probs = [
            jnp.exp(mask_scores(score, block, blocks, block_len) - lse_ref[0, pl.ds(slot, 1), :])
            for score, (block, _, _), slot in zip(scores, places, slots)
        ]
        row_dots = [jnp.sum(prob * grad, axis=0, keepdims=True) for prob, grad in zip(probs, grad_probs)]
        grad_scores = [
            (prob * (grad - dot)).astype(jnp.bfloat16) for prob, grad, dot in zip(probs, grad_probs, row_dots)
        ]
        grad_values = [
            jnp.dot(prob.astype(jnp.bfloat16), grad, preferred_element_type=f32) for prob, grad in zip(probs, grads_out)
        ]
        grad_keys = [jnp.dot(grad, query, preferred_element_type=f32) for grad, query in zip(grad_scores, queries)]
        for r, grad, key in zip(rows, grad_scores, keys):
            dq_ref[r, :] = (pick_heads(down(grad, key), masks_f, block_len) * scale).astype(jnp.bfloat16)
        for grad, key_grad, (_, near, rand) in zip(grad_values, grad_keys, places):
            add_back(grad, near, rand, dv_all, dv_glob)
            add_back(key_grad, near, rand, dk_all, dk_glob)
        return carry

    lax.fori_loop(0, half_blocks // 2, several, 0, unroll=4)
    for n in range(2):
        dk_all[glob[n]] += dk_glob[n]
        dv_all[glob[n]] += dv_glob[n]
    for target, start in ((own_ref, 0), (other_ref, half_blocks)):
        for n, source in enumerate((dk_all, dv_all)):
            cells = source[start : start + half_blocks].astype(jnp.bfloat16)
            target[:, n * lanes : (n + 1) * lanes] = cells.reshape(half_blocks * block_len, lanes)


def norm_parts(values):
    average = jnp.mean(values, axis=-1, keepdims=True)
    centred = values - average
    rstd = lax.rsqrt(jnp.mean(centred * centred, axis=-1, keepdims=True) + epsilon)
    return centred * rstd, rstd


def norm_back(grad, normal, rstd, gain):
    scaled = grad * gain
    first = jnp.mean(scaled, axis=-1, keepdims=True)
    second = jnp.mean(scaled * normal, axis=-1, keepdims=True)
    return rstd * (scaled - first - normal * second)


def normal_parts(values):
    cdf = 0.5 + 0.5 * lax.erf(values * 0.5**0.5)
    return cdf, values * jnp.exp(-0.5 * values * values) * 0.3989422804014327


def column_sum(values):
    return jnp.sum(values, axis=0, keepdims=True)


MESH = pl.DeviceIdType.MESH


def tile_order(number):
    return jnp.where(number == 0, 2, jnp.where(number == 2, 3, jnp.where(number == 3, 0, number)))


def position():
    win, blk = lax.axis_index("win"), lax.axis_index("blk")
    return win, blk, win % 2, blk // 2, blk % 2


def owner_of(tile, layers):
    win, blk, core, layer, side = position()
    return (win // 2) * 2 + side, ((layer + layers - tile) % layers) * 2 + core


def greet_owners(layers, peers):
    barrier = pltpu.get_barrier_semaphore()
    others = len(peers)
    for peer in peers:
        pl.semaphore_signal(barrier, inc=1, device_id=peer, device_id_type=MESH)
    _, _, core, _, side = position()
    for tile in range(1, layers):
        pl.semaphore_signal(barrier, inc=1, device_id=owner_of(tile, layers), device_id_type=MESH)

    @pl.when(side != core)
    def _():
        pl.semaphore_signal(barrier, inc=1, device_id=owner_of(0, layers), device_id_type=MESH)
        pl.semaphore_wait(barrier, layers + others)

    @pl.when(side == core)
    def _():
        pl.semaphore_wait(barrier, layers - 1 + others)


def return_tile(tile, source, target, send_sem, recv_sems, start):
    _, _, core, layer, side = position()
    layers = target.shape[0]
    stays = (tile == 0) & (side == core)

    @pl.when(stays)
    def _():
        move = pltpu.make_async_copy(source, target.at[layer], recv_sems.at[tile])
        move.start() if start else move.wait()

    @pl.when(jnp.logical_not(stays))
    def _():
        move = pltpu.make_async_remote_copy(
            src_ref=source, dst_ref=target.at[layer], send_sem=send_sem, recv_sem=recv_sems.at[tile],
            device_id=owner_of(tile, layers), device_id_type=MESH,
        )
        move.start() if start else move.wait()


def regroup_move(source, target, tile, send_sem, recv_sem, start):
    win, _, core, layer, side = position()
    layers = source.shape[0]
    goal = (layer + tile) % layers
    stays = (tile == 0) & (side == core)

    def local():
        return pltpu.make_async_copy(source.at[goal], target, recv_sem)

    def far():
        return pltpu.make_async_remote_copy(
            src_ref=source.at[goal], dst_ref=target, send_sem=send_sem, recv_sem=recv_sem,
            device_id=((win // 2) * 2 + side, goal * 2 + core), device_id_type=MESH,
        )

    @pl.when(stays)
    def _():
        local().start() if start else local().wait()

    @pl.when(jnp.logical_not(stays))
    def _():
        far().start() if start else far().wait()


def arrival_order(number):
    return jnp.where(number == 2, 3, jnp.where(number == 3, 2, number))


def front_kernel(
    scale, tokens, vectors, weight,
    rows_ref, q_ref, kv_ref, other_ref,
    held, kv_rows, send_sems, recv_sems, kv_sems, kv_send, kv_recv, row_sems,
):
    f32, bf16 = jnp.float32, jnp.bfloat16
    step, steps = pl.program_id(0), pl.num_programs(0)
    length, width = held.shape[1:]
    win, blk, core, layer, side = position()
    layers = held.shape[0]
    peer = (win + 1 - 2 * core, blk)

    def token_move(tile, start):
        regroup_move(tokens, held.at[tile], tile, send_sems.at[tile], recv_sems.at[tile], start)

    def rows_of(tile):
        return pl.ds(pl.multiple_of(tile * length, length), length)

    def kv_moves(number):
        tile = arrival_order(number)
        return [
            pltpu.make_async_copy(kv_rows.at[number], kv_ref.at[rows_of(tile)], kv_sems.at[number]),
            pltpu.make_async_copy(held.at[tile], rows_ref.at[rows_of(tile)], row_sems.at[number]),
            pltpu.make_async_remote_copy(
                src_ref=kv_rows.at[number], dst_ref=other_ref.at[rows_of(tile)], send_sem=kv_send.at[number], recv_sem=kv_recv.at[number],
                device_id=peer, device_id_type=MESH,
            ),
        ]

    @pl.when(step == 0)
    def _():
        greet_owners(layers, [peer])
        for n in range(4):
            token_move(arrival_order(n), True)

    tile = arrival_order(step)
    token_move(tile, False)
    normal, _ = norm_parts(held[tile].astype(f32))
    normed = (normal * vectors[0:1] + vectors[1:2]).astype(bf16)

    def part(n):
        return jnp.dot(normed, weight[:, n * width : (n + 1) * width], preferred_element_type=f32)

    kv_rows[step, :, :width] = part(1).astype(bf16)
    kv_rows[step, :, width:] = (part(2) + vectors[3:4]).astype(bf16)
    for move in kv_moves(step):
        move.start()
    q_ref[...] = (part(0) + vectors[2:3]).astype(bf16) * jnp.asarray(scale, bf16)

    @pl.when(step == steps - 1)
    def _():
        for n in range(4):
            for move in kv_moves(n):
                move.wait()


def ffn_forward_kernel(
    chunk, cot_tiles,
    rows_ref, att_ref, w_out, vectors, w_up, b_up, w_down, cotangent,
    out_ref, last_ref, normal_ref, second_ref, att_turned_ref, rstd_ref, active_ref, slope_ref, cot_ref,
    send_sems, recv_sems, up_rows, down_rows, load_sems,
):
    f32, bf16 = jnp.float32, jnp.bfloat16
    step, steps = pl.program_id(0), pl.num_programs(0)

    fetch_up = pltpu.make_async_copy(w_up, up_rows, load_sems.at[0])
    fetch_down = pltpu.make_async_copy(w_down, down_rows, load_sems.at[1])

    @pl.when(step == 0)
    def _():
        fetch_up.start()
        fetch_down.start()
        greet_owners(4, [])
        for n, tile in reversed(list(enumerate(cot_tiles))):
            regroup_move(cotangent, cot_ref.at[n], tile, send_sems.at[n], recv_sems.at[n], True)

    wide = up_rows.shape[1]
    b_out, gain, shift, b_down = (vectors.at[n : n + 1] for n in range(4))
    att = att_ref[...]
    residual = rows_ref[...].astype(f32) + (jnp.dot(att, w_out[...], preferred_element_type=f32) + b_out[...])
    normal, rstd = norm_parts(residual)
    second = (normal * gain[...] + shift[...]).astype(bf16)
    normal_ref[...] = normal.astype(bf16)
    second_ref[...] = second.T
    att_turned_ref[...] = att.T
    rstd_ref[...] = jnp.broadcast_to(rstd, rstd_ref.shape)

    @pl.when(step == 0)
    def _():
        fetch_up.wait()
        fetch_down.wait()

    def raise_part(first):
        part = slice(first, first + chunk)
        return jnp.dot(second, up_rows[:, part], preferred_element_type=f32) + b_up[:, part]

    ahead = raise_part(0)
    for first in range(0, wide, chunk):
        inner = ahead
        if first + chunk < wide:
            ahead = raise_part(first + chunk)
        cdf, slope = normal_parts(inner)
        active_ref[:, first : first + chunk] = (inner * cdf).astype(bf16)
        slope_ref[:, first : first + chunk] = (cdf + slope).astype(bf16)
    total = residual + b_down[...] + jnp.dot(active_ref[...], down_rows[...], preferred_element_type=f32)
    out_ref[...] = total.astype(bf16)

    @pl.when(step == steps - 1)
    def _():
        last_ref[...] = total.astype(bf16)
        for n, tile in enumerate(cot_tiles):
            regroup_move(cotangent, cot_ref.at[n], tile, send_sems.at[n], recv_sems.at[n], False)


def ffn_back_kernel(
    chunks, shards, kept_tiles,
    species, active_ref, slope_ref, w_up, w_down, second_t, vectors, normal_in, rstd_in, att_in, w_out_in,
    cot_even, cot_odd, output,
    resid_ref, go_ref, vec_ref, vec_up_ref, keep_ref, other_ref, out_ref,
    cot_rows, branch, branch_t, grad_inner, grad_second, stage_up, stage_down,
    cot_sems, ship_send, ship_recv, cell_send, cell_recv, done_sems, normal_ref, rstd_ref, att_t, w_out, load_sems,
):
    f32, bf16 = jnp.float32, jnp.bfloat16
    step = pl.program_id(0)
    slot = step % 2
    width = w_up.shape[0]
    tiles, length = cot_rows.shape[:2]
    part = width // shards
    half = width // 2
    size = keep_ref.shape[2]
    win, blk, core, _, _ = position()
    peer = (win + 1 - 2 * core, blk)

    def rows_of(n):
        return slice(n * length, (n + 1) * length)

    def ship(what):
        for n, tile in enumerate(kept_tiles):
            return_tile(tile, output.at[rows_of(tile)], out_ref, ship_send.at[n], ship_recv, what)

    def moves(c):
        cuts = []
        if c < chunks:
            base = 4 * c
            for first, count, piece, row in span_cuts(c * part, part, size):
                cuts.append((base + len(cuts), stage_up.at[c % 2, :, pl.ds(first, count)], slice(0, shards), piece, row, count))
            mine = slice(2 * c, 2 * c + 2)
            for first, count, piece, row in span_cuts(chunks * part, half, size):
                cuts.append((24 + base + len(cuts), stage_down.at[c % 2, :, pl.ds(first, count)], mine, piece, row, count))
        else:
            start = chunks * part + half
            for first, count, piece, row in span_cuts(start, 4 * size - start, size):
                cuts.append((20 + len(cuts), stage_up.at[0, :, pl.ds(first, count)], slice(0, shards), piece, row, count))
        return cuts

    def act(c, what):
        for number, source, mine, piece, row, count in moves(c):
            cell = (pl.ds(mine.start, mine.stop - mine.start), piece // 2, pl.ds(row, count))
            def far():
                return pltpu.make_async_remote_copy(
                    src_ref=source, dst_ref=other_ref.at[cell], send_sem=cell_send.at[number], recv_sem=cell_recv.at[number],
                    device_id=peer, device_id_type=MESH,
                )

            @pl.when(core == piece % 2)
            def _():
                if what == "receive":
                    far().wait_recv()
                else:
                    near = pltpu.make_async_copy(source, keep_ref.at[cell], cell_send.at[number])
                    near.start() if what == "start" else near.wait()

            if what != "receive":
                @pl.when(core != piece % 2)
                def _():
                    far().start() if what == "start" else far().wait_send()

    def late_loads():
        pairs = ((normal_in, normal_ref), (rstd_in, rstd_ref), (att_in, att_t), (w_out_in, w_out))
        return [pltpu.make_async_copy(a, b, load_sems.at[n]) for n, (a, b) in enumerate(pairs)]

    windows = species.shape[0]
    mine = species[((win // 2) * 2 + blk % 2) * tiles + blk // 2]
    alike = jnp.zeros((), f32)
    for n in range(windows):
        alike = alike + jnp.where(species[n] == mine, 1.0, 0.0)
    scale = jnp.sqrt(windows / (SPECIES * jnp.full((1, width), alike, f32)))

    def cot_moves():
        return [
            pltpu.make_async_copy((cot_even, cot_odd)[n % 2].at[n // 2], cot_rows.at[n], cot_sems.at[n]) for n in range(4)
        ]

    @pl.when(step == 0)
    def _():
        for move in cot_moves() + late_loads():
            move.start()
        greet_owners(tiles, [peer])
        ship(True)
        vec_ref[...] = jnp.zeros_like(vec_ref)
        for n, move in enumerate(cot_moves()):
            move.wait()
            upstream = cot_rows[n].astype(f32) * scale
            vec_ref[3:4] += column_sum(upstream)
            branch[rows_of(n), :] = upstream.astype(bf16)
            branch_t[:, rows_of(n)] = upstream.astype(bf16).T
        grad_second[...] = jnp.zeros_like(grad_second)

    for c in range(2, chunks):
        @pl.when(step == c)
        def _():
            act(c - 2, "wait")

    full = jnp.dot(branch_t[...], active_ref[...], preferred_element_type=f32)
    for n in range(2):
        for k in range(2):
            stage_down[slot, n, :, k * half : (k + 1) * half] = full[k * half : (k + 1) * half, n * half : (n + 1) * half].astype(bf16)
    total = jnp.zeros((1, w_up.shape[1]), f32)
    for n in range(tiles):
        grad = across(branch[rows_of(n), :], w_down[...]) * slope_ref[rows_of(n), :].astype(f32)
        total = total + column_sum(grad)
        grad_inner[rows_of(n), :] = grad.astype(bf16)
        grad_second[rows_of(n), :] += across(grad_inner[rows_of(n), :], w_up[...])
    vec_up_ref[pl.ds(step, 1), :] = total
    full = jnp.dot(second_t[...], grad_inner[...], preferred_element_type=f32)
    for b in range(shards):
        stage_up[slot, b, 0:part] = full[b * part : (b + 1) * part].astype(bf16)
    for c in range(chunks):
        @pl.when(step == c)
        def _():
            act(c, "start")

    @pl.when(step == chunks - 1)
    def _():
        for move in late_loads():
            move.wait()
        for n in range(tiles):
            upstream = cot_rows[n].astype(f32) * scale
            grad = grad_second[rows_of(n), :]
            normal = normal_ref[rows_of(n), :].astype(f32)
            grad_resid = upstream + norm_back(grad, normal, rstd_ref[rows_of(n), 0:1], vectors[1:2])
            grad_proj = grad_resid.astype(bf16)
            grad_inner[rows_of(n), :] = grad_proj
            branch[rows_of(n), :] = across(grad_proj, w_out[...]).astype(bf16)
            vec_ref[0:1] += column_sum(grad_resid)
            vec_ref[1:2] += column_sum(grad * normal)
            vec_ref[2:3] += column_sum(grad)
        results = [
            pltpu.make_async_copy(grad_inner, resid_ref, done_sems.at[0]),
            pltpu.make_async_copy(branch, go_ref, done_sems.at[1]),
        ]
        for move in results:
            move.start()
        full = jnp.dot(att_t[...], grad_inner[...], preferred_element_type=f32)
        act(chunks - 2, "wait")
        for b in range(shards):
            stage_up[0, b, 0:part] = full[b * part : (b + 1) * part].astype(bf16)
            stage_up[0, b, part:] = jnp.zeros((stage_up.shape[2] - part, width), bf16)
        act(chunks, "start")
        act(chunks - 1, "wait")
        act(chunks, "wait")
        for c in range(chunks + 1):
            act(c, "receive")
        for move in results:
            move.wait()
        ship(False)


def span_cuts(start, count, size):
    cuts, at = [], start
    while at < start + count:
        end = min(start + count, (at // size + 1) * size)
        cuts.append((at - start, end - at, at // size, at % size))
        at = end
    return cuts


def row_cuts(count, part, size):
    cuts = []
    for k in range(count):
        start = k * part
        while start < (k + 1) * part:
            end = min((k + 1) * part, (start // size + 1) * size)
            cuts.append((k, start - k * part, end - start, start // size, start % size))
            start = end
    return cuts


def add_into(target, got):
    target[...] = (target[...].astype(jnp.float32) + got[...].astype(jnp.float32)).astype(jnp.bfloat16)


def finish_kernel(groups, *refs):
    f32, bf16 = jnp.float32, jnp.bfloat16
    parts, others = refs[: 2 * groups], refs[2 * groups : 3 * groups]
    (
        rows_ref, resid_ref, vectors, weight, vec_two, vec_up, early_a, early_b, early_c, early_d,
        tok_ref, late_ref, early_ref,
        joined, turned, vec, out_rows, cells, core_got, late_bufs, early_bufs, send_sems, recv_sems, load_sems, chain_send, chain_recv, keep_sems, last_rows, last_send, last_recv,
    ) = refs[3 * groups :]
    step, steps = pl.program_id(0), pl.num_programs(0)
    length, width = rows_ref.shape
    lanes = width // groups
    part = width // 8
    win, blk, core, layer, side = position()
    pair = win // 2
    core_peer = (win + 1 - 2 * core, blk)
    pair_peer = (win + 2 - 4 * pair, blk)
    side_peer = (win, blk + 1 - 2 * side)
    layer_peers = [(win, ((layer + n) % 4) * 2 + side) for n in (1, 2, 3)]

    def remote(source, target, number, peer):
        return pltpu.make_async_remote_copy(
            src_ref=source, dst_ref=target, send_sem=chain_send.at[number], recv_sem=chain_recv.at[number],
            device_id=peer, device_id_type=MESH,
        )

    early_got, early_final = early_bufs

    def loads():
        return [
            pltpu.make_async_copy(source, early_got.at[n], load_sems.at[n])
            for n, source in enumerate((early_a, early_b, early_c, early_d))
        ]

    def second_step(state, got, base):
        return [
            remote(state.at[0, :, 1 - pair], got.at[0], base, pair_peer),
            remote(state.at[1, :, 1 - side], got.at[1], base + 1, side_peer),
        ]

    def add_second(state, got, mid):
        for z in range(2):
            mid[0, z] = (state[0, z, pair].astype(f32) + got[0, z].astype(f32)).astype(bf16)
            mid[1, z] = (state[1, z, side].astype(f32) + got[1, z].astype(f32)).astype(bf16)

    def layer_step(mid, got, base):
        moves = []
        for n in range(3):
            other = (layer + n + 1) % 4
            moves.append(remote(mid.at[other // 2, other % 2], got.at[n], base + n, layer_peers[n]))
        return moves

    def sum_into(final, parts):
        total = parts[0].astype(f32)
        for one in parts[1:]:
            total = total + one.astype(f32)
        final[...] = total.astype(bf16)

    def share(final, target, base):
        return [
            remote(final, target.at[win], base, core_peer),
            remote(final, target.at[win], base + 1, pair_peer),
        ]

    def pass_on(target, base):
        return [remote(target.at[win + 2 - 4 * pair], target.at[win + 2 - 4 * pair], base, core_peer)]

    def start(moves):
        for move in moves:
            move.start()

    def wait(moves):
        for move in moves:
            move.wait()

    def swap_moves(number):
        first = pl.multiple_of(tile_order(number) * length, length)
        return [
            pltpu.make_async_remote_copy(
                src_ref=others[g].at[pl.ds(first, length)], dst_ref=last_rows.at[g, number], send_sem=last_send.at[g, number],
                recv_sem=last_recv.at[g, number], device_id=core_peer, device_id_type=MESH,
            )
            for g in range(groups)
        ]

    late_first, late_second, late_mid, late_got, late_final = late_bufs
    early_base, late_base = 8, 0
    held = 1

    @pl.when(step == 0)
    def _():
        start(loads())
        greet_owners(steps, [core_peer, pair_peer, side_peer] + layer_peers)
        for n in range(4):
            start(swap_moves(n))
        vec[...] = jnp.zeros_like(vec)

    tile = tile_order(step)
    rows = pl.ds(pl.multiple_of(tile * length, length), length)
    wait(swap_moves(step))
    for g in range(groups):
        dq, own = parts[2 * g : 2 * g + 2]
        other = last_rows.at[g, step]
        columns = slice(g * lanes, (g + 1) * lanes)
        joined[rows, columns] = dq[...]
        both = (own[...].astype(f32) + other[...].astype(f32)).astype(bf16)
        joined[rows, width + g * lanes : width + (g + 1) * lanes] = both[:, :lanes]
        joined[rows, 2 * width + g * lanes : 2 * width + (g + 1) * lanes] = both[:, lanes:]
        vec[0:1, columns] += column_sum(dq[...].astype(f32))
        vec[1:2, columns] += column_sum(both[:, lanes:].astype(f32))
    grad = across(joined[rows, :], weight[...])
    normal, rstd = norm_parts(rows_ref[...].astype(f32))
    turned[tile] = (normal * vectors[0:1] + vectors[1:2]).astype(bf16).T
    vec[2:3] += column_sum(grad * normal)
    vec[3:4] += column_sum(grad)
    out_rows[step] = (resid_ref[...].astype(f32) + norm_back(grad, normal, rstd, vectors[0:1])).astype(bf16)

    @pl.when(step != held)
    def _():
        return_tile(tile, out_rows.at[step], tok_ref, send_sems.at[step], recv_sems, True)


    @pl.when(step == 0)
    def _():
        wait(loads())
        sum_into(early_final, [early_got[n] for n in range(4)])
        start(share(early_final, early_ref, early_base))
        pltpu.make_async_copy(early_final, early_ref.at[win], keep_sems.at[0]).start()

    @pl.when(step == steps - 1)
    def _():
        size = cells.shape[5]
        cuts = row_cuts(3, part, size)
        for k in range(3):
            full = jnp.dot(turned[0], joined[0:length, k * width : (k + 1) * width], preferred_element_type=f32)
            for n in range(1, 4):
                full = full + jnp.dot(
                    turned[n], joined[n * length : (n + 1) * length, k * width : (k + 1) * width], preferred_element_type=f32
                )
            for b in range(8):
                for which, first, count, piece, row in cuts:
                    if which == k:
                        cells[piece % 2, b // 4, b // 2 % 2, b % 2, piece // 2, row : row + count] = full[
                            b * part + first : b * part + first + count
                        ].astype(bf16)
        tail = jnp.concatenate(
            [vec[...], vec_two[...], vec_up[...]]
            + [jnp.zeros((4 * size - 3 * part - 12, width), f32)],
            axis=0,
        ).astype(bf16)
        for b in range(8):
            cells[1, b // 4, b // 2 % 2, b % 2, 1, 3 * part - 3 * size :] = tail
        exchange = [remote(cells.at[1 - core], core_got, late_base, core_peer)]
        start(exchange)
        wait(share(early_final, early_ref, early_base))
        start(pass_on(early_ref, early_base + 2))
        wait(exchange)
        mine = cells.at[core]
        for b in range(8):
            for x in range(2):
                add_into(mine.at[b // 4, b // 2 % 2, b % 2, x], core_got.at[b // 4, b // 2 % 2, b % 2, x])
        first = [
            remote(mine.at[0, :, 1 - side], late_first.at[0], late_base + 1, side_peer),
            remote(mine.at[1, :, :, 1 - pair], late_first.at[1], late_base + 2, pair_peer),
        ]
        start(first)
        wait(first)
        state = core_got.at[0]
        for z in range(2):
            for n in range(2):
                state[0, z, n] = (mine[0, z, side, n].astype(f32) + late_first[0, z, n].astype(f32)).astype(bf16)
                state[1, z, n] = (mine[1, z, n, pair].astype(f32) + late_first[1, z, n].astype(f32)).astype(bf16)
        start(second_step(state, late_second, late_base + 3))
        wait(second_step(state, late_second, late_base + 3))
        add_second(state, late_second, late_mid)
        across_layers = layer_step(late_mid, late_got, late_base + 5)
        start(across_layers)
        return_tile(tile_order(held), out_rows.at[held], tok_ref, send_sems.at[held], recv_sems, True)
        wait(across_layers)
        sum_into(late_final, [late_mid[layer // 2, layer % 2]] + [late_got[n] for n in range(3)])
        start(share(late_final, late_ref, early_base + 3))
        keep_late = pltpu.make_async_copy(late_final, late_ref.at[win], keep_sems.at[1])
        keep_late.start()
        wait(share(late_final, late_ref, early_base + 3))
        start(pass_on(late_ref, early_base + 5))
        wait(pass_on(early_ref, early_base + 2))
        wait(pass_on(late_ref, early_base + 5))
        pltpu.make_async_copy(early_final, early_ref.at[win], keep_sems.at[0]).wait()
        keep_late.wait()
        for n in range(4):
            return_tile(tile_order(n), out_rows.at[n], tok_ref, send_sems.at[n], recv_sems, False)


def first_send_kernel(place, keep_left, other_left, keep_right, other_right, left_ref, right_ref):
    for keep, other, target in ((keep_left, other_left, left_ref), (keep_right, other_right, right_ref)):
        target[...] = (keep[...] + other[...]).reshape(target.shape)


def sum_low(target, refs):
    total = refs[0][...].astype(jnp.float32)
    for ref in refs[1:]:
        total = total + ref[...].astype(jnp.float32)
    target[...] = total.astype(jnp.bfloat16).reshape(target.shape)


def second_send_kernel(place, keep_left, other_left, got_left, keep_right, other_right, got_right, kept, left, right):
    side, pair = place[0], place[1]

    def total(refs, index):
        return sum(ref[index].astype(jnp.float32) for ref in refs).astype(jnp.bfloat16)

    for bit, first, second in ((0, kept.at[0, 0], kept.at[1, 0]), (1, left.at[0], right.at[0])):
        across_pair = pair if bit == 0 else 1 - pair
        across_side = side if bit == 0 else 1 - side
        first[...] = total((keep_left.at[0, 0, 0], other_left.at[0, 0, 0], got_left.at[0]), across_pair)
        second[...] = total((keep_right.at[0, 0, :, 0], other_right.at[0, 0, :, 0], got_right.at[0]), across_side)


def third_send_kernel(place, *refs):
    for n in range(4):
        keep, left, right = refs[3 * n : 3 * n + 3]
        in_left = (place[3] + n) % 4 < 2
        got = jnp.where(in_left, left[...].astype(jnp.float32), right[...].astype(jnp.float32))
        target = refs[12 + n]
        target[...] = (keep[...].reshape(target.shape).astype(jnp.float32) + got.reshape(target.shape)).astype(jnp.bfloat16)


def unpack_kernel(early, late, qkv_ref, out_ref, up_ref, down_ref):
    f32 = jnp.float32
    part, width = out_ref.shape
    count = up_ref.shape[1] // width
    half = width // 2

    def cells(source, first, rows):
        size = source.shape[1]
        parts = []
        while rows > 0:
            take = min(rows, size - first % size)
            parts.append(source[first // size, first % size : first % size + take])
            first, rows = first + take, rows - take
        return (parts[0] if len(parts) == 1 else jnp.concatenate(parts, axis=0)).astype(f32)

    for k in range(3):
        qkv_ref[:, k * width : (k + 1) * width] = cells(late, k * part, part)
    for k in range(count):
        up_ref[:, k * width : (k + 1) * width] = cells(early, k * part, part)
    turned = cells(early, count * part, half)
    down_ref[:, :half] = turned[:, :half].T
    down_ref[:, half:] = turned[:, half:].T
    out_ref[...] = cells(early, count * part + half, part)


def general_body(
    tokens,
    cotangent,
    w_qkv,
    b_q,
    b_v,
    w_out,
    b_out,
    gain_one,
    shift_one,
    gain_two,
    shift_two,
    w_up,
    b_up,
    w_down,
    b_down,
    rand_owner,
    rand_sub,
    global_ids,
    species,
):
    blk_count = lax.axis_size("blk")
    blk_pos = lax.axis_index("blk")
    win_pos = lax.axis_index("win")
    windows, length, model_width = tokens.shape
    blocks = rand_owner.shape[1]
    heads = rand_owner.shape[2]
    picks = rand_owner.shape[3]
    glob_count = global_ids.shape[1]
    own_blocks = blocks // blk_count
    block_len = length // own_blocks
    head_dim = model_width // heads
    pair_width = 2 * head_dim
    all_rows = windows * length
    key_count = 3 + glob_count + picks
    per_device = own_blocks * heads * picks
    slot_cap = max(2, 2 * per_device // blk_count)
    score_scale = head_dim ** (-0.5)
    f32 = jnp.float32
    bf16 = jnp.bfloat16
    tokens_f = tokens.reshape(all_rows, model_width).astype(f32)
    normed_f, norm_one_pull = jax.vjp(layer_norm, tokens_f, gain_one, shift_one)
    normed = normed_f.astype(bf16)
    joined = jnp.dot(normed, w_qkv, preferred_element_type=f32)
    query_vals = (joined[:, :model_width] + b_q).astype(bf16)
    key_vals = joined[:, model_width : 2 * model_width].astype(bf16)
    value_vals = (joined[:, 2 * model_width :] + b_v).astype(bf16)

    def to_heads(tensor):
        return tensor.reshape(windows, own_blocks, block_len, heads, head_dim).transpose(
            0, 1, 3, 2, 4
        )

    def from_heads(tensor):
        return tensor.transpose(0, 1, 3, 2, 4).reshape(all_rows, model_width)

    query_heads = to_heads(query_vals)
    local_pairs = jnp.concatenate([to_heads(key_vals), to_heads(value_vals)], axis=-1)
    rimmed = padded(local_pairs, (("blk", 1),), 1)
    block_ids = blk_pos * own_blocks + jnp.arange(own_blocks, dtype=jnp.int32)
    owned_glob = (global_ids[:, :, None] == block_ids[None, None, :]).astype(bf16)
    glob_terms = jnp.einsum("wgb,wbhsc->wghsc", owned_glob, local_pairs, preferred_element_type=f32)
    glob_pairs = lax.psum(glob_terms.astype(jnp.bfloat16), "blk").astype(jnp.float32).astype(bf16)
    owner_rows = rand_owner.reshape(windows, blk_count, per_device)
    sub_rows = rand_sub.reshape(windows, blk_count, per_device)
    owner_hits = (owner_rows[..., None] == jnp.arange(blk_count, dtype=jnp.int32)).astype(jnp.int32)
    slot_rows = jnp.sum(owner_hits * (jnp.cumsum(owner_hits, axis=2) - 1), axis=-1)
    my_owner = lax.dynamic_index_in_dim(owner_rows, blk_pos, 1, keepdims=False)
    my_slot = lax.dynamic_index_in_dim(slot_rows, blk_pos, 1, keepdims=False)
    fetch_index = my_owner * slot_cap + my_slot
    head_of_row = jnp.arange(per_device, dtype=jnp.int32) // picks % heads
    source_rows = sub_rows * heads + head_of_row[None, None, :]
    requester = jnp.arange(blk_count, dtype=jnp.int32)[None, :, None]
    target_rows = jnp.where(
        owner_rows == blk_pos, requester * slot_cap + slot_rows, blk_count * slot_cap
    )
    send_table = jnp.full((windows, blk_count * slot_cap + 1), own_blocks * heads, jnp.int32)
    send_table = jax.vmap(set_rows)(
        send_table, target_rows.reshape(windows, -1), source_rows.reshape(windows, -1)
    )[:, : blk_count * slot_cap]
    flat_pairs = jnp.concatenate(
        [
            local_pairs.reshape(windows, own_blocks * heads, block_len, pair_width),
            jnp.zeros((windows, 1, block_len, pair_width), bf16),
        ],
        axis=1,
    )
    outgoing = jax.vmap(take_rows)(flat_pairs, send_table).reshape(
        windows, blk_count, slot_cap, block_len, pair_width
    )
    incoming = lax.all_to_all(outgoing, "blk", split_axis=1, concat_axis=1, tiled=True).reshape(
        windows, blk_count * slot_cap, block_len, pair_width
    )
    rand_pairs = jax.vmap(take_rows)(incoming, fetch_index).reshape(
        windows, own_blocks, heads, picks, block_len, pair_width
    )
    near_pairs = jnp.stack(
        [rimmed[:, 0:own_blocks], rimmed[:, 1 : own_blocks + 1], rimmed[:, 2 : own_blocks + 2]],
        axis=3,
    )
    far_pairs = jnp.broadcast_to(
        glob_pairs.transpose(0, 2, 1, 3, 4)[:, None],
        (windows, own_blocks, heads, glob_count, block_len, pair_width),
    )
    gathered_keys = jnp.concatenate([near_pairs, far_pairs, rand_pairs], axis=3).reshape(
        windows, own_blocks, heads, key_count * block_len, pair_width
    )
    set_keys = gathered_keys[..., :head_dim]
    set_values = gathered_keys[..., head_dim:]
    block_flags = jnp.concatenate(
        [
            (block_ids > 0)[:, None],
            jnp.ones((own_blocks, 1), jnp.bool_),
            (block_ids < blocks - 1)[:, None],
            jnp.ones((own_blocks, glob_count + picks), jnp.bool_),
        ],
        axis=1,
    )
    key_valid = jnp.repeat(block_flags, block_len, axis=1)[None, :, None, None, :]

    def score_block():
        raw_scores = (
            jnp.einsum("wbhqe,wbhke->wbhqk", query_heads, set_keys, preferred_element_type=f32)
            * score_scale
        )
        return jnp.where(key_valid, raw_scores, masked_score)

    score_matrix = score_block()
    top_score = jnp.max(score_matrix, axis=-1, keepdims=True)
    log_total = top_score + jnp.log(
        jnp.sum(jnp.exp(score_matrix - top_score), axis=-1, keepdims=True)
    )
    probs_low = jnp.exp(score_matrix - log_total).astype(bf16)
    attended = jnp.einsum(
        "wbhqk,wbhke->wbhqe", probs_low, set_values, preferred_element_type=f32
    ).astype(bf16)
    merged = from_heads(attended)
    residual = tokens_f + (jnp.dot(merged, w_out, preferred_element_type=f32) + b_out)
    second_f, norm_two_pull = jax.vjp(layer_norm, residual, gain_two, shift_two)
    second = second_f.astype(bf16)
    inner_f = jnp.dot(second, w_up, preferred_element_type=f32) + b_up
    active_f, gelu_pull = jax.vjp(partial(jax.nn.gelu, approximate=False), inner_f)
    active = active_f.astype(bf16)
    output = residual + (jnp.dot(active, w_down, preferred_element_type=f32) + b_down)
    species_count = jnp.sum(
        (species[:, None] == jnp.arange(SPECIES, dtype=jnp.int32)[None, :]).astype(f32), axis=0
    )
    my_species = lax.dynamic_slice_in_dim(species, win_pos * windows, windows)
    own_count = jnp.sum(
        (my_species[:, None] == jnp.arange(SPECIES, dtype=jnp.int32)[None, :]).astype(f32)
        * species_count[None, :],
        axis=1,
    )
    window_scale = jnp.sqrt(species.shape[0] / (SPECIES * own_count))
    upstream = (cotangent.astype(f32) * window_scale[:, None, None]).reshape(all_rows, model_width)
    grad_branch = upstream.astype(bf16)
    grad_w_down = jnp.einsum("tf,td->fd", active, grad_branch, preferred_element_type=f32)
    grad_b_down = jnp.sum(grad_branch, axis=0, dtype=f32)
    grad_active = jnp.einsum("td,fd->tf", grad_branch, w_down, preferred_element_type=f32)
    grad_inner = gelu_pull(grad_active)[0].astype(bf16)
    grad_w_up = jnp.einsum("td,tf->df", second, grad_inner, preferred_element_type=f32)
    grad_b_up = jnp.sum(grad_inner, axis=0, dtype=f32)
    grad_second = jnp.einsum("tf,df->td", grad_inner, w_up, preferred_element_type=f32)
    grad_resid_norm, grad_gain_two, grad_shift_two = norm_two_pull(grad_second)
    grad_resid = upstream + grad_resid_norm
    grad_proj = grad_resid.astype(bf16)
    grad_w_out = jnp.einsum("ti,to->io", merged, grad_proj, preferred_element_type=f32)
    grad_b_out = jnp.sum(grad_proj, axis=0, dtype=f32)
    grad_attended = to_heads(
        jnp.einsum("to,io->ti", grad_proj, w_out, preferred_element_type=f32).astype(bf16)
    )
    probs_full = jnp.exp(score_block() - log_total)
    grad_probs = jnp.einsum(
        "wbhqe,wbhke->wbhqk", grad_attended, set_values, preferred_element_type=f32
    )
    grad_set_values = jnp.einsum(
        "wbhqk,wbhqe->wbhke", probs_full.astype(bf16), grad_attended, preferred_element_type=f32
    )
    row_dot = jnp.sum(probs_full * grad_probs, axis=-1, keepdims=True)
    grad_scores = (probs_full * (grad_probs - row_dot)).astype(bf16)
    grad_query = (
        jnp.einsum("wbhqk,wbhke->wbhqe", grad_scores, set_keys, preferred_element_type=f32)
        * score_scale
    )
    grad_set_keys = (
        jnp.einsum("wbhqk,wbhqe->wbhke", grad_scores, query_heads, preferred_element_type=f32)
        * score_scale
    )
    grad_set = jnp.concatenate([grad_set_keys, grad_set_values], axis=-1).reshape(
        windows, own_blocks, heads, key_count, block_len, pair_width
    )
    extended = (
        jnp.pad(grad_set[:, :, :, 1], ((0, 0), (1, 1), (0, 0), (0, 0), (0, 0)))
        + jnp.pad(grad_set[:, :, :, 0], ((0, 0), (0, 2), (0, 0), (0, 0), (0, 0)))
        + jnp.pad(grad_set[:, :, :, 2], ((0, 0), (2, 0), (0, 0), (0, 0), (0, 0)))
    )
    edge_grads = jnp.concatenate([extended[:, :1], extended[:, own_blocks + 1 :]], axis=1)
    edge_back = padded(edge_grads.astype(jnp.bfloat16), (("blk", 1),), 1).astype(edge_grads.dtype)
    pair_grad = extended[:, 1 : own_blocks + 1]
    pair_grad = pair_grad.at[:, 0].add(edge_back[:, 0]).at[:, own_blocks - 1].add(edge_back[:, 3])
    glob_grad = jnp.sum(grad_set[:, :, :, 3 : 3 + glob_count], axis=1).transpose(0, 2, 1, 3, 4)
    glob_total = lax.psum(glob_grad.astype(jnp.bfloat16), "blk").astype(jnp.float32)
    pair_grad = pair_grad + jnp.einsum(
        "wgb,wghsc->wbhsc", owned_glob.astype(f32), glob_total, precision=lax.Precision.HIGHEST
    )
    rand_grad = grad_set[:, :, :, 3 + glob_count :].reshape(
        windows, per_device, block_len, pair_width
    )
    back_out = jax.vmap(add_rows)(
        jnp.zeros((windows, blk_count * slot_cap, block_len, pair_width), f32),
        fetch_index,
        rand_grad,
    )
    back_in = lax.all_to_all(
        back_out.reshape(windows, blk_count, slot_cap, block_len, pair_width).astype(jnp.bfloat16),
        "blk",
        split_axis=1,
        concat_axis=1,
        tiled=True,
    ).astype(jnp.float32)
    owner_sum = jax.vmap(add_rows)(
        jnp.zeros((windows, own_blocks * heads + 1, block_len, pair_width), f32),
        send_table,
        back_in.reshape(windows, blk_count * slot_cap, block_len, pair_width),
    )
    pair_grad = pair_grad + owner_sum[:, : own_blocks * heads].reshape(
        windows, own_blocks, heads, block_len, pair_width
    )
    grad_keys = from_heads(pair_grad[..., :head_dim].astype(bf16))
    grad_values = from_heads(pair_grad[..., head_dim:].astype(bf16))
    grad_joined = jnp.concatenate(
        [from_heads(grad_query.astype(bf16)), grad_keys, grad_values], axis=1
    )
    grad_w_qkv = jnp.einsum("td,tc->dc", normed, grad_joined, preferred_element_type=f32)
    grad_b_q = jnp.sum(grad_joined[:, :model_width], axis=0, dtype=f32)
    grad_b_v = jnp.sum(grad_joined[:, 2 * model_width :], axis=0, dtype=f32)
    grad_normed = jnp.einsum("tc,dc->td", grad_joined, w_qkv, preferred_element_type=f32)
    grad_tok_norm, grad_gain_one, grad_shift_one = norm_one_pull(grad_normed)
    grad_tokens = (grad_resid + grad_tok_norm).astype(bf16).reshape(windows, length, model_width)
    local_grads = (
        grad_w_qkv,
        grad_b_q,
        grad_b_v,
        grad_w_out,
        grad_b_out,
        grad_gain_one,
        grad_shift_one,
        grad_gain_two,
        grad_shift_two,
        grad_w_up,
        grad_b_up,
        grad_w_down,
        grad_b_down,
    )
    packed_grads = jnp.concatenate(
        [grad_item.reshape(blk_count, -1) for grad_item in local_grads], axis=1
    )
    total_cols = packed_grads.shape[1]
    win_count = lax.axis_size("win")
    pad_cols = -total_cols % win_count
    shard_sum = lax.psum_scatter(
        packed_grads.astype(jnp.bfloat16), "blk", scatter_dimension=0, tiled=True
    ).astype(jnp.float32)
    split_shard = jnp.pad(shard_sum, ((0, 0), (0, pad_cols))).reshape(win_count, -1)
    group_piece = lax.psum_scatter(
        split_shard.astype(jnp.bfloat16), "win", scatter_dimension=0, tiled=True
    ).astype(jnp.float32)
    summed = (
        lax.all_gather(group_piece.astype(jnp.bfloat16), "win", axis=0, tiled=True)
        .astype(group_piece.dtype)
        .reshape(1, -1)[:, :total_cols]
    )
    shards = []
    offset = 0
    for grad_item in local_grads:
        entry_count = grad_item.size // blk_count
        shards.append(
            summed[0, offset : offset + entry_count].reshape(
                (grad_item.shape[0] // blk_count,) + grad_item.shape[1:]
            )
        )
        offset = offset + entry_count
    out_tokens = output.astype(bf16).reshape(windows, length, model_width)
    return (
        out_tokens,
        grad_tokens,
        shards[0],
        shards[1],
        shards[2],
        shards[3],
        shards[4],
        shards[5],
        shards[6],
        shards[7],
        shards[8],
        shards[9],
        shards[10],
        shards[11],
        shards[12],
    )


def layer_step(*arguments):
    windows = arguments[0].shape[0]
    paired = lax.axis_size("blk") == 2 * windows and lax.axis_size("win") == 4 and windows == 4
    return (paired_body if paired else general_body)(*arguments)


def paired_body(
    tokens,
    cotangent,
    w_qkv,
    b_q,
    b_v,
    w_out,
    b_out,
    gain_one,
    shift_one,
    gain_two,
    shift_two,
    w_up,
    b_up,
    w_down,
    b_down,
    rand_owner,
    rand_sub,
    global_ids,
    species,
):
    f32 = jnp.float32
    bf16 = jnp.bfloat16
    win_count = lax.axis_size("win")
    blk_count = lax.axis_size("blk")
    win_pos = lax.axis_index("win")
    blk_pos = lax.axis_index("blk")
    layers, length, width = tokens.shape
    core, layer, side = win_pos % 2, blk_pos // 2, blk_pos % 2
    blocks, heads, picks = rand_owner.shape[1:]
    own_blocks = blocks // blk_count
    half_blocks = blocks // 2
    block_len = length // own_blocks
    head_dim = width // heads
    all_rows = layers * length
    lanes = HEADS_PER_GROUP * head_dim
    groups = heads // HEADS_PER_GROUP
    score_scale = head_dim ** (-0.5)

    def takes(micros):
        return pl.CostEstimate(flops=micros * 1_000_000_000, bytes_accessed=micros * 1_000_000, transcendentals=0)


    rand_size = blocks * heads * picks
    named = jnp.concatenate(
        [
            lax.dynamic_index_in_dim((rand_owner * own_blocks + rand_sub).reshape(layers, rand_size), layer, 0, keepdims=False),
            lax.dynamic_index_in_dim(global_ids, layer, 0, keepdims=False),
        ]
    )
    slot = jnp.arange(half_blocks, dtype=jnp.int32)

    def table_for(which):
        block = (((layer - slot // own_blocks) % layers) * 2 + which) * own_blocks + slot % own_blocks
        reads = jnp.concatenate([named, jnp.maximum(block - 1, 0), jnp.minimum(block + 1, blocks - 1)])
        owner = reads // own_blocks
        half = jnp.where(owner % 2 == which, 0, half_blocks)
        places = half + ((layer - owner // 2) % layers) * own_blocks + reads % own_blocks
        return jnp.concatenate([places, block])

    table = jnp.where(side == core, table_for(core), swap(table_for(1 - core), 1, 0))
    sizes = (heads, picks, rand_size, half_blocks)

    tile = length

    def by_rows(columns):
        return pl.BlockSpec((tile, columns), lambda i: (i, 0))

    def by_tile(columns):
        return pl.BlockSpec((tile, columns), lambda i: (tile_order(i), 0))

    def whole(*shape, once=True):
        mode = pl.Buffered(1) if once else None
        return pl.BlockSpec(shape, lambda i: (0,) * len(shape), pipeline_mode=mode)

    scalars = pl.BlockSpec(memory_space=pltpu.SMEM)
    wide = w_up.shape[1]
    params = pltpu.CompilerParams(vmem_limit_bytes=60 << 20)
    row = lambda vector: vector.reshape(1, -1)
    def remote_params(number, mib):
        return pltpu.CompilerParams(vmem_limit_bytes=mib << 20, collective_id=number, has_side_effects=True)

    any_place = pl.BlockSpec(memory_space=pl.ANY)
    hbm = pl.BlockSpec(memory_space=pltpu.HBM)

    def keep(*shape):
        return pltpu.VMEM(shape, bf16)

    copies = pltpu.SemaphoreType.DMA((layers,))
    vectors_one = jnp.stack([gain_one, shift_one, b_q, b_v])
    vectors_two = jnp.stack([b_out, gain_two, shift_two, b_down])
    rows_in, query, key_value, key_value_other = pl.pallas_call(
        partial(front_kernel, score_scale),
        grid=(layers,),
        in_specs=[any_place, whole(4, width), whole(width, 3 * width)],
        out_specs=[hbm, pl.BlockSpec((tile, width), lambda i: (arrival_order(i), 0)), hbm, hbm],
        out_shape=[
            jax.ShapeDtypeStruct((all_rows, width), bf16),
            jax.ShapeDtypeStruct((all_rows, width), bf16),
            jax.ShapeDtypeStruct((all_rows, 2 * width), bf16),
            jax.ShapeDtypeStruct((all_rows, 2 * width), bf16),
        ],
        scratch_shapes=[keep(layers, length, width), keep(layers, length, 2 * width)] + [copies] * 6,
        compiler_params=remote_params(1, 48),
        cost_estimate=takes(80),
        name="front",
    )(tokens, vectors_one, w_qkv)

    def lane_group(first):
        return pl.BlockSpec((all_rows, lanes), lambda g: (0, first + g))

    store = pltpu.VMEM((blocks, block_len, lanes), bf16)
    halves = layers // 2
    attended, log_total, cot_even = pl.pallas_call(
        partial(attend_kernel, sizes, blocks, head_dim, (0, 2)),
        grid=(groups,),
        in_specs=[scalars] + [lane_group(0), lane_group(0), lane_group(0), lane_group(groups), lane_group(groups), any_place],
        out_specs=[lane_group(0), pl.BlockSpec((1, half_blocks, lanes), lambda g: (g, 0, 0)), hbm],
        out_shape=[
            jax.ShapeDtypeStruct((all_rows, width), bf16),
            jax.ShapeDtypeStruct((groups, half_blocks, lanes), f32),
            jax.ShapeDtypeStruct((halves, length, width), bf16),
        ],
        scratch_shapes=[store, store] + [pltpu.SemaphoreType.DMA((halves,))] * 2,
        compiler_params=remote_params(4, 56),
        cost_estimate=takes(38),
        name="attend",
    )(table, query, key_value, key_value_other, key_value, key_value_other, cotangent)

    payload = 2 * wide // blk_count + width // blk_count
    payload += -payload % (16 * win_count)
    stays = jax.ShapeDtypeStruct((blk_count, win_count // 2, payload // win_count, width), bf16)
    output, out_last, normal, second_t, attended_t, rstd, active, slope, cot_odd = pl.pallas_call(
        partial(ffn_forward_kernel, 256, (1, 3)),
        grid=(layers,),
        in_specs=[
            by_rows(width), by_rows(width), whole(width, width), whole(4, width), any_place, whole(1, wide), any_place, any_place,
        ],
        out_specs=[
            by_rows(width), whole(length, width, once=False), by_rows(width), pl.BlockSpec((width, length), lambda i: (0, i)), pl.BlockSpec((width, length), lambda i: (0, i)),
            by_rows(128), by_rows(wide), by_rows(wide), hbm,
        ],
        out_shape=[
            jax.ShapeDtypeStruct((all_rows, width), bf16),
            jax.ShapeDtypeStruct((length, width), bf16),
            jax.ShapeDtypeStruct((all_rows, width), bf16),
            jax.ShapeDtypeStruct((width, all_rows), bf16),
            jax.ShapeDtypeStruct((width, all_rows), bf16),
            jax.ShapeDtypeStruct((all_rows, 128), f32),
            jax.ShapeDtypeStruct((all_rows, wide), bf16),
            jax.ShapeDtypeStruct((all_rows, wide), bf16),
            jax.ShapeDtypeStruct((halves, length, width), bf16),
        ],
        scratch_shapes=[pltpu.SemaphoreType.DMA((halves,))] * 2 + [keep(width, wide), keep(wide, width), pltpu.SemaphoreType.DMA((2,))],
        compiler_params=remote_params(5, 60),
        cost_estimate=takes(35),
        name="ffn_forward",
    )(rows_in, attended, w_out, vectors_two, w_up, row(b_up), w_down, cotangent)

    chunks = wide // width

    grad_resid, grad_attended, vec_two, vec_up, early_keep, early_other, out_tokens = pl.pallas_call(
        partial(ffn_back_kernel, chunks, blk_count, (2, 1, 0)),
        grid=(chunks,),
        in_specs=[
            scalars, pl.BlockSpec((all_rows, width), lambda i: (0, i)), pl.BlockSpec((all_rows, width), lambda i: (0, i)),
            pl.BlockSpec((width, width), lambda i: (0, i)), pl.BlockSpec((width, width), lambda i: (i, 0)),
            whole(width, all_rows), whole(4, width), *[any_place] * 7,
        ],
        out_specs=[hbm, hbm, whole(4, width), whole(chunks, width), hbm, hbm, hbm],
        out_shape=[
            jax.ShapeDtypeStruct((all_rows, width), bf16),
            jax.ShapeDtypeStruct((all_rows, width), bf16),
            jax.ShapeDtypeStruct((4, width), f32),
            jax.ShapeDtypeStruct((chunks, width), f32),
            stays,
            stays,
            jax.ShapeDtypeStruct((layers, length, width), bf16),
        ],
        scratch_shapes=[
            keep(layers, length, width),
            keep(all_rows, width),
            keep(width, all_rows),
            keep(all_rows, width),
            pltpu.VMEM((all_rows, width), f32),
            keep(2, blk_count, payload - chunks * width // blk_count - width // 2, width),
            keep(2, 2, width // 2, width),
            pltpu.SemaphoreType.DMA((layers,)),
            pltpu.SemaphoreType.DMA((layers,)),
            pltpu.SemaphoreType.DMA((layers,)),
            pltpu.SemaphoreType.DMA((48,)),
            pltpu.SemaphoreType.DMA((48,)),
            pltpu.SemaphoreType.DMA((2,)),
            keep(all_rows, width),
            pltpu.VMEM((all_rows, 128), f32),
            keep(width, all_rows),
            keep(width, width),
            pltpu.SemaphoreType.DMA((4,)),
        ],
        compiler_params=remote_params(3, 63),
        cost_estimate=takes(60),
        name="ffn_back",
    )(
        species, active, slope, w_up, w_down, second_t, vectors_two, normal, rstd, attended_t, w_out, cot_even, cot_odd, output,
    )
    last_pairs = [(there, here) for here, there in regroup_pairs(win_count, layers, 3)]
    out_last = lax.ppermute(out_last, ("win", "blk"), last_pairs)
    pair = win_pos // 2
    early_rows = payload // win_count
    late_rows = 3 * width // blk_count + 32
    late_size = late_rows // win_count
    cell = (early_rows, width)
    early_keep = early_keep.reshape((2, 2, 2, 2) + cell)
    early_other = early_other.reshape((2, 2, 2, 2) + cell)
    place = jnp.stack([side, pair, side, layer])

    def picked(index):
        return pl.BlockSpec((1, 1, 1, 1) + cell, lambda z, n, p: index(z, n, p) + (0, 0))

    def listed(index):
        return pl.BlockSpec((1, 1) + cell, lambda z, n, p: index(z, n, p) + (0, 0))

    def cells_of(count):
        return [jax.ShapeDtypeStruct((2, 2) + cell, bf16)] * count

    def first_send():
        left = picked(lambda z, n, p: (0, z, 1 - p[0], n))
        right = picked(lambda z, n, p: (1, z, n, 1 - p[1]))
        return pl.pallas_call(
            first_send_kernel,
            grid_spec=pltpu.PrefetchScalarGridSpec(
                num_scalar_prefetch=1, grid=(2, 2), in_specs=[left, left, right, right], out_specs=[listed(lambda z, n, p: (z, n))] * 2
            ),
            out_shape=cells_of(2),
            cost_estimate=takes(3),
            name="first_send",
        )(place, early_keep, early_other, early_keep, early_other)

    def second_send(got_left, got_right):
        left = pl.BlockSpec((1, 1, 1, 2) + cell, lambda z, p: (0, z, p[0], 0, 0, 0))
        right = pl.BlockSpec((1, 1, 2, 1) + cell, lambda z, p: (1, z, 0, p[1], 0, 0))
        got = pl.BlockSpec((1, 2) + cell, lambda z, p: (z, 0, 0, 0))
        rows_spec = pl.BlockSpec((1,) + cell, lambda z, p: (z, 0, 0))
        both_spec = pl.BlockSpec((2, 1) + cell, lambda z, p: (0, z, 0, 0))
        return pl.pallas_call(
            second_send_kernel,
            grid_spec=pltpu.PrefetchScalarGridSpec(
                num_scalar_prefetch=1, grid=(2,), in_specs=[left, left, got, right, right, got], out_specs=[both_spec, rows_spec, rows_spec]
            ),
            out_shape=cells_of(1) + [jax.ShapeDtypeStruct((2,) + cell, bf16)] * 2,
            compiler_params=params,
            cost_estimate=takes(4),
            name="second_send",
        )(place, early_keep, early_other, got_left, early_keep, early_other, got_right)

    def third_send(keep, left, right):
        specs = []
        for step in range(layers):
            goal = lambda p, step=step: (p[3] + step) % layers
            specs.append(listed(lambda z, n, p, goal=goal: (goal(p) // 2, goal(p) % 2)))
            specs += [pl.BlockSpec((1,) + cell, lambda z, n, p, goal=goal: (goal(p) % 2, 0, 0))] * 2
        out = pl.BlockSpec(cell, lambda z, n, p: (0, 0))
        return pl.pallas_call(
            third_send_kernel,
            grid_spec=pltpu.PrefetchScalarGridSpec(num_scalar_prefetch=1, grid=(1, 1), in_specs=specs, out_specs=[out] * layers),
            out_shape=[jax.ShapeDtypeStruct(cell, bf16)] * layers,
            cost_estimate=takes(3),
            name="third_send",
        )(place, *[keep, left, right] * layers)

    def to_layer(value, step):
        pairs = [
            (win * blk_count + blk, win * blk_count + (blk + 2 * step) % blk_count)
            for win in range(win_count)
            for blk in range(blk_count)
        ]
        return lax.ppermute(value, ("win", "blk"), pairs)

    first_left, first_right = first_send()
    first_left, first_right = swap(first_left, 0, 1), swap(first_right, 2, 0)

    grad_parts, grad_others = [], []
    for group in range(groups):
        after = []
        if group == 1:
            early_kept, send_left, send_right = second_send(first_left, first_right)
            after = [early_kept, out_last]
            second = swap(send_left, 2, 0), swap(send_right, 0, 1)
        if group == 2:
            early_parts = third_send(early_kept, *second)
            after = [early_parts[0]]
            early_parts = [early_parts[0]] + [to_layer(early_parts[n], n) for n in range(1, layers)]

        def column(first):
            return pl.BlockSpec((all_rows, lanes), lambda g, t: (0, first))

        def full(columns):
            return pl.BlockSpec((all_rows, columns), lambda g, t: (0, 0))

        grad_store = pltpu.VMEM((blocks, block_len, lanes), f32)
        glob_store = pltpu.VMEM((2, block_len, lanes), f32)
        dq, own, other = pl.pallas_call(
            partial(attend_back_kernel, sizes, blocks, head_dim, score_scale, group),
            grid_spec=pltpu.PrefetchScalarGridSpec(
                num_scalar_prefetch=1,
                grid=(1,),
                in_specs=[
                    column(group), column(group), column(group), column(groups + group), column(groups + group), column(group),
                    pl.BlockSpec((1, half_blocks, lanes), lambda g, t: (group, 0, 0)),
                    *[any_place] * len(after),
                ],
                out_specs=[full(lanes), full(2 * lanes), full(2 * lanes)],
                scratch_shapes=[store, store, grad_store, grad_store, glob_store, glob_store],
            ),
            out_shape=[jax.ShapeDtypeStruct((all_rows, n * lanes), bf16) for n in (1, 2, 2)],
            compiler_params=params,
            cost_estimate=takes(25),
            name="attend_back",
        )(table, query, key_value, key_value_other, key_value, key_value_other, grad_attended, log_total, *after)
        grad_parts += [dq, own]
        grad_others.append(other)

    def vmem(*shape):
        return pltpu.VMEM(shape, bf16)

    first_shape, mid_shape = (2, 2, 2), (2, 2)
    chain = lambda size: [vmem(*lead, size, width) for lead in (first_shape, mid_shape, mid_shape, (3,), ())]
    grad_tokens, late, early = pl.pallas_call(
        partial(finish_kernel, groups),
        grid=(layers,),
        in_specs=[by_tile(p.shape[1]) for p in grad_parts]
        + [any_place] * groups
        + [by_tile(width), by_tile(width), whole(4, width), whole(width, 3 * width), whole(4, width), whole(chunks, width)]
        + [any_place] * layers,
        out_specs=[hbm] * 3,
        out_shape=[
            jax.ShapeDtypeStruct((layers, length, width), bf16),
            jax.ShapeDtypeStruct((win_count, late_size, width), bf16),
            jax.ShapeDtypeStruct((win_count, early_rows, width), bf16),
        ],
        scratch_shapes=[
            vmem(all_rows, 3 * width),
            vmem(layers, width, length),
            pltpu.VMEM((4, width), f32),
            vmem(layers, length, width),
            vmem(2, 2, 2, 2, 2, late_size, width),
            vmem(2, 2, 2, 2, late_size, width),
            chain(late_size),
            [vmem(*lead, early_rows, width) for lead in ((4,), ())],
            pltpu.SemaphoreType.DMA((layers,)),
            pltpu.SemaphoreType.DMA((layers,)),
            pltpu.SemaphoreType.DMA((4,)),
            pltpu.SemaphoreType.DMA((14,)),
            pltpu.SemaphoreType.DMA((14,)),
            pltpu.SemaphoreType.DMA((2,)),
            vmem(groups, layers, length, 2 * lanes),
            pltpu.SemaphoreType.DMA((groups, layers)),
            pltpu.SemaphoreType.DMA((groups, layers)),
        ],
        compiler_params=remote_params(2, 62),
        cost_estimate=takes(90),
        name="finish",
    )(
        *grad_parts, *grad_others, rows_in, grad_resid, vectors_one, w_qkv, vec_two, vec_up,
        *early_parts,
    )
    part = width // blk_count
    count = wide // width
    done_qkv, done_out, done_up, done_down = pl.pallas_call(
        unpack_kernel,
        out_shape=[
            jax.ShapeDtypeStruct(shape, f32)
            for shape in ((part, 3 * width), (part, width), (part, wide), (wide // blk_count, width))
        ],
        compiler_params=params,
        cost_estimate=takes(4),
        name="unpack",
    )(early, late)
    late = late.reshape(-1, width)[3 * part :].astype(f32)
    vec = lax.dynamic_slice_in_dim(late[:8], blk_pos * part, part, axis=1)
    vec_wide = lax.dynamic_slice_in_dim(late[8 : 8 + count].reshape(-1), blk_pos * (wide // blk_count), wide // blk_count)
    return (
        lax.dynamic_update_index_in_dim(out_tokens, out_last, (layer + 3) % layers, 0),
        grad_tokens,
        done_qkv,
        vec[0],
        vec[1],
        done_out,
        vec[4],
        vec[2],
        vec[3],
        vec[5],
        vec[6],
        done_up,
        vec_wide,
        done_down,
        vec[7],
    )


def solution(mesh):
    placed = (
        P("win", "blk", None),
        P("win", "blk", None),
        P(),
        P(),
        P(),
        P(),
        P(),
        P(),
        P(),
        P(),
        P(),
        P(),
        P(),
        P(),
        P(),
        P("win", None, None, None),
        P("win", None, None, None),
        P("win", None),
        P(),
    )
    return jax.shard_map(
        layer_step,
        mesh=mesh,
        in_specs=placed,
        out_specs=(
            P("win", "blk", None),
            P("win", "blk", None),
            P("blk", None),
            P("blk"),
            P("blk"),
            P("blk", None),
            P("blk"),
            P("blk"),
            P("blk"),
            P("blk"),
            P("blk"),
            P("blk", None),
            P("blk"),
            P("blk", None),
            P("blk"),
        ),
        check_vma=False,
    )
```
